32 devices in a mesh: wide: 8 (over z, x), narrow: 4 (over y, core).
Axes of the slice: x: 2, y: 2, z: 4, core: 2. Of those that a mesh axis runs over, the one named last changes fastest.
Arguments:
- frames: bfloat16 [26624, 1024], P(('wide', 'narrow')), may hold values from -6 to 6
- text_states: bfloat16 [16, 64, 1024], P('wide'), may hold values from -6 to 6
- lengths: int32 [16], P('wide'), may hold values from 1457 to 1664, as said below
- loss_mask: int32 [26624], P(('wide', 'narrow')), may hold values 0 or 1
- norm_gain: float32 [3, 1024], replicated, may hold values from 0.25 to 1.75
- norm_bias: float32 [3, 1024], replicated, may hold values from -2 to 2
- w_qkv: bfloat16 [3, 1024, 1024], P(None, None, 'narrow'), may hold values from -0.1875 to 0.1875
- w_out: bfloat16 [1024, 1024], P('narrow'), may hold values from -1.5 to 1.5
- w_cross_q: bfloat16 [1024, 1024], P(None, 'narrow'), may hold values from -0.1875 to 0.1875
- w_cross_kv: bfloat16 [2, 1024, 1024], P(None, None, 'narrow'), may hold values from -0.1875 to 0.1875
- w_cross_out: bfloat16 [1024, 1024], P('narrow'), may hold values from -0.75 to 0.75
- w_up: bfloat16 [1024, 4096], P(None, 'narrow'), may hold values from -0.1875 to 0.1875
- w_down: bfloat16 [4096, 1024], P('narrow'), may hold values from -0.09375 to 0.09375
- cotangent: bfloat16 [26624, 1024], P(('wide', 'narrow')), may hold values from -6 to 6
Outputs:
- out: bfloat16 [26624, 1024], P(('wide', 'narrow'))
- grad_frames: bfloat16 [26624, 1024], P(('wide', 'narrow'))
- grad_text: bfloat16 [16, 64, 1024], P('wide')
- grad_norm_gain: float32 [3, 1024], replicated
- grad_norm_bias: float32 [3, 1024], replicated
- grad_qkv: float32 [3, 1024, 1024], P(None, None, 'narrow')
- grad_out: float32 [1024, 1024], P('narrow')
- grad_cross_q: float32 [1024, 1024], P(None, 'narrow')
- grad_cross_kv: float32 [2, 1024, 1024], P(None, None, 'narrow')
- grad_cross_out: float32 [1024, 1024], P('narrow')
- grad_up: float32 [1024, 4096], P(None, 'narrow')
- grad_down: float32 [4096, 1024], P('narrow')
The draws below stay inside these ranges and needn't reach their ends.
Inputs may be any that keep to these rules, and one draw needn't show every extreme that they name: `lengths`: in every draw one item has all 1664 frames real.
All inputs are finite; a program needn't handle non-finite values. No bound on the sum of `loss_mask` on one device may be relied on, other than what follows from the above.
Results may differ from the reference program's by a relative error of at most 0.019.
The reference program's roundings to bfloat16 on the way count: a program that leaves them out, or rounds other values in their place, can miss the bound.
Values may be sent and summed in bfloat16 or wider, within the bound.
No kernel may reach another device: no remote copies, remote signals or barrier semaphores. Data moves between devices by JAX's collectives and lax.ppermute only.
A program may use at most 320 MiB of HBM per device.

```python
import jax
import jax.numpy as jnp
from jax import lax

D = 1024
HEADS = 16
HEAD = 64
FF = 4096
TEXT = 64
FRAMES = 1664
ITEMS = 16


def draw_lengths(key, part):
    shorten = jax.random.randint(jax.random.fold_in(key, 11), (ITEMS,), 0, FRAMES // 8)
    chosen = jax.random.randint(jax.random.fold_in(key, 12), (), 0, ITEMS)
    places = jnp.arange(ITEMS)
    return jnp.where(places == chosen, FRAMES, FRAMES - shorten).astype(jnp.int32)


def with_ends(result, key, low, high):
    index_at = [jax.random.randint(jax.random.fold_in(key, axis), (), 0, length) for axis, length in enumerate(result.shape)]
    main_axis = result.shape.index(max(result.shape))
    beside = index_at[:main_axis] + [(index_at[main_axis] + 1) % result.shape[main_axis]] + index_at[main_axis + 1:]
    return result.at[tuple(index_at)].set(low).at[tuple(beside)].set(high)


def level_of(stream_key, dims, cuts, least, top_value):
    loudness = 1.0
    for axis_at, shards_of in cuts:
        draws = jax.random.uniform(jax.random.fold_in(jax.random.fold_in(stream_key, 6), axis_at), (shards_of,), jnp.float32, least / len(cuts), top_value / len(cuts))
        loudness = loudness * jnp.repeat(jnp.exp(draws), dims[axis_at] // shards_of).reshape((-1,) + (1,) * (len(dims) - 1 - axis_at))
    return loudness


def normal_values(stream_key, dims, width, reach, shards=(), kind=jnp.bfloat16):
    level = level_of(stream_key, dims, shards, -0.22, 0.18) if shards else 1.0
    array = jax.random.normal(stream_key, dims, jnp.float32) * width * level
    return jnp.minimum(jnp.maximum(array, -reach), reach).astype(kind)


def setup_inputs(seed: int = 0) -> dict:
    key_list = jax.random.split(jax.random.key(seed), 15)
    return {
        "frames": normal_values(key_list[0], (ITEMS * FRAMES, D), 1.0, 6.0, ((0, 32),)),
        "text_states": normal_values(key_list[1], (ITEMS, TEXT, D), 1.0, 6.0, ((0, 8),)),
        "lengths": draw_lengths(jax.random.fold_in(key_list[14], 71), 0),
        "loss_mask": with_ends((jax.random.randint(key_list[3], (ITEMS * FRAMES,), 0, 8) < 7).astype(jnp.int32), jax.random.fold_in(key_list[3], 1), 0, 1),
        "norm_gain": jnp.clip(1.0 + 0.15 * jax.random.normal(key_list[4], (3, D), jnp.float32), 0.25, 1.75),
        "norm_bias": normal_values(key_list[5], (3, D), 0.3, 2.0, (), jnp.float32),
        "w_qkv": normal_values(key_list[6], (3, D, D), D ** -0.5, 0.1875, ((2, 4),)),
        "w_out": normal_values(key_list[7], (D, D), (D // 64) ** -0.5, 1.5, ((0, 4),)),
        "w_cross_q": normal_values(key_list[8], (D, D), D ** -0.5, 0.1875, ((1, 4),)),
        "w_cross_kv": normal_values(key_list[9], (2, D, D), D ** -0.5, 0.1875, ((2, 4),)),
        "w_cross_out": normal_values(key_list[10], (D, D), (D // 16) ** -0.5, 0.75, ((0, 4),)),
        "w_up": normal_values(key_list[11], (D, FF), D ** -0.5, 0.1875, ((1, 4),)),
        "w_down": normal_values(key_list[12], (FF, D), FF ** -0.5, 0.09375, ((0, 4),)),
        "cotangent": normal_values(key_list[13], (ITEMS * FRAMES, D), 1.0, 6.0, ((0, 32),)),
    }


EPS = 1e-05
NEG = -1e+30
HIGHEST = lax.Precision.HIGHEST

@jax.custom_vjp
def low(v):
    return lax.optimization_barrier(v.astype(jnp.bfloat16)).astype(jnp.float32)

@jax.custom_vjp
def low_back(v):
    return v

def low_keep(v):
    return (low(v), None)

def low_pass(kept, grad):
    return (grad,)

def back_keep(v):
    return (v, None)

def back_low(kept, grad):
    return (low(grad),)
low.defvjp(low_keep, low_pass)
low_back.defvjp(back_keep, back_low)

def rounded(value):
    return low(low_back(value))

def mix(form, left_side, right_side):
    return jnp.einsum(form, left_side, right_side, precision=HIGHEST)

def normalize(values_in, gain_row, bias_row):
    row_mean = lax.optimization_barrier(jnp.mean(values_in, axis=-1, keepdims=True))
    centered = values_in - row_mean
    variance = lax.optimization_barrier(jnp.mean(centered * centered, axis=-1, keepdims=True))
    return centered * lax.rsqrt(variance + EPS) * gain_row + bias_row

def gelu_exact(values_in):
    return values_in * 0.5 * (1.0 + jax.scipy.special.erf(values_in * 0.7071067811865476))

def attention(query_part, key_part, value_part, valid):
    scores = low_back(mix('fhe,khe->hfk', query_part, key_part) * HEAD ** (-0.5))
    scores = jnp.where(valid, scores, NEG)
    row_top = lax.optimization_barrier(jnp.max(scores, axis=-1, keepdims=True))
    weights_exp = jnp.exp(scores - row_top)
    probability = weights_exp / lax.optimization_barrier(jnp.sum(weights_exp, axis=-1, keepdims=True))
    return mix('hfk,khe->fhe', low(probability), value_part)

def item_layer(frame_rows, text_rows, item_limit, gains, biases, w_qkv, w_out, w_cross_q, w_cross_kv, w_cross_out, w_up, w_down):
    span = frame_rows.shape[0]
    places = jnp.arange(span)
    valid = (places[None, :] <= places[:, None]) & (places[None, :] < item_limit)
    normed = low(normalize(frame_rows, gains[0], biases[0]))
    triple = rounded(mix('rd,cde->cre', normed, w_qkv)).reshape(3, span, HEADS, HEAD)
    attended = rounded(attention(triple[0], triple[1], triple[2], valid)).reshape(span, D)
    first = frame_rows + low_back(mix('re,ed->rd', attended, w_out))
    normed = low(normalize(first, gains[1], biases[1]))
    cross_query = rounded(mix('rd,de->re', normed, w_cross_q)).reshape(span, HEADS, HEAD)
    cross_pair = rounded(mix('td,cde->cte', text_rows, w_cross_kv)).reshape(2, text_rows.shape[0], HEADS, HEAD)
    cross_mixed = rounded(attention(cross_query, cross_pair[0], cross_pair[1], True)).reshape(span, D)
    second = first + low_back(mix('re,ed->rd', cross_mixed, w_cross_out))
    normed = low(normalize(second, gains[2], biases[2]))
    hidden_pre = low_back(mix('rd,df->rf', normed, w_up))
    active = low(gelu_exact(hidden_pre))
    return second + low_back(mix('rf,fd->rd', active, w_down))

def reference(frames, text_states, lengths, loss_mask, norm_gain, norm_bias, w_qkv, w_out, w_cross_q, w_cross_kv, w_cross_out, w_up, w_down, cotangent):

    def forward(frame_all, text_all, gains, biases, wqkv, wout, wcq, wckv, wco, wup, wdown):

        def one_item(packed):
            frame_rows, text_rows, item_limit = packed
            return item_layer(frame_rows, text_rows, item_limit, gains, biases, wqkv, wout, wcq, wckv, wco, wup, wdown)
        stacked = lax.map(jax.checkpoint(one_item), (frame_all.reshape(ITEMS, FRAMES, D), text_all, lengths))
        return stacked.reshape(ITEMS * FRAMES, D)
    inputs = tuple((array_in.astype(jnp.float32) for array_in in (frames, text_states, norm_gain, norm_bias, w_qkv, w_out, w_cross_q, w_cross_kv, w_cross_out, w_up, w_down)))
    output, pull = jax.vjp(forward, *inputs)
    upstream = cotangent.astype(jnp.float32) * loss_mask.astype(jnp.float32)[:, None]
    grads = pull(upstream)
    return (output.astype(jnp.bfloat16), grads[0].astype(jnp.bfloat16), grads[1].astype(jnp.bfloat16), grads[2], grads[3], grads[4], grads[5], grads[6], grads[7], grads[8], grads[9], grads[10])
```

```python
import functools

import jax
import jax.numpy as jnp
from jax import lax
from jax.experimental import pallas as pl
from jax.experimental.pallas import tpu as pltpu
from jax.sharding import PartitionSpec as P

HEAD = 64


EPS = 1e-05
NEG = -1e30


def lower(values_in):
    return values_in.astype(jnp.bfloat16)


def product(left_side, right_side, transposed):
    if transposed:
        return lax.dot_general(
            left_side, right_side, (((1,), (1,)), ((), ())), preferred_element_type=jnp.float32
        )
    return jnp.dot(left_side, right_side, preferred_element_type=jnp.float32)


def outer_sum(left_side, right_side):
    return lax.dot_general(
        left_side, right_side, (((0,), (0,)), ((), ())), preferred_element_type=jnp.float32
    )


def normalize(values_in, gain_row, bias_row):
    row_mean = jnp.mean(values_in, axis=-1, keepdims=True)
    centered = values_in - row_mean
    inverse = lax.rsqrt(jnp.mean(centered * centered, axis=-1, keepdims=True) + EPS)
    scaled = centered * inverse
    return (scaled * gain_row + bias_row, scaled, inverse)


def normalize_back(upstream, scaled, inverse, gain_row):
    weighted = upstream * gain_row
    inner_mean = jnp.mean(weighted, axis=-1, keepdims=True)
    along_mean = jnp.mean(weighted * scaled, axis=-1, keepdims=True)
    grad_input = inverse * (weighted - inner_mean - scaled * along_mean)
    return (grad_input, jnp.sum(upstream * scaled, axis=0), jnp.sum(upstream, axis=0))


def gelu_parts(values_in):
    normal_cdf = 0.5 * (1.0 + jax.scipy.special.erf(values_in * 0.7071067811865476))
    normal_pdf = jnp.exp(-0.5 * values_in * values_in) * 0.3989422804014327
    return (values_in * normal_cdf, normal_cdf + values_in * normal_pdf)


def scores_of(query_part, key_part, valid):
    scores = jnp.einsum(
        "bhe,khe->hbk", query_part, key_part, preferred_element_type=jnp.float32
    ) * HEAD ** (-0.5)
    return jnp.where(valid, scores, NEG)


def attend(query_part, key_part, value_part, valid):
    scores = scores_of(query_part, key_part, valid)
    row_top = jnp.max(scores, axis=-1, keepdims=True)
    weights_exp = jnp.exp(scores - row_top)
    denominator = jnp.sum(weights_exp, axis=-1, keepdims=True)
    probability = weights_exp / denominator
    mixed = jnp.einsum(
        "hbk,khe->bhe", lower(probability), value_part, preferred_element_type=jnp.float32
    )
    return (lower(mixed), (row_top + jnp.log(denominator))[..., 0])


def attend_back(query_part, key_part, value_part, valid, summary, upstream):
    scores = scores_of(query_part, key_part, valid)
    probability = jnp.exp(scores - summary[..., None])
    pressure = jnp.einsum("bhe,khe->hbk", upstream, value_part, preferred_element_type=jnp.float32)
    grad_scores = lower(
        probability * (pressure - jnp.sum(probability * pressure, axis=-1, keepdims=True))
    )
    factor = HEAD ** (-0.5)
    grad_query = (
        jnp.einsum("hbk,khe->bhe", grad_scores, key_part, preferred_element_type=jnp.float32)
        * factor
    )
    grad_key = (
        jnp.einsum("hbk,bhe->khe", grad_scores, query_part, preferred_element_type=jnp.float32)
        * factor
    )
    grad_value = jnp.einsum(
        "hbk,bhe->khe", lower(probability), upstream, preferred_element_type=jnp.float32
    )
    return (grad_query, grad_key, grad_value)


def general_local(
    frames,
    text_states,
    lengths,
    loss_mask,
    norm_gain,
    norm_bias,
    w_qkv,
    w_out,
    w_cross_q,
    w_cross_kv,
    w_cross_out,
    w_up,
    w_down,
    cotangent,
):
    row_count = frames.shape[0]
    width = frames.shape[1]
    item_count = lengths.shape[0]
    span = row_count * lax.axis_size("narrow") // item_count
    half_span = span // 2
    inner_width = w_qkv.shape[2]
    head_count = inner_width // HEAD
    text_count = text_states.shape[1]
    full_rows = item_count * span
    places = jnp.arange(span, dtype=jnp.int32)

    def spread(shard_rows):
        return lax.all_gather(shard_rows, "narrow", axis=0, tiled=True)

    def collect(left_side, right_side, transposed):
        return lax.psum_scatter(
            product(
                lax.slice_in_dim(left_side, 0, lax.axis_size("narrow") * row_count, axis=0),
                right_side,
                transposed,
            ),
            "narrow",
            scatter_dimension=0,
            tiled=True,
        )

    def causal(block_index, item_limit):
        query_place = block_index * half_span + jnp.arange(half_span, dtype=jnp.int32)
        return (places[None, :] <= query_place[:, None]) & (places[None, :] < item_limit)

    frame_rows = frames.astype(jnp.float32)
    normed_one, scaled_one, inverse_one = normalize(frame_rows, norm_gain[0], norm_bias[0])
    first_input = spread(lower(normed_one))
    triple = lower(
        jnp.einsum("rd,cde->cre", first_input, w_qkv, preferred_element_type=jnp.float32)
    )
    triple = triple.reshape(3, item_count, span, head_count, HEAD)

    def self_item(packed):
        query_part, key_part, value_part, item_limit = packed
        mixed_list = []
        summary_list = []
        for block_index in range(2):
            mixed, summary = attend(
                query_part[block_index * half_span : (block_index + 1) * half_span],
                key_part,
                value_part,
                causal(block_index, item_limit),
            )
            mixed_list.append(mixed)
            summary_list.append(summary)
        return (jnp.concatenate(mixed_list, axis=0), jnp.stack(summary_list, axis=0))

    attended, self_summary = lax.map(self_item, (triple[0], triple[1], triple[2], lengths))
    attended_flat = attended.reshape(full_rows, inner_width)
    first_rows = frame_rows + collect(attended_flat, w_out, False)
    normed_two, scaled_two, inverse_two = normalize(first_rows, norm_gain[1], norm_bias[1])
    second_input = spread(lower(normed_two))
    cross_query = lower(product(second_input, w_cross_q, False)).reshape(
        item_count, span, head_count, HEAD
    )
    cross_pair = lower(
        jnp.einsum("ntd,cde->cnte", text_states, w_cross_kv, preferred_element_type=jnp.float32)
    )
    cross_pair = cross_pair.reshape(2, item_count, text_count, head_count, HEAD)

    def cross_item(packed):
        query_part, key_part, value_part = packed
        return attend(query_part, key_part, value_part, True)

    cross_mixed, cross_summary = lax.map(cross_item, (cross_query, cross_pair[0], cross_pair[1]))
    cross_flat = cross_mixed.reshape(full_rows, inner_width)
    second_rows = first_rows + collect(cross_flat, w_cross_out, False)
    normed_three, scaled_three, inverse_three = normalize(second_rows, norm_gain[2], norm_bias[2])
    upstream = cotangent.astype(jnp.float32) * loss_mask.astype(jnp.float32)[:, None]
    ffn_grad = lower(upstream)
    ffn_input = spread(lower(normed_three))
    hidden_pre = product(ffn_input, w_up, False)
    active, slope = gelu_parts(hidden_pre)
    active = lower(active)
    out_rows = second_rows + collect(active, w_down, False)
    ffn_full = spread(ffn_grad)
    grad_down = outer_sum(active, ffn_full)
    grad_hidden = lower(product(ffn_full, w_down, True) * slope)
    grad_up = outer_sum(ffn_input, grad_hidden)
    back_three = collect(grad_hidden, w_up, True)
    grad_up, grad_down = (grad_up, grad_down)
    grad_in_three, gain_three, bias_three = normalize_back(
        back_three, scaled_three, inverse_three, norm_gain[2]
    )
    grad_second = upstream + grad_in_three
    cross_full = spread(lower(grad_second))
    grad_cross_out = outer_sum(cross_flat, cross_full)
    cross_upstream = lower(product(cross_full, w_cross_out, True)).reshape(
        item_count, span, head_count, HEAD
    )

    def cross_back(packed):
        query_part, key_part, value_part, summary, upstream_item = packed
        return attend_back(query_part, key_part, value_part, True, summary, upstream_item)

    grad_cq, grad_ck, grad_cv = lax.map(
        cross_back, (cross_query, cross_pair[0], cross_pair[1], cross_summary, cross_upstream)
    )
    grad_cq = lower(grad_cq).reshape(full_rows, inner_width)
    grad_pair = lower(jnp.stack((grad_ck, grad_cv), axis=0)).reshape(
        2, item_count, text_count, inner_width
    )
    grad_cross_q = outer_sum(second_input, grad_cq)
    grad_cross_kv = jnp.einsum(
        "ntd,cnte->cde", text_states, grad_pair, preferred_element_type=jnp.float32
    )
    grad_cross_q, grad_cross_kv, grad_cross_out = (grad_cross_q, grad_cross_kv, grad_cross_out)
    text_partial = jnp.einsum(
        "cnte,cde->ntd", grad_pair, w_cross_kv, preferred_element_type=jnp.float32
    )
    grad_text = lower(lax.psum(text_partial, "narrow"))
    back_two = collect(grad_cq, w_cross_q, True)
    grad_in_two, gain_two, bias_two = normalize_back(
        back_two, scaled_two, inverse_two, norm_gain[1]
    )
    grad_first = grad_second + grad_in_two
    self_full = spread(lower(grad_first))
    grad_out = outer_sum(attended_flat, self_full)
    self_upstream = lower(product(self_full, w_out, True)).reshape(
        item_count, span, head_count, HEAD
    )

    def self_back(packed):
        query_part, key_part, value_part, item_limit, summary, upstream_item = packed
        query_list = []
        key_list = []
        value_list = []
        for block_index in range(2):
            lower_row = block_index * half_span
            grad_query, grad_key, grad_value = attend_back(
                query_part[lower_row : lower_row + half_span],
                key_part,
                value_part,
                causal(block_index, item_limit),
                summary[block_index],
                upstream_item[lower_row : lower_row + half_span],
            )
            query_list.append(grad_query)
            key_list.append(grad_key)
            value_list.append(grad_value)
        return (
            jnp.concatenate(query_list, axis=0),
            key_list[0] + key_list[1],
            value_list[0] + value_list[1],
        )

    grad_q, grad_k, grad_v = lax.map(
        self_back, (triple[0], triple[1], triple[2], lengths, self_summary, self_upstream)
    )
    grad_triple = lower(jnp.stack((grad_q, grad_k, grad_v), axis=0)).reshape(
        3, full_rows, inner_width
    )
    grad_qkv = jnp.einsum(
        "rd,cre->cde", first_input, grad_triple, preferred_element_type=jnp.float32
    )
    grad_qkv, grad_out = (grad_qkv, grad_out)
    merged = grad_triple.transpose(1, 0, 2).reshape(full_rows, 3 * inner_width)
    stacked_weights = w_qkv.transpose(0, 2, 1).reshape(3 * inner_width, width)
    back_one = collect(merged, stacked_weights, False)
    grad_in_one, gain_one, bias_one = normalize_back(
        back_one, scaled_one, inverse_one, norm_gain[0]
    )
    grad_frames = lower(grad_first + grad_in_one)
    gain_terms = jnp.stack((gain_one, gain_two, gain_three), axis=0)
    bias_terms = jnp.stack((bias_one, bias_two, bias_three), axis=0)
    grad_norm_gain, grad_norm_bias = lax.psum((gain_terms, bias_terms), ("wide", "narrow"))
    grad_qkv, grad_out, grad_cross_q, grad_cross_kv, grad_cross_out, grad_up, grad_down = lax.psum(
        (grad_qkv, grad_out, grad_cross_q, grad_cross_kv, grad_cross_out, grad_up, grad_down),
        "wide",
    )
    return (
        lower(out_rows),
        grad_frames,
        grad_text,
        grad_norm_gain,
        grad_norm_bias,
        grad_qkv,
        grad_out,
        grad_cross_q,
        grad_cross_kv,
        grad_cross_out,
        grad_up,
        grad_down,
    )


ROUND = jnp.bfloat16
FULL = jnp.float32
CORE_PAIRS = ((0, 1), (1, 0), (2, 3), (3, 2))
Y_PAIRS = ((0, 2), (2, 0), (1, 3), (3, 1))
X_PAIRS = tuple((i, i ^ 1) for i in range(8))
Z_INWARD = ((0, 2), (1, 3), (6, 4), (7, 5))
Z_MIDDLE = ((2, 4), (4, 2), (3, 5), (5, 3))
Z_OUTWARD = ((2, 0), (3, 1), (4, 6), (5, 7))
Z_NEAR = tuple((i, i ^ 2) for i in range(8))
Z_FAR = tuple((i, i ^ 4) for i in range(8))
MIB = 1 << 20


def nt(a, b):
    return lax.dot_general(a, b, (((1,), (1,)), ((), ())), preferred_element_type=FULL)


def nn(a, b):
    return lax.dot_general(a, b, (((1,), (0,)), ((), ())), preferred_element_type=FULL)


def tn(a, b):
    return lax.dot_general(a, b, (((0,), (0,)), ((), ())), preferred_element_type=FULL)


def shape(dims, kind):
    return jax.ShapeDtypeStruct(dims, kind)


def resident(dims):
    zeros = (0,) * len(dims)
    return pl.BlockSpec(dims, lambda i, s: zeros, pipeline_mode=pl.Buffered(1))


def rows_of(block, width):
    return pl.BlockSpec((block, width), lambda i, s: (i, 0))


def cost(flops, moved):
    return pl.CostEstimate(flops=int(flops), bytes_accessed=int(moved), transcendentals=0)


def params(mib):
    return pltpu.CompilerParams(vmem_limit_bytes=mib * MIB)


def norm_parts(v):
    centered = v - jnp.mean(v, axis=-1, keepdims=True)
    inverse = lax.rsqrt(jnp.mean(centered * centered, axis=-1, keepdims=True) + EPS)
    return centered * inverse, inverse


def norm_pull(y, scaled, inverse, gain_row):
    weighted = y * gain_row
    inner = jnp.mean(weighted, axis=-1, keepdims=True)
    along = jnp.mean(weighted * scaled, axis=-1, keepdims=True)
    return inverse * (weighted - inner - scaled * along)


def project_kernel(where_ref, mine_ref, other_ref, weight_ref, *out_refs, transposed, count):
    half = pl.program_id(0)

    def run(source):
        for c in range(count):
            if transposed:
                result = nt(source[...], weight_ref[c])
            else:
                result = nn(source[...], weight_ref[c])
            out_refs[c][...] = lower(result)

    @pl.when(half == 0)
    def _():
        run(mine_ref)

    @pl.when(half == 1)
    def _():
        run(other_ref)


def project(where, mine, other, weights, transposed):
    rows, depth = mine.shape
    count = weights.shape[0]
    wide = weights.shape[1] if transposed else weights.shape[2]
    whole = pl.BlockSpec((rows, depth), lambda i, s: (0, 0), pipeline_mode=pl.Buffered(1))
    out = pl.BlockSpec((rows, wide), lambda i, s: ((i + s[0]) % 2, 0))
    return pl.pallas_call(
        functools.partial(project_kernel, transposed=transposed, count=count),
        grid_spec=pltpu.PrefetchScalarGridSpec(
            num_scalar_prefetch=1,
            grid=(2,),
            in_specs=[whole, whole, resident(weights.shape)],
            out_specs=[out] * count,
        ),
        out_shape=[shape((2 * rows, wide), ROUND)] * count,
        compiler_params=params(32),
        cost_estimate=cost(4 * rows * depth * wide * count, 8e6),
        name="project",
    )(where, mine, other, weights)


def blocks_of(span, block):
    return [(start, min(block, span - start)) for start in range(0, span, block)]


def self_forward_kernel(limit_ref, q_ref, k_ref, v_ref, o_ref, lse_ref, *, span, floor, block):
    limit = limit_ref[0]
    lane = lax.broadcasted_iota(jnp.int32, (1, 128), 1)
    zero = jnp.zeros((), ROUND)
    for start, size in blocks_of(span, block):
        end = start + size
        mixed_list = []
        for h in range(2):
            own_lanes = (lane < HEAD) if h == 0 else (lane >= HEAD)
            query = jnp.where(own_lanes, q_ref[start:end, :] * HEAD ** (-0.5), zero)
            cuts = [(0, start)] if start <= floor else [(0, floor), (floor, start)]
            parts = []
            for low, high in cuts + [(start, end)]:
                if low == high:
                    continue
                scores = nt(query, k_ref[low:high, :])
                key = lax.broadcasted_iota(jnp.int32, (size, high - low), 1)
                if low == start:
                    valid = key <= lax.broadcasted_iota(jnp.int32, (size, high - low), 0)
                    if high > floor:
                        valid = valid & (key + low < limit)
                    scores = jnp.where(valid, scores, NEG)
                elif high > floor:
                    scores = jnp.where(key + low < limit, scores, NEG)
                parts.append((low, high, scores))
            top = functools.reduce(
                jnp.maximum, [jnp.max(s, axis=1, keepdims=True) for _, _, s in parts]
            )
            total = 0.0
            mixed = 0.0
            for low, high, scores in parts:
                weights_exp = jnp.exp(scores - top)
                total = total + jnp.sum(weights_exp, axis=1, keepdims=True)
                mixed = mixed + nn(lower(weights_exp), v_ref[low:high, :])
            mixed_list.append(mixed / total)
            summary = jnp.broadcast_to(top + jnp.log(total), (size, 128))
            lse_ref[0, h : h + 1, start:end] = summary.T[0:1, :]
        o_ref[start:end, :] = lower(jnp.where(lane < HEAD, mixed_list[0], mixed_list[1]))


def self_forward(limit, q, k, v):
    span, wide = q.shape
    pairs = wide // 128
    floor = (span - span // 8 + 1) // 128 * 128
    pair = pl.BlockSpec((span, 128), lambda p, s: (0, p))
    return pl.pallas_call(
        functools.partial(self_forward_kernel, span=span, floor=floor, block=256),
        grid_spec=pltpu.PrefetchScalarGridSpec(
            num_scalar_prefetch=1,
            grid=(pairs,),
            in_specs=[pair] * 3,
            out_specs=[pair, pl.BlockSpec((1, 8, span), lambda p, s: (p, 0, 0))],
        ),
        out_shape=[shape((span, wide), ROUND), shape((pairs, 8, span), FULL)],
        compiler_params=params(40),
        cost_estimate=cost(16e9, 4e6),
        name="self_forward",
    )(limit, q, k, v)


def self_back_kernel(
    limit_ref, q_ref, k_ref, v_ref, o_ref, do_ref, lse_ref, dq_ref, dk_ref, dv_ref, dqt,
    *, span, floor, block
):
    limit = limit_ref[0]
    lane = lax.broadcasted_iota(jnp.int32, (1, 128), 1)
    row = lax.broadcasted_iota(jnp.int32, (128, 1), 0)
    zero = jnp.zeros((), ROUND)
    factor = HEAD ** (-0.5)
    product_rows = do_ref[...].astype(FULL) * o_ref[...].astype(FULL)
    high = lower(product_rows)
    rest = lower(product_rows - high.astype(FULL))
    pick = lower(
        jnp.concatenate(
            [
                jnp.where(lane < HEAD, 1.0, 0.0),
                jnp.where(lane >= HEAD, 1.0, 0.0),
                jnp.zeros((6, 128), FULL),
            ],
            axis=0,
        )
    )
    delta = nt(pick, high) + nt(pick, rest)
    for start, size in blocks_of(span, block):
        end = start + size
        key = k_ref[start:end, :]
        value = v_ref[start:end, :]
        key_turned = key.T
        dk = 0.0
        dv = 0.0
        dq_add = 0.0
        for h in range(2):
            own_lanes = (lane < HEAD) if h == 0 else (lane >= HEAD)
            own_rows = (row < HEAD) if h == 0 else (row >= HEAD)
            query = jnp.where(own_lanes, q_ref[start:, :] * factor, zero)
            pulled = jnp.where(own_lanes, do_ref[start:, :], zero)
            probability = jnp.exp(nt(key, query) - lse_ref[0, h : h + 1, start:])
            pressure = nt(value, pulled)
            below = lax.broadcasted_iota(jnp.int32, (size, size), 0)
            across = lax.broadcasted_iota(jnp.int32, (size, size), 1)
            corner = jnp.where(below <= across, probability[:, :size], 0.0)
            if end < span:
                probability = jnp.concatenate([corner, probability[:, size:]], axis=1)
            else:
                probability = corner
            if end > floor:
                place = lax.broadcasted_iota(jnp.int32, (size, 1), 0) + start
                probability = jnp.where(place < limit, probability, 0.0)
            grad_scores = lower(probability * (pressure - delta[h : h + 1, start:]))
            dv = dv + nn(lower(probability), pulled)
            dk = dk + nn(grad_scores, query)
            dq_add = dq_add + nn(jnp.where(own_rows, key_turned, zero), grad_scores)
        dk_ref[start:end, :] = lower(dk)
        dv_ref[start:end, :] = lower(dv)
        if start == 0:
            dqt[...] = dq_add
        else:
            dqt[:, start:] += dq_add
    dq_ref[...] = lower(dqt[...].T * factor)


def self_back(limit, q, k, v, o, do, lse):
    span, wide = q.shape
    pairs = wide // 128
    floor = (span - span // 8 + 1) // 128 * 128
    pair = pl.BlockSpec((span, 128), lambda p, s: (0, p))
    return pl.pallas_call(
        functools.partial(self_back_kernel, span=span, floor=floor, block=256),
        grid_spec=pltpu.PrefetchScalarGridSpec(
            num_scalar_prefetch=1,
            grid=(pairs,),
            in_specs=[pair] * 5 + [pl.BlockSpec((1, 8, span), lambda p, s: (p, 0, 0))],
            out_specs=[pair] * 3,
            scratch_shapes=[pltpu.VMEM((128, span), FULL)],
        ),
        out_shape=[shape((span, wide), ROUND)] * 3,
        compiler_params=params(48),
        cost_estimate=cost(20e9, 6e6),
        name="self_back",
    )(limit, q, k, v, o, do, lse)


def by_head(values_in, reduce, empty):
    lane = lax.broadcasted_iota(jnp.int32, (1, 128), 1)
    pieces = []
    for start in range(0, values_in.shape[1], 128):
        part = values_in[:, start : start + 128]
        first = reduce(jnp.where(lane < HEAD, part, empty), axis=1, keepdims=True)
        second = reduce(jnp.where(lane >= HEAD, part, empty), axis=1, keepdims=True)
        pieces.append(jnp.where(lane < HEAD, first, second))
    return jnp.concatenate(pieces, axis=1)


def cross_probability(query, keys):
    scores = nt(query * HEAD ** (-0.5), keys)
    weights_exp = jnp.exp(scores - by_head(scores, jnp.max, NEG))
    return weights_exp / by_head(weights_exp, jnp.sum, 0.0)


def middle_forward_kernel(
    where_ref, frame_ref, a0_ref, a1_ref, a2_ref, a3_ref, gain_ref, bias_ref, wo0_ref, wo1_ref,
    wq0_ref, wq1_ref, ck0_ref, ck1_ref, cv0_ref, cv1_ref, wc0_ref, wc1_ref,
    x1_ref, x2_ref, h2_ref, cq_ref, ca_ref, h3_ref
):
    mixed = (a0_ref, a1_ref, a2_ref, a3_ref)
    x1 = frame_ref[...].astype(FULL)
    for g in range(4):
        part = (wo0_ref, wo1_ref)[g // 2][(g % 2) * 256 : (g % 2 + 1) * 256, :]
        x1 = x1 + nn(mixed[g][...], part)
    x1_ref[...] = x1
    scaled, _ = norm_parts(x1)
    h2 = lower(scaled * gain_ref[1:2, :] + bias_ref[1:2, :])
    h2_ref[...] = h2
    for g in range(4):
        lanes = slice(g * 256, (g + 1) * 256)
        cq = lower(nn(h2, (wq0_ref, wq1_ref)[g // 2][g % 2]))
        cq_ref[:, lanes] = cq
        probability = cross_probability(cq, (ck0_ref, ck1_ref)[g // 2][g % 2])
        ca_ref[:, lanes] = lower(nn(lower(probability), (cv0_ref, cv1_ref)[g // 2][g % 2]))
    crossed = nn(ca_ref[:, :512], wc0_ref[...]) + nn(ca_ref[:, 512:], wc1_ref[...])
    x2 = x1_ref[...] + crossed
    x2_ref[...] = x2
    scaled, _ = norm_parts(x2)
    h3_ref[...] = lower(scaled * gain_ref[2:3, :] + bias_ref[2:3, :])


def middle_forward(where, frames, attended, received, gains, biases, wo, wq, ck, cv, wc):
    rows, width = frames.shape
    block = 208
    steps = rows // block
    piece = pl.BlockSpec((block, 256), lambda i, s: (s[0] * steps + i, 0))
    wide = rows_of(block, width)
    return pl.pallas_call(
        middle_forward_kernel,
        grid_spec=pltpu.PrefetchScalarGridSpec(
            num_scalar_prefetch=1,
            grid=(steps,),
            in_specs=[wide, piece, piece, rows_of(block, 256), rows_of(block, 256)]
            + [resident(a.shape) for a in (gains, biases, *wo, *wq, *ck, *cv, *wc)],
            out_specs=[wide] * 6,
        ),
        out_shape=[shape((rows, width), FULL)] * 2 + [shape((rows, width), ROUND)] * 4,
        compiler_params=params(40),
        cost_estimate=cost(7e9, 25e6),
        name="middle_forward",
    )(where, frames, *attended, *received, gains, biases, *wo, *wq, *ck, *cv, *wc)


def feed_kernel(
    where_ref, h_ref, d_ref, up0_ref, up1_ref, down0_ref, down1_ref,
    g0_ref, g1_ref, du0_ref, du1_ref, out_ref, y_ref
):
    h = h_ref[...]
    d = d_ref[...]
    out = 0.0
    y = 0.0
    for up, down, g_ref, du_ref in (
        (up0_ref, down0_ref, g0_ref, du0_ref),
        (up1_ref, down1_ref, g1_ref, du1_ref),
    ):
        u = nn(h, up[...])
        active, slope = gelu_parts(u)
        g = lower(active)
        g_ref[...] = g
        du = lower(nt(d, down[...]) * slope)
        du_ref[...] = du
        out = out + nn(g, down[...])
        y = y + nt(du, up[...])
    out_ref[...] = out.astype(out_ref.dtype)
    y_ref[...] = y.astype(y_ref.dtype)


def feed(where, h, d, up, down, kind):
    rows, width = h.shape
    block = 208
    hidden = up[0].shape[1]
    wide = rows_of(block, width)
    return pl.pallas_call(
        feed_kernel,
        grid_spec=pltpu.PrefetchScalarGridSpec(
            num_scalar_prefetch=1,
            grid=(rows // block,),
            in_specs=[wide, wide] + [resident(a.shape) for a in (*up, *down)],
            out_specs=[rows_of(block, hidden)] * 4 + [wide] * 2,
        ),
        out_shape=[shape((rows, hidden), ROUND)] * 4 + [shape((rows, width), kind)] * 2,
        compiler_params=params(48),
        cost_estimate=cost(16 * rows * width * hidden, 30e6),
        name="feed",
    )(where, h, d, *up, *down)


def middle_back_kernel(
    where_ref, ym_ref, yr_ref, x1_ref, x2_ref, d_ref, cq_ref, gain_ref,
    wq0_ref, wq1_ref, ck0_ref, ck1_ref, cv0_ref, cv1_ref, wc0_ref, wc1_ref,
    dx1_ref, dself_ref, dcross_ref, dcq_ref, dck_ref, dcv_ref, sums_ref, dck_all, dcv_all
):
    step = pl.program_id(0)

    @pl.when(step == 0)
    def _():
        dck_all[...] = jnp.zeros_like(dck_all)
        dcv_all[...] = jnp.zeros_like(dcv_all)
        sums_ref[...] = jnp.zeros_like(sums_ref)

    y3 = ym_ref[...] + yr_ref[...].astype(FULL)
    scaled, inverse = norm_parts(x2_ref[...])
    sums_ref[4:5, :] += jnp.sum(y3 * scaled, axis=0, keepdims=True)
    sums_ref[5:6, :] += jnp.sum(y3, axis=0, keepdims=True)
    dx2 = d_ref[...].astype(FULL) + norm_pull(y3, scaled, inverse, gain_ref[2:3, :])
    dx1_ref[...] = dx2
    dcross = lower(dx2)
    dcross_ref[...] = dcross
    y2 = 0.0
    for g in range(4):
        lanes = slice(g * 256, (g + 1) * 256)
        part = (wc0_ref, wc1_ref)[g // 2][(g % 2) * 256 : (g % 2 + 1) * 256, :]
        keys = (ck0_ref, ck1_ref)[g // 2][g % 2]
        values = (cv0_ref, cv1_ref)[g // 2][g % 2]
        dcatt = lower(nt(dcross, part))
        cq = cq_ref[:, lanes]
        probability = cross_probability(cq, keys)
        weighed = nt(dcatt, values)
        inner = by_head(probability * weighed, jnp.sum, 0.0)
        dcs = lower(probability * (weighed - inner))
        dcq = lower(nn(dcs, keys) * HEAD ** (-0.5))
        dcq_ref[:, lanes] = dcq
        dck_all[g] += tn(dcs, cq * HEAD ** (-0.5))
        dcv_all[g] += tn(lower(probability), dcatt)
        y2 = y2 + nt(dcq, (wq0_ref, wq1_ref)[g // 2][g % 2])
    scaled, inverse = norm_parts(x1_ref[...])
    sums_ref[2:3, :] += jnp.sum(y2 * scaled, axis=0, keepdims=True)
    sums_ref[3:4, :] += jnp.sum(y2, axis=0, keepdims=True)
    dx1 = dx1_ref[...] + norm_pull(y2, scaled, inverse, gain_ref[1:2, :])
    dx1_ref[...] = dx1
    dself_ref[...] = lower(dx1)

    @pl.when(step == pl.num_programs(0) - 1)
    def _():
        for every, result in ((dck_all, dck_ref), (dcv_all, dcv_ref)):
            for g in range(4):
                total = 0.0
                for h in range(4):
                    lane = lax.broadcasted_iota(jnp.int32, (1, 256), 1) // HEAD
                    total = total + jnp.where(lane == h, every[g, h * 64 : (h + 1) * 64, :], 0.0)
                result[g] = total


def middle_back(where, ym, yr, x1, x2, d, cq, gains, wq, ck, cv, wc):
    rows, width = x1.shape
    block = 208
    wide = rows_of(block, width)
    small = pl.BlockSpec((4, 64, 256), lambda i, s: (0, 0, 0))
    return pl.pallas_call(
        middle_back_kernel,
        grid_spec=pltpu.PrefetchScalarGridSpec(
            num_scalar_prefetch=1,
            grid=(rows // block,),
            in_specs=[wide] * 6 + [resident(a.shape) for a in (gains, *wq, *ck, *cv, *wc)],
            out_specs=[wide] * 4 + [small, small, pl.BlockSpec((8, width), lambda i, s: (0, 0))],
            scratch_shapes=[pltpu.VMEM((4, 256, 256), FULL)] * 2,
        ),
        out_shape=[shape((rows, width), FULL)]
        + [shape((rows, width), ROUND)] * 3
        + [shape((4, 64, 256), FULL)] * 2
        + [shape((8, width), FULL)],
        compiler_params=params(40),
        cost_estimate=cost(7e9, 25e6),
        name="middle_back",
    )(where, ym, yr, x1, x2, d, cq, gains, *wq, *ck, *cv, *wc)


def first_back_kernel(where_ref, *refs):
    grads = refs[:6]
    w0_ref, w1_ref, y_ref = refs[6:]
    y = 0.0
    for g in range(2):
        for c in range(3):
            y = y + nt(grads[3 * g + c][...], (w0_ref, w1_ref)[g][c])
    y_ref[...] = y.astype(y_ref.dtype)


def first_back(half, grads, weights, kind):
    span = grads[0].shape[0]
    rows = span // 2
    width = weights[0].shape[1]
    block = 208
    steps = rows // block
    piece = pl.BlockSpec((block, 256), lambda i, s: (s[0] * steps + i, 0))
    return pl.pallas_call(
        first_back_kernel,
        grid_spec=pltpu.PrefetchScalarGridSpec(
            num_scalar_prefetch=1,
            grid=(steps,),
            in_specs=[piece] * 6 + [resident(a.shape) for a in weights],
            out_specs=rows_of(block, width),
        ),
        out_shape=shape((rows, width), kind),
        compiler_params=params(24),
        cost_estimate=cost(2 * rows * width * 1536, 8e6),
        name="first_back",
    )(half, *grads, *weights)


def frames_back_kernel(where_ref, ym_ref, yr_ref, dx1_ref, frame_ref, gain_ref, out_ref, sums_ref):
    @pl.when(pl.program_id(0) == 0)
    def _():
        sums_ref[...] = jnp.zeros_like(sums_ref)

    y = ym_ref[...] + yr_ref[...].astype(FULL)
    scaled, inverse = norm_parts(frame_ref[...].astype(FULL))
    sums_ref[0:1, :] += jnp.sum(y * scaled, axis=0, keepdims=True)
    sums_ref[1:2, :] += jnp.sum(y, axis=0, keepdims=True)
    out_ref[...] = lower(dx1_ref[...] + norm_pull(y, scaled, inverse, gain_ref[0:1, :]))


def frames_back(where, ym, yr, dx1, frames, gains):
    rows, width = dx1.shape
    block = 208
    wide = rows_of(block, width)
    return pl.pallas_call(
        frames_back_kernel,
        grid_spec=pltpu.PrefetchScalarGridSpec(
            num_scalar_prefetch=1,
            grid=(rows // block,),
            in_specs=[wide] * 4 + [resident(gains.shape)],
            out_specs=[wide, pl.BlockSpec((8, width), lambda i, s: (0, 0))],
        ),
        out_shape=[shape((rows, width), ROUND), shape((8, width), FULL)],
        compiler_params=params(24),
        cost_estimate=cost(1e7, 12e6),
        name="frames_back",
    )(where, ym, yr, dx1, frames, gains)


def chip_local(
    frames, text_states, lengths, loss_mask, norm_gain, norm_bias, w_qkv, w_out, w_cross_q,
    w_cross_kv, w_cross_out, w_up, w_down, cotangent,
):
    at = lax.axis_index("narrow")
    core = at % 2
    side = at // 2
    layer = lax.axis_index("wide") // 2
    where = core.reshape(1).astype(jnp.int32)
    away = (1 - core).reshape(1).astype(jnp.int32)
    limit = lax.dynamic_slice(lengths, (side,), (1,))

    def over_core(v):
        return lax.ppermute(v, "narrow", CORE_PAIRS)

    def over_y(v):
        return lax.ppermute(v, "narrow", Y_PAIRS)

    def along_wide(v, pairs):
        return lax.ppermute(v, "wide", pairs)

    def in_order(mine, other):
        return jnp.where(
            core == 0,
            jnp.concatenate([mine, other], axis=0),
            jnp.concatenate([other, mine], axis=0),
        )

    def over_chips(partial):
        def plus(a, b):
            return lower(a.astype(FULL) + b.astype(FULL))

        total = plus(partial, along_wide(partial, X_PAIRS))
        total = plus(total, along_wide(total, Z_INWARD))
        total = plus(total, along_wide(total, Z_MIDDLE))
        outer = along_wide(total, Z_OUTWARD)
        return jnp.where((layer == 1) | (layer == 2), total, outer).astype(FULL)

    def reduced(own, partner):
        return over_chips(lower(own + over_y(lower(partner)).astype(FULL)))

    qkv_y = over_y(w_qkv)
    out_y = over_y(w_out)
    cross_q_y = over_y(w_cross_q)
    cross_kv_y = over_y(w_cross_kv)
    cross_out_y = over_y(w_cross_out)
    up_y = over_y(w_up)
    down_y = over_y(w_down)

    scaled, _ = norm_parts(frames.astype(FULL))
    h1 = lower(scaled * norm_gain[0] + norm_bias[0])
    h1_other = over_core(h1)
    dout = jnp.where(loss_mask[:, None] != 0, cotangent, jnp.zeros((), ROUND))
    dout_other = over_core(dout)

    q0, k0, v0 = project(where, h1, h1_other, w_qkv, False)
    o0, lse0 = self_forward(limit, q0, k0, v0)
    q1, k1, v1 = project(where, h1, h1_other, qkv_y, False)
    o1, lse1 = self_forward(limit, q1, k1, v1)
    rows = frames.shape[0]

    def away_rows(v):
        return lax.dynamic_slice(v, ((1 - core) * rows, 0), (rows, v.shape[1]))

    o0_other = over_core(away_rows(o0))
    o1_other = over_core(away_rows(o1))

    wo = jnp.concatenate([w_out, out_y], axis=0)
    wo = (wo, over_core(wo))
    wq = jnp.stack([w_cross_q, cross_q_y], axis=0)
    wq = (wq, over_core(wq))
    wc = jnp.concatenate([w_cross_out, cross_out_y], axis=0)
    wc = (wc, over_core(wc))
    text = lax.dynamic_slice(text_states, (side, 0, 0), (1, *text_states.shape[1:]))[0]
    pair = lower(
        jnp.einsum(
            "td,gcde->gcte", text, jnp.stack([w_cross_kv, cross_kv_y]), preferred_element_type=FULL
        )
    )
    pair_other = over_core(pair)
    head_of = jnp.arange(256) // HEAD
    same = head_of[:, None] == head_of[None, :]

    def spread_heads(v):
        return jnp.where(same, jnp.tile(v, (1, 4, 1)), jnp.zeros((), ROUND))

    ck = (spread_heads(pair[:, 0]), spread_heads(pair_other[:, 0]))
    cv = (spread_heads(pair[:, 1]), spread_heads(pair_other[:, 1]))

    x1, x2, h2, cq, ca, h3 = middle_forward(
        where, frames, (o0, o1), (o0_other, o1_other), norm_gain, norm_bias, wo, wq, ck, cv, wc
    )
    h3_other = over_core(h3)
    h2_other = over_core(h2)
    ca_other = over_core(ca[:, 512:])

    up = (w_up, up_y)
    down = (w_down, down_y)
    g0m, g1m, du0m, du1m, outm, ym = feed(where, h3, dout, up, down, FULL)
    g0o, g1o, du0o, du1o, outo, yo = feed(where, h3_other, dout_other, up, down, ROUND)
    y_received = over_core(yo)
    out_received = over_core(outo)

    def rows_sum(left_mine, right_mine, left_other, right_other):
        return tn(left_mine, right_mine) + tn(left_other, right_other)

    grad_up = reduced(
        rows_sum(h3, du0m, h3_other, du0o), rows_sum(h3, du1m, h3_other, du1o)
    )
    grad_down = reduced(
        rows_sum(g0m, dout, g0o, dout_other), rows_sum(g1m, dout, g1o, dout_other)
    )

    dx1, dself, dcross, dcq, dck, dcv, sums = middle_back(
        where, ym, y_received, x1, x2, dout, cq, norm_gain, wq, ck, cv, wc
    )
    out_rows = lower(x2 + outm + out_received.astype(FULL))
    dself_other = over_core(dself)
    dcross_other = over_core(dcross)
    dcq_other = over_core(dcq[:, 512:])
    d_pair = jnp.stack([dck, dcv], axis=1)
    d_pair = lower(d_pair[:2] + over_core(d_pair[2:]))

    do0, do1 = project(where, dself, dself_other, jnp.stack([w_out, out_y]), True)
    dself_rows = in_order(dself, dself_other)
    h1_rows = in_order(h1, h1_other)

    def cross_term(g):
        lanes = slice(g * 256, (g + 1) * 256)
        return (
            rows_sum(ca[:, lanes], dcross, ca_other[:, lanes], dcross_other),
            jnp.concatenate(
                [
                    rows_sum(h2, dcq[:, lanes], h2_other, dcq_other[:, lanes]),
                    tn(text, d_pair[g, 0]),
                    tn(text, d_pair[g, 1]),
                ],
                axis=0,
            ),
        )

    term0 = cross_term(0)
    term1 = cross_term(1)
    grad_cross_out = reduced(term0[0], term1[0])
    grad_cross_in = reduced(term0[1], term1[1])
    width = frames.shape[1]
    grad_cross_q = grad_cross_in[:width]
    grad_cross_kv = grad_cross_in[width:].reshape(2, width, 256)
    grad_out = reduced(tn(o0, dself_rows), tn(o1, dself_rows))

    text_part = 0.0
    for g, weights in ((0, w_cross_kv), (1, cross_kv_y)):
        for c in range(2):
            text_part = text_part + nt(d_pair[g, c], weights[c])
    text_grad = lower(text_part + over_core(text_part))
    text_away = over_y(text_grad)
    grad_text = jnp.where(
        side == 0, jnp.stack([text_grad, text_away]), jnp.stack([text_away, text_grad])
    )

    grads1 = self_back(limit, q1, k1, v1, o1, do1, lse1)
    term1 = jnp.concatenate([tn(h1_rows, g) for g in grads1], axis=0)
    grads0 = self_back(limit, q0, k0, v0, o0, do0, lse0)
    term0 = jnp.concatenate([tn(h1_rows, g) for g in grads0], axis=0)
    grad_qkv = reduced(term0, term1).reshape(3, width, 256)

    yo = first_back(away, (*grads0, *grads1), (w_qkv, qkv_y), ROUND)
    y_received = over_core(yo)
    ym = first_back(where, (*grads0, *grads1), (w_qkv, qkv_y), FULL)
    grad_frames, first_sums = frames_back(where, ym, y_received, dx1, frames, norm_gain)

    sums = sums + first_sums
    sums = sums + over_core(sums)
    sums = sums + over_y(sums)
    sums = sums + along_wide(sums, X_PAIRS)
    sums = sums + along_wide(sums, Z_NEAR)
    sums = sums + along_wide(sums, Z_FAR)
    return (
        out_rows,
        grad_frames,
        grad_text,
        sums[0:6:2],
        sums[1:6:2],
        grad_qkv,
        grad_out,
        grad_cross_q,
        grad_cross_kv,
        grad_cross_out,
        grad_up,
        grad_down,
    )


def solution(mesh):
    chips = dict(mesh.shape) == {"wide": 8, "narrow": 4}
    return jax.shard_map(
        chip_local if chips else general_local,
        mesh=mesh,
        in_specs=(
            P(("wide", "narrow"), None),
            P("wide", None, None),
            P("wide"),
            P(("wide", "narrow")),
            P(),
            P(),
            P(None, None, "narrow"),
            P("narrow", None),
            P(None, "narrow"),
            P(None, None, "narrow"),
            P("narrow", None),
            P(None, "narrow"),
            P("narrow", None),
            P(("wide", "narrow"), None),
        ),
        out_specs=(
            P(("wide", "narrow"), None),
            P(("wide", "narrow"), None),
            P("wide", None, None),
            P(),
            P(),
            P(None, None, "narrow"),
            P("narrow", None),
            P(None, "narrow"),
            P(None, None, "narrow"),
            P("narrow", None),
            P(None, "narrow"),
            P("narrow", None),
        ),
        check_vma=False,
    )
```

```python
import functools

import jax
import jax.numpy as jnp
from jax import lax
from jax.experimental import pallas as pl
from jax.experimental.pallas import tpu as pltpu
from jax.sharding import PartitionSpec as P

HEAD = 64


EPS = 1e-05
NEG = -1e30


def lower(values_in):
    return values_in.astype(jnp.bfloat16)


def product(left_side, right_side, transposed):
    if transposed:
        return lax.dot_general(
            left_side, right_side, (((1,), (1,)), ((), ())), preferred_element_type=jnp.float32
        )
    return jnp.dot(left_side, right_side, preferred_element_type=jnp.float32)


def outer_sum(left_side, right_side):
    return lax.dot_general(
        left_side, right_side, (((0,), (0,)), ((), ())), preferred_element_type=jnp.float32
    )


def normalize(values_in, gain_row, bias_row):
    row_mean = jnp.mean(values_in, axis=-1, keepdims=True)
    centered = values_in - row_mean
    inverse = lax.rsqrt(jnp.mean(centered * centered, axis=-1, keepdims=True) + EPS)
    scaled = centered * inverse
    return (scaled * gain_row + bias_row, scaled, inverse)


def normalize_back(upstream, scaled, inverse, gain_row):
    weighted = upstream * gain_row
    inner_mean = jnp.mean(weighted, axis=-1, keepdims=True)
    along_mean = jnp.mean(weighted * scaled, axis=-1, keepdims=True)
    grad_input = inverse * (weighted - inner_mean - scaled * along_mean)
    return (grad_input, jnp.sum(upstream * scaled, axis=0), jnp.sum(upstream, axis=0))


def gelu_parts(values_in):
    normal_cdf = 0.5 * (1.0 + jax.scipy.special.erf(values_in * 0.7071067811865476))
    normal_pdf = jnp.exp(-0.5 * values_in * values_in) * 0.3989422804014327
    return (values_in * normal_cdf, normal_cdf + values_in * normal_pdf)


def scores_of(query_part, key_part, valid):
    scores = jnp.einsum(
        "bhe,khe->hbk", query_part, key_part, preferred_element_type=jnp.float32
    ) * HEAD ** (-0.5)
    return jnp.where(valid, scores, NEG)


def attend(query_part, key_part, value_part, valid):
    scores = scores_of(query_part, key_part, valid)
    row_top = jnp.max(scores, axis=-1, keepdims=True)
    weights_exp = jnp.exp(scores - row_top)
    denominator = jnp.sum(weights_exp, axis=-1, keepdims=True)
    probability = weights_exp / denominator
    mixed = jnp.einsum(
        "hbk,khe->bhe", lower(probability), value_part, preferred_element_type=jnp.float32
    )
    return (lower(mixed), (row_top + jnp.log(denominator))[..., 0])


def attend_back(query_part, key_part, value_part, valid, summary, upstream):
    scores = scores_of(query_part, key_part, valid)
    probability = jnp.exp(scores - summary[..., None])
    pressure = jnp.einsum("bhe,khe->hbk", upstream, value_part, preferred_element_type=jnp.float32)
    grad_scores = lower(
        probability * (pressure - jnp.sum(probability * pressure, axis=-1, keepdims=True))
    )
    factor = HEAD ** (-0.5)
    grad_query = (
        jnp.einsum("hbk,khe->bhe", grad_scores, key_part, preferred_element_type=jnp.float32)
        * factor
    )
    grad_key = (
        jnp.einsum("hbk,bhe->khe", grad_scores, query_part, preferred_element_type=jnp.float32)
        * factor
    )
    grad_value = jnp.einsum(
        "hbk,bhe->khe", lower(probability), upstream, preferred_element_type=jnp.float32
    )
    return (grad_query, grad_key, grad_value)


def general_local(
    frames,
    text_states,
    lengths,
    loss_mask,
    norm_gain,
    norm_bias,
    w_qkv,
    w_out,
    w_cross_q,
    w_cross_kv,
    w_cross_out,
    w_up,
    w_down,
    cotangent,
):
    row_count = frames.shape[0]
    width = frames.shape[1]
    item_count = lengths.shape[0]
    span = row_count * lax.axis_size("narrow") // item_count
    half_span = span // 2
    inner_width = w_qkv.shape[2]
    head_count = inner_width // HEAD
    text_count = text_states.shape[1]
    full_rows = item_count * span
    places = jnp.arange(span, dtype=jnp.int32)

    def spread(shard_rows):
        return lax.all_gather(shard_rows, "narrow", axis=0, tiled=True)

    def collect(left_side, right_side, transposed):
        return lax.psum_scatter(
            product(
                lax.slice_in_dim(left_side, 0, lax.axis_size("narrow") * row_count, axis=0),
                right_side,
                transposed,
            ),
            "narrow",
            scatter_dimension=0,
            tiled=True,
        )

    def causal(block_index, item_limit):
        query_place = block_index * half_span + jnp.arange(half_span, dtype=jnp.int32)
        return (places[None, :] <= query_place[:, None]) & (places[None, :] < item_limit)

    frame_rows = frames.astype(jnp.float32)
    normed_one, scaled_one, inverse_one = normalize(frame_rows, norm_gain[0], norm_bias[0])
    first_input = spread(lower(normed_one))
    triple = lower(
        jnp.einsum("rd,cde->cre", first_input, w_qkv, preferred_element_type=jnp.float32)
    )
    triple = triple.reshape(3, item_count, span, head_count, HEAD)

    def self_item(packed):
        query_part, key_part, value_part, item_limit = packed
        mixed_list = []
        summary_list = []
        for block_index in range(2):
            mixed, summary = attend(
                query_part[block_index * half_span : (block_index + 1) * half_span],
                key_part,
                value_part,
                causal(block_index, item_limit),
            )
            mixed_list.append(mixed)
            summary_list.append(summary)
        return (jnp.concatenate(mixed_list, axis=0), jnp.stack(summary_list, axis=0))

    attended, self_summary = lax.map(self_item, (triple[0], triple[1], triple[2], lengths))
    attended_flat = attended.reshape(full_rows, inner_width)
    first_rows = frame_rows + collect(attended_flat, w_out, False)
    normed_two, scaled_two, inverse_two = normalize(first_rows, norm_gain[1], norm_bias[1])
    second_input = spread(lower(normed_two))
    cross_query = lower(product(second_input, w_cross_q, False)).reshape(
        item_count, span, head_count, HEAD
    )
    cross_pair = lower(
        jnp.einsum("ntd,cde->cnte", text_states, w_cross_kv, preferred_element_type=jnp.float32)
    )
    cross_pair = cross_pair.reshape(2, item_count, text_count, head_count, HEAD)

    def cross_item(packed):
        query_part, key_part, value_part = packed
        return attend(query_part, key_part, value_part, True)

    cross_mixed, cross_summary = lax.map(cross_item, (cross_query, cross_pair[0], cross_pair[1]))
    cross_flat = cross_mixed.reshape(full_rows, inner_width)
    second_rows = first_rows + collect(cross_flat, w_cross_out, False)
    normed_three, scaled_three, inverse_three = normalize(second_rows, norm_gain[2], norm_bias[2])
    upstream = cotangent.astype(jnp.float32) * loss_mask.astype(jnp.float32)[:, None]
    ffn_grad = lower(upstream)
    ffn_input = spread(lower(normed_three))
    hidden_pre = product(ffn_input, w_up, False)
    active, slope = gelu_parts(hidden_pre)
    active = lower(active)
    out_rows = second_rows + collect(active, w_down, False)
    ffn_full = spread(ffn_grad)
    grad_down = outer_sum(active, ffn_full)
    grad_hidden = lower(product(ffn_full, w_down, True) * slope)
    grad_up = outer_sum(ffn_input, grad_hidden)
    back_three = collect(grad_hidden, w_up, True)
    grad_up, grad_down = (grad_up, grad_down)
    grad_in_three, gain_three, bias_three = normalize_back(
        back_three, scaled_three, inverse_three, norm_gain[2]
    )
    grad_second = upstream + grad_in_three
    cross_full = spread(lower(grad_second))
    grad_cross_out = outer_sum(cross_flat, cross_full)
    cross_upstream = lower(product(cross_full, w_cross_out, True)).reshape(
        item_count, span, head_count, HEAD
    )

    def cross_back(packed):
        query_part, key_part, value_part, summary, upstream_item = packed
        return attend_back(query_part, key_part, value_part, True, summary, upstream_item)

    grad_cq, grad_ck, grad_cv = lax.map(
        cross_back, (cross_query, cross_pair[0], cross_pair[1], cross_summary, cross_upstream)
    )
    grad_cq = lower(grad_cq).reshape(full_rows, inner_width)
    grad_pair = lower(jnp.stack((grad_ck, grad_cv), axis=0)).reshape(
        2, item_count, text_count, inner_width
    )
    grad_cross_q = outer_sum(second_input, grad_cq)
    grad_cross_kv = jnp.einsum(
        "ntd,cnte->cde", text_states, grad_pair, preferred_element_type=jnp.float32
    )
    grad_cross_q, grad_cross_kv, grad_cross_out = (grad_cross_q, grad_cross_kv, grad_cross_out)
    text_partial = jnp.einsum(
        "cnte,cde->ntd", grad_pair, w_cross_kv, preferred_element_type=jnp.float32
    )
    grad_text = lower(lax.psum(text_partial, "narrow"))
    back_two = collect(grad_cq, w_cross_q, True)
    grad_in_two, gain_two, bias_two = normalize_back(
        back_two, scaled_two, inverse_two, norm_gain[1]
    )
    grad_first = grad_second + grad_in_two
    self_full = spread(lower(grad_first))
    grad_out = outer_sum(attended_flat, self_full)
    self_upstream = lower(product(self_full, w_out, True)).reshape(
        item_count, span, head_count, HEAD
    )

    def self_back(packed):
        query_part, key_part, value_part, item_limit, summary, upstream_item = packed
        query_list = []
        key_list = []
        value_list = []
        for block_index in range(2):
            lower_row = block_index * half_span
            grad_query, grad_key, grad_value = attend_back(
                query_part[lower_row : lower_row + half_span],
                key_part,
                value_part,
                causal(block_index, item_limit),
                summary[block_index],
                upstream_item[lower_row : lower_row + half_span],
            )
            query_list.append(grad_query)
            key_list.append(grad_key)
            value_list.append(grad_value)
        return (
            jnp.concatenate(query_list, axis=0),
            key_list[0] + key_list[1],
            value_list[0] + value_list[1],
        )

    grad_q, grad_k, grad_v = lax.map(
        self_back, (triple[0], triple[1], triple[2], lengths, self_summary, self_upstream)
    )
    grad_triple = lower(jnp.stack((grad_q, grad_k, grad_v), axis=0)).reshape(
        3, full_rows, inner_width
    )
    grad_qkv = jnp.einsum(
        "rd,cre->cde", first_input, grad_triple, preferred_element_type=jnp.float32
    )
    grad_qkv, grad_out = (grad_qkv, grad_out)
    merged = grad_triple.transpose(1, 0, 2).reshape(full_rows, 3 * inner_width)
    stacked_weights = w_qkv.transpose(0, 2, 1).reshape(3 * inner_width, width)
    back_one = collect(merged, stacked_weights, False)
    grad_in_one, gain_one, bias_one = normalize_back(
        back_one, scaled_one, inverse_one, norm_gain[0]
    )
    grad_frames = lower(grad_first + grad_in_one)
    gain_terms = jnp.stack((gain_one, gain_two, gain_three), axis=0)
    bias_terms = jnp.stack((bias_one, bias_two, bias_three), axis=0)
    grad_norm_gain, grad_norm_bias = lax.psum((gain_terms, bias_terms), ("wide", "narrow"))
    grad_qkv, grad_out, grad_cross_q, grad_cross_kv, grad_cross_out, grad_up, grad_down = lax.psum(
        (grad_qkv, grad_out, grad_cross_q, grad_cross_kv, grad_cross_out, grad_up, grad_down),
        "wide",
    )
    return (
        lower(out_rows),
        grad_frames,
        grad_text,
        grad_norm_gain,
        grad_norm_bias,
        grad_qkv,
        grad_out,
        grad_cross_q,
        grad_cross_kv,
        grad_cross_out,
        grad_up,
        grad_down,
    )


ROUND = jnp.bfloat16
FULL = jnp.float32
CORE_PAIRS = ((0, 1), (1, 0), (2, 3), (3, 2))
Y_PAIRS = ((0, 2), (2, 0), (1, 3), (3, 1))
X_PAIRS = tuple((i, i ^ 1) for i in range(8))
Z_INWARD = ((0, 2), (1, 3), (6, 4), (7, 5))
Z_MIDDLE = ((2, 4), (4, 2), (3, 5), (5, 3))
Z_OUTWARD = ((2, 0), (3, 1), (4, 6), (5, 7))
Z_NEAR = tuple((i, i ^ 2) for i in range(8))
Z_FAR = tuple((i, i ^ 4) for i in range(8))
MIB = 1 << 20


def nt(a, b):
    return lax.dot_general(a, b, (((1,), (1,)), ((), ())), preferred_element_type=FULL)


def nn(a, b):
    return lax.dot_general(a, b, (((1,), (0,)), ((), ())), preferred_element_type=FULL)


def tn(a, b):
    return lax.dot_general(a, b, (((0,), (0,)), ((), ())), preferred_element_type=FULL)


def shape(dims, kind):
    return jax.ShapeDtypeStruct(dims, kind)


def resident(dims):
    zeros = (0,) * len(dims)
    return pl.BlockSpec(dims, lambda i, s: zeros, pipeline_mode=pl.Buffered(1))


def rows_of(block, width):
    return pl.BlockSpec((block, width), lambda i, s: (i, 0))


def cost(flops, moved):
    return pl.CostEstimate(flops=int(flops), bytes_accessed=int(moved), transcendentals=0)


def params(mib):
    return pltpu.CompilerParams(vmem_limit_bytes=mib * MIB)


def norm_parts(v):
    centered = v - jnp.mean(v, axis=-1, keepdims=True)
    inverse = lax.rsqrt(jnp.mean(centered * centered, axis=-1, keepdims=True) + EPS)
    return centered * inverse, inverse


def norm_pull(y, scaled, inverse, gain_row):
    weighted = y * gain_row
    inner = jnp.mean(weighted, axis=-1, keepdims=True)
    along = jnp.mean(weighted * scaled, axis=-1, keepdims=True)
    return inverse * (weighted - inner - scaled * along)


def project_kernel(where_ref, mine_ref, other_ref, weight_ref, *out_refs, transposed, count):
    half = pl.program_id(0)

    def run(source):
        for c in range(count):
            if transposed:
                result = nt(source[...], weight_ref[c])
            else:
                result = nn(source[...], weight_ref[c])
            out_refs[c][...] = lower(result)

    @pl.when(half == 0)
    def _():
        run(mine_ref)

    @pl.when(half == 1)
    def _():
        run(other_ref)


def project(where, mine, other, weights, transposed):
    rows, depth = mine.shape
    count = weights.shape[0]
    wide = weights.shape[1] if transposed else weights.shape[2]
    whole = pl.BlockSpec((rows, depth), lambda i, s: (0, 0), pipeline_mode=pl.Buffered(1))
    out = pl.BlockSpec((rows, wide), lambda i, s: ((i + s[0]) % 2, 0))
    return pl.pallas_call(
        functools.partial(project_kernel, transposed=transposed, count=count),
        grid_spec=pltpu.PrefetchScalarGridSpec(
            num_scalar_prefetch=1,
            grid=(2,),
            in_specs=[whole, whole, resident(weights.shape)],
            out_specs=[out] * count,
        ),
        out_shape=[shape((2 * rows, wide), ROUND)] * count,
        compiler_params=params(32),
        cost_estimate=cost(4 * rows * depth * wide * count, 8e6),
        name="project",
    )(where, mine, other, weights)


def blocks_of(span, block):
    return [(start, min(block, span - start)) for start in range(0, span, block)]


def self_forward_kernel(limit_ref, q_ref, k_ref, v_ref, o_ref, lse_ref, *, span, floor, block):
    limit = limit_ref[0]
    lane = lax.broadcasted_iota(jnp.int32, (1, 128), 1)
    zero = jnp.zeros((), ROUND)
    for start, size in blocks_of(span, block):
        end = start + size
        mixed_list = []
        for h in range(2):
            own_lanes = (lane < HEAD) if h == 0 else (lane >= HEAD)
            query = jnp.where(own_lanes, q_ref[start:end, :] * HEAD ** (-0.5), zero)
            cuts = [(0, start)] if start <= floor else [(0, floor), (floor, start)]
            parts = []
            for low, high in cuts + [(start, end)]:
                if low == high:
                    continue
                scores = nt(query, k_ref[low:high, :])
                key = lax.broadcasted_iota(jnp.int32, (size, high - low), 1)
                if low == start:
                    valid = key <= lax.broadcasted_iota(jnp.int32, (size, high - low), 0)
                    if high > floor:
                        valid = valid & (key + low < limit)
                    scores = jnp.where(valid, scores, NEG)
                elif high > floor:
                    scores = jnp.where(key + low < limit, scores, NEG)
                parts.append((low, high, scores))
            top = functools.reduce(
                jnp.maximum, [jnp.max(s, axis=1, keepdims=True) for _, _, s in parts]
            )
            total = 0.0
            mixed = 0.0
            for low, high, scores in parts:
                weights_exp = jnp.exp(scores - top)
                total = total + jnp.sum(weights_exp, axis=1, keepdims=True)
                mixed = mixed + nn(lower(weights_exp), v_ref[low:high, :])
            mixed_list.append(mixed / total)
            summary = jnp.broadcast_to(top + jnp.log(total), (size, 128))
            lse_ref[0, h : h + 1, start:end] = summary.T[0:1, :]
        o_ref[start:end, :] = lower(jnp.where(lane < HEAD, mixed_list[0], mixed_list[1]))


def self_forward(limit, q, k, v):
    span, wide = q.shape
    pairs = wide // 128
    floor = (span - span // 8 + 1) // 128 * 128
    pair = pl.BlockSpec((span, 128), lambda p, s: (0, p))
    return pl.pallas_call(
        functools.partial(self_forward_kernel, span=span, floor=floor, block=256),
        grid_spec=pltpu.PrefetchScalarGridSpec(
            num_scalar_prefetch=1,
            grid=(pairs,),
            in_specs=[pair] * 3,
            out_specs=[pair, pl.BlockSpec((1, 8, span), lambda p, s: (p, 0, 0))],
        ),
        out_shape=[shape((span, wide), ROUND), shape((pairs, 8, span), FULL)],
        compiler_params=params(40),
        cost_estimate=cost(16e9, 4e6),
        name="self_forward",
    )(limit, q, k, v)


def self_back_kernel(
    limit_ref, q_ref, k_ref, v_ref, o_ref, do_ref, lse_ref, dq_ref, dk_ref, dv_ref, dqt,
    *, span, floor, block
):
    limit = limit_ref[0]
    lane = lax.broadcasted_iota(jnp.int32, (1, 128), 1)
    row = lax.broadcasted_iota(jnp.int32, (128, 1), 0)
    zero = jnp.zeros((), ROUND)
    factor = HEAD ** (-0.5)
    product_rows = do_ref[...].astype(FULL) * o_ref[...].astype(FULL)
    high = lower(product_rows)
    rest = lower(product_rows - high.astype(FULL))
    pick = lower(
        jnp.concatenate(
            [
                jnp.where(lane < HEAD, 1.0, 0.0),
                jnp.where(lane >= HEAD, 1.0, 0.0),
                jnp.zeros((6, 128), FULL),
            ],
            axis=0,
        )
    )
    delta = nt(pick, high) + nt(pick, rest)
    for start, size in blocks_of(span, block):
        end = start + size
        key = k_ref[start:end, :]
        value = v_ref[start:end, :]
        key_turned = key.T
        dk = 0.0
        dv = 0.0
        dq_add = 0.0
        for h in range(2):
            own_lanes = (lane < HEAD) if h == 0 else (lane >= HEAD)
            own_rows = (row < HEAD) if h == 0 else (row >= HEAD)
            query = jnp.where(own_lanes, q_ref[start:, :] * factor, zero)
            pulled = jnp.where(own_lanes, do_ref[start:, :], zero)
            probability = jnp.exp(nt(key, query) - lse_ref[0, h : h + 1, start:])
            pressure = nt(value, pulled)
            below = lax.broadcasted_iota(jnp.int32, (size, size), 0)
            across = lax.broadcasted_iota(jnp.int32, (size, size), 1)
            corner = jnp.where(below <= across, probability[:, :size], 0.0)
            if end < span:
                probability = jnp.concatenate([corner, probability[:, size:]], axis=1)
            else:
                probability = corner
            if end > floor:
                place = lax.broadcasted_iota(jnp.int32, (size, 1), 0) + start
                probability = jnp.where(place < limit, probability, 0.0)
            grad_scores = lower(probability * (pressure - delta[h : h + 1, start:]))
            dv = dv + nn(lower(probability), pulled)
            dk = dk + nn(grad_scores, query)
            dq_add = dq_add + nn(jnp.where(own_rows, key_turned, zero), grad_scores)
        dk_ref[start:end, :] = lower(dk)
        dv_ref[start:end, :] = lower(dv)
        if start == 0:
            dqt[...] = dq_add
        else:
            dqt[:, start:] += dq_add
    dq_ref[...] = lower(dqt[...].T * factor)


def self_back(limit, q, k, v, o, do, lse):
    span, wide = q.shape
    pairs = wide // 128
    floor = (span - span // 8 + 1) // 128 * 128
    pair = pl.BlockSpec((span, 128), lambda p, s: (0, p))
    return pl.pallas_call(
        functools.partial(self_back_kernel, span=span, floor=floor, block=256),
        grid_spec=pltpu.PrefetchScalarGridSpec(
            num_scalar_prefetch=1,
            grid=(pairs,),
            in_specs=[pair] * 5 + [pl.BlockSpec((1, 8, span), lambda p, s: (p, 0, 0))],
            out_specs=[pair] * 3,
            scratch_shapes=[pltpu.VMEM((128, span), FULL)],
        ),
        out_shape=[shape((span, wide), ROUND)] * 3,
        compiler_params=params(48),
        cost_estimate=cost(20e9, 6e6),
        name="self_back",
    )(limit, q, k, v, o, do, lse)


def by_head(values_in, reduce, empty):
    lane = lax.broadcasted_iota(jnp.int32, (1, 128), 1)
    pieces = []
    for start in range(0, values_in.shape[1], 128):
        part = values_in[:, start : start + 128]
        first = reduce(jnp.where(lane < HEAD, part, empty), axis=1, keepdims=True)
        second = reduce(jnp.where(lane >= HEAD, part, empty), axis=1, keepdims=True)
        pieces.append(jnp.where(lane < HEAD, first, second))
    return jnp.concatenate(pieces, axis=1)


def cross_probability(query, keys):
    scores = nt(query * HEAD ** (-0.5), keys)
    weights_exp = jnp.exp(scores - by_head(scores, jnp.max, NEG))
    return weights_exp / by_head(weights_exp, jnp.sum, 0.0)


def middle_forward_kernel(
    where_ref, frame_ref, a0_ref, a1_ref, a2_ref, a3_ref, gain_ref, bias_ref, *refs
):
    mixed = (a0_ref, a1_ref, a2_ref, a3_ref)
    wo, wq, wc = refs[0:4], refs[4:8], refs[12:16]
    ck0_ref, ck1_ref, cv0_ref, cv1_ref = refs[8:12]
    x1_ref, x2_ref, h2_ref, cq_ref, ca_ref, h3_ref = refs[16:]
    x1 = frame_ref[...].astype(FULL)
    for g in range(4):
        x1 = x1 + nn(mixed[g][...], wo[g][...])
    x1_ref[...] = x1
    scaled, _ = norm_parts(x1)
    h2 = lower(scaled * gain_ref[1:2, :] + bias_ref[1:2, :])
    h2_ref[...] = h2
    for g in range(4):
        lanes = slice(g * 256, (g + 1) * 256)
        cq = lower(nn(h2, wq[g][...]))
        cq_ref[:, lanes] = cq
        probability = cross_probability(cq, (ck0_ref, ck1_ref)[g // 2][g % 2])
        ca_ref[:, lanes] = lower(nn(lower(probability), (cv0_ref, cv1_ref)[g // 2][g % 2]))
    crossed = 0.0
    for g in range(4):
        crossed = crossed + nn(ca_ref[:, g * 256 : (g + 1) * 256], wc[g][...])
    x2 = x1_ref[...] + crossed
    x2_ref[...] = x2
    scaled, _ = norm_parts(x2)
    h3_ref[...] = lower(scaled * gain_ref[2:3, :] + bias_ref[2:3, :])


def middle_forward(where, frames, attended, received, gains, biases, wo, wq, ck, cv, wc):
    rows, width = frames.shape
    block = 208
    steps = rows // block
    piece = pl.BlockSpec((block, 256), lambda i, s: (s[0] * steps + i, 0))
    wide = rows_of(block, width)
    return pl.pallas_call(
        middle_forward_kernel,
        grid_spec=pltpu.PrefetchScalarGridSpec(
            num_scalar_prefetch=1,
            grid=(steps,),
            in_specs=[wide, piece, piece, rows_of(block, 256), rows_of(block, 256)]
            + [resident(a.shape) for a in (gains, biases, *wo, *wq, *ck, *cv, *wc)],
            out_specs=[wide] * 6,
        ),
        out_shape=[shape((rows, width), FULL)] * 2 + [shape((rows, width), ROUND)] * 4,
        compiler_params=params(40),
        cost_estimate=cost(7e9, 25e6),
        name="middle_forward",
    )(where, frames, *attended, *received, gains, biases, *wo, *wq, *ck, *cv, *wc)


def feed_kernel(where_ref, h_ref, d_ref, up_ref, down_ref, *refs, carried, shared):
    before = refs[: 2 * carried]
    g_ref, du_ref, out_ref, y_ref = refs[2 * carried + 2 * shared :]
    u = nn(h_ref[...], up_ref[...])
    active, slope = gelu_parts(u)
    g = lower(active)
    g_ref[...] = g
    du = lower(nt(d_ref[...], down_ref[...]) * slope)
    du_ref[...] = du
    out = nn(g, down_ref[...])
    y = nt(du, up_ref[...])
    if carried:
        out = before[0][...] + out
        y = before[1][...] + y
    out_ref[...] = out.astype(out_ref.dtype)
    y_ref[...] = y.astype(y_ref.dtype)


def feed(where, h, d, up, down, kind, before=(), shared=()):
    rows, width = h.shape
    block = 208
    steps = rows // block
    hidden = up.shape[1]
    wide = rows_of(block, width)
    first = steps if shared else 0
    kept = pl.BlockSpec((block, hidden), lambda i, s: (i + first, 0))
    there = pl.BlockSpec(memory_space=pl.ANY)
    carried = 1 if before else 0
    at = 5 + len(before)
    return pl.pallas_call(
        functools.partial(feed_kernel, carried=carried, shared=1 if shared else 0),
        grid_spec=pltpu.PrefetchScalarGridSpec(
            num_scalar_prefetch=1,
            grid=(steps,),
            in_specs=[wide, wide, resident(up.shape), resident(down.shape)]
            + [wide] * len(before)
            + [there] * len(shared),
            out_specs=[kept, kept, wide, wide],
        ),
        out_shape=[shape((2 * rows, hidden), ROUND)] * 2 + [shape((rows, width), kind)] * 2,
        input_output_aliases={at: 0, at + 1: 1} if shared else {},
        compiler_params=params(56),
        cost_estimate=cost(8 * rows * width * hidden, 20e6),
        name="feed",
    )(where, h, d, up, down, *before, *shared)


def middle_back_kernel(
    where_ref, ym_ref, yr_ref, x1_ref, x2_ref, d_ref, cq_ref, gain_ref, *refs
):
    wq, wc = refs[0:4], refs[8:12]
    ck0_ref, ck1_ref, cv0_ref, cv1_ref = refs[4:8]
    dx1_ref, dself_ref, dcross_ref, dcq_ref, dck_ref, dcv_ref, sums_ref = refs[12:19]
    dck_all, dcv_all = refs[19:]
    step = pl.program_id(0)

    @pl.when(step == 0)
    def _():
        dck_all[...] = jnp.zeros_like(dck_all)
        dcv_all[...] = jnp.zeros_like(dcv_all)
        sums_ref[...] = jnp.zeros_like(sums_ref)

    y3 = ym_ref[...] + yr_ref[...].astype(FULL)
    scaled, inverse = norm_parts(x2_ref[...])
    sums_ref[4:5, :] += jnp.sum(y3 * scaled, axis=0, keepdims=True)
    sums_ref[5:6, :] += jnp.sum(y3, axis=0, keepdims=True)
    dx2 = d_ref[...].astype(FULL) + norm_pull(y3, scaled, inverse, gain_ref[2:3, :])
    dx1_ref[...] = dx2
    dcross = lower(dx2)
    dcross_ref[...] = dcross
    y2 = 0.0
    for g in range(4):
        lanes = slice(g * 256, (g + 1) * 256)
        keys = (ck0_ref, ck1_ref)[g // 2][g % 2]
        values = (cv0_ref, cv1_ref)[g // 2][g % 2]
        dcatt = lower(nt(dcross, wc[g][...]))
        cq = cq_ref[:, lanes]
        probability = cross_probability(cq, keys)
        weighed = nt(dcatt, values)
        inner = by_head(probability * weighed, jnp.sum, 0.0)
        dcs = lower(probability * (weighed - inner))
        dcq = lower(nn(dcs, keys) * HEAD ** (-0.5))
        dcq_ref[:, lanes] = dcq
        dck_all[g] += tn(dcs, cq * HEAD ** (-0.5))
        dcv_all[g] += tn(lower(probability), dcatt)
        y2 = y2 + nt(dcq, wq[g][...])
    scaled, inverse = norm_parts(x1_ref[...])
    sums_ref[2:3, :] += jnp.sum(y2 * scaled, axis=0, keepdims=True)
    sums_ref[3:4, :] += jnp.sum(y2, axis=0, keepdims=True)
    dx1 = dx1_ref[...] + norm_pull(y2, scaled, inverse, gain_ref[1:2, :])
    dx1_ref[...] = dx1
    dself_ref[...] = lower(dx1)

    @pl.when(step == pl.num_programs(0) - 1)
    def _():
        for every, result in ((dck_all, dck_ref), (dcv_all, dcv_ref)):
            for g in range(4):
                total = 0.0
                for h in range(4):
                    lane = lax.broadcasted_iota(jnp.int32, (1, 256), 1) // HEAD
                    total = total + jnp.where(lane == h, every[g, h * 64 : (h + 1) * 64, :], 0.0)
                result[g] = total


def middle_back(where, ym, yr, x1, x2, d, cq, gains, wq, ck, cv, wc):
    rows, width = x1.shape
    block = 208
    wide = rows_of(block, width)
    small = pl.BlockSpec((4, 64, 256), lambda i, s: (0, 0, 0))
    return pl.pallas_call(
        middle_back_kernel,
        grid_spec=pltpu.PrefetchScalarGridSpec(
            num_scalar_prefetch=1,
            grid=(rows // block,),
            in_specs=[wide] * 6 + [resident(a.shape) for a in (gains, *wq, *ck, *cv, *wc)],
            out_specs=[wide] * 4 + [small, small, pl.BlockSpec((8, width), lambda i, s: (0, 0))],
            scratch_shapes=[pltpu.VMEM((4, 256, 256), FULL)] * 2,
        ),
        out_shape=[shape((rows, width), FULL)]
        + [shape((rows, width), ROUND)] * 3
        + [shape((4, 64, 256), FULL)] * 2
        + [shape((8, width), FULL)],
        compiler_params=params(40),
        cost_estimate=cost(7e9, 25e6),
        name="middle_back",
    )(where, ym, yr, x1, x2, d, cq, gains, *wq, *ck, *cv, *wc)


def first_back_kernel(where_ref, *refs):
    grads = refs[:6]
    w0_ref, w1_ref, y_ref = refs[6:]
    y = 0.0
    for g in range(2):
        for c in range(3):
            y = y + nt(grads[3 * g + c][...], (w0_ref, w1_ref)[g][c])
    y_ref[...] = y.astype(y_ref.dtype)


def first_back(half, grads, weights, kind):
    span = grads[0].shape[0]
    rows = span // 2
    width = weights[0].shape[1]
    block = 208
    steps = rows // block
    piece = pl.BlockSpec((block, 256), lambda i, s: (s[0] * steps + i, 0))
    return pl.pallas_call(
        first_back_kernel,
        grid_spec=pltpu.PrefetchScalarGridSpec(
            num_scalar_prefetch=1,
            grid=(steps,),
            in_specs=[piece] * 6 + [resident(a.shape) for a in weights],
            out_specs=rows_of(block, width),
        ),
        out_shape=shape((rows, width), kind),
        compiler_params=params(24),
        cost_estimate=cost(2 * rows * width * 1536, 8e6),
        name="first_back",
    )(half, *grads, *weights)


def frames_back_kernel(where_ref, ym_ref, yr_ref, dx1_ref, frame_ref, gain_ref, out_ref, sums_ref):
    @pl.when(pl.program_id(0) == 0)
    def _():
        sums_ref[...] = jnp.zeros_like(sums_ref)

    y = ym_ref[...] + yr_ref[...].astype(FULL)
    scaled, inverse = norm_parts(frame_ref[...].astype(FULL))
    sums_ref[0:1, :] += jnp.sum(y * scaled, axis=0, keepdims=True)
    sums_ref[1:2, :] += jnp.sum(y, axis=0, keepdims=True)
    out_ref[...] = lower(dx1_ref[...] + norm_pull(y, scaled, inverse, gain_ref[0:1, :]))


def frames_back(where, ym, yr, dx1, frames, gains):
    rows, width = dx1.shape
    block = 208
    wide = rows_of(block, width)
    return pl.pallas_call(
        frames_back_kernel,
        grid_spec=pltpu.PrefetchScalarGridSpec(
            num_scalar_prefetch=1,
            grid=(rows // block,),
            in_specs=[wide] * 4 + [resident(gains.shape)],
            out_specs=[wide, pl.BlockSpec((8, width), lambda i, s: (0, 0))],
        ),
        out_shape=[shape((rows, width), ROUND), shape((8, width), FULL)],
        compiler_params=params(24),
        cost_estimate=cost(1e7, 12e6),
        name="frames_back",
    )(where, ym, yr, dx1, frames, gains)


def chip_local(
    frames, text_states, lengths, loss_mask, norm_gain, norm_bias, w_qkv, w_out, w_cross_q,
    w_cross_kv, w_cross_out, w_up, w_down, cotangent,
):
    at = lax.axis_index("narrow")
    core = at % 2
    side = at // 2
    column = lax.axis_index("wide") % 2
    layer = lax.axis_index("wide") // 2
    where = core.reshape(1).astype(jnp.int32)
    away = (1 - core).reshape(1).astype(jnp.int32)
    limit = lax.dynamic_slice(lengths, (side,), (1,))
    rows, width = frames.shape
    join = lax.optimization_barrier

    def over_core(v):
        return lax.ppermute(v, "narrow", CORE_PAIRS)

    def over_y(v):
        return lax.ppermute(v, "narrow", Y_PAIRS)

    def along_wide(v, pairs):
        return lax.ppermute(v, "wide", pairs)

    def half_of(v, which):
        half = v.shape[0] // 2
        return lax.dynamic_slice_in_dim(v, which * half, half, axis=0)

    def ordered(first, second, which):
        return jnp.where(
            which == 0,
            jnp.concatenate([first, second], axis=0),
            jnp.concatenate([second, first], axis=0),
        )

    near = layer % 2

    def ask(v, which):
        return over_y(half_of(v, which))

    bundle = jnp.concatenate(
        [w_out, w_cross_out, w_cross_q.reshape(256, 1024), w_cross_kv.reshape(512, 1024)], axis=0
    )
    qkv_first = ask(w_qkv.reshape(3 * width, 256), near)
    scaled, _ = norm_parts(frames.astype(FULL))
    h1 = lower(scaled * norm_gain[0] + norm_bias[0])
    h1_other = over_core(h1)
    dout = jnp.where(loss_mask[:, None] != 0, cotangent, jnp.zeros((), ROUND))
    q0, k0, v0 = project(where, h1, h1_other, w_qkv, False)

    q0, qkv_first, bundle, dout = join((q0, qkv_first, bundle, dout))
    qkv_second = along_wide(qkv_first, Z_NEAR)
    bundle_first = ask(bundle, column)
    dout_other = over_core(dout)
    o0, lse0 = self_forward(limit, q0, k0, v0)

    o0, qkv_second, w_up_sent = join((o0, qkv_second, w_up))
    qkv_y = ordered(qkv_first, qkv_second, near).reshape(3, width, 256)
    q1, k1, v1 = project(where, h1, h1_other, qkv_y, False)

    def away_rows(v):
        return half_of(v, 1 - core)

    o0_other = over_core(away_rows(o0))
    q1, bundle_first, w_up_sent, o0_other = join((q1, bundle_first, w_up_sent, o0_other))
    bundle_second = along_wide(bundle_first, X_PAIRS)
    up_first = ask(w_up_sent, column)
    own_wo = over_core(jnp.concatenate([w_out, w_cross_out], axis=0))
    own_wq = over_core(w_cross_q)
    o1, lse1 = self_forward(limit, q1, k1, v1)
    o1_other = over_core(away_rows(o1))

    o1, bundle_second, up_first, w_down_sent = join((o1, bundle_second, up_first, w_down))
    up_second = along_wide(up_first, X_PAIRS)
    down_first = ask(w_down_sent, near)
    bundle_y = ordered(bundle_first, bundle_second, column)
    out_y = bundle_y[:256]
    cross_out_y = bundle_y[256:512]
    cross_q_y = bundle_y[512:768].reshape(width, 256)
    cross_kv_y = bundle_y[768:].reshape(2, width, 256)
    y_wo = over_core(bundle_y[:512])
    y_wq = over_core(cross_q_y)
    wo = (w_out, out_y, own_wo[:256], y_wo[:256])
    wc = (w_cross_out, cross_out_y, own_wo[256:], y_wo[256:])
    wq = (w_cross_q, cross_q_y, own_wq, y_wq)
    text = lax.dynamic_slice(text_states, (side, 0, 0), (1, *text_states.shape[1:]))[0]
    pair = lower(
        jnp.einsum(
            "td,gcde->gcte", text, jnp.stack([w_cross_kv, cross_kv_y]), preferred_element_type=FULL
        )
    )
    pair_other = over_core(pair)
    head_of = jnp.arange(256) // HEAD
    same = head_of[:, None] == head_of[None, :]

    def spread_heads(v):
        return jnp.where(same, jnp.tile(v, (1, 4, 1)), jnp.zeros((), ROUND))

    ck = (spread_heads(pair[:, 0]), spread_heads(pair_other[:, 0]))
    cv = (spread_heads(pair[:, 1]), spread_heads(pair_other[:, 1]))
    x1, x2, h2, cq, ca, h3 = middle_forward(
        where, frames, (o0, o1), (o0_other, o1_other), norm_gain, norm_bias, wo, wq, ck, cv, wc
    )
    h3_other = over_core(h3)
    h2_other = over_core(h2)
    ca_other = over_core(ca[:, 512:])

    h3, up_second, down_first = join((h3, up_second, down_first))
    down_second = along_wide(down_first, Z_NEAR)
    up_y = ordered(up_first, up_second, column)
    g0, du0, out_m, y_m = feed(where, h3, dout, w_up, w_down, FULL)
    g0, du0, out_o, y_o = feed(
        where, h3_other, dout_other, w_up, w_down, FULL, shared=(g0, du0)
    )
    y_o, down_second = join((y_o, down_second))
    down_y = ordered(down_first, down_second, near)
    h3_rows = jnp.concatenate([h3, h3_other], axis=0)
    dout_rows = jnp.concatenate([dout, dout_other], axis=0)
    g1, du1, out_m, y_m = feed(where, h3, dout, up_y, down_y, FULL, before=(out_m, y_m))
    g1, du1, out_o, y_o = feed(
        where, h3_other, dout_other, up_y, down_y, ROUND, before=(out_o, y_o), shared=(g1, du1)
    )
    y_received = over_core(y_o)

    def plus(a, b):
        return lower(a.astype(FULL) + b.astype(FULL))

    def x_send(own, received):
        away_half = lower(half_of(own, 1 - column) + half_of(received, 1 - column).astype(FULL))
        return along_wide(away_half, X_PAIRS)

    def x_sum(own, received, over_x):
        return plus(half_of(own, column) + half_of(received, column).astype(FULL), over_x)

    def z_first(total):
        return along_wide(total, Z_INWARD)

    def z_second(total):
        return along_wide(total, Z_MIDDLE)

    def z_third(total):
        return along_wide(total, Z_OUTWARD)

    def z_pick(total, outer):
        return jnp.where((layer == 1) | (layer == 2), total, outer)

    def finish(mine, over_x):
        return ordered(mine, over_x, column).astype(FULL)

    up1 = lower(tn(h3_rows, du1))
    up1, g1 = join((up1, g1))
    up_y_got = over_y(up1)
    down1 = lower(tn(g1, dout_rows))
    up0 = tn(h3_rows, du0)
    down0 = tn(g0, dout_rows)
    dx1, dself, dcross, dcq, dck, dcv, sums = middle_back(
        where, y_m, y_received, x1, x2, dout, cq, norm_gain, wq, ck, cv, wc
    )
    dself, up_y_got, down1, up0, down0 = join((dself, up_y_got, down1, up0, down0))

    down_y_got = over_y(down1)
    up_x = x_send(up0, up_y_got)
    dself_other = over_core(dself)
    dcross_other = over_core(dcross)
    dcq_other = over_core(dcq[:, 512:])
    d_pair = jnp.stack([dck, dcv], axis=1)
    d_pair = lower(d_pair[:2] + over_core(d_pair[2:]))
    do0, do1 = project(where, dself, dself_other, jnp.stack([w_out, out_y]), True)
    grads1 = self_back(limit, q1, k1, v1, o1, do1, lse1)
    h1_rows = ordered(h1, h1_other, core)
    qkv1 = lower(jnp.concatenate([tn(h1_rows, g) for g in grads1], axis=0))
    dself_rows = ordered(dself, dself_other, core)
    dcross_rows = jnp.concatenate([dcross, dcross_other], axis=0)
    h2_rows = jnp.concatenate([h2, h2_other], axis=0)

    def both(mine, other, g):
        lanes = slice(g * 256, (g + 1) * 256)
        return jnp.concatenate([mine[:, lanes], other[:, lanes]], axis=0)

    def into(g):
        return jnp.concatenate(
            [tn(h2_rows, both(dcq, dcq_other, g)), tn(text, d_pair[g, 0]), tn(text, d_pair[g, 1])],
            axis=0,
        )

    def outof(g, o):
        return jnp.concatenate(
            [tn(o, dself_rows), tn(both(ca, ca_other, g), dcross_rows)], axis=0
        )

    into1 = lower(into(1))
    outof1 = lower(outof(1, o1))
    qkv1, into1, outof1, down_y_got, up_x, do0 = join((qkv1, into1, outof1, down_y_got, up_x, do0))

    qkv_y_got = over_y(qkv1)
    down_x = x_send(down0, down_y_got)
    up_sum = x_sum(up0, up_y_got, up_x)
    up_z = z_first(up_sum)
    grads0 = self_back(limit, q0, k0, v0, o0, do0, lse0)
    yo = first_back(away, (*grads0, *grads1), (w_qkv, qkv_y), ROUND)
    y_received = over_core(yo)
    qkv0 = jnp.concatenate([tn(h1_rows, g) for g in grads0], axis=0)
    qkv0, yo, qkv_y_got, down_x, up_z, into1 = join((qkv0, yo, qkv_y_got, down_x, up_z, into1))

    into_y_got = over_y(into1)
    qkv_x = x_send(qkv0, qkv_y_got)
    down_sum = x_sum(down0, down_y_got, down_x)
    down_z = z_first(down_sum)
    up_sum = plus(up_sum, up_z)
    up_z = z_second(up_sum)
    ym = first_back(where, (*grads0, *grads1), (w_qkv, qkv_y), FULL)
    grad_frames, first_sums = frames_back(where, ym, y_received, dx1, frames, norm_gain)
    out_rows = lower(x2 + out_m + over_core(out_o).astype(FULL))
    into0 = into(0)
    outof0 = outof(0, o0)
    text_part = 0.0
    for g, weights in ((0, w_cross_kv), (1, cross_kv_y)):
        for c in range(2):
            text_part = text_part + nt(d_pair[g, c], weights[c])
    text_grad = lower(text_part + over_core(text_part))
    text_away = over_y(text_grad)
    grad_text = ordered(text_grad[None], text_away[None], side)
    sums = sums + first_sums
    sums = sums + over_core(sums)
    sums = sums + over_y(sums)
    into_y_got, qkv_x, down_z, up_z, outof1, into0, outof0, grad_frames = join(
        (into_y_got, qkv_x, down_z, up_z, outof1, into0, outof0, grad_frames)
    )

    outof_y_got = over_y(outof1)
    into_x = x_send(into0, into_y_got)
    qkv_sum = x_sum(qkv0, qkv_y_got, qkv_x)
    qkv_z = z_first(qkv_sum)
    down_sum = plus(down_sum, down_z)
    down_z = z_second(down_sum)
    up_sum = plus(up_sum, up_z)
    up_z = z_third(up_sum)
    sums = sums + along_wide(sums, X_PAIRS)
    sums = sums + along_wide(sums, Z_NEAR)
    sums = sums + along_wide(sums, Z_FAR)
    outof_y_got, into_x, qkv_z, down_z, up_z = join((outof_y_got, into_x, qkv_z, down_z, up_z))

    outof_x = x_send(outof0, outof_y_got)
    into_sum = x_sum(into0, into_y_got, into_x)
    into_z = z_first(into_sum)
    qkv_sum = plus(qkv_sum, qkv_z)
    qkv_z = z_second(qkv_sum)
    down_sum = plus(down_sum, down_z)
    down_z = z_third(down_sum)
    up_sum = z_pick(up_sum, up_z)
    up_x = along_wide(up_sum, X_PAIRS)
    outof_x, into_z, qkv_z, down_z, up_x = join((outof_x, into_z, qkv_z, down_z, up_x))

    outof_sum = x_sum(outof0, outof_y_got, outof_x)
    outof_z = z_first(outof_sum)
    into_sum = plus(into_sum, into_z)
    into_z = z_second(into_sum)
    qkv_sum = plus(qkv_sum, qkv_z)
    qkv_z = z_third(qkv_sum)
    down_sum = z_pick(down_sum, down_z)
    down_x = along_wide(down_sum, X_PAIRS)
    outof_z, into_z, qkv_z, down_x = join((outof_z, into_z, qkv_z, down_x))

    outof_sum = plus(outof_sum, outof_z)
    outof_z = z_second(outof_sum)
    into_sum = plus(into_sum, into_z)
    into_z = z_third(into_sum)
    qkv_sum = z_pick(qkv_sum, qkv_z)
    qkv_x = along_wide(qkv_sum, X_PAIRS)
    grad_up = finish(up_sum, up_x)
    outof_z, into_z, qkv_x, grad_up = join((outof_z, into_z, qkv_x, grad_up))

    outof_sum = plus(outof_sum, outof_z)
    outof_z = z_third(outof_sum)
    into_sum = z_pick(into_sum, into_z)
    into_x = along_wide(into_sum, X_PAIRS)
    grad_down = finish(down_sum, down_x)
    outof_z, into_x, grad_down = join((outof_z, into_x, grad_down))

    outof_sum = z_pick(outof_sum, outof_z)
    outof_x = along_wide(outof_sum, X_PAIRS)
    grad_qkv = finish(qkv_sum, qkv_x).reshape(3, width, 256)
    grad_cross_in = finish(into_sum, into_x)
    grad_outs = finish(outof_sum, outof_x)
    return (
        out_rows,
        grad_frames,
        grad_text,
        sums[0:6:2],
        sums[1:6:2],
        grad_qkv,
        grad_outs[:256],
        grad_cross_in[:width],
        grad_cross_in[width:].reshape(2, width, 256),
        grad_outs[256:],
        grad_up,
        grad_down,
    )


def solution(mesh):
    chips = dict(mesh.shape) == {"wide": 8, "narrow": 4}
    return jax.shard_map(
        chip_local if chips else general_local,
        mesh=mesh,
        in_specs=(
            P(("wide", "narrow"), None),
            P("wide", None, None),
            P("wide"),
            P(("wide", "narrow")),
            P(),
            P(),
            P(None, None, "narrow"),
            P("narrow", None),
            P(None, "narrow"),
            P(None, None, "narrow"),
            P("narrow", None),
            P(None, "narrow"),
            P("narrow", None),
            P(("wide", "narrow"), None),
        ),
        out_specs=(
            P(("wide", "narrow"), None),
            P(("wide", "narrow"), None),
            P("wide", None, None),
            P(),
            P(),
            P(None, None, "narrow"),
            P("narrow", None),
            P(None, "narrow"),
            P(None, None, "narrow"),
            P("narrow", None),
            P(None, "narrow"),
            P("narrow", None),
        ),
        check_vma=False,
    )
```

```python
import functools

import jax
import jax.numpy as jnp
from jax import lax
from jax.experimental import pallas as pl
from jax.experimental.pallas import tpu as pltpu
from jax.sharding import PartitionSpec as P

HEAD = 64


EPS = 1e-05
NEG = -1e30


def lower(values_in):
    return values_in.astype(jnp.bfloat16)


def product(left_side, right_side, transposed):
    if transposed:
        return lax.dot_general(
            left_side, right_side, (((1,), (1,)), ((), ())), preferred_element_type=jnp.float32
        )
    return jnp.dot(left_side, right_side, preferred_element_type=jnp.float32)


def outer_sum(left_side, right_side):
    return lax.dot_general(
        left_side, right_side, (((0,), (0,)), ((), ())), preferred_element_type=jnp.float32
    )


def normalize(values_in, gain_row, bias_row):
    row_mean = jnp.mean(values_in, axis=-1, keepdims=True)
    centered = values_in - row_mean
    inverse = lax.rsqrt(jnp.mean(centered * centered, axis=-1, keepdims=True) + EPS)
    scaled = centered * inverse
    return (scaled * gain_row + bias_row, scaled, inverse)


def normalize_back(upstream, scaled, inverse, gain_row):
    weighted = upstream * gain_row
    inner_mean = jnp.mean(weighted, axis=-1, keepdims=True)
    along_mean = jnp.mean(weighted * scaled, axis=-1, keepdims=True)
    grad_input = inverse * (weighted - inner_mean - scaled * along_mean)
    return (grad_input, jnp.sum(upstream * scaled, axis=0), jnp.sum(upstream, axis=0))


def gelu_parts(values_in):
    normal_cdf = 0.5 * (1.0 + jax.scipy.special.erf(values_in * 0.7071067811865476))
    normal_pdf = jnp.exp(-0.5 * values_in * values_in) * 0.3989422804014327
    return (values_in * normal_cdf, normal_cdf + values_in * normal_pdf)


def scores_of(query_part, key_part, valid):
    scores = jnp.einsum(
        "bhe,khe->hbk", query_part, key_part, preferred_element_type=jnp.float32
    ) * HEAD ** (-0.5)
    return jnp.where(valid, scores, NEG)


def attend(query_part, key_part, value_part, valid):
    scores = scores_of(query_part, key_part, valid)
    row_top = jnp.max(scores, axis=-1, keepdims=True)
    weights_exp = jnp.exp(scores - row_top)
    denominator = jnp.sum(weights_exp, axis=-1, keepdims=True)
    probability = weights_exp / denominator
    mixed = jnp.einsum(
        "hbk,khe->bhe", lower(probability), value_part, preferred_element_type=jnp.float32
    )
    return (lower(mixed), (row_top + jnp.log(denominator))[..., 0])


def attend_back(query_part, key_part, value_part, valid, summary, upstream):
    scores = scores_of(query_part, key_part, valid)
    probability = jnp.exp(scores - summary[..., None])
    pressure = jnp.einsum("bhe,khe->hbk", upstream, value_part, preferred_element_type=jnp.float32)
    grad_scores = lower(
        probability * (pressure - jnp.sum(probability * pressure, axis=-1, keepdims=True))
    )
    factor = HEAD ** (-0.5)
    grad_query = (
        jnp.einsum("hbk,khe->bhe", grad_scores, key_part, preferred_element_type=jnp.float32)
        * factor
    )
    grad_key = (
        jnp.einsum("hbk,bhe->khe", grad_scores, query_part, preferred_element_type=jnp.float32)
        * factor
    )
    grad_value = jnp.einsum(
        "hbk,bhe->khe", lower(probability), upstream, preferred_element_type=jnp.float32
    )
    return (grad_query, grad_key, grad_value)


def general_local(
    frames,
    text_states,
    lengths,
    loss_mask,
    norm_gain,
    norm_bias,
    w_qkv,
    w_out,
    w_cross_q,
    w_cross_kv,
    w_cross_out,
    w_up,
    w_down,
    cotangent,
):
    row_count = frames.shape[0]
    width = frames.shape[1]
    item_count = lengths.shape[0]
    span = row_count * lax.axis_size("narrow") // item_count
    half_span = span // 2
    inner_width = w_qkv.shape[2]
    head_count = inner_width // HEAD
    text_count = text_states.shape[1]
    full_rows = item_count * span
    places = jnp.arange(span, dtype=jnp.int32)

    def spread(shard_rows):
        return lax.all_gather(shard_rows, "narrow", axis=0, tiled=True)

    def collect(left_side, right_side, transposed):
        return lax.psum_scatter(
            product(
                lax.slice_in_dim(left_side, 0, lax.axis_size("narrow") * row_count, axis=0),
                right_side,
                transposed,
            ),
            "narrow",
            scatter_dimension=0,
            tiled=True,
        )

    def causal(block_index, item_limit):
        query_place = block_index * half_span + jnp.arange(half_span, dtype=jnp.int32)
        return (places[None, :] <= query_place[:, None]) & (places[None, :] < item_limit)

    frame_rows = frames.astype(jnp.float32)
    normed_one, scaled_one, inverse_one = normalize(frame_rows, norm_gain[0], norm_bias[0])
    first_input = spread(lower(normed_one))
    triple = lower(
        jnp.einsum("rd,cde->cre", first_input, w_qkv, preferred_element_type=jnp.float32)
    )
    triple = triple.reshape(3, item_count, span, head_count, HEAD)

    def self_item(packed):
        query_part, key_part, value_part, item_limit = packed
        mixed_list = []
        summary_list = []
        for block_index in range(2):
            mixed, summary = attend(
                query_part[block_index * half_span : (block_index + 1) * half_span],
                key_part,
                value_part,
                causal(block_index, item_limit),
            )
            mixed_list.append(mixed)
            summary_list.append(summary)
        return (jnp.concatenate(mixed_list, axis=0), jnp.stack(summary_list, axis=0))

    attended, self_summary = lax.map(self_item, (triple[0], triple[1], triple[2], lengths))
    attended_flat = attended.reshape(full_rows, inner_width)
    first_rows = frame_rows + collect(attended_flat, w_out, False)
    normed_two, scaled_two, inverse_two = normalize(first_rows, norm_gain[1], norm_bias[1])
    second_input = spread(lower(normed_two))
    cross_query = lower(product(second_input, w_cross_q, False)).reshape(
        item_count, span, head_count, HEAD
    )
    cross_pair = lower(
        jnp.einsum("ntd,cde->cnte", text_states, w_cross_kv, preferred_element_type=jnp.float32)
    )
    cross_pair = cross_pair.reshape(2, item_count, text_count, head_count, HEAD)

    def cross_item(packed):
        query_part, key_part, value_part = packed
        return attend(query_part, key_part, value_part, True)

    cross_mixed, cross_summary = lax.map(cross_item, (cross_query, cross_pair[0], cross_pair[1]))
    cross_flat = cross_mixed.reshape(full_rows, inner_width)
    second_rows = first_rows + collect(cross_flat, w_cross_out, False)
    normed_three, scaled_three, inverse_three = normalize(second_rows, norm_gain[2], norm_bias[2])
    upstream = cotangent.astype(jnp.float32) * loss_mask.astype(jnp.float32)[:, None]
    ffn_grad = lower(upstream)
    ffn_input = spread(lower(normed_three))
    hidden_pre = product(ffn_input, w_up, False)
    active, slope = gelu_parts(hidden_pre)
    active = lower(active)
    out_rows = second_rows + collect(active, w_down, False)
    ffn_full = spread(ffn_grad)
    grad_down = outer_sum(active, ffn_full)
    grad_hidden = lower(product(ffn_full, w_down, True) * slope)
    grad_up = outer_sum(ffn_input, grad_hidden)
    back_three = collect(grad_hidden, w_up, True)
    grad_up, grad_down = (grad_up, grad_down)
    grad_in_three, gain_three, bias_three = normalize_back(
        back_three, scaled_three, inverse_three, norm_gain[2]
    )
    grad_second = upstream + grad_in_three
    cross_full = spread(lower(grad_second))
    grad_cross_out = outer_sum(cross_flat, cross_full)
    cross_upstream = lower(product(cross_full, w_cross_out, True)).reshape(
        item_count, span, head_count, HEAD
    )

    def cross_back(packed):
        query_part, key_part, value_part, summary, upstream_item = packed
        return attend_back(query_part, key_part, value_part, True, summary, upstream_item)

    grad_cq, grad_ck, grad_cv = lax.map(
        cross_back, (cross_query, cross_pair[0], cross_pair[1], cross_summary, cross_upstream)
    )
    grad_cq = lower(grad_cq).reshape(full_rows, inner_width)
    grad_pair = lower(jnp.stack((grad_ck, grad_cv), axis=0)).reshape(
        2, item_count, text_count, inner_width
    )
    grad_cross_q = outer_sum(second_input, grad_cq)
    grad_cross_kv = jnp.einsum(
        "ntd,cnte->cde", text_states, grad_pair, preferred_element_type=jnp.float32
    )
    grad_cross_q, grad_cross_kv, grad_cross_out = (grad_cross_q, grad_cross_kv, grad_cross_out)
    text_partial = jnp.einsum(
        "cnte,cde->ntd", grad_pair, w_cross_kv, preferred_element_type=jnp.float32
    )
    grad_text = lower(lax.psum(text_partial, "narrow"))
    back_two = collect(grad_cq, w_cross_q, True)
    grad_in_two, gain_two, bias_two = normalize_back(
        back_two, scaled_two, inverse_two, norm_gain[1]
    )
    grad_first = grad_second + grad_in_two
    self_full = spread(lower(grad_first))
    grad_out = outer_sum(attended_flat, self_full)
    self_upstream = lower(product(self_full, w_out, True)).reshape(
        item_count, span, head_count, HEAD
    )

    def self_back(packed):
        query_part, key_part, value_part, item_limit, summary, upstream_item = packed
        query_list = []
        key_list = []
        value_list = []
        for block_index in range(2):
            lower_row = block_index * half_span
            grad_query, grad_key, grad_value = attend_back(
                query_part[lower_row : lower_row + half_span],
                key_part,
                value_part,
                causal(block_index, item_limit),
                summary[block_index],
                upstream_item[lower_row : lower_row + half_span],
            )
            query_list.append(grad_query)
            key_list.append(grad_key)
            value_list.append(grad_value)
        return (
            jnp.concatenate(query_list, axis=0),
            key_list[0] + key_list[1],
            value_list[0] + value_list[1],
        )

    grad_q, grad_k, grad_v = lax.map(
        self_back, (triple[0], triple[1], triple[2], lengths, self_summary, self_upstream)
    )
    grad_triple = lower(jnp.stack((grad_q, grad_k, grad_v), axis=0)).reshape(
        3, full_rows, inner_width
    )
    grad_qkv = jnp.einsum(
        "rd,cre->cde", first_input, grad_triple, preferred_element_type=jnp.float32
    )
    grad_qkv, grad_out = (grad_qkv, grad_out)
    merged = grad_triple.transpose(1, 0, 2).reshape(full_rows, 3 * inner_width)
    stacked_weights = w_qkv.transpose(0, 2, 1).reshape(3 * inner_width, width)
    back_one = collect(merged, stacked_weights, False)
    grad_in_one, gain_one, bias_one = normalize_back(
        back_one, scaled_one, inverse_one, norm_gain[0]
    )
    grad_frames = lower(grad_first + grad_in_one)
    gain_terms = jnp.stack((gain_one, gain_two, gain_three), axis=0)
    bias_terms = jnp.stack((bias_one, bias_two, bias_three), axis=0)
    grad_norm_gain, grad_norm_bias = lax.psum((gain_terms, bias_terms), ("wide", "narrow"))
    grad_qkv, grad_out, grad_cross_q, grad_cross_kv, grad_cross_out, grad_up, grad_down = lax.psum(
        (grad_qkv, grad_out, grad_cross_q, grad_cross_kv, grad_cross_out, grad_up, grad_down),
        "wide",
    )
    return (
        lower(out_rows),
        grad_frames,
        grad_text,
        grad_norm_gain,
        grad_norm_bias,
        grad_qkv,
        grad_out,
        grad_cross_q,
        grad_cross_kv,
        grad_cross_out,
        grad_up,
        grad_down,
    )


ROUND = jnp.bfloat16
FULL = jnp.float32
CORE_PAIRS = ((0, 1), (1, 0), (2, 3), (3, 2))
Y_PAIRS = ((0, 2), (2, 0), (1, 3), (3, 1))
X_PAIRS = tuple((i, i ^ 1) for i in range(8))
Z_INWARD = ((0, 2), (1, 3), (6, 4), (7, 5))
Z_MIDDLE = ((2, 4), (4, 2), (3, 5), (5, 3))
Z_OUTWARD = ((2, 0), (3, 1), (4, 6), (5, 7))
Z_NEAR = tuple((i, i ^ 2) for i in range(8))
Z_FAR = tuple((i, i ^ 4) for i in range(8))
MIB = 1 << 20


def nt(a, b):
    return lax.dot_general(a, b, (((1,), (1,)), ((), ())), preferred_element_type=FULL)


def nn(a, b):
    return lax.dot_general(a, b, (((1,), (0,)), ((), ())), preferred_element_type=FULL)


def tn(a, b):
    return lax.dot_general(a, b, (((0,), (0,)), ((), ())), preferred_element_type=FULL)


def shape(dims, kind):
    return jax.ShapeDtypeStruct(dims, kind)


def resident(dims):
    zeros = (0,) * len(dims)
    return pl.BlockSpec(dims, lambda i, s: zeros, pipeline_mode=pl.Buffered(1))


def rows_of(block, width):
    return pl.BlockSpec((block, width), lambda i, s: (i, 0))


def cost(flops, moved):
    return pl.CostEstimate(flops=int(flops), bytes_accessed=int(moved), transcendentals=0)


def params(mib):
    return pltpu.CompilerParams(vmem_limit_bytes=mib * MIB)


def norm_parts(v):
    centered = v - jnp.mean(v, axis=-1, keepdims=True)
    inverse = lax.rsqrt(jnp.mean(centered * centered, axis=-1, keepdims=True) + EPS)
    return centered * inverse, inverse


def norm_pull(y, scaled, inverse, gain_row):
    weighted = y * gain_row
    inner = jnp.mean(weighted, axis=-1, keepdims=True)
    along = jnp.mean(weighted * scaled, axis=-1, keepdims=True)
    return inverse * (weighted - inner - scaled * along)


def project_kernel(where_ref, mine_ref, other_ref, weight_ref, *out_refs, transposed, count):
    half = pl.program_id(0)

    def run(source):
        for c in range(count):
            if transposed:
                result = nt(source[...], weight_ref[c])
            else:
                result = nn(source[...], weight_ref[c])
            out_refs[c][...] = lower(result)

    @pl.when(half == 0)
    def _():
        run(mine_ref)

    @pl.when(half == 1)
    def _():
        run(other_ref)


def project(where, mine, other, weights, transposed):
    rows, depth = mine.shape
    count = weights.shape[0]
    wide = weights.shape[1] if transposed else weights.shape[2]
    whole = pl.BlockSpec((rows, depth), lambda i, s: (0, 0), pipeline_mode=pl.Buffered(1))
    out = pl.BlockSpec((rows, wide), lambda i, s: ((i + s[0]) % 2, 0))
    return pl.pallas_call(
        functools.partial(project_kernel, transposed=transposed, count=count),
        grid_spec=pltpu.PrefetchScalarGridSpec(
            num_scalar_prefetch=1,
            grid=(2,),
            in_specs=[whole, whole, resident(weights.shape)],
            out_specs=[out] * count,
        ),
        out_shape=[shape((2 * rows, wide), ROUND)] * count,
        compiler_params=params(32),
        cost_estimate=cost(4 * rows * depth * wide * count, 8e6),
        name="project",
    )(where, mine, other, weights)


def blocks_of(span, block):
    return [(start, min(block, span - start)) for start in range(0, span, block)]


def self_forward_kernel(limit_ref, q_ref, k_ref, v_ref, o_ref, lse_ref, *, span, floor, block):
    limit = limit_ref[0]
    lane = lax.broadcasted_iota(jnp.int32, (1, 128), 1)
    zero = jnp.zeros((), ROUND)
    for start, size in blocks_of(span, block):
        end = start + size
        mixed_list = []
        for h in range(2):
            own_lanes = (lane < HEAD) if h == 0 else (lane >= HEAD)
            query = jnp.where(own_lanes, q_ref[start:end, :] * HEAD ** (-0.5), zero)
            cuts = [(0, start)] if start <= floor else [(0, floor), (floor, start)]
            parts = []
            for low, high in cuts + [(start, end)]:
                if low == high:
                    continue
                scores = nt(query, k_ref[low:high, :])
                key = lax.broadcasted_iota(jnp.int32, (size, high - low), 1)
                if low == start:
                    valid = key <= lax.broadcasted_iota(jnp.int32, (size, high - low), 0)
                    if high > floor:
                        valid = valid & (key + low < limit)
                    scores = jnp.where(valid, scores, NEG)
                elif high > floor:
                    scores = jnp.where(key + low < limit, scores, NEG)
                parts.append((low, high, scores))
            top = functools.reduce(
                jnp.maximum, [jnp.max(s, axis=1, keepdims=True) for _, _, s in parts]
            )
            total = 0.0
            mixed = 0.0
            for low, high, scores in parts:
                weights_exp = jnp.exp(scores - top)
                total = total + jnp.sum(weights_exp, axis=1, keepdims=True)
                mixed = mixed + nn(lower(weights_exp), v_ref[low:high, :])
            mixed_list.append(mixed / total)
            summary = jnp.broadcast_to(top + jnp.log(total), (size, 128))
            lse_ref[0, h : h + 1, start:end] = summary.T[0:1, :]
        o_ref[start:end, :] = lower(jnp.where(lane < HEAD, mixed_list[0], mixed_list[1]))


def self_forward(limit, q, k, v):
    span, wide = q.shape
    pairs = wide // 128
    floor = (span - span // 8 + 1) // 128 * 128
    pair = pl.BlockSpec((span, 128), lambda p, s: (0, p))
    return pl.pallas_call(
        functools.partial(self_forward_kernel, span=span, floor=floor, block=256),
        grid_spec=pltpu.PrefetchScalarGridSpec(
            num_scalar_prefetch=1,
            grid=(pairs,),
            in_specs=[pair] * 3,
            out_specs=[pair, pl.BlockSpec((1, 8, span), lambda p, s: (p, 0, 0))],
        ),
        out_shape=[shape((span, wide), ROUND), shape((pairs, 8, span), FULL)],
        compiler_params=params(40),
        cost_estimate=cost(16e9, 4e6),
        name="self_forward",
    )(limit, q, k, v)


def self_back_kernel(
    limit_ref, q_ref, k_ref, v_ref, o_ref, do_ref, lse_ref, dq_ref, dk_ref, dv_ref, dqt,
    *, span, floor, block
):
    limit = limit_ref[0]
    lane = lax.broadcasted_iota(jnp.int32, (1, 128), 1)
    row = lax.broadcasted_iota(jnp.int32, (128, 1), 0)
    zero = jnp.zeros((), ROUND)
    factor = HEAD ** (-0.5)
    product_rows = do_ref[...].astype(FULL) * o_ref[...].astype(FULL)
    high = lower(product_rows)
    rest = lower(product_rows - high.astype(FULL))
    pick = lower(
        jnp.concatenate(
            [
                jnp.where(lane < HEAD, 1.0, 0.0),
                jnp.where(lane >= HEAD, 1.0, 0.0),
                jnp.zeros((6, 128), FULL),
            ],
            axis=0,
        )
    )
    delta = nt(pick, high) + nt(pick, rest)
    for start, size in blocks_of(span, block):
        end = start + size
        key = k_ref[start:end, :]
        value = v_ref[start:end, :]
        key_turned = key.T
        dk = 0.0
        dv = 0.0
        dq_add = 0.0
        for h in range(2):
            own_lanes = (lane < HEAD) if h == 0 else (lane >= HEAD)
            own_rows = (row < HEAD) if h == 0 else (row >= HEAD)
            query = jnp.where(own_lanes, q_ref[start:, :] * factor, zero)
            pulled = jnp.where(own_lanes, do_ref[start:, :], zero)
            probability = jnp.exp(nt(key, query) - lse_ref[0, h : h + 1, start:])
            pressure = nt(value, pulled)
            below = lax.broadcasted_iota(jnp.int32, (size, size), 0)
            across = lax.broadcasted_iota(jnp.int32, (size, size), 1)
            corner = jnp.where(below <= across, probability[:, :size], 0.0)
            if end < span:
                probability = jnp.concatenate([corner, probability[:, size:]], axis=1)
            else:
                probability = corner
            if end > floor:
                place = lax.broadcasted_iota(jnp.int32, (size, 1), 0) + start
                probability = jnp.where(place < limit, probability, 0.0)
            grad_scores = lower(probability * (pressure - delta[h : h + 1, start:]))
            dv = dv + nn(lower(probability), pulled)
            dk = dk + nn(grad_scores, query)
            dq_add = dq_add + nn(jnp.where(own_rows, key_turned, zero), grad_scores)
        dk_ref[start:end, :] = lower(dk)
        dv_ref[start:end, :] = lower(dv)
        if start == 0:
            dqt[...] = dq_add
        else:
            dqt[:, start:] += dq_add
    dq_ref[...] = lower(dqt[...].T * factor)


def self_back(limit, q, k, v, o, do, lse):
    span, wide = q.shape
    pairs = wide // 128
    floor = (span - span // 8 + 1) // 128 * 128
    pair = pl.BlockSpec((span, 128), lambda p, s: (0, p))
    return pl.pallas_call(
        functools.partial(self_back_kernel, span=span, floor=floor, block=256),
        grid_spec=pltpu.PrefetchScalarGridSpec(
            num_scalar_prefetch=1,
            grid=(pairs,),
            in_specs=[pair] * 5 + [pl.BlockSpec((1, 8, span), lambda p, s: (p, 0, 0))],
            out_specs=[pair] * 3,
            scratch_shapes=[pltpu.VMEM((128, span), FULL)],
        ),
        out_shape=[shape((span, wide), ROUND)] * 3,
        compiler_params=params(48),
        cost_estimate=cost(20e9, 6e6),
        name="self_back",
    )(limit, q, k, v, o, do, lse)


def by_head(values_in, reduce, empty):
    lane = lax.broadcasted_iota(jnp.int32, (1, 128), 1)
    pieces = []
    for start in range(0, values_in.shape[1], 128):
        part = values_in[:, start : start + 128]
        first = reduce(jnp.where(lane < HEAD, part, empty), axis=1, keepdims=True)
        second = reduce(jnp.where(lane >= HEAD, part, empty), axis=1, keepdims=True)
        pieces.append(jnp.where(lane < HEAD, first, second))
    return jnp.concatenate(pieces, axis=1)


def cross_probability(query, keys):
    scores = nt(query * HEAD ** (-0.5), keys)
    weights_exp = jnp.exp(scores - by_head(scores, jnp.max, NEG))
    return weights_exp / by_head(weights_exp, jnp.sum, 0.0)


def middle_forward_kernel(
    where_ref, frame_ref, a0_ref, a1_ref, a2_ref, a3_ref, gain_ref, bias_ref, *refs
):
    mixed = (a0_ref, a1_ref, a2_ref, a3_ref)
    wo, wq, wc = refs[0:4], refs[4:8], refs[12:16]
    ck0_ref, ck1_ref, cv0_ref, cv1_ref = refs[8:12]
    x1_ref, x2_ref, h2_ref, cq_ref, ca_ref, h3_ref = refs[16:]
    x1 = frame_ref[...].astype(FULL)
    for g in range(4):
        x1 = x1 + nn(mixed[g][...], wo[g][...])
    x1_ref[...] = x1
    scaled, _ = norm_parts(x1)
    h2 = lower(scaled * gain_ref[1:2, :] + bias_ref[1:2, :])
    h2_ref[...] = h2
    for g in range(4):
        lanes = slice(g * 256, (g + 1) * 256)
        cq = lower(nn(h2, wq[g][...]))
        cq_ref[:, lanes] = cq
        probability = cross_probability(cq, (ck0_ref, ck1_ref)[g // 2][g % 2])
        ca_ref[:, lanes] = lower(nn(lower(probability), (cv0_ref, cv1_ref)[g // 2][g % 2]))
    crossed = 0.0
    for g in range(4):
        crossed = crossed + nn(ca_ref[:, g * 256 : (g + 1) * 256], wc[g][...])
    x2 = x1_ref[...] + crossed
    x2_ref[...] = x2
    scaled, _ = norm_parts(x2)
    h3_ref[...] = lower(scaled * gain_ref[2:3, :] + bias_ref[2:3, :])


def middle_forward(where, frames, attended, received, gains, biases, wo, wq, ck, cv, wc):
    rows, width = frames.shape
    block = 208
    steps = rows // block
    piece = pl.BlockSpec((block, 256), lambda i, s: (s[0] * steps + i, 0))
    wide = rows_of(block, width)
    return pl.pallas_call(
        middle_forward_kernel,
        grid_spec=pltpu.PrefetchScalarGridSpec(
            num_scalar_prefetch=1,
            grid=(steps,),
            in_specs=[wide, piece, piece, rows_of(block, 256), rows_of(block, 256)]
            + [resident(a.shape) for a in (gains, biases, *wo, *wq, *ck, *cv, *wc)],
            out_specs=[wide] * 6,
        ),
        out_shape=[shape((rows, width), FULL)] * 2 + [shape((rows, width), ROUND)] * 4,
        compiler_params=params(40),
        cost_estimate=cost(7e9, 25e6),
        name="middle_forward",
    )(where, frames, *attended, *received, gains, biases, *wo, *wq, *ck, *cv, *wc)


def feed_kernel(where_ref, h_ref, d_ref, up_ref, down_ref, *refs, carried, shared):
    before = refs[: 2 * carried]
    g_ref, du_ref, out_ref, y_ref = refs[2 * carried + 2 * shared :]
    u = nn(h_ref[...], up_ref[...])
    active, slope = gelu_parts(u)
    g = lower(active)
    g_ref[...] = g
    du = lower(nt(d_ref[...], down_ref[...]) * slope)
    du_ref[...] = du
    out = nn(g, down_ref[...])
    y = nt(du, up_ref[...])
    if carried:
        out = before[0][...] + out
        y = before[1][...] + y
    out_ref[...] = out.astype(out_ref.dtype)
    y_ref[...] = y.astype(y_ref.dtype)


def feed(where, h, d, up, down, kind, before=(), shared=()):
    rows, width = h.shape
    block = 208
    steps = rows // block
    hidden = up.shape[1]
    wide = rows_of(block, width)
    first = steps if shared else 0
    kept = pl.BlockSpec((block, hidden), lambda i, s: (i + first, 0))
    there = pl.BlockSpec(memory_space=pl.ANY)
    carried = 1 if before else 0
    at = 5 + len(before)
    return pl.pallas_call(
        functools.partial(feed_kernel, carried=carried, shared=1 if shared else 0),
        grid_spec=pltpu.PrefetchScalarGridSpec(
            num_scalar_prefetch=1,
            grid=(steps,),
            in_specs=[wide, wide, resident(up.shape), resident(down.shape)]
            + [wide] * len(before)
            + [there] * len(shared),
            out_specs=[kept, kept, wide, wide],
        ),
        out_shape=[shape((2 * rows, hidden), ROUND)] * 2 + [shape((rows, width), kind)] * 2,
        input_output_aliases={at: 0, at + 1: 1} if shared else {},
        compiler_params=params(56),
        cost_estimate=cost(8 * rows * width * hidden, 20e6),
        name="feed",
    )(where, h, d, up, down, *before, *shared)


def middle_back_kernel(
    where_ref, ym_ref, yr_ref, x1_ref, x2_ref, d_ref, cq_ref, gain_ref, *refs
):
    wq, wc = refs[0:4], refs[8:12]
    ck0_ref, ck1_ref, cv0_ref, cv1_ref = refs[4:8]
    dx1_ref, dself_ref, dcross_ref, dcq_ref, dck_ref, dcv_ref, sums_ref = refs[12:19]
    dck_all, dcv_all = refs[19:]
    step = pl.program_id(0)

    @pl.when(step == 0)
    def _():
        dck_all[...] = jnp.zeros_like(dck_all)
        dcv_all[...] = jnp.zeros_like(dcv_all)
        sums_ref[...] = jnp.zeros_like(sums_ref)

    y3 = ym_ref[...] + yr_ref[...].astype(FULL)
    scaled, inverse = norm_parts(x2_ref[...])
    sums_ref[4:5, :] += jnp.sum(y3 * scaled, axis=0, keepdims=True)
    sums_ref[5:6, :] += jnp.sum(y3, axis=0, keepdims=True)
    dx2 = d_ref[...].astype(FULL) + norm_pull(y3, scaled, inverse, gain_ref[2:3, :])
    dx1_ref[...] = dx2
    dcross = lower(dx2)
    dcross_ref[...] = dcross
    y2 = 0.0
    for g in range(4):
        lanes = slice(g * 256, (g + 1) * 256)
        keys = (ck0_ref, ck1_ref)[g // 2][g % 2]
        values = (cv0_ref, cv1_ref)[g // 2][g % 2]
        dcatt = lower(nt(dcross, wc[g][...]))
        cq = cq_ref[:, lanes]
        probability = cross_probability(cq, keys)
        weighed = nt(dcatt, values)
        inner = by_head(probability * weighed, jnp.sum, 0.0)
        dcs = lower(probability * (weighed - inner))
        dcq = lower(nn(dcs, keys) * HEAD ** (-0.5))
        dcq_ref[:, lanes] = dcq
        dck_all[g] += tn(dcs, cq * HEAD ** (-0.5))
        dcv_all[g] += tn(lower(probability), dcatt)
        y2 = y2 + nt(dcq, wq[g][...])
    scaled, inverse = norm_parts(x1_ref[...])
    sums_ref[2:3, :] += jnp.sum(y2 * scaled, axis=0, keepdims=True)
    sums_ref[3:4, :] += jnp.sum(y2, axis=0, keepdims=True)
    dx1 = dx1_ref[...] + norm_pull(y2, scaled, inverse, gain_ref[1:2, :])
    dx1_ref[...] = dx1
    dself_ref[...] = lower(dx1)

    @pl.when(step == pl.num_programs(0) - 1)
    def _():
        for every, result in ((dck_all, dck_ref), (dcv_all, dcv_ref)):
            for g in range(4):
                total = 0.0
                for h in range(4):
                    lane = lax.broadcasted_iota(jnp.int32, (1, 256), 1) // HEAD
                    total = total + jnp.where(lane == h, every[g, h * 64 : (h + 1) * 64, :], 0.0)
                result[g] = total


def middle_back(where, ym, yr, x1, x2, d, cq, gains, wq, ck, cv, wc):
    rows, width = x1.shape
    block = 208
    wide = rows_of(block, width)
    small = pl.BlockSpec((4, 64, 256), lambda i, s: (0, 0, 0))
    return pl.pallas_call(
        middle_back_kernel,
        grid_spec=pltpu.PrefetchScalarGridSpec(
            num_scalar_prefetch=1,
            grid=(rows // block,),
            in_specs=[wide] * 6 + [resident(a.shape) for a in (gains, *wq, *ck, *cv, *wc)],
            out_specs=[wide] * 4 + [small, small, pl.BlockSpec((8, width), lambda i, s: (0, 0))],
            scratch_shapes=[pltpu.VMEM((4, 256, 256), FULL)] * 2,
        ),
        out_shape=[shape((rows, width), FULL)]
        + [shape((rows, width), ROUND)] * 3
        + [shape((4, 64, 256), FULL)] * 2
        + [shape((8, width), FULL)],
        compiler_params=params(40),
        cost_estimate=cost(7e9, 25e6),
        name="middle_back",
    )(where, ym, yr, x1, x2, d, cq, gains, *wq, *ck, *cv, *wc)


def first_back_kernel(where_ref, *refs):
    grads = refs[:6]
    w0_ref, w1_ref, y_ref = refs[6:]
    y = 0.0
    for g in range(2):
        for c in range(3):
            y = y + nt(grads[3 * g + c][...], (w0_ref, w1_ref)[g][c])
    y_ref[...] = y.astype(y_ref.dtype)


def first_back(half, grads, weights, kind):
    span = grads[0].shape[0]
    rows = span // 2
    width = weights[0].shape[1]
    block = 208
    steps = rows // block
    piece = pl.BlockSpec((block, 256), lambda i, s: (s[0] * steps + i, 0))
    return pl.pallas_call(
        first_back_kernel,
        grid_spec=pltpu.PrefetchScalarGridSpec(
            num_scalar_prefetch=1,
            grid=(steps,),
            in_specs=[piece] * 6 + [resident(a.shape) for a in weights],
            out_specs=rows_of(block, width),
        ),
        out_shape=shape((rows, width), kind),
        compiler_params=params(24),
        cost_estimate=cost(2 * rows * width * 1536, 8e6),
        name="first_back",
    )(half, *grads, *weights)


def frames_back_kernel(where_ref, ym_ref, yr_ref, dx1_ref, frame_ref, gain_ref, out_ref, sums_ref):
    @pl.when(pl.program_id(0) == 0)
    def _():
        sums_ref[...] = jnp.zeros_like(sums_ref)

    y = ym_ref[...] + yr_ref[...].astype(FULL)
    scaled, inverse = norm_parts(frame_ref[...].astype(FULL))
    sums_ref[0:1, :] += jnp.sum(y * scaled, axis=0, keepdims=True)
    sums_ref[1:2, :] += jnp.sum(y, axis=0, keepdims=True)
    out_ref[...] = lower(dx1_ref[...] + norm_pull(y, scaled, inverse, gain_ref[0:1, :]))


def frames_back(where, ym, yr, dx1, frames, gains):
    rows, width = dx1.shape
    block = 208
    wide = rows_of(block, width)
    return pl.pallas_call(
        frames_back_kernel,
        grid_spec=pltpu.PrefetchScalarGridSpec(
            num_scalar_prefetch=1,
            grid=(rows // block,),
            in_specs=[wide] * 4 + [resident(gains.shape)],
            out_specs=[wide, pl.BlockSpec((8, width), lambda i, s: (0, 0))],
        ),
        out_shape=[shape((rows, width), ROUND), shape((8, width), FULL)],
        compiler_params=params(24),
        cost_estimate=cost(1e7, 12e6),
        name="frames_back",
    )(where, ym, yr, dx1, frames, gains)


def chip_local(
    frames, text_states, lengths, loss_mask, norm_gain, norm_bias, w_qkv, w_out, w_cross_q,
    w_cross_kv, w_cross_out, w_up, w_down, cotangent,
):
    at = lax.axis_index("narrow")
    core = at % 2
    side = at // 2
    column = lax.axis_index("wide") % 2
    layer = lax.axis_index("wide") // 2
    where = core.reshape(1).astype(jnp.int32)
    away = (1 - core).reshape(1).astype(jnp.int32)
    limit = lax.dynamic_slice(lengths, (side,), (1,))
    rows, width = frames.shape
    join = lax.optimization_barrier

    def over_core(v):
        return lax.ppermute(v, "narrow", CORE_PAIRS)

    def over_y(v):
        return lax.ppermute(v, "narrow", Y_PAIRS)

    def along_wide(v, pairs):
        return lax.ppermute(v, "wide", pairs)

    def half_of(v, which):
        half = v.shape[0] // 2
        return lax.dynamic_slice_in_dim(v, which * half, half, axis=0)

    def ordered(first, second, which):
        return jnp.where(
            which == 0,
            jnp.concatenate([first, second], axis=0),
            jnp.concatenate([second, first], axis=0),
        )

    near = layer % 2

    def ask(v, which):
        return over_y(half_of(v, which))

    inward = jnp.concatenate([w_cross_q, w_cross_kv.reshape(2 * width, 256)], axis=0)
    outward = jnp.concatenate([w_out, w_cross_out], axis=0)
    qkv_first = ask(w_qkv.reshape(3 * width, 256), near)
    scaled, _ = norm_parts(frames.astype(FULL))
    h1 = lower(scaled * norm_gain[0] + norm_bias[0])
    h1_other = over_core(h1)
    dout = jnp.where(loss_mask[:, None] != 0, cotangent, jnp.zeros((), ROUND))
    q0, k0, v0 = project(where, h1, h1_other, w_qkv, False)

    q0, qkv_first, inward, outward, dout = join((q0, qkv_first, inward, outward, dout))
    qkv_second = along_wide(qkv_first, Z_NEAR)
    outward_first = ask(outward, column)
    inward_first = ask(inward, column)
    own_wo = over_core(outward)
    own_wq = over_core(w_cross_q)
    dout_other = over_core(dout)
    o0, lse0 = self_forward(limit, q0, k0, v0)

    o0, qkv_second, w_up_sent = join((o0, qkv_second, w_up))
    qkv_y = ordered(qkv_first, qkv_second, near).reshape(3, width, 256)
    q1, k1, v1 = project(where, h1, h1_other, qkv_y, False)

    def away_rows(v):
        return half_of(v, 1 - core)

    o0_other = over_core(away_rows(o0))
    q1, outward_first, inward_first, w_up_sent, o0_other, own_wo, own_wq = join(
        (q1, outward_first, inward_first, w_up_sent, o0_other, own_wo, own_wq)
    )
    outward_second = along_wide(outward_first, X_PAIRS)
    inward_second = along_wide(inward_first, X_PAIRS)
    up_first = ask(w_up_sent, column)
    o1, lse1 = self_forward(limit, q1, k1, v1)
    o1_other = over_core(away_rows(o1))

    o1, outward_second, inward_second, up_first, w_down_sent = join(
        (o1, outward_second, inward_second, up_first, w_down)
    )
    up_second = along_wide(up_first, X_PAIRS)
    down_first = ask(w_down_sent, near)
    outward_y = ordered(outward_first, outward_second, column)
    inward_y = ordered(inward_first, inward_second, column)
    out_y = outward_y[:256]
    cross_out_y = outward_y[256:]
    cross_q_y = inward_y[:width]
    cross_kv_y = inward_y[width:].reshape(2, width, 256)
    y_wo = over_core(outward_y)
    y_wq = over_core(cross_q_y)
    wo = (w_out, out_y, own_wo[:256], y_wo[:256])
    wc = (w_cross_out, cross_out_y, own_wo[256:], y_wo[256:])
    wq = (w_cross_q, cross_q_y, own_wq, y_wq)
    text = lax.dynamic_slice(text_states, (side, 0, 0), (1, *text_states.shape[1:]))[0]
    pair = jnp.stack(
        [jnp.stack([lower(nn(text, w[c])) for c in range(2)]) for w in (w_cross_kv, cross_kv_y)]
    )
    pair_other = over_core(pair)
    head_of = jnp.arange(256) // HEAD
    same = head_of[:, None] == head_of[None, :]

    def spread_heads(v):
        return jnp.where(same, jnp.tile(v, (1, 4, 1)), jnp.zeros((), ROUND))

    ck = (spread_heads(pair[:, 0]), spread_heads(pair_other[:, 0]))
    cv = (spread_heads(pair[:, 1]), spread_heads(pair_other[:, 1]))
    x1, x2, h2, cq, ca, h3 = middle_forward(
        where, frames, (o0, o1), (o0_other, o1_other), norm_gain, norm_bias, wo, wq, ck, cv, wc
    )
    h3_other = over_core(h3)
    h2_other = over_core(h2)
    ca_other = over_core(ca[:, 512:])

    h3, up_second, down_first = join((h3, up_second, down_first))
    down_second = along_wide(down_first, Z_NEAR)
    up_y = ordered(up_first, up_second, column)
    g0, du0, out_m, y_m = feed(where, h3, dout, w_up, w_down, FULL)
    g0, du0, out_o, y_o = feed(
        where, h3_other, dout_other, w_up, w_down, FULL, shared=(g0, du0)
    )
    y_o, down_second = join((y_o, down_second))
    down_y = ordered(down_first, down_second, near)
    h3_rows = jnp.concatenate([h3, h3_other], axis=0)
    dout_rows = jnp.concatenate([dout, dout_other], axis=0)
    g1, du1, out_m, y_m = feed(where, h3, dout, up_y, down_y, FULL, before=(out_m, y_m))
    g1, du1, out_o, y_o = feed(
        where, h3_other, dout_other, up_y, down_y, ROUND, before=(out_o, y_o), shared=(g1, du1)
    )
    y_received = over_core(y_o)

    def plus(a, b):
        return lower(a.astype(FULL) + b.astype(FULL))

    class Sum:
        def __init__(self, partner):
            self.fly = over_y(partner)

        def x(self, own):
            away_half = lower(half_of(own, 1 - column) + half_of(self.fly, 1 - column).astype(FULL))
            self.kept = half_of(own, column) + half_of(self.fly, column).astype(FULL)
            self.fly = along_wide(away_half, X_PAIRS)

        def near(self):
            total = self.kept + self.fly.astype(FULL)
            self.kept = half_of(total, near)
            self.fly = along_wide(lower(half_of(total, 1 - near)), Z_NEAR)

        def far(self):
            self.kept = plus(self.kept, self.fly)
            self.fly = along_wide(self.kept, Z_FAR)

        def back(self):
            self.kept = plus(self.kept, self.fly)
            self.fly = along_wide(self.kept, Z_NEAR)

        def along(self):
            self.kept = ordered(self.kept, self.fly, near)
            self.fly = along_wide(self.kept, X_PAIRS)

        def end(self):
            return ordered(self.kept, self.fly, column).astype(FULL)

    def sync(sums_in_flight, *values):
        done = join((*[each.fly for each in sums_in_flight], *values))
        for each, fly in zip(sums_in_flight, done):
            each.fly = fly
        return done[len(sums_in_flight) :]

    up1 = lower(tn(h3_rows, du1))
    up1, g1 = join((up1, g1))
    up = Sum(up1)
    down1 = lower(tn(g1, dout_rows))
    up0 = tn(h3_rows, du0)
    down0 = tn(g0, dout_rows)
    dx1, dself, dcross, dcq, dck, dcv, sums = middle_back(
        where, y_m, y_received, x1, x2, dout, cq, norm_gain, wq, ck, cv, wc
    )
    dself, down1, up0, down0 = sync([up], dself, down1, up0, down0)

    down = Sum(down1)
    up.x(up0)
    dself_other = over_core(dself)
    dcross_other = over_core(dcross)
    dcq_other = over_core(dcq[:, 512:])
    d_pair = jnp.stack([dck, dcv], axis=1)
    d_pair = lower(d_pair[:2] + over_core(d_pair[2:]))
    do0, do1 = project(where, dself, dself_other, jnp.stack([w_out, out_y]), True)
    do1, dcross_other, dcq_other = join((do1, dcross_other, dcq_other))
    dq1, dk1, dv1 = self_back(limit, q1, k1, v1, o1, do1, lse1)
    dq1, dcross_other = sync([up], dq1, dcross_other)

    up.near()
    h1_rows = ordered(h1, h1_other, core)
    qkv1 = lower(jnp.concatenate([tn(h1_rows, g) for g in (dq1, dk1, dv1)], axis=0))
    dself_rows = ordered(dself, dself_other, core)
    dcross_rows = jnp.concatenate([dcross, dcross_other], axis=0)
    h2_rows = jnp.concatenate([h2, h2_other], axis=0)

    def both(mine, other, g):
        lanes = slice(g * 256, (g + 1) * 256)
        return jnp.concatenate([mine[:, lanes], other[:, lanes]], axis=0)

    def into(g):
        return jnp.concatenate(
            [tn(h2_rows, both(dcq, dcq_other, g)), tn(text, d_pair[g, 0]), tn(text, d_pair[g, 1])],
            axis=0,
        )

    def outof(g, o):
        return jnp.concatenate(
            [tn(o, dself_rows), tn(both(ca, ca_other, g), dcross_rows)], axis=0
        )

    into1 = lower(into(1))
    qkv1, into1, do0 = sync([down, up], qkv1, into1, do0)

    qkv = Sum(qkv1)
    down.x(down0)
    up.far()
    dq0, dk0, dv0 = self_back(limit, q0, k0, v0, o0, do0, lse0)
    dq0, dself_rows, dcross_rows = sync([down, up], dq0, dself_rows, dcross_rows)

    down.near()
    up.back()
    grads = (dq0, dk0, dv0, dq1, dk1, dv1)
    yo = first_back(away, grads, (w_qkv, qkv_y), ROUND)
    y_received = over_core(yo)
    qkv0 = jnp.concatenate([tn(h1_rows, g) for g in (dq0, dk0, dv0)], axis=0)
    outof1 = lower(outof(1, o1))
    ym = first_back(where, grads, (w_qkv, qkv_y), FULL)
    qkv0, ym, y_received, outof1 = sync([qkv, down, up], qkv0, ym, y_received, outof1)

    cross_in = Sum(into1)
    qkv.x(qkv0)
    down.far()
    up.along()
    grad_frames, first_sums = frames_back(where, ym, y_received, dx1, frames, norm_gain)
    sums = sums + first_sums
    sums_other = over_core(sums)
    into0 = into(0)
    outof0 = outof(0, o0)
    text_part = 0.0
    for g, weights in ((0, w_cross_kv), (1, cross_kv_y)):
        for c in range(2):
            text_part = text_part + nt(d_pair[g, c], weights[c])
    text_other = over_core(text_part)
    sums_other, text_other, into0, outof0, grad_frames = sync(
        [qkv, down], sums_other, text_other, into0, outof0, grad_frames
    )

    qkv.near()
    down.back()
    sums = sums + sums_other
    sums_other = over_y(sums)
    text_grad = lower(text_part + text_other)
    text_away = over_y(text_grad)
    out_rows = lower(x2 + out_m + over_core(out_o).astype(FULL))
    sums_other, text_away, out_rows = sync(
        [cross_in, qkv, down, up], sums_other, text_away, out_rows
    )

    outs = Sum(outof1)
    cross_in.x(into0)
    qkv.far()
    down.along()
    sums = sums + sums_other
    sums_other = along_wide(sums, X_PAIRS)
    grad_up = up.end()
    sums_other, grad_up = sync([cross_in, qkv], sums_other, grad_up)

    cross_in.near()
    qkv.back()
    sums = sums + sums_other
    sums_other = along_wide(sums, Z_NEAR)
    grad_text = ordered(text_grad[None], text_away[None], side)
    sums_other, grad_text = sync([outs, cross_in, qkv], sums_other, grad_text)

    outs.x(outof0)
    cross_in.far()
    qkv.along()
    sums = sums + sums_other
    sums_other = along_wide(sums, Z_FAR)
    (down.fly,) = join((down.fly,))
    grad_down = down.end()
    sums_other, grad_down = sync([outs, cross_in], sums_other, grad_down)

    outs.near()
    cross_in.back()
    sums = sums + sums_other
    sync([outs, cross_in])

    outs.far()
    cross_in.along()
    grad_qkv = qkv.end().reshape(3, width, 256)
    (grad_qkv,) = sync([outs], grad_qkv)

    outs.back()
    sync([outs])

    outs.along()
    grad_cross_in = cross_in.end()
    grad_outs = outs.end()
    return (
        out_rows,
        grad_frames,
        grad_text,
        sums[0:6:2],
        sums[1:6:2],
        grad_qkv,
        grad_outs[:256],
        grad_cross_in[:width],
        grad_cross_in[width:].reshape(2, width, 256),
        grad_outs[256:],
        grad_up,
        grad_down,
    )


def solution(mesh):
    chips = dict(mesh.shape) == {"wide": 8, "narrow": 4}
    return jax.shard_map(
        chip_local if chips else general_local,
        mesh=mesh,
        in_specs=(
            P(("wide", "narrow"), None),
            P("wide", None, None),
            P("wide"),
            P(("wide", "narrow")),
            P(),
            P(),
            P(None, None, "narrow"),
            P("narrow", None),
            P(None, "narrow"),
            P(None, None, "narrow"),
            P("narrow", None),
            P(None, "narrow"),
            P("narrow", None),
            P(("wide", "narrow"), None),
        ),
        out_specs=(
            P(("wide", "narrow"), None),
            P(("wide", "narrow"), None),
            P("wide", None, None),
            P(),
            P(),
            P(None, None, "narrow"),
            P("narrow", None),
            P(None, "narrow"),
            P(None, None, "narrow"),
            P("narrow", None),
            P(None, "narrow"),
            P("narrow", None),
        ),
        check_vma=False,
    )
```

```python
import functools

import jax
import jax.numpy as jnp
from jax import lax
from jax.experimental import pallas as pl
from jax.experimental.pallas import tpu as pltpu
from jax.sharding import PartitionSpec as P

HEAD = 64


EPS = 1e-05
NEG = -1e30


def lower(values_in):
    return values_in.astype(jnp.bfloat16)


def product(left_side, right_side, transposed):
    if transposed:
        return lax.dot_general(
            left_side, right_side, (((1,), (1,)), ((), ())), preferred_element_type=jnp.float32
        )
    return jnp.dot(left_side, right_side, preferred_element_type=jnp.float32)


def outer_sum(left_side, right_side):
    return lax.dot_general(
        left_side, right_side, (((0,), (0,)), ((), ())), preferred_element_type=jnp.float32
    )


def normalize(values_in, gain_row, bias_row):
    row_mean = jnp.mean(values_in, axis=-1, keepdims=True)
    centered = values_in - row_mean
    inverse = lax.rsqrt(jnp.mean(centered * centered, axis=-1, keepdims=True) + EPS)
    scaled = centered * inverse
    return (scaled * gain_row + bias_row, scaled, inverse)


def normalize_back(upstream, scaled, inverse, gain_row):
    weighted = upstream * gain_row
    inner_mean = jnp.mean(weighted, axis=-1, keepdims=True)
    along_mean = jnp.mean(weighted * scaled, axis=-1, keepdims=True)
    grad_input = inverse * (weighted - inner_mean - scaled * along_mean)
    return (grad_input, jnp.sum(upstream * scaled, axis=0), jnp.sum(upstream, axis=0))


def gelu_parts(values_in):
    normal_cdf = 0.5 * (1.0 + jax.scipy.special.erf(values_in * 0.7071067811865476))
    normal_pdf = jnp.exp(-0.5 * values_in * values_in) * 0.3989422804014327
    return (values_in * normal_cdf, normal_cdf + values_in * normal_pdf)


def scores_of(query_part, key_part, valid):
    scores = jnp.einsum(
        "bhe,khe->hbk", query_part, key_part, preferred_element_type=jnp.float32
    ) * HEAD ** (-0.5)
    return jnp.where(valid, scores, NEG)


def attend(query_part, key_part, value_part, valid):
    scores = scores_of(query_part, key_part, valid)
    row_top = jnp.max(scores, axis=-1, keepdims=True)
    weights_exp = jnp.exp(scores - row_top)
    denominator = jnp.sum(weights_exp, axis=-1, keepdims=True)
    probability = weights_exp / denominator
    mixed = jnp.einsum(
        "hbk,khe->bhe", lower(probability), value_part, preferred_element_type=jnp.float32
    )
    return (lower(mixed), (row_top + jnp.log(denominator))[..., 0])


def attend_back(query_part, key_part, value_part, valid, summary, upstream):
    scores = scores_of(query_part, key_part, valid)
    probability = jnp.exp(scores - summary[..., None])
    pressure = jnp.einsum("bhe,khe->hbk", upstream, value_part, preferred_element_type=jnp.float32)
    grad_scores = lower(
        probability * (pressure - jnp.sum(probability * pressure, axis=-1, keepdims=True))
    )
    factor = HEAD ** (-0.5)
    grad_query = (
        jnp.einsum("hbk,khe->bhe", grad_scores, key_part, preferred_element_type=jnp.float32)
        * factor
    )
    grad_key = (
        jnp.einsum("hbk,bhe->khe", grad_scores, query_part, preferred_element_type=jnp.float32)
        * factor
    )
    grad_value = jnp.einsum(
        "hbk,bhe->khe", lower(probability), upstream, preferred_element_type=jnp.float32
    )
    return (grad_query, grad_key, grad_value)


def general_local(
    frames,
    text_states,
    lengths,
    loss_mask,
    norm_gain,
    norm_bias,
    w_qkv,
    w_out,
    w_cross_q,
    w_cross_kv,
    w_cross_out,
    w_up,
    w_down,
    cotangent,
):
    row_count = frames.shape[0]
    width = frames.shape[1]
    item_count = lengths.shape[0]
    span = row_count * lax.axis_size("narrow") // item_count
    half_span = span // 2
    inner_width = w_qkv.shape[2]
    head_count = inner_width // HEAD
    text_count = text_states.shape[1]
    full_rows = item_count * span
    places = jnp.arange(span, dtype=jnp.int32)

    def spread(shard_rows):
        return lax.all_gather(shard_rows, "narrow", axis=0, tiled=True)

    def collect(left_side, right_side, transposed):
        return lax.psum_scatter(
            product(
                lax.slice_in_dim(left_side, 0, lax.axis_size("narrow") * row_count, axis=0),
                right_side,
                transposed,
            ),
            "narrow",
            scatter_dimension=0,
            tiled=True,
        )

    def causal(block_index, item_limit):
        query_place = block_index * half_span + jnp.arange(half_span, dtype=jnp.int32)
        return (places[None, :] <= query_place[:, None]) & (places[None, :] < item_limit)

    frame_rows = frames.astype(jnp.float32)
    normed_one, scaled_one, inverse_one = normalize(frame_rows, norm_gain[0], norm_bias[0])
    first_input = spread(lower(normed_one))
    triple = lower(
        jnp.einsum("rd,cde->cre", first_input, w_qkv, preferred_element_type=jnp.float32)
    )
    triple = triple.reshape(3, item_count, span, head_count, HEAD)

    def self_item(packed):
        query_part, key_part, value_part, item_limit = packed
        mixed_list = []
        summary_list = []
        for block_index in range(2):
            mixed, summary = attend(
                query_part[block_index * half_span : (block_index + 1) * half_span],
                key_part,
                value_part,
                causal(block_index, item_limit),
            )
            mixed_list.append(mixed)
            summary_list.append(summary)
        return (jnp.concatenate(mixed_list, axis=0), jnp.stack(summary_list, axis=0))

    attended, self_summary = lax.map(self_item, (triple[0], triple[1], triple[2], lengths))
    attended_flat = attended.reshape(full_rows, inner_width)
    first_rows = frame_rows + collect(attended_flat, w_out, False)
    normed_two, scaled_two, inverse_two = normalize(first_rows, norm_gain[1], norm_bias[1])
    second_input = spread(lower(normed_two))
    cross_query = lower(product(second_input, w_cross_q, False)).reshape(
        item_count, span, head_count, HEAD
    )
    cross_pair = lower(
        jnp.einsum("ntd,cde->cnte", text_states, w_cross_kv, preferred_element_type=jnp.float32)
    )
    cross_pair = cross_pair.reshape(2, item_count, text_count, head_count, HEAD)

    def cross_item(packed):
        query_part, key_part, value_part = packed
        return attend(query_part, key_part, value_part, True)

    cross_mixed, cross_summary = lax.map(cross_item, (cross_query, cross_pair[0], cross_pair[1]))
    cross_flat = cross_mixed.reshape(full_rows, inner_width)
    second_rows = first_rows + collect(cross_flat, w_cross_out, False)
    normed_three, scaled_three, inverse_three = normalize(second_rows, norm_gain[2], norm_bias[2])
    upstream = cotangent.astype(jnp.float32) * loss_mask.astype(jnp.float32)[:, None]
    ffn_grad = lower(upstream)
    ffn_input = spread(lower(normed_three))
    hidden_pre = product(ffn_input, w_up, False)
    active, slope = gelu_parts(hidden_pre)
    active = lower(active)
    out_rows = second_rows + collect(active, w_down, False)
    ffn_full = spread(ffn_grad)
    grad_down = outer_sum(active, ffn_full)
    grad_hidden = lower(product(ffn_full, w_down, True) * slope)
    grad_up = outer_sum(ffn_input, grad_hidden)
    back_three = collect(grad_hidden, w_up, True)
    grad_up, grad_down = (grad_up, grad_down)
    grad_in_three, gain_three, bias_three = normalize_back(
        back_three, scaled_three, inverse_three, norm_gain[2]
    )
    grad_second = upstream + grad_in_three
    cross_full = spread(lower(grad_second))
    grad_cross_out = outer_sum(cross_flat, cross_full)
    cross_upstream = lower(product(cross_full, w_cross_out, True)).reshape(
        item_count, span, head_count, HEAD
    )

    def cross_back(packed):
        query_part, key_part, value_part, summary, upstream_item = packed
        return attend_back(query_part, key_part, value_part, True, summary, upstream_item)

    grad_cq, grad_ck, grad_cv = lax.map(
        cross_back, (cross_query, cross_pair[0], cross_pair[1], cross_summary, cross_upstream)
    )
    grad_cq = lower(grad_cq).reshape(full_rows, inner_width)
    grad_pair = lower(jnp.stack((grad_ck, grad_cv), axis=0)).reshape(
        2, item_count, text_count, inner_width
    )
    grad_cross_q = outer_sum(second_input, grad_cq)
    grad_cross_kv = jnp.einsum(
        "ntd,cnte->cde", text_states, grad_pair, preferred_element_type=jnp.float32
    )
    grad_cross_q, grad_cross_kv, grad_cross_out = (grad_cross_q, grad_cross_kv, grad_cross_out)
    text_partial = jnp.einsum(
        "cnte,cde->ntd", grad_pair, w_cross_kv, preferred_element_type=jnp.float32
    )
    grad_text = lower(lax.psum(text_partial, "narrow"))
    back_two = collect(grad_cq, w_cross_q, True)
    grad_in_two, gain_two, bias_two = normalize_back(
        back_two, scaled_two, inverse_two, norm_gain[1]
    )
    grad_first = grad_second + grad_in_two
    self_full = spread(lower(grad_first))
    grad_out = outer_sum(attended_flat, self_full)
    self_upstream = lower(product(self_full, w_out, True)).reshape(
        item_count, span, head_count, HEAD
    )

    def self_back(packed):
        query_part, key_part, value_part, item_limit, summary, upstream_item = packed
        query_list = []
        key_list = []
        value_list = []
        for block_index in range(2):
            lower_row = block_index * half_span
            grad_query, grad_key, grad_value = attend_back(
                query_part[lower_row : lower_row + half_span],
                key_part,
                value_part,
                causal(block_index, item_limit),
                summary[block_index],
                upstream_item[lower_row : lower_row + half_span],
            )
            query_list.append(grad_query)
            key_list.append(grad_key)
            value_list.append(grad_value)
        return (
            jnp.concatenate(query_list, axis=0),
            key_list[0] + key_list[1],
            value_list[0] + value_list[1],
        )

    grad_q, grad_k, grad_v = lax.map(
        self_back, (triple[0], triple[1], triple[2], lengths, self_summary, self_upstream)
    )
    grad_triple = lower(jnp.stack((grad_q, grad_k, grad_v), axis=0)).reshape(
        3, full_rows, inner_width
    )
    grad_qkv = jnp.einsum(
        "rd,cre->cde", first_input, grad_triple, preferred_element_type=jnp.float32
    )
    grad_qkv, grad_out = (grad_qkv, grad_out)
    merged = grad_triple.transpose(1, 0, 2).reshape(full_rows, 3 * inner_width)
    stacked_weights = w_qkv.transpose(0, 2, 1).reshape(3 * inner_width, width)
    back_one = collect(merged, stacked_weights, False)
    grad_in_one, gain_one, bias_one = normalize_back(
        back_one, scaled_one, inverse_one, norm_gain[0]
    )
    grad_frames = lower(grad_first + grad_in_one)
    gain_terms = jnp.stack((gain_one, gain_two, gain_three), axis=0)
    bias_terms = jnp.stack((bias_one, bias_two, bias_three), axis=0)
    grad_norm_gain, grad_norm_bias = lax.psum((gain_terms, bias_terms), ("wide", "narrow"))
    grad_qkv, grad_out, grad_cross_q, grad_cross_kv, grad_cross_out, grad_up, grad_down = lax.psum(
        (grad_qkv, grad_out, grad_cross_q, grad_cross_kv, grad_cross_out, grad_up, grad_down),
        "wide",
    )
    return (
        lower(out_rows),
        grad_frames,
        grad_text,
        grad_norm_gain,
        grad_norm_bias,
        grad_qkv,
        grad_out,
        grad_cross_q,
        grad_cross_kv,
        grad_cross_out,
        grad_up,
        grad_down,
    )


ROUND = jnp.bfloat16
FULL = jnp.float32
CORE_PAIRS = ((0, 1), (1, 0), (2, 3), (3, 2))
Y_PAIRS = ((0, 2), (2, 0), (1, 3), (3, 1))
X_PAIRS = tuple((i, i ^ 1) for i in range(8))
Z_INWARD = ((0, 2), (1, 3), (6, 4), (7, 5))
Z_MIDDLE = ((2, 4), (4, 2), (3, 5), (5, 3))
Z_OUTWARD = ((2, 0), (3, 1), (4, 6), (5, 7))
Z_NEAR = tuple((i, i ^ 2) for i in range(8))
Z_FAR = tuple((i, i ^ 4) for i in range(8))
MIB = 1 << 20


def nt(a, b):
    return lax.dot_general(a, b, (((1,), (1,)), ((), ())), preferred_element_type=FULL)


def nn(a, b):
    return lax.dot_general(a, b, (((1,), (0,)), ((), ())), preferred_element_type=FULL)


def tn(a, b):
    return lax.dot_general(a, b, (((0,), (0,)), ((), ())), preferred_element_type=FULL)


def shape(dims, kind):
    return jax.ShapeDtypeStruct(dims, kind)


def resident(dims):
    zeros = (0,) * len(dims)
    return pl.BlockSpec(dims, lambda i, s: zeros, pipeline_mode=pl.Buffered(1))


def rows_of(block, width):
    return pl.BlockSpec((block, width), lambda i, s: (i, 0))


def brief():
    return pl.CostEstimate(flops=1000, bytes_accessed=1000, transcendentals=0)


def params(mib):
    return pltpu.CompilerParams(vmem_limit_bytes=mib * MIB)


def norm_parts(v):
    centered = v - jnp.mean(v, axis=-1, keepdims=True)
    inverse = lax.rsqrt(jnp.mean(centered * centered, axis=-1, keepdims=True) + EPS)
    return centered * inverse, inverse


def norm_pull(y, scaled, inverse, gain_row):
    weighted = y * gain_row
    inner = jnp.mean(weighted, axis=-1, keepdims=True)
    along = jnp.mean(weighted * scaled, axis=-1, keepdims=True)
    return inverse * (weighted - inner - scaled * along)


def project_kernel(where_ref, mine_ref, other_ref, weight_ref, *out_refs, transposed, count):
    half = pl.program_id(0)

    def run(source):
        for c in range(count):
            if transposed:
                result = nt(source[...], weight_ref[c])
            else:
                result = nn(source[...], weight_ref[c])
            out_refs[c][...] = lower(result)

    @pl.when(half == 0)
    def _():
        run(mine_ref)

    @pl.when(half == 1)
    def _():
        run(other_ref)


def project(where, mine, other, weights, transposed):
    rows, depth = mine.shape
    count = weights.shape[0]
    wide = weights.shape[1] if transposed else weights.shape[2]
    whole = pl.BlockSpec((rows, depth), lambda i, s: (0, 0), pipeline_mode=pl.Buffered(1))
    out = pl.BlockSpec((rows, wide), lambda i, s: ((i + s[0]) % 2, 0))
    return pl.pallas_call(
        functools.partial(project_kernel, transposed=transposed, count=count),
        grid_spec=pltpu.PrefetchScalarGridSpec(
            num_scalar_prefetch=1,
            grid=(2,),
            in_specs=[whole, whole, resident(weights.shape)],
            out_specs=[out] * count,
        ),
        out_shape=[shape((2 * rows, wide), ROUND)] * count,
        compiler_params=params(32),
        cost_estimate=brief(),
        name="project",
    )(where, mine, other, weights)


def blocks_of(span, block):
    return [(start, min(block, span - start)) for start in range(0, span, block)]


def self_forward_kernel(limit_ref, q_ref, k_ref, v_ref, o_ref, lse_ref, *, span, floor, block):
    limit = limit_ref[0]
    lane = lax.broadcasted_iota(jnp.int32, (1, 128), 1)
    zero = jnp.zeros((), ROUND)
    for start, size in blocks_of(span, block):
        end = start + size
        mixed_list = []
        for h in range(2):
            own_lanes = (lane < HEAD) if h == 0 else (lane >= HEAD)
            query = jnp.where(own_lanes, q_ref[start:end, :] * HEAD ** (-0.5), zero)
            cuts = [(0, start)] if start <= floor else [(0, floor), (floor, start)]
            parts = []
            for low, high in cuts + [(start, end)]:
                if low == high:
                    continue
                scores = nt(query, k_ref[low:high, :])
                key = lax.broadcasted_iota(jnp.int32, (size, high - low), 1)
                if low == start:
                    valid = key <= lax.broadcasted_iota(jnp.int32, (size, high - low), 0)
                    if high > floor:
                        valid = valid & (key + low < limit)
                    scores = jnp.where(valid, scores, NEG)
                elif high > floor:
                    scores = jnp.where(key + low < limit, scores, NEG)
                parts.append((low, high, scores))
            top = functools.reduce(
                jnp.maximum, [jnp.max(s, axis=1, keepdims=True) for _, _, s in parts]
            )
            total = 0.0
            mixed = 0.0
            for low, high, scores in parts:
                weights_exp = jnp.exp(scores - top)
                total = total + jnp.sum(weights_exp, axis=1, keepdims=True)
                mixed = mixed + nn(lower(weights_exp), v_ref[low:high, :])
            mixed_list.append(mixed / total)
            summary = jnp.broadcast_to(top + jnp.log(total), (size, 128))
            lse_ref[0, h : h + 1, start:end] = summary.T[0:1, :]
        o_ref[start:end, :] = lower(jnp.where(lane < HEAD, mixed_list[0], mixed_list[1]))


def self_forward(limit, q, k, v):
    span, wide = q.shape
    pairs = wide // 128
    floor = (span - span // 8 + 1) // 128 * 128
    pair = pl.BlockSpec((span, 128), lambda p, s: (0, p))
    return pl.pallas_call(
        functools.partial(self_forward_kernel, span=span, floor=floor, block=256),
        grid_spec=pltpu.PrefetchScalarGridSpec(
            num_scalar_prefetch=1,
            grid=(pairs,),
            in_specs=[pair] * 3,
            out_specs=[pair, pl.BlockSpec((1, 8, span), lambda p, s: (p, 0, 0))],
        ),
        out_shape=[shape((span, wide), ROUND), shape((pairs, 8, span), FULL)],
        compiler_params=params(40),
        cost_estimate=brief(),
        name="self_forward",
    )(limit, q, k, v)


def self_back_kernel(
    limit_ref, q_ref, k_ref, v_ref, o_ref, do_ref, lse_ref, dq_ref, dk_ref, dv_ref, dqt,
    *, span, floor, block
):
    limit = limit_ref[0]
    lane = lax.broadcasted_iota(jnp.int32, (1, 128), 1)
    row = lax.broadcasted_iota(jnp.int32, (128, 1), 0)
    zero = jnp.zeros((), ROUND)
    factor = HEAD ** (-0.5)
    product_rows = do_ref[...].astype(FULL) * o_ref[...].astype(FULL)
    high = lower(product_rows)
    rest = lower(product_rows - high.astype(FULL))
    pick = lower(
        jnp.concatenate(
            [
                jnp.where(lane < HEAD, 1.0, 0.0),
                jnp.where(lane >= HEAD, 1.0, 0.0),
                jnp.zeros((6, 128), FULL),
            ],
            axis=0,
        )
    )
    delta = nt(pick, high) + nt(pick, rest)
    for start, size in blocks_of(span, block):
        end = start + size
        key = k_ref[start:end, :]
        value = v_ref[start:end, :]
        key_turned = key.T
        dk = 0.0
        dv = 0.0
        dq_add = 0.0
        for h in range(2):
            own_lanes = (lane < HEAD) if h == 0 else (lane >= HEAD)
            own_rows = (row < HEAD) if h == 0 else (row >= HEAD)
            query = jnp.where(own_lanes, q_ref[start:, :] * factor, zero)
            pulled = jnp.where(own_lanes, do_ref[start:, :], zero)
            probability = jnp.exp(nt(key, query) - lse_ref[0, h : h + 1, start:])
            pressure = nt(value, pulled)
            below = lax.broadcasted_iota(jnp.int32, (size, size), 0)
            across = lax.broadcasted_iota(jnp.int32, (size, size), 1)
            corner = jnp.where(below <= across, probability[:, :size], 0.0)
            if end < span:
                probability = jnp.concatenate([corner, probability[:, size:]], axis=1)
            else:
                probability = corner
            if end > floor:
                place = lax.broadcasted_iota(jnp.int32, (size, 1), 0) + start
                probability = jnp.where(place < limit, probability, 0.0)
            grad_scores = lower(probability * (pressure - delta[h : h + 1, start:]))
            dv = dv + nn(lower(probability), pulled)
            dk = dk + nn(grad_scores, query)
            dq_add = dq_add + nn(jnp.where(own_rows, key_turned, zero), grad_scores)
        dk_ref[start:end, :] = lower(dk)
        dv_ref[start:end, :] = lower(dv)
        if start == 0:
            dqt[...] = dq_add
        else:
            dqt[:, start:] += dq_add
    dq_ref[...] = lower(dqt[...].T * factor)


def self_back(limit, q, k, v, o, do, lse):
    span, wide = q.shape
    pairs = wide // 128
    floor = (span - span // 8 + 1) // 128 * 128
    pair = pl.BlockSpec((span, 128), lambda p, s: (0, p))
    return pl.pallas_call(
        functools.partial(self_back_kernel, span=span, floor=floor, block=256),
        grid_spec=pltpu.PrefetchScalarGridSpec(
            num_scalar_prefetch=1,
            grid=(pairs,),
            in_specs=[pair] * 5 + [pl.BlockSpec((1, 8, span), lambda p, s: (p, 0, 0))],
            out_specs=[pair] * 3,
            scratch_shapes=[pltpu.VMEM((128, span), FULL)],
        ),
        out_shape=[shape((span, wide), ROUND)] * 3,
        compiler_params=params(48),
        cost_estimate=brief(),
        name="self_back",
    )(limit, q, k, v, o, do, lse)


def by_head(values_in, reduce, empty):
    lane = lax.broadcasted_iota(jnp.int32, (1, 128), 1)
    pieces = []
    for start in range(0, values_in.shape[1], 128):
        part = values_in[:, start : start + 128]
        first = reduce(jnp.where(lane < HEAD, part, empty), axis=1, keepdims=True)
        second = reduce(jnp.where(lane >= HEAD, part, empty), axis=1, keepdims=True)
        pieces.append(jnp.where(lane < HEAD, first, second))
    return jnp.concatenate(pieces, axis=1)


def cross_probability(query, keys):
    scores = nt(query * HEAD ** (-0.5), keys)
    weights_exp = jnp.exp(scores - by_head(scores, jnp.max, NEG))
    return weights_exp / by_head(weights_exp, jnp.sum, 0.0)


def middle_forward_kernel(
    where_ref, frame_ref, a0_ref, a1_ref, a2_ref, a3_ref, gain_ref, bias_ref, *refs
):
    mixed = (a0_ref, a1_ref, a2_ref, a3_ref)
    wo, wq, wc = refs[0:4], refs[4:8], refs[12:16]
    ck0_ref, ck1_ref, cv0_ref, cv1_ref = refs[8:12]
    x1_ref, x2_ref, h2_ref, cq_ref, ca_ref, h3_ref = refs[16:]
    x1 = frame_ref[...].astype(FULL)
    for g in range(4):
        x1 = x1 + nn(mixed[g][...], wo[g][...])
    x1_ref[...] = x1
    scaled, _ = norm_parts(x1)
    h2 = lower(scaled * gain_ref[1:2, :] + bias_ref[1:2, :])
    h2_ref[...] = h2
    for g in range(4):
        lanes = slice(g * 256, (g + 1) * 256)
        cq = lower(nn(h2, wq[g][...]))
        cq_ref[:, lanes] = cq
        probability = cross_probability(cq, (ck0_ref, ck1_ref)[g // 2][g % 2])
        ca_ref[:, lanes] = lower(nn(lower(probability), (cv0_ref, cv1_ref)[g // 2][g % 2]))
    crossed = 0.0
    for g in range(4):
        crossed = crossed + nn(ca_ref[:, g * 256 : (g + 1) * 256], wc[g][...])
    x2 = x1_ref[...] + crossed
    x2_ref[...] = x2
    scaled, _ = norm_parts(x2)
    h3_ref[...] = lower(scaled * gain_ref[2:3, :] + bias_ref[2:3, :])


def middle_forward(where, frames, attended, received, gains, biases, wo, wq, ck, cv, wc):
    rows, width = frames.shape
    block = 208
    steps = rows // block
    piece = pl.BlockSpec((block, 256), lambda i, s: (s[0] * steps + i, 0))
    wide = rows_of(block, width)
    return pl.pallas_call(
        middle_forward_kernel,
        grid_spec=pltpu.PrefetchScalarGridSpec(
            num_scalar_prefetch=1,
            grid=(steps,),
            in_specs=[wide, piece, piece, rows_of(block, 256), rows_of(block, 256)]
            + [resident(a.shape) for a in (gains, biases, *wo, *wq, *ck, *cv, *wc)],
            out_specs=[wide] * 6,
        ),
        out_shape=[shape((rows, width), FULL)] * 2 + [shape((rows, width), ROUND)] * 4,
        compiler_params=params(40),
        cost_estimate=brief(),
        name="middle_forward",
    )(where, frames, *attended, *received, gains, biases, *wo, *wq, *ck, *cv, *wc)


def feed_kernel(where_ref, h_ref, d_ref, up_ref, down_ref, *refs, carried, shared):
    before = refs[: 2 * carried]
    g_ref, du_ref, out_ref, y_ref = refs[2 * carried + 2 * shared :]
    u = nn(h_ref[...], up_ref[...])
    active, slope = gelu_parts(u)
    g = lower(active)
    g_ref[...] = g
    du = lower(nt(d_ref[...], down_ref[...]) * slope)
    du_ref[...] = du
    out = nn(g, down_ref[...])
    y = nt(du, up_ref[...])
    if carried:
        out = before[0][...] + out
        y = before[1][...] + y
    out_ref[...] = out.astype(out_ref.dtype)
    y_ref[...] = y.astype(y_ref.dtype)


def feed(where, h, d, up, down, kind, before=(), shared=()):
    rows, width = h.shape
    block = 208
    steps = rows // block
    hidden = up.shape[1]
    wide = rows_of(block, width)
    first = steps if shared else 0
    kept = pl.BlockSpec((block, hidden), lambda i, s: (i + first, 0))
    there = pl.BlockSpec(memory_space=pl.ANY)
    carried = 1 if before else 0
    at = 5 + len(before)
    return pl.pallas_call(
        functools.partial(feed_kernel, carried=carried, shared=1 if shared else 0),
        grid_spec=pltpu.PrefetchScalarGridSpec(
            num_scalar_prefetch=1,
            grid=(steps,),
            in_specs=[wide, wide, resident(up.shape), resident(down.shape)]
            + [wide] * len(before)
            + [there] * len(shared),
            out_specs=[kept, kept, wide, wide],
        ),
        out_shape=[shape((2 * rows, hidden), ROUND)] * 2 + [shape((rows, width), kind)] * 2,
        input_output_aliases={at: 0, at + 1: 1} if shared else {},
        compiler_params=params(56),
        cost_estimate=brief(),
        name="feed",
    )(where, h, d, up, down, *before, *shared)


def middle_back_kernel(
    where_ref, ym_ref, yr_ref, x1_ref, x2_ref, d_ref, cq_ref, gain_ref, *refs
):
    wq, wc = refs[0:4], refs[8:12]
    ck0_ref, ck1_ref, cv0_ref, cv1_ref = refs[4:8]
    dx1_ref, dself_ref, dcross_ref, dcq_ref, dck_ref, dcv_ref, sums_ref = refs[12:19]
    dck_all, dcv_all = refs[19:]
    step = pl.program_id(0)

    @pl.when(step == 0)
    def _():
        dck_all[...] = jnp.zeros_like(dck_all)
        dcv_all[...] = jnp.zeros_like(dcv_all)
        sums_ref[...] = jnp.zeros_like(sums_ref)

    y3 = ym_ref[...] + yr_ref[...].astype(FULL)
    scaled, inverse = norm_parts(x2_ref[...])
    sums_ref[4:5, :] += jnp.sum(y3 * scaled, axis=0, keepdims=True)
    sums_ref[5:6, :] += jnp.sum(y3, axis=0, keepdims=True)
    dx2 = d_ref[...].astype(FULL) + norm_pull(y3, scaled, inverse, gain_ref[2:3, :])
    dx1_ref[...] = dx2
    dcross = lower(dx2)
    dcross_ref[...] = dcross
    y2 = 0.0
    for g in range(4):
        lanes = slice(g * 256, (g + 1) * 256)
        keys = (ck0_ref, ck1_ref)[g // 2][g % 2]
        values = (cv0_ref, cv1_ref)[g // 2][g % 2]
        dcatt = lower(nt(dcross, wc[g][...]))
        cq = cq_ref[:, lanes]
        probability = cross_probability(cq, keys)
        weighed = nt(dcatt, values)
        inner = by_head(probability * weighed, jnp.sum, 0.0)
        dcs = lower(probability * (weighed - inner))
        dcq = lower(nn(dcs, keys) * HEAD ** (-0.5))
        dcq_ref[:, lanes] = dcq
        dck_all[g] += tn(dcs, cq * HEAD ** (-0.5))
        dcv_all[g] += tn(lower(probability), dcatt)
        y2 = y2 + nt(dcq, wq[g][...])
    scaled, inverse = norm_parts(x1_ref[...])
    sums_ref[2:3, :] += jnp.sum(y2 * scaled, axis=0, keepdims=True)
    sums_ref[3:4, :] += jnp.sum(y2, axis=0, keepdims=True)
    dx1 = dx1_ref[...] + norm_pull(y2, scaled, inverse, gain_ref[1:2, :])
    dx1_ref[...] = dx1
    dself_ref[...] = lower(dx1)

    @pl.when(step == pl.num_programs(0) - 1)
    def _():
        for every, result in ((dck_all, dck_ref), (dcv_all, dcv_ref)):
            for g in range(4):
                total = 0.0
                for h in range(4):
                    lane = lax.broadcasted_iota(jnp.int32, (1, 256), 1) // HEAD
                    total = total + jnp.where(lane == h, every[g, h * 64 : (h + 1) * 64, :], 0.0)
                result[g] = total


def middle_back(where, ym, yr, x1, x2, d, cq, gains, wq, ck, cv, wc):
    rows, width = x1.shape
    block = 208
    wide = rows_of(block, width)
    small = pl.BlockSpec((4, 64, 256), lambda i, s: (0, 0, 0))
    return pl.pallas_call(
        middle_back_kernel,
        grid_spec=pltpu.PrefetchScalarGridSpec(
            num_scalar_prefetch=1,
            grid=(rows // block,),
            in_specs=[wide] * 6 + [resident(a.shape) for a in (gains, *wq, *ck, *cv, *wc)],
            out_specs=[wide] * 4 + [small, small, pl.BlockSpec((8, width), lambda i, s: (0, 0))],
            scratch_shapes=[pltpu.VMEM((4, 256, 256), FULL)] * 2,
        ),
        out_shape=[shape((rows, width), FULL)]
        + [shape((rows, width), ROUND)] * 3
        + [shape((4, 64, 256), FULL)] * 2
        + [shape((8, width), FULL)],
        compiler_params=params(40),
        cost_estimate=brief(),
        name="middle_back",
    )(where, ym, yr, x1, x2, d, cq, gains, *wq, *ck, *cv, *wc)


def first_back_kernel(where_ref, *refs):
    grads = refs[:6]
    w0_ref, w1_ref, y_ref = refs[6:]
    y = 0.0
    for g in range(2):
        for c in range(3):
            y = y + nt(grads[3 * g + c][...], (w0_ref, w1_ref)[g][c])
    y_ref[...] = y.astype(y_ref.dtype)


def first_back(half, grads, weights, kind):
    span = grads[0].shape[0]
    rows = span // 2
    width = weights[0].shape[1]
    block = 208
    steps = rows // block
    piece = pl.BlockSpec((block, 256), lambda i, s: (s[0] * steps + i, 0))
    return pl.pallas_call(
        first_back_kernel,
        grid_spec=pltpu.PrefetchScalarGridSpec(
            num_scalar_prefetch=1,
            grid=(steps,),
            in_specs=[piece] * 6 + [resident(a.shape) for a in weights],
            out_specs=rows_of(block, width),
        ),
        out_shape=shape((rows, width), kind),
        compiler_params=params(24),
        cost_estimate=brief(),
        name="first_back",
    )(half, *grads, *weights)


def frames_back_kernel(where_ref, ym_ref, yr_ref, dx1_ref, frame_ref, gain_ref, out_ref, sums_ref):
    @pl.when(pl.program_id(0) == 0)
    def _():
        sums_ref[...] = jnp.zeros_like(sums_ref)

    y = ym_ref[...] + yr_ref[...].astype(FULL)
    scaled, inverse = norm_parts(frame_ref[...].astype(FULL))
    sums_ref[0:1, :] += jnp.sum(y * scaled, axis=0, keepdims=True)
    sums_ref[1:2, :] += jnp.sum(y, axis=0, keepdims=True)
    out_ref[...] = lower(dx1_ref[...] + norm_pull(y, scaled, inverse, gain_ref[0:1, :]))


def frames_back(where, ym, yr, dx1, frames, gains):
    rows, width = dx1.shape
    block = 208
    wide = rows_of(block, width)
    return pl.pallas_call(
        frames_back_kernel,
        grid_spec=pltpu.PrefetchScalarGridSpec(
            num_scalar_prefetch=1,
            grid=(rows // block,),
            in_specs=[wide] * 4 + [resident(gains.shape)],
            out_specs=[wide, pl.BlockSpec((8, width), lambda i, s: (0, 0))],
        ),
        out_shape=[shape((rows, width), ROUND), shape((8, width), FULL)],
        compiler_params=params(24),
        cost_estimate=brief(),
        name="frames_back",
    )(where, ym, yr, dx1, frames, gains)


def chip_local(
    frames, text_states, lengths, loss_mask, norm_gain, norm_bias, w_qkv, w_out, w_cross_q,
    w_cross_kv, w_cross_out, w_up, w_down, cotangent,
):
    at = lax.axis_index("narrow")
    core = at % 2
    side = at // 2
    column = lax.axis_index("wide") % 2
    layer = lax.axis_index("wide") // 2
    where = core.reshape(1).astype(jnp.int32)
    away = (1 - core).reshape(1).astype(jnp.int32)
    limit = lax.dynamic_slice(lengths, (side,), (1,))
    rows, width = frames.shape
    join = lax.optimization_barrier

    def over_core(v):
        return lax.ppermute(v, "narrow", CORE_PAIRS)

    def over_y(v):
        return lax.ppermute(v, "narrow", Y_PAIRS)

    def along_wide(v, pairs):
        return lax.ppermute(v, "wide", pairs)

    def half_of(v, which):
        half = v.shape[0] // 2
        return lax.dynamic_slice_in_dim(v, which * half, half, axis=0)

    def ordered(first, second, which):
        return jnp.where(
            which == 0,
            jnp.concatenate([first, second], axis=0),
            jnp.concatenate([second, first], axis=0),
        )

    near = layer % 2

    def ask(v, which):
        return over_y(half_of(v, which))

    inward = jnp.concatenate([w_cross_q, w_cross_kv.reshape(2 * width, 256)], axis=0)
    outward = jnp.concatenate([w_out, w_cross_out], axis=0)
    qkv_first = ask(w_qkv.reshape(3 * width, 256), near)
    scaled, _ = norm_parts(frames.astype(FULL))
    h1 = lower(scaled * norm_gain[0] + norm_bias[0])
    h1_other = over_core(h1)
    dout = jnp.where(loss_mask[:, None] != 0, cotangent, jnp.zeros((), ROUND))
    q0, k0, v0 = project(where, h1, h1_other, w_qkv, False)

    q0, qkv_first, inward, outward, dout = join((q0, qkv_first, inward, outward, dout))
    qkv_second = along_wide(qkv_first, Z_NEAR)
    outward_first = ask(outward, column)
    inward_first = ask(inward, column)
    own_wo = over_core(outward)
    own_wq = over_core(w_cross_q)
    dout_other = over_core(dout)
    o0, lse0 = self_forward(limit, q0, k0, v0)

    o0, qkv_second, w_up_sent = join((o0, qkv_second, w_up))
    qkv_y = ordered(qkv_first, qkv_second, near).reshape(3, width, 256)
    q1, k1, v1 = project(where, h1, h1_other, qkv_y, False)

    def away_rows(v):
        return half_of(v, 1 - core)

    o0_other = over_core(away_rows(o0))
    q1, outward_first, inward_first, w_up_sent, o0_other, own_wo, own_wq = join(
        (q1, outward_first, inward_first, w_up_sent, o0_other, own_wo, own_wq)
    )
    outward_second = along_wide(outward_first, X_PAIRS)
    inward_second = along_wide(inward_first, X_PAIRS)
    up_first = ask(w_up_sent, column)
    o1, lse1 = self_forward(limit, q1, k1, v1)
    o1_other = over_core(away_rows(o1))

    o1, outward_second, inward_second, up_first, w_down_sent = join(
        (o1, outward_second, inward_second, up_first, w_down)
    )
    up_second = along_wide(up_first, X_PAIRS)
    down_first = ask(w_down_sent, near)
    outward_y = ordered(outward_first, outward_second, column)
    inward_y = ordered(inward_first, inward_second, column)
    out_y = outward_y[:256]
    cross_out_y = outward_y[256:]
    cross_q_y = inward_y[:width]
    cross_kv_y = inward_y[width:].reshape(2, width, 256)
    y_wo = over_core(outward_y)
    y_wq = over_core(cross_q_y)
    wo = (w_out, out_y, own_wo[:256], y_wo[:256])
    wc = (w_cross_out, cross_out_y, own_wo[256:], y_wo[256:])
    wq = (w_cross_q, cross_q_y, own_wq, y_wq)
    text = lax.dynamic_slice(text_states, (side, 0, 0), (1, *text_states.shape[1:]))[0]
    pair = jnp.stack(
        [jnp.stack([lower(nn(text, w[c])) for c in range(2)]) for w in (w_cross_kv, cross_kv_y)]
    )
    pair_other = over_core(pair)
    head_of = jnp.arange(256) // HEAD
    same = head_of[:, None] == head_of[None, :]

    def spread_heads(v):
        return jnp.where(same, jnp.tile(v, (1, 4, 1)), jnp.zeros((), ROUND))

    ck = (spread_heads(pair[:, 0]), spread_heads(pair_other[:, 0]))
    cv = (spread_heads(pair[:, 1]), spread_heads(pair_other[:, 1]))
    x1, x2, h2, cq, ca, h3 = middle_forward(
        where, frames, (o0, o1), (o0_other, o1_other), norm_gain, norm_bias, wo, wq, ck, cv, wc
    )
    h3_other = over_core(h3)
    h2_other = over_core(h2)
    ca_other = over_core(ca[:, 512:])

    h3, up_second, down_first = join((h3, up_second, down_first))
    down_second = along_wide(down_first, Z_NEAR)
    up_y = ordered(up_first, up_second, column)
    g0, du0, out_m, y_m = feed(where, h3, dout, w_up, w_down, FULL)
    g0, du0, out_o, y_o = feed(
        where, h3_other, dout_other, w_up, w_down, FULL, shared=(g0, du0)
    )
    y_o, down_second = join((y_o, down_second))
    down_y = ordered(down_first, down_second, near)
    h3_rows = jnp.concatenate([h3, h3_other], axis=0)
    dout_rows = jnp.concatenate([dout, dout_other], axis=0)
    g1, du1, out_m, y_m = feed(where, h3, dout, up_y, down_y, FULL, before=(out_m, y_m))
    g1, du1, out_o, y_o = feed(
        where, h3_other, dout_other, up_y, down_y, ROUND, before=(out_o, y_o), shared=(g1, du1)
    )
    y_received = over_core(y_o)

    def plus(a, b):
        return lower(a.astype(FULL) + b.astype(FULL))

    across = (column, X_PAIRS)
    down_z = (near, Z_NEAR)

    class Sum:
        def __init__(self, partner, order=(across, down_z)):
            self.order = order
            self.fly = over_y(partner)

        def first(self, own):
            which, pairs = self.order[0]
            away_half = lower(half_of(own, 1 - which) + half_of(self.fly, 1 - which).astype(FULL))
            self.kept = half_of(own, which) + half_of(self.fly, which).astype(FULL)
            self.fly = along_wide(away_half, pairs)

        def second(self):
            which, pairs = self.order[1]
            total = self.kept + self.fly.astype(FULL)
            self.kept = half_of(total, which)
            self.fly = along_wide(lower(half_of(total, 1 - which)), pairs)

        def far(self):
            self.kept = plus(self.kept, self.fly)
            self.fly = along_wide(self.kept, Z_FAR)

        def back(self):
            self.kept = plus(self.kept, self.fly)
            self.fly = along_wide(self.kept, self.order[1][1])

        def along(self):
            self.kept = ordered(self.kept, self.fly, self.order[1][0])
            self.fly = along_wide(self.kept, self.order[0][1])

        def end(self):
            return ordered(self.kept, self.fly, self.order[0][0]).astype(FULL)

    def sync(in_flight, *values):
        done = join((*[each.fly for each in in_flight], *values))
        for each, fly in zip(in_flight, done):
            each.fly = fly
        return done[len(in_flight) :]

    class Row:
        def __init__(self, value, step):
            self.kept = value
            self.fly = step(value)

        def then(self, step):
            self.kept = self.kept + self.fly
            self.fly = step(self.kept)

    up1 = lower(tn(h3_rows, du1))
    up1, g1, du0, g0 = join((up1, g1, du0, g0))
    up = Sum(up1)
    down1 = lower(tn(g1, dout_rows))
    up0 = tn(h3_rows, du0)
    down0 = tn(g0, dout_rows)
    dx1, dself, dcross, dcq, dck, dcv, sums = middle_back(
        where, y_m, y_received, x1, x2, dout, cq, norm_gain, wq, ck, cv, wc
    )
    dself, dcross, dcq, down1, up0, down0 = sync([up], dself, dcross, dcq, down1, up0, down0)

    down = Sum(down1, (down_z, across))
    up.first(up0)
    dself_other = over_core(dself)
    do0, do1 = project(where, dself, dself_other, jnp.stack([w_out, out_y]), True)
    dcross_other = over_core(dcross)
    dcq_other = over_core(dcq[:, 512:])
    d_pair = jnp.stack([dck, dcv], axis=1)
    d_pair_other = over_core(d_pair[2:])
    dq1, dk1, dv1 = self_back(limit, q1, k1, v1, o1, do1, lse1)
    dq1, dcross_other, dcq_other, d_pair_other = sync(
        [up], dq1, dcross_other, dcq_other, d_pair_other
    )

    up.second()
    d_pair = lower(d_pair[:2] + d_pair_other)
    h1_rows = ordered(h1, h1_other, core)
    qkv1 = lower(jnp.concatenate([tn(h1_rows, g) for g in (dq1, dk1, dv1)], axis=0))
    h2_rows = jnp.concatenate([h2, h2_other], axis=0)

    def both(mine, other, g):
        lanes = slice(g * 256, (g + 1) * 256)
        return jnp.concatenate([mine[:, lanes], other[:, lanes]], axis=0)

    def into(g):
        return jnp.concatenate(
            [tn(h2_rows, both(dcq, dcq_other, g)), tn(text, d_pair[g, 0]), tn(text, d_pair[g, 1])],
            axis=0,
        )

    def outof(g, o):
        return jnp.concatenate(
            [tn(o, dself_rows), tn(both(ca, ca_other, g), dcross_rows)], axis=0
        )

    into1 = lower(into(1))
    qkv1, into1, do0, dself, dcross = sync([down, up], qkv1, into1, do0, dself, dcross)

    qkv = Sum(qkv1)
    down.first(down0)
    up.far()
    dq0, dk0, dv0 = self_back(limit, q0, k0, v0, o0, do0, lse0)
    dself_rows = ordered(dself, dself_other, core)
    dcross_rows = jnp.concatenate([dcross, dcross_other], axis=0)
    grads = (dq0, dk0, dv0, dq1, dk1, dv1)
    yo = first_back(away, grads, (w_qkv, qkv_y), ROUND)
    dq0, dself_rows, dcross_rows, yo = sync([down, up], dq0, dself_rows, dcross_rows, yo)

    down.second()
    up.back()
    y_received = over_core(yo)
    qkv0 = jnp.concatenate([tn(h1_rows, g) for g in (dq0, dk0, dv0)], axis=0)
    grads = (dq0, dk0, dv0, dq1, dk1, dv1)
    ym = first_back(where, grads, (w_qkv, qkv_y), FULL)
    outof1 = lower(outof(1, o1))
    qkv0, ym, y_received, outof1, x2 = sync(
        [qkv, down, up], qkv0, ym, y_received, outof1, x2
    )

    cross_in = Sum(into1)
    qkv.first(qkv0)
    down.far()
    up.along()
    grad_frames, first_sums = frames_back(where, ym, y_received, dx1, frames, norm_gain)
    norms = Row(sums + first_sums, over_core)
    into0 = into(0)
    outof0 = outof(0, o0)
    text_part = 0.0
    for g, weights in ((0, w_cross_kv), (1, cross_kv_y)):
        for c in range(2):
            text_part = text_part + nt(d_pair[g, c], weights[c])
    texts = Row(text_part, over_core)
    out_rows = lower(x2 + out_m + over_core(out_o).astype(FULL))
    into0, outof0, grad_frames, out_rows = sync(
        [qkv, down, norms, texts], into0, outof0, grad_frames, out_rows
    )

    qkv.second()
    down.back()
    norms.then(over_y)
    text_grad = lower(texts.kept + texts.fly)
    (outof1,) = sync([cross_in, norms], outof1)

    outs = Sum(outof1)
    cross_in.first(into0)
    norms.then(lambda v: along_wide(v, X_PAIRS))
    text_away = over_y(text_grad)
    (text_away,) = sync([qkv, down, up], text_away)

    qkv.far()
    down.along()
    grad_up = up.end()
    grad_text = ordered(text_grad[None], text_away[None], side)
    grad_up, grad_text = sync([outs, cross_in, norms], grad_up, grad_text)

    outs.first(outof0)
    cross_in.second()
    norms.then(lambda v: along_wide(v, Z_NEAR))
    sync([qkv, down])

    qkv.back()
    grad_down = down.end()
    (grad_down,) = sync([outs, cross_in, norms], grad_down)

    outs.second()
    cross_in.far()
    norms.then(lambda v: along_wide(v, Z_FAR))
    sync([qkv, outs])

    qkv.along()
    outs.far()
    sync([cross_in, norms])

    cross_in.back()
    sums = norms.kept + norms.fly
    sync([outs])

    outs.back()
    sync([cross_in, qkv])

    cross_in.along()
    grad_qkv = qkv.end().reshape(3, width, 256)
    sync([outs])
    outs.along()
    grad_cross_in = cross_in.end()
    grad_outs = outs.end()
    return (
        out_rows,
        grad_frames,
        grad_text,
        sums[0:6:2],
        sums[1:6:2],
        grad_qkv,
        grad_outs[:256],
        grad_cross_in[:width],
        grad_cross_in[width:].reshape(2, width, 256),
        grad_outs[256:],
        grad_up,
        grad_down,
    )


def solution(mesh):
    chips = dict(mesh.shape) == {"wide": 8, "narrow": 4}
    return jax.shard_map(
        chip_local if chips else general_local,
        mesh=mesh,
        in_specs=(
            P(("wide", "narrow"), None),
            P("wide", None, None),
            P("wide"),
            P(("wide", "narrow")),
            P(),
            P(),
            P(None, None, "narrow"),
            P("narrow", None),
            P(None, "narrow"),
            P(None, None, "narrow"),
            P("narrow", None),
            P(None, "narrow"),
            P("narrow", None),
            P(("wide", "narrow"), None),
        ),
        out_specs=(
            P(("wide", "narrow"), None),
            P(("wide", "narrow"), None),
            P("wide", None, None),
            P(),
            P(),
            P(None, None, "narrow"),
            P("narrow", None),
            P(None, "narrow"),
            P(None, None, "narrow"),
            P("narrow", None),
            P(None, "narrow"),
            P("narrow", None),
        ),
        check_vma=False,
    )
```

```python
import functools

import jax
import jax.numpy as jnp
from jax import lax
from jax.experimental import pallas as pl
from jax.experimental.pallas import tpu as pltpu
from jax.sharding import PartitionSpec as P

HEAD = 64


EPS = 1e-05
NEG = -1e30


def lower(values_in):
    return values_in.astype(jnp.bfloat16)


def product(left_side, right_side, transposed):
    if transposed:
        return lax.dot_general(
            left_side, right_side, (((1,), (1,)), ((), ())), preferred_element_type=jnp.float32
        )
    return jnp.dot(left_side, right_side, preferred_element_type=jnp.float32)


def outer_sum(left_side, right_side):
    return lax.dot_general(
        left_side, right_side, (((0,), (0,)), ((), ())), preferred_element_type=jnp.float32
    )


def normalize(values_in, gain_row, bias_row):
    row_mean = jnp.mean(values_in, axis=-1, keepdims=True)
    centered = values_in - row_mean
    inverse = lax.rsqrt(jnp.mean(centered * centered, axis=-1, keepdims=True) + EPS)
    scaled = centered * inverse
    return (scaled * gain_row + bias_row, scaled, inverse)


def normalize_back(upstream, scaled, inverse, gain_row):
    weighted = upstream * gain_row
    inner_mean = jnp.mean(weighted, axis=-1, keepdims=True)
    along_mean = jnp.mean(weighted * scaled, axis=-1, keepdims=True)
    grad_input = inverse * (weighted - inner_mean - scaled * along_mean)
    return (grad_input, jnp.sum(upstream * scaled, axis=0), jnp.sum(upstream, axis=0))


def gelu_parts(values_in):
    normal_cdf = 0.5 * (1.0 + jax.scipy.special.erf(values_in * 0.7071067811865476))
    normal_pdf = jnp.exp(-0.5 * values_in * values_in) * 0.3989422804014327
    return (values_in * normal_cdf, normal_cdf + values_in * normal_pdf)


def scores_of(query_part, key_part, valid):
    scores = jnp.einsum(
        "bhe,khe->hbk", query_part, key_part, preferred_element_type=jnp.float32
    ) * HEAD ** (-0.5)
    return jnp.where(valid, scores, NEG)


def attend(query_part, key_part, value_part, valid):
    scores = scores_of(query_part, key_part, valid)
    row_top = jnp.max(scores, axis=-1, keepdims=True)
    weights_exp = jnp.exp(scores - row_top)
    denominator = jnp.sum(weights_exp, axis=-1, keepdims=True)
    probability = weights_exp / denominator
    mixed = jnp.einsum(
        "hbk,khe->bhe", lower(probability), value_part, preferred_element_type=jnp.float32
    )
    return (lower(mixed), (row_top + jnp.log(denominator))[..., 0])


def attend_back(query_part, key_part, value_part, valid, summary, upstream):
    scores = scores_of(query_part, key_part, valid)
    probability = jnp.exp(scores - summary[..., None])
    pressure = jnp.einsum("bhe,khe->hbk", upstream, value_part, preferred_element_type=jnp.float32)
    grad_scores = lower(
        probability * (pressure - jnp.sum(probability * pressure, axis=-1, keepdims=True))
    )
    factor = HEAD ** (-0.5)
    grad_query = (
        jnp.einsum("hbk,khe->bhe", grad_scores, key_part, preferred_element_type=jnp.float32)
        * factor
    )
    grad_key = (
        jnp.einsum("hbk,bhe->khe", grad_scores, query_part, preferred_element_type=jnp.float32)
        * factor
    )
    grad_value = jnp.einsum(
        "hbk,bhe->khe", lower(probability), upstream, preferred_element_type=jnp.float32
    )
    return (grad_query, grad_key, grad_value)


def general_local(
    frames,
    text_states,
    lengths,
    loss_mask,
    norm_gain,
    norm_bias,
    w_qkv,
    w_out,
    w_cross_q,
    w_cross_kv,
    w_cross_out,
    w_up,
    w_down,
    cotangent,
):
    row_count = frames.shape[0]
    width = frames.shape[1]
    item_count = lengths.shape[0]
    span = row_count * lax.axis_size("narrow") // item_count
    half_span = span // 2
    inner_width = w_qkv.shape[2]
    head_count = inner_width // HEAD
    text_count = text_states.shape[1]
    full_rows = item_count * span
    places = jnp.arange(span, dtype=jnp.int32)

    def spread(shard_rows):
        return lax.all_gather(shard_rows, "narrow", axis=0, tiled=True)

    def collect(left_side, right_side, transposed):
        return lax.psum_scatter(
            product(
                lax.slice_in_dim(left_side, 0, lax.axis_size("narrow") * row_count, axis=0),
                right_side,
                transposed,
            ),
            "narrow",
            scatter_dimension=0,
            tiled=True,
        )

    def causal(block_index, item_limit):
        query_place = block_index * half_span + jnp.arange(half_span, dtype=jnp.int32)
        return (places[None, :] <= query_place[:, None]) & (places[None, :] < item_limit)

    frame_rows = frames.astype(jnp.float32)
    normed_one, scaled_one, inverse_one = normalize(frame_rows, norm_gain[0], norm_bias[0])
    first_input = spread(lower(normed_one))
    triple = lower(
        jnp.einsum("rd,cde->cre", first_input, w_qkv, preferred_element_type=jnp.float32)
    )
    triple = triple.reshape(3, item_count, span, head_count, HEAD)

    def self_item(packed):
        query_part, key_part, value_part, item_limit = packed
        mixed_list = []
        summary_list = []
        for block_index in range(2):
            mixed, summary = attend(
                query_part[block_index * half_span : (block_index + 1) * half_span],
                key_part,
                value_part,
                causal(block_index, item_limit),
            )
            mixed_list.append(mixed)
            summary_list.append(summary)
        return (jnp.concatenate(mixed_list, axis=0), jnp.stack(summary_list, axis=0))

    attended, self_summary = lax.map(self_item, (triple[0], triple[1], triple[2], lengths))
    attended_flat = attended.reshape(full_rows, inner_width)
    first_rows = frame_rows + collect(attended_flat, w_out, False)
    normed_two, scaled_two, inverse_two = normalize(first_rows, norm_gain[1], norm_bias[1])
    second_input = spread(lower(normed_two))
    cross_query = lower(product(second_input, w_cross_q, False)).reshape(
        item_count, span, head_count, HEAD
    )
    cross_pair = lower(
        jnp.einsum("ntd,cde->cnte", text_states, w_cross_kv, preferred_element_type=jnp.float32)
    )
    cross_pair = cross_pair.reshape(2, item_count, text_count, head_count, HEAD)

    def cross_item(packed):
        query_part, key_part, value_part = packed
        return attend(query_part, key_part, value_part, True)

    cross_mixed, cross_summary = lax.map(cross_item, (cross_query, cross_pair[0], cross_pair[1]))
    cross_flat = cross_mixed.reshape(full_rows, inner_width)
    second_rows = first_rows + collect(cross_flat, w_cross_out, False)
    normed_three, scaled_three, inverse_three = normalize(second_rows, norm_gain[2], norm_bias[2])
    upstream = cotangent.astype(jnp.float32) * loss_mask.astype(jnp.float32)[:, None]
    ffn_grad = lower(upstream)
    ffn_input = spread(lower(normed_three))
    hidden_pre = product(ffn_input, w_up, False)
    active, slope = gelu_parts(hidden_pre)
    active = lower(active)
    out_rows = second_rows + collect(active, w_down, False)
    ffn_full = spread(ffn_grad)
    grad_down = outer_sum(active, ffn_full)
    grad_hidden = lower(product(ffn_full, w_down, True) * slope)
    grad_up = outer_sum(ffn_input, grad_hidden)
    back_three = collect(grad_hidden, w_up, True)
    grad_up, grad_down = (grad_up, grad_down)
    grad_in_three, gain_three, bias_three = normalize_back(
        back_three, scaled_three, inverse_three, norm_gain[2]
    )
    grad_second = upstream + grad_in_three
    cross_full = spread(lower(grad_second))
    grad_cross_out = outer_sum(cross_flat, cross_full)
    cross_upstream = lower(product(cross_full, w_cross_out, True)).reshape(
        item_count, span, head_count, HEAD
    )

    def cross_back(packed):
        query_part, key_part, value_part, summary, upstream_item = packed
        return attend_back(query_part, key_part, value_part, True, summary, upstream_item)

    grad_cq, grad_ck, grad_cv = lax.map(
        cross_back, (cross_query, cross_pair[0], cross_pair[1], cross_summary, cross_upstream)
    )
    grad_cq = lower(grad_cq).reshape(full_rows, inner_width)
    grad_pair = lower(jnp.stack((grad_ck, grad_cv), axis=0)).reshape(
        2, item_count, text_count, inner_width
    )
    grad_cross_q = outer_sum(second_input, grad_cq)
    grad_cross_kv = jnp.einsum(
        "ntd,cnte->cde", text_states, grad_pair, preferred_element_type=jnp.float32
    )
    grad_cross_q, grad_cross_kv, grad_cross_out = (grad_cross_q, grad_cross_kv, grad_cross_out)
    text_partial = jnp.einsum(
        "cnte,cde->ntd", grad_pair, w_cross_kv, preferred_element_type=jnp.float32
    )
    grad_text = lower(lax.psum(text_partial, "narrow"))
    back_two = collect(grad_cq, w_cross_q, True)
    grad_in_two, gain_two, bias_two = normalize_back(
        back_two, scaled_two, inverse_two, norm_gain[1]
    )
    grad_first = grad_second + grad_in_two
    self_full = spread(lower(grad_first))
    grad_out = outer_sum(attended_flat, self_full)
    self_upstream = lower(product(self_full, w_out, True)).reshape(
        item_count, span, head_count, HEAD
    )

    def self_back(packed):
        query_part, key_part, value_part, item_limit, summary, upstream_item = packed
        query_list = []
        key_list = []
        value_list = []
        for block_index in range(2):
            lower_row = block_index * half_span
            grad_query, grad_key, grad_value = attend_back(
                query_part[lower_row : lower_row + half_span],
                key_part,
                value_part,
                causal(block_index, item_limit),
                summary[block_index],
                upstream_item[lower_row : lower_row + half_span],
            )
            query_list.append(grad_query)
            key_list.append(grad_key)
            value_list.append(grad_value)
        return (
            jnp.concatenate(query_list, axis=0),
            key_list[0] + key_list[1],
            value_list[0] + value_list[1],
        )

    grad_q, grad_k, grad_v = lax.map(
        self_back, (triple[0], triple[1], triple[2], lengths, self_summary, self_upstream)
    )
    grad_triple = lower(jnp.stack((grad_q, grad_k, grad_v), axis=0)).reshape(
        3, full_rows, inner_width
    )
    grad_qkv = jnp.einsum(
        "rd,cre->cde", first_input, grad_triple, preferred_element_type=jnp.float32
    )
    grad_qkv, grad_out = (grad_qkv, grad_out)
    merged = grad_triple.transpose(1, 0, 2).reshape(full_rows, 3 * inner_width)
    stacked_weights = w_qkv.transpose(0, 2, 1).reshape(3 * inner_width, width)
    back_one = collect(merged, stacked_weights, False)
    grad_in_one, gain_one, bias_one = normalize_back(
        back_one, scaled_one, inverse_one, norm_gain[0]
    )
    grad_frames = lower(grad_first + grad_in_one)
    gain_terms = jnp.stack((gain_one, gain_two, gain_three), axis=0)
    bias_terms = jnp.stack((bias_one, bias_two, bias_three), axis=0)
    grad_norm_gain, grad_norm_bias = lax.psum((gain_terms, bias_terms), ("wide", "narrow"))
    grad_qkv, grad_out, grad_cross_q, grad_cross_kv, grad_cross_out, grad_up, grad_down = lax.psum(
        (grad_qkv, grad_out, grad_cross_q, grad_cross_kv, grad_cross_out, grad_up, grad_down),
        "wide",
    )
    return (
        lower(out_rows),
        grad_frames,
        grad_text,
        grad_norm_gain,
        grad_norm_bias,
        grad_qkv,
        grad_out,
        grad_cross_q,
        grad_cross_kv,
        grad_cross_out,
        grad_up,
        grad_down,
    )


ROUND = jnp.bfloat16
FULL = jnp.float32
CORE_PAIRS = ((0, 1), (1, 0), (2, 3), (3, 2))
Y_PAIRS = ((0, 2), (2, 0), (1, 3), (3, 1))
X_PAIRS = tuple((i, i ^ 1) for i in range(8))
Z_INWARD = ((0, 2), (1, 3), (6, 4), (7, 5))
Z_MIDDLE = ((2, 4), (4, 2), (3, 5), (5, 3))
Z_OUTWARD = ((2, 0), (3, 1), (4, 6), (5, 7))
Z_NEAR = tuple((i, i ^ 2) for i in range(8))
Z_FAR = tuple((i, i ^ 4) for i in range(8))
MIB = 1 << 20


def nt(a, b):
    return lax.dot_general(a, b, (((1,), (1,)), ((), ())), preferred_element_type=FULL)


def nn(a, b):
    return lax.dot_general(a, b, (((1,), (0,)), ((), ())), preferred_element_type=FULL)


def tn(a, b):
    return lax.dot_general(a, b, (((0,), (0,)), ((), ())), preferred_element_type=FULL)


def shape(dims, kind):
    return jax.ShapeDtypeStruct(dims, kind)


def resident(dims):
    zeros = (0,) * len(dims)
    return pl.BlockSpec(dims, lambda i, s: zeros, pipeline_mode=pl.Buffered(1))


def rows_of(block, width):
    return pl.BlockSpec((block, width), lambda i, s: (i, 0))


def brief():
    return pl.CostEstimate(flops=1000, bytes_accessed=1000, transcendentals=0)


def params(mib):
    return pltpu.CompilerParams(vmem_limit_bytes=mib * MIB)


def norm_parts(v):
    centered = v - jnp.mean(v, axis=-1, keepdims=True)
    inverse = lax.rsqrt(jnp.mean(centered * centered, axis=-1, keepdims=True) + EPS)
    return centered * inverse, inverse


def norm_pull(y, scaled, inverse, gain_row):
    weighted = y * gain_row
    inner = jnp.mean(weighted, axis=-1, keepdims=True)
    along = jnp.mean(weighted * scaled, axis=-1, keepdims=True)
    return inverse * (weighted - inner - scaled * along)


def first_project_kernel(
    place_ref, mine_ref, other_ref, gain_ref, bias_ref, weight_ref, h_ref, *out_refs
):
    half = pl.program_id(0)

    def run(source):
        for start in range(0, source.shape[0], 208):
            part = slice(start, start + 208)
            scaled, _ = norm_parts(source[part, :].astype(FULL))
            h = lower(scaled * gain_ref[0:1, :] + bias_ref[0:1, :])
            h_ref[part, :] = h
            for c, out_ref in enumerate(out_refs):
                out_ref[part, :] = lower(nn(h, weight_ref[c]))

    @pl.when(half == 0)
    def _():
        run(mine_ref)

    @pl.when(half == 1)
    def _():
        run(other_ref)


def first_project(place, mine, other, gains, biases, weights):
    rows, depth = mine.shape
    count, _, wide = weights.shape
    out = pl.BlockSpec((rows, wide), lambda i, s: ((i + s[0]) % 2, 0))
    return pl.pallas_call(
        first_project_kernel,
        grid_spec=pltpu.PrefetchScalarGridSpec(
            num_scalar_prefetch=1,
            grid=(2,),
            in_specs=[resident(a.shape) for a in (mine, other, gains, biases, weights)],
            out_specs=[rows_of(rows, depth)] + [out] * count,
        ),
        out_shape=[shape((2 * rows, depth), ROUND)] + [shape((2 * rows, wide), ROUND)] * count,
        compiler_params=params(40),
        cost_estimate=brief(),
        name="first_project",
    )(place, mine, other, gains, biases, weights)


def project_kernel(place_ref, h_ref, first_ref, second_ref, *out_refs):
    depth = first_ref.shape[1]
    near = place_ref[1]
    left = h_ref[:, pl.ds(pl.multiple_of(near * depth, 128), depth)]
    right = h_ref[:, pl.ds(pl.multiple_of((1 - near) * depth, 128), depth)]
    for c, out_ref in enumerate(out_refs):
        out_ref[...] = lower(nn(left, first_ref[c]) + nn(right, second_ref[c]))


def project(place, h, first, second):
    rows, depth = h.shape[0] // 2, h.shape[1]
    count, _, wide = first.shape
    out = pl.BlockSpec((rows, wide), lambda i, s: ((i + s[0]) % 2, 0))
    return pl.pallas_call(
        project_kernel,
        grid_spec=pltpu.PrefetchScalarGridSpec(
            num_scalar_prefetch=1,
            grid=(2,),
            in_specs=[rows_of(rows, depth), resident(first.shape), resident(second.shape)],
            out_specs=[out] * count,
        ),
        out_shape=[shape((2 * rows, wide), ROUND)] * count,
        compiler_params=params(32),
        cost_estimate=brief(),
        name="project",
    )(place, h, first, second)


def pull_kernel(place_ref, mine_ref, other_ref, *refs):
    half = pl.program_id(0)
    count = len(refs) // 2

    def run(source):
        for weight_ref, out_ref in zip(refs[:count], refs[count:]):
            out_ref[...] = lower(nt(source[...], weight_ref[...]))

    @pl.when(half == 0)
    def _():
        run(mine_ref)

    @pl.when(half == 1)
    def _():
        run(other_ref)


def pull(place, mine, other, weights):
    rows = mine.shape[0]
    wide = weights[0].shape[0]
    out = pl.BlockSpec((rows, wide), lambda i, s: ((i + s[0]) % 2, 0))
    return pl.pallas_call(
        pull_kernel,
        grid_spec=pltpu.PrefetchScalarGridSpec(
            num_scalar_prefetch=1,
            grid=(2,),
            in_specs=[resident(a.shape) for a in (mine, other, *weights)],
            out_specs=[out] * len(weights),
        ),
        out_shape=[shape((2 * rows, wide), ROUND)] * len(weights),
        compiler_params=params(32),
        cost_estimate=brief(),
        name="pull",
    )(place, mine, other, *weights)


def blocks_of(span, block):
    return [(start, min(block, span - start)) for start in range(0, span, block)]


def self_forward_kernel(
    limit_ref, q_ref, k_ref, v_ref, o_ref, lse_ref, *, span, floor, block
):
    limit = limit_ref[0]
    lane = lax.broadcasted_iota(jnp.int32, (1, 128), 1)
    row = lax.broadcasted_iota(jnp.int32, (128, 1), 0)
    zero = jnp.zeros((), ROUND)
    value_turned = v_ref[...].T
    for start, size in blocks_of(span, block):
        end = start + size
        mixed_list = []
        for h in range(2):
            own_lanes = (lane < HEAD) if h == 0 else (lane >= HEAD)
            query = jnp.where(own_lanes, q_ref[start:end, :] * HEAD ** (-0.5), zero)
            parts = []
            for low in range(0, end, block):
                high = min(low + block, end)
                scores = nt(k_ref[low:high, :], query)
                if low == start:
                    key = lax.broadcasted_iota(jnp.int32, (size, size), 0)
                    valid = key <= lax.broadcasted_iota(jnp.int32, (size, size), 1)
                    if high > floor:
                        valid = valid & (key + low < limit)
                    scores = jnp.where(valid, scores, NEG)
                elif high > floor:
                    key = lax.broadcasted_iota(jnp.int32, (high - low, 1), 0)
                    scores = jnp.where(key + low < limit, scores, NEG)
                parts.append((low, high, scores))
            top = functools.reduce(
                jnp.maximum, [jnp.max(s, axis=0, keepdims=True) for _, _, s in parts]
            )
            total = 0.0
            mixed = 0.0
            for low, high, scores in parts:
                weights_exp = jnp.exp(scores - top)
                total = total + jnp.sum(weights_exp, axis=0, keepdims=True)
                mixed = mixed + nn(value_turned[:, low:high], lower(weights_exp))
            mixed_list.append(mixed / total)
            lse_ref[0, h : h + 1, start:end] = top + jnp.log(total)
        o_ref[start:end, :] = lower(jnp.where(row < HEAD, mixed_list[0], mixed_list[1]).T)


def self_forward(limit, q, k, v):
    span, wide = q.shape
    pairs = wide // 128
    floor = (span - span // 8 + 1) // 128 * 128
    pair = pl.BlockSpec((span, 128), lambda p, s: (0, p))
    return pl.pallas_call(
        functools.partial(self_forward_kernel, span=span, floor=floor, block=512),
        grid_spec=pltpu.PrefetchScalarGridSpec(
            num_scalar_prefetch=1,
            grid=(pairs,),
            in_specs=[pair] * 3,
            out_specs=[pair, pl.BlockSpec((1, 8, span), lambda p, s: (p, 0, 0))],
        ),
        out_shape=[shape((span, wide), ROUND), shape((pairs, 8, span), FULL)],
        compiler_params=params(56),
        cost_estimate=brief(),
        name="self_forward",
    )(limit, q, k, v)


def self_back_kernel(
    limit_ref, q_ref, k_ref, v_ref, o_ref, do_ref, lse_ref, dq_ref, dk_ref, dv_ref, dqt,
    *, span, floor, block
):
    limit = limit_ref[0]
    lane = lax.broadcasted_iota(jnp.int32, (1, 128), 1)
    row = lax.broadcasted_iota(jnp.int32, (128, 1), 0)
    zero = jnp.zeros((), ROUND)
    factor = HEAD ** (-0.5)
    product_rows = do_ref[...].astype(FULL) * o_ref[...].astype(FULL)
    high = lower(product_rows)
    rest = lower(product_rows - high.astype(FULL))
    pick = lower(
        jnp.concatenate(
            [
                jnp.where(lane < HEAD, 1.0, 0.0),
                jnp.where(lane >= HEAD, 1.0, 0.0),
                jnp.zeros((6, 128), FULL),
            ],
            axis=0,
        )
    )
    delta = nt(pick, high) + nt(pick, rest)
    for start, size in blocks_of(span, block):
        end = start + size
        key = k_ref[start:end, :]
        value = v_ref[start:end, :]
        key_turned = key.T
        dk = 0.0
        dv = 0.0
        dq_add = 0.0
        for h in range(2):
            own_lanes = (lane < HEAD) if h == 0 else (lane >= HEAD)
            own_rows = (row < HEAD) if h == 0 else (row >= HEAD)
            query = jnp.where(own_lanes, q_ref[start:, :] * factor, zero)
            pulled = jnp.where(own_lanes, do_ref[start:, :], zero)
            probability = jnp.exp(nt(key, query) - lse_ref[0, h : h + 1, start:])
            pressure = nt(value, pulled)
            below = lax.broadcasted_iota(jnp.int32, (size, size), 0)
            across = lax.broadcasted_iota(jnp.int32, (size, size), 1)
            corner = jnp.where(below <= across, probability[:, :size], 0.0)
            if end < span:
                probability = jnp.concatenate([corner, probability[:, size:]], axis=1)
            else:
                probability = corner
            if end > floor:
                place = lax.broadcasted_iota(jnp.int32, (size, 1), 0) + start
                probability = jnp.where(place < limit, probability, 0.0)
            grad_scores = lower(probability * (pressure - delta[h : h + 1, start:]))
            dv = dv + nn(lower(probability), pulled)
            dk = dk + nn(grad_scores, query)
            dq_add = dq_add + nn(jnp.where(own_rows, key_turned, zero), grad_scores)
        dk_ref[start:end, :] = lower(dk)
        dv_ref[start:end, :] = lower(dv)
        if start == 0:
            dqt[...] = dq_add
        else:
            dqt[:, start:] += dq_add
    dq_ref[...] = lower(dqt[...].T * factor)


def self_back(limit, q, k, v, o, do, lse):
    span, wide = q.shape
    pairs = wide // 128
    floor = (span - span // 8 + 1) // 128 * 128
    pair = pl.BlockSpec((span, 128), lambda p, s: (0, p))
    return pl.pallas_call(
        functools.partial(self_back_kernel, span=span, floor=floor, block=256),
        grid_spec=pltpu.PrefetchScalarGridSpec(
            num_scalar_prefetch=1,
            grid=(pairs,),
            in_specs=[pair] * 5 + [pl.BlockSpec((1, 8, span), lambda p, s: (p, 0, 0))],
            out_specs=[pair] * 3,
            scratch_shapes=[pltpu.VMEM((128, span), FULL)],
        ),
        out_shape=[shape((span, wide), ROUND)] * 3,
        compiler_params=params(48),
        cost_estimate=brief(),
        name="self_back",
    )(limit, q, k, v, o, do, lse)


def by_head(values_in, reduce, empty):
    lane = lax.broadcasted_iota(jnp.int32, (1, 128), 1)
    pieces = []
    for start in range(0, values_in.shape[1], 128):
        part = values_in[:, start : start + 128]
        first = reduce(jnp.where(lane < HEAD, part, empty), axis=1, keepdims=True)
        second = reduce(jnp.where(lane >= HEAD, part, empty), axis=1, keepdims=True)
        pieces.append(jnp.where(lane < HEAD, first, second))
    return jnp.concatenate(pieces, axis=1)


def cross_probability(query, keys):
    scores = nt(query * HEAD ** (-0.5), keys)
    weights_exp = jnp.exp(scores - by_head(scores, jnp.max, NEG))
    return weights_exp / by_head(weights_exp, jnp.sum, 0.0)


def middle_forward_kernel(
    place_ref, frame_ref, a0_ref, a1_ref, a2_ref, a3_ref, gain_ref, bias_ref, *refs
):
    mixed = (a0_ref, a1_ref, a2_ref, a3_ref)
    wo, wq, wc = refs[0:4], refs[4:8], refs[12:16]
    ck0_ref, ck1_ref, cv0_ref, cv1_ref = refs[8:12]
    x1_ref, x2_ref, h2_ref, cq_ref, ca_ref, h3_ref = refs[16:]
    x1 = frame_ref[...].astype(FULL)
    for g in range(4):
        x1 = x1 + nn(mixed[g][...], wo[g][...])
    x1_ref[...] = x1
    scaled, _ = norm_parts(x1)
    h2 = lower(scaled * gain_ref[1:2, :] + bias_ref[1:2, :])
    h2_ref[...] = h2
    for g in range(4):
        lanes = slice(g * 256, (g + 1) * 256)
        cq = lower(nn(h2, wq[g][...]))
        cq_ref[:, lanes] = cq
        probability = cross_probability(cq, (ck0_ref, ck1_ref)[g // 2][g % 2])
        ca_ref[:, lanes] = lower(nn(lower(probability), (cv0_ref, cv1_ref)[g // 2][g % 2]))
    crossed = 0.0
    for g in range(4):
        crossed = crossed + nn(ca_ref[:, g * 256 : (g + 1) * 256], wc[g][...])
    x2 = x1_ref[...] + crossed
    x2_ref[...] = x2
    scaled, _ = norm_parts(x2)
    h3_ref[...] = lower(scaled * gain_ref[2:3, :] + bias_ref[2:3, :])


def middle_forward(place, frames, attended, received, gains, biases, wo, wq, ck, cv, wc):
    rows, width = frames.shape
    block = 416
    steps = rows // block
    piece = pl.BlockSpec((block, 256), lambda i, s: (s[0] * steps + i, 0))
    wide = rows_of(block, width)
    return pl.pallas_call(
        middle_forward_kernel,
        grid_spec=pltpu.PrefetchScalarGridSpec(
            num_scalar_prefetch=1,
            grid=(steps,),
            in_specs=[wide, piece, piece, rows_of(block, 256), rows_of(block, 256)]
            + [resident(a.shape) for a in (gains, biases, *wo, *wq, *ck, *cv, *wc)],
            out_specs=[wide] * 6,
        ),
        out_shape=[shape((rows, width), FULL)] * 2 + [shape((rows, width), ROUND)] * 4,
        compiler_params=params(56),
        cost_estimate=brief(),
        name="middle_forward",
    )(place, frames, *attended, *received, gains, biases, *wo, *wq, *ck, *cv, *wc)


def feed_kernel(place_ref, h_ref, d_ref, *refs, parts, carried):
    ups, downs = refs[:parts], refs[parts : 2 * parts]
    before = refs[2 * parts : 2 * parts + carried]
    g_ref, du_ref, out_ref, y_ref = refs[-4:]
    h = h_ref[...]
    d = d_ref[...]
    out = 0.0
    y = 0.0
    for n, (up_ref, down_ref) in enumerate(zip(ups, downs)):
        size = down_ref.shape[0]
        if parts == 1:
            lanes = slice(0, size)
        else:
            near = place_ref[1]
            which = near if n == 0 else 1 - near
            lanes = pl.ds(pl.multiple_of(which * size, 128), size)
        u = nn(h, up_ref[...])
        active, slope = gelu_parts(u)
        g = lower(active)
        g_ref[:, lanes] = g
        du = lower(nt(d, down_ref[...]) * slope)
        du_ref[:, lanes] = du
        out = out + nn(g, down_ref[...])
        y = y + nt(du, up_ref[...])
    if carried:
        out = before[0][...] + out
        y = before[1][...] + y
    out_ref[...] = out.astype(out_ref.dtype)
    y_ref[...] = y.astype(y_ref.dtype)


def feed(place, h, d, ups, downs, kind, half, before=(), shared=()):
    rows, width = h.shape
    block = 416
    steps = rows // block
    hidden = sum(a.shape[0] for a in downs)
    wide = rows_of(block, width)
    kept = pl.BlockSpec((block, hidden), lambda i, s: (i + half * steps, 0))
    there = pl.BlockSpec(memory_space=pl.ANY)
    parts = len(ups)
    at = 3 + 2 * parts + len(before)
    return pl.pallas_call(
        functools.partial(feed_kernel, parts=parts, carried=len(before)),
        grid_spec=pltpu.PrefetchScalarGridSpec(
            num_scalar_prefetch=1,
            grid=(steps,),
            in_specs=[wide, wide]
            + [resident(a.shape) for a in (*ups, *downs)]
            + [wide] * len(before)
            + [there] * len(shared),
            out_specs=[kept, kept, wide, wide],
        ),
        out_shape=[shape((2 * rows, hidden), ROUND)] * 2 + [shape((rows, width), kind)] * 2,
        input_output_aliases={at: 0, at + 1: 1} if shared else {},
        compiler_params=params(58),
        cost_estimate=brief(),
        name="feed",
    )(place, h, d, *ups, *downs, *before, *shared)


def up_grad_kernel(mine_ref, other_ref, du_ref, out_ref):
    rows = mine_ref.shape[0]
    total = tn(mine_ref[...], du_ref[:rows, :]) + tn(other_ref[...], du_ref[rows:, :])
    out_ref[...] = total.astype(out_ref.dtype)


def up_grad(mine, other, du, kind):
    rows, width = mine.shape
    hidden = du.shape[1]
    tile = 512
    whole = pl.BlockSpec((rows, width), lambda i: (0, 0), pipeline_mode=pl.Buffered(1))
    return pl.pallas_call(
        up_grad_kernel,
        grid=(hidden // tile,),
        in_specs=[whole, whole, pl.BlockSpec((2 * rows, tile), lambda i: (0, i))],
        out_specs=pl.BlockSpec((width, tile), lambda i: (0, i)),
        out_shape=shape((width, hidden), kind),
        compiler_params=params(48),
        cost_estimate=brief(),
        name="up_grad",
    )(mine, other, du)


def down_grad_kernel(g_ref, mine_ref, other_ref, out_ref):
    rows = mine_ref.shape[0]
    total = tn(g_ref[:rows, :], mine_ref[...]) + tn(g_ref[rows:, :], other_ref[...])
    out_ref[...] = total.astype(out_ref.dtype)


def down_grad(g, mine, other, kind):
    rows, width = mine.shape
    hidden = g.shape[1]
    tile = 512
    whole = pl.BlockSpec((rows, width), lambda i: (0, 0), pipeline_mode=pl.Buffered(1))
    return pl.pallas_call(
        down_grad_kernel,
        grid=(hidden // tile,),
        in_specs=[pl.BlockSpec((2 * rows, tile), lambda i: (0, i)), whole, whole],
        out_specs=pl.BlockSpec((tile, width), lambda i: (i, 0)),
        out_shape=shape((hidden, width), kind),
        compiler_params=params(48),
        cost_estimate=brief(),
        name="down_grad",
    )(g, mine, other)


def qkv_grad_kernel(place_ref, h_ref, *refs):
    out_ref = refs[-1]
    rows, width = h_ref.shape[0] // 2, h_ref.shape[1]
    core = place_ref[0]
    total = [0.0] * 3
    for half in range(2):
        turned = h_ref[half * rows : (half + 1) * rows, :].T
        at = pl.multiple_of((core if half == 0 else 1 - core) * rows, 16)
        for c in range(3):
            total[c] = total[c] + nn(turned, refs[c][pl.ds(at, rows), :])
    for c in range(3):
        out_ref[c * width : (c + 1) * width, :] = total[c].astype(out_ref.dtype)


def qkv_grad(place, h, grads, kind):
    width = h.shape[1]
    wide = grads[0].shape[1]
    return pl.pallas_call(
        qkv_grad_kernel,
        grid_spec=pltpu.PrefetchScalarGridSpec(
            num_scalar_prefetch=1,
            grid=(1,),
            in_specs=[resident(a.shape) for a in (h, *grads)],
            out_specs=resident((3 * width, wide)),
        ),
        out_shape=shape((3 * width, wide), kind),
        compiler_params=params(48),
        cost_estimate=brief(),
        name="qkv_grad",
    )(place, h, *grads)


def cross_in_grad_kernel(mine_ref, other_ref, dm_ref, do_ref, text_ref, pair_ref, out_ref):
    width = mine_ref.shape[1]
    total = tn(mine_ref[...], dm_ref[...]) + tn(other_ref[...], do_ref[...])
    out_ref[:width, :] = total.astype(out_ref.dtype)
    turned = text_ref[...].T
    for c in range(2):
        part = nn(turned, pair_ref[c]).astype(out_ref.dtype)
        out_ref[(1 + c) * width : (2 + c) * width, :] = part


def cross_in_grad(group, mine, other, d_mine, d_other, text, pair, kind):
    rows, width = mine.shape
    lanes = pl.BlockSpec((rows, 256), lambda i: (0, group))

    def whole(a):
        zeros = (0,) * a.ndim
        return pl.BlockSpec(a.shape, lambda i: zeros)

    return pl.pallas_call(
        cross_in_grad_kernel,
        grid=(1,),
        in_specs=[whole(mine), whole(other), lanes, lanes, whole(text), whole(pair)],
        out_specs=pl.BlockSpec((3 * width, 256), lambda i: (0, 0)),
        out_shape=shape((3 * width, 256), kind),
        compiler_params=params(48),
        cost_estimate=brief(),
        name="cross_in_grad",
    )(mine, other, d_mine, d_other, text, pair)


def outputs_grad_kernel(
    place_ref, o_ref, sm_ref, so_ref, am_ref, ao_ref, cm_ref, co_ref, out_ref
):
    rows = sm_ref.shape[0]
    core = place_ref[0]
    mine = o_ref[pl.ds(pl.multiple_of(core * rows, 16), rows), :]
    other = o_ref[pl.ds(pl.multiple_of((1 - core) * rows, 16), rows), :]
    out_ref[:256, :] = (tn(mine, sm_ref[...]) + tn(other, so_ref[...])).astype(out_ref.dtype)
    total = tn(am_ref[...], cm_ref[...]) + tn(ao_ref[...], co_ref[...])
    out_ref[256:, :] = total.astype(out_ref.dtype)


def outputs_grad(place, group, o, dself, dself_other, ca, ca_other, dcross, dcross_other, kind):
    rows, width = dself.shape
    lanes = pl.BlockSpec((rows, 256), lambda i, s: (0, group))
    whole = resident((rows, width))
    return pl.pallas_call(
        outputs_grad_kernel,
        grid_spec=pltpu.PrefetchScalarGridSpec(
            num_scalar_prefetch=1,
            grid=(1,),
            in_specs=[resident(o.shape), whole, whole, lanes, lanes, whole, whole],
            out_specs=resident((512, width)),
        ),
        out_shape=shape((512, width), kind),
        compiler_params=params(48),
        cost_estimate=brief(),
        name="outputs_grad",
    )(place, o, dself, dself_other, ca, ca_other, dcross, dcross_other)


def middle_back_kernel(
    place_ref, ym_ref, yr_ref, x1_ref, x2_ref, d_ref, cq_ref, gain_ref, *refs
):
    wq, wc = refs[0:4], refs[8:12]
    ck0_ref, ck1_ref, cv0_ref, cv1_ref = refs[4:8]
    dx1_ref, dself_ref, dcross_ref, dcq_ref, dck_ref, dcv_ref, sums_ref = refs[12:19]
    dck_all, dcv_all = refs[19:]
    step = pl.program_id(0)

    @pl.when(step == 0)
    def _():
        dck_all[...] = jnp.zeros_like(dck_all)
        dcv_all[...] = jnp.zeros_like(dcv_all)
        sums_ref[...] = jnp.zeros_like(sums_ref)

    y3 = ym_ref[...] + yr_ref[...].astype(FULL)
    scaled, inverse = norm_parts(x2_ref[...])
    sums_ref[4:5, :] += jnp.sum(y3 * scaled, axis=0, keepdims=True)
    sums_ref[5:6, :] += jnp.sum(y3, axis=0, keepdims=True)
    dx2 = d_ref[...].astype(FULL) + norm_pull(y3, scaled, inverse, gain_ref[2:3, :])
    dx1_ref[...] = dx2
    dcross = lower(dx2)
    dcross_ref[...] = dcross
    y2 = 0.0
    for g in range(4):
        lanes = slice(g * 256, (g + 1) * 256)
        keys = (ck0_ref, ck1_ref)[g // 2][g % 2]
        values = (cv0_ref, cv1_ref)[g // 2][g % 2]
        dcatt = lower(nt(dcross, wc[g][...]))
        cq = cq_ref[:, lanes]
        probability = cross_probability(cq, keys)
        weighed = nt(dcatt, values)
        inner = by_head(probability * weighed, jnp.sum, 0.0)
        dcs = lower(probability * (weighed - inner))
        dcq = lower(nn(dcs, keys) * HEAD ** (-0.5))
        dcq_ref[:, lanes] = dcq
        dck_all[g] += tn(dcs, cq * HEAD ** (-0.5))
        dcv_all[g] += tn(lower(probability), dcatt)
        y2 = y2 + nt(dcq, wq[g][...])
    scaled, inverse = norm_parts(x1_ref[...])
    sums_ref[2:3, :] += jnp.sum(y2 * scaled, axis=0, keepdims=True)
    sums_ref[3:4, :] += jnp.sum(y2, axis=0, keepdims=True)
    dx1 = dx1_ref[...] + norm_pull(y2, scaled, inverse, gain_ref[1:2, :])
    dx1_ref[...] = dx1
    dself_ref[...] = lower(dx1)

    @pl.when(step == pl.num_programs(0) - 1)
    def _():
        for every, result in ((dck_all, dck_ref), (dcv_all, dcv_ref)):
            for g in range(4):
                total = 0.0
                for h in range(4):
                    lane = lax.broadcasted_iota(jnp.int32, (1, 256), 1) // HEAD
                    total = total + jnp.where(lane == h, every[g, h * 64 : (h + 1) * 64, :], 0.0)
                result[g] = total


def middle_back(place, ym, yr, x1, x2, d, cq, gains, wq, ck, cv, wc):
    rows, width = x1.shape
    block = 416
    wide = rows_of(block, width)
    small = pl.BlockSpec((4, 64, 256), lambda i, s: (0, 0, 0))
    return pl.pallas_call(
        middle_back_kernel,
        grid_spec=pltpu.PrefetchScalarGridSpec(
            num_scalar_prefetch=1,
            grid=(rows // block,),
            in_specs=[wide] * 6 + [resident(a.shape) for a in (gains, *wq, *ck, *cv, *wc)],
            out_specs=[wide] * 4 + [small, small, pl.BlockSpec((8, width), lambda i, s: (0, 0))],
            scratch_shapes=[pltpu.VMEM((4, 256, 256), FULL)] * 2,
        ),
        out_shape=[shape((rows, width), FULL)]
        + [shape((rows, width), ROUND)] * 3
        + [shape((4, 64, 256), FULL)] * 2
        + [shape((8, width), FULL)],
        compiler_params=params(56),
        cost_estimate=brief(),
        name="middle_back",
    )(place, ym, yr, x1, x2, d, cq, gains, *wq, *ck, *cv, *wc)


def first_back_kernel(place_ref, *refs):
    grads = refs[:6]
    own_ref, first_ref, second_ref, y_ref, total = refs[6:]
    depth = first_ref.shape[1]
    y = 0.0
    left = 0.0
    right = 0.0
    for c in range(3):
        y = y + nt(grads[c][...], own_ref[c])
        left = left + nt(grads[3 + c][...], first_ref[c])
        right = right + nt(grads[3 + c][...], second_ref[c])
    near = place_ref[1]
    total[...] = y
    total[:, pl.ds(pl.multiple_of(near * depth, 128), depth)] += left
    total[:, pl.ds(pl.multiple_of((1 - near) * depth, 128), depth)] += right
    y_ref[...] = total[...].astype(y_ref.dtype)


def first_back(place, grads, own, first, second, kind):
    span = grads[0].shape[0]
    rows = span // 2
    width = own.shape[1]
    block = 416
    steps = rows // block
    piece = pl.BlockSpec((block, 256), lambda i, s: (s[0] * steps + i, 0))
    return pl.pallas_call(
        first_back_kernel,
        grid_spec=pltpu.PrefetchScalarGridSpec(
            num_scalar_prefetch=1,
            grid=(steps,),
            in_specs=[piece] * 6 + [resident(a.shape) for a in (own, first, second)],
            out_specs=rows_of(block, width),
            scratch_shapes=[pltpu.VMEM((block, width), FULL)],
        ),
        out_shape=shape((rows, width), kind),
        compiler_params=params(40),
        cost_estimate=brief(),
        name="first_back",
    )(place, *grads, own, first, second)


def frames_back_kernel(place_ref, ym_ref, yr_ref, dx1_ref, frame_ref, gain_ref, out_ref, sums_ref):
    @pl.when(pl.program_id(0) == 0)
    def _():
        sums_ref[...] = jnp.zeros_like(sums_ref)

    y = ym_ref[...] + yr_ref[...].astype(FULL)
    scaled, inverse = norm_parts(frame_ref[...].astype(FULL))
    sums_ref[0:1, :] += jnp.sum(y * scaled, axis=0, keepdims=True)
    sums_ref[1:2, :] += jnp.sum(y, axis=0, keepdims=True)
    out_ref[...] = lower(dx1_ref[...] + norm_pull(y, scaled, inverse, gain_ref[0:1, :]))


def frames_back(place, ym, yr, dx1, frames, gains):
    rows, width = dx1.shape
    block = 208
    wide = rows_of(block, width)
    return pl.pallas_call(
        frames_back_kernel,
        grid_spec=pltpu.PrefetchScalarGridSpec(
            num_scalar_prefetch=1,
            grid=(rows // block,),
            in_specs=[wide] * 4 + [resident(gains.shape)],
            out_specs=[wide, pl.BlockSpec((8, width), lambda i, s: (0, 0))],
        ),
        out_shape=[shape((rows, width), ROUND), shape((8, width), FULL)],
        compiler_params=params(24),
        cost_estimate=brief(),
        name="frames_back",
    )(place, ym, yr, dx1, frames, gains)


def chip_local(
    frames, text_states, lengths, loss_mask, norm_gain, norm_bias, w_qkv, w_out, w_cross_q,
    w_cross_kv, w_cross_out, w_up, w_down, cotangent,
):
    at = lax.axis_index("narrow")
    core = at % 2
    side = at // 2
    column = lax.axis_index("wide") % 2
    layer = lax.axis_index("wide") // 2
    near = layer % 2
    place = jnp.stack([core, near]).astype(jnp.int32)
    away = jnp.stack([1 - core, near]).astype(jnp.int32)
    limit = lax.dynamic_slice(lengths, (side,), (1,))
    rows, width = frames.shape
    join = lax.optimization_barrier

    def over_core(v):
        return lax.ppermute(v, "narrow", CORE_PAIRS)

    def over_y(v):
        return lax.ppermute(v, "narrow", Y_PAIRS)

    def along_wide(v, pairs):
        return lax.ppermute(v, "wide", pairs)

    def half_of(v, which, axis=0):
        half = v.shape[axis] // 2
        return lax.dynamic_slice_in_dim(v, which * half, half, axis=axis)

    def ordered(first, second, which):
        return jnp.where(
            which == 0,
            jnp.concatenate([first, second], axis=0),
            jnp.concatenate([second, first], axis=0),
        )

    frames_other = over_core(frames)
    qkv_first = over_y(half_of(w_qkv, near, 1))
    dout = jnp.where(loss_mask[:, None] != 0, cotangent, jnp.zeros((), ROUND))
    inward = jnp.concatenate([w_cross_q, w_cross_kv.reshape(2 * width, 256)], axis=0)
    outward = jnp.concatenate([w_out, w_cross_out], axis=0)
    h1, q0, k0, v0 = first_project(place, frames, frames_other, norm_gain, norm_bias, w_qkv)

    q0, qkv_first, inward, outward, dout = join((q0, qkv_first, inward, outward, dout))
    qkv_second = along_wide(qkv_first, Z_NEAR)
    outward_first = over_y(half_of(outward, column))
    inward_first = over_y(half_of(inward, near))
    dout_other = over_core(dout)
    own_wo = over_core(outward)
    own_wq = over_core(w_cross_q)
    o0, lse0 = self_forward(limit, q0, k0, v0)

    o0, qkv_second, w_up, w_down = join((o0, qkv_second, w_up, w_down))
    q1, k1, v1 = project(place, h1, qkv_first, qkv_second)

    def away_rows(v):
        return half_of(v, 1 - core)

    o0_other = over_core(away_rows(o0))
    up_sent = half_of(w_up, near, 1)
    down_sent = half_of(w_down, near)
    q1, outward_first, inward_first, up_sent, down_sent, o0_other, own_wo, own_wq = join(
        (q1, outward_first, inward_first, up_sent, down_sent, o0_other, own_wo, own_wq)
    )
    outward_second = along_wide(outward_first, X_PAIRS)
    inward_second = along_wide(inward_first, Z_NEAR)
    up_first = over_y(up_sent)
    o1, lse1 = self_forward(limit, q1, k1, v1)
    o1_other = over_core(away_rows(o1))
    o1, outward_second, inward_second, down_sent, dout_other = join(
        (o1, outward_second, inward_second, down_sent, dout_other)
    )

    down_first = over_y(down_sent)
    outward_y = ordered(outward_first, outward_second, column)
    inward_y = ordered(inward_first, inward_second, near)
    out_y = outward_y[:256]
    cross_out_y = outward_y[256:]
    cross_q_y = inward_y[:width]
    cross_kv_y = inward_y[width:].reshape(2, width, 256)
    y_wo = over_core(outward_y)
    y_wq = over_core(cross_q_y)
    wo = (w_out, out_y, own_wo[:256], y_wo[:256])
    wc = (w_cross_out, cross_out_y, own_wo[256:], y_wo[256:])
    wq = (w_cross_q, cross_q_y, own_wq, y_wq)
    text = lax.dynamic_slice(text_states, (side, 0, 0), (1, *text_states.shape[1:]))[0]
    pair = jnp.stack(
        [jnp.stack([lower(nn(text, w[c])) for c in range(2)]) for w in (w_cross_kv, cross_kv_y)]
    )
    pair_other = over_core(pair)
    head_of = jnp.arange(256) // HEAD
    same = head_of[:, None] == head_of[None, :]

    def spread_heads(v):
        return jnp.where(same, jnp.tile(v, (1, 4, 1)), jnp.zeros((), ROUND))

    ck = (spread_heads(pair[:, 0]), spread_heads(pair_other[:, 0]))
    cv = (spread_heads(pair[:, 1]), spread_heads(pair_other[:, 1]))
    x1, x2, h2, cq, ca, h3 = middle_forward(
        place, frames, (o0, o1), (o0_other, o1_other), norm_gain, norm_bias, wo, wq, ck, cv, wc
    )
    h3, ca, h2, up_first, down_first = join((h3, ca, h2, up_first, down_first))

    h3_other = over_core(h3)
    up_second = along_wide(up_first, Z_NEAR)
    down_second = along_wide(down_first, Z_NEAR)
    g0, du0, out_m, y_m = feed(place, h3, dout, (w_up,), (w_down,), FULL, 0)
    g0, du0, out_o, y_o = feed(
        place, h3_other, dout_other, (w_up,), (w_down,), FULL, 1, shared=(g0, du0)
    )
    y_o, up_second, down_second, ca, h2 = join((y_o, up_second, down_second, ca, h2))

    ups = (up_first, up_second)
    downs = (down_first, down_second)
    g1, du1, out_o, y_o = feed(
        place, h3_other, dout_other, ups, downs, ROUND, 1, before=(out_o, y_o)
    )
    y_received = over_core(y_o)
    h2_other = over_core(h2)
    ca_other = over_core(ca[:, 512:])
    g1, du1, out_m, y_m = feed(
        place, h3, dout, ups, downs, FULL, 0, before=(out_m, y_m), shared=(g1, du1)
    )

    def plus(a, b):
        return lower(a.astype(FULL) + b.astype(FULL))

    across = (column, X_PAIRS)
    down_z = (near, Z_NEAR)

    class Sum:
        def __init__(self, partner, order=(across, down_z)):
            self.order = order
            self.fly = over_y(partner)

        def first(self, own):
            which, pairs = self.order[0]
            away_half = lower(half_of(own, 1 - which) + half_of(self.fly, 1 - which).astype(FULL))
            self.kept = half_of(own, which) + half_of(self.fly, which).astype(FULL)
            self.fly = along_wide(away_half, pairs)

        def second(self):
            which, pairs = self.order[1]
            total = self.kept + self.fly.astype(FULL)
            self.kept = half_of(total, which)
            self.fly = along_wide(lower(half_of(total, 1 - which)), pairs)

        def far(self):
            self.kept = plus(self.kept, self.fly)
            self.fly = along_wide(self.kept, Z_FAR)

        def back(self):
            self.kept = plus(self.kept, self.fly)
            self.fly = along_wide(self.kept, self.order[1][1])

        def along(self):
            self.kept = ordered(self.kept, self.fly, self.order[1][0])
            self.fly = along_wide(self.kept, self.order[0][1])

        def end(self):
            return ordered(self.kept, self.fly, self.order[0][0]).astype(FULL)

    def sync(in_flight, *values):
        done = join((*[each.fly for each in in_flight], *values))
        for each, fly in zip(in_flight, done):
            each.fly = fly
        return done[len(in_flight) :]

    class Row:
        def __init__(self, value, step):
            self.kept = value
            self.fly = step(value)

        def then(self, step):
            self.kept = self.kept + self.fly
            self.fly = step(self.kept)

    up1 = up_grad(h3, h3_other, du1, ROUND)
    up1, g1, du0, g0 = join((up1, g1, du0, g0))
    up = Sum(up1)
    down1 = down_grad(g1, dout, dout_other, ROUND)
    (y_received, down1) = join((y_received, down1))
    dx1, dself, dcross, dcq, dck, dcv, sums = middle_back(
        place, y_m, y_received, x1, x2, dout, cq, norm_gain, wq, ck, cv, wc
    )
    du0, dself = join((du0, dself))
    up0 = up_grad(h3, h3_other, du0, FULL)
    dself_other = over_core(dself)
    dself, dself_other, dcross, dcq, down1, up0, g0 = sync(
        [up], dself, dself_other, dcross, dcq, down1, up0, g0
    )

    down = Sum(down1, (down_z, across))
    up.first(up0)
    do0, do1 = pull(place, dself, dself_other, (w_out, out_y))
    dcross_other = over_core(dcross)
    dcq_other = over_core(dcq[:, 512:])
    d_pair = jnp.stack([dck, dcv], axis=1)
    d_pair_other = over_core(d_pair[2:])
    dq1, dk1, dv1 = self_back(limit, q1, k1, v1, o1, do1, lse1)
    dq1, dcross_other, dcq_other, d_pair_other = sync(
        [up], dq1, dcross_other, dcq_other, d_pair_other
    )

    up.second()
    d_pair = lower(d_pair[:2] + d_pair_other)
    qkv1 = qkv_grad(place, h1, (dq1, dk1, dv1), ROUND)
    down0 = down_grad(g0, dout, dout_other, FULL)
    cross = (h2, h2_other, dcq, dcq_other, text)
    outer = (dself, dself_other, ca, ca_other, dcross, dcross_other)
    into1 = cross_in_grad(1, *cross, d_pair[1], ROUND)
    qkv1, into1, do0, down0 = sync([down, up], qkv1, into1, do0, down0)

    qkv = Sum(qkv1)
    down.first(down0)
    up.far()
    dq0, dk0, dv0 = self_back(limit, q0, k0, v0, o0, do0, lse0)
    grads = (dq0, dk0, dv0, dq1, dk1, dv1)
    yo = first_back(away, grads, w_qkv, qkv_first, qkv_second, ROUND)
    dq0, yo = sync([down, up], dq0, yo)

    down.second()
    up.back()
    y_received = over_core(yo)
    qkv0 = qkv_grad(place, h1, (dq0, dk0, dv0), FULL)
    grads = (dq0, dk0, dv0, dq1, dk1, dv1)
    ym = first_back(place, grads, w_qkv, qkv_first, qkv_second, FULL)
    outof1 = outputs_grad(place, 1, o1, *outer, ROUND)
    qkv0, ym, y_received, outof1, x2 = sync(
        [qkv, down, up], qkv0, ym, y_received, outof1, x2
    )

    cross_in = Sum(into1)
    qkv.first(qkv0)
    down.far()
    up.along()
    grad_frames, first_sums = frames_back(place, ym, y_received, dx1, frames, norm_gain)
    norms = Row(sums + first_sums, over_core)
    into0 = cross_in_grad(0, *cross, d_pair[0], FULL)
    outof0 = outputs_grad(place, 0, o0, *outer, FULL)
    text_part = 0.0
    for g, weights in ((0, w_cross_kv), (1, cross_kv_y)):
        for c in range(2):
            text_part = text_part + nt(d_pair[g, c], weights[c])
    texts = Row(text_part, over_core)
    out_rows = lower(x2 + out_m + over_core(out_o).astype(FULL))
    into0, outof0, grad_frames, out_rows = sync(
        [qkv, down, norms, texts], into0, outof0, grad_frames, out_rows
    )

    qkv.second()
    down.back()
    norms.then(over_y)
    text_grad = lower(texts.kept + texts.fly)
    (outof1,) = sync([cross_in, norms], outof1)

    outs = Sum(outof1)
    cross_in.first(into0)
    norms.then(lambda v: along_wide(v, X_PAIRS))
    text_away = over_y(text_grad)
    (text_away,) = sync([qkv, down, up], text_away)

    qkv.far()
    down.along()
    grad_up = up.end()
    grad_text = ordered(text_grad[None], text_away[None], side)
    grad_up, grad_text = sync([outs, cross_in, norms], grad_up, grad_text)

    outs.first(outof0)
    cross_in.second()
    norms.then(lambda v: along_wide(v, Z_NEAR))
    sync([qkv, down])

    qkv.back()
    grad_down = down.end()
    (grad_down,) = sync([outs, cross_in, norms], grad_down)

    outs.second()
    cross_in.far()
    norms.then(lambda v: along_wide(v, Z_FAR))
    sync([qkv, outs])

    qkv.along()
    outs.far()
    sync([cross_in, norms])

    cross_in.back()
    sums = norms.kept + norms.fly
    sync([outs])

    outs.back()
    sync([cross_in, qkv])

    cross_in.along()
    grad_qkv = qkv.end().reshape(3, width, 256)
    sync([outs])
    outs.along()
    grad_cross_in = cross_in.end()
    grad_outs = outs.end()
    return (
        out_rows,
        grad_frames,
        grad_text,
        sums[0:6:2],
        sums[1:6:2],
        grad_qkv,
        grad_outs[:256],
        grad_cross_in[:width],
        grad_cross_in[width:].reshape(2, width, 256),
        grad_outs[256:],
        grad_up,
        grad_down,
    )


def solution(mesh):
    chips = dict(mesh.shape) == {"wide": 8, "narrow": 4}
    return jax.shard_map(
        chip_local if chips else general_local,
        mesh=mesh,
        in_specs=(
            P(("wide", "narrow"), None),
            P("wide", None, None),
            P("wide"),
            P(("wide", "narrow")),
            P(),
            P(),
            P(None, None, "narrow"),
            P("narrow", None),
            P(None, "narrow"),
            P(None, None, "narrow"),
            P("narrow", None),
            P(None, "narrow"),
            P("narrow", None),
            P(("wide", "narrow"), None),
        ),
        out_specs=(
            P(("wide", "narrow"), None),
            P(("wide", "narrow"), None),
            P("wide", None, None),
            P(),
            P(),
            P(None, None, "narrow"),
            P("narrow", None),
            P(None, "narrow"),
            P(None, None, "narrow"),
            P("narrow", None),
            P(None, "narrow"),
            P("narrow", None),
        ),
        check_vma=False,
    )
```

```python
import functools

import jax
import jax.numpy as jnp
from jax import lax
from jax.experimental import pallas as pl
from jax.experimental.pallas import tpu as pltpu
from jax.sharding import PartitionSpec as P

HEAD = 64


EPS = 1e-05
NEG = -1e30


def lower(values_in):
    return values_in.astype(jnp.bfloat16)


def product(left_side, right_side, transposed):
    if transposed:
        return lax.dot_general(
            left_side, right_side, (((1,), (1,)), ((), ())), preferred_element_type=jnp.float32
        )
    return jnp.dot(left_side, right_side, preferred_element_type=jnp.float32)


def outer_sum(left_side, right_side):
    return lax.dot_general(
        left_side, right_side, (((0,), (0,)), ((), ())), preferred_element_type=jnp.float32
    )


def normalize(values_in, gain_row, bias_row):
    row_mean = jnp.mean(values_in, axis=-1, keepdims=True)
    centered = values_in - row_mean
    inverse = lax.rsqrt(jnp.mean(centered * centered, axis=-1, keepdims=True) + EPS)
    scaled = centered * inverse
    return (scaled * gain_row + bias_row, scaled, inverse)


def normalize_back(upstream, scaled, inverse, gain_row):
    weighted = upstream * gain_row
    inner_mean = jnp.mean(weighted, axis=-1, keepdims=True)
    along_mean = jnp.mean(weighted * scaled, axis=-1, keepdims=True)
    grad_input = inverse * (weighted - inner_mean - scaled * along_mean)
    return (grad_input, jnp.sum(upstream * scaled, axis=0), jnp.sum(upstream, axis=0))


def gelu_parts(values_in):
    normal_cdf = 0.5 * (1.0 + jax.scipy.special.erf(values_in * 0.7071067811865476))
    normal_pdf = jnp.exp(-0.5 * values_in * values_in) * 0.3989422804014327
    return (values_in * normal_cdf, normal_cdf + values_in * normal_pdf)


def scores_of(query_part, key_part, valid):
    scores = jnp.einsum(
        "bhe,khe->hbk", query_part, key_part, preferred_element_type=jnp.float32
    ) * HEAD ** (-0.5)
    return jnp.where(valid, scores, NEG)


def attend(query_part, key_part, value_part, valid):
    scores = scores_of(query_part, key_part, valid)
    row_top = jnp.max(scores, axis=-1, keepdims=True)
    weights_exp = jnp.exp(scores - row_top)
    denominator = jnp.sum(weights_exp, axis=-1, keepdims=True)
    probability = weights_exp / denominator
    mixed = jnp.einsum(
        "hbk,khe->bhe", lower(probability), value_part, preferred_element_type=jnp.float32
    )
    return (lower(mixed), (row_top + jnp.log(denominator))[..., 0])


def attend_back(query_part, key_part, value_part, valid, summary, upstream):
    scores = scores_of(query_part, key_part, valid)
    probability = jnp.exp(scores - summary[..., None])
    pressure = jnp.einsum("bhe,khe->hbk", upstream, value_part, preferred_element_type=jnp.float32)
    grad_scores = lower(
        probability * (pressure - jnp.sum(probability * pressure, axis=-1, keepdims=True))
    )
    factor = HEAD ** (-0.5)
    grad_query = (
        jnp.einsum("hbk,khe->bhe", grad_scores, key_part, preferred_element_type=jnp.float32)
        * factor
    )
    grad_key = (
        jnp.einsum("hbk,bhe->khe", grad_scores, query_part, preferred_element_type=jnp.float32)
        * factor
    )
    grad_value = jnp.einsum(
        "hbk,bhe->khe", lower(probability), upstream, preferred_element_type=jnp.float32
    )
    return (grad_query, grad_key, grad_value)


def general_local(
    frames,
    text_states,
    lengths,
    loss_mask,
    norm_gain,
    norm_bias,
    w_qkv,
    w_out,
    w_cross_q,
    w_cross_kv,
    w_cross_out,
    w_up,
    w_down,
    cotangent,
):
    row_count = frames.shape[0]
    width = frames.shape[1]
    item_count = lengths.shape[0]
    span = row_count * lax.axis_size("narrow") // item_count
    half_span = span // 2
    inner_width = w_qkv.shape[2]
    head_count = inner_width // HEAD
    text_count = text_states.shape[1]
    full_rows = item_count * span
    places = jnp.arange(span, dtype=jnp.int32)

    def spread(shard_rows):
        return lax.all_gather(shard_rows, "narrow", axis=0, tiled=True)

    def collect(left_side, right_side, transposed):
        return lax.psum_scatter(
            product(
                lax.slice_in_dim(left_side, 0, lax.axis_size("narrow") * row_count, axis=0),
                right_side,
                transposed,
            ),
            "narrow",
            scatter_dimension=0,
            tiled=True,
        )

    def causal(block_index, item_limit):
        query_place = block_index * half_span + jnp.arange(half_span, dtype=jnp.int32)
        return (places[None, :] <= query_place[:, None]) & (places[None, :] < item_limit)

    frame_rows = frames.astype(jnp.float32)
    normed_one, scaled_one, inverse_one = normalize(frame_rows, norm_gain[0], norm_bias[0])
    first_input = spread(lower(normed_one))
    triple = lower(
        jnp.einsum("rd,cde->cre", first_input, w_qkv, preferred_element_type=jnp.float32)
    )
    triple = triple.reshape(3, item_count, span, head_count, HEAD)

    def self_item(packed):
        query_part, key_part, value_part, item_limit = packed
        mixed_list = []
        summary_list = []
        for block_index in range(2):
            mixed, summary = attend(
                query_part[block_index * half_span : (block_index + 1) * half_span],
                key_part,
                value_part,
                causal(block_index, item_limit),
            )
            mixed_list.append(mixed)
            summary_list.append(summary)
        return (jnp.concatenate(mixed_list, axis=0), jnp.stack(summary_list, axis=0))

    attended, self_summary = lax.map(self_item, (triple[0], triple[1], triple[2], lengths))
    attended_flat = attended.reshape(full_rows, inner_width)
    first_rows = frame_rows + collect(attended_flat, w_out, False)
    normed_two, scaled_two, inverse_two = normalize(first_rows, norm_gain[1], norm_bias[1])
    second_input = spread(lower(normed_two))
    cross_query = lower(product(second_input, w_cross_q, False)).reshape(
        item_count, span, head_count, HEAD
    )
    cross_pair = lower(
        jnp.einsum("ntd,cde->cnte", text_states, w_cross_kv, preferred_element_type=jnp.float32)
    )
    cross_pair = cross_pair.reshape(2, item_count, text_count, head_count, HEAD)

    def cross_item(packed):
        query_part, key_part, value_part = packed
        return attend(query_part, key_part, value_part, True)

    cross_mixed, cross_summary = lax.map(cross_item, (cross_query, cross_pair[0], cross_pair[1]))
    cross_flat = cross_mixed.reshape(full_rows, inner_width)
    second_rows = first_rows + collect(cross_flat, w_cross_out, False)
    normed_three, scaled_three, inverse_three = normalize(second_rows, norm_gain[2], norm_bias[2])
    upstream = cotangent.astype(jnp.float32) * loss_mask.astype(jnp.float32)[:, None]
    ffn_grad = lower(upstream)
    ffn_input = spread(lower(normed_three))
    hidden_pre = product(ffn_input, w_up, False)
    active, slope = gelu_parts(hidden_pre)
    active = lower(active)
    out_rows = second_rows + collect(active, w_down, False)
    ffn_full = spread(ffn_grad)
    grad_down = outer_sum(active, ffn_full)
    grad_hidden = lower(product(ffn_full, w_down, True) * slope)
    grad_up = outer_sum(ffn_input, grad_hidden)
    back_three = collect(grad_hidden, w_up, True)
    grad_up, grad_down = (grad_up, grad_down)
    grad_in_three, gain_three, bias_three = normalize_back(
        back_three, scaled_three, inverse_three, norm_gain[2]
    )
    grad_second = upstream + grad_in_three
    cross_full = spread(lower(grad_second))
    grad_cross_out = outer_sum(cross_flat, cross_full)
    cross_upstream = lower(product(cross_full, w_cross_out, True)).reshape(
        item_count, span, head_count, HEAD
    )

    def cross_back(packed):
        query_part, key_part, value_part, summary, upstream_item = packed
        return attend_back(query_part, key_part, value_part, True, summary, upstream_item)

    grad_cq, grad_ck, grad_cv = lax.map(
        cross_back, (cross_query, cross_pair[0], cross_pair[1], cross_summary, cross_upstream)
    )
    grad_cq = lower(grad_cq).reshape(full_rows, inner_width)
    grad_pair = lower(jnp.stack((grad_ck, grad_cv), axis=0)).reshape(
        2, item_count, text_count, inner_width
    )
    grad_cross_q = outer_sum(second_input, grad_cq)
    grad_cross_kv = jnp.einsum(
        "ntd,cnte->cde", text_states, grad_pair, preferred_element_type=jnp.float32
    )
    grad_cross_q, grad_cross_kv, grad_cross_out = (grad_cross_q, grad_cross_kv, grad_cross_out)
    text_partial = jnp.einsum(
        "cnte,cde->ntd", grad_pair, w_cross_kv, preferred_element_type=jnp.float32
    )
    grad_text = lower(lax.psum(text_partial, "narrow"))
    back_two = collect(grad_cq, w_cross_q, True)
    grad_in_two, gain_two, bias_two = normalize_back(
        back_two, scaled_two, inverse_two, norm_gain[1]
    )
    grad_first = grad_second + grad_in_two
    self_full = spread(lower(grad_first))
    grad_out = outer_sum(attended_flat, self_full)
    self_upstream = lower(product(self_full, w_out, True)).reshape(
        item_count, span, head_count, HEAD
    )

    def self_back(packed):
        query_part, key_part, value_part, item_limit, summary, upstream_item = packed
        query_list = []
        key_list = []
        value_list = []
        for block_index in range(2):
            lower_row = block_index * half_span
            grad_query, grad_key, grad_value = attend_back(
                query_part[lower_row : lower_row + half_span],
                key_part,
                value_part,
                causal(block_index, item_limit),
                summary[block_index],
                upstream_item[lower_row : lower_row + half_span],
            )
            query_list.append(grad_query)
            key_list.append(grad_key)
            value_list.append(grad_value)
        return (
            jnp.concatenate(query_list, axis=0),
            key_list[0] + key_list[1],
            value_list[0] + value_list[1],
        )

    grad_q, grad_k, grad_v = lax.map(
        self_back, (triple[0], triple[1], triple[2], lengths, self_summary, self_upstream)
    )
    grad_triple = lower(jnp.stack((grad_q, grad_k, grad_v), axis=0)).reshape(
        3, full_rows, inner_width
    )
    grad_qkv = jnp.einsum(
        "rd,cre->cde", first_input, grad_triple, preferred_element_type=jnp.float32
    )
    grad_qkv, grad_out = (grad_qkv, grad_out)
    merged = grad_triple.transpose(1, 0, 2).reshape(full_rows, 3 * inner_width)
    stacked_weights = w_qkv.transpose(0, 2, 1).reshape(3 * inner_width, width)
    back_one = collect(merged, stacked_weights, False)
    grad_in_one, gain_one, bias_one = normalize_back(
        back_one, scaled_one, inverse_one, norm_gain[0]
    )
    grad_frames = lower(grad_first + grad_in_one)
    gain_terms = jnp.stack((gain_one, gain_two, gain_three), axis=0)
    bias_terms = jnp.stack((bias_one, bias_two, bias_three), axis=0)
    grad_norm_gain, grad_norm_bias = lax.psum((gain_terms, bias_terms), ("wide", "narrow"))
    grad_qkv, grad_out, grad_cross_q, grad_cross_kv, grad_cross_out, grad_up, grad_down = lax.psum(
        (grad_qkv, grad_out, grad_cross_q, grad_cross_kv, grad_cross_out, grad_up, grad_down),
        "wide",
    )
    return (
        lower(out_rows),
        grad_frames,
        grad_text,
        grad_norm_gain,
        grad_norm_bias,
        grad_qkv,
        grad_out,
        grad_cross_q,
        grad_cross_kv,
        grad_cross_out,
        grad_up,
        grad_down,
    )


ROUND = jnp.bfloat16
FULL = jnp.float32
CORE_PAIRS = ((0, 1), (1, 0), (2, 3), (3, 2))
Y_PAIRS = ((0, 2), (2, 0), (1, 3), (3, 1))
X_PAIRS = tuple((i, i ^ 1) for i in range(8))
Z_INWARD = ((0, 2), (1, 3), (6, 4), (7, 5))
Z_MIDDLE = ((2, 4), (4, 2), (3, 5), (5, 3))
Z_OUTWARD = ((2, 0), (3, 1), (4, 6), (5, 7))
Z_NEAR = tuple((i, i ^ 2) for i in range(8))
Z_FAR = tuple((i, i ^ 4) for i in range(8))
MIB = 1 << 20


def nt(a, b):
    return lax.dot_general(a, b, (((1,), (1,)), ((), ())), preferred_element_type=FULL)


def nn(a, b):
    return lax.dot_general(a, b, (((1,), (0,)), ((), ())), preferred_element_type=FULL)


def tn(a, b):
    return lax.dot_general(a, b, (((0,), (0,)), ((), ())), preferred_element_type=FULL)


def shape(dims, kind):
    return jax.ShapeDtypeStruct(dims, kind)


def resident(dims):
    zeros = (0,) * len(dims)
    return pl.BlockSpec(dims, lambda i, s: zeros, pipeline_mode=pl.Buffered(1))


def rows_of(block, width):
    return pl.BlockSpec((block, width), lambda i, s: (i, 0))


def brief():
    return pl.CostEstimate(flops=1000, bytes_accessed=1000, transcendentals=0)


def params(mib):
    return pltpu.CompilerParams(vmem_limit_bytes=mib * MIB)


def norm_parts(v):
    centered = v - jnp.mean(v, axis=-1, keepdims=True)
    inverse = lax.rsqrt(jnp.mean(centered * centered, axis=-1, keepdims=True) + EPS)
    return centered * inverse, inverse


def norm_pull(y, scaled, inverse, gain_row):
    weighted = y * gain_row
    inner = jnp.mean(weighted, axis=-1, keepdims=True)
    along = jnp.mean(weighted * scaled, axis=-1, keepdims=True)
    return inverse * (weighted - inner - scaled * along)


def first_project_kernel(
    place_ref, mine_ref, other_ref, gain_ref, bias_ref, weight_ref, h_ref, *out_refs
):
    half = pl.program_id(0)

    def run(source):
        for start in range(0, source.shape[0], 208):
            part = slice(start, start + 208)
            scaled, _ = norm_parts(source[part, :].astype(FULL))
            h = lower(scaled * gain_ref[0:1, :] + bias_ref[0:1, :])
            h_ref[part, :] = h
            for c, out_ref in enumerate(out_refs):
                out_ref[part, :] = lower(nn(h, weight_ref[c]))

    @pl.when(half == 0)
    def _():
        run(mine_ref)

    @pl.when(half == 1)
    def _():
        run(other_ref)


def first_project(place, mine, other, gains, biases, weights):
    rows, depth = mine.shape
    count, _, wide = weights.shape
    out = pl.BlockSpec((rows, wide), lambda i, s: ((i + s[0]) % 2, 0))
    return pl.pallas_call(
        first_project_kernel,
        grid_spec=pltpu.PrefetchScalarGridSpec(
            num_scalar_prefetch=1,
            grid=(2,),
            in_specs=[resident(a.shape) for a in (mine, other, gains, biases, weights)],
            out_specs=[rows_of(rows, depth)] + [out] * count,
        ),
        out_shape=[shape((2 * rows, depth), ROUND)] + [shape((2 * rows, wide), ROUND)] * count,
        compiler_params=params(40),
        cost_estimate=brief(),
        name="first_project",
    )(place, mine, other, gains, biases, weights)


def project_kernel(place_ref, h_ref, first_ref, second_ref, *out_refs):
    depth = first_ref.shape[1]
    near = place_ref[1]
    left = h_ref[:, pl.ds(pl.multiple_of(near * depth, 128), depth)]
    right = h_ref[:, pl.ds(pl.multiple_of((1 - near) * depth, 128), depth)]
    for c, out_ref in enumerate(out_refs):
        out_ref[...] = lower(nn(left, first_ref[c]) + nn(right, second_ref[c]))


def project(place, h, first, second):
    rows, depth = h.shape[0] // 2, h.shape[1]
    count, _, wide = first.shape
    out = pl.BlockSpec((rows, wide), lambda i, s: ((i + s[0]) % 2, 0))
    return pl.pallas_call(
        project_kernel,
        grid_spec=pltpu.PrefetchScalarGridSpec(
            num_scalar_prefetch=1,
            grid=(2,),
            in_specs=[rows_of(rows, depth), resident(first.shape), resident(second.shape)],
            out_specs=[out] * count,
        ),
        out_shape=[shape((2 * rows, wide), ROUND)] * count,
        compiler_params=params(32),
        cost_estimate=brief(),
        name="project",
    )(place, h, first, second)


def pull_kernel(place_ref, mine_ref, other_ref, *refs):
    half = pl.program_id(0)
    count = len(refs) // 2

    def run(source):
        for weight_ref, out_ref in zip(refs[:count], refs[count:]):
            out_ref[...] = lower(nt(source[...], weight_ref[...]))

    @pl.when(half == 0)
    def _():
        run(mine_ref)

    @pl.when(half == 1)
    def _():
        run(other_ref)


def pull(place, mine, other, weights):
    rows = mine.shape[0]
    wide = weights[0].shape[0]
    out = pl.BlockSpec((rows, wide), lambda i, s: ((i + s[0]) % 2, 0))
    return pl.pallas_call(
        pull_kernel,
        grid_spec=pltpu.PrefetchScalarGridSpec(
            num_scalar_prefetch=1,
            grid=(2,),
            in_specs=[resident(a.shape) for a in (mine, other, *weights)],
            out_specs=[out] * len(weights),
        ),
        out_shape=[shape((2 * rows, wide), ROUND)] * len(weights),
        compiler_params=params(32),
        cost_estimate=brief(),
        name="pull",
    )(place, mine, other, *weights)


def blocks_of(span, block):
    return [(start, min(block, span - start)) for start in range(0, span, block)]


def self_forward_kernel(
    limit_ref, q_ref, k_ref, v_ref, o_ref, lse_ref, *, span, floor, block
):
    limit = limit_ref[0]
    lane = lax.broadcasted_iota(jnp.int32, (1, 128), 1)
    row = lax.broadcasted_iota(jnp.int32, (128, 1), 0)
    zero = jnp.zeros((), ROUND)
    value_turned = v_ref[...].T
    for start, size in blocks_of(span, block):
        end = start + size
        mixed_list = []
        for h in range(2):
            own_lanes = (lane < HEAD) if h == 0 else (lane >= HEAD)
            query = jnp.where(own_lanes, q_ref[start:end, :] * HEAD ** (-0.5), zero)
            parts = []
            for low in range(0, end, block):
                high = min(low + block, end)
                scores = nt(k_ref[low:high, :], query)
                if low == start:
                    key = lax.broadcasted_iota(jnp.int32, (size, size), 0)
                    valid = key <= lax.broadcasted_iota(jnp.int32, (size, size), 1)
                    if high > floor:
                        valid = valid & (key + low < limit)
                    scores = jnp.where(valid, scores, NEG)
                elif high > floor:
                    key = lax.broadcasted_iota(jnp.int32, (high - low, 1), 0)
                    scores = jnp.where(key + low < limit, scores, NEG)
                parts.append((low, high, scores))
            top = functools.reduce(
                jnp.maximum, [jnp.max(s, axis=0, keepdims=True) for _, _, s in parts]
            )
            total = 0.0
            mixed = 0.0
            for low, high, scores in parts:
                weights_exp = jnp.exp(scores - top)
                total = total + jnp.sum(weights_exp, axis=0, keepdims=True)
                mixed = mixed + nn(value_turned[:, low:high], lower(weights_exp))
            mixed_list.append(mixed / total)
            lse_ref[0, h : h + 1, start:end] = top + jnp.log(total)
        o_ref[start:end, :] = lower(jnp.where(row < HEAD, mixed_list[0], mixed_list[1]).T)


def self_forward(limit, q, k, v):
    span, wide = q.shape
    pairs = wide // 128
    floor = (span - span // 8 + 1) // 128 * 128
    pair = pl.BlockSpec((span, 128), lambda p, s: (0, p))
    return pl.pallas_call(
        functools.partial(self_forward_kernel, span=span, floor=floor, block=512),
        grid_spec=pltpu.PrefetchScalarGridSpec(
            num_scalar_prefetch=1,
            grid=(pairs,),
            in_specs=[pair] * 3,
            out_specs=[pair, pl.BlockSpec((1, 8, span), lambda p, s: (p, 0, 0))],
        ),
        out_shape=[shape((span, wide), ROUND), shape((pairs, 8, span), FULL)],
        compiler_params=params(56),
        cost_estimate=brief(),
        name="self_forward",
    )(limit, q, k, v)


def self_back_kernel(
    limit_ref, q_ref, k_ref, v_ref, o_ref, do_ref, lse_ref, dq_ref, dk_ref, dv_ref, dqt,
    *, span, floor, block
):
    limit = limit_ref[0]
    lane = lax.broadcasted_iota(jnp.int32, (1, 128), 1)
    row = lax.broadcasted_iota(jnp.int32, (128, 1), 0)
    zero = jnp.zeros((), ROUND)
    factor = HEAD ** (-0.5)
    product_rows = do_ref[...].astype(FULL) * o_ref[...].astype(FULL)
    high = lower(product_rows)
    rest = lower(product_rows - high.astype(FULL))
    pick = lower(
        jnp.concatenate(
            [
                jnp.where(lane < HEAD, 1.0, 0.0),
                jnp.where(lane >= HEAD, 1.0, 0.0),
                jnp.zeros((6, 128), FULL),
            ],
            axis=0,
        )
    )
    delta = nt(pick, high) + nt(pick, rest)
    for start, size in blocks_of(span, block):
        end = start + size
        key = k_ref[start:end, :]
        value = v_ref[start:end, :]
        key_turned = key.T
        dk = 0.0
        dv = 0.0
        dq_add = 0.0
        for h in range(2):
            own_lanes = (lane < HEAD) if h == 0 else (lane >= HEAD)
            own_rows = (row < HEAD) if h == 0 else (row >= HEAD)
            query = jnp.where(own_lanes, q_ref[start:, :] * factor, zero)
            pulled = jnp.where(own_lanes, do_ref[start:, :], zero)
            probability = jnp.exp(nt(key, query) - lse_ref[0, h : h + 1, start:])
            pressure = nt(value, pulled)
            below = lax.broadcasted_iota(jnp.int32, (size, size), 0)
            across = lax.broadcasted_iota(jnp.int32, (size, size), 1)
            corner = jnp.where(below <= across, probability[:, :size], 0.0)
            if end < span:
                probability = jnp.concatenate([corner, probability[:, size:]], axis=1)
            else:
                probability = corner
            if end > floor:
                place = lax.broadcasted_iota(jnp.int32, (size, 1), 0) + start
                probability = jnp.where(place < limit, probability, 0.0)
            grad_scores = lower(probability * (pressure - delta[h : h + 1, start:]))
            dv = dv + nn(lower(probability), pulled)
            dk = dk + nn(grad_scores, query)
            dq_add = dq_add + nn(jnp.where(own_rows, key_turned, zero), grad_scores)
        dk_ref[start:end, :] = lower(dk)
        dv_ref[start:end, :] = lower(dv)
        if start == 0:
            dqt[...] = dq_add
        else:
            dqt[:, start:] += dq_add
    dq_ref[...] = lower(dqt[...].T * factor)


def self_back(limit, q, k, v, o, do, lse):
    span, wide = q.shape
    pairs = wide // 128
    floor = (span - span // 8 + 1) // 128 * 128
    pair = pl.BlockSpec((span, 128), lambda p, s: (0, p))
    return pl.pallas_call(
        functools.partial(self_back_kernel, span=span, floor=floor, block=256),
        grid_spec=pltpu.PrefetchScalarGridSpec(
            num_scalar_prefetch=1,
            grid=(pairs,),
            in_specs=[pair] * 5 + [pl.BlockSpec((1, 8, span), lambda p, s: (p, 0, 0))],
            out_specs=[pair] * 3,
            scratch_shapes=[pltpu.VMEM((128, span), FULL)],
        ),
        out_shape=[shape((span, wide), ROUND)] * 3,
        compiler_params=params(48),
        cost_estimate=brief(),
        name="self_back",
    )(limit, q, k, v, o, do, lse)


def by_head(values_in, reduce, empty):
    lane = lax.broadcasted_iota(jnp.int32, (1, 128), 1)
    pieces = []
    for start in range(0, values_in.shape[1], 128):
        part = values_in[:, start : start + 128]
        first = reduce(jnp.where(lane < HEAD, part, empty), axis=1, keepdims=True)
        second = reduce(jnp.where(lane >= HEAD, part, empty), axis=1, keepdims=True)
        pieces.append(jnp.where(lane < HEAD, first, second))
    return jnp.concatenate(pieces, axis=1)


def cross_probability(query, keys):
    scores = nt(query * HEAD ** (-0.5), keys)
    weights_exp = jnp.exp(scores - by_head(scores, jnp.max, NEG))
    return weights_exp / by_head(weights_exp, jnp.sum, 0.0)


def middle_forward_kernel(
    place_ref, frame_ref, a0_ref, a1_ref, a2_ref, a3_ref, gain_ref, bias_ref, *refs
):
    mixed = (a0_ref, a1_ref, a2_ref, a3_ref)
    wo, wq, wc = refs[0:4], refs[4:8], refs[12:16]
    ck0_ref, ck1_ref, cv0_ref, cv1_ref = refs[8:12]
    x1_ref, x2_ref, h2_ref, cq_ref, ca_ref, h3_ref = refs[16:]
    x1 = frame_ref[...].astype(FULL)
    for g in range(4):
        x1 = x1 + nn(mixed[g][...], wo[g][...])
    x1_ref[...] = x1
    scaled, _ = norm_parts(x1)
    h2 = lower(scaled * gain_ref[1:2, :] + bias_ref[1:2, :])
    h2_ref[...] = h2
    for g in range(4):
        lanes = slice(g * 256, (g + 1) * 256)
        cq = lower(nn(h2, wq[g][...]))
        cq_ref[:, lanes] = cq
        probability = cross_probability(cq, (ck0_ref, ck1_ref)[g // 2][g % 2])
        ca_ref[:, lanes] = lower(nn(lower(probability), (cv0_ref, cv1_ref)[g // 2][g % 2]))
    crossed = 0.0
    for g in range(4):
        crossed = crossed + nn(ca_ref[:, g * 256 : (g + 1) * 256], wc[g][...])
    x2 = x1_ref[...] + crossed
    x2_ref[...] = x2
    scaled, _ = norm_parts(x2)
    h3_ref[...] = lower(scaled * gain_ref[2:3, :] + bias_ref[2:3, :])


def middle_forward(place, frames, attended, received, gains, biases, wo, wq, ck, cv, wc):
    rows, width = frames.shape
    block = 416
    steps = rows // block
    piece = pl.BlockSpec((block, 256), lambda i, s: (s[0] * steps + i, 0))
    wide = rows_of(block, width)
    return pl.pallas_call(
        middle_forward_kernel,
        grid_spec=pltpu.PrefetchScalarGridSpec(
            num_scalar_prefetch=1,
            grid=(steps,),
            in_specs=[wide, piece, piece, rows_of(block, 256), rows_of(block, 256)]
            + [resident(a.shape) for a in (gains, biases, *wo, *wq, *ck, *cv, *wc)],
            out_specs=[wide] * 6,
        ),
        out_shape=[shape((rows, width), FULL)] * 2 + [shape((rows, width), ROUND)] * 4,
        compiler_params=params(56),
        cost_estimate=brief(),
        name="middle_forward",
    )(place, frames, *attended, *received, gains, biases, *wo, *wq, *ck, *cv, *wc)


def feed_kernel(place_ref, h_ref, d_ref, *refs, parts, carried):
    ups, downs = refs[:parts], refs[parts : 2 * parts]
    before = refs[2 * parts : 2 * parts + carried]
    g_ref, du_ref, out_ref, y_ref = refs[-4:]
    h = h_ref[...]
    d = d_ref[...]
    out = 0.0
    y = 0.0
    for n, (up_ref, down_ref) in enumerate(zip(ups, downs)):
        size = down_ref.shape[0]
        if parts == 1:
            lanes = slice(0, size)
        else:
            near = place_ref[1]
            which = near if n == 0 else 1 - near
            lanes = pl.ds(pl.multiple_of(which * size, 128), size)
        u = nn(h, up_ref[...])
        active, slope = gelu_parts(u)
        g = lower(active)
        g_ref[:, lanes] = g
        du = lower(nt(d, down_ref[...]) * slope)
        du_ref[:, lanes] = du
        out = out + nn(g, down_ref[...])
        y = y + nt(du, up_ref[...])
    if carried:
        out = before[0][...] + out
        y = before[1][...] + y
    out_ref[...] = out.astype(out_ref.dtype)
    y_ref[...] = y.astype(y_ref.dtype)


def feed(place, h, d, ups, downs, kind, half, before=(), shared=()):
    rows, width = h.shape
    block = 416
    steps = rows // block
    hidden = sum(a.shape[0] for a in downs)
    wide = rows_of(block, width)
    kept = pl.BlockSpec((block, hidden), lambda i, s: (i + half * steps, 0))
    there = pl.BlockSpec(memory_space=pl.ANY)
    parts = len(ups)
    at = 3 + 2 * parts + len(before)
    return pl.pallas_call(
        functools.partial(feed_kernel, parts=parts, carried=len(before)),
        grid_spec=pltpu.PrefetchScalarGridSpec(
            num_scalar_prefetch=1,
            grid=(steps,),
            in_specs=[wide, wide]
            + [resident(a.shape) for a in (*ups, *downs)]
            + [wide] * len(before)
            + [there] * len(shared),
            out_specs=[kept, kept, wide, wide],
        ),
        out_shape=[shape((2 * rows, hidden), ROUND)] * 2 + [shape((rows, width), kind)] * 2,
        input_output_aliases={at: 0, at + 1: 1} if shared else {},
        compiler_params=params(58),
        cost_estimate=brief(),
        name="feed",
    )(place, h, d, *ups, *downs, *before, *shared)


def up_grad_kernel(mine_ref, other_ref, du_ref, out_ref):
    rows = mine_ref.shape[0]
    total = tn(mine_ref[...], du_ref[:rows, :]) + tn(other_ref[...], du_ref[rows:, :])
    out_ref[...] = total.astype(out_ref.dtype)


def up_grad(mine, other, du, kind):
    rows, width = mine.shape
    hidden = du.shape[1]
    tile = 512
    whole = pl.BlockSpec((rows, width), lambda i: (0, 0), pipeline_mode=pl.Buffered(1))
    return pl.pallas_call(
        up_grad_kernel,
        grid=(hidden // tile,),
        in_specs=[whole, whole, pl.BlockSpec((2 * rows, tile), lambda i: (0, i))],
        out_specs=pl.BlockSpec((width, tile), lambda i: (0, i)),
        out_shape=shape((width, hidden), kind),
        compiler_params=params(48),
        cost_estimate=brief(),
        name="up_grad",
    )(mine, other, du)


def down_grad_kernel(g_ref, mine_ref, other_ref, out_ref):
    rows = mine_ref.shape[0]
    total = tn(g_ref[:rows, :], mine_ref[...]) + tn(g_ref[rows:, :], other_ref[...])
    out_ref[...] = total.astype(out_ref.dtype)


def down_grad(g, mine, other, kind, first=0, tiles=2):
    rows, width = mine.shape
    tile = 512
    whole = pl.BlockSpec((rows, width), lambda i: (0, 0), pipeline_mode=pl.Buffered(1))
    return pl.pallas_call(
        down_grad_kernel,
        grid=(tiles,),
        in_specs=[pl.BlockSpec((2 * rows, tile), lambda i: (0, i + first)), whole, whole],
        out_specs=pl.BlockSpec((tile, width), lambda i: (i, 0)),
        out_shape=shape((tiles * tile, width), kind),
        compiler_params=params(48),
        cost_estimate=brief(),
        name="down_grad",
    )(g, mine, other)


def qkv_grad_kernel(place_ref, h_ref, *refs):
    out_ref = refs[-1]
    rows, width = h_ref.shape[0] // 2, h_ref.shape[1]
    core = place_ref[0]
    total = [0.0] * 3
    for half in range(2):
        turned = h_ref[half * rows : (half + 1) * rows, :].T
        at = pl.multiple_of((core if half == 0 else 1 - core) * rows, 16)
        for c in range(3):
            total[c] = total[c] + nn(turned, refs[c][pl.ds(at, rows), :])
    for c in range(3):
        out_ref[c * width : (c + 1) * width, :] = total[c].astype(out_ref.dtype)


def qkv_grad(place, h, grads, kind):
    width = h.shape[1]
    wide = grads[0].shape[1]
    return pl.pallas_call(
        qkv_grad_kernel,
        grid_spec=pltpu.PrefetchScalarGridSpec(
            num_scalar_prefetch=1,
            grid=(1,),
            in_specs=[resident(a.shape) for a in (h, *grads)],
            out_specs=resident((3 * width, wide)),
        ),
        out_shape=shape((3 * width, wide), kind),
        compiler_params=params(48),
        cost_estimate=brief(),
        name="qkv_grad",
    )(place, h, *grads)


def cross_in_grad_kernel(mine_ref, other_ref, dm_ref, do_ref, text_ref, pair_ref, out_ref):
    width = mine_ref.shape[1]
    total = tn(mine_ref[...], dm_ref[...]) + tn(other_ref[...], do_ref[...])
    out_ref[:width, :] = total.astype(out_ref.dtype)
    turned = text_ref[...].T
    for c in range(2):
        part = nn(turned, pair_ref[c]).astype(out_ref.dtype)
        out_ref[(1 + c) * width : (2 + c) * width, :] = part


def cross_in_grad(group, mine, other, d_mine, d_other, text, pair, kind):
    rows, width = mine.shape
    lanes = pl.BlockSpec((rows, 256), lambda i: (0, group))

    def whole(a):
        zeros = (0,) * a.ndim
        return pl.BlockSpec(a.shape, lambda i: zeros)

    return pl.pallas_call(
        cross_in_grad_kernel,
        grid=(1,),
        in_specs=[whole(mine), whole(other), lanes, lanes, whole(text), whole(pair)],
        out_specs=pl.BlockSpec((3 * width, 256), lambda i: (0, 0)),
        out_shape=shape((3 * width, 256), kind),
        compiler_params=params(48),
        cost_estimate=brief(),
        name="cross_in_grad",
    )(mine, other, d_mine, d_other, text, pair)


def outputs_grad_kernel(
    place_ref, o_ref, sm_ref, so_ref, am_ref, ao_ref, cm_ref, co_ref, out_ref
):
    rows = sm_ref.shape[0]
    core = place_ref[0]
    mine = o_ref[pl.ds(pl.multiple_of(core * rows, 16), rows), :]
    other = o_ref[pl.ds(pl.multiple_of((1 - core) * rows, 16), rows), :]
    out_ref[:256, :] = (tn(mine, sm_ref[...]) + tn(other, so_ref[...])).astype(out_ref.dtype)
    total = tn(am_ref[...], cm_ref[...]) + tn(ao_ref[...], co_ref[...])
    out_ref[256:, :] = total.astype(out_ref.dtype)


def outputs_grad(place, group, o, dself, dself_other, ca, ca_other, dcross, dcross_other, kind):
    rows, width = dself.shape
    lanes = pl.BlockSpec((rows, 256), lambda i, s: (0, group))
    whole = resident((rows, width))
    return pl.pallas_call(
        outputs_grad_kernel,
        grid_spec=pltpu.PrefetchScalarGridSpec(
            num_scalar_prefetch=1,
            grid=(1,),
            in_specs=[resident(o.shape), whole, whole, lanes, lanes, whole, whole],
            out_specs=resident((512, width)),
        ),
        out_shape=shape((512, width), kind),
        compiler_params=params(48),
        cost_estimate=brief(),
        name="outputs_grad",
    )(place, o, dself, dself_other, ca, ca_other, dcross, dcross_other)


def middle_back_kernel(
    place_ref, ym_ref, yr_ref, x1_ref, x2_ref, d_ref, cq_ref, gain_ref, *refs
):
    wq, wc = refs[0:4], refs[8:12]
    ck0_ref, ck1_ref, cv0_ref, cv1_ref = refs[4:8]
    dx1_ref, dself_ref, dcross_ref, dcq_ref, dck_ref, dcv_ref, sums_ref = refs[12:19]
    dck_all, dcv_all = refs[19:]
    step = pl.program_id(0)

    @pl.when(step == 0)
    def _():
        dck_all[...] = jnp.zeros_like(dck_all)
        dcv_all[...] = jnp.zeros_like(dcv_all)
        sums_ref[...] = jnp.zeros_like(sums_ref)

    y3 = ym_ref[...] + yr_ref[...].astype(FULL)
    scaled, inverse = norm_parts(x2_ref[...])
    sums_ref[4:5, :] += jnp.sum(y3 * scaled, axis=0, keepdims=True)
    sums_ref[5:6, :] += jnp.sum(y3, axis=0, keepdims=True)
    dx2 = d_ref[...].astype(FULL) + norm_pull(y3, scaled, inverse, gain_ref[2:3, :])
    dx1_ref[...] = dx2
    dcross = lower(dx2)
    dcross_ref[...] = dcross
    y2 = 0.0
    for g in range(4):
        lanes = slice(g * 256, (g + 1) * 256)
        keys = (ck0_ref, ck1_ref)[g // 2][g % 2]
        values = (cv0_ref, cv1_ref)[g // 2][g % 2]
        dcatt = lower(nt(dcross, wc[g][...]))
        cq = cq_ref[:, lanes]
        probability = cross_probability(cq, keys)
        weighed = nt(dcatt, values)
        inner = by_head(probability * weighed, jnp.sum, 0.0)
        dcs = lower(probability * (weighed - inner))
        dcq = lower(nn(dcs, keys) * HEAD ** (-0.5))
        dcq_ref[:, lanes] = dcq
        dck_all[g] += tn(dcs, cq * HEAD ** (-0.5))
        dcv_all[g] += tn(lower(probability), dcatt)
        y2 = y2 + nt(dcq, wq[g][...])
    scaled, inverse = norm_parts(x1_ref[...])
    sums_ref[2:3, :] += jnp.sum(y2 * scaled, axis=0, keepdims=True)
    sums_ref[3:4, :] += jnp.sum(y2, axis=0, keepdims=True)
    dx1 = dx1_ref[...] + norm_pull(y2, scaled, inverse, gain_ref[1:2, :])
    dx1_ref[...] = dx1
    dself_ref[...] = lower(dx1)

    @pl.when(step == pl.num_programs(0) - 1)
    def _():
        for every, result in ((dck_all, dck_ref), (dcv_all, dcv_ref)):
            for g in range(4):
                total = 0.0
                for h in range(4):
                    lane = lax.broadcasted_iota(jnp.int32, (1, 256), 1) // HEAD
                    total = total + jnp.where(lane == h, every[g, h * 64 : (h + 1) * 64, :], 0.0)
                result[g] = total


def middle_back(place, ym, yr, x1, x2, d, cq, gains, wq, ck, cv, wc):
    rows, width = x1.shape
    block = 416
    wide = rows_of(block, width)
    small = pl.BlockSpec((4, 64, 256), lambda i, s: (0, 0, 0))
    return pl.pallas_call(
        middle_back_kernel,
        grid_spec=pltpu.PrefetchScalarGridSpec(
            num_scalar_prefetch=1,
            grid=(rows // block,),
            in_specs=[wide] * 6 + [resident(a.shape) for a in (gains, *wq, *ck, *cv, *wc)],
            out_specs=[wide] * 4 + [small, small, pl.BlockSpec((8, width), lambda i, s: (0, 0))],
            scratch_shapes=[pltpu.VMEM((4, 256, 256), FULL)] * 2,
        ),
        out_shape=[shape((rows, width), FULL)]
        + [shape((rows, width), ROUND)] * 3
        + [shape((4, 64, 256), FULL)] * 2
        + [shape((8, width), FULL)],
        compiler_params=params(56),
        cost_estimate=brief(),
        name="middle_back",
    )(place, ym, yr, x1, x2, d, cq, gains, *wq, *ck, *cv, *wc)


def first_back_kernel(place_ref, *refs):
    grads = refs[:6]
    own_ref, first_ref, second_ref, y_ref, total = refs[6:]
    depth = first_ref.shape[1]
    y = 0.0
    left = 0.0
    right = 0.0
    for c in range(3):
        y = y + nt(grads[c][...], own_ref[c])
        left = left + nt(grads[3 + c][...], first_ref[c])
        right = right + nt(grads[3 + c][...], second_ref[c])
    near = place_ref[1]
    total[...] = y
    total[:, pl.ds(pl.multiple_of(near * depth, 128), depth)] += left
    total[:, pl.ds(pl.multiple_of((1 - near) * depth, 128), depth)] += right
    y_ref[...] = total[...].astype(y_ref.dtype)


def first_back(place, grads, own, first, second, kind):
    span = grads[0].shape[0]
    rows = span // 2
    width = own.shape[1]
    block = 416
    steps = rows // block
    piece = pl.BlockSpec((block, 256), lambda i, s: (s[0] * steps + i, 0))
    return pl.pallas_call(
        first_back_kernel,
        grid_spec=pltpu.PrefetchScalarGridSpec(
            num_scalar_prefetch=1,
            grid=(steps,),
            in_specs=[piece] * 6 + [resident(a.shape) for a in (own, first, second)],
            out_specs=rows_of(block, width),
            scratch_shapes=[pltpu.VMEM((block, width), FULL)],
        ),
        out_shape=shape((rows, width), kind),
        compiler_params=params(40),
        cost_estimate=brief(),
        name="first_back",
    )(place, *grads, own, first, second)


def frames_back_kernel(place_ref, ym_ref, yr_ref, dx1_ref, frame_ref, gain_ref, out_ref, sums_ref):
    @pl.when(pl.program_id(0) == 0)
    def _():
        sums_ref[...] = jnp.zeros_like(sums_ref)

    y = ym_ref[...] + yr_ref[...].astype(FULL)
    scaled, inverse = norm_parts(frame_ref[...].astype(FULL))
    sums_ref[0:1, :] += jnp.sum(y * scaled, axis=0, keepdims=True)
    sums_ref[1:2, :] += jnp.sum(y, axis=0, keepdims=True)
    out_ref[...] = lower(dx1_ref[...] + norm_pull(y, scaled, inverse, gain_ref[0:1, :]))


def frames_back(place, ym, yr, dx1, frames, gains):
    rows, width = dx1.shape
    block = 208
    wide = rows_of(block, width)
    return pl.pallas_call(
        frames_back_kernel,
        grid_spec=pltpu.PrefetchScalarGridSpec(
            num_scalar_prefetch=1,
            grid=(rows // block,),
            in_specs=[wide] * 4 + [resident(gains.shape)],
            out_specs=[wide, pl.BlockSpec((8, width), lambda i, s: (0, 0))],
        ),
        out_shape=[shape((rows, width), ROUND), shape((8, width), FULL)],
        compiler_params=params(24),
        cost_estimate=brief(),
        name="frames_back",
    )(place, ym, yr, dx1, frames, gains)


def chip_local(
    frames, text_states, lengths, loss_mask, norm_gain, norm_bias, w_qkv, w_out, w_cross_q,
    w_cross_kv, w_cross_out, w_up, w_down, cotangent,
):
    at = lax.axis_index("narrow")
    core = at % 2
    side = at // 2
    column = lax.axis_index("wide") % 2
    layer = lax.axis_index("wide") // 2
    near = layer % 2
    place = jnp.stack([core, near]).astype(jnp.int32)
    away = jnp.stack([1 - core, near]).astype(jnp.int32)
    limit = lax.dynamic_slice(lengths, (side,), (1,))
    rows, width = frames.shape
    join = lax.optimization_barrier

    def over_core(v):
        return lax.ppermute(v, "narrow", CORE_PAIRS)

    def over_y(v):
        return lax.ppermute(v, "narrow", Y_PAIRS)

    def along_wide(v, pairs):
        return lax.ppermute(v, "wide", pairs)

    def half_of(v, which, axis=0):
        half = v.shape[axis] // 2
        return lax.dynamic_slice_in_dim(v, which * half, half, axis=axis)

    def ordered(first, second, which):
        return jnp.where(
            which == 0,
            jnp.concatenate([first, second], axis=0),
            jnp.concatenate([second, first], axis=0),
        )

    frames_other = over_core(frames)
    qkv_first = over_y(half_of(w_qkv, near, 1))
    dout = jnp.where(loss_mask[:, None] != 0, cotangent, jnp.zeros((), ROUND))
    inward = jnp.concatenate([w_cross_q, w_cross_kv.reshape(2 * width, 256)], axis=0)
    outward = jnp.concatenate([w_out, w_cross_out], axis=0)
    h1, q0, k0, v0 = first_project(place, frames, frames_other, norm_gain, norm_bias, w_qkv)

    q0, qkv_first, inward, outward, dout = join((q0, qkv_first, inward, outward, dout))
    qkv_second = along_wide(qkv_first, Z_NEAR)
    outward_first = over_y(half_of(outward, column))
    inward_first = over_y(half_of(inward, near))
    dout_other = over_core(dout)
    own_wo = over_core(outward)
    own_wq = over_core(w_cross_q)
    o0, lse0 = self_forward(limit, q0, k0, v0)

    o0, qkv_second, w_up, w_down = join((o0, qkv_second, w_up, w_down))
    q1, k1, v1 = project(place, h1, qkv_first, qkv_second)

    def away_rows(v):
        return half_of(v, 1 - core)

    o0_other = over_core(away_rows(o0))
    up_sent = half_of(w_up, near, 1)
    down_sent = half_of(w_down, near)
    q1, outward_first, inward_first, up_sent, down_sent, o0_other, own_wo, own_wq = join(
        (q1, outward_first, inward_first, up_sent, down_sent, o0_other, own_wo, own_wq)
    )
    outward_second = along_wide(outward_first, X_PAIRS)
    inward_second = along_wide(inward_first, Z_NEAR)
    up_first = over_y(up_sent)
    o1, lse1 = self_forward(limit, q1, k1, v1)
    o1_other = over_core(away_rows(o1))
    o1, outward_second, inward_second, down_sent, dout_other = join(
        (o1, outward_second, inward_second, down_sent, dout_other)
    )

    down_first = over_y(down_sent)
    outward_y = ordered(outward_first, outward_second, column)
    inward_y = ordered(inward_first, inward_second, near)
    out_y = outward_y[:256]
    cross_out_y = outward_y[256:]
    cross_q_y = inward_y[:width]
    cross_kv_y = inward_y[width:].reshape(2, width, 256)
    y_wo = over_core(outward_y)
    y_wq = over_core(cross_q_y)
    wo = (w_out, out_y, own_wo[:256], y_wo[:256])
    wc = (w_cross_out, cross_out_y, own_wo[256:], y_wo[256:])
    wq = (w_cross_q, cross_q_y, own_wq, y_wq)
    text = lax.dynamic_slice(text_states, (side, 0, 0), (1, *text_states.shape[1:]))[0]
    pair = jnp.stack(
        [jnp.stack([lower(nn(text, w[c])) for c in range(2)]) for w in (w_cross_kv, cross_kv_y)]
    )
    pair_other = over_core(pair)
    head_of = jnp.arange(256) // HEAD
    same = head_of[:, None] == head_of[None, :]

    def spread_heads(v):
        return jnp.where(same, jnp.tile(v, (1, 4, 1)), jnp.zeros((), ROUND))

    ck = (spread_heads(pair[:, 0]), spread_heads(pair_other[:, 0]))
    cv = (spread_heads(pair[:, 1]), spread_heads(pair_other[:, 1]))
    x1, x2, h2, cq, ca, h3 = middle_forward(
        place, frames, (o0, o1), (o0_other, o1_other), norm_gain, norm_bias, wo, wq, ck, cv, wc
    )
    h3, ca, h2, up_first, down_first = join((h3, ca, h2, up_first, down_first))

    h3_other = over_core(h3)
    up_second = along_wide(up_first, Z_NEAR)
    down_second = along_wide(down_first, Z_NEAR)
    g0, du0, out_m, y_m = feed(place, h3, dout, (w_up,), (w_down,), FULL, 0)
    g0, du0, out_o, y_o = feed(
        place, h3_other, dout_other, (w_up,), (w_down,), FULL, 1, shared=(g0, du0)
    )
    y_o, up_second, down_second, ca, h2 = join((y_o, up_second, down_second, ca, h2))

    ups = (up_first, up_second)
    downs = (down_first, down_second)
    g1, du1, out_o, y_o = feed(
        place, h3_other, dout_other, ups, downs, ROUND, 1, before=(out_o, y_o)
    )
    y_received = over_core(y_o)
    h2_other = over_core(h2)
    ca_other = over_core(ca[:, 512:])
    g1, du1, out_m, y_m = feed(
        place, h3, dout, ups, downs, FULL, 0, before=(out_m, y_m), shared=(g1, du1)
    )

    def plus(a, b):
        return lower(a.astype(FULL) + b.astype(FULL))

    across = (column, X_PAIRS)
    down_z = (near, Z_NEAR)

    class Sum:
        def __init__(self, partner, order=(across, down_z)):
            self.order = order
            self.fly = over_y(partner)

        def first(self, own):
            which, pairs = self.order[0]
            away_half = lower(half_of(own, 1 - which) + half_of(self.fly, 1 - which).astype(FULL))
            self.kept = half_of(own, which) + half_of(self.fly, which).astype(FULL)
            self.fly = along_wide(away_half, pairs)

        def second(self):
            which, pairs = self.order[1]
            total = self.kept + self.fly.astype(FULL)
            self.kept = half_of(total, which)
            self.fly = along_wide(lower(half_of(total, 1 - which)), pairs)

        def far(self):
            self.kept = plus(self.kept, self.fly)
            self.fly = along_wide(self.kept, Z_FAR)

        def back(self):
            self.kept = plus(self.kept, self.fly)
            self.fly = along_wide(self.kept, self.order[1][1])

        def along(self):
            self.kept = ordered(self.kept, self.fly, self.order[1][0])
            self.fly = along_wide(self.kept, self.order[0][1])

        def end(self):
            return ordered(self.kept, self.fly, self.order[0][0]).astype(FULL)

    def sync(in_flight, *values):
        done = join((*[each.fly for each in in_flight], *values))
        for each, fly in zip(in_flight, done):
            each.fly = fly
        return done[len(in_flight) :]

    class Row:
        def __init__(self, value, step):
            self.kept = value
            self.fly = step(value)

        def then(self, step):
            self.kept = self.kept + self.fly
            self.fly = step(self.kept)

    up1 = up_grad(h3, h3_other, du1, ROUND)
    up1, g1, du0, g0 = join((up1, g1, du0, g0))
    up = Sum(up1)
    down1a = down_grad(g1, dout, dout_other, ROUND, 0, 1)
    down1b = down_grad(g1, dout, dout_other, ROUND, 1, 1)
    y_received, down1a, down1b = join((y_received, down1a, down1b))
    dx1, dself, dcross, dcq, dck, dcv, sums = middle_back(
        place, y_m, y_received, x1, x2, dout, cq, norm_gain, wq, ck, cv, wc
    )
    du0, dself = join((du0, dself))
    up0 = up_grad(h3, h3_other, du0, FULL)
    dself_other = over_core(dself)
    dself, dself_other, dcross, dcq, down1a, down1b, up0, g0 = sync(
        [up], dself, dself_other, dcross, dcq, down1a, down1b, up0, g0
    )

    down_a = Sum(down1a)
    up_total = lax.psum(lower(up0 + up.fly.astype(FULL)), "wide")
    do0, do1 = pull(place, dself, dself_other, (w_out, out_y))
    dcross_other = over_core(dcross)
    dcq_other = over_core(dcq[:, 512:])
    d_pair = jnp.stack([dck, dcv], axis=1)
    d_pair_other = over_core(d_pair[2:])
    dq1, dk1, dv1 = self_back(limit, q1, k1, v1, o1, do1, lse1)
    dq1, dcross_other, dcq_other, d_pair_other, down1b = sync(
        [down_a], dq1, dcross_other, dcq_other, d_pair_other, down1b
    )

    down_b = Sum(down1b)
    d_pair = lower(d_pair[:2] + d_pair_other)
    qkv1 = qkv_grad(place, h1, (dq1, dk1, dv1), ROUND)
    down0 = down_grad(g0, dout, dout_other, FULL)
    cross = (h2, h2_other, dcq, dcq_other, text)
    outer = (dself, dself_other, ca, ca_other, dcross, dcross_other)
    into1 = cross_in_grad(1, *cross, d_pair[1], ROUND)
    outof1 = outputs_grad(place, 1, o1, *outer, ROUND)
    qkv1, into1, outof1, do0, down0 = sync([down_b], qkv1, into1, outof1, do0, down0)

    qkv = Sum(qkv1)
    dq0, dk0, dv0 = self_back(limit, q0, k0, v0, o0, do0, lse0)
    grads = (dq0, dk0, dv0, dq1, dk1, dv1)
    yo = first_back(away, grads, w_qkv, qkv_first, qkv_second, ROUND)
    dq0, yo, into1, outof1, d_pair = sync([qkv], dq0, yo, into1, outof1, d_pair)

    cross_in = Sum(into1)
    y_received = over_core(yo)
    qkv0 = qkv_grad(place, h1, (dq0, dk0, dv0), FULL)
    qkv.first(qkv0)
    grads = (dq0, dk0, dv0, dq1, dk1, dv1)
    ym = first_back(place, grads, w_qkv, qkv_first, qkv_second, FULL)
    into0 = cross_in_grad(0, *cross, d_pair[0], FULL)
    outof0 = outputs_grad(place, 0, o0, *outer, FULL)
    grad_frames, first_sums = frames_back(place, ym, y_received, dx1, frames, norm_gain)
    outof1, into0, outof0, grad_frames, x2, down0, up_total = sync(
        [cross_in, qkv], outof1, into0, outof0, grad_frames, x2, down0, up_total
    )

    outs = Sum(outof1)
    received = jnp.concatenate([down_a.fly, down_b.fly], axis=0)
    down_total = lax.psum(lower(down0 + received.astype(FULL)), "wide")
    cross_in.first(into0)
    qkv.second()
    norms = Row(sums + first_sums, over_core)
    text_part = 0.0
    for g, weights in ((0, w_cross_kv), (1, cross_kv_y)):
        for c in range(2):
            text_part = text_part + nt(d_pair[g, c], weights[c])
    texts = Row(text_part, over_core)
    out_rows = lower(x2 + out_m + over_core(out_o).astype(FULL))
    (out_rows,) = sync([outs, cross_in, qkv, norms, texts], out_rows)

    outs.first(outof0)
    cross_in.second()
    qkv.far()
    norms.then(over_y)
    text_grad = lower(texts.kept + texts.fly)
    text_away = over_y(text_grad)
    grad_up = up_total.astype(FULL)
    text_away, grad_up = sync([outs, cross_in, qkv, norms], text_away, grad_up)

    outs.second()
    cross_in.far()
    qkv.back()
    norms.then(lambda v: along_wide(v, X_PAIRS))
    grad_text = ordered(text_grad[None], text_away[None], side)
    (grad_text,) = sync([outs, cross_in, qkv, norms], grad_text)

    outs.far()
    cross_in.back()
    qkv.along()
    norms.then(lambda v: along_wide(v, Z_NEAR))
    sync([outs, cross_in, norms])

    outs.back()
    cross_in.along()
    norms.then(lambda v: along_wide(v, Z_FAR))
    sync([outs, qkv])

    outs.along()
    grad_qkv = qkv.end().reshape(3, width, 256)
    (grad_qkv,) = sync([cross_in, norms], grad_qkv)
    sums = norms.kept + norms.fly
    grad_cross_in = cross_in.end()
    grad_outs = outs.end()
    return (
        out_rows,
        grad_frames,
        grad_text,
        sums[0:6:2],
        sums[1:6:2],
        grad_qkv,
        grad_outs[:256],
        grad_cross_in[:width],
        grad_cross_in[width:].reshape(2, width, 256),
        grad_outs[256:],
        grad_up,
        down_total.astype(FULL),
    )


def solution(mesh):
    chips = dict(mesh.shape) == {"wide": 8, "narrow": 4}
    return jax.shard_map(
        chip_local if chips else general_local,
        mesh=mesh,
        in_specs=(
            P(("wide", "narrow"), None),
            P("wide", None, None),
            P("wide"),
            P(("wide", "narrow")),
            P(),
            P(),
            P(None, None, "narrow"),
            P("narrow", None),
            P(None, "narrow"),
            P(None, None, "narrow"),
            P("narrow", None),
            P(None, "narrow"),
            P("narrow", None),
            P(("wide", "narrow"), None),
        ),
        out_specs=(
            P(("wide", "narrow"), None),
            P(("wide", "narrow"), None),
            P("wide", None, None),
            P(),
            P(),
            P(None, None, "narrow"),
            P("narrow", None),
            P(None, "narrow"),
            P(None, None, "narrow"),
            P("narrow", None),
            P(None, "narrow"),
            P("narrow", None),
        ),
        check_vma=False,
    )
```

```python
import functools

import jax
import jax.numpy as jnp
from jax import lax
from jax.experimental import pallas as pl
from jax.experimental.pallas import tpu as pltpu
from jax.sharding import PartitionSpec as P

HEAD = 64


EPS = 1e-05
NEG = -1e30


def lower(values_in):
    return values_in.astype(jnp.bfloat16)


def product(left_side, right_side, transposed):
    if transposed:
        return lax.dot_general(
            left_side, right_side, (((1,), (1,)), ((), ())), preferred_element_type=jnp.float32
        )
    return jnp.dot(left_side, right_side, preferred_element_type=jnp.float32)


def outer_sum(left_side, right_side):
    return lax.dot_general(
        left_side, right_side, (((0,), (0,)), ((), ())), preferred_element_type=jnp.float32
    )


def normalize(values_in, gain_row, bias_row):
    row_mean = jnp.mean(values_in, axis=-1, keepdims=True)
    centered = values_in - row_mean
    inverse = lax.rsqrt(jnp.mean(centered * centered, axis=-1, keepdims=True) + EPS)
    scaled = centered * inverse
    return (scaled * gain_row + bias_row, scaled, inverse)


def normalize_back(upstream, scaled, inverse, gain_row):
    weighted = upstream * gain_row
    inner_mean = jnp.mean(weighted, axis=-1, keepdims=True)
    along_mean = jnp.mean(weighted * scaled, axis=-1, keepdims=True)
    grad_input = inverse * (weighted - inner_mean - scaled * along_mean)
    return (grad_input, jnp.sum(upstream * scaled, axis=0), jnp.sum(upstream, axis=0))


def gelu_parts(values_in):
    normal_cdf = 0.5 * (1.0 + jax.scipy.special.erf(values_in * 0.7071067811865476))
    normal_pdf = jnp.exp(-0.5 * values_in * values_in) * 0.3989422804014327
    return (values_in * normal_cdf, normal_cdf + values_in * normal_pdf)


def scores_of(query_part, key_part, valid):
    scores = jnp.einsum(
        "bhe,khe->hbk", query_part, key_part, preferred_element_type=jnp.float32
    ) * HEAD ** (-0.5)
    return jnp.where(valid, scores, NEG)


def attend(query_part, key_part, value_part, valid):
    scores = scores_of(query_part, key_part, valid)
    row_top = jnp.max(scores, axis=-1, keepdims=True)
    weights_exp = jnp.exp(scores - row_top)
    denominator = jnp.sum(weights_exp, axis=-1, keepdims=True)
    probability = weights_exp / denominator
    mixed = jnp.einsum(
        "hbk,khe->bhe", lower(probability), value_part, preferred_element_type=jnp.float32
    )
    return (lower(mixed), (row_top + jnp.log(denominator))[..., 0])


def attend_back(query_part, key_part, value_part, valid, summary, upstream):
    scores = scores_of(query_part, key_part, valid)
    probability = jnp.exp(scores - summary[..., None])
    pressure = jnp.einsum("bhe,khe->hbk", upstream, value_part, preferred_element_type=jnp.float32)
    grad_scores = lower(
        probability * (pressure - jnp.sum(probability * pressure, axis=-1, keepdims=True))
    )
    factor = HEAD ** (-0.5)
    grad_query = (
        jnp.einsum("hbk,khe->bhe", grad_scores, key_part, preferred_element_type=jnp.float32)
        * factor
    )
    grad_key = (
        jnp.einsum("hbk,bhe->khe", grad_scores, query_part, preferred_element_type=jnp.float32)
        * factor
    )
    grad_value = jnp.einsum(
        "hbk,bhe->khe", lower(probability), upstream, preferred_element_type=jnp.float32
    )
    return (grad_query, grad_key, grad_value)


def general_local(
    frames,
    text_states,
    lengths,
    loss_mask,
    norm_gain,
    norm_bias,
    w_qkv,
    w_out,
    w_cross_q,
    w_cross_kv,
    w_cross_out,
    w_up,
    w_down,
    cotangent,
):
    row_count = frames.shape[0]
    width = frames.shape[1]
    item_count = lengths.shape[0]
    span = row_count * lax.axis_size("narrow") // item_count
    half_span = span // 2
    inner_width = w_qkv.shape[2]
    head_count = inner_width // HEAD
    text_count = text_states.shape[1]
    full_rows = item_count * span
    places = jnp.arange(span, dtype=jnp.int32)

    def spread(shard_rows):
        return lax.all_gather(shard_rows, "narrow", axis=0, tiled=True)

    def collect(left_side, right_side, transposed):
        return lax.psum_scatter(
            product(
                lax.slice_in_dim(left_side, 0, lax.axis_size("narrow") * row_count, axis=0),
                right_side,
                transposed,
            ),
            "narrow",
            scatter_dimension=0,
            tiled=True,
        )

    def causal(block_index, item_limit):
        query_place = block_index * half_span + jnp.arange(half_span, dtype=jnp.int32)
        return (places[None, :] <= query_place[:, None]) & (places[None, :] < item_limit)

    frame_rows = frames.astype(jnp.float32)
    normed_one, scaled_one, inverse_one = normalize(frame_rows, norm_gain[0], norm_bias[0])
    first_input = spread(lower(normed_one))
    triple = lower(
        jnp.einsum("rd,cde->cre", first_input, w_qkv, preferred_element_type=jnp.float32)
    )
    triple = triple.reshape(3, item_count, span, head_count, HEAD)

    def self_item(packed):
        query_part, key_part, value_part, item_limit = packed
        mixed_list = []
        summary_list = []
        for block_index in range(2):
            mixed, summary = attend(
                query_part[block_index * half_span : (block_index + 1) * half_span],
                key_part,
                value_part,
                causal(block_index, item_limit),
            )
            mixed_list.append(mixed)
            summary_list.append(summary)
        return (jnp.concatenate(mixed_list, axis=0), jnp.stack(summary_list, axis=0))

    attended, self_summary = lax.map(self_item, (triple[0], triple[1], triple[2], lengths))
    attended_flat = attended.reshape(full_rows, inner_width)
    first_rows = frame_rows + collect(attended_flat, w_out, False)
    normed_two, scaled_two, inverse_two = normalize(first_rows, norm_gain[1], norm_bias[1])
    second_input = spread(lower(normed_two))
    cross_query = lower(product(second_input, w_cross_q, False)).reshape(
        item_count, span, head_count, HEAD
    )
    cross_pair = lower(
        jnp.einsum("ntd,cde->cnte", text_states, w_cross_kv, preferred_element_type=jnp.float32)
    )
    cross_pair = cross_pair.reshape(2, item_count, text_count, head_count, HEAD)

    def cross_item(packed):
        query_part, key_part, value_part = packed
        return attend(query_part, key_part, value_part, True)

    cross_mixed, cross_summary = lax.map(cross_item, (cross_query, cross_pair[0], cross_pair[1]))
    cross_flat = cross_mixed.reshape(full_rows, inner_width)
    second_rows = first_rows + collect(cross_flat, w_cross_out, False)
    normed_three, scaled_three, inverse_three = normalize(second_rows, norm_gain[2], norm_bias[2])
    upstream = cotangent.astype(jnp.float32) * loss_mask.astype(jnp.float32)[:, None]
    ffn_grad = lower(upstream)
    ffn_input = spread(lower(normed_three))
    hidden_pre = product(ffn_input, w_up, False)
    active, slope = gelu_parts(hidden_pre)
    active = lower(active)
    out_rows = second_rows + collect(active, w_down, False)
    ffn_full = spread(ffn_grad)
    grad_down = outer_sum(active, ffn_full)
    grad_hidden = lower(product(ffn_full, w_down, True) * slope)
    grad_up = outer_sum(ffn_input, grad_hidden)
    back_three = collect(grad_hidden, w_up, True)
    grad_up, grad_down = (grad_up, grad_down)
    grad_in_three, gain_three, bias_three = normalize_back(
        back_three, scaled_three, inverse_three, norm_gain[2]
    )
    grad_second = upstream + grad_in_three
    cross_full = spread(lower(grad_second))
    grad_cross_out = outer_sum(cross_flat, cross_full)
    cross_upstream = lower(product(cross_full, w_cross_out, True)).reshape(
        item_count, span, head_count, HEAD
    )

    def cross_back(packed):
        query_part, key_part, value_part, summary, upstream_item = packed
        return attend_back(query_part, key_part, value_part, True, summary, upstream_item)

    grad_cq, grad_ck, grad_cv = lax.map(
        cross_back, (cross_query, cross_pair[0], cross_pair[1], cross_summary, cross_upstream)
    )
    grad_cq = lower(grad_cq).reshape(full_rows, inner_width)
    grad_pair = lower(jnp.stack((grad_ck, grad_cv), axis=0)).reshape(
        2, item_count, text_count, inner_width
    )
    grad_cross_q = outer_sum(second_input, grad_cq)
    grad_cross_kv = jnp.einsum(
        "ntd,cnte->cde", text_states, grad_pair, preferred_element_type=jnp.float32
    )
    grad_cross_q, grad_cross_kv, grad_cross_out = (grad_cross_q, grad_cross_kv, grad_cross_out)
    text_partial = jnp.einsum(
        "cnte,cde->ntd", grad_pair, w_cross_kv, preferred_element_type=jnp.float32
    )
    grad_text = lower(lax.psum(text_partial, "narrow"))
    back_two = collect(grad_cq, w_cross_q, True)
    grad_in_two, gain_two, bias_two = normalize_back(
        back_two, scaled_two, inverse_two, norm_gain[1]
    )
    grad_first = grad_second + grad_in_two
    self_full = spread(lower(grad_first))
    grad_out = outer_sum(attended_flat, self_full)
    self_upstream = lower(product(self_full, w_out, True)).reshape(
        item_count, span, head_count, HEAD
    )

    def self_back(packed):
        query_part, key_part, value_part, item_limit, summary, upstream_item = packed
        query_list = []
        key_list = []
        value_list = []
        for block_index in range(2):
            lower_row = block_index * half_span
            grad_query, grad_key, grad_value = attend_back(
                query_part[lower_row : lower_row + half_span],
                key_part,
                value_part,
                causal(block_index, item_limit),
                summary[block_index],
                upstream_item[lower_row : lower_row + half_span],
            )
            query_list.append(grad_query)
            key_list.append(grad_key)
            value_list.append(grad_value)
        return (
            jnp.concatenate(query_list, axis=0),
            key_list[0] + key_list[1],
            value_list[0] + value_list[1],
        )

    grad_q, grad_k, grad_v = lax.map(
        self_back, (triple[0], triple[1], triple[2], lengths, self_summary, self_upstream)
    )
    grad_triple = lower(jnp.stack((grad_q, grad_k, grad_v), axis=0)).reshape(
        3, full_rows, inner_width
    )
    grad_qkv = jnp.einsum(
        "rd,cre->cde", first_input, grad_triple, preferred_element_type=jnp.float32
    )
    grad_qkv, grad_out = (grad_qkv, grad_out)
    merged = grad_triple.transpose(1, 0, 2).reshape(full_rows, 3 * inner_width)
    stacked_weights = w_qkv.transpose(0, 2, 1).reshape(3 * inner_width, width)
    back_one = collect(merged, stacked_weights, False)
    grad_in_one, gain_one, bias_one = normalize_back(
        back_one, scaled_one, inverse_one, norm_gain[0]
    )
    grad_frames = lower(grad_first + grad_in_one)
    gain_terms = jnp.stack((gain_one, gain_two, gain_three), axis=0)
    bias_terms = jnp.stack((bias_one, bias_two, bias_three), axis=0)
    grad_norm_gain, grad_norm_bias = lax.psum((gain_terms, bias_terms), ("wide", "narrow"))
    grad_qkv, grad_out, grad_cross_q, grad_cross_kv, grad_cross_out, grad_up, grad_down = lax.psum(
        (grad_qkv, grad_out, grad_cross_q, grad_cross_kv, grad_cross_out, grad_up, grad_down),
        "wide",
    )
    return (
        lower(out_rows),
        grad_frames,
        grad_text,
        grad_norm_gain,
        grad_norm_bias,
        grad_qkv,
        grad_out,
        grad_cross_q,
        grad_cross_kv,
        grad_cross_out,
        grad_up,
        grad_down,
    )


ROUND = jnp.bfloat16
FULL = jnp.float32
CORE_PAIRS = ((0, 1), (1, 0), (2, 3), (3, 2))
Y_PAIRS = ((0, 2), (2, 0), (1, 3), (3, 1))
X_PAIRS = tuple((i, i ^ 1) for i in range(8))
Z_INWARD = ((0, 2), (1, 3), (6, 4), (7, 5))
Z_MIDDLE = ((2, 4), (4, 2), (3, 5), (5, 3))
Z_OUTWARD = ((2, 0), (3, 1), (4, 6), (5, 7))
Z_NEAR = tuple((i, i ^ 2) for i in range(8))
Z_FAR = tuple((i, i ^ 4) for i in range(8))
MIB = 1 << 20


def nt(a, b):
    return lax.dot_general(a, b, (((1,), (1,)), ((), ())), preferred_element_type=FULL)


def nn(a, b):
    return lax.dot_general(a, b, (((1,), (0,)), ((), ())), preferred_element_type=FULL)


def tn(a, b):
    return lax.dot_general(a, b, (((0,), (0,)), ((), ())), preferred_element_type=FULL)


def shape(dims, kind):
    return jax.ShapeDtypeStruct(dims, kind)


def resident(dims):
    zeros = (0,) * len(dims)
    return pl.BlockSpec(dims, lambda i, s: zeros, pipeline_mode=pl.Buffered(1))


def rows_of(block, width):
    return pl.BlockSpec((block, width), lambda i, s: (i, 0))


def brief():
    return pl.CostEstimate(flops=1000, bytes_accessed=1000, transcendentals=0)


def params(mib):
    return pltpu.CompilerParams(vmem_limit_bytes=mib * MIB)


def norm_parts(v):
    centered = v - jnp.mean(v, axis=-1, keepdims=True)
    inverse = lax.rsqrt(jnp.mean(centered * centered, axis=-1, keepdims=True) + EPS)
    return centered * inverse, inverse


def norm_pull(y, scaled, inverse, gain_row):
    weighted = y * gain_row
    inner = jnp.mean(weighted, axis=-1, keepdims=True)
    along = jnp.mean(weighted * scaled, axis=-1, keepdims=True)
    return inverse * (weighted - inner - scaled * along)


def first_project_kernel(
    place_ref, mine_ref, other_ref, gain_ref, bias_ref, weight_ref, h_ref, *out_refs
):
    half = pl.program_id(0)

    def run(source):
        for start in range(0, source.shape[0], 208):
            part = slice(start, start + 208)
            scaled, _ = norm_parts(source[part, :].astype(FULL))
            h = lower(scaled * gain_ref[0:1, :] + bias_ref[0:1, :])
            h_ref[part, :] = h
            for c, out_ref in enumerate(out_refs):
                out_ref[part, :] = lower(nn(h, weight_ref[c]))

    @pl.when(half == 0)
    def _():
        run(mine_ref)

    @pl.when(half == 1)
    def _():
        run(other_ref)


def first_project(place, mine, other, gains, biases, weights):
    rows, depth = mine.shape
    count, _, wide = weights.shape
    out = pl.BlockSpec((rows, wide), lambda i, s: ((i + s[0]) % 2, 0))
    return pl.pallas_call(
        first_project_kernel,
        grid_spec=pltpu.PrefetchScalarGridSpec(
            num_scalar_prefetch=1,
            grid=(2,),
            in_specs=[resident(a.shape) for a in (mine, other, gains, biases, weights)],
            out_specs=[rows_of(rows, depth)] + [out] * count,
        ),
        out_shape=[shape((2 * rows, depth), ROUND)] + [shape((2 * rows, wide), ROUND)] * count,
        compiler_params=params(40),
        cost_estimate=brief(),
        name="first_project",
    )(place, mine, other, gains, biases, weights)


def project_kernel(place_ref, h_ref, first_ref, second_ref, *out_refs):
    depth = first_ref.shape[1]
    near = place_ref[1]
    left = h_ref[:, pl.ds(pl.multiple_of(near * depth, 128), depth)]
    right = h_ref[:, pl.ds(pl.multiple_of((1 - near) * depth, 128), depth)]
    for c, out_ref in enumerate(out_refs):
        out_ref[...] = lower(nn(left, first_ref[c]) + nn(right, second_ref[c]))


def project(place, h, first, second):
    rows, depth = h.shape[0] // 2, h.shape[1]
    count, _, wide = first.shape
    out = pl.BlockSpec((rows, wide), lambda i, s: ((i + s[0]) % 2, 0))
    return pl.pallas_call(
        project_kernel,
        grid_spec=pltpu.PrefetchScalarGridSpec(
            num_scalar_prefetch=1,
            grid=(2,),
            in_specs=[rows_of(rows, depth), resident(first.shape), resident(second.shape)],
            out_specs=[out] * count,
        ),
        out_shape=[shape((2 * rows, wide), ROUND)] * count,
        compiler_params=params(32),
        cost_estimate=brief(),
        name="project",
    )(place, h, first, second)


def pull_kernel(place_ref, mine_ref, other_ref, *refs):
    half = pl.program_id(0)
    count = len(refs) // 2

    def run(source):
        for weight_ref, out_ref in zip(refs[:count], refs[count:]):
            out_ref[...] = lower(nt(source[...], weight_ref[...]))

    @pl.when(half == 0)
    def _():
        run(mine_ref)

    @pl.when(half == 1)
    def _():
        run(other_ref)


def pull(place, mine, other, weights):
    rows = mine.shape[0]
    wide = weights[0].shape[0]
    out = pl.BlockSpec((rows, wide), lambda i, s: ((i + s[0]) % 2, 0))
    return pl.pallas_call(
        pull_kernel,
        grid_spec=pltpu.PrefetchScalarGridSpec(
            num_scalar_prefetch=1,
            grid=(2,),
            in_specs=[resident(a.shape) for a in (mine, other, *weights)],
            out_specs=[out] * len(weights),
        ),
        out_shape=[shape((2 * rows, wide), ROUND)] * len(weights),
        compiler_params=params(32),
        cost_estimate=brief(),
        name="pull",
    )(place, mine, other, *weights)


def blocks_of(span, block):
    return [(start, min(block, span - start)) for start in range(0, span, block)]


def self_forward_kernel(
    limit_ref, q_ref, k_ref, v_ref, o_ref, lse_ref, *, span, floor, block
):
    limit = limit_ref[0]
    lane = lax.broadcasted_iota(jnp.int32, (1, 128), 1)
    row = lax.broadcasted_iota(jnp.int32, (128, 1), 0)
    zero = jnp.zeros((), ROUND)
    value_turned = v_ref[...].T
    for start, size in blocks_of(span, block):
        end = start + size
        mixed_list = []
        for h in range(2):
            own_lanes = (lane < HEAD) if h == 0 else (lane >= HEAD)
            query = jnp.where(own_lanes, q_ref[start:end, :] * HEAD ** (-0.5), zero)
            parts = []
            for low in range(0, end, block):
                high = min(low + block, end)
                scores = nt(k_ref[low:high, :], query)
                if low == start:
                    key = lax.broadcasted_iota(jnp.int32, (size, size), 0)
                    valid = key <= lax.broadcasted_iota(jnp.int32, (size, size), 1)
                    if high > floor:
                        valid = valid & (key + low < limit)
                    scores = jnp.where(valid, scores, NEG)
                elif high > floor:
                    key = lax.broadcasted_iota(jnp.int32, (high - low, 1), 0)
                    scores = jnp.where(key + low < limit, scores, NEG)
                parts.append((low, high, scores))
            top = functools.reduce(
                jnp.maximum, [jnp.max(s, axis=0, keepdims=True) for _, _, s in parts]
            )
            total = 0.0
            mixed = 0.0
            for low, high, scores in parts:
                weights_exp = jnp.exp(scores - top)
                total = total + jnp.sum(weights_exp, axis=0, keepdims=True)
                mixed = mixed + nn(value_turned[:, low:high], lower(weights_exp))
            mixed_list.append(mixed / total)
            lse_ref[0, h : h + 1, start:end] = top + jnp.log(total)
        o_ref[start:end, :] = lower(jnp.where(row < HEAD, mixed_list[0], mixed_list[1]).T)


def self_forward(limit, q, k, v):
    span, wide = q.shape
    pairs = wide // 128
    floor = (span - span // 8 + 1) // 128 * 128
    pair = pl.BlockSpec((span, 128), lambda p, s: (0, p))
    return pl.pallas_call(
        functools.partial(self_forward_kernel, span=span, floor=floor, block=512),
        grid_spec=pltpu.PrefetchScalarGridSpec(
            num_scalar_prefetch=1,
            grid=(pairs,),
            in_specs=[pair] * 3,
            out_specs=[pair, pl.BlockSpec((1, 8, span), lambda p, s: (p, 0, 0))],
        ),
        out_shape=[shape((span, wide), ROUND), shape((pairs, 8, span), FULL)],
        compiler_params=params(56),
        cost_estimate=brief(),
        name="self_forward",
    )(limit, q, k, v)


def self_back_kernel(
    limit_ref, q_ref, k_ref, v_ref, o_ref, do_ref, lse_ref, dq_ref, dk_ref, dv_ref, dqt,
    *, span, floor, block
):
    limit = limit_ref[0]
    lane = lax.broadcasted_iota(jnp.int32, (1, 128), 1)
    row = lax.broadcasted_iota(jnp.int32, (128, 1), 0)
    zero = jnp.zeros((), ROUND)
    factor = HEAD ** (-0.5)
    product_rows = do_ref[...].astype(FULL) * o_ref[...].astype(FULL)
    high = lower(product_rows)
    rest = lower(product_rows - high.astype(FULL))
    pick = lower(
        jnp.concatenate(
            [
                jnp.where(lane < HEAD, 1.0, 0.0),
                jnp.where(lane >= HEAD, 1.0, 0.0),
                jnp.zeros((6, 128), FULL),
            ],
            axis=0,
        )
    )
    delta = nt(pick, high) + nt(pick, rest)
    for start, size in blocks_of(span, block):
        end = start + size
        key = k_ref[start:end, :]
        value = v_ref[start:end, :]
        key_turned = key.T
        dk = 0.0
        dv = 0.0
        dq_add = 0.0
        for h in range(2):
            own_lanes = (lane < HEAD) if h == 0 else (lane >= HEAD)
            own_rows = (row < HEAD) if h == 0 else (row >= HEAD)
            query = jnp.where(own_lanes, q_ref[start:, :] * factor, zero)
            pulled = jnp.where(own_lanes, do_ref[start:, :], zero)
            probability = jnp.exp(nt(key, query) - lse_ref[0, h : h + 1, start:])
            pressure = nt(value, pulled)
            below = lax.broadcasted_iota(jnp.int32, (size, size), 0)
            across = lax.broadcasted_iota(jnp.int32, (size, size), 1)
            corner = jnp.where(below <= across, probability[:, :size], 0.0)
            if end < span:
                probability = jnp.concatenate([corner, probability[:, size:]], axis=1)
            else:
                probability = corner
            if end > floor:
                place = lax.broadcasted_iota(jnp.int32, (size, 1), 0) + start
                probability = jnp.where(place < limit, probability, 0.0)
            grad_scores = lower(probability * (pressure - delta[h : h + 1, start:]))
            dv = dv + nn(lower(probability), pulled)
            dk = dk + nn(grad_scores, query)
            dq_add = dq_add + nn(jnp.where(own_rows, key_turned, zero), grad_scores)
        dk_ref[start:end, :] = lower(dk)
        dv_ref[start:end, :] = lower(dv)
        if start == 0:
            dqt[...] = dq_add
        else:
            dqt[:, start:] += dq_add
    dq_ref[...] = lower(dqt[...].T * factor)


def self_back(limit, q, k, v, o, do, lse):
    span, wide = q.shape
    pairs = wide // 128
    floor = (span - span // 8 + 1) // 128 * 128
    pair = pl.BlockSpec((span, 128), lambda p, s: (0, p))
    return pl.pallas_call(
        functools.partial(self_back_kernel, span=span, floor=floor, block=256),
        grid_spec=pltpu.PrefetchScalarGridSpec(
            num_scalar_prefetch=1,
            grid=(pairs,),
            in_specs=[pair] * 5 + [pl.BlockSpec((1, 8, span), lambda p, s: (p, 0, 0))],
            out_specs=[pair] * 3,
            scratch_shapes=[pltpu.VMEM((128, span), FULL)],
        ),
        out_shape=[shape((span, wide), ROUND)] * 3,
        compiler_params=params(48),
        cost_estimate=brief(),
        name="self_back",
    )(limit, q, k, v, o, do, lse)


def by_head(values_in, reduce, empty):
    lane = lax.broadcasted_iota(jnp.int32, (1, 128), 1)
    pieces = []
    for start in range(0, values_in.shape[1], 128):
        part = values_in[:, start : start + 128]
        first = reduce(jnp.where(lane < HEAD, part, empty), axis=1, keepdims=True)
        second = reduce(jnp.where(lane >= HEAD, part, empty), axis=1, keepdims=True)
        pieces.append(jnp.where(lane < HEAD, first, second))
    return jnp.concatenate(pieces, axis=1)


def cross_probability(query, keys):
    scores = nt(query * HEAD ** (-0.5), keys)
    weights_exp = jnp.exp(scores - by_head(scores, jnp.max, NEG))
    return weights_exp / by_head(weights_exp, jnp.sum, 0.0)


def middle_forward_kernel(
    place_ref, frame_ref, a0_ref, a1_ref, a2_ref, a3_ref, gain_ref, bias_ref, *refs
):
    mixed = (a0_ref, a1_ref, a2_ref, a3_ref)
    wo, wq, wc = refs[0:4], refs[4:8], refs[12:16]
    ck0_ref, ck1_ref, cv0_ref, cv1_ref = refs[8:12]
    x1_ref, x2_ref, h2_ref, cq_ref, ca_ref, h3_ref = refs[16:]
    x1 = frame_ref[...].astype(FULL)
    for g in range(4):
        x1 = x1 + nn(mixed[g][...], wo[g][...])
    x1_ref[...] = x1
    scaled, _ = norm_parts(x1)
    h2 = lower(scaled * gain_ref[1:2, :] + bias_ref[1:2, :])
    h2_ref[...] = h2
    for g in range(4):
        lanes = slice(g * 256, (g + 1) * 256)
        cq = lower(nn(h2, wq[g][...]))
        cq_ref[:, lanes] = cq
        probability = cross_probability(cq, (ck0_ref, ck1_ref)[g // 2][g % 2])
        ca_ref[:, lanes] = lower(nn(lower(probability), (cv0_ref, cv1_ref)[g // 2][g % 2]))
    crossed = 0.0
    for g in range(4):
        crossed = crossed + nn(ca_ref[:, g * 256 : (g + 1) * 256], wc[g][...])
    x2 = x1_ref[...] + crossed
    x2_ref[...] = x2
    scaled, _ = norm_parts(x2)
    h3_ref[...] = lower(scaled * gain_ref[2:3, :] + bias_ref[2:3, :])


def middle_forward(place, frames, attended, received, gains, biases, wo, wq, ck, cv, wc):
    rows, width = frames.shape
    block = 416
    steps = rows // block
    piece = pl.BlockSpec((block, 256), lambda i, s: (s[0] * steps + i, 0))
    wide = rows_of(block, width)
    return pl.pallas_call(
        middle_forward_kernel,
        grid_spec=pltpu.PrefetchScalarGridSpec(
            num_scalar_prefetch=1,
            grid=(steps,),
            in_specs=[wide, piece, piece, rows_of(block, 256), rows_of(block, 256)]
            + [resident(a.shape) for a in (gains, biases, *wo, *wq, *ck, *cv, *wc)],
            out_specs=[wide] * 6,
        ),
        out_shape=[shape((rows, width), FULL)] * 2 + [shape((rows, width), ROUND)] * 4,
        compiler_params=params(56),
        cost_estimate=brief(),
        name="middle_forward",
    )(place, frames, *attended, *received, gains, biases, *wo, *wq, *ck, *cv, *wc)


def feed_kernel(place_ref, h_ref, d_ref, *refs, parts, carried):
    ups, downs = refs[:parts], refs[parts : 2 * parts]
    before = refs[2 * parts : 2 * parts + carried]
    g_ref, du_ref, out_ref, y_ref = refs[-4:]
    h = h_ref[...]
    d = d_ref[...]
    out = 0.0
    y = 0.0
    for n, (up_ref, down_ref) in enumerate(zip(ups, downs)):
        size = down_ref.shape[0]
        if parts == 1:
            lanes = slice(0, size)
        else:
            near = place_ref[1]
            which = near if n == 0 else 1 - near
            lanes = pl.ds(pl.multiple_of(which * size, 128), size)
        u = nn(h, up_ref[...])
        active, slope = gelu_parts(u)
        g = lower(active)
        g_ref[:, lanes] = g
        du = lower(nt(d, down_ref[...]) * slope)
        du_ref[:, lanes] = du
        out = out + nn(g, down_ref[...])
        y = y + nt(du, up_ref[...])
    if carried:
        out = before[0][...] + out
        y = before[1][...] + y
    out_ref[...] = out.astype(out_ref.dtype)
    y_ref[...] = y.astype(y_ref.dtype)


def feed(place, h, d, ups, downs, kind, half, before=(), shared=()):
    rows, width = h.shape
    block = 416
    steps = rows // block
    hidden = sum(a.shape[0] for a in downs)
    wide = rows_of(block, width)
    kept = pl.BlockSpec((block, hidden), lambda i, s: (i + half * steps, 0))
    there = pl.BlockSpec(memory_space=pl.ANY)
    parts = len(ups)
    at = 3 + 2 * parts + len(before)
    return pl.pallas_call(
        functools.partial(feed_kernel, parts=parts, carried=len(before)),
        grid_spec=pltpu.PrefetchScalarGridSpec(
            num_scalar_prefetch=1,
            grid=(steps,),
            in_specs=[wide, wide]
            + [resident(a.shape) for a in (*ups, *downs)]
            + [wide] * len(before)
            + [there] * len(shared),
            out_specs=[kept, kept, wide, wide],
        ),
        out_shape=[shape((2 * rows, hidden), ROUND)] * 2 + [shape((rows, width), kind)] * 2,
        input_output_aliases={at: 0, at + 1: 1} if shared else {},
        compiler_params=params(58),
        cost_estimate=brief(),
        name="feed",
    )(place, h, d, *ups, *downs, *before, *shared)


def up_grad_kernel(mine_ref, other_ref, du_ref, out_ref):
    rows = mine_ref.shape[0]
    total = tn(mine_ref[...], du_ref[:rows, :]) + tn(other_ref[...], du_ref[rows:, :])
    out_ref[...] = total.astype(out_ref.dtype)


def up_grad(mine, other, du, kind):
    rows, width = mine.shape
    hidden = du.shape[1]
    tile = 512
    whole = pl.BlockSpec((rows, width), lambda i: (0, 0), pipeline_mode=pl.Buffered(1))
    return pl.pallas_call(
        up_grad_kernel,
        grid=(hidden // tile,),
        in_specs=[whole, whole, pl.BlockSpec((2 * rows, tile), lambda i: (0, i))],
        out_specs=pl.BlockSpec((width, tile), lambda i: (0, i)),
        out_shape=shape((width, hidden), kind),
        compiler_params=params(48),
        cost_estimate=brief(),
        name="up_grad",
    )(mine, other, du)


def down_grad_kernel(g_ref, mine_ref, other_ref, out_ref):
    rows = mine_ref.shape[0]
    total = tn(g_ref[:rows, :], mine_ref[...]) + tn(g_ref[rows:, :], other_ref[...])
    out_ref[...] = total.astype(out_ref.dtype)


def down_grad(g, mine, other, kind):
    rows, width = mine.shape
    hidden = g.shape[1]
    tile = 512
    whole = pl.BlockSpec((rows, width), lambda i: (0, 0), pipeline_mode=pl.Buffered(1))
    return pl.pallas_call(
        down_grad_kernel,
        grid=(hidden // tile,),
        in_specs=[pl.BlockSpec((2 * rows, tile), lambda i: (0, i)), whole, whole],
        out_specs=pl.BlockSpec((tile, width), lambda i: (i, 0)),
        out_shape=shape((hidden, width), kind),
        compiler_params=params(48),
        cost_estimate=brief(),
        name="down_grad",
    )(g, mine, other)


def qkv_grad_kernel(place_ref, h_ref, *refs):
    out_ref = refs[-1]
    rows, width = h_ref.shape[0] // 2, h_ref.shape[1]
    core = place_ref[0]
    total = [0.0] * 3
    for half in range(2):
        turned = h_ref[half * rows : (half + 1) * rows, :].T
        at = pl.multiple_of((core if half == 0 else 1 - core) * rows, 16)
        for c in range(3):
            total[c] = total[c] + nn(turned, refs[c][pl.ds(at, rows), :])
    for c in range(3):
        out_ref[c * width : (c + 1) * width, :] = total[c].astype(out_ref.dtype)


def qkv_grad(place, h, grads, kind):
    width = h.shape[1]
    wide = grads[0].shape[1]
    return pl.pallas_call(
        qkv_grad_kernel,
        grid_spec=pltpu.PrefetchScalarGridSpec(
            num_scalar_prefetch=1,
            grid=(1,),
            in_specs=[resident(a.shape) for a in (h, *grads)],
            out_specs=resident((3 * width, wide)),
        ),
        out_shape=shape((3 * width, wide), kind),
        compiler_params=params(48),
        cost_estimate=brief(),
        name="qkv_grad",
    )(place, h, *grads)


def cross_in_grad_kernel(mine_ref, other_ref, dm_ref, do_ref, text_ref, pair_ref, out_ref):
    width = mine_ref.shape[1]
    total = tn(mine_ref[...], dm_ref[...]) + tn(other_ref[...], do_ref[...])
    out_ref[:width, :] = total.astype(out_ref.dtype)
    turned = text_ref[...].T
    for c in range(2):
        part = nn(turned, pair_ref[c]).astype(out_ref.dtype)
        out_ref[(1 + c) * width : (2 + c) * width, :] = part


def cross_in_grad(group, mine, other, d_mine, d_other, text, pair, kind):
    rows, width = mine.shape
    lanes = pl.BlockSpec((rows, 256), lambda i: (0, group))

    def whole(a):
        zeros = (0,) * a.ndim
        return pl.BlockSpec(a.shape, lambda i: zeros)

    return pl.pallas_call(
        cross_in_grad_kernel,
        grid=(1,),
        in_specs=[whole(mine), whole(other), lanes, lanes, whole(text), whole(pair)],
        out_specs=pl.BlockSpec((3 * width, 256), lambda i: (0, 0)),
        out_shape=shape((3 * width, 256), kind),
        compiler_params=params(48),
        cost_estimate=brief(),
        name="cross_in_grad",
    )(mine, other, d_mine, d_other, text, pair)


def outputs_grad_kernel(
    place_ref, o_ref, sm_ref, so_ref, am_ref, ao_ref, cm_ref, co_ref, out_ref
):
    rows = sm_ref.shape[0]
    core = place_ref[0]
    mine = o_ref[pl.ds(pl.multiple_of(core * rows, 16), rows), :]
    other = o_ref[pl.ds(pl.multiple_of((1 - core) * rows, 16), rows), :]
    out_ref[:256, :] = (tn(mine, sm_ref[...]) + tn(other, so_ref[...])).astype(out_ref.dtype)
    total = tn(am_ref[...], cm_ref[...]) + tn(ao_ref[...], co_ref[...])
    out_ref[256:, :] = total.astype(out_ref.dtype)


def outputs_grad(place, group, o, dself, dself_other, ca, ca_other, dcross, dcross_other, kind):
    rows, width = dself.shape
    lanes = pl.BlockSpec((rows, 256), lambda i, s: (0, group))
    whole = resident((rows, width))
    return pl.pallas_call(
        outputs_grad_kernel,
        grid_spec=pltpu.PrefetchScalarGridSpec(
            num_scalar_prefetch=1,
            grid=(1,),
            in_specs=[resident(o.shape), whole, whole, lanes, lanes, whole, whole],
            out_specs=resident((512, width)),
        ),
        out_shape=shape((512, width), kind),
        compiler_params=params(48),
        cost_estimate=brief(),
        name="outputs_grad",
    )(place, o, dself, dself_other, ca, ca_other, dcross, dcross_other)


def middle_back_kernel(
    place_ref, ym_ref, yr_ref, x1_ref, x2_ref, d_ref, cq_ref, gain_ref, *refs
):
    wq, wc = refs[0:4], refs[8:12]
    ck0_ref, ck1_ref, cv0_ref, cv1_ref = refs[4:8]
    dx1_ref, dself_ref, dcross_ref, dcq_ref, dck_ref, dcv_ref, sums_ref = refs[12:19]
    dck_all, dcv_all = refs[19:]
    step = pl.program_id(0)

    @pl.when(step == 0)
    def _():
        dck_all[...] = jnp.zeros_like(dck_all)
        dcv_all[...] = jnp.zeros_like(dcv_all)
        sums_ref[...] = jnp.zeros_like(sums_ref)

    y3 = ym_ref[...] + yr_ref[...].astype(FULL)
    scaled, inverse = norm_parts(x2_ref[...])
    sums_ref[4:5, :] += jnp.sum(y3 * scaled, axis=0, keepdims=True)
    sums_ref[5:6, :] += jnp.sum(y3, axis=0, keepdims=True)
    dx2 = d_ref[...].astype(FULL) + norm_pull(y3, scaled, inverse, gain_ref[2:3, :])
    dx1_ref[...] = dx2
    dcross = lower(dx2)
    dcross_ref[...] = dcross
    y2 = 0.0
    for g in range(4):
        lanes = slice(g * 256, (g + 1) * 256)
        keys = (ck0_ref, ck1_ref)[g // 2][g % 2]
        values = (cv0_ref, cv1_ref)[g // 2][g % 2]
        dcatt = lower(nt(dcross, wc[g][...]))
        cq = cq_ref[:, lanes]
        probability = cross_probability(cq, keys)
        weighed = nt(dcatt, values)
        inner = by_head(probability * weighed, jnp.sum, 0.0)
        dcs = lower(probability * (weighed - inner))
        dcq = lower(nn(dcs, keys) * HEAD ** (-0.5))
        dcq_ref[:, lanes] = dcq
        dck_all[g] += tn(dcs, cq * HEAD ** (-0.5))
        dcv_all[g] += tn(lower(probability), dcatt)
        y2 = y2 + nt(dcq, wq[g][...])
    scaled, inverse = norm_parts(x1_ref[...])
    sums_ref[2:3, :] += jnp.sum(y2 * scaled, axis=0, keepdims=True)
    sums_ref[3:4, :] += jnp.sum(y2, axis=0, keepdims=True)
    dx1 = dx1_ref[...] + norm_pull(y2, scaled, inverse, gain_ref[1:2, :])
    dx1_ref[...] = dx1
    dself_ref[...] = lower(dx1)

    @pl.when(step == pl.num_programs(0) - 1)
    def _():
        for every, result in ((dck_all, dck_ref), (dcv_all, dcv_ref)):
            for g in range(4):
                total = 0.0
                for h in range(4):
                    lane = lax.broadcasted_iota(jnp.int32, (1, 256), 1) // HEAD
                    total = total + jnp.where(lane == h, every[g, h * 64 : (h + 1) * 64, :], 0.0)
                result[g] = total


def middle_back(place, ym, yr, x1, x2, d, cq, gains, wq, ck, cv, wc):
    rows, width = x1.shape
    block = 416
    wide = rows_of(block, width)
    small = pl.BlockSpec((4, 64, 256), lambda i, s: (0, 0, 0))
    return pl.pallas_call(
        middle_back_kernel,
        grid_spec=pltpu.PrefetchScalarGridSpec(
            num_scalar_prefetch=1,
            grid=(rows // block,),
            in_specs=[wide] * 6 + [resident(a.shape) for a in (gains, *wq, *ck, *cv, *wc)],
            out_specs=[wide] * 4 + [small, small, pl.BlockSpec((8, width), lambda i, s: (0, 0))],
            scratch_shapes=[pltpu.VMEM((4, 256, 256), FULL)] * 2,
        ),
        out_shape=[shape((rows, width), FULL)]
        + [shape((rows, width), ROUND)] * 3
        + [shape((4, 64, 256), FULL)] * 2
        + [shape((8, width), FULL)],
        compiler_params=params(56),
        cost_estimate=brief(),
        name="middle_back",
    )(place, ym, yr, x1, x2, d, cq, gains, *wq, *ck, *cv, *wc)


def first_back_kernel(place_ref, *refs):
    grads = refs[:6]
    own_ref, first_ref, second_ref, y_ref, total = refs[6:]
    depth = first_ref.shape[1]
    y = 0.0
    left = 0.0
    right = 0.0
    for c in range(3):
        y = y + nt(grads[c][...], own_ref[c])
        left = left + nt(grads[3 + c][...], first_ref[c])
        right = right + nt(grads[3 + c][...], second_ref[c])
    near = place_ref[1]
    total[...] = y
    total[:, pl.ds(pl.multiple_of(near * depth, 128), depth)] += left
    total[:, pl.ds(pl.multiple_of((1 - near) * depth, 128), depth)] += right
    y_ref[...] = total[...].astype(y_ref.dtype)


def first_back(place, grads, own, first, second, kind):
    span = grads[0].shape[0]
    rows = span // 2
    width = own.shape[1]
    block = 416
    steps = rows // block
    piece = pl.BlockSpec((block, 256), lambda i, s: (s[0] * steps + i, 0))
    return pl.pallas_call(
        first_back_kernel,
        grid_spec=pltpu.PrefetchScalarGridSpec(
            num_scalar_prefetch=1,
            grid=(steps,),
            in_specs=[piece] * 6 + [resident(a.shape) for a in (own, first, second)],
            out_specs=rows_of(block, width),
            scratch_shapes=[pltpu.VMEM((block, width), FULL)],
        ),
        out_shape=shape((rows, width), kind),
        compiler_params=params(40),
        cost_estimate=brief(),
        name="first_back",
    )(place, *grads, own, first, second)


def frames_back_kernel(place_ref, ym_ref, yr_ref, dx1_ref, frame_ref, gain_ref, out_ref, sums_ref):
    @pl.when(pl.program_id(0) == 0)
    def _():
        sums_ref[...] = jnp.zeros_like(sums_ref)

    y = ym_ref[...] + yr_ref[...].astype(FULL)
    scaled, inverse = norm_parts(frame_ref[...].astype(FULL))
    sums_ref[0:1, :] += jnp.sum(y * scaled, axis=0, keepdims=True)
    sums_ref[1:2, :] += jnp.sum(y, axis=0, keepdims=True)
    out_ref[...] = lower(dx1_ref[...] + norm_pull(y, scaled, inverse, gain_ref[0:1, :]))


def frames_back(place, ym, yr, dx1, frames, gains):
    rows, width = dx1.shape
    block = 208
    wide = rows_of(block, width)
    return pl.pallas_call(
        frames_back_kernel,
        grid_spec=pltpu.PrefetchScalarGridSpec(
            num_scalar_prefetch=1,
            grid=(rows // block,),
            in_specs=[wide] * 4 + [resident(gains.shape)],
            out_specs=[wide, pl.BlockSpec((8, width), lambda i, s: (0, 0))],
        ),
        out_shape=[shape((rows, width), ROUND), shape((8, width), FULL)],
        compiler_params=params(24),
        cost_estimate=brief(),
        name="frames_back",
    )(place, ym, yr, dx1, frames, gains)


def chip_local(
    frames, text_states, lengths, loss_mask, norm_gain, norm_bias, w_qkv, w_out, w_cross_q,
    w_cross_kv, w_cross_out, w_up, w_down, cotangent,
):
    at = lax.axis_index("narrow")
    core = at % 2
    side = at // 2
    column = lax.axis_index("wide") % 2
    layer = lax.axis_index("wide") // 2
    near = layer % 2
    place = jnp.stack([core, near]).astype(jnp.int32)
    away = jnp.stack([1 - core, near]).astype(jnp.int32)
    limit = lax.dynamic_slice(lengths, (side,), (1,))
    rows, width = frames.shape
    join = lax.optimization_barrier

    def over_core(v):
        return lax.ppermute(v, "narrow", CORE_PAIRS)

    def over_y(v):
        return lax.ppermute(v, "narrow", Y_PAIRS)

    def along_wide(v, pairs):
        return lax.ppermute(v, "wide", pairs)

    def half_of(v, which, axis=0):
        half = v.shape[axis] // 2
        return lax.dynamic_slice_in_dim(v, which * half, half, axis=axis)

    def ordered(first, second, which):
        return jnp.where(
            which == 0,
            jnp.concatenate([first, second], axis=0),
            jnp.concatenate([second, first], axis=0),
        )

    frames_other = over_core(frames)
    qkv_first = over_y(half_of(w_qkv, near, 1))
    dout = jnp.where(loss_mask[:, None] != 0, cotangent, jnp.zeros((), ROUND))
    inward = jnp.concatenate([w_cross_q, w_cross_kv.reshape(2 * width, 256)], axis=0)
    outward = jnp.concatenate([w_out, w_cross_out], axis=0)
    h1, q0, k0, v0 = first_project(place, frames, frames_other, norm_gain, norm_bias, w_qkv)

    q0, qkv_first, inward, outward, dout = join((q0, qkv_first, inward, outward, dout))
    qkv_second = along_wide(qkv_first, Z_NEAR)
    outward_first = over_y(half_of(outward, column))
    inward_first = over_y(half_of(inward, near))
    dout_other = over_core(dout)
    own_wo = over_core(outward)
    own_wq = over_core(w_cross_q)
    o0, lse0 = self_forward(limit, q0, k0, v0)

    o0, qkv_second, w_up, w_down = join((o0, qkv_second, w_up, w_down))
    q1, k1, v1 = project(place, h1, qkv_first, qkv_second)

    def away_rows(v):
        return half_of(v, 1 - core)

    o0_other = over_core(away_rows(o0))
    up_sent = half_of(w_up, near, 1)
    down_sent = half_of(w_down, near)
    q1, outward_first, inward_first, up_sent, down_sent, o0_other, own_wo, own_wq = join(
        (q1, outward_first, inward_first, up_sent, down_sent, o0_other, own_wo, own_wq)
    )
    outward_second = along_wide(outward_first, X_PAIRS)
    inward_second = along_wide(inward_first, Z_NEAR)
    up_first = over_y(up_sent)
    o1, lse1 = self_forward(limit, q1, k1, v1)
    o1_other = over_core(away_rows(o1))
    o1, outward_second, inward_second, down_sent, dout_other = join(
        (o1, outward_second, inward_second, down_sent, dout_other)
    )

    down_first = over_y(down_sent)
    outward_y = ordered(outward_first, outward_second, column)
    inward_y = ordered(inward_first, inward_second, near)
    out_y = outward_y[:256]
    cross_out_y = outward_y[256:]
    cross_q_y = inward_y[:width]
    cross_kv_y = inward_y[width:].reshape(2, width, 256)
    y_wo = over_core(outward_y)
    y_wq = over_core(cross_q_y)
    wo = (w_out, out_y, own_wo[:256], y_wo[:256])
    wc = (w_cross_out, cross_out_y, own_wo[256:], y_wo[256:])
    wq = (w_cross_q, cross_q_y, own_wq, y_wq)
    text = lax.dynamic_slice(text_states, (side, 0, 0), (1, *text_states.shape[1:]))[0]
    pair = jnp.stack(
        [jnp.stack([lower(nn(text, w[c])) for c in range(2)]) for w in (w_cross_kv, cross_kv_y)]
    )
    pair_other = over_core(pair)
    head_of = jnp.arange(256) // HEAD
    same = head_of[:, None] == head_of[None, :]

    def spread_heads(v):
        return jnp.where(same, jnp.tile(v, (1, 4, 1)), jnp.zeros((), ROUND))

    ck = (spread_heads(pair[:, 0]), spread_heads(pair_other[:, 0]))
    cv = (spread_heads(pair[:, 1]), spread_heads(pair_other[:, 1]))
    x1, x2, h2, cq, ca, h3 = middle_forward(
        place, frames, (o0, o1), (o0_other, o1_other), norm_gain, norm_bias, wo, wq, ck, cv, wc
    )
    h3, ca, h2, up_first, down_first = join((h3, ca, h2, up_first, down_first))

    h3_other = over_core(h3)
    up_second = along_wide(up_first, Z_NEAR)
    down_second = along_wide(down_first, Z_NEAR)
    g0, du0, out_m, y_m = feed(place, h3, dout, (w_up,), (w_down,), FULL, 0)
    g0, du0, out_o, y_o = feed(
        place, h3_other, dout_other, (w_up,), (w_down,), FULL, 1, shared=(g0, du0)
    )
    y_o, up_second, down_second, ca, h2 = join((y_o, up_second, down_second, ca, h2))

    ups = (up_first, up_second)
    downs = (down_first, down_second)
    g1, du1, out_o, y_o = feed(
        place, h3_other, dout_other, ups, downs, ROUND, 1, before=(out_o, y_o)
    )
    y_received = over_core(y_o)
    h2_other = over_core(h2)
    ca_other = over_core(ca[:, 512:])
    g1, du1, out_m, y_m = feed(
        place, h3, dout, ups, downs, FULL, 0, before=(out_m, y_m), shared=(g1, du1)
    )

    def plus(a, b):
        return lower(a.astype(FULL) + b.astype(FULL))

    across = (column, X_PAIRS)
    down_z = (near, Z_NEAR)
    store = {}
    last = []

    def order(*names):
        names = tuple(dict.fromkeys((*names, *last)))
        for name, value in zip(names, join(tuple(store[name] for name in names))):
            store[name] = value

    def get(*names):
        return tuple(store[name] for name in names)

    def step(results, make, *needs):
        order(*needs)
        made = make()
        made = made if isinstance(made, (tuple, list)) else (made,)
        store.update(zip(results, made))
        last[:] = results[:1]

    class Sum:
        def __init__(self, name, axes=(across, down_z)):
            self.fly, self.kept, self.axes = name + "_fly", name + "_kept", axes

        def over_y(self, partner):
            order(partner)
            store[self.fly] = over_y(store[partner])

        def first(self, own):
            which, pairs = self.axes[0]
            order(self.fly, own)
            mine, fly = get(own, self.fly)
            away_half = plus(half_of(mine, 1 - which), half_of(fly, 1 - which))
            store[self.kept] = half_of(mine, which).astype(FULL) + half_of(fly, which).astype(FULL)
            store[self.fly] = along_wide(away_half, pairs)
            last[:] = [self.kept]

        def second(self):
            which, pairs = self.axes[1]
            order(self.fly, self.kept)
            total = store[self.kept] + store[self.fly].astype(FULL)
            store[self.kept] = half_of(total, which)
            store[self.fly] = along_wide(lower(half_of(total, 1 - which)), pairs)
            last[:] = [self.kept]

        def add(self, pairs):
            order(self.fly, self.kept)
            store[self.kept] = plus(*get(self.kept, self.fly))
            store[self.fly] = along_wide(store[self.kept], pairs)
            last[:] = [self.kept]

        def far(self):
            self.add(Z_FAR)

        def back(self):
            self.add(self.axes[1][1])

        def along(self):
            order(self.fly, self.kept)
            store[self.kept] = ordered(*get(self.kept, self.fly), self.axes[1][0])
            store[self.fly] = along_wide(store[self.kept], self.axes[0][1])
            last[:] = [self.kept]

        def end(self, result):
            order(self.fly, self.kept)
            store[result] = ordered(*get(self.kept, self.fly), self.axes[0][0]).astype(FULL)
            last[:] = [result]

    class Row:
        def __init__(self, name, value, move):
            self.fly, self.kept = name + "_fly", name + "_kept"
            store[self.kept] = value
            store[self.fly] = move(value)

        def then(self, move):
            order(self.fly, self.kept)
            store[self.kept] = store[self.kept] + store[self.fly]
            store[self.fly] = move(store[self.kept])
            last[:] = [self.kept]

        def total(self):
            return store[self.kept] + store[self.fly]

    up, down, outs, cross_in = Sum("up"), Sum("down"), Sum("outs"), Sum("cross_in")
    qkv = Sum("qkv", (down_z, across))
    store.update(h3_other=h3_other, du1=du1, g1=g1, du0=du0, g0=g0, y_m=y_m, y_fly=y_received)
    store.update(o1=o1, o0=o0, x2=x2, h2_other=h2_other, ca_other=ca_other)

    step(["up1"], lambda: up_grad(h3, *get("h3_other", "du1"), ROUND), "du1", "du0")
    up.over_y("up1")
    step(["down1"], lambda: down_grad(store["g1"], dout, dout_other, ROUND), "g1")
    down.over_y("down1")
    step(
        ["dself", "dx1", "dcross", "dcq", "dck", "dcv", "sums"],
        lambda: (
            lambda r: (r[1], r[0], *r[2:])
        )(
            middle_back(
                place, *get("y_m", "y_fly"), x1, store["x2"], dout, cq, norm_gain, wq, ck, cv, wc
            )
        ),
        "y_fly",
        "y_m",
        "x2",
    )
    store["dself_other"] = over_core(store["dself"])
    step(["up0"], lambda: up_grad(h3, *get("h3_other", "du0"), ROUND), "du0")
    store["dcross_other"] = over_core(store["dcross"])
    store["dcq_other"] = over_core(store["dcq"][:, 512:])
    d_pair = jnp.stack(get("dck", "dcv"), axis=1)
    store["pair_kept"] = d_pair[:2]
    store["pair_fly"] = over_core(d_pair[2:])
    step(
        ["do1", "do0"],
        lambda: pull(place, *get("dself", "dself_other"), (out_y, w_out)),
        "dself",
        "dself_other",
    )
    step(
        ["dq1", "dk1", "dv1"],
        lambda: self_back(limit, q1, k1, v1, store["o1"], store["do1"], lse1),
        "do1",
    )
    up.first("up0")
    step(["down0"], lambda: down_grad(store["g0"], dout, dout_other, ROUND), "g0")
    step(["qkv1"], lambda: qkv_grad(place, h1, get("dq1", "dk1", "dv1"), ROUND), "dq1")
    qkv.over_y("qkv1")
    order("dcross_other", "dcq_other", "pair_fly", "pair_kept")
    store["pair"] = lower(store["pair_kept"] + store["pair_fly"])

    def into(g):
        return cross_in_grad(
            g, h2, *get("h2_other", "dcq", "dcq_other"), text, store["pair"][g], ROUND
        )

    def outof(g, o):
        return outputs_grad(
            place, g, o, *get("dself", "dself_other"), ca,
            *get("ca_other", "dcross", "dcross_other"), ROUND,
        )

    step(["into1"], lambda: into(1), "pair", "dcq_other", "h2_other")
    cross_in.over_y("into1")
    down.first("down0")
    up.second()
    step(["outs1"], lambda: outof(1, store["o1"]), "dcross_other", "ca_other")
    step(
        ["dq0", "dk0", "dv0"],
        lambda: self_back(limit, q0, k0, v0, store["o0"], store["do0"], lse0),
        "do0",
    )
    outs.over_y("outs1")
    up.far()
    down.second()
    six = ("dq0", "dk0", "dv0", "dq1", "dk1", "dv1")
    step(
        ["yo"],
        lambda: first_back(away, get(*six), w_qkv, qkv_first, qkv_second, ROUND),
        "dq0",
    )
    store["yo_fly"] = over_core(store["yo"])
    step(["qkv0"], lambda: qkv_grad(place, h1, get("dq0", "dk0", "dv0"), ROUND), "dq0")
    qkv.first("qkv0")
    step(["into0"], lambda: into(0), "dcq")
    cross_in.first("into0")
    down.far()
    up.back()
    step(["outs0"], lambda: outof(0, store["o0"]), "dcross")
    qkv.second()
    outs.first("outs0")
    cross_in.second()
    step(
        ["ym"],
        lambda: first_back(place, get(*six), w_qkv, qkv_first, qkv_second, FULL),
        "dq0",
    )
    down.back()
    qkv.far()
    up.along()
    outs.second()
    cross_in.far()
    down.along()
    step(
        ["grad_frames", "first_sums"],
        lambda: frames_back(place, *get("ym", "yo_fly", "dx1"), frames, norm_gain),
        "ym",
        "yo_fly",
    )
    norms = Row("norms", store["sums"] + store["first_sums"], over_core)
    qkv.back()
    outs.far()
    norms.then(over_y)
    up.end("grad_up")
    norms.then(lambda v: along_wide(v, X_PAIRS))
    cross_in.back()
    order("pair")
    text_part = 0.0
    for g, weights in ((0, w_cross_kv), (1, cross_kv_y)):
        for c in range(2):
            text_part = text_part + nt(store["pair"][g, c], weights[c])
    texts = Row("texts", text_part, over_core)
    norms.then(lambda v: along_wide(v, Z_NEAR))
    store["out_fly"] = over_core(out_o)
    outs.back()
    cross_in.along()
    norms.then(lambda v: along_wide(v, Z_FAR))
    order("texts_fly", "texts_kept")
    text_grad = lower(texts.total())
    text_away = over_y(text_grad)
    down.end("grad_down")
    order("out_fly", "x2")
    out_rows = lower(store["x2"] + out_m + store["out_fly"].astype(FULL))
    qkv.along()
    outs.along()
    grad_text = ordered(text_grad[None], text_away[None], side)
    cross_in.end("grad_in")
    sums = norms.total()
    qkv.end("grad_qkv")
    outs.end("grad_outs")
    grad_in, grad_outs = get("grad_in", "grad_outs")
    return (
        out_rows,
        store["grad_frames"],
        grad_text,
        sums[0:6:2],
        sums[1:6:2],
        store["grad_qkv"].reshape(3, width, 256),
        grad_outs[:256],
        grad_in[:width],
        grad_in[width:].reshape(2, width, 256),
        grad_outs[256:],
        store["grad_up"],
        store["grad_down"],
    )


def solution(mesh):
    chips = dict(mesh.shape) == {"wide": 8, "narrow": 4}
    return jax.shard_map(
        chip_local if chips else general_local,
        mesh=mesh,
        in_specs=(
            P(("wide", "narrow"), None),
            P("wide", None, None),
            P("wide"),
            P(("wide", "narrow")),
            P(),
            P(),
            P(None, None, "narrow"),
            P("narrow", None),
            P(None, "narrow"),
            P(None, None, "narrow"),
            P("narrow", None),
            P(None, "narrow"),
            P("narrow", None),
            P(("wide", "narrow"), None),
        ),
        out_specs=(
            P(("wide", "narrow"), None),
            P(("wide", "narrow"), None),
            P("wide", None, None),
            P(),
            P(),
            P(None, None, "narrow"),
            P("narrow", None),
            P(None, "narrow"),
            P(None, None, "narrow"),
            P("narrow", None),
            P(None, "narrow"),
            P("narrow", None),
        ),
        check_vma=False,
    )
```

```python
import functools

import jax
import jax.numpy as jnp
from jax import lax
from jax.experimental import pallas as pl
from jax.experimental.pallas import tpu as pltpu
from jax.sharding import PartitionSpec as P

HEAD = 64


EPS = 1e-05
NEG = -1e30


def lower(values_in):
    return values_in.astype(jnp.bfloat16)


def product(left_side, right_side, transposed):
    if transposed:
        return lax.dot_general(
            left_side, right_side, (((1,), (1,)), ((), ())), preferred_element_type=jnp.float32
        )
    return jnp.dot(left_side, right_side, preferred_element_type=jnp.float32)


def outer_sum(left_side, right_side):
    return lax.dot_general(
        left_side, right_side, (((0,), (0,)), ((), ())), preferred_element_type=jnp.float32
    )


def normalize(values_in, gain_row, bias_row):
    row_mean = jnp.mean(values_in, axis=-1, keepdims=True)
    centered = values_in - row_mean
    inverse = lax.rsqrt(jnp.mean(centered * centered, axis=-1, keepdims=True) + EPS)
    scaled = centered * inverse
    return (scaled * gain_row + bias_row, scaled, inverse)


def normalize_back(upstream, scaled, inverse, gain_row):
    weighted = upstream * gain_row
    inner_mean = jnp.mean(weighted, axis=-1, keepdims=True)
    along_mean = jnp.mean(weighted * scaled, axis=-1, keepdims=True)
    grad_input = inverse * (weighted - inner_mean - scaled * along_mean)
    return (grad_input, jnp.sum(upstream * scaled, axis=0), jnp.sum(upstream, axis=0))


def gelu_parts(values_in):
    normal_cdf = 0.5 * (1.0 + jax.scipy.special.erf(values_in * 0.7071067811865476))
    normal_pdf = jnp.exp(-0.5 * values_in * values_in) * 0.3989422804014327
    return (values_in * normal_cdf, normal_cdf + values_in * normal_pdf)


def scores_of(query_part, key_part, valid):
    scores = jnp.einsum(
        "bhe,khe->hbk", query_part, key_part, preferred_element_type=jnp.float32
    ) * HEAD ** (-0.5)
    return jnp.where(valid, scores, NEG)


def attend(query_part, key_part, value_part, valid):
    scores = scores_of(query_part, key_part, valid)
    row_top = jnp.max(scores, axis=-1, keepdims=True)
    weights_exp = jnp.exp(scores - row_top)
    denominator = jnp.sum(weights_exp, axis=-1, keepdims=True)
    probability = weights_exp / denominator
    mixed = jnp.einsum(
        "hbk,khe->bhe", lower(probability), value_part, preferred_element_type=jnp.float32
    )
    return (lower(mixed), (row_top + jnp.log(denominator))[..., 0])


def attend_back(query_part, key_part, value_part, valid, summary, upstream):
    scores = scores_of(query_part, key_part, valid)
    probability = jnp.exp(scores - summary[..., None])
    pressure = jnp.einsum("bhe,khe->hbk", upstream, value_part, preferred_element_type=jnp.float32)
    grad_scores = lower(
        probability * (pressure - jnp.sum(probability * pressure, axis=-1, keepdims=True))
    )
    factor = HEAD ** (-0.5)
    grad_query = (
        jnp.einsum("hbk,khe->bhe", grad_scores, key_part, preferred_element_type=jnp.float32)
        * factor
    )
    grad_key = (
        jnp.einsum("hbk,bhe->khe", grad_scores, query_part, preferred_element_type=jnp.float32)
        * factor
    )
    grad_value = jnp.einsum(
        "hbk,bhe->khe", lower(probability), upstream, preferred_element_type=jnp.float32
    )
    return (grad_query, grad_key, grad_value)


def general_local(
    frames,
    text_states,
    lengths,
    loss_mask,
    norm_gain,
    norm_bias,
    w_qkv,
    w_out,
    w_cross_q,
    w_cross_kv,
    w_cross_out,
    w_up,
    w_down,
    cotangent,
):
    row_count = frames.shape[0]
    width = frames.shape[1]
    item_count = lengths.shape[0]
    span = row_count * lax.axis_size("narrow") // item_count
    half_span = span // 2
    inner_width = w_qkv.shape[2]
    head_count = inner_width // HEAD
    text_count = text_states.shape[1]
    full_rows = item_count * span
    places = jnp.arange(span, dtype=jnp.int32)

    def spread(shard_rows):
        return lax.all_gather(shard_rows, "narrow", axis=0, tiled=True)

    def collect(left_side, right_side, transposed):
        return lax.psum_scatter(
            product(
                lax.slice_in_dim(left_side, 0, lax.axis_size("narrow") * row_count, axis=0),
                right_side,
                transposed,
            ),
            "narrow",
            scatter_dimension=0,
            tiled=True,
        )

    def causal(block_index, item_limit):
        query_place = block_index * half_span + jnp.arange(half_span, dtype=jnp.int32)
        return (places[None, :] <= query_place[:, None]) & (places[None, :] < item_limit)

    frame_rows = frames.astype(jnp.float32)
    normed_one, scaled_one, inverse_one = normalize(frame_rows, norm_gain[0], norm_bias[0])
    first_input = spread(lower(normed_one))
    triple = lower(
        jnp.einsum("rd,cde->cre", first_input, w_qkv, preferred_element_type=jnp.float32)
    )
    triple = triple.reshape(3, item_count, span, head_count, HEAD)

    def self_item(packed):
        query_part, key_part, value_part, item_limit = packed
        mixed_list = []
        summary_list = []
        for block_index in range(2):
            mixed, summary = attend(
                query_part[block_index * half_span : (block_index + 1) * half_span],
                key_part,
                value_part,
                causal(block_index, item_limit),
            )
            mixed_list.append(mixed)
            summary_list.append(summary)
        return (jnp.concatenate(mixed_list, axis=0), jnp.stack(summary_list, axis=0))

    attended, self_summary = lax.map(self_item, (triple[0], triple[1], triple[2], lengths))
    attended_flat = attended.reshape(full_rows, inner_width)
    first_rows = frame_rows + collect(attended_flat, w_out, False)
    normed_two, scaled_two, inverse_two = normalize(first_rows, norm_gain[1], norm_bias[1])
    second_input = spread(lower(normed_two))
    cross_query = lower(product(second_input, w_cross_q, False)).reshape(
        item_count, span, head_count, HEAD
    )
    cross_pair = lower(
        jnp.einsum("ntd,cde->cnte", text_states, w_cross_kv, preferred_element_type=jnp.float32)
    )
    cross_pair = cross_pair.reshape(2, item_count, text_count, head_count, HEAD)

    def cross_item(packed):
        query_part, key_part, value_part = packed
        return attend(query_part, key_part, value_part, True)

    cross_mixed, cross_summary = lax.map(cross_item, (cross_query, cross_pair[0], cross_pair[1]))
    cross_flat = cross_mixed.reshape(full_rows, inner_width)
    second_rows = first_rows + collect(cross_flat, w_cross_out, False)
    normed_three, scaled_three, inverse_three = normalize(second_rows, norm_gain[2], norm_bias[2])
    upstream = cotangent.astype(jnp.float32) * loss_mask.astype(jnp.float32)[:, None]
    ffn_grad = lower(upstream)
    ffn_input = spread(lower(normed_three))
    hidden_pre = product(ffn_input, w_up, False)
    active, slope = gelu_parts(hidden_pre)
    active = lower(active)
    out_rows = second_rows + collect(active, w_down, False)
    ffn_full = spread(ffn_grad)
    grad_down = outer_sum(active, ffn_full)
    grad_hidden = lower(product(ffn_full, w_down, True) * slope)
    grad_up = outer_sum(ffn_input, grad_hidden)
    back_three = collect(grad_hidden, w_up, True)
    grad_up, grad_down = (grad_up, grad_down)
    grad_in_three, gain_three, bias_three = normalize_back(
        back_three, scaled_three, inverse_three, norm_gain[2]
    )
    grad_second = upstream + grad_in_three
    cross_full = spread(lower(grad_second))
    grad_cross_out = outer_sum(cross_flat, cross_full)
    cross_upstream = lower(product(cross_full, w_cross_out, True)).reshape(
        item_count, span, head_count, HEAD
    )

    def cross_back(packed):
        query_part, key_part, value_part, summary, upstream_item = packed
        return attend_back(query_part, key_part, value_part, True, summary, upstream_item)

    grad_cq, grad_ck, grad_cv = lax.map(
        cross_back, (cross_query, cross_pair[0], cross_pair[1], cross_summary, cross_upstream)
    )
    grad_cq = lower(grad_cq).reshape(full_rows, inner_width)
    grad_pair = lower(jnp.stack((grad_ck, grad_cv), axis=0)).reshape(
        2, item_count, text_count, inner_width
    )
    grad_cross_q = outer_sum(second_input, grad_cq)
    grad_cross_kv = jnp.einsum(
        "ntd,cnte->cde", text_states, grad_pair, preferred_element_type=jnp.float32
    )
    grad_cross_q, grad_cross_kv, grad_cross_out = (grad_cross_q, grad_cross_kv, grad_cross_out)
    text_partial = jnp.einsum(
        "cnte,cde->ntd", grad_pair, w_cross_kv, preferred_element_type=jnp.float32
    )
    grad_text = lower(lax.psum(text_partial, "narrow"))
    back_two = collect(grad_cq, w_cross_q, True)
    grad_in_two, gain_two, bias_two = normalize_back(
        back_two, scaled_two, inverse_two, norm_gain[1]
    )
    grad_first = grad_second + grad_in_two
    self_full = spread(lower(grad_first))
    grad_out = outer_sum(attended_flat, self_full)
    self_upstream = lower(product(self_full, w_out, True)).reshape(
        item_count, span, head_count, HEAD
    )

    def self_back(packed):
        query_part, key_part, value_part, item_limit, summary, upstream_item = packed
        query_list = []
        key_list = []
        value_list = []
        for block_index in range(2):
            lower_row = block_index * half_span
            grad_query, grad_key, grad_value = attend_back(
                query_part[lower_row : lower_row + half_span],
                key_part,
                value_part,
                causal(block_index, item_limit),
                summary[block_index],
                upstream_item[lower_row : lower_row + half_span],
            )
            query_list.append(grad_query)
            key_list.append(grad_key)
            value_list.append(grad_value)
        return (
            jnp.concatenate(query_list, axis=0),
            key_list[0] + key_list[1],
            value_list[0] + value_list[1],
        )

    grad_q, grad_k, grad_v = lax.map(
        self_back, (triple[0], triple[1], triple[2], lengths, self_summary, self_upstream)
    )
    grad_triple = lower(jnp.stack((grad_q, grad_k, grad_v), axis=0)).reshape(
        3, full_rows, inner_width
    )
    grad_qkv = jnp.einsum(
        "rd,cre->cde", first_input, grad_triple, preferred_element_type=jnp.float32
    )
    grad_qkv, grad_out = (grad_qkv, grad_out)
    merged = grad_triple.transpose(1, 0, 2).reshape(full_rows, 3 * inner_width)
    stacked_weights = w_qkv.transpose(0, 2, 1).reshape(3 * inner_width, width)
    back_one = collect(merged, stacked_weights, False)
    grad_in_one, gain_one, bias_one = normalize_back(
        back_one, scaled_one, inverse_one, norm_gain[0]
    )
    grad_frames = lower(grad_first + grad_in_one)
    gain_terms = jnp.stack((gain_one, gain_two, gain_three), axis=0)
    bias_terms = jnp.stack((bias_one, bias_two, bias_three), axis=0)
    grad_norm_gain, grad_norm_bias = lax.psum((gain_terms, bias_terms), ("wide", "narrow"))
    grad_qkv, grad_out, grad_cross_q, grad_cross_kv, grad_cross_out, grad_up, grad_down = lax.psum(
        (grad_qkv, grad_out, grad_cross_q, grad_cross_kv, grad_cross_out, grad_up, grad_down),
        "wide",
    )
    return (
        lower(out_rows),
        grad_frames,
        grad_text,
        grad_norm_gain,
        grad_norm_bias,
        grad_qkv,
        grad_out,
        grad_cross_q,
        grad_cross_kv,
        grad_cross_out,
        grad_up,
        grad_down,
    )


ROUND = jnp.bfloat16
FULL = jnp.float32
CORE_PAIRS = ((0, 1), (1, 0), (2, 3), (3, 2))
Y_PAIRS = ((0, 2), (2, 0), (1, 3), (3, 1))
X_PAIRS = tuple((i, i ^ 1) for i in range(8))
Z_INWARD = ((0, 2), (1, 3), (6, 4), (7, 5))
Z_MIDDLE = ((2, 4), (4, 2), (3, 5), (5, 3))
Z_OUTWARD = ((2, 0), (3, 1), (4, 6), (5, 7))
Z_NEAR = tuple((i, i ^ 2) for i in range(8))
Z_FAR = tuple((i, i ^ 4) for i in range(8))
MIB = 1 << 20


def nt(a, b):
    return lax.dot_general(a, b, (((1,), (1,)), ((), ())), preferred_element_type=FULL)


def nn(a, b):
    return lax.dot_general(a, b, (((1,), (0,)), ((), ())), preferred_element_type=FULL)


def tn(a, b):
    return lax.dot_general(a, b, (((0,), (0,)), ((), ())), preferred_element_type=FULL)


def shape(dims, kind):
    return jax.ShapeDtypeStruct(dims, kind)


def resident(dims):
    zeros = (0,) * len(dims)
    return pl.BlockSpec(dims, lambda i, s: zeros, pipeline_mode=pl.Buffered(1))


def rows_of(block, width):
    return pl.BlockSpec((block, width), lambda i, s: (i, 0))


def brief():
    return pl.CostEstimate(flops=1000, bytes_accessed=1000, transcendentals=0)


def params(mib):
    return pltpu.CompilerParams(vmem_limit_bytes=mib * MIB)


def norm_parts(v):
    centered = v - jnp.mean(v, axis=-1, keepdims=True)
    inverse = lax.rsqrt(jnp.mean(centered * centered, axis=-1, keepdims=True) + EPS)
    return centered * inverse, inverse


def norm_pull(y, scaled, inverse, gain_row):
    weighted = y * gain_row
    inner = jnp.mean(weighted, axis=-1, keepdims=True)
    along = jnp.mean(weighted * scaled, axis=-1, keepdims=True)
    return inverse * (weighted - inner - scaled * along)


def first_project_kernel(
    place_ref, mine_ref, other_ref, gain_ref, bias_ref, weight_ref, h_ref, *out_refs
):
    half = pl.program_id(0)

    def run(source):
        for start in range(0, source.shape[0], 208):
            part = slice(start, start + 208)
            scaled, _ = norm_parts(source[part, :].astype(FULL))
            h = lower(scaled * gain_ref[0:1, :] + bias_ref[0:1, :])
            h_ref[part, :] = h
            for c, out_ref in enumerate(out_refs):
                out_ref[part, :] = lower(nn(h, weight_ref[c]))

    @pl.when(half == 0)
    def _():
        run(mine_ref)

    @pl.when(half == 1)
    def _():
        run(other_ref)


def first_project(place, mine, other, gains, biases, weights):
    rows, depth = mine.shape
    count, _, wide = weights.shape
    out = pl.BlockSpec((rows, wide), lambda i, s: ((i + s[0]) % 2, 0))
    return pl.pallas_call(
        first_project_kernel,
        grid_spec=pltpu.PrefetchScalarGridSpec(
            num_scalar_prefetch=1,
            grid=(2,),
            in_specs=[resident(a.shape) for a in (mine, other, gains, biases, weights)],
            out_specs=[rows_of(rows, depth)] + [out] * count,
        ),
        out_shape=[shape((2 * rows, depth), ROUND)] + [shape((2 * rows, wide), ROUND)] * count,
        compiler_params=params(40),
        cost_estimate=brief(),
        name="first_project",
    )(place, mine, other, gains, biases, weights)


def project_kernel(place_ref, h_ref, weight_ref, *out_refs):
    count = len(out_refs)
    wide = weight_ref.shape[2]
    weights = jnp.concatenate([weight_ref[c] for c in range(count)], axis=1)
    for start in range(0, h_ref.shape[0], 416):
        part = slice(start, start + 416)
        result = lower(nn(h_ref[part, :], weights))
        for c, out_ref in enumerate(out_refs):
            out_ref[part, :] = result[:, c * wide : (c + 1) * wide]


def project(place, h, weights):
    rows, depth = h.shape[0] // 2, h.shape[1]
    count, _, wide = weights.shape
    out = pl.BlockSpec((rows, wide), lambda i, s: ((i + s[0]) % 2, 0))
    return pl.pallas_call(
        project_kernel,
        grid_spec=pltpu.PrefetchScalarGridSpec(
            num_scalar_prefetch=1,
            grid=(2,),
            in_specs=[rows_of(rows, depth), resident(weights.shape)],
            out_specs=[out] * count,
        ),
        out_shape=[shape((2 * rows, wide), ROUND)] * count,
        compiler_params=params(40),
        cost_estimate=brief(),
        name="project",
    )(place, h, weights)


def pull_kernel(place_ref, mine_ref, other_ref, *refs):
    half = pl.program_id(0)
    count = len(refs) // 2

    def run(source):
        for weight_ref, out_ref in zip(refs[:count], refs[count:]):
            out_ref[...] = lower(nt(source[...], weight_ref[...]))

    @pl.when(half == 0)
    def _():
        run(mine_ref)

    @pl.when(half == 1)
    def _():
        run(other_ref)


def pull(place, mine, other, weights):
    rows = mine.shape[0]
    return pl.pallas_call(
        pull_kernel,
        grid_spec=pltpu.PrefetchScalarGridSpec(
            num_scalar_prefetch=1,
            grid=(2,),
            in_specs=[resident(a.shape) for a in (mine, other, *weights)],
            out_specs=[
                pl.BlockSpec((rows, a.shape[0]), lambda i, s: ((i + s[0]) % 2, 0)) for a in weights
            ],
        ),
        out_shape=[shape((2 * rows, a.shape[0]), ROUND) for a in weights],
        compiler_params=params(32),
        cost_estimate=brief(),
        name="pull",
    )(place, mine, other, *weights)


def blocks_of(span, block):
    return [(start, min(block, span - start)) for start in range(0, span, block)]


def self_forward_kernel(
    limit_ref, q_ref, k_ref, v_ref, o_ref, lse_ref, *, span, floor, block
):
    limit = limit_ref[0]
    lane = lax.broadcasted_iota(jnp.int32, (1, 128), 1)
    row = lax.broadcasted_iota(jnp.int32, (128, 1), 0)
    zero = jnp.zeros((), ROUND)
    value_turned = v_ref[...].T
    for start, size in blocks_of(span, block):
        end = start + size
        mixed_list = []
        for h in range(2):
            own_lanes = (lane < HEAD) if h == 0 else (lane >= HEAD)
            query = jnp.where(own_lanes, q_ref[start:end, :] * HEAD ** (-0.5), zero)
            parts = []
            for low in range(0, end, block):
                high = min(low + block, end)
                scores = nt(k_ref[low:high, :], query)
                if low == start:
                    key = lax.broadcasted_iota(jnp.int32, (size, size), 0)
                    valid = key <= lax.broadcasted_iota(jnp.int32, (size, size), 1)
                    if high > floor:
                        valid = valid & (key + low < limit)
                    scores = jnp.where(valid, scores, NEG)
                elif high > floor:
                    key = lax.broadcasted_iota(jnp.int32, (high - low, 1), 0)
                    scores = jnp.where(key + low < limit, scores, NEG)
                parts.append((low, high, scores))
            top = functools.reduce(
                jnp.maximum, [jnp.max(s, axis=0, keepdims=True) for _, _, s in parts]
            )
            total = 0.0
            mixed = 0.0
            for low, high, scores in parts:
                weights_exp = jnp.exp(scores - top)
                total = total + jnp.sum(weights_exp, axis=0, keepdims=True)
                mixed = mixed + nn(value_turned[:, low:high], lower(weights_exp))
            mixed_list.append(mixed / total)
            lse_ref[0, h : h + 1, start:end] = top + jnp.log(total)
        o_ref[start:end, :] = lower(jnp.where(row < HEAD, mixed_list[0], mixed_list[1]).T)


def self_forward(limit, q, k, v):
    span, wide = q.shape
    pairs = wide // 128
    floor = (span - span // 8 + 1) // 128 * 128
    pair = pl.BlockSpec((span, 128), lambda p, s: (0, p))
    return pl.pallas_call(
        functools.partial(self_forward_kernel, span=span, floor=floor, block=512),
        grid_spec=pltpu.PrefetchScalarGridSpec(
            num_scalar_prefetch=1,
            grid=(pairs,),
            in_specs=[pair] * 3,
            out_specs=[pair, pl.BlockSpec((1, 8, span), lambda p, s: (p, 0, 0))],
        ),
        out_shape=[shape((span, wide), ROUND), shape((pairs, 8, span), FULL)],
        compiler_params=params(56),
        cost_estimate=brief(),
        name="self_forward",
    )(limit, q, k, v)


def self_back_kernel(
    limit_ref, q_ref, k_ref, v_ref, o_ref, do_ref, lse_ref, dq_ref, dk_ref, dv_ref, dqt,
    *, span, floor, block
):
    limit = limit_ref[0]
    lane = lax.broadcasted_iota(jnp.int32, (1, 128), 1)
    row = lax.broadcasted_iota(jnp.int32, (128, 1), 0)
    zero = jnp.zeros((), ROUND)
    factor = HEAD ** (-0.5)
    product_rows = do_ref[...].astype(FULL) * o_ref[...].astype(FULL)
    high = lower(product_rows)
    rest = lower(product_rows - high.astype(FULL))
    pick = lower(
        jnp.concatenate(
            [
                jnp.where(lane < HEAD, 1.0, 0.0),
                jnp.where(lane >= HEAD, 1.0, 0.0),
                jnp.zeros((6, 128), FULL),
            ],
            axis=0,
        )
    )
    delta = nt(pick, high) + nt(pick, rest)
    for start, size in blocks_of(span, block):
        end = start + size
        key = k_ref[start:end, :]
        value = v_ref[start:end, :]
        key_turned = key.T
        dk = 0.0
        dv = 0.0
        dq_add = 0.0
        for h in range(2):
            own_lanes = (lane < HEAD) if h == 0 else (lane >= HEAD)
            own_rows = (row < HEAD) if h == 0 else (row >= HEAD)
            query = jnp.where(own_lanes, q_ref[start:, :] * factor, zero)
            pulled = jnp.where(own_lanes, do_ref[start:, :], zero)
            probability = jnp.exp(nt(key, query) - lse_ref[0, h : h + 1, start:])
            pressure = nt(value, pulled)
            below = lax.broadcasted_iota(jnp.int32, (size, size), 0)
            across = lax.broadcasted_iota(jnp.int32, (size, size), 1)
            corner = jnp.where(below <= across, probability[:, :size], 0.0)
            if end < span:
                probability = jnp.concatenate([corner, probability[:, size:]], axis=1)
            else:
                probability = corner
            if end > floor:
                place = lax.broadcasted_iota(jnp.int32, (size, 1), 0) + start
                probability = jnp.where(place < limit, probability, 0.0)
            grad_scores = lower(probability * (pressure - delta[h : h + 1, start:]))
            dv = dv + nn(lower(probability), pulled)
            dk = dk + nn(grad_scores, query)
            dq_add = dq_add + nn(jnp.where(own_rows, key_turned, zero), grad_scores)
        dk_ref[start:end, :] = lower(dk)
        dv_ref[start:end, :] = lower(dv)
        if start == 0:
            dqt[...] = dq_add
        else:
            dqt[:, start:] += dq_add
    dq_ref[...] = lower(dqt[...].T * factor)


def self_back(limit, q, k, v, o, do, lse):
    span, wide = q.shape
    pairs = wide // 128
    floor = (span - span // 8 + 1) // 128 * 128
    pair = pl.BlockSpec((span, 128), lambda p, s: (0, p))
    return pl.pallas_call(
        functools.partial(self_back_kernel, span=span, floor=floor, block=256),
        grid_spec=pltpu.PrefetchScalarGridSpec(
            num_scalar_prefetch=1,
            grid=(pairs,),
            in_specs=[pair] * 5 + [pl.BlockSpec((1, 8, span), lambda p, s: (p, 0, 0))],
            out_specs=[pair] * 3,
            scratch_shapes=[pltpu.VMEM((128, span), FULL)],
        ),
        out_shape=[shape((span, wide), ROUND)] * 3,
        compiler_params=params(48),
        cost_estimate=brief(),
        name="self_back",
    )(limit, q, k, v, o, do, lse)


def by_head(values_in, reduce, empty):
    lane = lax.broadcasted_iota(jnp.int32, (1, 128), 1)
    pieces = []
    for start in range(0, values_in.shape[1], 128):
        part = values_in[:, start : start + 128]
        first = reduce(jnp.where(lane < HEAD, part, empty), axis=1, keepdims=True)
        second = reduce(jnp.where(lane >= HEAD, part, empty), axis=1, keepdims=True)
        pieces.append(jnp.where(lane < HEAD, first, second))
    return jnp.concatenate(pieces, axis=1)


def cross_probability(query, keys):
    scores = nt(query * HEAD ** (-0.5), keys)
    weights_exp = jnp.exp(scores - by_head(scores, jnp.max, NEG))
    return weights_exp / by_head(weights_exp, jnp.sum, 0.0)


PIECES = ((0, 256), (256, 128), (384, 128), (512, 256), (768, 128), (896, 128))


def middle_forward_kernel(place_ref, frame_ref, *refs):
    mixed, wo, wq, wc = refs[0:6], refs[6:12], refs[12:18], refs[18:24]
    ck_ref, cv_ref, gain_ref, bias_ref = refs[24:28]
    x1_ref, x2_ref, h2_ref, cq_ref, ca_ref, h3_ref = refs[28:]
    x1 = frame_ref[...].astype(FULL)
    for o_ref, weight_ref in zip(mixed, wo):
        x1 = x1 + nn(o_ref[...], weight_ref[...])
    x1_ref[...] = x1
    scaled, _ = norm_parts(x1)
    h2 = lower(scaled * gain_ref[1:2, :] + bias_ref[1:2, :])
    h2_ref[...] = h2
    for (start, size), weight_ref in zip(PIECES, wq):
        cq_ref[:, start : start + size] = lower(nn(h2, weight_ref[...]))
    for g in range(4):
        lanes = slice(g * 256, (g + 1) * 256)
        probability = cross_probability(cq_ref[:, lanes], ck_ref[g])
        ca_ref[:, lanes] = lower(nn(lower(probability), cv_ref[g]))
    crossed = 0.0
    for (start, size), weight_ref in zip(PIECES, wc):
        crossed = crossed + nn(ca_ref[:, start : start + size], weight_ref[...])
    x2 = x1_ref[...] + crossed
    x2_ref[...] = x2
    scaled, _ = norm_parts(x2)
    h3_ref[...] = lower(scaled * gain_ref[2:3, :] + bias_ref[2:3, :])


def middle_forward(place, frames, attended, received, wo, wq, wc, ck, cv, gains, biases):
    rows, width = frames.shape
    block = 416
    steps = rows // block
    wide = rows_of(block, width)
    whole = (*wo, *wq, *wc, ck, cv, gains, biases)
    return pl.pallas_call(
        middle_forward_kernel,
        grid_spec=pltpu.PrefetchScalarGridSpec(
            num_scalar_prefetch=1,
            grid=(steps,),
            in_specs=[wide]
            + [
                pl.BlockSpec((block, a.shape[1]), lambda i, s: (s[0] * steps + i, 0))
                for a in attended
            ]
            + [rows_of(block, a.shape[1]) for a in received]
            + [resident(a.shape) for a in whole],
            out_specs=[wide] * 6,
        ),
        out_shape=[shape((rows, width), FULL)] * 2 + [shape((rows, width), ROUND)] * 4,
        compiler_params=params(56),
        cost_estimate=brief(),
        name="middle_forward",
    )(place, frames, *attended, *received, *whole)


def keys_kernel(text_ref, weight_ref, out_ref):
    for item in range(2):
        for c in range(2):
            out_ref[item, c] = lower(nn(text_ref[item], weight_ref[c]))


def keys_of(text_states, weights):
    items, states, _ = text_states.shape
    return pl.pallas_call(
        keys_kernel,
        out_shape=shape((items, 2, states, weights.shape[2]), ROUND),
        compiler_params=params(24),
        cost_estimate=brief(),
        name="keys_of",
    )(text_states, weights)


def feed_kernel(place_ref, h_ref, d_ref, *refs, parts, carried):
    ups, downs = refs[:parts], refs[parts : 2 * parts]
    before = refs[2 * parts : 2 * parts + carried]
    g_ref, du_ref, out_ref, y_ref = refs[-4:]
    h = h_ref[...]
    d = d_ref[...]
    out = 0.0
    y = 0.0
    for n, (up_ref, down_ref) in enumerate(zip(ups, downs)):
        size = down_ref.shape[0]
        if parts == 1:
            lanes = slice(0, size)
        else:
            column = place_ref[2]
            which = column if n == 0 else 1 - column
            lanes = pl.ds(pl.multiple_of(which * size, 128), size)
        u = nn(h, up_ref[...])
        active, slope = gelu_parts(u)
        g = lower(active)
        g_ref[:, lanes] = g
        du = lower(nt(d, down_ref[...]) * slope)
        du_ref[:, lanes] = du
        out = out + nn(g, down_ref[...])
        y = y + nt(du, up_ref[...])
    if carried:
        out = before[0][...] + out
        y = before[1][...] + y
    out_ref[...] = out.astype(out_ref.dtype)
    y_ref[...] = y.astype(y_ref.dtype)


def feed(place, h, d, ups, downs, kind, half, before=(), shared=()):
    rows, width = h.shape
    block = 416
    steps = rows // block
    hidden = sum(a.shape[0] for a in downs)
    wide = rows_of(block, width)
    kept = pl.BlockSpec((block, hidden), lambda i, s: (i + half * steps, 0))
    there = pl.BlockSpec(memory_space=pl.ANY)
    parts = len(ups)
    at = 3 + 2 * parts + len(before)
    return pl.pallas_call(
        functools.partial(feed_kernel, parts=parts, carried=len(before)),
        grid_spec=pltpu.PrefetchScalarGridSpec(
            num_scalar_prefetch=1,
            grid=(steps,),
            in_specs=[wide, wide]
            + [resident(a.shape) for a in (*ups, *downs)]
            + [wide] * len(before)
            + [there] * len(shared),
            out_specs=[kept, kept, wide, wide],
        ),
        out_shape=[shape((2 * rows, hidden), ROUND)] * 2 + [shape((rows, width), kind)] * 2,
        input_output_aliases={at: 0, at + 1: 1} if shared else {},
        compiler_params=params(58),
        cost_estimate=brief(),
        name="feed",
    )(place, h, d, *ups, *downs, *before, *shared)


def up_grad_kernel(mine_ref, other_ref, du_ref, out_ref):
    rows = mine_ref.shape[0]
    total = tn(mine_ref[...], du_ref[:rows, :]) + tn(other_ref[...], du_ref[rows:, :])
    out_ref[...] = total.astype(out_ref.dtype)


def up_grad(mine, other, du, kind):
    rows, width = mine.shape
    hidden = du.shape[1]
    tile = 512
    whole = pl.BlockSpec((rows, width), lambda i: (0, 0), pipeline_mode=pl.Buffered(1))
    return pl.pallas_call(
        up_grad_kernel,
        grid=(hidden // tile,),
        in_specs=[whole, whole, pl.BlockSpec((2 * rows, tile), lambda i: (0, i))],
        out_specs=pl.BlockSpec((width, tile), lambda i: (0, i)),
        out_shape=shape((width, hidden), kind),
        compiler_params=params(48),
        cost_estimate=brief(),
        name="up_grad",
    )(mine, other, du)


def down_grad_kernel(g_ref, mine_ref, other_ref, out_ref):
    rows = mine_ref.shape[0]
    total = tn(g_ref[:rows, :], mine_ref[...]) + tn(g_ref[rows:, :], other_ref[...])
    out_ref[...] = total.astype(out_ref.dtype)


def down_grad(g, mine, other, kind):
    rows, width = mine.shape
    hidden = g.shape[1]
    tile = 512
    whole = pl.BlockSpec((rows, width), lambda i: (0, 0), pipeline_mode=pl.Buffered(1))
    return pl.pallas_call(
        down_grad_kernel,
        grid=(hidden // tile,),
        in_specs=[pl.BlockSpec((2 * rows, tile), lambda i: (0, i)), whole, whole],
        out_specs=pl.BlockSpec((tile, width), lambda i: (i, 0)),
        out_shape=shape((hidden, width), kind),
        compiler_params=params(48),
        cost_estimate=brief(),
        name="down_grad",
    )(g, mine, other)


def qkv_grad_kernel(place_ref, h_ref, *refs):
    out_ref = refs[-1]
    rows, width = h_ref.shape[0] // 2, h_ref.shape[1]
    core, near = place_ref[0], place_ref[1]
    halves = (len(refs) - 1) // 3
    total = [0.0] * 3
    for half in range(2):
        turned = h_ref[half * rows : (half + 1) * rows, :].T
        at = pl.multiple_of((core if half == 0 else 1 - core) * rows, 16)
        for c in range(3):
            parts = [refs[3 * n + c][pl.ds(at, rows), :] for n in range(halves)]
            grads = parts[0] if halves == 1 else jnp.concatenate(parts, axis=1)
            total[c] = total[c] + nn(turned, grads)
    for c in range(3):
        part = slice(c * width, (c + 1) * width)
        value = total[c].astype(out_ref.dtype)
        if halves == 1:
            out_ref[part, :] = value
        else:
            out_ref[part, pl.ds(pl.multiple_of(near * 128, 128), 128)] = value[:, :128]
            out_ref[part, pl.ds(pl.multiple_of((1 - near) * 128, 128), 128)] = value[:, 128:]


def qkv_grad(place, h, grads, kind):
    width = h.shape[1]
    return pl.pallas_call(
        qkv_grad_kernel,
        grid_spec=pltpu.PrefetchScalarGridSpec(
            num_scalar_prefetch=1,
            grid=(1,),
            in_specs=[resident(a.shape) for a in (h, *grads)],
            out_specs=resident((3 * width, 256)),
        ),
        out_shape=shape((3 * width, 256), kind),
        compiler_params=params(48),
        cost_estimate=brief(),
        name="qkv_grad",
    )(place, h, *grads)


def query_grad_kernel(place_ref, mine_ref, other_ref, dm_ref, do_ref, out_ref, *, split):
    column = place_ref[2]
    total = tn(mine_ref[...], dm_ref[...]) + tn(other_ref[...], do_ref[...])
    value = total.astype(out_ref.dtype)
    if split:
        out_ref[:, pl.ds(pl.multiple_of(column * 128, 128), 128)] = value[:, :128]
        out_ref[:, pl.ds(pl.multiple_of((1 - column) * 128, 128), 128)] = value[:, 128:]
    else:
        out_ref[...] = value


def query_grad(place, group, mine, other, d_mine, d_other, kind):
    rows, width = mine.shape
    lanes = pl.BlockSpec((rows, 256), lambda i, s: (0, group))
    return pl.pallas_call(
        functools.partial(query_grad_kernel, split=group == 1),
        grid_spec=pltpu.PrefetchScalarGridSpec(
            num_scalar_prefetch=1,
            grid=(1,),
            in_specs=[resident(mine.shape), resident(other.shape), lanes, lanes],
            out_specs=resident((width, 256)),
        ),
        out_shape=shape((width, 256), kind),
        compiler_params=params(48),
        cost_estimate=brief(),
        name="query_grad",
    )(place, mine, other, d_mine, d_other)


def outputs_grad_kernel(place_ref, *refs, count):
    o_refs = refs[:count]
    sm_ref, so_ref, am_ref, ao_ref, cm_ref, co_ref, out_ref = refs[count:]
    rows = sm_ref.shape[0]
    core, near, column = place_ref[0], place_ref[1], place_ref[2]
    mine_at = pl.ds(pl.multiple_of(core * rows, 16), rows)
    other_at = pl.ds(pl.multiple_of((1 - core) * rows, 16), rows)
    for n, o_ref in enumerate(o_refs):
        total = tn(o_ref[mine_at, :], sm_ref[...]) + tn(o_ref[other_at, :], so_ref[...])
        if count == 1:
            at = slice(0, 256)
        else:
            at = pl.ds(pl.multiple_of((near if n == 0 else 1 - near) * 128, 128), 128)
        out_ref[at, :] = total.astype(out_ref.dtype)
    total = tn(am_ref[...], cm_ref[...]) + tn(ao_ref[...], co_ref[...])
    value = total.astype(out_ref.dtype)
    if count == 1:
        out_ref[256:, :] = value
    else:
        out_ref[pl.ds(pl.multiple_of(256 + column * 128, 128), 128), :] = value[:128, :]
        out_ref[pl.ds(pl.multiple_of(384 - column * 128, 128), 128), :] = value[128:, :]


def outputs_grad(place, group, o, dself, dself_other, ca, ca_other, dcross, dcross_other, kind):
    rows, width = dself.shape
    lanes = pl.BlockSpec((rows, 256), lambda i, s: (0, group))
    whole = resident((rows, width))
    return pl.pallas_call(
        functools.partial(outputs_grad_kernel, count=len(o)),
        grid_spec=pltpu.PrefetchScalarGridSpec(
            num_scalar_prefetch=1,
            grid=(1,),
            in_specs=[resident(a.shape) for a in o] + [whole, whole, lanes, lanes, whole, whole],
            out_specs=resident((512, width)),
        ),
        out_shape=shape((512, width), kind),
        compiler_params=params(48),
        cost_estimate=brief(),
        name="outputs_grad",
    )(place, *o, dself, dself_other, ca, ca_other, dcross, dcross_other)


def middle_back_kernel(place_ref, ym_ref, yr_ref, x1_ref, x2_ref, d_ref, cq_ref, *refs):
    wq, wc = refs[0:6], refs[6:12]
    ck_ref, cv_ref, gain_ref = refs[12:15]
    dx1_ref, dself_ref, dcross_ref, dcq_ref, dck_ref, dcv_ref, sums_ref = refs[15:22]
    dck_all, dcv_all = refs[22:]
    step = pl.program_id(0)

    @pl.when(step == 0)
    def _():
        dck_all[...] = jnp.zeros_like(dck_all)
        dcv_all[...] = jnp.zeros_like(dcv_all)
        sums_ref[...] = jnp.zeros_like(sums_ref)

    y3 = ym_ref[...] + yr_ref[...].astype(FULL)
    scaled, inverse = norm_parts(x2_ref[...])
    sums_ref[4:5, :] += jnp.sum(y3 * scaled, axis=0, keepdims=True)
    sums_ref[5:6, :] += jnp.sum(y3, axis=0, keepdims=True)
    dx2 = d_ref[...].astype(FULL) + norm_pull(y3, scaled, inverse, gain_ref[2:3, :])
    dx1_ref[...] = dx2
    dcross = lower(dx2)
    dcross_ref[...] = dcross
    pulled = [lower(nt(dcross, weight_ref[...])) for weight_ref in wc]
    for g in range(4):
        lanes = slice(g * 256, (g + 1) * 256)
        at = 3 * (g // 2)
        if g % 2 == 0:
            dcatt = pulled[at]
        else:
            dcatt = jnp.concatenate(pulled[at + 1 : at + 3], axis=1)
        keys = ck_ref[g]
        cq = cq_ref[:, lanes]
        probability = cross_probability(cq, keys)
        weighed = nt(dcatt, cv_ref[g])
        inner = by_head(probability * weighed, jnp.sum, 0.0)
        dcs = lower(probability * (weighed - inner))
        dcq_ref[:, lanes] = lower(nn(dcs, keys) * HEAD ** (-0.5))
        dck_all[g] += tn(dcs, cq * HEAD ** (-0.5))
        dcv_all[g] += tn(lower(probability), dcatt)
    y2 = 0.0
    for (start, size), weight_ref in zip(PIECES, wq):
        y2 = y2 + nt(dcq_ref[:, start : start + size], weight_ref[...])
    scaled, inverse = norm_parts(x1_ref[...])
    sums_ref[2:3, :] += jnp.sum(y2 * scaled, axis=0, keepdims=True)
    sums_ref[3:4, :] += jnp.sum(y2, axis=0, keepdims=True)
    dx1 = dx1_ref[...] + norm_pull(y2, scaled, inverse, gain_ref[1:2, :])
    dx1_ref[...] = dx1
    dself_ref[...] = lower(dx1)

    @pl.when(step == pl.num_programs(0) - 1)
    def _():
        for every, result in ((dck_all, dck_ref), (dcv_all, dcv_ref)):
            for g in range(4):
                total = 0.0
                for h in range(4):
                    lane = lax.broadcasted_iota(jnp.int32, (1, 256), 1) // HEAD
                    total = total + jnp.where(lane == h, every[g, h * 64 : (h + 1) * 64, :], 0.0)
                result[g] = total


def middle_back(place, ym, yr, x1, x2, d, cq, wq, wc, ck, cv, gains):
    rows, width = x1.shape
    block = 416
    wide = rows_of(block, width)
    small = pl.BlockSpec((4, 64, 256), lambda i, s: (0, 0, 0))
    whole = (*wq, *wc, ck, cv, gains)
    return pl.pallas_call(
        middle_back_kernel,
        grid_spec=pltpu.PrefetchScalarGridSpec(
            num_scalar_prefetch=1,
            grid=(rows // block,),
            in_specs=[wide] * 6 + [resident(a.shape) for a in whole],
            out_specs=[wide] * 4 + [small, small, pl.BlockSpec((8, width), lambda i, s: (0, 0))],
            scratch_shapes=[pltpu.VMEM((4, 256, 256), FULL)] * 2,
        ),
        out_shape=[shape((rows, width), FULL)]
        + [shape((rows, width), ROUND)] * 3
        + [shape((4, 64, 256), FULL)] * 2
        + [shape((8, width), FULL)],
        compiler_params=params(56),
        cost_estimate=brief(),
        name="middle_back",
    )(place, ym, yr, x1, x2, d, cq, *whole)


def first_back_kernel(place_ref, *refs):
    y_ref = refs[-1]
    y = 0.0
    for n in range(3):
        for c in range(3):
            y = y + nt(refs[3 * n + c][...], refs[9 + n][c])
    y_ref[...] = y.astype(y_ref.dtype)


def first_back(place, grads, weights, kind):
    span = grads[0].shape[0]
    rows = span // 2
    width = weights[0].shape[1]
    block = 416
    steps = rows // block
    return pl.pallas_call(
        first_back_kernel,
        grid_spec=pltpu.PrefetchScalarGridSpec(
            num_scalar_prefetch=1,
            grid=(steps,),
            in_specs=[
                pl.BlockSpec((block, a.shape[1]), lambda i, s: (s[0] * steps + i, 0))
                for a in grads
            ]
            + [resident(a.shape) for a in weights],
            out_specs=rows_of(block, width),
        ),
        out_shape=shape((rows, width), kind),
        compiler_params=params(40),
        cost_estimate=brief(),
        name="first_back",
    )(place, *grads, *weights)


def frames_back_kernel(place_ref, ym_ref, yr_ref, dx1_ref, frame_ref, gain_ref, out_ref, sums_ref):
    @pl.when(pl.program_id(0) == 0)
    def _():
        sums_ref[...] = jnp.zeros_like(sums_ref)

    y = ym_ref[...] + yr_ref[...].astype(FULL)
    scaled, inverse = norm_parts(frame_ref[...].astype(FULL))
    sums_ref[0:1, :] += jnp.sum(y * scaled, axis=0, keepdims=True)
    sums_ref[1:2, :] += jnp.sum(y, axis=0, keepdims=True)
    out_ref[...] = lower(dx1_ref[...] + norm_pull(y, scaled, inverse, gain_ref[0:1, :]))


def frames_back(place, ym, yr, dx1, frames, gains):
    rows, width = dx1.shape
    block = 208
    wide = rows_of(block, width)
    return pl.pallas_call(
        frames_back_kernel,
        grid_spec=pltpu.PrefetchScalarGridSpec(
            num_scalar_prefetch=1,
            grid=(rows // block,),
            in_specs=[wide] * 4 + [resident(gains.shape)],
            out_specs=[wide, pl.BlockSpec((8, width), lambda i, s: (0, 0))],
        ),
        out_shape=[shape((rows, width), ROUND), shape((8, width), FULL)],
        compiler_params=params(24),
        cost_estimate=brief(),
        name="frames_back",
    )(place, ym, yr, dx1, frames, gains)


def chip_local(
    frames, text_states, lengths, loss_mask, norm_gain, norm_bias, w_qkv, w_out, w_cross_q,
    w_cross_kv, w_cross_out, w_up, w_down, cotangent,
):
    at = lax.axis_index("narrow")
    core = at % 2
    side = at // 2
    column = lax.axis_index("wide") % 2
    layer = lax.axis_index("wide") // 2
    near = layer % 2
    place = jnp.stack([core, near, column]).astype(jnp.int32)
    away = jnp.stack([1 - core, near, column]).astype(jnp.int32)
    limit = lax.dynamic_slice(lengths, (side,), (1,))
    rows, width = frames.shape
    join = lax.optimization_barrier

    def over_core(v):
        return lax.ppermute(v, "narrow", CORE_PAIRS)

    def over_y(v):
        return lax.ppermute(v, "narrow", Y_PAIRS)

    def along_wide(v, pairs):
        return lax.ppermute(v, "wide", pairs)

    def half_of(v, which, axis=0):
        half = v.shape[axis] // 2
        return lax.dynamic_slice_in_dim(v, which * half, half, axis=axis)

    def ordered(first, second, which):
        return jnp.where(
            which == 0,
            jnp.concatenate([first, second], axis=0),
            jnp.concatenate([second, first], axis=0),
        )

    def over_z(v):
        return along_wide(v, Z_NEAR)

    def over_x(v):
        return along_wide(v, X_PAIRS)

    def away_rows(v):
        return half_of(v, 1 - core)

    def cross_order(v):
        return jnp.where(column == 0, v, jnp.concatenate([v[..., 128:], v[..., :128]], axis=-1))

    qkv_first = over_y(half_of(w_qkv, near, 2))
    frames_other = over_core(frames)
    h1, q0, k0, v0 = first_project(place, frames, frames_other, norm_gain, norm_bias, w_qkv)
    q0, qkv_first, w_out, w_cross_q, w_cross_out, cotangent = join(
        (q0, qkv_first, w_out, w_cross_q, w_cross_out, cotangent)
    )

    qkv_second = over_z(qkv_first)
    out_first = over_y(half_of(w_out, near))
    query_first = over_y(half_of(w_cross_q, column, 1))
    cross_out_first = over_y(half_of(w_cross_out, column))
    o0, lse0 = self_forward(limit, q0, k0, v0)
    qf, kf, vf = project(place, h1, qkv_first)
    out_other, query_other, cross_out_other = map(over_core, (w_out, w_cross_q, w_cross_out))
    qf, o0, out_first, query_first, cross_out_first, w_up, w_down, *core_got = join(
        (qf, o0, out_first, query_first, cross_out_first, w_up, w_down)
        + (out_other, query_other, cross_out_other)
    )

    out_other, query_other, cross_out_other = core_got
    out_second = over_z(out_first)
    query_second = over_x(query_first)
    cross_out_second = over_x(cross_out_first)
    up_first = over_y(half_of(w_up, column, 1))
    down_sent = half_of(w_down, column)
    o0_other = over_core(away_rows(o0))
    keys = keys_of(text_states, w_cross_kv)
    own_keys = lax.dynamic_index_in_dim(keys, side, keepdims=False)
    keys_y = over_y(lax.dynamic_index_in_dim(keys, 1 - side, keepdims=False))
    of, lse_f = self_forward(limit, qf, kf, vf)
    of, qkv_second, keys_y, o0_other = join((of, qkv_second, keys_y, o0_other))

    qs, ks, vs = project(place, h1, qkv_second)
    of_other = over_core(away_rows(of))
    pair = jnp.stack([own_keys, cross_order(keys_y)])
    pair_other = over_core(pair)
    o_s, lse_s = self_forward(limit, qs, ks, vs)
    o_s, out_second, query_second, cross_out_second, up_first, down_sent, pair_other, of_other = join(
        (o_s, out_second, query_second, cross_out_second, up_first, down_sent, pair_other, of_other)
    )

    down_first = over_y(down_sent)
    up_second = over_x(up_first)
    os_other = over_core(away_rows(o_s))
    dout = jnp.where(loss_mask[:, None] != 0, cotangent, jnp.zeros((), ROUND))

    def pieces(own, first, second, own_other):
        return (own, first, second, own_other, over_core(first), over_core(second))

    wo = pieces(w_out, out_first, out_second, out_other)
    wq = pieces(w_cross_q, query_first, query_second, query_other)
    wc = pieces(w_cross_out, cross_out_first, cross_out_second, cross_out_other)
    text = lax.dynamic_index_in_dim(text_states, side, keepdims=False)
    head_of = jnp.arange(256) // HEAD
    same = head_of[:, None] == head_of[None, :]

    def spread_heads(v):
        return jnp.where(same, jnp.tile(v, (1, 4, 1)), jnp.zeros((), ROUND))

    every = jnp.concatenate([pair, pair_other], axis=0)
    ck, cv = spread_heads(every[:, 0]), spread_heads(every[:, 1])
    x1, x2, h2, cq, ca, h3 = middle_forward(
        place, frames, (o0, of, o_s), (o0_other, of_other, os_other), wo, wq, wc, ck, cv,
        norm_gain, norm_bias,
    )
    h3, ca, h2, down_first, dout = join((h3, ca, h2, down_first, dout))

    h3_other = over_core(h3)
    dout_other = over_core(dout)
    down_second = over_x(down_first)
    g0, du0, out_m, y_m = feed(place, h3, dout, (w_up,), (w_down,), FULL, 0)
    g0, du0, out_o, y_o = feed(
        place, h3_other, dout_other, (w_up,), (w_down,), FULL, 1, shared=(g0, du0)
    )
    y_o, up_second, down_second, ca, h2 = join((y_o, up_second, down_second, ca, h2))

    ups = (up_first, up_second)
    downs = (down_first, down_second)
    g1, du1, out_o, y_o = feed(
        place, h3_other, dout_other, ups, downs, ROUND, 1, before=(out_o, y_o)
    )
    y_received = over_core(y_o)
    h2_other = over_core(h2)
    ca_other = over_core(ca[:, 512:])
    g1, du1, out_m, y_m = feed(
        place, h3, dout, ups, downs, FULL, 0, before=(out_m, y_m), shared=(g1, du1)
    )

    def plus(a, b):
        return lower(a.astype(FULL) + b.astype(FULL))

    across = (column, X_PAIRS)
    down_z = (near, Z_NEAR)
    store = {}
    last = []

    def order(*names):
        names = tuple(dict.fromkeys((*names, *last)))
        for name, value in zip(names, join(tuple(store[name] for name in names))):
            store[name] = value

    def get(*names):
        return tuple(store[name] for name in names)

    def step(results, make, *needs):
        order(*needs)
        made = make()
        made = made if isinstance(made, (tuple, list)) else (made,)
        store.update(zip(results, made))
        last[:] = results[:1]

    class Sum:
        def __init__(self, name, axes=(across, down_z)):
            self.fly, self.kept, self.axes = name + "_fly", name + "_kept", axes

        def over_y(self, partner):
            order(partner)
            store[self.fly] = over_y(store[partner])

        def first(self, own):
            which, pairs = self.axes[0]
            order(self.fly, own)
            mine, fly = get(own, self.fly)
            away_half = plus(half_of(mine, 1 - which), half_of(fly, 1 - which))
            store[self.kept] = half_of(mine, which).astype(FULL) + half_of(fly, which).astype(FULL)
            store[self.fly] = along_wide(away_half, pairs)
            last[:] = [self.kept]

        def first_alone(self, own):
            which, pairs = self.axes[0]
            store[self.kept] = half_of(store[own], which).astype(FULL)
            store[self.fly] = along_wide(half_of(store[own], 1 - which), pairs)
            last[:] = [self.kept]

        def second(self):
            which, pairs = self.axes[1]
            order(self.fly, self.kept)
            total = store[self.kept] + store[self.fly].astype(FULL)
            store[self.kept] = half_of(total, which)
            store[self.fly] = along_wide(lower(half_of(total, 1 - which)), pairs)
            last[:] = [self.kept]

        def add(self, pairs):
            order(self.fly, self.kept)
            store[self.kept] = plus(*get(self.kept, self.fly))
            store[self.fly] = along_wide(store[self.kept], pairs)
            last[:] = [self.kept]

        def far(self):
            self.add(Z_FAR)

        def back(self):
            self.add(self.axes[1][1])

        def along(self):
            order(self.fly, self.kept)
            store[self.kept] = ordered(*get(self.kept, self.fly), self.axes[1][0])
            store[self.fly] = along_wide(store[self.kept], self.axes[0][1])
            last[:] = [self.kept]

        def end(self, result):
            order(self.fly, self.kept)
            store[result] = ordered(*get(self.kept, self.fly), self.axes[0][0]).astype(FULL)
            last[:] = [result]

    class Row:
        def __init__(self, name, value, move):
            self.fly, self.kept = name + "_fly", name + "_kept"
            store[self.kept] = value
            store[self.fly] = move(value)

        def then(self, move):
            order(self.fly, self.kept)
            store[self.kept] = store[self.kept] + store[self.fly]
            store[self.fly] = move(store[self.kept])
            last[:] = [self.kept]

        def total(self):
            return store[self.kept] + store[self.fly]

    up, down, outs, cross_in = Sum("up"), Sum("down"), Sum("outs"), Sum("cross_in")
    qkv = Sum("qkv", (down_z, across))
    store.update(h3_other=h3_other, du1=du1, g1=g1, du0=du0, g0=g0, y_m=y_m, y_fly=y_received)
    store.update(of=of, o_s=o_s, o0=o0, x2=x2, h2_other=h2_other, ca_other=ca_other)

    def middle():
        dx1, *rest = middle_back(
            place, *get("y_m", "y_fly"), x1, store["x2"], dout, cq, wq, wc, ck, cv, norm_gain
        )
        return (rest[0], dx1, *rest[1:])

    step(["up1"], lambda: up_grad(h3, *get("h3_other", "du1"), ROUND), "du1", "du0")
    up.over_y("up1")
    step(["down1"], lambda: down_grad(store["g1"], dout, dout_other, ROUND), "g1")
    down.over_y("down1")
    step(["dself", "dx1", "dcross", "dcq", "dck", "dcv", "sums"], middle, "y_fly", "y_m", "x2")
    store["dself_other"] = over_core(store["dself"])
    step(["up0"], lambda: up_grad(h3, *get("h3_other", "du0"), ROUND), "du0")
    step(
        ["dof", "dos", "do0"],
        lambda: pull(place, *get("dself", "dself_other"), (out_first, out_second, w_out)),
        "dself",
        "dself_other",
        "dcross",
        "dcq",
    )
    store["dcross_other"] = over_core(store["dcross"])
    store["dcq_other"] = over_core(store["dcq"][:, 512:])
    d_pair = jnp.stack(get("dck", "dcv"), axis=1)
    store["pair_kept"] = d_pair[:2]
    store["pair_fly"] = over_core(d_pair[2:])
    step(
        ["dqf", "dkf", "dvf"],
        lambda: self_back(limit, qf, kf, vf, store["of"], store["dof"], lse_f),
        "dof",
    )
    order("dcross_other", "dcq_other", "pair_fly", "pair_kept")
    pair_sum = lower(store["pair_kept"] + store["pair_fly"])
    store["pair"] = pair_sum[0]
    store["pair_y"] = over_y(cross_order(pair_sum[1]))
    step(
        ["dqs", "dks", "dvs"],
        lambda: self_back(limit, qs, ks, vs, store["o_s"], store["dos"], lse_s),
        "dos",
    )
    up.first("up0")
    step(["down0"], lambda: down_grad(store["g0"], dout, dout_other, ROUND), "g0")
    yp = ("dqf", "dkf", "dvf", "dqs", "dks", "dvs")
    step(["qkv1"], lambda: qkv_grad(place, h1, get(*yp), ROUND), "dqs", "pair_y")
    qkv.over_y("qkv1")

    def query(g):
        return query_grad(place, g, h2, *get("h2_other", "dcq", "dcq_other"), ROUND)

    def outof(g, *o):
        return outputs_grad(
            place, g, get(*o), *get("dself", "dself_other"), ca,
            *get("ca_other", "dcross", "dcross_other"), ROUND,
        )

    step(["query1"], lambda: query(1), "dcq_other", "h2_other")
    store["query_fly"] = over_y(store["query1"])
    down.first("down0")
    up.second()
    step(["outs1"], lambda: outof(1, "of", "o_s"), "dcross_other", "ca_other")
    step(
        ["dq0", "dk0", "dv0"],
        lambda: self_back(limit, q0, k0, v0, store["o0"], store["do0"], lse0),
        "do0",
    )
    outs.over_y("outs1")
    up.far()
    down.second()
    nine = ("dq0", "dk0", "dv0", *yp)
    weights = (w_qkv, qkv_first, qkv_second)
    step(["yo"], lambda: first_back(away, get(*nine), weights, ROUND), "dq0")
    store["yo_fly"] = over_core(store["yo"])
    step(["qkv0"], lambda: qkv_grad(place, h1, get("dq0", "dk0", "dv0"), ROUND), "dq0")
    qkv.first("qkv0")
    up.back()
    step(["query0"], lambda: query(0), "dcq", "query_fly")
    other_text = lax.dynamic_index_in_dim(text_states, 1 - side, keepdims=False)
    texts = jnp.concatenate([text, other_text], axis=0)
    pairs = jnp.concatenate(get("pair", "pair_y"), axis=1)
    store["into0"] = jnp.concatenate(
        [
            lower(store["query0"].astype(FULL) + store["query_fly"].astype(FULL)),
            lower(tn(texts, pairs[0])),
            lower(tn(texts, pairs[1])),
        ],
        axis=0,
    )
    cross_in.first_alone("into0")
    down.far()
    step(["outs0"], lambda: outof(0, "o0"), "dcross")
    up.along()
    outs.first("outs0")
    qkv.second()
    step(["ym"], lambda: first_back(place, get(*nine), weights, FULL), "dq0")
    cross_in.second()
    qkv.far()
    outs.second()
    down.back()
    step(
        ["grad_frames", "first_sums"],
        lambda: frames_back(place, *get("ym", "yo_fly", "dx1"), frames, norm_gain),
        "ym",
        "yo_fly",
    )
    norms = Row("norms", store["sums"] + store["first_sums"], over_core)
    up.end("grad_up")
    cross_in.far()
    down.along()
    norms.then(over_y)
    qkv.back()
    outs.far()
    norms.then(over_x)
    cross_in.back()
    text_part = 0.0
    for c in range(2):
        text_part = text_part + nt(pairs[c], w_cross_kv[c])
    text_mine, text_theirs = text_part[:64], text_part[64:]
    text_rows = Row("texts", text_mine, lambda v: over_y(text_theirs))
    qkv.along()
    norms.then(over_z)
    store["out_fly"] = over_core(out_o)
    outs.back()
    text_rows.then(over_core)
    cross_in.along()
    norms.then(lambda v: along_wide(v, Z_FAR))
    down.end("grad_down")
    order("texts_fly", "texts_kept")
    text_grad = lower(text_rows.total())
    text_away = over_y(text_grad)
    outs.along()
    order("out_fly", "x2")
    out_rows = lower(store["x2"] + out_m + store["out_fly"].astype(FULL))
    qkv.end("grad_qkv")
    grad_text = ordered(text_grad[None], text_away[None], side)
    cross_in.end("grad_in")
    sums = norms.total()
    outs.end("grad_outs")
    grad_in, grad_outs = get("grad_in", "grad_outs")
    return (
        out_rows,
        store["grad_frames"],
        grad_text,
        sums[0:6:2],
        sums[1:6:2],
        store["grad_qkv"].reshape(3, width, 256),
        grad_outs[:256],
        grad_in[:width],
        grad_in[width:].reshape(2, width, 256),
        grad_outs[256:],
        store["grad_up"],
        store["grad_down"],
    )


def solution(mesh):
    chips = dict(mesh.shape) == {"wide": 8, "narrow": 4}
    return jax.shard_map(
        chip_local if chips else general_local,
        mesh=mesh,
        in_specs=(
            P(("wide", "narrow"), None),
            P("wide", None, None),
            P("wide"),
            P(("wide", "narrow")),
            P(),
            P(),
            P(None, None, "narrow"),
            P("narrow", None),
            P(None, "narrow"),
            P(None, None, "narrow"),
            P("narrow", None),
            P(None, "narrow"),
            P("narrow", None),
            P(("wide", "narrow"), None),
        ),
        out_specs=(
            P(("wide", "narrow"), None),
            P(("wide", "narrow"), None),
            P("wide", None, None),
            P(),
            P(),
            P(None, None, "narrow"),
            P("narrow", None),
            P(None, "narrow"),
            P(None, None, "narrow"),
            P("narrow", None),
            P(None, "narrow"),
            P("narrow", None),
        ),
        check_vma=False,
    )
```

```python
import functools

import jax
import jax.numpy as jnp
from jax import lax
from jax.experimental import pallas as pl
from jax.experimental.pallas import tpu as pltpu
from jax.sharding import PartitionSpec as P

HEAD = 64


EPS = 1e-05
NEG = -1e30


def lower(values_in):
    return values_in.astype(jnp.bfloat16)


def product(left_side, right_side, transposed):
    if transposed:
        return lax.dot_general(
            left_side, right_side, (((1,), (1,)), ((), ())), preferred_element_type=jnp.float32
        )
    return jnp.dot(left_side, right_side, preferred_element_type=jnp.float32)


def outer_sum(left_side, right_side):
    return lax.dot_general(
        left_side, right_side, (((0,), (0,)), ((), ())), preferred_element_type=jnp.float32
    )


def normalize(values_in, gain_row, bias_row):
    row_mean = jnp.mean(values_in, axis=-1, keepdims=True)
    centered = values_in - row_mean
    inverse = lax.rsqrt(jnp.mean(centered * centered, axis=-1, keepdims=True) + EPS)
    scaled = centered * inverse
    return (scaled * gain_row + bias_row, scaled, inverse)


def normalize_back(upstream, scaled, inverse, gain_row):
    weighted = upstream * gain_row
    inner_mean = jnp.mean(weighted, axis=-1, keepdims=True)
    along_mean = jnp.mean(weighted * scaled, axis=-1, keepdims=True)
    grad_input = inverse * (weighted - inner_mean - scaled * along_mean)
    return (grad_input, jnp.sum(upstream * scaled, axis=0), jnp.sum(upstream, axis=0))


def gelu_parts(values_in):
    normal_cdf = 0.5 * (1.0 + jax.scipy.special.erf(values_in * 0.7071067811865476))
    normal_pdf = jnp.exp(-0.5 * values_in * values_in) * 0.3989422804014327
    return (values_in * normal_cdf, normal_cdf + values_in * normal_pdf)


def scores_of(query_part, key_part, valid):
    scores = jnp.einsum(
        "bhe,khe->hbk", query_part, key_part, preferred_element_type=jnp.float32
    ) * HEAD ** (-0.5)
    return jnp.where(valid, scores, NEG)


def attend(query_part, key_part, value_part, valid):
    scores = scores_of(query_part, key_part, valid)
    row_top = jnp.max(scores, axis=-1, keepdims=True)
    weights_exp = jnp.exp(scores - row_top)
    denominator = jnp.sum(weights_exp, axis=-1, keepdims=True)
    probability = weights_exp / denominator
    mixed = jnp.einsum(
        "hbk,khe->bhe", lower(probability), value_part, preferred_element_type=jnp.float32
    )
    return (lower(mixed), (row_top + jnp.log(denominator))[..., 0])


def attend_back(query_part, key_part, value_part, valid, summary, upstream):
    scores = scores_of(query_part, key_part, valid)
    probability = jnp.exp(scores - summary[..., None])
    pressure = jnp.einsum("bhe,khe->hbk", upstream, value_part, preferred_element_type=jnp.float32)
    grad_scores = lower(
        probability * (pressure - jnp.sum(probability * pressure, axis=-1, keepdims=True))
    )
    factor = HEAD ** (-0.5)
    grad_query = (
        jnp.einsum("hbk,khe->bhe", grad_scores, key_part, preferred_element_type=jnp.float32)
        * factor
    )
    grad_key = (
        jnp.einsum("hbk,bhe->khe", grad_scores, query_part, preferred_element_type=jnp.float32)
        * factor
    )
    grad_value = jnp.einsum(
        "hbk,bhe->khe", lower(probability), upstream, preferred_element_type=jnp.float32
    )
    return (grad_query, grad_key, grad_value)


def general_local(
    frames,
    text_states,
    lengths,
    loss_mask,
    norm_gain,
    norm_bias,
    w_qkv,
    w_out,
    w_cross_q,
    w_cross_kv,
    w_cross_out,
    w_up,
    w_down,
    cotangent,
):
    row_count = frames.shape[0]
    width = frames.shape[1]
    item_count = lengths.shape[0]
    span = row_count * lax.axis_size("narrow") // item_count
    half_span = span // 2
    inner_width = w_qkv.shape[2]
    head_count = inner_width // HEAD
    text_count = text_states.shape[1]
    full_rows = item_count * span
    places = jnp.arange(span, dtype=jnp.int32)

    def spread(shard_rows):
        return lax.all_gather(shard_rows, "narrow", axis=0, tiled=True)

    def collect(left_side, right_side, transposed):
        return lax.psum_scatter(
            product(
                lax.slice_in_dim(left_side, 0, lax.axis_size("narrow") * row_count, axis=0),
                right_side,
                transposed,
            ),
            "narrow",
            scatter_dimension=0,
            tiled=True,
        )

    def causal(block_index, item_limit):
        query_place = block_index * half_span + jnp.arange(half_span, dtype=jnp.int32)
        return (places[None, :] <= query_place[:, None]) & (places[None, :] < item_limit)

    frame_rows = frames.astype(jnp.float32)
    normed_one, scaled_one, inverse_one = normalize(frame_rows, norm_gain[0], norm_bias[0])
    first_input = spread(lower(normed_one))
    triple = lower(
        jnp.einsum("rd,cde->cre", first_input, w_qkv, preferred_element_type=jnp.float32)
    )
    triple = triple.reshape(3, item_count, span, head_count, HEAD)

    def self_item(packed):
        query_part, key_part, value_part, item_limit = packed
        mixed_list = []
        summary_list = []
        for block_index in range(2):
            mixed, summary = attend(
                query_part[block_index * half_span : (block_index + 1) * half_span],
                key_part,
                value_part,
                causal(block_index, item_limit),
            )
            mixed_list.append(mixed)
            summary_list.append(summary)
        return (jnp.concatenate(mixed_list, axis=0), jnp.stack(summary_list, axis=0))

    attended, self_summary = lax.map(self_item, (triple[0], triple[1], triple[2], lengths))
    attended_flat = attended.reshape(full_rows, inner_width)
    first_rows = frame_rows + collect(attended_flat, w_out, False)
    normed_two, scaled_two, inverse_two = normalize(first_rows, norm_gain[1], norm_bias[1])
    second_input = spread(lower(normed_two))
    cross_query = lower(product(second_input, w_cross_q, False)).reshape(
        item_count, span, head_count, HEAD
    )
    cross_pair = lower(
        jnp.einsum("ntd,cde->cnte", text_states, w_cross_kv, preferred_element_type=jnp.float32)
    )
    cross_pair = cross_pair.reshape(2, item_count, text_count, head_count, HEAD)

    def cross_item(packed):
        query_part, key_part, value_part = packed
        return attend(query_part, key_part, value_part, True)

    cross_mixed, cross_summary = lax.map(cross_item, (cross_query, cross_pair[0], cross_pair[1]))
    cross_flat = cross_mixed.reshape(full_rows, inner_width)
    second_rows = first_rows + collect(cross_flat, w_cross_out, False)
    normed_three, scaled_three, inverse_three = normalize(second_rows, norm_gain[2], norm_bias[2])
    upstream = cotangent.astype(jnp.float32) * loss_mask.astype(jnp.float32)[:, None]
    ffn_grad = lower(upstream)
    ffn_input = spread(lower(normed_three))
    hidden_pre = product(ffn_input, w_up, False)
    active, slope = gelu_parts(hidden_pre)
    active = lower(active)
    out_rows = second_rows + collect(active, w_down, False)
    ffn_full = spread(ffn_grad)
    grad_down = outer_sum(active, ffn_full)
    grad_hidden = lower(product(ffn_full, w_down, True) * slope)
    grad_up = outer_sum(ffn_input, grad_hidden)
    back_three = collect(grad_hidden, w_up, True)
    grad_up, grad_down = (grad_up, grad_down)
    grad_in_three, gain_three, bias_three = normalize_back(
        back_three, scaled_three, inverse_three, norm_gain[2]
    )
    grad_second = upstream + grad_in_three
    cross_full = spread(lower(grad_second))
    grad_cross_out = outer_sum(cross_flat, cross_full)
    cross_upstream = lower(product(cross_full, w_cross_out, True)).reshape(
        item_count, span, head_count, HEAD
    )

    def cross_back(packed):
        query_part, key_part, value_part, summary, upstream_item = packed
        return attend_back(query_part, key_part, value_part, True, summary, upstream_item)

    grad_cq, grad_ck, grad_cv = lax.map(
        cross_back, (cross_query, cross_pair[0], cross_pair[1], cross_summary, cross_upstream)
    )
    grad_cq = lower(grad_cq).reshape(full_rows, inner_width)
    grad_pair = lower(jnp.stack((grad_ck, grad_cv), axis=0)).reshape(
        2, item_count, text_count, inner_width
    )
    grad_cross_q = outer_sum(second_input, grad_cq)
    grad_cross_kv = jnp.einsum(
        "ntd,cnte->cde", text_states, grad_pair, preferred_element_type=jnp.float32
    )
    grad_cross_q, grad_cross_kv, grad_cross_out = (grad_cross_q, grad_cross_kv, grad_cross_out)
    text_partial = jnp.einsum(
        "cnte,cde->ntd", grad_pair, w_cross_kv, preferred_element_type=jnp.float32
    )
    grad_text = lower(lax.psum(text_partial, "narrow"))
    back_two = collect(grad_cq, w_cross_q, True)
    grad_in_two, gain_two, bias_two = normalize_back(
        back_two, scaled_two, inverse_two, norm_gain[1]
    )
    grad_first = grad_second + grad_in_two
    self_full = spread(lower(grad_first))
    grad_out = outer_sum(attended_flat, self_full)
    self_upstream = lower(product(self_full, w_out, True)).reshape(
        item_count, span, head_count, HEAD
    )

    def self_back(packed):
        query_part, key_part, value_part, item_limit, summary, upstream_item = packed
        query_list = []
        key_list = []
        value_list = []
        for block_index in range(2):
            lower_row = block_index * half_span
            grad_query, grad_key, grad_value = attend_back(
                query_part[lower_row : lower_row + half_span],
                key_part,
                value_part,
                causal(block_index, item_limit),
                summary[block_index],
                upstream_item[lower_row : lower_row + half_span],
            )
            query_list.append(grad_query)
            key_list.append(grad_key)
            value_list.append(grad_value)
        return (
            jnp.concatenate(query_list, axis=0),
            key_list[0] + key_list[1],
            value_list[0] + value_list[1],
        )

    grad_q, grad_k, grad_v = lax.map(
        self_back, (triple[0], triple[1], triple[2], lengths, self_summary, self_upstream)
    )
    grad_triple = lower(jnp.stack((grad_q, grad_k, grad_v), axis=0)).reshape(
        3, full_rows, inner_width
    )
    grad_qkv = jnp.einsum(
        "rd,cre->cde", first_input, grad_triple, preferred_element_type=jnp.float32
    )
    grad_qkv, grad_out = (grad_qkv, grad_out)
    merged = grad_triple.transpose(1, 0, 2).reshape(full_rows, 3 * inner_width)
    stacked_weights = w_qkv.transpose(0, 2, 1).reshape(3 * inner_width, width)
    back_one = collect(merged, stacked_weights, False)
    grad_in_one, gain_one, bias_one = normalize_back(
        back_one, scaled_one, inverse_one, norm_gain[0]
    )
    grad_frames = lower(grad_first + grad_in_one)
    gain_terms = jnp.stack((gain_one, gain_two, gain_three), axis=0)
    bias_terms = jnp.stack((bias_one, bias_two, bias_three), axis=0)
    grad_norm_gain, grad_norm_bias = lax.psum((gain_terms, bias_terms), ("wide", "narrow"))
    grad_qkv, grad_out, grad_cross_q, grad_cross_kv, grad_cross_out, grad_up, grad_down = lax.psum(
        (grad_qkv, grad_out, grad_cross_q, grad_cross_kv, grad_cross_out, grad_up, grad_down),
        "wide",
    )
    return (
        lower(out_rows),
        grad_frames,
        grad_text,
        grad_norm_gain,
        grad_norm_bias,
        grad_qkv,
        grad_out,
        grad_cross_q,
        grad_cross_kv,
        grad_cross_out,
        grad_up,
        grad_down,
    )


ROUND = jnp.bfloat16
FULL = jnp.float32
CORE_PAIRS = ((0, 1), (1, 0), (2, 3), (3, 2))
Y_PAIRS = ((0, 2), (2, 0), (1, 3), (3, 1))
X_PAIRS = tuple((i, i ^ 1) for i in range(8))
Z_INWARD = ((0, 2), (1, 3), (6, 4), (7, 5))
Z_MIDDLE = ((2, 4), (4, 2), (3, 5), (5, 3))
Z_OUTWARD = ((2, 0), (3, 1), (4, 6), (5, 7))
Z_NEAR = tuple((i, i ^ 2) for i in range(8))
Z_FAR = tuple((i, i ^ 4) for i in range(8))
MIB = 1 << 20


def nt(a, b):
    return lax.dot_general(a, b, (((1,), (1,)), ((), ())), preferred_element_type=FULL)


def nn(a, b):
    return lax.dot_general(a, b, (((1,), (0,)), ((), ())), preferred_element_type=FULL)


def tn(a, b):
    return lax.dot_general(a, b, (((0,), (0,)), ((), ())), preferred_element_type=FULL)


def shape(dims, kind):
    return jax.ShapeDtypeStruct(dims, kind)


def resident(dims):
    zeros = (0,) * len(dims)
    return pl.BlockSpec(dims, lambda i, s: zeros, pipeline_mode=pl.Buffered(1))


def rows_of(block, width):
    return pl.BlockSpec((block, width), lambda i, s: (i, 0))


def lasting(microseconds):
    flops = int(microseconds * 0.28 * 1.15e9)
    return pl.CostEstimate(flops=flops, bytes_accessed=1000, transcendentals=0)


def params(mib):
    return pltpu.CompilerParams(vmem_limit_bytes=mib * MIB)


def norm_parts(v):
    centered = v - jnp.mean(v, axis=-1, keepdims=True)
    inverse = lax.rsqrt(jnp.mean(centered * centered, axis=-1, keepdims=True) + EPS)
    return centered * inverse, inverse


def norm_pull(y, scaled, inverse, gain_row):
    weighted = y * gain_row
    inner = jnp.mean(weighted, axis=-1, keepdims=True)
    along = jnp.mean(weighted * scaled, axis=-1, keepdims=True)
    return inverse * (weighted - inner - scaled * along)


def first_project_kernel(
    place_ref, mine_ref, other_ref, gain_ref, bias_ref, weight_ref, h_ref, *out_refs
):
    half = pl.program_id(0)

    def run(source):
        for start in range(0, source.shape[0], 208):
            part = slice(start, start + 208)
            scaled, _ = norm_parts(source[part, :].astype(FULL))
            h = lower(scaled * gain_ref[0:1, :] + bias_ref[0:1, :])
            h_ref[part, :] = h
            for c, out_ref in enumerate(out_refs):
                out_ref[part, :] = lower(nn(h, weight_ref[c]))

    @pl.when(half == 0)
    def _():
        run(mine_ref)

    @pl.when(half == 1)
    def _():
        run(other_ref)


def first_project(place, mine, other, gains, biases, weights):
    rows, depth = mine.shape
    count, _, wide = weights.shape
    out = pl.BlockSpec((rows, wide), lambda i, s: ((i + s[0]) % 2, 0))
    return pl.pallas_call(
        first_project_kernel,
        grid_spec=pltpu.PrefetchScalarGridSpec(
            num_scalar_prefetch=1,
            grid=(2,),
            in_specs=[resident(a.shape) for a in (mine, other, gains, biases, weights)],
            out_specs=[rows_of(rows, depth)] + [out] * count,
        ),
        out_shape=[shape((2 * rows, depth), ROUND)] + [shape((2 * rows, wide), ROUND)] * count,
        compiler_params=params(40),
        cost_estimate=lasting(5),
        name="first_project",
    )(place, mine, other, gains, biases, weights)


def project_kernel(place_ref, h_ref, weight_ref, *out_refs):
    count = len(out_refs)
    wide = weight_ref.shape[2]
    weights = jnp.concatenate([weight_ref[c] for c in range(count)], axis=1)
    for start in range(0, h_ref.shape[0], 416):
        part = slice(start, start + 416)
        result = lower(nn(h_ref[part, :], weights))
        for c, out_ref in enumerate(out_refs):
            out_ref[part, :] = result[:, c * wide : (c + 1) * wide]


def project(place, h, weights):
    rows, depth = h.shape[0] // 2, h.shape[1]
    count, _, wide = weights.shape
    out = pl.BlockSpec((rows, wide), lambda i, s: ((i + s[0]) % 2, 0))
    return pl.pallas_call(
        project_kernel,
        grid_spec=pltpu.PrefetchScalarGridSpec(
            num_scalar_prefetch=1,
            grid=(2,),
            in_specs=[rows_of(rows, depth), resident(weights.shape)],
            out_specs=[out] * count,
        ),
        out_shape=[shape((2 * rows, wide), ROUND)] * count,
        compiler_params=params(40),
        cost_estimate=lasting(4),
        name="project",
    )(place, h, weights)


def pull_kernel(place_ref, mine_ref, other_ref, *refs):
    half = pl.program_id(0)
    count = len(refs) // 2

    def run(source):
        for weight_ref, out_ref in zip(refs[:count], refs[count:]):
            out_ref[...] = lower(nt(source[...], weight_ref[...]))

    @pl.when(half == 0)
    def _():
        run(mine_ref)

    @pl.when(half == 1)
    def _():
        run(other_ref)


def pull(place, mine, other, weights):
    rows = mine.shape[0]
    return pl.pallas_call(
        pull_kernel,
        grid_spec=pltpu.PrefetchScalarGridSpec(
            num_scalar_prefetch=1,
            grid=(2,),
            in_specs=[resident(a.shape) for a in (mine, other, *weights)],
            out_specs=[
                pl.BlockSpec((rows, a.shape[0]), lambda i, s: ((i + s[0]) % 2, 0)) for a in weights
            ],
        ),
        out_shape=[shape((2 * rows, a.shape[0]), ROUND) for a in weights],
        compiler_params=params(32),
        cost_estimate=lasting(3.5),
        name="pull",
    )(place, mine, other, *weights)


def blocks_of(span, block):
    return [(start, min(block, span - start)) for start in range(0, span, block)]


def self_forward_kernel(
    limit_ref, q_ref, k_ref, v_ref, o_ref, lse_ref, *, span, floor, block
):
    limit = limit_ref[0]
    lane = lax.broadcasted_iota(jnp.int32, (1, 128), 1)
    row = lax.broadcasted_iota(jnp.int32, (128, 1), 0)
    zero = jnp.zeros((), ROUND)
    value_turned = v_ref[...].T
    for start, size in blocks_of(span, block):
        end = start + size
        mixed_list = []
        for h in range(2):
            own_lanes = (lane < HEAD) if h == 0 else (lane >= HEAD)
            query = jnp.where(own_lanes, q_ref[start:end, :] * HEAD ** (-0.5), zero)
            parts = []
            for low in range(0, end, block):
                high = min(low + block, end)
                scores = nt(k_ref[low:high, :], query)
                if low == start:
                    key = lax.broadcasted_iota(jnp.int32, (size, size), 0)
                    valid = key <= lax.broadcasted_iota(jnp.int32, (size, size), 1)
                    if high > floor:
                        valid = valid & (key + low < limit)
                    scores = jnp.where(valid, scores, NEG)
                elif high > floor:
                    key = lax.broadcasted_iota(jnp.int32, (high - low, 1), 0)
                    scores = jnp.where(key + low < limit, scores, NEG)
                parts.append((low, high, scores))
            top = functools.reduce(
                jnp.maximum, [jnp.max(s, axis=0, keepdims=True) for _, _, s in parts]
            )
            total = 0.0
            mixed = 0.0
            for low, high, scores in parts:
                weights_exp = jnp.exp(scores - top)
                total = total + jnp.sum(weights_exp, axis=0, keepdims=True)
                mixed = mixed + nn(value_turned[:, low:high], lower(weights_exp))
            mixed_list.append(mixed / total)
            lse_ref[0, h : h + 1, start:end] = top + jnp.log(total)
        o_ref[start:end, :] = lower(jnp.where(row < HEAD, mixed_list[0], mixed_list[1]).T)


def self_forward(limit, q, k, v):
    span, wide = q.shape
    pairs = wide // 128
    floor = (span - span // 8 + 1) // 128 * 128
    pair = pl.BlockSpec((span, 128), lambda p, s: (0, p))
    return pl.pallas_call(
        functools.partial(self_forward_kernel, span=span, floor=floor, block=512),
        grid_spec=pltpu.PrefetchScalarGridSpec(
            num_scalar_prefetch=1,
            grid=(pairs,),
            in_specs=[pair] * 3,
            out_specs=[pair, pl.BlockSpec((1, 8, span), lambda p, s: (p, 0, 0))],
        ),
        out_shape=[shape((span, wide), ROUND), shape((pairs, 8, span), FULL)],
        compiler_params=params(56),
        cost_estimate=lasting(7.3 * pairs),
        name="self_forward",
    )(limit, q, k, v)


def self_back_kernel(
    limit_ref, q_ref, k_ref, v_ref, o_ref, do_ref, lse_ref, dq_ref, dk_ref, dv_ref, dqt,
    *, span, floor, block
):
    limit = limit_ref[0]
    lane = lax.broadcasted_iota(jnp.int32, (1, 128), 1)
    row = lax.broadcasted_iota(jnp.int32, (128, 1), 0)
    zero = jnp.zeros((), ROUND)
    factor = HEAD ** (-0.5)
    product_rows = do_ref[...].astype(FULL) * o_ref[...].astype(FULL)
    high = lower(product_rows)
    rest = lower(product_rows - high.astype(FULL))
    pick = lower(
        jnp.concatenate(
            [
                jnp.where(lane < HEAD, 1.0, 0.0),
                jnp.where(lane >= HEAD, 1.0, 0.0),
                jnp.zeros((6, 128), FULL),
            ],
            axis=0,
        )
    )
    delta = nt(pick, high) + nt(pick, rest)
    for start, size in blocks_of(span, block):
        end = start + size
        key = k_ref[start:end, :]
        value = v_ref[start:end, :]
        key_turned = key.T
        dk = 0.0
        dv = 0.0
        dq_add = 0.0
        for h in range(2):
            own_lanes = (lane < HEAD) if h == 0 else (lane >= HEAD)
            own_rows = (row < HEAD) if h == 0 else (row >= HEAD)
            query = jnp.where(own_lanes, q_ref[start:, :] * factor, zero)
            pulled = jnp.where(own_lanes, do_ref[start:, :], zero)
            probability = jnp.exp(nt(key, query) - lse_ref[0, h : h + 1, start:])
            pressure = nt(value, pulled)
            below = lax.broadcasted_iota(jnp.int32, (size, size), 0)
            across = lax.broadcasted_iota(jnp.int32, (size, size), 1)
            corner = jnp.where(below <= across, probability[:, :size], 0.0)
            if end < span:
                probability = jnp.concatenate([corner, probability[:, size:]], axis=1)
            else:
                probability = corner
            if end > floor:
                place = lax.broadcasted_iota(jnp.int32, (size, 1), 0) + start
                probability = jnp.where(place < limit, probability, 0.0)
            grad_scores = lower(probability * (pressure - delta[h : h + 1, start:]))
            dv = dv + nn(lower(probability), pulled)
            dk = dk + nn(grad_scores, query)
            dq_add = dq_add + nn(jnp.where(own_rows, key_turned, zero), grad_scores)
        dk_ref[start:end, :] = lower(dk)
        dv_ref[start:end, :] = lower(dv)
        if start == 0:
            dqt[...] = dq_add
        else:
            dqt[:, start:] += dq_add
    dq_ref[...] = lower(dqt[...].T * factor)


def self_back(limit, q, k, v, o, do, lse):
    span, wide = q.shape
    pairs = wide // 128
    floor = (span - span // 8 + 1) // 128 * 128
    pair = pl.BlockSpec((span, 128), lambda p, s: (0, p))
    return pl.pallas_call(
        functools.partial(self_back_kernel, span=span, floor=floor, block=256),
        grid_spec=pltpu.PrefetchScalarGridSpec(
            num_scalar_prefetch=1,
            grid=(pairs,),
            in_specs=[pair] * 5 + [pl.BlockSpec((1, 8, span), lambda p, s: (p, 0, 0))],
            out_specs=[pair] * 3,
            scratch_shapes=[pltpu.VMEM((128, span), FULL)],
        ),
        out_shape=[shape((span, wide), ROUND)] * 3,
        compiler_params=params(48),
        cost_estimate=lasting(9.8 * pairs),
        name="self_back",
    )(limit, q, k, v, o, do, lse)


def by_head(values_in, reduce, empty):
    lane = lax.broadcasted_iota(jnp.int32, (1, 128), 1)
    pieces = []
    for start in range(0, values_in.shape[1], 128):
        part = values_in[:, start : start + 128]
        first = reduce(jnp.where(lane < HEAD, part, empty), axis=1, keepdims=True)
        second = reduce(jnp.where(lane >= HEAD, part, empty), axis=1, keepdims=True)
        pieces.append(jnp.where(lane < HEAD, first, second))
    return jnp.concatenate(pieces, axis=1)


def cross_probability(query, keys):
    scores = nt(query * HEAD ** (-0.5), keys)
    weights_exp = jnp.exp(scores - by_head(scores, jnp.max, NEG))
    return weights_exp / by_head(weights_exp, jnp.sum, 0.0)


def in_groups(refs, axis):
    for at in (0, 3):
        yield refs[at][...]
        yield jnp.concatenate([refs[at + 1][...], refs[at + 2][...]], axis=axis)


def middle_forward_kernel(place_ref, frame_ref, *refs):
    mixed, wo, wq, wc = refs[0:6], refs[6:12], refs[12:18], refs[18:24]
    ck_ref, cv_ref, gain_ref, bias_ref = refs[24:28]
    x1_ref, x2_ref, h2_ref, cq_ref, ca_ref, h3_ref = refs[28:]
    x1 = frame_ref[...].astype(FULL)
    for o, weight in zip(in_groups(mixed, 1), in_groups(wo, 0)):
        x1 = x1 + nn(o, weight)
    x1_ref[...] = x1
    scaled, _ = norm_parts(x1)
    h2 = lower(scaled * gain_ref[1:2, :] + bias_ref[1:2, :])
    h2_ref[...] = h2
    for g, weight in enumerate(in_groups(wq, 1)):
        lanes = slice(g * 256, (g + 1) * 256)
        cq_ref[:, lanes] = lower(nn(h2, weight))
        probability = cross_probability(cq_ref[:, lanes], ck_ref[g])
        ca_ref[:, lanes] = lower(nn(lower(probability), cv_ref[g]))
    crossed = 0.0
    for g, weight in enumerate(in_groups(wc, 0)):
        crossed = crossed + nn(ca_ref[:, g * 256 : (g + 1) * 256], weight)
    x2 = x1_ref[...] + crossed
    x2_ref[...] = x2
    scaled, _ = norm_parts(x2)
    h3_ref[...] = lower(scaled * gain_ref[2:3, :] + bias_ref[2:3, :])


def middle_forward(place, frames, attended, received, wo, wq, wc, ck, cv, gains, biases):
    rows, width = frames.shape
    block = 416
    steps = rows // block
    wide = rows_of(block, width)
    whole = (*wo, *wq, *wc, ck, cv, gains, biases)
    return pl.pallas_call(
        middle_forward_kernel,
        grid_spec=pltpu.PrefetchScalarGridSpec(
            num_scalar_prefetch=1,
            grid=(steps,),
            in_specs=[wide]
            + [
                pl.BlockSpec((block, a.shape[1]), lambda i, s: (s[0] * steps + i, 0))
                for a in attended
            ]
            + [rows_of(block, a.shape[1]) for a in received]
            + [resident(a.shape) for a in whole],
            out_specs=[wide] * 6,
        ),
        out_shape=[shape((rows, width), FULL)] * 2 + [shape((rows, width), ROUND)] * 4,
        compiler_params=params(56),
        cost_estimate=lasting(22),
        name="middle_forward",
    )(place, frames, *attended, *received, *whole)


def keys_kernel(text_ref, weight_ref, out_ref):
    for item in range(2):
        for c in range(2):
            out_ref[item, c] = lower(nn(text_ref[item], weight_ref[c]))


def keys_of(text_states, weights):
    items, states, _ = text_states.shape
    return pl.pallas_call(
        keys_kernel,
        out_shape=shape((items, 2, states, weights.shape[2]), ROUND),
        compiler_params=params(24),
        cost_estimate=lasting(2),
        name="keys_of",
    )(text_states, weights)


def feed_kernel(place_ref, h_ref, d_ref, *refs, parts, carried):
    ups, downs = refs[:parts], refs[parts : 2 * parts]
    before = refs[2 * parts : 2 * parts + carried]
    g_ref, du_ref, out_ref, y_ref = refs[-4:]
    h = h_ref[...]
    d = d_ref[...]
    out = 0.0
    y = 0.0
    for n, (up_ref, down_ref) in enumerate(zip(ups, downs)):
        size = down_ref.shape[0]
        if parts == 1:
            lanes = slice(0, size)
        else:
            column = place_ref[2]
            which = column if n == 0 else 1 - column
            lanes = pl.ds(pl.multiple_of(which * size, 128), size)
        u = nn(h, up_ref[...])
        active, slope = gelu_parts(u)
        g = lower(active)
        g_ref[:, lanes] = g
        du = lower(nt(d, down_ref[...]) * slope)
        du_ref[:, lanes] = du
        out = out + nn(g, down_ref[...])
        y = y + nt(du, up_ref[...])
    if carried:
        out = before[0][...] + out
        y = before[1][...] + y
    out_ref[...] = out.astype(out_ref.dtype)
    y_ref[...] = y.astype(y_ref.dtype)


def feed(place, h, d, ups, downs, kind, half, before=(), shared=()):
    rows, width = h.shape
    block = 416
    steps = rows // block
    hidden = sum(a.shape[0] for a in downs)
    wide = rows_of(block, width)
    kept = pl.BlockSpec((block, hidden), lambda i, s: (i + half * steps, 0))
    there = pl.BlockSpec(memory_space=pl.ANY)
    parts = len(ups)
    at = 3 + 2 * parts + len(before)
    return pl.pallas_call(
        functools.partial(feed_kernel, parts=parts, carried=len(before)),
        grid_spec=pltpu.PrefetchScalarGridSpec(
            num_scalar_prefetch=1,
            grid=(steps,),
            in_specs=[wide, wide]
            + [resident(a.shape) for a in (*ups, *downs)]
            + [wide] * len(before)
            + [there] * len(shared),
            out_specs=[kept, kept, wide, wide],
        ),
        out_shape=[shape((2 * rows, hidden), ROUND)] * 2 + [shape((rows, width), kind)] * 2,
        input_output_aliases={at: 0, at + 1: 1} if shared else {},
        compiler_params=params(58),
        cost_estimate=lasting(13),
        name="feed",
    )(place, h, d, *ups, *downs, *before, *shared)


def up_grad_kernel(mine_ref, other_ref, du_ref, out_ref):
    rows = mine_ref.shape[0]
    total = tn(mine_ref[...], du_ref[:rows, :]) + tn(other_ref[...], du_ref[rows:, :])
    out_ref[...] = total.astype(out_ref.dtype)


def up_grad(mine, other, du, kind):
    rows, width = mine.shape
    hidden = du.shape[1]
    tile = 512
    whole = pl.BlockSpec((rows, width), lambda i: (0, 0), pipeline_mode=pl.Buffered(1))
    return pl.pallas_call(
        up_grad_kernel,
        grid=(hidden // tile,),
        in_specs=[whole, whole, pl.BlockSpec((2 * rows, tile), lambda i: (0, i))],
        out_specs=pl.BlockSpec((width, tile), lambda i: (0, i)),
        out_shape=shape((width, hidden), kind),
        compiler_params=params(48),
        cost_estimate=lasting(7),
        name="up_grad",
    )(mine, other, du)


def down_grad_kernel(g_ref, mine_ref, other_ref, out_ref):
    rows = mine_ref.shape[0]
    total = tn(g_ref[:rows, :], mine_ref[...]) + tn(g_ref[rows:, :], other_ref[...])
    out_ref[...] = total.astype(out_ref.dtype)


def down_grad(g, mine, other, kind):
    rows, width = mine.shape
    hidden = g.shape[1]
    tile = 512
    whole = pl.BlockSpec((rows, width), lambda i: (0, 0), pipeline_mode=pl.Buffered(1))
    return pl.pallas_call(
        down_grad_kernel,
        grid=(hidden // tile,),
        in_specs=[pl.BlockSpec((2 * rows, tile), lambda i: (0, i)), whole, whole],
        out_specs=pl.BlockSpec((tile, width), lambda i: (i, 0)),
        out_shape=shape((hidden, width), kind),
        compiler_params=params(48),
        cost_estimate=lasting(7),
        name="down_grad",
    )(g, mine, other)


def qkv_grad_kernel(place_ref, h_ref, *refs):
    out_ref = refs[-1]
    rows, width = h_ref.shape[0] // 2, h_ref.shape[1]
    core, near = place_ref[0], place_ref[1]
    halves = (len(refs) - 1) // 3
    total = [0.0] * 3
    for half in range(2):
        turned = h_ref[half * rows : (half + 1) * rows, :].T
        at = pl.multiple_of((core if half == 0 else 1 - core) * rows, 16)
        for c in range(3):
            parts = [refs[3 * n + c][pl.ds(at, rows), :] for n in range(halves)]
            grads = parts[0] if halves == 1 else jnp.concatenate(parts, axis=1)
            total[c] = total[c] + nn(turned, grads)
    for c in range(3):
        part = slice(c * width, (c + 1) * width)
        value = total[c].astype(out_ref.dtype)
        if halves == 1:
            out_ref[part, :] = value
        else:
            out_ref[part, pl.ds(pl.multiple_of(near * 128, 128), 128)] = value[:, :128]
            out_ref[part, pl.ds(pl.multiple_of((1 - near) * 128, 128), 128)] = value[:, 128:]


def qkv_grad(place, h, grads, kind):
    width = h.shape[1]
    return pl.pallas_call(
        qkv_grad_kernel,
        grid_spec=pltpu.PrefetchScalarGridSpec(
            num_scalar_prefetch=1,
            grid=(1,),
            in_specs=[resident(a.shape) for a in (h, *grads)],
            out_specs=resident((3 * width, 256)),
        ),
        out_shape=shape((3 * width, 256), kind),
        compiler_params=params(48),
        cost_estimate=lasting(7),
        name="qkv_grad",
    )(place, h, *grads)


def query_grad_kernel(place_ref, mine_ref, other_ref, dm_ref, do_ref, out_ref, *, split):
    column = place_ref[2]
    total = tn(mine_ref[...], dm_ref[...]) + tn(other_ref[...], do_ref[...])
    value = total.astype(out_ref.dtype)
    if split:
        out_ref[:, pl.ds(pl.multiple_of(column * 128, 128), 128)] = value[:, :128]
        out_ref[:, pl.ds(pl.multiple_of((1 - column) * 128, 128), 128)] = value[:, 128:]
    else:
        out_ref[...] = value


def query_grad(place, group, mine, other, d_mine, d_other, kind):
    rows, width = mine.shape
    lanes = pl.BlockSpec((rows, 256), lambda i, s: (0, group))
    return pl.pallas_call(
        functools.partial(query_grad_kernel, split=group == 1),
        grid_spec=pltpu.PrefetchScalarGridSpec(
            num_scalar_prefetch=1,
            grid=(1,),
            in_specs=[resident(mine.shape), resident(other.shape), lanes, lanes],
            out_specs=resident((width, 256)),
        ),
        out_shape=shape((width, 256), kind),
        compiler_params=params(48),
        cost_estimate=lasting(4),
        name="query_grad",
    )(place, mine, other, d_mine, d_other)


def outputs_grad_kernel(place_ref, *refs, count):
    o_refs = refs[:count]
    sm_ref, so_ref, am_ref, ao_ref, cm_ref, co_ref, out_ref = refs[count:]
    rows = sm_ref.shape[0]
    core, near, column = place_ref[0], place_ref[1], place_ref[2]
    mine_at = pl.ds(pl.multiple_of(core * rows, 16), rows)
    other_at = pl.ds(pl.multiple_of((1 - core) * rows, 16), rows)
    for n, o_ref in enumerate(o_refs):
        total = tn(o_ref[mine_at, :], sm_ref[...]) + tn(o_ref[other_at, :], so_ref[...])
        if count == 1:
            at = slice(0, 256)
        else:
            at = pl.ds(pl.multiple_of((near if n == 0 else 1 - near) * 128, 128), 128)
        out_ref[at, :] = total.astype(out_ref.dtype)
    total = tn(am_ref[...], cm_ref[...]) + tn(ao_ref[...], co_ref[...])
    value = total.astype(out_ref.dtype)
    if count == 1:
        out_ref[256:, :] = value
    else:
        out_ref[pl.ds(pl.multiple_of(256 + column * 128, 128), 128), :] = value[:128, :]
        out_ref[pl.ds(pl.multiple_of(384 - column * 128, 128), 128), :] = value[128:, :]


def outputs_grad(place, group, o, dself, dself_other, ca, ca_other, dcross, dcross_other, kind):
    rows, width = dself.shape
    lanes = pl.BlockSpec((rows, 256), lambda i, s: (0, group))
    whole = resident((rows, width))
    return pl.pallas_call(
        functools.partial(outputs_grad_kernel, count=len(o)),
        grid_spec=pltpu.PrefetchScalarGridSpec(
            num_scalar_prefetch=1,
            grid=(1,),
            in_specs=[resident(a.shape) for a in o] + [whole, whole, lanes, lanes, whole, whole],
            out_specs=resident((512, width)),
        ),
        out_shape=shape((512, width), kind),
        compiler_params=params(48),
        cost_estimate=lasting(6),
        name="outputs_grad",
    )(place, *o, dself, dself_other, ca, ca_other, dcross, dcross_other)


def middle_back_kernel(place_ref, ym_ref, yr_ref, x1_ref, x2_ref, d_ref, cq_ref, *refs):
    wq, wc = refs[0:6], refs[6:12]
    ck_ref, cv_ref, gain_ref = refs[12:15]
    dx1_ref, dself_ref, dcross_ref, dcq_ref, dck_ref, dcv_ref, sums_ref = refs[15:22]
    dck_all, dcv_all = refs[22:]
    step = pl.program_id(0)

    @pl.when(step == 0)
    def _():
        dck_all[...] = jnp.zeros_like(dck_all)
        dcv_all[...] = jnp.zeros_like(dcv_all)
        sums_ref[...] = jnp.zeros_like(sums_ref)

    y3 = ym_ref[...] + yr_ref[...].astype(FULL)
    scaled, inverse = norm_parts(x2_ref[...])
    sums_ref[4:5, :] += jnp.sum(y3 * scaled, axis=0, keepdims=True)
    sums_ref[5:6, :] += jnp.sum(y3, axis=0, keepdims=True)
    dx2 = d_ref[...].astype(FULL) + norm_pull(y3, scaled, inverse, gain_ref[2:3, :])
    dx1_ref[...] = dx2
    dcross = lower(dx2)
    dcross_ref[...] = dcross
    for g, weight in enumerate(in_groups(wc, 0)):
        lanes = slice(g * 256, (g + 1) * 256)
        dcatt = lower(nt(dcross, weight))
        keys = ck_ref[g]
        cq = cq_ref[:, lanes]
        probability = cross_probability(cq, keys)
        weighed = nt(dcatt, cv_ref[g])
        inner = by_head(probability * weighed, jnp.sum, 0.0)
        dcs = lower(probability * (weighed - inner))
        dcq_ref[:, lanes] = lower(nn(dcs, keys) * HEAD ** (-0.5))
        dck_all[g] += tn(dcs, cq * HEAD ** (-0.5))
        dcv_all[g] += tn(lower(probability), dcatt)
    y2 = 0.0
    for g, weight in enumerate(in_groups(wq, 1)):
        y2 = y2 + nt(dcq_ref[:, g * 256 : (g + 1) * 256], weight)
    scaled, inverse = norm_parts(x1_ref[...])
    sums_ref[2:3, :] += jnp.sum(y2 * scaled, axis=0, keepdims=True)
    sums_ref[3:4, :] += jnp.sum(y2, axis=0, keepdims=True)
    dx1 = dx1_ref[...] + norm_pull(y2, scaled, inverse, gain_ref[1:2, :])
    dx1_ref[...] = dx1
    dself_ref[...] = lower(dx1)

    @pl.when(step == pl.num_programs(0) - 1)
    def _():
        for every, result in ((dck_all, dck_ref), (dcv_all, dcv_ref)):
            for g in range(4):
                total = 0.0
                for h in range(4):
                    lane = lax.broadcasted_iota(jnp.int32, (1, 256), 1) // HEAD
                    total = total + jnp.where(lane == h, every[g, h * 64 : (h + 1) * 64, :], 0.0)
                result[g] = total


def middle_back(place, ym, yr, x1, x2, d, cq, wq, wc, ck, cv, gains):
    rows, width = x1.shape
    block = 416
    wide = rows_of(block, width)
    small = pl.BlockSpec((4, 64, 256), lambda i, s: (0, 0, 0))
    whole = (*wq, *wc, ck, cv, gains)
    return pl.pallas_call(
        middle_back_kernel,
        grid_spec=pltpu.PrefetchScalarGridSpec(
            num_scalar_prefetch=1,
            grid=(rows // block,),
            in_specs=[wide] * 6 + [resident(a.shape) for a in whole],
            out_specs=[wide] * 4 + [small, small, pl.BlockSpec((8, width), lambda i, s: (0, 0))],
            scratch_shapes=[pltpu.VMEM((4, 256, 256), FULL)] * 2,
        ),
        out_shape=[shape((rows, width), FULL)]
        + [shape((rows, width), ROUND)] * 3
        + [shape((4, 64, 256), FULL)] * 2
        + [shape((8, width), FULL)],
        compiler_params=params(56),
        cost_estimate=lasting(24),
        name="middle_back",
    )(place, ym, yr, x1, x2, d, cq, *whole)


def first_back_kernel(place_ref, *refs):
    y_ref = refs[-1]
    y = 0.0
    for n in range(3):
        for c in range(3):
            y = y + nt(refs[3 * n + c][...], refs[9 + n][c])
    y_ref[...] = y.astype(y_ref.dtype)


def first_back(place, grads, weights, kind):
    span = grads[0].shape[0]
    rows = span // 2
    width = weights[0].shape[1]
    block = 416
    steps = rows // block
    return pl.pallas_call(
        first_back_kernel,
        grid_spec=pltpu.PrefetchScalarGridSpec(
            num_scalar_prefetch=1,
            grid=(steps,),
            in_specs=[
                pl.BlockSpec((block, a.shape[1]), lambda i, s: (s[0] * steps + i, 0))
                for a in grads
            ]
            + [resident(a.shape) for a in weights],
            out_specs=rows_of(block, width),
        ),
        out_shape=shape((rows, width), kind),
        compiler_params=params(40),
        cost_estimate=lasting(5),
        name="first_back",
    )(place, *grads, *weights)


def frames_back_kernel(place_ref, ym_ref, yr_ref, dx1_ref, frame_ref, gain_ref, out_ref, sums_ref):
    @pl.when(pl.program_id(0) == 0)
    def _():
        sums_ref[...] = jnp.zeros_like(sums_ref)

    y = ym_ref[...] + yr_ref[...].astype(FULL)
    scaled, inverse = norm_parts(frame_ref[...].astype(FULL))
    sums_ref[0:1, :] += jnp.sum(y * scaled, axis=0, keepdims=True)
    sums_ref[1:2, :] += jnp.sum(y, axis=0, keepdims=True)
    out_ref[...] = lower(dx1_ref[...] + norm_pull(y, scaled, inverse, gain_ref[0:1, :]))


def frames_back(place, ym, yr, dx1, frames, gains):
    rows, width = dx1.shape
    block = 208
    wide = rows_of(block, width)
    return pl.pallas_call(
        frames_back_kernel,
        grid_spec=pltpu.PrefetchScalarGridSpec(
            num_scalar_prefetch=1,
            grid=(rows // block,),
            in_specs=[wide] * 4 + [resident(gains.shape)],
            out_specs=[wide, pl.BlockSpec((8, width), lambda i, s: (0, 0))],
        ),
        out_shape=[shape((rows, width), ROUND), shape((8, width), FULL)],
        compiler_params=params(24),
        cost_estimate=lasting(6),
        name="frames_back",
    )(place, ym, yr, dx1, frames, gains)


def chip_local(
    frames, text_states, lengths, loss_mask, norm_gain, norm_bias, w_qkv, w_out, w_cross_q,
    w_cross_kv, w_cross_out, w_up, w_down, cotangent,
):
    at = lax.axis_index("narrow")
    core = at % 2
    side = at // 2
    column = lax.axis_index("wide") % 2
    layer = lax.axis_index("wide") // 2
    near = layer % 2
    place = jnp.stack([core, near, column]).astype(jnp.int32)
    away = jnp.stack([1 - core, near, column]).astype(jnp.int32)
    limit = lax.dynamic_slice(lengths, (side,), (1,))
    rows, width = frames.shape
    join = lax.optimization_barrier

    def over_core(v):
        return lax.ppermute(v, "narrow", CORE_PAIRS)

    def over_y(v):
        return lax.ppermute(v, "narrow", Y_PAIRS)

    def along_wide(v, pairs):
        return lax.ppermute(v, "wide", pairs)

    def half_of(v, which, axis=0):
        half = v.shape[axis] // 2
        return lax.dynamic_slice_in_dim(v, which * half, half, axis=axis)

    def ordered(first, second, which):
        return jnp.where(
            which == 0,
            jnp.concatenate([first, second], axis=0),
            jnp.concatenate([second, first], axis=0),
        )

    def over_z(v):
        return along_wide(v, Z_NEAR)

    def over_x(v):
        return along_wide(v, X_PAIRS)

    def away_rows(v):
        return half_of(v, 1 - core)

    def cross_order(v):
        return jnp.where(column == 0, v, jnp.concatenate([v[..., 128:], v[..., :128]], axis=-1))

    qkv_first = over_y(half_of(w_qkv, near, 2))
    frames_other = over_core(frames)
    h1, q0, k0, v0 = first_project(place, frames, frames_other, norm_gain, norm_bias, w_qkv)
    q0, qkv_first, w_out, w_cross_q, w_cross_out, cotangent = join(
        (q0, qkv_first, w_out, w_cross_q, w_cross_out, cotangent)
    )

    qkv_second = over_z(qkv_first)
    out_first = over_y(half_of(w_out, near))
    query_first = over_y(half_of(w_cross_q, column, 1))
    cross_out_first = over_y(half_of(w_cross_out, column))
    o0, lse0 = self_forward(limit, q0, k0, v0)
    qf, kf, vf = project(place, h1, qkv_first)
    out_other, query_other, cross_out_other = map(over_core, (w_out, w_cross_q, w_cross_out))
    qf, o0, out_first, query_first, cross_out_first, w_up, w_down, *core_got = join(
        (qf, o0, out_first, query_first, cross_out_first, w_up, w_down)
        + (out_other, query_other, cross_out_other)
    )

    out_other, query_other, cross_out_other = core_got
    out_second = over_z(out_first)
    query_second = over_x(query_first)
    cross_out_second = over_x(cross_out_first)
    up_first = over_y(half_of(w_up, column, 1))
    down_sent = half_of(w_down, column)
    o0_other = over_core(away_rows(o0))
    keys = keys_of(text_states, w_cross_kv)
    own_keys = lax.dynamic_index_in_dim(keys, side, keepdims=False)
    keys_y = over_y(lax.dynamic_index_in_dim(keys, 1 - side, keepdims=False))
    of, lse_f = self_forward(limit, qf, kf, vf)
    of, qkv_second, keys_y, o0_other = join((of, qkv_second, keys_y, o0_other))

    qs, ks, vs = project(place, h1, qkv_second)
    of_other = over_core(away_rows(of))
    pair = jnp.stack([own_keys, cross_order(keys_y)])
    pair_other = over_core(pair)
    o_s, lse_s = self_forward(limit, qs, ks, vs)
    o_s, out_second, query_second, cross_out_second, up_first, down_sent, pair_other, of_other = join(
        (o_s, out_second, query_second, cross_out_second, up_first, down_sent, pair_other, of_other)
    )

    down_first = over_y(down_sent)
    up_second = over_x(up_first)
    os_other = over_core(away_rows(o_s))
    dout = jnp.where(loss_mask[:, None] != 0, cotangent, jnp.zeros((), ROUND))

    def pieces(own, first, second, own_other):
        return (own, first, second, own_other, over_core(first), over_core(second))

    wo = pieces(w_out, out_first, out_second, out_other)
    wq = pieces(w_cross_q, query_first, query_second, query_other)
    wc = pieces(w_cross_out, cross_out_first, cross_out_second, cross_out_other)
    text = lax.dynamic_index_in_dim(text_states, side, keepdims=False)
    head_of = jnp.arange(256) // HEAD
    same = head_of[:, None] == head_of[None, :]

    def spread_heads(v):
        return jnp.where(same, jnp.tile(v, (1, 4, 1)), jnp.zeros((), ROUND))

    every = jnp.concatenate([pair, pair_other], axis=0)
    ck, cv = spread_heads(every[:, 0]), spread_heads(every[:, 1])
    x1, x2, h2, cq, ca, h3 = middle_forward(
        place, frames, (o0, of, o_s), (o0_other, of_other, os_other), wo, wq, wc, ck, cv,
        norm_gain, norm_bias,
    )
    h3, ca, h2, down_first, dout = join((h3, ca, h2, down_first, dout))

    h3_other = over_core(h3)
    dout_other = over_core(dout)
    down_second = over_x(down_first)
    g0, du0, out_m, y_m = feed(place, h3, dout, (w_up,), (w_down,), FULL, 0)
    g0, du0, out_o, y_o = feed(
        place, h3_other, dout_other, (w_up,), (w_down,), FULL, 1, shared=(g0, du0)
    )
    y_o, up_second, down_second, ca, h2 = join((y_o, up_second, down_second, ca, h2))

    ups = (up_first, up_second)
    downs = (down_first, down_second)
    g1, du1, out_o, y_o = feed(
        place, h3_other, dout_other, ups, downs, ROUND, 1, before=(out_o, y_o)
    )
    y_received = over_core(y_o)
    h2_other = over_core(h2)
    ca_other = over_core(ca[:, 512:])
    g1, du1, out_m, y_m = feed(
        place, h3, dout, ups, downs, FULL, 0, before=(out_m, y_m), shared=(g1, du1)
    )

    def plus(a, b):
        return lower(a.astype(FULL) + b.astype(FULL))

    across = (column, X_PAIRS)
    down_z = (near, Z_NEAR)
    store = {}
    last = []

    def order(*names):
        names = tuple(dict.fromkeys((*names, *last)))
        for name, value in zip(names, join(tuple(store[name] for name in names))):
            store[name] = value

    def get(*names):
        return tuple(store[name] for name in names)

    def step(results, make, *needs):
        order(*needs)
        made = make()
        made = made if isinstance(made, (tuple, list)) else (made,)
        store.update(zip(results, made))
        last[:] = results[:1]

    class Sum:
        def __init__(self, name, axes=(across, down_z)):
            self.fly, self.kept, self.axes = name + "_fly", name + "_kept", axes

        def over_y(self, partner):
            order(partner)
            store[self.fly] = over_y(store[partner])

        def first(self, own):
            which, pairs = self.axes[0]
            order(self.fly, own)
            mine, fly = get(own, self.fly)
            away_half = plus(half_of(mine, 1 - which), half_of(fly, 1 - which))
            store[self.kept] = half_of(mine, which).astype(FULL) + half_of(fly, which).astype(FULL)
            store[self.fly] = along_wide(away_half, pairs)
            last[:] = [self.kept]

        def first_alone(self, own):
            which, pairs = self.axes[0]
            store[self.kept] = half_of(store[own], which).astype(FULL)
            store[self.fly] = along_wide(half_of(store[own], 1 - which), pairs)
            last[:] = [self.kept]

        def second(self):
            which, pairs = self.axes[1]
            order(self.fly, self.kept)
            total = store[self.kept] + store[self.fly].astype(FULL)
            store[self.kept] = half_of(total, which)
            store[self.fly] = along_wide(lower(half_of(total, 1 - which)), pairs)
            last[:] = [self.kept]

        def add(self, pairs):
            order(self.fly, self.kept)
            store[self.kept] = plus(*get(self.kept, self.fly))
            store[self.fly] = along_wide(store[self.kept], pairs)
            last[:] = [self.kept]

        def far(self):
            self.add(Z_FAR)

        def back(self):
            self.add(self.axes[1][1])

        def along(self):
            order(self.fly, self.kept)
            store[self.kept] = ordered(*get(self.kept, self.fly), self.axes[1][0])
            store[self.fly] = along_wide(store[self.kept], self.axes[0][1])
            last[:] = [self.kept]

        def end(self, result):
            order(self.fly, self.kept)
            store[result] = ordered(*get(self.kept, self.fly), self.axes[0][0]).astype(FULL)
            last[:] = [result]

    class Row:
        def __init__(self, name, value, move):
            self.fly, self.kept = name + "_fly", name + "_kept"
            store[self.kept] = value
            store[self.fly] = move(value)

        def then(self, move):
            order(self.fly, self.kept)
            store[self.kept] = store[self.kept] + store[self.fly]
            store[self.fly] = move(store[self.kept])
            last[:] = [self.kept]

        def total(self):
            return store[self.kept] + store[self.fly]

    up, down, qkv = Sum("up"), Sum("down"), Sum("qkv")
    outs, cross_in = Sum("outs", (down_z, across)), Sum("cross_in", (down_z, across))
    store.update(h3_other=h3_other, du1=du1, g1=g1, du0=du0, g0=g0, y_m=y_m, y_fly=y_received)
    store.update(of=of, o_s=o_s, o0=o0, x2=x2, h2_other=h2_other, ca_other=ca_other)

    def middle():
        dx1, *rest = middle_back(
            place, *get("y_m", "y_fly"), x1, store["x2"], dout, cq, wq, wc, ck, cv, norm_gain
        )
        return (rest[0], dx1, *rest[1:])

    step(["up1"], lambda: up_grad(h3, *get("h3_other", "du1"), ROUND), "du1", "du0")
    up.over_y("up1")
    step(["down1"], lambda: down_grad(store["g1"], dout, dout_other, ROUND), "g1")
    step(["dself", "dx1", "dcross", "dcq", "dck", "dcv", "sums"], middle, "y_fly", "y_m", "x2")
    store["dself_other"] = over_core(store["dself"])
    step(["up0"], lambda: up_grad(h3, *get("h3_other", "du0"), ROUND), "du0")
    order(up.fly, "down1", "dself_other")
    down.over_y("down1")
    up.first("up0")
    step(
        ["dof", "dos", "do0"],
        lambda: pull(place, *get("dself", "dself_other"), (out_first, out_second, w_out)),
        "dself",
        "dself_other",
        "dcross",
        "dcq",
    )
    store["dcross_other"] = over_core(store["dcross"])
    store["dcq_other"] = over_core(store["dcq"][:, 512:])
    d_pair = jnp.stack(get("dck", "dcv"), axis=1)
    store["pair_kept"] = d_pair[:2]
    store["pair_fly"] = over_core(d_pair[2:])
    step(
        ["dqf", "dkf", "dvf"],
        lambda: self_back(limit, qf, kf, vf, store["of"], store["dof"], lse_f),
        "dof",
    )
    order("dcross_other", "dcq_other", "pair_fly", "pair_kept")
    pair_sum = lower(store["pair_kept"] + store["pair_fly"])
    store["pair"] = pair_sum[0]
    store["pair_other"] = cross_order(pair_sum[1])
    step(
        ["dqs", "dks", "dvs"],
        lambda: self_back(limit, qs, ks, vs, store["o_s"], store["dos"], lse_s),
        "dos",
    )
    up.second()
    step(["down0"], lambda: down_grad(store["g0"], dout, dout_other, ROUND), "g0")
    yp = ("dqf", "dkf", "dvf", "dqs", "dks", "dvs")
    step(["qkv1"], lambda: qkv_grad(place, h1, get(*yp), ROUND), "dqs")
    order(down.fly, "qkv1")
    qkv.over_y("qkv1")
    down.first("down0")
    up.far()

    def query(g):
        return query_grad(place, g, h2, *get("h2_other", "dcq", "dcq_other"), ROUND)

    def outof(g, *o):
        return outputs_grad(
            place, g, get(*o), *get("dself", "dself_other"), ca,
            *get("ca_other", "dcross", "dcross_other"), ROUND,
        )

    step(["query1"], lambda: query(1), "dcq_other", "h2_other")
    step(["outs1"], lambda: outof(1, "of", "o_s"), "dcross_other", "ca_other")
    step(
        ["dq0", "dk0", "dv0"],
        lambda: self_back(limit, q0, k0, v0, store["o0"], store["do0"], lse0),
        "do0",
    )
    order(qkv.fly, "outs1", "query1")
    outs.over_y("outs1")
    store["query_fly"] = over_y(store["query1"])
    store["pair_y"] = over_y(store["pair_other"])
    up.back()
    down.second()
    nine = ("dq0", "dk0", "dv0", *yp)
    weights = (w_qkv, qkv_first, qkv_second)
    step(["yo"], lambda: first_back(away, get(*nine), weights, ROUND), "dq0")
    store["yo_fly"] = over_core(store["yo"])
    step(["qkv0"], lambda: qkv_grad(place, h1, get("dq0", "dk0", "dv0"), ROUND), "dq0")
    qkv.first("qkv0")
    up.along()
    step(["query0"], lambda: query(0), "dcq")
    down.far()
    step(["outs0"], lambda: outof(0, "o0"), "dcross")
    outs.first("outs0")
    order("query0", "query_fly", "pair", "pair_y")
    other_text = lax.dynamic_index_in_dim(text_states, 1 - side, keepdims=False)
    texts = jnp.concatenate([text, other_text], axis=0)
    pairs = jnp.concatenate(get("pair", "pair_y"), axis=1)
    store["into0"] = jnp.concatenate(
        [
            lower(store["query0"].astype(FULL) + store["query_fly"].astype(FULL)),
            lower(tn(texts, pairs[0])),
            lower(tn(texts, pairs[1])),
        ],
        axis=0,
    )
    cross_in.first_alone("into0")
    qkv.second()
    step(["ym"], lambda: first_back(place, get(*nine), weights, FULL), "dq0")
    step(
        ["grad_frames", "first_sums"],
        lambda: frames_back(place, *get("ym", "yo_fly", "dx1"), frames, norm_gain),
        "ym",
        "yo_fly",
    )
    norms = Row("norms", store["sums"] + store["first_sums"], over_core)
    down.back()
    outs.second()
    up.end("grad_up")
    qkv.far()
    cross_in.second()
    norms.then(over_y)
    down.along()
    outs.far()
    norms.then(over_x)
    qkv.back()
    cross_in.far()
    text_part = 0.0
    for c in range(2):
        text_part = text_part + nt(pairs[c], w_cross_kv[c])
    text_mine, text_theirs = text_part[:64], text_part[64:]
    text_rows = Row("texts", text_mine, lambda v: over_y(text_theirs))
    qkv.along()
    outs.back()
    norms.then(over_z)
    store["out_fly"] = over_core(out_o)
    text_rows.then(over_core)
    cross_in.back()
    outs.along()
    norms.then(lambda v: along_wide(v, Z_FAR))
    down.end("grad_down")
    order("texts_fly", "texts_kept")
    text_grad = lower(text_rows.total())
    text_away = over_y(text_grad)
    cross_in.along()
    order("out_fly", "x2")
    out_rows = lower(store["x2"] + out_m + store["out_fly"].astype(FULL))
    qkv.end("grad_qkv")
    outs.end("grad_outs")
    grad_text = ordered(text_grad[None], text_away[None], side)
    sums = norms.total()
    cross_in.end("grad_in")
    grad_in, grad_outs = get("grad_in", "grad_outs")
    return (
        out_rows,
        store["grad_frames"],
        grad_text,
        sums[0:6:2],
        sums[1:6:2],
        store["grad_qkv"].reshape(3, width, 256),
        grad_outs[:256],
        grad_in[:width],
        grad_in[width:].reshape(2, width, 256),
        grad_outs[256:],
        store["grad_up"],
        store["grad_down"],
    )


def solution(mesh):
    chips = dict(mesh.shape) == {"wide": 8, "narrow": 4}
    return jax.shard_map(
        chip_local if chips else general_local,
        mesh=mesh,
        in_specs=(
            P(("wide", "narrow"), None),
            P("wide", None, None),
            P("wide"),
            P(("wide", "narrow")),
            P(),
            P(),
            P(None, None, "narrow"),
            P("narrow", None),
            P(None, "narrow"),
            P(None, None, "narrow"),
            P("narrow", None),
            P(None, "narrow"),
            P("narrow", None),
            P(("wide", "narrow"), None),
        ),
        out_specs=(
            P(("wide", "narrow"), None),
            P(("wide", "narrow"), None),
            P("wide", None, None),
            P(),
            P(),
            P(None, None, "narrow"),
            P("narrow", None),
            P(None, "narrow"),
            P(None, None, "narrow"),
            P("narrow", None),
            P(None, "narrow"),
            P("narrow", None),
        ),
        check_vma=False,
    )
```

```python
import functools

import jax
import jax.numpy as jnp
from jax import lax
from jax.experimental import pallas as pl
from jax.experimental.pallas import tpu as pltpu
from jax.sharding import PartitionSpec as P

HEAD = 64


EPS = 1e-05
NEG = -1e30


def lower(values_in):
    return values_in.astype(jnp.bfloat16)


def product(left_side, right_side, transposed):
    if transposed:
        return lax.dot_general(
            left_side, right_side, (((1,), (1,)), ((), ())), preferred_element_type=jnp.float32
        )
    return jnp.dot(left_side, right_side, preferred_element_type=jnp.float32)


def outer_sum(left_side, right_side):
    return lax.dot_general(
        left_side, right_side, (((0,), (0,)), ((), ())), preferred_element_type=jnp.float32
    )


def normalize(values_in, gain_row, bias_row):
    row_mean = jnp.mean(values_in, axis=-1, keepdims=True)
    centered = values_in - row_mean
    inverse = lax.rsqrt(jnp.mean(centered * centered, axis=-1, keepdims=True) + EPS)
    scaled = centered * inverse
    return (scaled * gain_row + bias_row, scaled, inverse)


def normalize_back(upstream, scaled, inverse, gain_row):
    weighted = upstream * gain_row
    inner_mean = jnp.mean(weighted, axis=-1, keepdims=True)
    along_mean = jnp.mean(weighted * scaled, axis=-1, keepdims=True)
    grad_input = inverse * (weighted - inner_mean - scaled * along_mean)
    return (grad_input, jnp.sum(upstream * scaled, axis=0), jnp.sum(upstream, axis=0))


def gelu_parts(values_in):
    normal_cdf = 0.5 * (1.0 + jax.scipy.special.erf(values_in * 0.7071067811865476))
    normal_pdf = jnp.exp(-0.5 * values_in * values_in) * 0.3989422804014327
    return (values_in * normal_cdf, normal_cdf + values_in * normal_pdf)


def scores_of(query_part, key_part, valid):
    scores = jnp.einsum(
        "bhe,khe->hbk", query_part, key_part, preferred_element_type=jnp.float32
    ) * HEAD ** (-0.5)
    return jnp.where(valid, scores, NEG)


def attend(query_part, key_part, value_part, valid):
    scores = scores_of(query_part, key_part, valid)
    row_top = jnp.max(scores, axis=-1, keepdims=True)
    weights_exp = jnp.exp(scores - row_top)
    denominator = jnp.sum(weights_exp, axis=-1, keepdims=True)
    probability = weights_exp / denominator
    mixed = jnp.einsum(
        "hbk,khe->bhe", lower(probability), value_part, preferred_element_type=jnp.float32
    )
    return (lower(mixed), (row_top + jnp.log(denominator))[..., 0])


def attend_back(query_part, key_part, value_part, valid, summary, upstream):
    scores = scores_of(query_part, key_part, valid)
    probability = jnp.exp(scores - summary[..., None])
    pressure = jnp.einsum("bhe,khe->hbk", upstream, value_part, preferred_element_type=jnp.float32)
    grad_scores = lower(
        probability * (pressure - jnp.sum(probability * pressure, axis=-1, keepdims=True))
    )
    factor = HEAD ** (-0.5)
    grad_query = (
        jnp.einsum("hbk,khe->bhe", grad_scores, key_part, preferred_element_type=jnp.float32)
        * factor
    )
    grad_key = (
        jnp.einsum("hbk,bhe->khe", grad_scores, query_part, preferred_element_type=jnp.float32)
        * factor
    )
    grad_value = jnp.einsum(
        "hbk,bhe->khe", lower(probability), upstream, preferred_element_type=jnp.float32
    )
    return (grad_query, grad_key, grad_value)


def general_local(
    frames,
    text_states,
    lengths,
    loss_mask,
    norm_gain,
    norm_bias,
    w_qkv,
    w_out,
    w_cross_q,
    w_cross_kv,
    w_cross_out,
    w_up,
    w_down,
    cotangent,
):
    row_count = frames.shape[0]
    width = frames.shape[1]
    item_count = lengths.shape[0]
    span = row_count * lax.axis_size("narrow") // item_count
    half_span = span // 2
    inner_width = w_qkv.shape[2]
    head_count = inner_width // HEAD
    text_count = text_states.shape[1]
    full_rows = item_count * span
    places = jnp.arange(span, dtype=jnp.int32)

    def spread(shard_rows):
        return lax.all_gather(shard_rows, "narrow", axis=0, tiled=True)

    def collect(left_side, right_side, transposed):
        return lax.psum_scatter(
            product(
                lax.slice_in_dim(left_side, 0, lax.axis_size("narrow") * row_count, axis=0),
                right_side,
                transposed,
            ),
            "narrow",
            scatter_dimension=0,
            tiled=True,
        )

    def causal(block_index, item_limit):
        query_place = block_index * half_span + jnp.arange(half_span, dtype=jnp.int32)
        return (places[None, :] <= query_place[:, None]) & (places[None, :] < item_limit)

    frame_rows = frames.astype(jnp.float32)
    normed_one, scaled_one, inverse_one = normalize(frame_rows, norm_gain[0], norm_bias[0])
    first_input = spread(lower(normed_one))
    triple = lower(
        jnp.einsum("rd,cde->cre", first_input, w_qkv, preferred_element_type=jnp.float32)
    )
    triple = triple.reshape(3, item_count, span, head_count, HEAD)

    def self_item(packed):
        query_part, key_part, value_part, item_limit = packed
        mixed_list = []
        summary_list = []
        for block_index in range(2):
            mixed, summary = attend(
                query_part[block_index * half_span : (block_index + 1) * half_span],
                key_part,
                value_part,
                causal(block_index, item_limit),
            )
            mixed_list.append(mixed)
            summary_list.append(summary)
        return (jnp.concatenate(mixed_list, axis=0), jnp.stack(summary_list, axis=0))

    attended, self_summary = lax.map(self_item, (triple[0], triple[1], triple[2], lengths))
    attended_flat = attended.reshape(full_rows, inner_width)
    first_rows = frame_rows + collect(attended_flat, w_out, False)
    normed_two, scaled_two, inverse_two = normalize(first_rows, norm_gain[1], norm_bias[1])
    second_input = spread(lower(normed_two))
    cross_query = lower(product(second_input, w_cross_q, False)).reshape(
        item_count, span, head_count, HEAD
    )
    cross_pair = lower(
        jnp.einsum("ntd,cde->cnte", text_states, w_cross_kv, preferred_element_type=jnp.float32)
    )
    cross_pair = cross_pair.reshape(2, item_count, text_count, head_count, HEAD)

    def cross_item(packed):
        query_part, key_part, value_part = packed
        return attend(query_part, key_part, value_part, True)

    cross_mixed, cross_summary = lax.map(cross_item, (cross_query, cross_pair[0], cross_pair[1]))
    cross_flat = cross_mixed.reshape(full_rows, inner_width)
    second_rows = first_rows + collect(cross_flat, w_cross_out, False)
    normed_three, scaled_three, inverse_three = normalize(second_rows, norm_gain[2], norm_bias[2])
    upstream = cotangent.astype(jnp.float32) * loss_mask.astype(jnp.float32)[:, None]
    ffn_grad = lower(upstream)
    ffn_input = spread(lower(normed_three))
    hidden_pre = product(ffn_input, w_up, False)
    active, slope = gelu_parts(hidden_pre)
    active = lower(active)
    out_rows = second_rows + collect(active, w_down, False)
    ffn_full = spread(ffn_grad)
    grad_down = outer_sum(active, ffn_full)
    grad_hidden = lower(product(ffn_full, w_down, True) * slope)
    grad_up = outer_sum(ffn_input, grad_hidden)
    back_three = collect(grad_hidden, w_up, True)
    grad_up, grad_down = (grad_up, grad_down)
    grad_in_three, gain_three, bias_three = normalize_back(
        back_three, scaled_three, inverse_three, norm_gain[2]
    )
    grad_second = upstream + grad_in_three
    cross_full = spread(lower(grad_second))
    grad_cross_out = outer_sum(cross_flat, cross_full)
    cross_upstream = lower(product(cross_full, w_cross_out, True)).reshape(
        item_count, span, head_count, HEAD
    )

    def cross_back(packed):
        query_part, key_part, value_part, summary, upstream_item = packed
        return attend_back(query_part, key_part, value_part, True, summary, upstream_item)

    grad_cq, grad_ck, grad_cv = lax.map(
        cross_back, (cross_query, cross_pair[0], cross_pair[1], cross_summary, cross_upstream)
    )
    grad_cq = lower(grad_cq).reshape(full_rows, inner_width)
    grad_pair = lower(jnp.stack((grad_ck, grad_cv), axis=0)).reshape(
        2, item_count, text_count, inner_width
    )
    grad_cross_q = outer_sum(second_input, grad_cq)
    grad_cross_kv = jnp.einsum(
        "ntd,cnte->cde", text_states, grad_pair, preferred_element_type=jnp.float32
    )
    grad_cross_q, grad_cross_kv, grad_cross_out = (grad_cross_q, grad_cross_kv, grad_cross_out)
    text_partial = jnp.einsum(
        "cnte,cde->ntd", grad_pair, w_cross_kv, preferred_element_type=jnp.float32
    )
    grad_text = lower(lax.psum(text_partial, "narrow"))
    back_two = collect(grad_cq, w_cross_q, True)
    grad_in_two, gain_two, bias_two = normalize_back(
        back_two, scaled_two, inverse_two, norm_gain[1]
    )
    grad_first = grad_second + grad_in_two
    self_full = spread(lower(grad_first))
    grad_out = outer_sum(attended_flat, self_full)
    self_upstream = lower(product(self_full, w_out, True)).reshape(
        item_count, span, head_count, HEAD
    )

    def self_back(packed):
        query_part, key_part, value_part, item_limit, summary, upstream_item = packed
        query_list = []
        key_list = []
        value_list = []
        for block_index in range(2):
            lower_row = block_index * half_span
            grad_query, grad_key, grad_value = attend_back(
                query_part[lower_row : lower_row + half_span],
                key_part,
                value_part,
                causal(block_index, item_limit),
                summary[block_index],
                upstream_item[lower_row : lower_row + half_span],
            )
            query_list.append(grad_query)
            key_list.append(grad_key)
            value_list.append(grad_value)
        return (
            jnp.concatenate(query_list, axis=0),
            key_list[0] + key_list[1],
            value_list[0] + value_list[1],
        )

    grad_q, grad_k, grad_v = lax.map(
        self_back, (triple[0], triple[1], triple[2], lengths, self_summary, self_upstream)
    )
    grad_triple = lower(jnp.stack((grad_q, grad_k, grad_v), axis=0)).reshape(
        3, full_rows, inner_width
    )
    grad_qkv = jnp.einsum(
        "rd,cre->cde", first_input, grad_triple, preferred_element_type=jnp.float32
    )
    grad_qkv, grad_out = (grad_qkv, grad_out)
    merged = grad_triple.transpose(1, 0, 2).reshape(full_rows, 3 * inner_width)
    stacked_weights = w_qkv.transpose(0, 2, 1).reshape(3 * inner_width, width)
    back_one = collect(merged, stacked_weights, False)
    grad_in_one, gain_one, bias_one = normalize_back(
        back_one, scaled_one, inverse_one, norm_gain[0]
    )
    grad_frames = lower(grad_first + grad_in_one)
    gain_terms = jnp.stack((gain_one, gain_two, gain_three), axis=0)
    bias_terms = jnp.stack((bias_one, bias_two, bias_three), axis=0)
    grad_norm_gain, grad_norm_bias = lax.psum((gain_terms, bias_terms), ("wide", "narrow"))
    grad_qkv, grad_out, grad_cross_q, grad_cross_kv, grad_cross_out, grad_up, grad_down = lax.psum(
        (grad_qkv, grad_out, grad_cross_q, grad_cross_kv, grad_cross_out, grad_up, grad_down),
        "wide",
    )
    return (
        lower(out_rows),
        grad_frames,
        grad_text,
        grad_norm_gain,
        grad_norm_bias,
        grad_qkv,
        grad_out,
        grad_cross_q,
        grad_cross_kv,
        grad_cross_out,
        grad_up,
        grad_down,
    )


ROUND = jnp.bfloat16
FULL = jnp.float32
CORE_PAIRS = ((0, 1), (1, 0), (2, 3), (3, 2))
Y_PAIRS = ((0, 2), (2, 0), (1, 3), (3, 1))
X_PAIRS = tuple((i, i ^ 1) for i in range(8))
Z_INWARD = ((0, 2), (1, 3), (6, 4), (7, 5))
Z_MIDDLE = ((2, 4), (4, 2), (3, 5), (5, 3))
Z_OUTWARD = ((2, 0), (3, 1), (4, 6), (5, 7))
Z_NEAR = tuple((i, i ^ 2) for i in range(8))
Z_FAR = tuple((i, i ^ 4) for i in range(8))
MIB = 1 << 20


def nt(a, b):
    return lax.dot_general(a, b, (((1,), (1,)), ((), ())), preferred_element_type=FULL)


def nn(a, b):
    return lax.dot_general(a, b, (((1,), (0,)), ((), ())), preferred_element_type=FULL)


def tn(a, b):
    return lax.dot_general(a, b, (((0,), (0,)), ((), ())), preferred_element_type=FULL)


def shape(dims, kind):
    return jax.ShapeDtypeStruct(dims, kind)


def resident(dims):
    zeros = (0,) * len(dims)
    return pl.BlockSpec(dims, lambda i, s: zeros, pipeline_mode=pl.Buffered(1))


def rows_of(block, width):
    return pl.BlockSpec((block, width), lambda i, s: (i, 0))


def lasting(microseconds):
    flops = int(microseconds * 0.28 * 1.15e9)
    return pl.CostEstimate(flops=flops, bytes_accessed=1000, transcendentals=0)


def params(mib):
    return pltpu.CompilerParams(vmem_limit_bytes=mib * MIB)


def norm_parts(v):
    centered = v - jnp.mean(v, axis=-1, keepdims=True)
    inverse = lax.rsqrt(jnp.mean(centered * centered, axis=-1, keepdims=True) + EPS)
    return centered * inverse, inverse


def norm_pull(y, scaled, inverse, gain_row):
    weighted = y * gain_row
    inner = jnp.mean(weighted, axis=-1, keepdims=True)
    along = jnp.mean(weighted * scaled, axis=-1, keepdims=True)
    return inverse * (weighted - inner - scaled * along)


def first_project_kernel(
    place_ref, mine_ref, other_ref, gain_ref, bias_ref, weight_ref, h_ref, *out_refs
):
    half = pl.program_id(0)

    def run(source):
        for start in range(0, source.shape[0], 208):
            part = slice(start, start + 208)
            scaled, _ = norm_parts(source[part, :].astype(FULL))
            h = lower(scaled * gain_ref[0:1, :] + bias_ref[0:1, :])
            h_ref[part, :] = h
            for c, out_ref in enumerate(out_refs):
                out_ref[part, :] = lower(nn(h, weight_ref[c]))

    @pl.when(half == 0)
    def _():
        run(mine_ref)

    @pl.when(half == 1)
    def _():
        run(other_ref)


def first_project(place, mine, other, gains, biases, weights):
    rows, depth = mine.shape
    count, _, wide = weights.shape
    out = pl.BlockSpec((rows, wide), lambda i, s: ((i + s[0]) % 2, 0))
    return pl.pallas_call(
        first_project_kernel,
        grid_spec=pltpu.PrefetchScalarGridSpec(
            num_scalar_prefetch=1,
            grid=(2,),
            in_specs=[resident(a.shape) for a in (mine, other, gains, biases, weights)],
            out_specs=[rows_of(rows, depth)] + [out] * count,
        ),
        out_shape=[shape((2 * rows, depth), ROUND)] + [shape((2 * rows, wide), ROUND)] * count,
        compiler_params=params(40),
        cost_estimate=lasting(5),
        name="first_project",
    )(place, mine, other, gains, biases, weights)


def project_kernel(place_ref, h_ref, weight_ref, *out_refs):
    count = len(out_refs)
    wide = weight_ref.shape[2]
    weights = jnp.concatenate([weight_ref[c] for c in range(count)], axis=1)
    for start in range(0, h_ref.shape[0], 416):
        part = slice(start, start + 416)
        result = lower(nn(h_ref[part, :], weights))
        for c, out_ref in enumerate(out_refs):
            out_ref[part, :] = result[:, c * wide : (c + 1) * wide]


def project(place, h, weights):
    rows, depth = h.shape[0] // 2, h.shape[1]
    count, _, wide = weights.shape
    out = pl.BlockSpec((rows, wide), lambda i, s: ((i + s[0]) % 2, 0))
    return pl.pallas_call(
        project_kernel,
        grid_spec=pltpu.PrefetchScalarGridSpec(
            num_scalar_prefetch=1,
            grid=(2,),
            in_specs=[rows_of(rows, depth), resident(weights.shape)],
            out_specs=[out] * count,
        ),
        out_shape=[shape((2 * rows, wide), ROUND)] * count,
        compiler_params=params(40),
        cost_estimate=lasting(4),
        name="project",
    )(place, h, weights)


def pull_kernel(place_ref, mine_ref, other_ref, *refs):
    half = pl.program_id(0)
    count = len(refs) // 2

    def run(source):
        for weight_ref, out_ref in zip(refs[:count], refs[count:]):
            out_ref[...] = lower(nt(source[...], weight_ref[...]))

    @pl.when(half == 0)
    def _():
        run(mine_ref)

    @pl.when(half == 1)
    def _():
        run(other_ref)


def pull(place, mine, other, weights):
    rows = mine.shape[0]
    return pl.pallas_call(
        pull_kernel,
        grid_spec=pltpu.PrefetchScalarGridSpec(
            num_scalar_prefetch=1,
            grid=(2,),
            in_specs=[resident(a.shape) for a in (mine, other, *weights)],
            out_specs=[
                pl.BlockSpec((rows, a.shape[0]), lambda i, s: ((i + s[0]) % 2, 0)) for a in weights
            ],
        ),
        out_shape=[shape((2 * rows, a.shape[0]), ROUND) for a in weights],
        compiler_params=params(32),
        cost_estimate=lasting(3.5),
        name="pull",
    )(place, mine, other, *weights)


def blocks_of(span, block):
    return [(start, min(block, span - start)) for start in range(0, span, block)]


def self_forward_kernel(
    limit_ref, q_ref, k_ref, v_ref, o_ref, lse_ref, *, span, floor, block
):
    limit = limit_ref[0]
    lane = lax.broadcasted_iota(jnp.int32, (1, 128), 1)
    row = lax.broadcasted_iota(jnp.int32, (128, 1), 0)
    zero = jnp.zeros((), ROUND)
    value_turned = v_ref[...].T
    for start, size in blocks_of(span, block):
        end = start + size
        mixed_list = []
        for h in range(2):
            own_lanes = (lane < HEAD) if h == 0 else (lane >= HEAD)
            query = jnp.where(own_lanes, q_ref[start:end, :] * HEAD ** (-0.5), zero)
            parts = []
            for low in range(0, end, block):
                high = min(low + block, end)
                scores = nt(k_ref[low:high, :], query)
                if low == start:
                    key = lax.broadcasted_iota(jnp.int32, (size, size), 0)
                    valid = key <= lax.broadcasted_iota(jnp.int32, (size, size), 1)
                    if high > floor:
                        valid = valid & (key + low < limit)
                    scores = jnp.where(valid, scores, NEG)
                elif high > floor:
                    key = lax.broadcasted_iota(jnp.int32, (high - low, 1), 0)
                    scores = jnp.where(key + low < limit, scores, NEG)
                parts.append((low, high, scores))
            top = functools.reduce(
                jnp.maximum, [jnp.max(s, axis=0, keepdims=True) for _, _, s in parts]
            )
            total = 0.0
            mixed = 0.0
            for low, high, scores in parts:
                weights_exp = jnp.exp(scores - top)
                total = total + jnp.sum(weights_exp, axis=0, keepdims=True)
                mixed = mixed + nn(value_turned[:, low:high], lower(weights_exp))
            mixed_list.append(mixed / total)
            lse_ref[0, h : h + 1, start:end] = top + jnp.log(total)
        o_ref[start:end, :] = lower(jnp.where(row < HEAD, mixed_list[0], mixed_list[1]).T)


def self_forward(limit, q, k, v):
    span, wide = q.shape
    pairs = wide // 128
    floor = (span - span // 8 + 1) // 128 * 128
    pair = pl.BlockSpec((span, 128), lambda p, s: (0, p))
    return pl.pallas_call(
        functools.partial(self_forward_kernel, span=span, floor=floor, block=512),
        grid_spec=pltpu.PrefetchScalarGridSpec(
            num_scalar_prefetch=1,
            grid=(pairs,),
            in_specs=[pair] * 3,
            out_specs=[pair, pl.BlockSpec((1, 8, span), lambda p, s: (p, 0, 0))],
        ),
        out_shape=[shape((span, wide), ROUND), shape((pairs, 8, span), FULL)],
        compiler_params=params(56),
        cost_estimate=lasting(7.3 * pairs),
        name="self_forward",
    )(limit, q, k, v)


def self_back_kernel(
    limit_ref, q_ref, k_ref, v_ref, o_ref, do_ref, lse_ref, dq_ref, dk_ref, dv_ref, dqt,
    *, span, floor, block
):
    limit = limit_ref[0]
    lane = lax.broadcasted_iota(jnp.int32, (1, 128), 1)
    row = lax.broadcasted_iota(jnp.int32, (128, 1), 0)
    zero = jnp.zeros((), ROUND)
    factor = HEAD ** (-0.5)
    product_rows = do_ref[...].astype(FULL) * o_ref[...].astype(FULL)
    high = lower(product_rows)
    rest = lower(product_rows - high.astype(FULL))
    pick = lower(
        jnp.concatenate(
            [
                jnp.where(lane < HEAD, 1.0, 0.0),
                jnp.where(lane >= HEAD, 1.0, 0.0),
                jnp.zeros((6, 128), FULL),
            ],
            axis=0,
        )
    )
    delta = nt(pick, high) + nt(pick, rest)
    for start, size in blocks_of(span, block):
        end = start + size
        key = k_ref[start:end, :]
        value = v_ref[start:end, :]
        key_turned = key.T
        dk = 0.0
        dv = 0.0
        dq_add = 0.0
        for h in range(2):
            own_lanes = (lane < HEAD) if h == 0 else (lane >= HEAD)
            own_rows = (row < HEAD) if h == 0 else (row >= HEAD)
            query = jnp.where(own_lanes, q_ref[start:, :] * factor, zero)
            pulled = jnp.where(own_lanes, do_ref[start:, :], zero)
            probability = jnp.exp(nt(key, query) - lse_ref[0, h : h + 1, start:])
            pressure = nt(value, pulled)
            below = lax.broadcasted_iota(jnp.int32, (size, size), 0)
            across = lax.broadcasted_iota(jnp.int32, (size, size), 1)
            corner = jnp.where(below <= across, probability[:, :size], 0.0)
            if end < span:
                probability = jnp.concatenate([corner, probability[:, size:]], axis=1)
            else:
                probability = corner
            if end > floor:
                place = lax.broadcasted_iota(jnp.int32, (size, 1), 0) + start
                probability = jnp.where(place < limit, probability, 0.0)
            grad_scores = lower(probability * (pressure - delta[h : h + 1, start:]))
            dv = dv + nn(lower(probability), pulled)
            dk = dk + nn(grad_scores, query)
            dq_add = dq_add + nn(jnp.where(own_rows, key_turned, zero), grad_scores)
        dk_ref[start:end, :] = lower(dk)
        dv_ref[start:end, :] = lower(dv)
        if start == 0:
            dqt[...] = dq_add
        else:
            dqt[:, start:] += dq_add
    dq_ref[...] = lower(dqt[...].T * factor)


def self_back(limit, q, k, v, o, do, lse):
    span, wide = q.shape
    pairs = wide // 128
    floor = (span - span // 8 + 1) // 128 * 128
    pair = pl.BlockSpec((span, 128), lambda p, s: (0, p))
    return pl.pallas_call(
        functools.partial(self_back_kernel, span=span, floor=floor, block=256),
        grid_spec=pltpu.PrefetchScalarGridSpec(
            num_scalar_prefetch=1,
            grid=(pairs,),
            in_specs=[pair] * 5 + [pl.BlockSpec((1, 8, span), lambda p, s: (p, 0, 0))],
            out_specs=[pair] * 3,
            scratch_shapes=[pltpu.VMEM((128, span), FULL)],
        ),
        out_shape=[shape((span, wide), ROUND)] * 3,
        compiler_params=params(48),
        cost_estimate=lasting(7.00 * pairs),
        name="self_back",
    )(limit, q, k, v, o, do, lse)


def by_head(values_in, reduce, empty):
    lane = lax.broadcasted_iota(jnp.int32, (1, 128), 1)
    pieces = []
    for start in range(0, values_in.shape[1], 128):
        part = values_in[:, start : start + 128]
        first = reduce(jnp.where(lane < HEAD, part, empty), axis=1, keepdims=True)
        second = reduce(jnp.where(lane >= HEAD, part, empty), axis=1, keepdims=True)
        pieces.append(jnp.where(lane < HEAD, first, second))
    return jnp.concatenate(pieces, axis=1)


def cross_probability(query, keys):
    scores = nt(query * HEAD ** (-0.5), keys)
    weights_exp = jnp.exp(scores - by_head(scores, jnp.max, NEG))
    return weights_exp / by_head(weights_exp, jnp.sum, 0.0)


def in_groups(refs, axis):
    for at in (0, 3):
        yield refs[at][...]
        yield jnp.concatenate([refs[at + 1][...], refs[at + 2][...]], axis=axis)


def middle_forward_kernel(place_ref, frame_ref, *refs):
    mixed, wo, wq, wc = refs[0:6], refs[6:12], refs[12:18], refs[18:24]
    ck_ref, cv_ref, gain_ref, bias_ref = refs[24:28]
    x1_ref, x2_ref, h2_ref, cq_ref, ca_ref, h3_ref = refs[28:]
    x1 = frame_ref[...].astype(FULL)
    for o, weight in zip(in_groups(mixed, 1), in_groups(wo, 0)):
        x1 = x1 + nn(o, weight)
    x1_ref[...] = x1
    scaled, _ = norm_parts(x1)
    h2 = lower(scaled * gain_ref[1:2, :] + bias_ref[1:2, :])
    h2_ref[...] = h2
    for g, weight in enumerate(in_groups(wq, 1)):
        lanes = slice(g * 256, (g + 1) * 256)
        cq = lower(nn(h2, weight))
        cq_ref[:, lanes] = cq
        probability = cross_probability(cq, ck_ref[g])
        ca_ref[:, lanes] = lower(nn(lower(probability), cv_ref[g]))
    crossed = 0.0
    for g, weight in enumerate(in_groups(wc, 0)):
        crossed = crossed + nn(ca_ref[:, g * 256 : (g + 1) * 256], weight)
    x2 = x1_ref[...] + crossed
    x2_ref[...] = x2
    scaled, _ = norm_parts(x2)
    h3_ref[...] = lower(scaled * gain_ref[2:3, :] + bias_ref[2:3, :])


def middle_forward(place, frames, attended, received, wo, wq, wc, ck, cv, gains, biases):
    rows, width = frames.shape
    block = 416
    steps = rows // block
    wide = rows_of(block, width)
    whole = (*wo, *wq, *wc, ck, cv, gains, biases)
    return pl.pallas_call(
        middle_forward_kernel,
        grid_spec=pltpu.PrefetchScalarGridSpec(
            num_scalar_prefetch=1,
            grid=(steps,),
            in_specs=[wide]
            + [
                pl.BlockSpec((block, a.shape[1]), lambda i, s: (s[0] * steps + i, 0))
                for a in attended
            ]
            + [rows_of(block, a.shape[1]) for a in received]
            + [resident(a.shape) for a in whole],
            out_specs=[wide] * 6,
        ),
        out_shape=[shape((rows, width), FULL)] * 2 + [shape((rows, width), ROUND)] * 4,
        compiler_params=params(56),
        cost_estimate=lasting(22),
        name="middle_forward",
    )(place, frames, *attended, *received, *whole)


def keys_kernel(text_ref, weight_ref, out_ref):
    for item in range(2):
        for c in range(2):
            out_ref[item, c] = lower(nn(text_ref[item], weight_ref[c]))


def keys_of(text_states, weights):
    items, states, _ = text_states.shape
    return pl.pallas_call(
        keys_kernel,
        out_shape=shape((items, 2, states, weights.shape[2]), ROUND),
        compiler_params=params(24),
        cost_estimate=lasting(2),
        name="keys_of",
    )(text_states, weights)


def feed_kernel(place_ref, h_ref, d_ref, *refs, parts, carried):
    ups, downs = refs[:parts], refs[parts : 2 * parts]
    before = refs[2 * parts : 2 * parts + carried]
    g_ref, du_ref, out_ref, y_ref = refs[-4:]
    h = h_ref[...]
    d = d_ref[...]
    out = 0.0
    y = 0.0
    for n, (up_ref, down_ref) in enumerate(zip(ups, downs)):
        size = down_ref.shape[0]
        if parts == 1:
            lanes = slice(0, size)
        else:
            column = place_ref[2]
            which = column if n == 0 else 1 - column
            lanes = pl.ds(pl.multiple_of(which * size, 128), size)
        u = nn(h, up_ref[...])
        active, slope = gelu_parts(u)
        g = lower(active)
        g_ref[:, lanes] = g
        du = lower(nt(d, down_ref[...]) * slope)
        du_ref[:, lanes] = du
        out = out + nn(g, down_ref[...])
        y = y + nt(du, up_ref[...])
    if carried:
        out = before[0][...] + out
        y = before[1][...] + y
    out_ref[...] = out.astype(out_ref.dtype)
    y_ref[...] = y.astype(y_ref.dtype)


def feed(place, h, d, ups, downs, kind, half, before=(), shared=()):
    rows, width = h.shape
    block = 416
    steps = rows // block
    hidden = sum(a.shape[0] for a in downs)
    wide = rows_of(block, width)
    kept = pl.BlockSpec((block, hidden), lambda i, s: (i + half * steps, 0))
    there = pl.BlockSpec(memory_space=pl.ANY)
    parts = len(ups)
    at = 3 + 2 * parts + len(before)
    return pl.pallas_call(
        functools.partial(feed_kernel, parts=parts, carried=len(before)),
        grid_spec=pltpu.PrefetchScalarGridSpec(
            num_scalar_prefetch=1,
            grid=(steps,),
            in_specs=[wide, wide]
            + [resident(a.shape) for a in (*ups, *downs)]
            + [wide] * len(before)
            + [there] * len(shared),
            out_specs=[kept, kept, wide, wide],
        ),
        out_shape=[shape((2 * rows, hidden), ROUND)] * 2 + [shape((rows, width), kind)] * 2,
        input_output_aliases={at: 0, at + 1: 1} if shared else {},
        compiler_params=params(58),
        cost_estimate=lasting(13),
        name="feed",
    )(place, h, d, *ups, *downs, *before, *shared)


def up_grad_kernel(mine_ref, other_ref, du_ref, out_ref):
    rows = mine_ref.shape[0]
    total = tn(mine_ref[...], du_ref[:rows, :]) + tn(other_ref[...], du_ref[rows:, :])
    out_ref[...] = total.astype(out_ref.dtype)


def up_grad(mine, other, du, kind):
    rows, width = mine.shape
    hidden = du.shape[1]
    tile = 512
    whole = pl.BlockSpec((rows, width), lambda i: (0, 0), pipeline_mode=pl.Buffered(1))
    return pl.pallas_call(
        up_grad_kernel,
        grid=(hidden // tile,),
        in_specs=[whole, whole, pl.BlockSpec((2 * rows, tile), lambda i: (0, i))],
        out_specs=pl.BlockSpec((width, tile), lambda i: (0, i)),
        out_shape=shape((width, hidden), kind),
        compiler_params=params(48),
        cost_estimate=lasting(5.00),
        name="up_grad",
    )(mine, other, du)


def down_grad_kernel(g_ref, mine_ref, other_ref, out_ref):
    rows = mine_ref.shape[0]
    total = tn(g_ref[:rows, :], mine_ref[...]) + tn(g_ref[rows:, :], other_ref[...])
    out_ref[...] = total.astype(out_ref.dtype)


def down_grad(g, mine, other, kind):
    rows, width = mine.shape
    hidden = g.shape[1]
    tile = 512
    whole = pl.BlockSpec((rows, width), lambda i: (0, 0), pipeline_mode=pl.Buffered(1))
    return pl.pallas_call(
        down_grad_kernel,
        grid=(hidden // tile,),
        in_specs=[pl.BlockSpec((2 * rows, tile), lambda i: (0, i)), whole, whole],
        out_specs=pl.BlockSpec((tile, width), lambda i: (i, 0)),
        out_shape=shape((hidden, width), kind),
        compiler_params=params(48),
        cost_estimate=lasting(5.00),
        name="down_grad",
    )(g, mine, other)


def qkv_grad_kernel(place_ref, h_ref, *refs):
    out_ref = refs[-1]
    rows, width = h_ref.shape[0] // 2, h_ref.shape[1]
    core, near = place_ref[0], place_ref[1]
    halves = (len(refs) - 1) // 3
    total = [0.0] * 3
    for half in range(2):
        turned = h_ref[half * rows : (half + 1) * rows, :].T
        at = pl.multiple_of((core if half == 0 else 1 - core) * rows, 16)
        for c in range(3):
            parts = [refs[3 * n + c][pl.ds(at, rows), :] for n in range(halves)]
            grads = parts[0] if halves == 1 else jnp.concatenate(parts, axis=1)
            total[c] = total[c] + nn(turned, grads)
    for c in range(3):
        part = slice(c * width, (c + 1) * width)
        value = total[c].astype(out_ref.dtype)
        if halves == 1:
            out_ref[part, :] = value
        else:
            out_ref[part, pl.ds(pl.multiple_of(near * 128, 128), 128)] = value[:, :128]
            out_ref[part, pl.ds(pl.multiple_of((1 - near) * 128, 128), 128)] = value[:, 128:]


def qkv_grad(place, h, grads, kind):
    width = h.shape[1]
    return pl.pallas_call(
        qkv_grad_kernel,
        grid_spec=pltpu.PrefetchScalarGridSpec(
            num_scalar_prefetch=1,
            grid=(1,),
            in_specs=[resident(a.shape) for a in (h, *grads)],
            out_specs=resident((3 * width, 256)),
        ),
        out_shape=shape((3 * width, 256), kind),
        compiler_params=params(48),
        cost_estimate=lasting(5.00),
        name="qkv_grad",
    )(place, h, *grads)


def query_grad_kernel(place_ref, mine_ref, other_ref, dm_ref, do_ref, out_ref, *, split):
    column = place_ref[2]
    total = tn(mine_ref[...], dm_ref[...]) + tn(other_ref[...], do_ref[...])
    value = total.astype(out_ref.dtype)
    if split:
        out_ref[:, pl.ds(pl.multiple_of(column * 128, 128), 128)] = value[:, :128]
        out_ref[:, pl.ds(pl.multiple_of((1 - column) * 128, 128), 128)] = value[:, 128:]
    else:
        out_ref[...] = value


def query_grad(place, group, mine, other, d_mine, d_other, kind):
    rows, width = mine.shape
    lanes = pl.BlockSpec((rows, 256), lambda i, s: (0, group))
    return pl.pallas_call(
        functools.partial(query_grad_kernel, split=group == 1),
        grid_spec=pltpu.PrefetchScalarGridSpec(
            num_scalar_prefetch=1,
            grid=(1,),
            in_specs=[resident(mine.shape), resident(other.shape), lanes, lanes],
            out_specs=resident((width, 256)),
        ),
        out_shape=shape((width, 256), kind),
        compiler_params=params(48),
        cost_estimate=lasting(2.86),
        name="query_grad",
    )(place, mine, other, d_mine, d_other)


def outputs_grad_kernel(place_ref, *refs, count):
    o_refs = refs[:count]
    sm_ref, so_ref, am_ref, ao_ref, cm_ref, co_ref, out_ref = refs[count:]
    rows = sm_ref.shape[0]
    core, near, column = place_ref[0], place_ref[1], place_ref[2]
    mine_at = pl.ds(pl.multiple_of(core * rows, 16), rows)
    other_at = pl.ds(pl.multiple_of((1 - core) * rows, 16), rows)
    for n, o_ref in enumerate(o_refs):
        total = tn(o_ref[mine_at, :], sm_ref[...]) + tn(o_ref[other_at, :], so_ref[...])
        if count == 1:
            at = slice(0, 256)
        else:
            at = pl.ds(pl.multiple_of((near if n == 0 else 1 - near) * 128, 128), 128)
        out_ref[at, :] = total.astype(out_ref.dtype)
    total = tn(am_ref[...], cm_ref[...]) + tn(ao_ref[...], co_ref[...])
    value = total.astype(out_ref.dtype)
    if count == 1:
        out_ref[256:, :] = value
    else:
        out_ref[pl.ds(pl.multiple_of(256 + column * 128, 128), 128), :] = value[:128, :]
        out_ref[pl.ds(pl.multiple_of(384 - column * 128, 128), 128), :] = value[128:, :]


def outputs_grad(place, group, o, dself, dself_other, ca, ca_other, dcross, dcross_other, kind):
    rows, width = dself.shape
    lanes = pl.BlockSpec((rows, 256), lambda i, s: (0, group))
    whole = resident((rows, width))
    return pl.pallas_call(
        functools.partial(outputs_grad_kernel, count=len(o)),
        grid_spec=pltpu.PrefetchScalarGridSpec(
            num_scalar_prefetch=1,
            grid=(1,),
            in_specs=[resident(a.shape) for a in o] + [whole, whole, lanes, lanes, whole, whole],
            out_specs=resident((512, width)),
        ),
        out_shape=shape((512, width), kind),
        compiler_params=params(48),
        cost_estimate=lasting(4.29),
        name="outputs_grad",
    )(place, *o, dself, dself_other, ca, ca_other, dcross, dcross_other)


def middle_back_kernel(place_ref, ym_ref, yr_ref, x1_ref, x2_ref, d_ref, cq_ref, *refs):
    wq, wc = refs[0:6], refs[6:12]
    ck_ref, cv_ref, gain_ref = refs[12:15]
    dx1_ref, dself_ref, dcross_ref, dcq_ref, dck_ref, dcv_ref, sums_ref = refs[15:22]
    dck_all, dcv_all = refs[22:]
    step = pl.program_id(0)

    @pl.when(step == 0)
    def _():
        dck_all[...] = jnp.zeros_like(dck_all)
        dcv_all[...] = jnp.zeros_like(dcv_all)
        sums_ref[...] = jnp.zeros_like(sums_ref)

    y3 = ym_ref[...] + yr_ref[...].astype(FULL)
    scaled, inverse = norm_parts(x2_ref[...])
    sums_ref[4:5, :] += jnp.sum(y3 * scaled, axis=0, keepdims=True)
    sums_ref[5:6, :] += jnp.sum(y3, axis=0, keepdims=True)
    dx2 = d_ref[...].astype(FULL) + norm_pull(y3, scaled, inverse, gain_ref[2:3, :])
    dx1_ref[...] = dx2
    dcross = lower(dx2)
    dcross_ref[...] = dcross
    for g, weight in enumerate(in_groups(wc, 0)):
        lanes = slice(g * 256, (g + 1) * 256)
        dcatt = lower(nt(dcross, weight))
        keys = ck_ref[g]
        cq = cq_ref[:, lanes]
        probability = cross_probability(cq, keys)
        weighed = nt(dcatt, cv_ref[g])
        inner = by_head(probability * weighed, jnp.sum, 0.0)
        dcs = lower(probability * (weighed - inner))
        dcq_ref[:, lanes] = lower(nn(dcs, keys) * HEAD ** (-0.5))
        dck_all[g] += tn(dcs, cq * HEAD ** (-0.5))
        dcv_all[g] += tn(lower(probability), dcatt)
    y2 = 0.0
    for g, weight in enumerate(in_groups(wq, 1)):
        y2 = y2 + nt(dcq_ref[:, g * 256 : (g + 1) * 256], weight)
    scaled, inverse = norm_parts(x1_ref[...])
    sums_ref[2:3, :] += jnp.sum(y2 * scaled, axis=0, keepdims=True)
    sums_ref[3:4, :] += jnp.sum(y2, axis=0, keepdims=True)
    dx1 = dx1_ref[...] + norm_pull(y2, scaled, inverse, gain_ref[1:2, :])
    dx1_ref[...] = dx1
    dself_ref[...] = lower(dx1)

    @pl.when(step == pl.num_programs(0) - 1)
    def _():
        for every, result in ((dck_all, dck_ref), (dcv_all, dcv_ref)):
            for g in range(4):
                total = 0.0
                for h in range(4):
                    lane = lax.broadcasted_iota(jnp.int32, (1, 256), 1) // HEAD
                    total = total + jnp.where(lane == h, every[g, h * 64 : (h + 1) * 64, :], 0.0)
                result[g] = total


def middle_back(place, ym, yr, x1, x2, d, cq, wq, wc, ck, cv, gains):
    rows, width = x1.shape
    block = 416
    wide = rows_of(block, width)
    small = pl.BlockSpec((4, 64, 256), lambda i, s: (0, 0, 0))
    whole = (*wq, *wc, ck, cv, gains)
    return pl.pallas_call(
        middle_back_kernel,
        grid_spec=pltpu.PrefetchScalarGridSpec(
            num_scalar_prefetch=1,
            grid=(rows // block,),
            in_specs=[wide] * 6 + [resident(a.shape) for a in whole],
            out_specs=[wide] * 4 + [small, small, pl.BlockSpec((8, width), lambda i, s: (0, 0))],
            scratch_shapes=[pltpu.VMEM((4, 256, 256), FULL)] * 2,
        ),
        out_shape=[shape((rows, width), FULL)]
        + [shape((rows, width), ROUND)] * 3
        + [shape((4, 64, 256), FULL)] * 2
        + [shape((8, width), FULL)],
        compiler_params=params(56),
        cost_estimate=lasting(24),
        name="middle_back",
    )(place, ym, yr, x1, x2, d, cq, *whole)


def first_back_kernel(place_ref, *refs):
    y_ref = refs[-1]
    y = 0.0
    for n in range(3):
        for c in range(3):
            y = y + nt(refs[3 * n + c][...], refs[9 + n][c])
    y_ref[...] = y.astype(y_ref.dtype)


def first_back(place, grads, weights, kind):
    span = grads[0].shape[0]
    rows = span // 2
    width = weights[0].shape[1]
    block = 416
    steps = rows // block
    return pl.pallas_call(
        first_back_kernel,
        grid_spec=pltpu.PrefetchScalarGridSpec(
            num_scalar_prefetch=1,
            grid=(steps,),
            in_specs=[
                pl.BlockSpec((block, a.shape[1]), lambda i, s: (s[0] * steps + i, 0))
                for a in grads
            ]
            + [resident(a.shape) for a in weights],
            out_specs=rows_of(block, width),
        ),
        out_shape=shape((rows, width), kind),
        compiler_params=params(40),
        cost_estimate=lasting(3.57),
        name="first_back",
    )(place, *grads, *weights)


def frames_back_kernel(place_ref, ym_ref, yr_ref, dx1_ref, frame_ref, gain_ref, out_ref, sums_ref):
    @pl.when(pl.program_id(0) == 0)
    def _():
        sums_ref[...] = jnp.zeros_like(sums_ref)

    y = ym_ref[...] + yr_ref[...].astype(FULL)
    scaled, inverse = norm_parts(frame_ref[...].astype(FULL))
    sums_ref[0:1, :] += jnp.sum(y * scaled, axis=0, keepdims=True)
    sums_ref[1:2, :] += jnp.sum(y, axis=0, keepdims=True)
    out_ref[...] = lower(dx1_ref[...] + norm_pull(y, scaled, inverse, gain_ref[0:1, :]))


def frames_back(place, ym, yr, dx1, frames, gains):
    rows, width = dx1.shape
    block = 208
    wide = rows_of(block, width)
    return pl.pallas_call(
        frames_back_kernel,
        grid_spec=pltpu.PrefetchScalarGridSpec(
            num_scalar_prefetch=1,
            grid=(rows // block,),
            in_specs=[wide] * 4 + [resident(gains.shape)],
            out_specs=[wide, pl.BlockSpec((8, width), lambda i, s: (0, 0))],
        ),
        out_shape=[shape((rows, width), ROUND), shape((8, width), FULL)],
        compiler_params=params(24),
        cost_estimate=lasting(4.29),
        name="frames_back",
    )(place, ym, yr, dx1, frames, gains)


def chip_local(
    frames, text_states, lengths, loss_mask, norm_gain, norm_bias, w_qkv, w_out, w_cross_q,
    w_cross_kv, w_cross_out, w_up, w_down, cotangent,
):
    at = lax.axis_index("narrow")
    core = at % 2
    side = at // 2
    column = lax.axis_index("wide") % 2
    layer = lax.axis_index("wide") // 2
    near = layer % 2
    place = jnp.stack([core, near, column]).astype(jnp.int32)
    away = jnp.stack([1 - core, near, column]).astype(jnp.int32)
    limit = lax.dynamic_slice(lengths, (side,), (1,))
    rows, width = frames.shape
    join = lax.optimization_barrier

    def over_core(v):
        return lax.ppermute(v, "narrow", CORE_PAIRS)

    def over_y(v):
        return lax.ppermute(v, "narrow", Y_PAIRS)

    def along_wide(v, pairs):
        return lax.ppermute(v, "wide", pairs)

    def half_of(v, which, axis=0):
        half = v.shape[axis] // 2
        return lax.dynamic_slice_in_dim(v, which * half, half, axis=axis)

    def ordered(first, second, which):
        return jnp.where(
            which == 0,
            jnp.concatenate([first, second], axis=0),
            jnp.concatenate([second, first], axis=0),
        )

    def over_z(v):
        return along_wide(v, Z_NEAR)

    def over_x(v):
        return along_wide(v, X_PAIRS)

    def away_rows(v):
        return half_of(v, 1 - core)

    def cross_order(v):
        return jnp.where(column == 0, v, jnp.concatenate([v[..., 128:], v[..., :128]], axis=-1))

    qkv_first = over_y(half_of(w_qkv, near, 2))
    frames_other = over_core(frames)
    h1, q0, k0, v0 = first_project(place, frames, frames_other, norm_gain, norm_bias, w_qkv)
    q0, qkv_first, w_out, w_cross_q, w_cross_out, cotangent = join(
        (q0, qkv_first, w_out, w_cross_q, w_cross_out, cotangent)
    )

    qkv_second = over_z(qkv_first)
    out_first = over_y(half_of(w_out, near))
    query_first = over_y(half_of(w_cross_q, column, 1))
    cross_out_first = over_y(half_of(w_cross_out, column))
    o0, lse0 = self_forward(limit, q0, k0, v0)
    qf, kf, vf = project(place, h1, qkv_first)
    out_other, query_other, cross_out_other = map(over_core, (w_out, w_cross_q, w_cross_out))
    qf, o0, out_first, query_first, cross_out_first, w_up, w_down, *core_got = join(
        (qf, o0, out_first, query_first, cross_out_first, w_up, w_down)
        + (out_other, query_other, cross_out_other)
    )

    out_other, query_other, cross_out_other = core_got
    out_second = over_z(out_first)
    query_second = over_x(query_first)
    cross_out_second = over_x(cross_out_first)
    up_first = over_y(half_of(w_up, column, 1))
    down_sent = half_of(w_down, column)
    o0_other = over_core(away_rows(o0))
    keys = keys_of(text_states, w_cross_kv)
    own_keys = lax.dynamic_index_in_dim(keys, side, keepdims=False)
    keys_y = over_y(lax.dynamic_index_in_dim(keys, 1 - side, keepdims=False))
    of, lse_f = self_forward(limit, qf, kf, vf)
    of, qkv_second, keys_y, o0_other = join((of, qkv_second, keys_y, o0_other))

    qs, ks, vs = project(place, h1, qkv_second)
    of_other = over_core(away_rows(of))
    pair = jnp.stack([own_keys, cross_order(keys_y)])
    pair_other = over_core(pair)
    o_s, lse_s = self_forward(limit, qs, ks, vs)
    o_s, out_second, query_second, cross_out_second, up_first, down_sent, pair_other, of_other = join(
        (o_s, out_second, query_second, cross_out_second, up_first, down_sent, pair_other, of_other)
    )

    down_first = over_y(down_sent)
    up_second = over_x(up_first)
    os_other = over_core(away_rows(o_s))
    dout = jnp.where(loss_mask[:, None] != 0, cotangent, jnp.zeros((), ROUND))

    def pieces(own, first, second, own_other):
        return (own, first, second, own_other, over_core(first), over_core(second))

    wo = pieces(w_out, out_first, out_second, out_other)
    wq = pieces(w_cross_q, query_first, query_second, query_other)
    wc = pieces(w_cross_out, cross_out_first, cross_out_second, cross_out_other)
    text = lax.dynamic_index_in_dim(text_states, side, keepdims=False)
    head_of = jnp.arange(256) // HEAD
    same = head_of[:, None] == head_of[None, :]

    def spread_heads(v):
        return jnp.where(same, jnp.tile(v, (1, 4, 1)), jnp.zeros((), ROUND))

    every = jnp.concatenate([pair, pair_other], axis=0)
    ck, cv = spread_heads(every[:, 0]), spread_heads(every[:, 1])
    x1, x2, h2, cq, ca, h3 = middle_forward(
        place, frames, (o0, of, o_s), (o0_other, of_other, os_other), wo, wq, wc, ck, cv,
        norm_gain, norm_bias,
    )
    h3, ca, h2, up_second, down_first, dout = join((h3, ca, h2, up_second, down_first, dout))

    h3_other = over_core(h3)
    dout_other = over_core(dout)
    down_second = over_x(down_first)
    g0, du0, out_m, y_m = feed(place, h3, dout, (w_up,), (w_down,), FULL, 0)
    g0, du0, out_o, y_o = feed(
        place, h3_other, dout_other, (w_up,), (w_down,), FULL, 1, shared=(g0, du0)
    )
    y_o, down_second, ca, h2 = join((y_o, down_second, ca, h2))

    ups = (up_first, up_second)
    downs = (down_first, down_second)
    g1, du1, out_o, y_o = feed(
        place, h3_other, dout_other, ups, downs, ROUND, 1, before=(out_o, y_o)
    )
    y_received = over_core(y_o)
    h2_other = over_core(h2)
    ca_other = over_core(ca[:, 512:])
    g1, du1, out_m, y_m = feed(
        place, h3, dout, ups, downs, FULL, 0, before=(out_m, y_m), shared=(g1, du1)
    )

    def plus(a, b):
        return lower(a.astype(FULL) + b.astype(FULL))

    across = (column, X_PAIRS)
    down_z = (near, Z_NEAR)
    store = {}
    last = []

    def order(*names):
        names = tuple(dict.fromkeys((*names, *last)))
        for name, value in zip(names, join(tuple(store[name] for name in names))):
            store[name] = value

    def get(*names):
        return tuple(store[name] for name in names)

    def step(results, make, *needs):
        order(*needs)
        made = make()
        made = made if isinstance(made, (tuple, list)) else (made,)
        store.update(zip(results, made))
        last[:] = results[:1]

    class Sum:
        def __init__(self, name, axes=(across, down_z)):
            self.fly, self.kept, self.axes = name + "_fly", name + "_kept", axes

        def over_y(self, partner):
            order(partner)
            store[self.fly] = over_y(store[partner])

        def first(self, own):
            which, pairs = self.axes[0]
            order(self.fly, own)
            mine, fly = get(own, self.fly)
            away_half = plus(half_of(mine, 1 - which), half_of(fly, 1 - which))
            store[self.kept] = half_of(mine, which).astype(FULL) + half_of(fly, which).astype(FULL)
            store[self.fly] = along_wide(away_half, pairs)
            last[:] = [self.kept]

        def first_alone(self, own):
            which, pairs = self.axes[0]
            store[self.kept] = half_of(store[own], which).astype(FULL)
            store[self.fly] = along_wide(half_of(store[own], 1 - which), pairs)
            last[:] = [self.kept]

        def second(self):
            which, pairs = self.axes[1]
            order(self.fly, self.kept)
            total = store[self.kept] + store[self.fly].astype(FULL)
            store[self.kept] = half_of(total, which)
            store[self.fly] = along_wide(lower(half_of(total, 1 - which)), pairs)
            last[:] = [self.kept]

        def add(self, pairs):
            order(self.fly, self.kept)
            store[self.kept] = plus(*get(self.kept, self.fly))
            store[self.fly] = along_wide(store[self.kept], pairs)
            last[:] = [self.kept]

        def far(self):
            self.add(Z_FAR)

        def back(self):
            self.add(self.axes[1][1])

        def along(self):
            order(self.fly, self.kept)
            store[self.kept] = ordered(*get(self.kept, self.fly), self.axes[1][0])
            store[self.fly] = along_wide(store[self.kept], self.axes[0][1])
            last[:] = [self.kept]

        def end(self, result):
            order(self.fly, self.kept)
            store[result] = ordered(*get(self.kept, self.fly), self.axes[0][0]).astype(FULL)
            last[:] = [result]

    class Row:
        def __init__(self, name, value, move):
            self.fly, self.kept = name + "_fly", name + "_kept"
            store[self.kept] = value
            store[self.fly] = move(value)

        def then(self, move):
            order(self.fly, self.kept)
            store[self.kept] = store[self.kept] + store[self.fly]
            store[self.fly] = move(store[self.kept])
            last[:] = [self.kept]

        def total(self):
            return store[self.kept] + store[self.fly]

    up, down, outs, cross_in = Sum("up"), Sum("down"), Sum("outs"), Sum("cross_in")
    qkv = Sum("qkv", (down_z, across))
    store.update(h3_other=h3_other, du1=du1, g1=g1, du0=du0, g0=g0, y_m=y_m, y_fly=y_received)
    store.update(of=of, o_s=o_s, o0=o0, x2=x2, h2_other=h2_other, ca_other=ca_other)

    def middle():
        dx1, *rest = middle_back(
            place, *get("y_m", "y_fly"), x1, store["x2"], dout, cq, wq, wc, ck, cv, norm_gain
        )
        return (rest[0], dx1, *rest[1:])

    step(["up1"], lambda: up_grad(h3, *get("h3_other", "du1"), ROUND), "du1", "du0")
    up.over_y("up1")
    step(["down1"], lambda: down_grad(store["g1"], dout, dout_other, ROUND), "g1")
    step(["dself", "dx1", "dcross", "dcq", "dck", "dcv", "sums"], middle, "y_fly", "y_m", "x2")
    store["dself_other"] = over_core(store["dself"])
    step(["up0"], lambda: up_grad(h3, *get("h3_other", "du0"), ROUND), "du0")
    order(up.fly, "down1", "dself_other")
    down.over_y("down1")
    store["up_total"] = lax.psum(plus(*get("up0", up.fly)), "wide")
    step(
        ["dof", "dos", "do0"],
        lambda: pull(place, *get("dself", "dself_other"), (out_first, out_second, w_out)),
        "dself",
        "dself_other",
        "dcross",
        "dcq",
    )
    store["dcross_other"] = over_core(store["dcross"])
    store["dcq_other"] = over_core(store["dcq"][:, 512:])
    d_pair = jnp.stack(get("dck", "dcv"), axis=1)
    store["pair_kept"] = d_pair[:2]
    store["pair_fly"] = over_core(d_pair[2:])
    step(
        ["dqf", "dkf", "dvf"],
        lambda: self_back(limit, qf, kf, vf, store["of"], store["dof"], lse_f),
        "dof",
    )
    def query(g):
        return query_grad(place, g, h2, *get("h2_other", "dcq", "dcq_other"), ROUND)

    def outof(g, *o):
        return outputs_grad(
            place, g, get(*o), *get("dself", "dself_other"), ca,
            *get("ca_other", "dcross", "dcross_other"), ROUND,
        )

    step(["query1"], lambda: query(1), "dcq_other", "h2_other", "pair_fly", "pair_kept")
    pair_sum = lower(store["pair_kept"] + store["pair_fly"])
    store["pair"] = pair_sum[0]
    store["pair_other"] = cross_order(pair_sum[1])
    step(
        ["dqs", "dks", "dvs"],
        lambda: self_back(limit, qs, ks, vs, store["o_s"], store["dos"], lse_s),
        "dos",
    )
    step(["down0"], lambda: down_grad(store["g0"], dout, dout_other, ROUND), "g0")
    yp = ("dqf", "dkf", "dvf", "dqs", "dks", "dvs")
    step(["qkv1"], lambda: qkv_grad(place, h1, get(*yp), ROUND), "dqs")
    order(down.fly, "qkv1", "query1", "pair_other")
    store["query_fly"] = over_y(store["query1"])
    store["pair_y"] = over_y(store["pair_other"])
    qkv.over_y("qkv1")
    down.first("down0")
    step(
        ["dq0", "dk0", "dv0"],
        lambda: self_back(limit, q0, k0, v0, store["o0"], store["do0"], lse0),
        "do0",
    )
    down.second()
    step(["outs1"], lambda: outof(1, "of", "o_s"), "dcross_other", "ca_other")
    outs.over_y("outs1")
    step(["query0"], lambda: query(0), "dcq")
    order("query0", "query_fly", "pair", "pair_y")
    other_text = lax.dynamic_index_in_dim(text_states, 1 - side, keepdims=False)
    texts = jnp.concatenate([text, other_text], axis=0)
    pairs = jnp.concatenate(get("pair", "pair_y"), axis=1)
    store["into0"] = jnp.concatenate(
        [
            lower(store["query0"].astype(FULL) + store["query_fly"].astype(FULL)),
            lower(tn(texts, pairs[0])),
            lower(tn(texts, pairs[1])),
        ],
        axis=0,
    )
    cross_in.first_alone("into0")
    nine = ("dq0", "dk0", "dv0", *yp)
    weights = (w_qkv, qkv_first, qkv_second)
    step(["yo"], lambda: first_back(away, get(*nine), weights, ROUND), "dq0")
    store["yo_fly"] = over_core(store["yo"])
    step(["qkv0"], lambda: qkv_grad(place, h1, get("dq0", "dk0", "dv0"), ROUND), "dq0")
    qkv.first("qkv0")
    down.far()
    cross_in.second()
    step(["outs0"], lambda: outof(0, "o0"), "dcross")
    outs.first("outs0")
    qkv.second()
    step(["ym"], lambda: first_back(place, get(*nine), weights, FULL), "dq0")
    cross_in.far()
    step(
        ["grad_frames", "first_sums"],
        lambda: frames_back(place, *get("ym", "yo_fly", "dx1"), frames, norm_gain),
        "ym",
        "yo_fly",
    )
    norms = Row("norms", store["sums"] + store["first_sums"], over_core)
    down.back()
    outs.second()
    qkv.far()
    norms.then(over_y)
    cross_in.back()
    down.along()
    norms.then(over_x)
    outs.far()
    text_part = 0.0
    for c in range(2):
        text_part = text_part + nt(pairs[c], w_cross_kv[c])
    text_mine, text_theirs = text_part[:64], text_part[64:]
    text_rows = Row("texts", text_mine, lambda v: over_y(text_theirs))
    store["out_fly"] = over_core(out_o)
    qkv.back()
    norms.then(over_z)
    cross_in.along()
    text_rows.then(over_core)
    outs.back()
    norms.then(lambda v: along_wide(v, Z_FAR))
    down.end("grad_down")
    order("up_total")
    store["grad_up"] = store["up_total"].astype(FULL)
    last[:] = ["grad_up"]
    order("texts_fly", "texts_kept", "out_fly", "x2")
    text_grad = lower(text_rows.total())
    text_away = over_y(text_grad)
    qkv.along()
    outs.along()
    out_rows = lower(store["x2"] + out_m + store["out_fly"].astype(FULL))
    grad_text = ordered(text_grad[None], text_away[None], side)
    sums = norms.total()
    cross_in.end("grad_in")
    qkv.end("grad_qkv")
    outs.end("grad_outs")
    grad_in, grad_outs = get("grad_in", "grad_outs")
    return (
        out_rows,
        store["grad_frames"],
        grad_text,
        sums[0:6:2],
        sums[1:6:2],
        store["grad_qkv"].reshape(3, width, 256),
        grad_outs[:256],
        grad_in[:width],
        grad_in[width:].reshape(2, width, 256),
        grad_outs[256:],
        store["grad_up"],
        store["grad_down"],
    )


def solution(mesh):
    chips = dict(mesh.shape) == {"wide": 8, "narrow": 4}
    return jax.shard_map(
        chip_local if chips else general_local,
        mesh=mesh,
        in_specs=(
            P(("wide", "narrow"), None),
            P("wide", None, None),
            P("wide"),
            P(("wide", "narrow")),
            P(),
            P(),
            P(None, None, "narrow"),
            P("narrow", None),
            P(None, "narrow"),
            P(None, None, "narrow"),
            P("narrow", None),
            P(None, "narrow"),
            P("narrow", None),
            P(("wide", "narrow"), None),
        ),
        out_specs=(
            P(("wide", "narrow"), None),
            P(("wide", "narrow"), None),
            P("wide", None, None),
            P(),
            P(),
            P(None, None, "narrow"),
            P("narrow", None),
            P(None, "narrow"),
            P(None, None, "narrow"),
            P("narrow", None),
            P(None, "narrow"),
            P("narrow", None),
        ),
        check_vma=False,
    )
```

```python
import functools

import jax
import jax.numpy as jnp
from jax import lax
from jax.experimental import pallas as pl
from jax.experimental.pallas import tpu as pltpu
from jax.sharding import PartitionSpec as P

HEAD = 64


EPS = 1e-05
NEG = -1e30


def lower(values_in):
    return values_in.astype(jnp.bfloat16)


def product(left_side, right_side, transposed):
    if transposed:
        return lax.dot_general(
            left_side, right_side, (((1,), (1,)), ((), ())), preferred_element_type=jnp.float32
        )
    return jnp.dot(left_side, right_side, preferred_element_type=jnp.float32)


def outer_sum(left_side, right_side):
    return lax.dot_general(
        left_side, right_side, (((0,), (0,)), ((), ())), preferred_element_type=jnp.float32
    )


def normalize(values_in, gain_row, bias_row):
    row_mean = jnp.mean(values_in, axis=-1, keepdims=True)
    centered = values_in - row_mean
    inverse = lax.rsqrt(jnp.mean(centered * centered, axis=-1, keepdims=True) + EPS)
    scaled = centered * inverse
    return (scaled * gain_row + bias_row, scaled, inverse)


def normalize_back(upstream, scaled, inverse, gain_row):
    weighted = upstream * gain_row
    inner_mean = jnp.mean(weighted, axis=-1, keepdims=True)
    along_mean = jnp.mean(weighted * scaled, axis=-1, keepdims=True)
    grad_input = inverse * (weighted - inner_mean - scaled * along_mean)
    return (grad_input, jnp.sum(upstream * scaled, axis=0), jnp.sum(upstream, axis=0))


def gelu_parts(values_in):
    normal_cdf = 0.5 * (1.0 + jax.scipy.special.erf(values_in * 0.7071067811865476))
    normal_pdf = jnp.exp(-0.5 * values_in * values_in) * 0.3989422804014327
    return (values_in * normal_cdf, normal_cdf + values_in * normal_pdf)


def scores_of(query_part, key_part, valid):
    scores = jnp.einsum(
        "bhe,khe->hbk", query_part, key_part, preferred_element_type=jnp.float32
    ) * HEAD ** (-0.5)
    return jnp.where(valid, scores, NEG)


def attend(query_part, key_part, value_part, valid):
    scores = scores_of(query_part, key_part, valid)
    row_top = jnp.max(scores, axis=-1, keepdims=True)
    weights_exp = jnp.exp(scores - row_top)
    denominator = jnp.sum(weights_exp, axis=-1, keepdims=True)
    probability = weights_exp / denominator
    mixed = jnp.einsum(
        "hbk,khe->bhe", lower(probability), value_part, preferred_element_type=jnp.float32
    )
    return (lower(mixed), (row_top + jnp.log(denominator))[..., 0])


def attend_back(query_part, key_part, value_part, valid, summary, upstream):
    scores = scores_of(query_part, key_part, valid)
    probability = jnp.exp(scores - summary[..., None])
    pressure = jnp.einsum("bhe,khe->hbk", upstream, value_part, preferred_element_type=jnp.float32)
    grad_scores = lower(
        probability * (pressure - jnp.sum(probability * pressure, axis=-1, keepdims=True))
    )
    factor = HEAD ** (-0.5)
    grad_query = (
        jnp.einsum("hbk,khe->bhe", grad_scores, key_part, preferred_element_type=jnp.float32)
        * factor
    )
    grad_key = (
        jnp.einsum("hbk,bhe->khe", grad_scores, query_part, preferred_element_type=jnp.float32)
        * factor
    )
    grad_value = jnp.einsum(
        "hbk,bhe->khe", lower(probability), upstream, preferred_element_type=jnp.float32
    )
    return (grad_query, grad_key, grad_value)


def general_local(
    frames,
    text_states,
    lengths,
    loss_mask,
    norm_gain,
    norm_bias,
    w_qkv,
    w_out,
    w_cross_q,
    w_cross_kv,
    w_cross_out,
    w_up,
    w_down,
    cotangent,
):
    row_count = frames.shape[0]
    width = frames.shape[1]
    item_count = lengths.shape[0]
    span = row_count * lax.axis_size("narrow") // item_count
    half_span = span // 2
    inner_width = w_qkv.shape[2]
    head_count = inner_width // HEAD
    text_count = text_states.shape[1]
    full_rows = item_count * span
    places = jnp.arange(span, dtype=jnp.int32)

    def spread(shard_rows):
        return lax.all_gather(shard_rows, "narrow", axis=0, tiled=True)

    def collect(left_side, right_side, transposed):
        return lax.psum_scatter(
            product(
                lax.slice_in_dim(left_side, 0, lax.axis_size("narrow") * row_count, axis=0),
                right_side,
                transposed,
            ),
            "narrow",
            scatter_dimension=0,
            tiled=True,
        )

    def causal(block_index, item_limit):
        query_place = block_index * half_span + jnp.arange(half_span, dtype=jnp.int32)
        return (places[None, :] <= query_place[:, None]) & (places[None, :] < item_limit)

    frame_rows = frames.astype(jnp.float32)
    normed_one, scaled_one, inverse_one = normalize(frame_rows, norm_gain[0], norm_bias[0])
    first_input = spread(lower(normed_one))
    triple = lower(
        jnp.einsum("rd,cde->cre", first_input, w_qkv, preferred_element_type=jnp.float32)
    )
    triple = triple.reshape(3, item_count, span, head_count, HEAD)

    def self_item(packed):
        query_part, key_part, value_part, item_limit = packed
        mixed_list = []
        summary_list = []
        for block_index in range(2):
            mixed, summary = attend(
                query_part[block_index * half_span : (block_index + 1) * half_span],
                key_part,
                value_part,
                causal(block_index, item_limit),
            )
            mixed_list.append(mixed)
            summary_list.append(summary)
        return (jnp.concatenate(mixed_list, axis=0), jnp.stack(summary_list, axis=0))

    attended, self_summary = lax.map(self_item, (triple[0], triple[1], triple[2], lengths))
    attended_flat = attended.reshape(full_rows, inner_width)
    first_rows = frame_rows + collect(attended_flat, w_out, False)
    normed_two, scaled_two, inverse_two = normalize(first_rows, norm_gain[1], norm_bias[1])
    second_input = spread(lower(normed_two))
    cross_query = lower(product(second_input, w_cross_q, False)).reshape(
        item_count, span, head_count, HEAD
    )
    cross_pair = lower(
        jnp.einsum("ntd,cde->cnte", text_states, w_cross_kv, preferred_element_type=jnp.float32)
    )
    cross_pair = cross_pair.reshape(2, item_count, text_count, head_count, HEAD)

    def cross_item(packed):
        query_part, key_part, value_part = packed
        return attend(query_part, key_part, value_part, True)

    cross_mixed, cross_summary = lax.map(cross_item, (cross_query, cross_pair[0], cross_pair[1]))
    cross_flat = cross_mixed.reshape(full_rows, inner_width)
    second_rows = first_rows + collect(cross_flat, w_cross_out, False)
    normed_three, scaled_three, inverse_three = normalize(second_rows, norm_gain[2], norm_bias[2])
    upstream = cotangent.astype(jnp.float32) * loss_mask.astype(jnp.float32)[:, None]
    ffn_grad = lower(upstream)
    ffn_input = spread(lower(normed_three))
    hidden_pre = product(ffn_input, w_up, False)
    active, slope = gelu_parts(hidden_pre)
    active = lower(active)
    out_rows = second_rows + collect(active, w_down, False)
    ffn_full = spread(ffn_grad)
    grad_down = outer_sum(active, ffn_full)
    grad_hidden = lower(product(ffn_full, w_down, True) * slope)
    grad_up = outer_sum(ffn_input, grad_hidden)
    back_three = collect(grad_hidden, w_up, True)
    grad_up, grad_down = (grad_up, grad_down)
    grad_in_three, gain_three, bias_three = normalize_back(
        back_three, scaled_three, inverse_three, norm_gain[2]
    )
    grad_second = upstream + grad_in_three
    cross_full = spread(lower(grad_second))
    grad_cross_out = outer_sum(cross_flat, cross_full)
    cross_upstream = lower(product(cross_full, w_cross_out, True)).reshape(
        item_count, span, head_count, HEAD
    )

    def cross_back(packed):
        query_part, key_part, value_part, summary, upstream_item = packed
        return attend_back(query_part, key_part, value_part, True, summary, upstream_item)

    grad_cq, grad_ck, grad_cv = lax.map(
        cross_back, (cross_query, cross_pair[0], cross_pair[1], cross_summary, cross_upstream)
    )
    grad_cq = lower(grad_cq).reshape(full_rows, inner_width)
    grad_pair = lower(jnp.stack((grad_ck, grad_cv), axis=0)).reshape(
        2, item_count, text_count, inner_width
    )
    grad_cross_q = outer_sum(second_input, grad_cq)
    grad_cross_kv = jnp.einsum(
        "ntd,cnte->cde", text_states, grad_pair, preferred_element_type=jnp.float32
    )
    grad_cross_q, grad_cross_kv, grad_cross_out = (grad_cross_q, grad_cross_kv, grad_cross_out)
    text_partial = jnp.einsum(
        "cnte,cde->ntd", grad_pair, w_cross_kv, preferred_element_type=jnp.float32
    )
    grad_text = lower(lax.psum(text_partial, "narrow"))
    back_two = collect(grad_cq, w_cross_q, True)
    grad_in_two, gain_two, bias_two = normalize_back(
        back_two, scaled_two, inverse_two, norm_gain[1]
    )
    grad_first = grad_second + grad_in_two
    self_full = spread(lower(grad_first))
    grad_out = outer_sum(attended_flat, self_full)
    self_upstream = lower(product(self_full, w_out, True)).reshape(
        item_count, span, head_count, HEAD
    )

    def self_back(packed):
        query_part, key_part, value_part, item_limit, summary, upstream_item = packed
        query_list = []
        key_list = []
        value_list = []
        for block_index in range(2):
            lower_row = block_index * half_span
            grad_query, grad_key, grad_value = attend_back(
                query_part[lower_row : lower_row + half_span],
                key_part,
                value_part,
                causal(block_index, item_limit),
                summary[block_index],
                upstream_item[lower_row : lower_row + half_span],
            )
            query_list.append(grad_query)
            key_list.append(grad_key)
            value_list.append(grad_value)
        return (
            jnp.concatenate(query_list, axis=0),
            key_list[0] + key_list[1],
            value_list[0] + value_list[1],
        )

    grad_q, grad_k, grad_v = lax.map(
        self_back, (triple[0], triple[1], triple[2], lengths, self_summary, self_upstream)
    )
    grad_triple = lower(jnp.stack((grad_q, grad_k, grad_v), axis=0)).reshape(
        3, full_rows, inner_width
    )
    grad_qkv = jnp.einsum(
        "rd,cre->cde", first_input, grad_triple, preferred_element_type=jnp.float32
    )
    grad_qkv, grad_out = (grad_qkv, grad_out)
    merged = grad_triple.transpose(1, 0, 2).reshape(full_rows, 3 * inner_width)
    stacked_weights = w_qkv.transpose(0, 2, 1).reshape(3 * inner_width, width)
    back_one = collect(merged, stacked_weights, False)
    grad_in_one, gain_one, bias_one = normalize_back(
        back_one, scaled_one, inverse_one, norm_gain[0]
    )
    grad_frames = lower(grad_first + grad_in_one)
    gain_terms = jnp.stack((gain_one, gain_two, gain_three), axis=0)
    bias_terms = jnp.stack((bias_one, bias_two, bias_three), axis=0)
    grad_norm_gain, grad_norm_bias = lax.psum((gain_terms, bias_terms), ("wide", "narrow"))
    grad_qkv, grad_out, grad_cross_q, grad_cross_kv, grad_cross_out, grad_up, grad_down = lax.psum(
        (grad_qkv, grad_out, grad_cross_q, grad_cross_kv, grad_cross_out, grad_up, grad_down),
        "wide",
    )
    return (
        lower(out_rows),
        grad_frames,
        grad_text,
        grad_norm_gain,
        grad_norm_bias,
        grad_qkv,
        grad_out,
        grad_cross_q,
        grad_cross_kv,
        grad_cross_out,
        grad_up,
        grad_down,
    )


ROUND = jnp.bfloat16
FULL = jnp.float32
CORE_PAIRS = ((0, 1), (1, 0), (2, 3), (3, 2))
Y_PAIRS = ((0, 2), (2, 0), (1, 3), (3, 1))
X_PAIRS = tuple((i, i ^ 1) for i in range(8))
Z_INWARD = ((0, 2), (1, 3), (6, 4), (7, 5))
Z_MIDDLE = ((2, 4), (4, 2), (3, 5), (5, 3))
Z_OUTWARD = ((2, 0), (3, 1), (4, 6), (5, 7))
Z_NEAR = tuple((i, i ^ 2) for i in range(8))
Z_FAR = tuple((i, i ^ 4) for i in range(8))
MIB = 1 << 20


def nt(a, b):
    return lax.dot_general(a, b, (((1,), (1,)), ((), ())), preferred_element_type=FULL)


def nn(a, b):
    return lax.dot_general(a, b, (((1,), (0,)), ((), ())), preferred_element_type=FULL)


def tn(a, b):
    return lax.dot_general(a, b, (((0,), (0,)), ((), ())), preferred_element_type=FULL)


def shape(dims, kind):
    return jax.ShapeDtypeStruct(dims, kind)


def resident(dims):
    zeros = (0,) * len(dims)
    return pl.BlockSpec(dims, lambda i, s: zeros, pipeline_mode=pl.Buffered(1))


def rows_of(block, width):
    return pl.BlockSpec((block, width), lambda i, s: (i, 0))


def lasting(microseconds):
    flops = int(microseconds * 0.28 * 1.15e9)
    return pl.CostEstimate(flops=flops, bytes_accessed=1000, transcendentals=0)


def params(mib):
    return pltpu.CompilerParams(vmem_limit_bytes=mib * MIB)


def norm_parts(v):
    centered = v - jnp.mean(v, axis=-1, keepdims=True)
    inverse = lax.rsqrt(jnp.mean(centered * centered, axis=-1, keepdims=True) + EPS)
    return centered * inverse, inverse


def norm_pull(y, scaled, inverse, gain_row):
    weighted = y * gain_row
    inner = jnp.mean(weighted, axis=-1, keepdims=True)
    along = jnp.mean(weighted * scaled, axis=-1, keepdims=True)
    return inverse * (weighted - inner - scaled * along)


def first_project_kernel(
    place_ref, mine_ref, other_ref, gain_ref, bias_ref, weight_ref, h_ref, *out_refs
):
    half = pl.program_id(0)

    def run(source):
        for start in range(0, source.shape[0], 208):
            part = slice(start, start + 208)
            scaled, _ = norm_parts(source[part, :].astype(FULL))
            h = lower(scaled * gain_ref[0:1, :] + bias_ref[0:1, :])
            h_ref[part, :] = h
            for c, out_ref in enumerate(out_refs):
                out_ref[part, :] = lower(nn(h, weight_ref[c]))

    @pl.when(half == 0)
    def _():
        run(mine_ref)

    @pl.when(half == 1)
    def _():
        run(other_ref)


def first_project(place, mine, other, gains, biases, weights):
    rows, depth = mine.shape
    count, _, wide = weights.shape
    out = pl.BlockSpec((rows, wide), lambda i, s: ((i + s[0]) % 2, 0))
    return pl.pallas_call(
        first_project_kernel,
        grid_spec=pltpu.PrefetchScalarGridSpec(
            num_scalar_prefetch=1,
            grid=(2,),
            in_specs=[resident(a.shape) for a in (mine, other, gains, biases, weights)],
            out_specs=[rows_of(rows, depth)] + [out] * count,
        ),
        out_shape=[shape((2 * rows, depth), ROUND)] + [shape((2 * rows, wide), ROUND)] * count,
        compiler_params=params(40),
        cost_estimate=lasting(5),
        name="first_project",
    )(place, mine, other, gains, biases, weights)


def project_kernel(place_ref, h_ref, weight_ref, *out_refs):
    count = len(out_refs)
    wide = weight_ref.shape[2]
    weights = jnp.concatenate([weight_ref[c] for c in range(count)], axis=1)
    for start in range(0, h_ref.shape[0], 416):
        part = slice(start, start + 416)
        result = lower(nn(h_ref[part, :], weights))
        for c, out_ref in enumerate(out_refs):
            out_ref[part, :] = result[:, c * wide : (c + 1) * wide]


def project(place, h, weights):
    rows, depth = h.shape[0] // 2, h.shape[1]
    count, _, wide = weights.shape
    out = pl.BlockSpec((rows, wide), lambda i, s: ((i + s[0]) % 2, 0))
    return pl.pallas_call(
        project_kernel,
        grid_spec=pltpu.PrefetchScalarGridSpec(
            num_scalar_prefetch=1,
            grid=(2,),
            in_specs=[rows_of(rows, depth), resident(weights.shape)],
            out_specs=[out] * count,
        ),
        out_shape=[shape((2 * rows, wide), ROUND)] * count,
        compiler_params=params(40),
        cost_estimate=lasting(4),
        name="project",
    )(place, h, weights)


def pull_kernel(place_ref, mine_ref, other_ref, *refs):
    half = pl.program_id(0)
    count = len(refs) // 2

    def run(source):
        for weight_ref, out_ref in zip(refs[:count], refs[count:]):
            out_ref[...] = lower(nt(source[...], weight_ref[...]))

    @pl.when(half == 0)
    def _():
        run(mine_ref)

    @pl.when(half == 1)
    def _():
        run(other_ref)


def pull(place, mine, other, weights):
    rows = mine.shape[0]
    return pl.pallas_call(
        pull_kernel,
        grid_spec=pltpu.PrefetchScalarGridSpec(
            num_scalar_prefetch=1,
            grid=(2,),
            in_specs=[resident(a.shape) for a in (mine, other, *weights)],
            out_specs=[
                pl.BlockSpec((rows, a.shape[0]), lambda i, s: ((i + s[0]) % 2, 0)) for a in weights
            ],
        ),
        out_shape=[shape((2 * rows, a.shape[0]), ROUND) for a in weights],
        compiler_params=params(32),
        cost_estimate=lasting(3.5),
        name="pull",
    )(place, mine, other, *weights)


def blocks_of(span, block):
    return [(start, min(block, span - start)) for start in range(0, span, block)]


def self_forward_kernel(
    limit_ref, q_ref, k_ref, v_ref, o_ref, lse_ref, *, span, floor, block
):
    limit = limit_ref[0]
    lane = lax.broadcasted_iota(jnp.int32, (1, 128), 1)
    row = lax.broadcasted_iota(jnp.int32, (128, 1), 0)
    zero = jnp.zeros((), ROUND)
    value_turned = v_ref[...].T
    for start, size in blocks_of(span, block):
        end = start + size
        mixed_list = []
        for h in range(2):
            own_lanes = (lane < HEAD) if h == 0 else (lane >= HEAD)
            query = jnp.where(own_lanes, q_ref[start:end, :] * HEAD ** (-0.5), zero)
            parts = []
            for low in range(0, end, block):
                high = min(low + block, end)
                scores = nt(k_ref[low:high, :], query)
                if low == start:
                    key = lax.broadcasted_iota(jnp.int32, (size, size), 0)
                    valid = key <= lax.broadcasted_iota(jnp.int32, (size, size), 1)
                    if high > floor:
                        valid = valid & (key + low < limit)
                    scores = jnp.where(valid, scores, NEG)
                elif high > floor:
                    key = lax.broadcasted_iota(jnp.int32, (high - low, 1), 0)
                    scores = jnp.where(key + low < limit, scores, NEG)
                parts.append((low, high, scores))
            top = functools.reduce(
                jnp.maximum, [jnp.max(s, axis=0, keepdims=True) for _, _, s in parts]
            )
            total = 0.0
            mixed = 0.0
            for low, high, scores in parts:
                weights_exp = jnp.exp(scores - top)
                total = total + jnp.sum(weights_exp, axis=0, keepdims=True)
                mixed = mixed + nn(value_turned[:, low:high], lower(weights_exp))
            mixed_list.append(mixed / total)
            lse_ref[0, h : h + 1, start:end] = top + jnp.log(total)
        o_ref[start:end, :] = lower(jnp.where(row < HEAD, mixed_list[0], mixed_list[1]).T)


def self_forward(limit, q, k, v):
    span, wide = q.shape
    pairs = wide // 128
    floor = (span - span // 8 + 1) // 128 * 128
    pair = pl.BlockSpec((span, 128), lambda p, s: (0, p))
    return pl.pallas_call(
        functools.partial(self_forward_kernel, span=span, floor=floor, block=512),
        grid_spec=pltpu.PrefetchScalarGridSpec(
            num_scalar_prefetch=1,
            grid=(pairs,),
            in_specs=[pair] * 3,
            out_specs=[pair, pl.BlockSpec((1, 8, span), lambda p, s: (p, 0, 0))],
        ),
        out_shape=[shape((span, wide), ROUND), shape((pairs, 8, span), FULL)],
        compiler_params=params(56),
        cost_estimate=lasting(7.3 * pairs),
        name="self_forward",
    )(limit, q, k, v)


def self_back_kernel(
    limit_ref, q_ref, k_ref, v_ref, o_ref, do_ref, lse_ref, dq_ref, dk_ref, dv_ref, dqt,
    *, span, floor, block
):
    limit = limit_ref[0]
    lane = lax.broadcasted_iota(jnp.int32, (1, 128), 1)
    row = lax.broadcasted_iota(jnp.int32, (128, 1), 0)
    zero = jnp.zeros((), ROUND)
    factor = HEAD ** (-0.5)
    product_rows = do_ref[...].astype(FULL) * o_ref[...].astype(FULL)
    high = lower(product_rows)
    rest = lower(product_rows - high.astype(FULL))
    pick = lower(
        jnp.concatenate(
            [
                jnp.where(lane < HEAD, 1.0, 0.0),
                jnp.where(lane >= HEAD, 1.0, 0.0),
                jnp.zeros((6, 128), FULL),
            ],
            axis=0,
        )
    )
    delta = nt(pick, high) + nt(pick, rest)
    for start, size in blocks_of(span, block):
        end = start + size
        key = k_ref[start:end, :]
        value = v_ref[start:end, :]
        key_turned = key.T
        dk = 0.0
        dv = 0.0
        dq_add = 0.0
        for h in range(2):
            own_lanes = (lane < HEAD) if h == 0 else (lane >= HEAD)
            own_rows = (row < HEAD) if h == 0 else (row >= HEAD)
            query = jnp.where(own_lanes, q_ref[start:, :] * factor, zero)
            pulled = jnp.where(own_lanes, do_ref[start:, :], zero)
            probability = jnp.exp(nt(key, query) - lse_ref[0, h : h + 1, start:])
            pressure = nt(value, pulled)
            below = lax.broadcasted_iota(jnp.int32, (size, size), 0)
            across = lax.broadcasted_iota(jnp.int32, (size, size), 1)
            corner = jnp.where(below <= across, probability[:, :size], 0.0)
            if end < span:
                probability = jnp.concatenate([corner, probability[:, size:]], axis=1)
            else:
                probability = corner
            if end > floor:
                place = lax.broadcasted_iota(jnp.int32, (size, 1), 0) + start
                probability = jnp.where(place < limit, probability, 0.0)
            grad_scores = lower(probability * (pressure - delta[h : h + 1, start:]))
            dv = dv + nn(lower(probability), pulled)
            dk = dk + nn(grad_scores, query)
            dq_add = dq_add + nn(jnp.where(own_rows, key_turned, zero), grad_scores)
        dk_ref[start:end, :] = lower(dk)
        dv_ref[start:end, :] = lower(dv)
        if start == 0:
            dqt[...] = dq_add
        else:
            dqt[:, start:] += dq_add
    dq_ref[...] = lower(dqt[...].T * factor)


def self_back(limit, q, k, v, o, do, lse):
    span, wide = q.shape
    pairs = wide // 128
    floor = (span - span // 8 + 1) // 128 * 128
    pair = pl.BlockSpec((span, 128), lambda p, s: (0, p))
    return pl.pallas_call(
        functools.partial(self_back_kernel, span=span, floor=floor, block=256),
        grid_spec=pltpu.PrefetchScalarGridSpec(
            num_scalar_prefetch=1,
            grid=(pairs,),
            in_specs=[pair] * 5 + [pl.BlockSpec((1, 8, span), lambda p, s: (p, 0, 0))],
            out_specs=[pair] * 3,
            scratch_shapes=[pltpu.VMEM((128, span), FULL)],
        ),
        out_shape=[shape((span, wide), ROUND)] * 3,
        compiler_params=params(48),
        cost_estimate=lasting(7.00 * pairs),
        name="self_back",
    )(limit, q, k, v, o, do, lse)


def by_head(values_in, reduce, empty):
    lane = lax.broadcasted_iota(jnp.int32, (1, 128), 1)
    pieces = []
    for start in range(0, values_in.shape[1], 128):
        part = values_in[:, start : start + 128]
        first = reduce(jnp.where(lane < HEAD, part, empty), axis=1, keepdims=True)
        second = reduce(jnp.where(lane >= HEAD, part, empty), axis=1, keepdims=True)
        pieces.append(jnp.where(lane < HEAD, first, second))
    return jnp.concatenate(pieces, axis=1)


def cross_probability(query, keys):
    scores = nt(query * HEAD ** (-0.5), keys)
    weights_exp = jnp.exp(scores - by_head(scores, jnp.max, NEG))
    return weights_exp / by_head(weights_exp, jnp.sum, 0.0)


def in_groups(refs, axis):
    for at in (0, 3):
        yield refs[at][...]
        yield jnp.concatenate([refs[at + 1][...], refs[at + 2][...]], axis=axis)


def middle_forward_kernel(place_ref, frame_ref, *refs):
    mixed, wo, wq, wc = refs[0:6], refs[6:12], refs[12:18], refs[18:24]
    ck_ref, cv_ref, gain_ref, bias_ref = refs[24:28]
    x1_ref, x2_ref, h2_ref, cq_ref, ca_ref, h3_ref = refs[28:]
    x1 = frame_ref[...].astype(FULL)
    for o, weight in zip(in_groups(mixed, 1), in_groups(wo, 0)):
        x1 = x1 + nn(o, weight)
    x1_ref[...] = x1
    scaled, _ = norm_parts(x1)
    h2 = lower(scaled * gain_ref[1:2, :] + bias_ref[1:2, :])
    h2_ref[...] = h2
    for g, weight in enumerate(in_groups(wq, 1)):
        lanes = slice(g * 256, (g + 1) * 256)
        cq = lower(nn(h2, weight))
        cq_ref[:, lanes] = cq
        probability = cross_probability(cq, ck_ref[g])
        ca_ref[:, lanes] = lower(nn(lower(probability), cv_ref[g]))
    crossed = 0.0
    for g, weight in enumerate(in_groups(wc, 0)):
        crossed = crossed + nn(ca_ref[:, g * 256 : (g + 1) * 256], weight)
    x2 = x1_ref[...] + crossed
    x2_ref[...] = x2
    scaled, _ = norm_parts(x2)
    h3_ref[...] = lower(scaled * gain_ref[2:3, :] + bias_ref[2:3, :])


def middle_forward(place, frames, attended, received, wo, wq, wc, ck, cv, gains, biases):
    rows, width = frames.shape
    block = 416
    steps = rows // block
    wide = rows_of(block, width)
    whole = (*wo, *wq, *wc, ck, cv, gains, biases)
    return pl.pallas_call(
        middle_forward_kernel,
        grid_spec=pltpu.PrefetchScalarGridSpec(
            num_scalar_prefetch=1,
            grid=(steps,),
            in_specs=[wide]
            + [
                pl.BlockSpec((block, a.shape[1]), lambda i, s: (s[0] * steps + i, 0))
                for a in attended
            ]
            + [rows_of(block, a.shape[1]) for a in received]
            + [resident(a.shape) for a in whole],
            out_specs=[wide] * 6,
        ),
        out_shape=[shape((rows, width), FULL)] * 2 + [shape((rows, width), ROUND)] * 4,
        compiler_params=params(56),
        cost_estimate=lasting(22),
        name="middle_forward",
    )(place, frames, *attended, *received, *whole)


def keys_kernel(text_ref, weight_ref, out_ref):
    for item in range(2):
        for c in range(2):
            out_ref[item, c] = lower(nn(text_ref[item], weight_ref[c]))


def keys_of(text_states, weights):
    items, states, _ = text_states.shape
    return pl.pallas_call(
        keys_kernel,
        out_shape=shape((items, 2, states, weights.shape[2]), ROUND),
        compiler_params=params(24),
        cost_estimate=lasting(2),
        name="keys_of",
    )(text_states, weights)


def feed_kernel(place_ref, h_ref, d_ref, *refs, parts, carried):
    ups, downs = refs[:parts], refs[parts : 2 * parts]
    before = refs[2 * parts : 2 * parts + carried]
    g_ref, du_ref, out_ref, y_ref = refs[-4:]
    h = h_ref[...]
    d = d_ref[...]
    out = 0.0
    y = 0.0
    for n, (up_ref, down_ref) in enumerate(zip(ups, downs)):
        size = down_ref.shape[0]
        if parts == 1:
            lanes = slice(0, size)
        else:
            column = place_ref[2]
            which = column if n == 0 else 1 - column
            lanes = pl.ds(pl.multiple_of(which * size, 128), size)
        u = nn(h, up_ref[...])
        active, slope = gelu_parts(u)
        g = lower(active)
        g_ref[:, lanes] = g
        du = lower(nt(d, down_ref[...]) * slope)
        du_ref[:, lanes] = du
        out = out + nn(g, down_ref[...])
        y = y + nt(du, up_ref[...])
    if carried:
        out = before[0][...] + out
        y = before[1][...] + y
    out_ref[...] = out.astype(out_ref.dtype)
    y_ref[...] = y.astype(y_ref.dtype)


def feed(place, h, d, ups, downs, kind, half, before=(), shared=()):
    rows, width = h.shape
    block = 416
    steps = rows // block
    hidden = sum(a.shape[0] for a in downs)
    wide = rows_of(block, width)
    kept = pl.BlockSpec((block, hidden), lambda i, s: (i + half * steps, 0))
    there = pl.BlockSpec(memory_space=pl.ANY)
    parts = len(ups)
    at = 3 + 2 * parts + len(before)
    return pl.pallas_call(
        functools.partial(feed_kernel, parts=parts, carried=len(before)),
        grid_spec=pltpu.PrefetchScalarGridSpec(
            num_scalar_prefetch=1,
            grid=(steps,),
            in_specs=[wide, wide]
            + [resident(a.shape) for a in (*ups, *downs)]
            + [wide] * len(before)
            + [there] * len(shared),
            out_specs=[kept, kept, wide, wide],
        ),
        out_shape=[shape((2 * rows, hidden), ROUND)] * 2 + [shape((rows, width), kind)] * 2,
        input_output_aliases={at: 0, at + 1: 1} if shared else {},
        compiler_params=params(58),
        cost_estimate=lasting(13),
        name="feed",
    )(place, h, d, *ups, *downs, *before, *shared)


def up_grad_kernel(mine_ref, other_ref, du_ref, out_ref):
    rows = mine_ref.shape[0]
    total = tn(mine_ref[...], du_ref[:rows, :]) + tn(other_ref[...], du_ref[rows:, :])
    out_ref[...] = total.astype(out_ref.dtype)


def up_grad(mine, other, du, kind):
    rows, width = mine.shape
    hidden = du.shape[1]
    tile = 512
    whole = pl.BlockSpec((rows, width), lambda i: (0, 0), pipeline_mode=pl.Buffered(1))
    return pl.pallas_call(
        up_grad_kernel,
        grid=(hidden // tile,),
        in_specs=[whole, whole, pl.BlockSpec((2 * rows, tile), lambda i: (0, i))],
        out_specs=pl.BlockSpec((width, tile), lambda i: (0, i)),
        out_shape=shape((width, hidden), kind),
        compiler_params=params(48),
        cost_estimate=lasting(5.00),
        name="up_grad",
    )(mine, other, du)


def down_grad_kernel(g_ref, mine_ref, other_ref, out_ref):
    rows = mine_ref.shape[0]
    total = tn(g_ref[:rows, :], mine_ref[...]) + tn(g_ref[rows:, :], other_ref[...])
    out_ref[...] = total.astype(out_ref.dtype)


def down_grad(g, mine, other, kind):
    rows, width = mine.shape
    hidden = g.shape[1]
    tile = 512
    whole = pl.BlockSpec((rows, width), lambda i: (0, 0), pipeline_mode=pl.Buffered(1))
    return pl.pallas_call(
        down_grad_kernel,
        grid=(hidden // tile,),
        in_specs=[pl.BlockSpec((2 * rows, tile), lambda i: (0, i)), whole, whole],
        out_specs=pl.BlockSpec((tile, width), lambda i: (i, 0)),
        out_shape=shape((hidden, width), kind),
        compiler_params=params(48),
        cost_estimate=lasting(5.00),
        name="down_grad",
    )(g, mine, other)


def qkv_grad_kernel(place_ref, h_ref, *refs):
    out_ref = refs[-1]
    rows, width = h_ref.shape[0] // 2, h_ref.shape[1]
    core, near = place_ref[0], place_ref[1]
    halves = (len(refs) - 1) // 3
    total = [0.0] * 3
    for half in range(2):
        turned = h_ref[half * rows : (half + 1) * rows, :].T
        at = pl.multiple_of((core if half == 0 else 1 - core) * rows, 16)
        for c in range(3):
            parts = [refs[3 * n + c][pl.ds(at, rows), :] for n in range(halves)]
            grads = parts[0] if halves == 1 else jnp.concatenate(parts, axis=1)
            total[c] = total[c] + nn(turned, grads)
    for c in range(3):
        part = slice(c * width, (c + 1) * width)
        value = total[c].astype(out_ref.dtype)
        if halves == 1:
            out_ref[part, :] = value
        else:
            out_ref[part, pl.ds(pl.multiple_of(near * 128, 128), 128)] = value[:, :128]
            out_ref[part, pl.ds(pl.multiple_of((1 - near) * 128, 128), 128)] = value[:, 128:]


def qkv_grad(place, h, grads, kind):
    width = h.shape[1]
    return pl.pallas_call(
        qkv_grad_kernel,
        grid_spec=pltpu.PrefetchScalarGridSpec(
            num_scalar_prefetch=1,
            grid=(1,),
            in_specs=[resident(a.shape) for a in (h, *grads)],
            out_specs=resident((3 * width, 256)),
        ),
        out_shape=shape((3 * width, 256), kind),
        compiler_params=params(48),
        cost_estimate=lasting(5.00),
        name="qkv_grad",
    )(place, h, *grads)


def query_grad_kernel(place_ref, mine_ref, other_ref, dm_ref, do_ref, out_ref, *, split):
    column = place_ref[2]
    total = tn(mine_ref[...], dm_ref[...]) + tn(other_ref[...], do_ref[...])
    value = total.astype(out_ref.dtype)
    if split:
        out_ref[:, pl.ds(pl.multiple_of(column * 128, 128), 128)] = value[:, :128]
        out_ref[:, pl.ds(pl.multiple_of((1 - column) * 128, 128), 128)] = value[:, 128:]
    else:
        out_ref[...] = value


def query_grad(place, group, mine, other, d_mine, d_other, kind):
    rows, width = mine.shape
    lanes = pl.BlockSpec((rows, 256), lambda i, s: (0, group))
    return pl.pallas_call(
        functools.partial(query_grad_kernel, split=group == 1),
        grid_spec=pltpu.PrefetchScalarGridSpec(
            num_scalar_prefetch=1,
            grid=(1,),
            in_specs=[resident(mine.shape), resident(other.shape), lanes, lanes],
            out_specs=resident((width, 256)),
        ),
        out_shape=shape((width, 256), kind),
        compiler_params=params(48),
        cost_estimate=lasting(2.86),
        name="query_grad",
    )(place, mine, other, d_mine, d_other)


def outputs_grad_kernel(place_ref, *refs, count):
    o_refs = refs[:count]
    sm_ref, so_ref, am_ref, ao_ref, cm_ref, co_ref, out_ref = refs[count:]
    rows = sm_ref.shape[0]
    core, near, column = place_ref[0], place_ref[1], place_ref[2]
    mine_at = pl.ds(pl.multiple_of(core * rows, 16), rows)
    other_at = pl.ds(pl.multiple_of((1 - core) * rows, 16), rows)
    for n, o_ref in enumerate(o_refs):
        total = tn(o_ref[mine_at, :], sm_ref[...]) + tn(o_ref[other_at, :], so_ref[...])
        if count == 1:
            at = slice(0, 256)
        else:
            at = pl.ds(pl.multiple_of((near if n == 0 else 1 - near) * 128, 128), 128)
        out_ref[at, :] = total.astype(out_ref.dtype)
    total = tn(am_ref[...], cm_ref[...]) + tn(ao_ref[...], co_ref[...])
    value = total.astype(out_ref.dtype)
    if count == 1:
        out_ref[256:, :] = value
    else:
        out_ref[pl.ds(pl.multiple_of(256 + column * 128, 128), 128), :] = value[:128, :]
        out_ref[pl.ds(pl.multiple_of(384 - column * 128, 128), 128), :] = value[128:, :]


def outputs_grad(place, group, o, dself, dself_other, ca, ca_other, dcross, dcross_other, kind):
    rows, width = dself.shape
    lanes = pl.BlockSpec((rows, 256), lambda i, s: (0, group))
    whole = resident((rows, width))
    return pl.pallas_call(
        functools.partial(outputs_grad_kernel, count=len(o)),
        grid_spec=pltpu.PrefetchScalarGridSpec(
            num_scalar_prefetch=1,
            grid=(1,),
            in_specs=[resident(a.shape) for a in o] + [whole, whole, lanes, lanes, whole, whole],
            out_specs=resident((512, width)),
        ),
        out_shape=shape((512, width), kind),
        compiler_params=params(48),
        cost_estimate=lasting(4.29),
        name="outputs_grad",
    )(place, *o, dself, dself_other, ca, ca_other, dcross, dcross_other)


def middle_back_kernel(place_ref, ym_ref, yr_ref, x1_ref, x2_ref, d_ref, cq_ref, *refs):
    wq, wc = refs[0:6], refs[6:12]
    ck_ref, cv_ref, gain_ref = refs[12:15]
    dx1_ref, dself_ref, dcross_ref, dcq_ref, dck_ref, dcv_ref, sums_ref = refs[15:22]
    dck_all, dcv_all = refs[22:]
    step = pl.program_id(0)

    @pl.when(step == 0)
    def _():
        dck_all[...] = jnp.zeros_like(dck_all)
        dcv_all[...] = jnp.zeros_like(dcv_all)
        sums_ref[...] = jnp.zeros_like(sums_ref)

    y3 = ym_ref[...] + yr_ref[...].astype(FULL)
    scaled, inverse = norm_parts(x2_ref[...])
    sums_ref[4:5, :] += jnp.sum(y3 * scaled, axis=0, keepdims=True)
    sums_ref[5:6, :] += jnp.sum(y3, axis=0, keepdims=True)
    dx2 = d_ref[...].astype(FULL) + norm_pull(y3, scaled, inverse, gain_ref[2:3, :])
    dx1_ref[...] = dx2
    dcross = lower(dx2)
    dcross_ref[...] = dcross
    for g, weight in enumerate(in_groups(wc, 0)):
        lanes = slice(g * 256, (g + 1) * 256)
        dcatt = lower(nt(dcross, weight))
        keys = ck_ref[g]
        cq = cq_ref[:, lanes]
        probability = cross_probability(cq, keys)
        weighed = nt(dcatt, cv_ref[g])
        inner = by_head(probability * weighed, jnp.sum, 0.0)
        dcs = lower(probability * (weighed - inner))
        dcq_ref[:, lanes] = lower(nn(dcs, keys) * HEAD ** (-0.5))
        dck_all[g] += tn(dcs, cq * HEAD ** (-0.5))
        dcv_all[g] += tn(lower(probability), dcatt)
    y2 = 0.0
    for g, weight in enumerate(in_groups(wq, 1)):
        y2 = y2 + nt(dcq_ref[:, g * 256 : (g + 1) * 256], weight)
    scaled, inverse = norm_parts(x1_ref[...])
    sums_ref[2:3, :] += jnp.sum(y2 * scaled, axis=0, keepdims=True)
    sums_ref[3:4, :] += jnp.sum(y2, axis=0, keepdims=True)
    dx1 = dx1_ref[...] + norm_pull(y2, scaled, inverse, gain_ref[1:2, :])
    dx1_ref[...] = dx1
    dself_ref[...] = lower(dx1)

    @pl.when(step == pl.num_programs(0) - 1)
    def _():
        for every, result in ((dck_all, dck_ref), (dcv_all, dcv_ref)):
            for g in range(4):
                total = 0.0
                for h in range(4):
                    lane = lax.broadcasted_iota(jnp.int32, (1, 256), 1) // HEAD
                    total = total + jnp.where(lane == h, every[g, h * 64 : (h + 1) * 64, :], 0.0)
                result[g] = total


def middle_back(place, ym, yr, x1, x2, d, cq, wq, wc, ck, cv, gains):
    rows, width = x1.shape
    block = 416
    wide = rows_of(block, width)
    small = pl.BlockSpec((4, 64, 256), lambda i, s: (0, 0, 0))
    whole = (*wq, *wc, ck, cv, gains)
    return pl.pallas_call(
        middle_back_kernel,
        grid_spec=pltpu.PrefetchScalarGridSpec(
            num_scalar_prefetch=1,
            grid=(rows // block,),
            in_specs=[wide] * 6 + [resident(a.shape) for a in whole],
            out_specs=[wide] * 4 + [small, small, pl.BlockSpec((8, width), lambda i, s: (0, 0))],
            scratch_shapes=[pltpu.VMEM((4, 256, 256), FULL)] * 2,
        ),
        out_shape=[shape((rows, width), FULL)]
        + [shape((rows, width), ROUND)] * 3
        + [shape((4, 64, 256), FULL)] * 2
        + [shape((8, width), FULL)],
        compiler_params=params(56),
        cost_estimate=lasting(24),
        name="middle_back",
    )(place, ym, yr, x1, x2, d, cq, *whole)


def first_back_kernel(place_ref, *refs):
    y_ref = refs[-1]
    y = 0.0
    for n in range(3):
        for c in range(3):
            y = y + nt(refs[3 * n + c][...], refs[9 + n][c])
    y_ref[...] = y.astype(y_ref.dtype)


def first_back(place, grads, weights, kind):
    span = grads[0].shape[0]
    rows = span // 2
    width = weights[0].shape[1]
    block = 416
    steps = rows // block
    return pl.pallas_call(
        first_back_kernel,
        grid_spec=pltpu.PrefetchScalarGridSpec(
            num_scalar_prefetch=1,
            grid=(steps,),
            in_specs=[
                pl.BlockSpec((block, a.shape[1]), lambda i, s: (s[0] * steps + i, 0))
                for a in grads
            ]
            + [resident(a.shape) for a in weights],
            out_specs=rows_of(block, width),
        ),
        out_shape=shape((rows, width), kind),
        compiler_params=params(40),
        cost_estimate=lasting(3.57),
        name="first_back",
    )(place, *grads, *weights)


def frames_back_kernel(place_ref, ym_ref, yr_ref, dx1_ref, frame_ref, gain_ref, out_ref, sums_ref):
    @pl.when(pl.program_id(0) == 0)
    def _():
        sums_ref[...] = jnp.zeros_like(sums_ref)

    y = ym_ref[...] + yr_ref[...].astype(FULL)
    scaled, inverse = norm_parts(frame_ref[...].astype(FULL))
    sums_ref[0:1, :] += jnp.sum(y * scaled, axis=0, keepdims=True)
    sums_ref[1:2, :] += jnp.sum(y, axis=0, keepdims=True)
    out_ref[...] = lower(dx1_ref[...] + norm_pull(y, scaled, inverse, gain_ref[0:1, :]))


def frames_back(place, ym, yr, dx1, frames, gains):
    rows, width = dx1.shape
    block = 208
    wide = rows_of(block, width)
    return pl.pallas_call(
        frames_back_kernel,
        grid_spec=pltpu.PrefetchScalarGridSpec(
            num_scalar_prefetch=1,
            grid=(rows // block,),
            in_specs=[wide] * 4 + [resident(gains.shape)],
            out_specs=[wide, pl.BlockSpec((8, width), lambda i, s: (0, 0))],
        ),
        out_shape=[shape((rows, width), ROUND), shape((8, width), FULL)],
        compiler_params=params(24),
        cost_estimate=lasting(4.29),
        name="frames_back",
    )(place, ym, yr, dx1, frames, gains)


def chip_local(
    frames, text_states, lengths, loss_mask, norm_gain, norm_bias, w_qkv, w_out, w_cross_q,
    w_cross_kv, w_cross_out, w_up, w_down, cotangent,
):
    at = lax.axis_index("narrow")
    core = at % 2
    side = at // 2
    column = lax.axis_index("wide") % 2
    layer = lax.axis_index("wide") // 2
    near = layer % 2
    place = jnp.stack([core, near, column]).astype(jnp.int32)
    away = jnp.stack([1 - core, near, column]).astype(jnp.int32)
    limit = lax.dynamic_slice(lengths, (side,), (1,))
    rows, width = frames.shape
    join = lax.optimization_barrier

    def over_core(v):
        return lax.ppermute(v, "narrow", CORE_PAIRS)

    def over_y(v):
        return lax.ppermute(v, "narrow", Y_PAIRS)

    def along_wide(v, pairs):
        return lax.ppermute(v, "wide", pairs)

    def half_of(v, which, axis=0):
        half = v.shape[axis] // 2
        return lax.dynamic_slice_in_dim(v, which * half, half, axis=axis)

    def ordered(first, second, which):
        return jnp.where(
            which == 0,
            jnp.concatenate([first, second], axis=0),
            jnp.concatenate([second, first], axis=0),
        )

    def over_z(v):
        return along_wide(v, Z_NEAR)

    def over_x(v):
        return along_wide(v, X_PAIRS)

    def away_rows(v):
        return half_of(v, 1 - core)

    def cross_order(v):
        return jnp.where(column == 0, v, jnp.concatenate([v[..., 128:], v[..., :128]], axis=-1))

    qkv_first = over_y(half_of(w_qkv, near, 2))
    frames_other = over_core(frames)
    h1, q0, k0, v0 = first_project(place, frames, frames_other, norm_gain, norm_bias, w_qkv)
    q0, qkv_first, w_out, w_cross_q, w_cross_out, cotangent = join(
        (q0, qkv_first, w_out, w_cross_q, w_cross_out, cotangent)
    )

    qkv_second = over_z(qkv_first)
    out_first = over_y(half_of(w_out, near))
    query_first = over_y(half_of(w_cross_q, column, 1))
    cross_out_first = over_y(half_of(w_cross_out, column))
    o0, lse0 = self_forward(limit, q0, k0, v0)
    qf, kf, vf = project(place, h1, qkv_first)
    out_other, query_other, cross_out_other = map(over_core, (w_out, w_cross_q, w_cross_out))
    qf, o0, out_first, query_first, cross_out_first, w_up, w_down, *core_got = join(
        (qf, o0, out_first, query_first, cross_out_first, w_up, w_down)
        + (out_other, query_other, cross_out_other)
    )

    out_other, query_other, cross_out_other = core_got
    out_second = over_z(out_first)
    query_second = over_x(query_first)
    cross_out_second = over_x(cross_out_first)
    up_first = over_y(half_of(w_up, column, 1))
    down_sent = half_of(w_down, column)
    o0_other = over_core(away_rows(o0))
    keys = keys_of(text_states, w_cross_kv)
    own_keys = lax.dynamic_index_in_dim(keys, side, keepdims=False)
    keys_y = over_y(lax.dynamic_index_in_dim(keys, 1 - side, keepdims=False))
    of, lse_f = self_forward(limit, qf, kf, vf)
    of, qkv_second, keys_y, o0_other = join((of, qkv_second, keys_y, o0_other))

    qs, ks, vs = project(place, h1, qkv_second)
    of_other = over_core(away_rows(of))
    pair = jnp.stack([own_keys, cross_order(keys_y)])
    pair_other = over_core(pair)
    o_s, lse_s = self_forward(limit, qs, ks, vs)
    o_s, out_second, query_second, cross_out_second, up_first, down_sent, pair_other, of_other = join(
        (o_s, out_second, query_second, cross_out_second, up_first, down_sent, pair_other, of_other)
    )

    down_first = over_y(down_sent)
    up_second = over_x(up_first)
    os_other = over_core(away_rows(o_s))
    dout = jnp.where(loss_mask[:, None] != 0, cotangent, jnp.zeros((), ROUND))

    def pieces(own, first, second, own_other):
        return (own, first, second, own_other, over_core(first), over_core(second))

    wo = pieces(w_out, out_first, out_second, out_other)
    wq = pieces(w_cross_q, query_first, query_second, query_other)
    wc = pieces(w_cross_out, cross_out_first, cross_out_second, cross_out_other)
    text = lax.dynamic_index_in_dim(text_states, side, keepdims=False)
    head_of = jnp.arange(256) // HEAD
    same = head_of[:, None] == head_of[None, :]

    def spread_heads(v):
        return jnp.where(same, jnp.tile(v, (1, 4, 1)), jnp.zeros((), ROUND))

    every = jnp.concatenate([pair, pair_other], axis=0)
    ck, cv = spread_heads(every[:, 0]), spread_heads(every[:, 1])
    x1, x2, h2, cq, ca, h3 = middle_forward(
        place, frames, (o0, of, o_s), (o0_other, of_other, os_other), wo, wq, wc, ck, cv,
        norm_gain, norm_bias,
    )
    h3, ca, h2, up_second, down_first, dout = join((h3, ca, h2, up_second, down_first, dout))

    h3_other = over_core(h3)
    dout_other = over_core(dout)
    down_second = over_x(down_first)
    g0, du0, out_m, y_m = feed(place, h3, dout, (w_up,), (w_down,), FULL, 0)
    g0, du0, out_o, y_o = feed(
        place, h3_other, dout_other, (w_up,), (w_down,), FULL, 1, shared=(g0, du0)
    )
    y_o, down_second, ca, h2 = join((y_o, down_second, ca, h2))

    ups = (up_first, up_second)
    downs = (down_first, down_second)
    g1, du1, out_o, y_o = feed(
        place, h3_other, dout_other, ups, downs, ROUND, 1, before=(out_o, y_o)
    )
    y_received = over_core(y_o)
    h2_other = over_core(h2)
    ca_other = over_core(ca[:, 512:])
    g1, du1, out_m, y_m = feed(
        place, h3, dout, ups, downs, FULL, 0, before=(out_m, y_m), shared=(g1, du1)
    )

    def plus(a, b):
        return lower(a.astype(FULL) + b.astype(FULL))

    across = (column, X_PAIRS)
    down_z = (near, Z_NEAR)
    store = {}
    last = []
    free = []

    def order(*names):
        if free:
            return
        names = tuple(dict.fromkeys((*names, *last)))
        for name, value in zip(names, join(tuple(store[name] for name in names))):
            store[name] = value

    def get(*names):
        return tuple(store[name] for name in names)

    def step(results, make, *needs):
        order(*needs)
        made = make()
        made = made if isinstance(made, (tuple, list)) else (made,)
        store.update(zip(results, made))
        last[:] = results[:1]

    class Sum:
        def __init__(self, name, axes=(across, down_z)):
            self.fly, self.kept, self.axes = name + "_fly", name + "_kept", axes

        def over_y(self, partner):
            order(partner)
            store[self.fly] = over_y(store[partner])

        def first(self, own):
            which, pairs = self.axes[0]
            order(self.fly, own)
            mine, fly = get(own, self.fly)
            away_half = plus(half_of(mine, 1 - which), half_of(fly, 1 - which))
            store[self.kept] = half_of(mine, which).astype(FULL) + half_of(fly, which).astype(FULL)
            store[self.fly] = along_wide(away_half, pairs)
            last[:] = [self.kept]

        def first_alone(self, own):
            which, pairs = self.axes[0]
            store[self.kept] = half_of(store[own], which).astype(FULL)
            store[self.fly] = along_wide(half_of(store[own], 1 - which), pairs)
            last[:] = [self.kept]

        def second(self):
            which, pairs = self.axes[1]
            order(self.fly, self.kept)
            total = store[self.kept] + store[self.fly].astype(FULL)
            store[self.kept] = half_of(total, which)
            store[self.fly] = along_wide(lower(half_of(total, 1 - which)), pairs)
            last[:] = [self.kept]

        def add(self, pairs):
            order(self.fly, self.kept)
            store[self.kept] = plus(*get(self.kept, self.fly))
            store[self.fly] = along_wide(store[self.kept], pairs)
            last[:] = [self.kept]

        def far(self):
            self.add(Z_FAR)

        def back(self):
            self.add(self.axes[1][1])

        def along(self):
            order(self.fly, self.kept)
            store[self.kept] = ordered(*get(self.kept, self.fly), self.axes[1][0])
            store[self.fly] = along_wide(store[self.kept], self.axes[0][1])
            last[:] = [self.kept]

        def end(self, result):
            order(self.fly, self.kept)
            store[result] = ordered(*get(self.kept, self.fly), self.axes[0][0]).astype(FULL)
            last[:] = [result]

    class Row:
        def __init__(self, name, value, move):
            self.fly, self.kept = name + "_fly", name + "_kept"
            store[self.kept] = value
            store[self.fly] = move(value)

        def then(self, move):
            order(self.fly, self.kept)
            store[self.kept] = store[self.kept] + store[self.fly]
            store[self.fly] = move(store[self.kept])
            last[:] = [self.kept]

        def total(self):
            return store[self.kept] + store[self.fly]

    up, down, outs, cross_in = Sum("up"), Sum("down"), Sum("outs"), Sum("cross_in")
    qkv = Sum("qkv", (down_z, across))
    store.update(h3_other=h3_other, du1=du1, g1=g1, du0=du0, g0=g0, y_m=y_m, y_fly=y_received)
    store.update(of=of, o_s=o_s, o0=o0, x2=x2, h2_other=h2_other, ca_other=ca_other)

    def middle():
        dx1, *rest = middle_back(
            place, *get("y_m", "y_fly"), x1, store["x2"], dout, cq, wq, wc, ck, cv, norm_gain
        )
        return (rest[0], dx1, *rest[1:])

    step(["up1"], lambda: up_grad(h3, *get("h3_other", "du1"), ROUND), "du1", "du0")
    up.over_y("up1")
    step(["down1"], lambda: down_grad(store["g1"], dout, dout_other, ROUND), "g1")
    step(["dself", "dx1", "dcross", "dcq", "dck", "dcv", "sums"], middle, "y_fly", "y_m", "x2")
    store["dself_other"] = over_core(store["dself"])
    step(["up0"], lambda: up_grad(h3, *get("h3_other", "du0"), ROUND), "du0")
    order(up.fly, "down1", "dself_other")
    down.over_y("down1")
    up.first("up0")
    step(
        ["dof", "dos", "do0"],
        lambda: pull(place, *get("dself", "dself_other"), (out_first, out_second, w_out)),
        "dself",
        "dself_other",
        "dcross",
        "dcq",
    )
    store["dcross_other"] = over_core(store["dcross"])
    store["dcq_other"] = over_core(store["dcq"][:, 512:])
    d_pair = jnp.stack(get("dck", "dcv"), axis=1)
    store["pair_kept"] = d_pair[:2]
    store["pair_fly"] = over_core(d_pair[2:])
    step(
        ["dqf", "dkf", "dvf"],
        lambda: self_back(limit, qf, kf, vf, store["of"], store["dof"], lse_f),
        "dof",
    )
    def query(g):
        return query_grad(place, g, h2, *get("h2_other", "dcq", "dcq_other"), ROUND)

    def outof(g, *o):
        return outputs_grad(
            place, g, get(*o), *get("dself", "dself_other"), ca,
            *get("ca_other", "dcross", "dcross_other"), ROUND,
        )

    step(["query1"], lambda: query(1), "dcq_other", "h2_other", "pair_fly", "pair_kept")
    pair_sum = lower(store["pair_kept"] + store["pair_fly"])
    store["pair"] = pair_sum[0]
    store["pair_other"] = cross_order(pair_sum[1])
    step(
        ["dqs", "dks", "dvs"],
        lambda: self_back(limit, qs, ks, vs, store["o_s"], store["dos"], lse_s),
        "dos",
    )
    up.second()
    step(["down0"], lambda: down_grad(store["g0"], dout, dout_other, ROUND), "g0")
    yp = ("dqf", "dkf", "dvf", "dqs", "dks", "dvs")
    step(["qkv1"], lambda: qkv_grad(place, h1, get(*yp), ROUND), "dqs")
    order(down.fly, "qkv1", "query1", "pair_other")
    store["query_fly"] = over_y(store["query1"])
    store["pair_y"] = over_y(store["pair_other"])
    qkv.over_y("qkv1")
    down.first("down0")
    up.far()
    step(
        ["dq0", "dk0", "dv0"],
        lambda: self_back(limit, q0, k0, v0, store["o0"], store["do0"], lse0),
        "do0",
    )
    down.second()
    step(["outs1"], lambda: outof(1, "of", "o_s"), "dcross_other", "ca_other")
    outs.over_y("outs1")
    step(["query0"], lambda: query(0), "dcq")
    order("query0", "query_fly", "pair", "pair_y")
    other_text = lax.dynamic_index_in_dim(text_states, 1 - side, keepdims=False)
    texts = jnp.concatenate([text, other_text], axis=0)
    pairs = jnp.concatenate(get("pair", "pair_y"), axis=1)
    store["into0"] = jnp.concatenate(
        [
            lower(store["query0"].astype(FULL) + store["query_fly"].astype(FULL)),
            lower(tn(texts, pairs[0])),
            lower(tn(texts, pairs[1])),
        ],
        axis=0,
    )
    cross_in.first_alone("into0")
    up.back()
    text_part = 0.0
    for c in range(2):
        text_part = text_part + nt(pairs[c], w_cross_kv[c])
    text_mine, text_theirs = text_part[:64], text_part[64:]
    text_rows = Row("texts", text_mine, lambda v: over_y(text_theirs))
    last[:] = ["texts_kept"]
    nine = ("dq0", "dk0", "dv0", *yp)
    weights = (w_qkv, qkv_first, qkv_second)
    step(["yo"], lambda: first_back(away, get(*nine), weights, ROUND), "dq0")
    store["yo_fly"] = over_core(store["yo"])
    step(["qkv0"], lambda: qkv_grad(place, h1, get("dq0", "dk0", "dv0"), ROUND), "dq0")
    qkv.first("qkv0")
    down.far()
    cross_in.second()
    up.along()
    store["out_fly"] = over_core(out_o)
    step(["outs0"], lambda: outof(0, "o0"), "dcross")
    outs.first("outs0")
    qkv.second()
    text_rows.then(over_core)
    step(["ym"], lambda: first_back(place, get(*nine), weights, FULL), "dq0")
    cross_in.far()
    step(
        ["grad_frames", "first_sums"],
        lambda: frames_back(place, *get("ym", "yo_fly", "dx1"), frames, norm_gain),
        "ym",
        "yo_fly",
    )
    norms = Row("norms", store["sums"] + store["first_sums"], over_core)
    up.end("grad_up")
    text_grad = lower(text_rows.total())
    text_away = over_y(text_grad)
    grad_text = ordered(text_grad[None], text_away[None], side)
    order("x2", "out_fly")
    out_rows = lower(store["x2"] + out_m + store["out_fly"].astype(FULL))
    free[:] = [True]
    for each in (down, outs, qkv, cross_in):
        if each is outs:
            each.second()
        if each is not cross_in and each is not down:
            each.far()
        each.back()
        each.along()
    for move in (over_y, over_x, over_z, lambda v: along_wide(v, Z_FAR)):
        norms.then(move)
    sums = norms.total()
    down.end("grad_down")
    cross_in.end("grad_in")
    qkv.end("grad_qkv")
    outs.end("grad_outs")
    grad_in, grad_outs = get("grad_in", "grad_outs")
    return (
        out_rows,
        store["grad_frames"],
        grad_text,
        sums[0:6:2],
        sums[1:6:2],
        store["grad_qkv"].reshape(3, width, 256),
        grad_outs[:256],
        grad_in[:width],
        grad_in[width:].reshape(2, width, 256),
        grad_outs[256:],
        store["grad_up"],
        store["grad_down"],
    )


def solution(mesh):
    chips = dict(mesh.shape) == {"wide": 8, "narrow": 4}
    return jax.shard_map(
        chip_local if chips else general_local,
        mesh=mesh,
        in_specs=(
            P(("wide", "narrow"), None),
            P("wide", None, None),
            P("wide"),
            P(("wide", "narrow")),
            P(),
            P(),
            P(None, None, "narrow"),
            P("narrow", None),
            P(None, "narrow"),
            P(None, None, "narrow"),
            P("narrow", None),
            P(None, "narrow"),
            P("narrow", None),
            P(("wide", "narrow"), None),
        ),
        out_specs=(
            P(("wide", "narrow"), None),
            P(("wide", "narrow"), None),
            P("wide", None, None),
            P(),
            P(),
            P(None, None, "narrow"),
            P("narrow", None),
            P(None, "narrow"),
            P(None, None, "narrow"),
            P("narrow", None),
            P(None, "narrow"),
            P("narrow", None),
        ),
        check_vma=False,
    )
```

```python
import functools

import jax
import jax.numpy as jnp
from jax import lax
from jax.experimental import pallas as pl
from jax.experimental.pallas import tpu as pltpu
from jax.sharding import PartitionSpec as P

HEAD = 64


EPS = 1e-05
NEG = -1e30


def lower(values_in):
    return values_in.astype(jnp.bfloat16)


def product(left_side, right_side, transposed):
    if transposed:
        return lax.dot_general(
            left_side, right_side, (((1,), (1,)), ((), ())), preferred_element_type=jnp.float32
        )
    return jnp.dot(left_side, right_side, preferred_element_type=jnp.float32)


def outer_sum(left_side, right_side):
    return lax.dot_general(
        left_side, right_side, (((0,), (0,)), ((), ())), preferred_element_type=jnp.float32
    )


def normalize(values_in, gain_row, bias_row):
    row_mean = jnp.mean(values_in, axis=-1, keepdims=True)
    centered = values_in - row_mean
    inverse = lax.rsqrt(jnp.mean(centered * centered, axis=-1, keepdims=True) + EPS)
    scaled = centered * inverse
    return (scaled * gain_row + bias_row, scaled, inverse)


def normalize_back(upstream, scaled, inverse, gain_row):
    weighted = upstream * gain_row
    inner_mean = jnp.mean(weighted, axis=-1, keepdims=True)
    along_mean = jnp.mean(weighted * scaled, axis=-1, keepdims=True)
    grad_input = inverse * (weighted - inner_mean - scaled * along_mean)
    return (grad_input, jnp.sum(upstream * scaled, axis=0), jnp.sum(upstream, axis=0))


def gelu_parts(values_in):
    normal_cdf = 0.5 * (1.0 + jax.scipy.special.erf(values_in * 0.7071067811865476))
    normal_pdf = jnp.exp(-0.5 * values_in * values_in) * 0.3989422804014327
    return (values_in * normal_cdf, normal_cdf + values_in * normal_pdf)


def scores_of(query_part, key_part, valid):
    scores = jnp.einsum(
        "bhe,khe->hbk", query_part, key_part, preferred_element_type=jnp.float32
    ) * HEAD ** (-0.5)
    return jnp.where(valid, scores, NEG)


def attend(query_part, key_part, value_part, valid):
    scores = scores_of(query_part, key_part, valid)
    row_top = jnp.max(scores, axis=-1, keepdims=True)
    weights_exp = jnp.exp(scores - row_top)
    denominator = jnp.sum(weights_exp, axis=-1, keepdims=True)
    probability = weights_exp / denominator
    mixed = jnp.einsum(
        "hbk,khe->bhe", lower(probability), value_part, preferred_element_type=jnp.float32
    )
    return (lower(mixed), (row_top + jnp.log(denominator))[..., 0])


def attend_back(query_part, key_part, value_part, valid, summary, upstream):
    scores = scores_of(query_part, key_part, valid)
    probability = jnp.exp(scores - summary[..., None])
    pressure = jnp.einsum("bhe,khe->hbk", upstream, value_part, preferred_element_type=jnp.float32)
    grad_scores = lower(
        probability * (pressure - jnp.sum(probability * pressure, axis=-1, keepdims=True))
    )
    factor = HEAD ** (-0.5)
    grad_query = (
        jnp.einsum("hbk,khe->bhe", grad_scores, key_part, preferred_element_type=jnp.float32)
        * factor
    )
    grad_key = (
        jnp.einsum("hbk,bhe->khe", grad_scores, query_part, preferred_element_type=jnp.float32)
        * factor
    )
    grad_value = jnp.einsum(
        "hbk,bhe->khe", lower(probability), upstream, preferred_element_type=jnp.float32
    )
    return (grad_query, grad_key, grad_value)


def general_local(
    frames,
    text_states,
    lengths,
    loss_mask,
    norm_gain,
    norm_bias,
    w_qkv,
    w_out,
    w_cross_q,
    w_cross_kv,
    w_cross_out,
    w_up,
    w_down,
    cotangent,
):
    row_count = frames.shape[0]
    width = frames.shape[1]
    item_count = lengths.shape[0]
    span = row_count * lax.axis_size("narrow") // item_count
    half_span = span // 2
    inner_width = w_qkv.shape[2]
    head_count = inner_width // HEAD
    text_count = text_states.shape[1]
    full_rows = item_count * span
    places = jnp.arange(span, dtype=jnp.int32)

    def spread(shard_rows):
        return lax.all_gather(shard_rows, "narrow", axis=0, tiled=True)

    def collect(left_side, right_side, transposed):
        return lax.psum_scatter(
            product(
                lax.slice_in_dim(left_side, 0, lax.axis_size("narrow") * row_count, axis=0),
                right_side,
                transposed,
            ),
            "narrow",
            scatter_dimension=0,
            tiled=True,
        )

    def causal(block_index, item_limit):
        query_place = block_index * half_span + jnp.arange(half_span, dtype=jnp.int32)
        return (places[None, :] <= query_place[:, None]) & (places[None, :] < item_limit)

    frame_rows = frames.astype(jnp.float32)
    normed_one, scaled_one, inverse_one = normalize(frame_rows, norm_gain[0], norm_bias[0])
    first_input = spread(lower(normed_one))
    triple = lower(
        jnp.einsum("rd,cde->cre", first_input, w_qkv, preferred_element_type=jnp.float32)
    )
    triple = triple.reshape(3, item_count, span, head_count, HEAD)

    def self_item(packed):
        query_part, key_part, value_part, item_limit = packed
        mixed_list = []
        summary_list = []
        for block_index in range(2):
            mixed, summary = attend(
                query_part[block_index * half_span : (block_index + 1) * half_span],
                key_part,
                value_part,
                causal(block_index, item_limit),
            )
            mixed_list.append(mixed)
            summary_list.append(summary)
        return (jnp.concatenate(mixed_list, axis=0), jnp.stack(summary_list, axis=0))

    attended, self_summary = lax.map(self_item, (triple[0], triple[1], triple[2], lengths))
    attended_flat = attended.reshape(full_rows, inner_width)
    first_rows = frame_rows + collect(attended_flat, w_out, False)
    normed_two, scaled_two, inverse_two = normalize(first_rows, norm_gain[1], norm_bias[1])
    second_input = spread(lower(normed_two))
    cross_query = lower(product(second_input, w_cross_q, False)).reshape(
        item_count, span, head_count, HEAD
    )
    cross_pair = lower(
        jnp.einsum("ntd,cde->cnte", text_states, w_cross_kv, preferred_element_type=jnp.float32)
    )
    cross_pair = cross_pair.reshape(2, item_count, text_count, head_count, HEAD)

    def cross_item(packed):
        query_part, key_part, value_part = packed
        return attend(query_part, key_part, value_part, True)

    cross_mixed, cross_summary = lax.map(cross_item, (cross_query, cross_pair[0], cross_pair[1]))
    cross_flat = cross_mixed.reshape(full_rows, inner_width)
    second_rows = first_rows + collect(cross_flat, w_cross_out, False)
    normed_three, scaled_three, inverse_three = normalize(second_rows, norm_gain[2], norm_bias[2])
    upstream = cotangent.astype(jnp.float32) * loss_mask.astype(jnp.float32)[:, None]
    ffn_grad = lower(upstream)
    ffn_input = spread(lower(normed_three))
    hidden_pre = product(ffn_input, w_up, False)
    active, slope = gelu_parts(hidden_pre)
    active = lower(active)
    out_rows = second_rows + collect(active, w_down, False)
    ffn_full = spread(ffn_grad)
    grad_down = outer_sum(active, ffn_full)
    grad_hidden = lower(product(ffn_full, w_down, True) * slope)
    grad_up = outer_sum(ffn_input, grad_hidden)
    back_three = collect(grad_hidden, w_up, True)
    grad_up, grad_down = (grad_up, grad_down)
    grad_in_three, gain_three, bias_three = normalize_back(
        back_three, scaled_three, inverse_three, norm_gain[2]
    )
    grad_second = upstream + grad_in_three
    cross_full = spread(lower(grad_second))
    grad_cross_out = outer_sum(cross_flat, cross_full)
    cross_upstream = lower(product(cross_full, w_cross_out, True)).reshape(
        item_count, span, head_count, HEAD
    )

    def cross_back(packed):
        query_part, key_part, value_part, summary, upstream_item = packed
        return attend_back(query_part, key_part, value_part, True, summary, upstream_item)

    grad_cq, grad_ck, grad_cv = lax.map(
        cross_back, (cross_query, cross_pair[0], cross_pair[1], cross_summary, cross_upstream)
    )
    grad_cq = lower(grad_cq).reshape(full_rows, inner_width)
    grad_pair = lower(jnp.stack((grad_ck, grad_cv), axis=0)).reshape(
        2, item_count, text_count, inner_width
    )
    grad_cross_q = outer_sum(second_input, grad_cq)
    grad_cross_kv = jnp.einsum(
        "ntd,cnte->cde", text_states, grad_pair, preferred_element_type=jnp.float32
    )
    grad_cross_q, grad_cross_kv, grad_cross_out = (grad_cross_q, grad_cross_kv, grad_cross_out)
    text_partial = jnp.einsum(
        "cnte,cde->ntd", grad_pair, w_cross_kv, preferred_element_type=jnp.float32
    )
    grad_text = lower(lax.psum(text_partial, "narrow"))
    back_two = collect(grad_cq, w_cross_q, True)
    grad_in_two, gain_two, bias_two = normalize_back(
        back_two, scaled_two, inverse_two, norm_gain[1]
    )
    grad_first = grad_second + grad_in_two
    self_full = spread(lower(grad_first))
    grad_out = outer_sum(attended_flat, self_full)
    self_upstream = lower(product(self_full, w_out, True)).reshape(
        item_count, span, head_count, HEAD
    )

    def self_back(packed):
        query_part, key_part, value_part, item_limit, summary, upstream_item = packed
        query_list = []
        key_list = []
        value_list = []
        for block_index in range(2):
            lower_row = block_index * half_span
            grad_query, grad_key, grad_value = attend_back(
                query_part[lower_row : lower_row + half_span],
                key_part,
                value_part,
                causal(block_index, item_limit),
                summary[block_index],
                upstream_item[lower_row : lower_row + half_span],
            )
            query_list.append(grad_query)
            key_list.append(grad_key)
            value_list.append(grad_value)
        return (
            jnp.concatenate(query_list, axis=0),
            key_list[0] + key_list[1],
            value_list[0] + value_list[1],
        )

    grad_q, grad_k, grad_v = lax.map(
        self_back, (triple[0], triple[1], triple[2], lengths, self_summary, self_upstream)
    )
    grad_triple = lower(jnp.stack((grad_q, grad_k, grad_v), axis=0)).reshape(
        3, full_rows, inner_width
    )
    grad_qkv = jnp.einsum(
        "rd,cre->cde", first_input, grad_triple, preferred_element_type=jnp.float32
    )
    grad_qkv, grad_out = (grad_qkv, grad_out)
    merged = grad_triple.transpose(1, 0, 2).reshape(full_rows, 3 * inner_width)
    stacked_weights = w_qkv.transpose(0, 2, 1).reshape(3 * inner_width, width)
    back_one = collect(merged, stacked_weights, False)
    grad_in_one, gain_one, bias_one = normalize_back(
        back_one, scaled_one, inverse_one, norm_gain[0]
    )
    grad_frames = lower(grad_first + grad_in_one)
    gain_terms = jnp.stack((gain_one, gain_two, gain_three), axis=0)
    bias_terms = jnp.stack((bias_one, bias_two, bias_three), axis=0)
    grad_norm_gain, grad_norm_bias = lax.psum((gain_terms, bias_terms), ("wide", "narrow"))
    grad_qkv, grad_out, grad_cross_q, grad_cross_kv, grad_cross_out, grad_up, grad_down = lax.psum(
        (grad_qkv, grad_out, grad_cross_q, grad_cross_kv, grad_cross_out, grad_up, grad_down),
        "wide",
    )
    return (
        lower(out_rows),
        grad_frames,
        grad_text,
        grad_norm_gain,
        grad_norm_bias,
        grad_qkv,
        grad_out,
        grad_cross_q,
        grad_cross_kv,
        grad_cross_out,
        grad_up,
        grad_down,
    )


ROUND = jnp.bfloat16
FULL = jnp.float32
CORE_PAIRS = ((0, 1), (1, 0), (2, 3), (3, 2))
Y_PAIRS = ((0, 2), (2, 0), (1, 3), (3, 1))
X_PAIRS = tuple((i, i ^ 1) for i in range(8))
Z_INWARD = ((0, 2), (1, 3), (6, 4), (7, 5))
Z_MIDDLE = ((2, 4), (4, 2), (3, 5), (5, 3))
Z_OUTWARD = ((2, 0), (3, 1), (4, 6), (5, 7))
Z_NEAR = tuple((i, i ^ 2) for i in range(8))
Z_FAR = tuple((i, i ^ 4) for i in range(8))
MIB = 1 << 20


def nt(a, b):
    return lax.dot_general(a, b, (((1,), (1,)), ((), ())), preferred_element_type=FULL)


def nn(a, b):
    return lax.dot_general(a, b, (((1,), (0,)), ((), ())), preferred_element_type=FULL)


def tn(a, b):
    return lax.dot_general(a, b, (((0,), (0,)), ((), ())), preferred_element_type=FULL)


def shape(dims, kind):
    return jax.ShapeDtypeStruct(dims, kind)


def resident(dims):
    zeros = (0,) * len(dims)
    return pl.BlockSpec(dims, lambda i, s: zeros, pipeline_mode=pl.Buffered(1))


def rows_of(block, width):
    return pl.BlockSpec((block, width), lambda i, s: (i, 0))


def lasting(microseconds):
    flops = int(microseconds * 0.28 * 1.15e9)
    return pl.CostEstimate(flops=flops, bytes_accessed=1000, transcendentals=0)


def params(mib):
    return pltpu.CompilerParams(vmem_limit_bytes=mib * MIB)


def norm_parts(v):
    centered = v - jnp.mean(v, axis=-1, keepdims=True)
    inverse = lax.rsqrt(jnp.mean(centered * centered, axis=-1, keepdims=True) + EPS)
    return centered * inverse, inverse


def norm_pull(y, scaled, inverse, gain_row):
    weighted = y * gain_row
    inner = jnp.mean(weighted, axis=-1, keepdims=True)
    along = jnp.mean(weighted * scaled, axis=-1, keepdims=True)
    return inverse * (weighted - inner - scaled * along)


def first_project_kernel(
    place_ref, mine_ref, other_ref, gain_ref, bias_ref, weight_ref, h_ref, *out_refs
):
    half = pl.program_id(0)

    def run(source):
        for start in range(0, source.shape[0], 208):
            part = slice(start, start + 208)
            scaled, _ = norm_parts(source[part, :].astype(FULL))
            h = lower(scaled * gain_ref[0:1, :] + bias_ref[0:1, :])
            h_ref[part, :] = h
            for c, out_ref in enumerate(out_refs):
                out_ref[part, :] = lower(nn(h, weight_ref[c]))

    @pl.when(half == 0)
    def _():
        run(mine_ref)

    @pl.when(half == 1)
    def _():
        run(other_ref)


def first_project(place, mine, other, gains, biases, weights):
    rows, depth = mine.shape
    count, _, wide = weights.shape
    out = pl.BlockSpec((rows, wide), lambda i, s: ((i + s[0]) % 2, 0))
    return pl.pallas_call(
        first_project_kernel,
        grid_spec=pltpu.PrefetchScalarGridSpec(
            num_scalar_prefetch=1,
            grid=(2,),
            in_specs=[resident(a.shape) for a in (mine, other, gains, biases, weights)],
            out_specs=[rows_of(rows, depth)] + [out] * count,
        ),
        out_shape=[shape((2 * rows, depth), ROUND)] + [shape((2 * rows, wide), ROUND)] * count,
        compiler_params=params(40),
        cost_estimate=lasting(5),
        name="first_project",
    )(place, mine, other, gains, biases, weights)


def project_kernel(place_ref, h_ref, weight_ref, *out_refs):
    count = len(out_refs)
    wide = weight_ref.shape[2]
    weights = jnp.concatenate([weight_ref[c] for c in range(count)], axis=1)
    for start in range(0, h_ref.shape[0], 416):
        part = slice(start, start + 416)
        result = lower(nn(h_ref[part, :], weights))
        for c, out_ref in enumerate(out_refs):
            out_ref[part, :] = result[:, c * wide : (c + 1) * wide]


def project(place, h, weights):
    rows, depth = h.shape[0] // 2, h.shape[1]
    count, _, wide = weights.shape
    out = pl.BlockSpec((rows, wide), lambda i, s: ((i + s[0]) % 2, 0))
    return pl.pallas_call(
        project_kernel,
        grid_spec=pltpu.PrefetchScalarGridSpec(
            num_scalar_prefetch=1,
            grid=(2,),
            in_specs=[rows_of(rows, depth), resident(weights.shape)],
            out_specs=[out] * count,
        ),
        out_shape=[shape((2 * rows, wide), ROUND)] * count,
        compiler_params=params(40),
        cost_estimate=lasting(4),
        name="project",
    )(place, h, weights)


def pull_kernel(place_ref, mine_ref, other_ref, *refs):
    half = pl.program_id(0)
    count = len(refs) // 2

    def run(source):
        for weight_ref, out_ref in zip(refs[:count], refs[count:]):
            out_ref[...] = lower(nt(source[...], weight_ref[...]))

    @pl.when(half == 0)
    def _():
        run(mine_ref)

    @pl.when(half == 1)
    def _():
        run(other_ref)


def pull(place, mine, other, weights):
    rows = mine.shape[0]
    return pl.pallas_call(
        pull_kernel,
        grid_spec=pltpu.PrefetchScalarGridSpec(
            num_scalar_prefetch=1,
            grid=(2,),
            in_specs=[resident(a.shape) for a in (mine, other, *weights)],
            out_specs=[
                pl.BlockSpec((rows, a.shape[0]), lambda i, s: ((i + s[0]) % 2, 0)) for a in weights
            ],
        ),
        out_shape=[shape((2 * rows, a.shape[0]), ROUND) for a in weights],
        compiler_params=params(32),
        cost_estimate=lasting(0.375),
        name="pull",
    )(place, mine, other, *weights)


def blocks_of(span, block):
    return [(start, min(block, span - start)) for start in range(0, span, block)]


def self_forward_kernel(
    limit_ref, q_ref, k_ref, v_ref, o_ref, lse_ref, *, span, floor, block
):
    limit = limit_ref[0]
    lane = lax.broadcasted_iota(jnp.int32, (1, 128), 1)
    row = lax.broadcasted_iota(jnp.int32, (128, 1), 0)
    zero = jnp.zeros((), ROUND)
    value_turned = v_ref[...].T
    for start, size in blocks_of(span, block):
        end = start + size
        mixed_list = []
        for h in range(2):
            own_lanes = (lane < HEAD) if h == 0 else (lane >= HEAD)
            query = jnp.where(own_lanes, q_ref[start:end, :] * HEAD ** (-0.5), zero)
            parts = []
            for low in range(0, end, block):
                high = min(low + block, end)
                scores = nt(k_ref[low:high, :], query)
                if low == start:
                    key = lax.broadcasted_iota(jnp.int32, (size, size), 0)
                    valid = key <= lax.broadcasted_iota(jnp.int32, (size, size), 1)
                    if high > floor:
                        valid = valid & (key + low < limit)
                    scores = jnp.where(valid, scores, NEG)
                elif high > floor:
                    key = lax.broadcasted_iota(jnp.int32, (high - low, 1), 0)
                    scores = jnp.where(key + low < limit, scores, NEG)
                parts.append((low, high, scores))
            top = functools.reduce(
                jnp.maximum, [jnp.max(s, axis=0, keepdims=True) for _, _, s in parts]
            )
            total = 0.0
            mixed = 0.0
            for low, high, scores in parts:
                weights_exp = jnp.exp(scores - top)
                total = total + jnp.sum(weights_exp, axis=0, keepdims=True)
                mixed = mixed + nn(value_turned[:, low:high], lower(weights_exp))
            mixed_list.append(mixed / total)
            lse_ref[0, h : h + 1, start:end] = top + jnp.log(total)
        o_ref[start:end, :] = lower(jnp.where(row < HEAD, mixed_list[0], mixed_list[1]).T)


def self_forward(limit, q, k, v):
    span, wide = q.shape
    pairs = wide // 128
    floor = (span - span // 8 + 1) // 128 * 128
    pair = pl.BlockSpec((span, 128), lambda p, s: (0, p))
    return pl.pallas_call(
        functools.partial(self_forward_kernel, span=span, floor=floor, block=512),
        grid_spec=pltpu.PrefetchScalarGridSpec(
            num_scalar_prefetch=1,
            grid=(pairs,),
            in_specs=[pair] * 3,
            out_specs=[pair, pl.BlockSpec((1, 8, span), lambda p, s: (p, 0, 0))],
        ),
        out_shape=[shape((span, wide), ROUND), shape((pairs, 8, span), FULL)],
        compiler_params=params(56),
        cost_estimate=lasting(7.3 * pairs),
        name="self_forward",
    )(limit, q, k, v)


def self_back_kernel(
    limit_ref, q_ref, k_ref, v_ref, o_ref, do_ref, lse_ref, dq_ref, dk_ref, dv_ref, dqt,
    *, span, floor, block
):
    limit = limit_ref[0]
    lane = lax.broadcasted_iota(jnp.int32, (1, 128), 1)
    row = lax.broadcasted_iota(jnp.int32, (128, 1), 0)
    zero = jnp.zeros((), ROUND)
    factor = HEAD ** (-0.5)
    product_rows = do_ref[...].astype(FULL) * o_ref[...].astype(FULL)
    high = lower(product_rows)
    rest = lower(product_rows - high.astype(FULL))
    pick = lower(
        jnp.concatenate(
            [
                jnp.where(lane < HEAD, 1.0, 0.0),
                jnp.where(lane >= HEAD, 1.0, 0.0),
                jnp.zeros((6, 128), FULL),
            ],
            axis=0,
        )
    )
    delta = nt(pick, high) + nt(pick, rest)
    for start, size in blocks_of(span, block):
        end = start + size
        key = k_ref[start:end, :]
        value = v_ref[start:end, :]
        key_turned = key.T
        dk = 0.0
        dv = 0.0
        dq_add = 0.0
        for h in range(2):
            own_lanes = (lane < HEAD) if h == 0 else (lane >= HEAD)
            own_rows = (row < HEAD) if h == 0 else (row >= HEAD)
            query = jnp.where(own_lanes, q_ref[start:, :] * factor, zero)
            pulled = jnp.where(own_lanes, do_ref[start:, :], zero)
            probability = jnp.exp(nt(key, query) - lse_ref[0, h : h + 1, start:])
            pressure = nt(value, pulled)
            below = lax.broadcasted_iota(jnp.int32, (size, size), 0)
            across = lax.broadcasted_iota(jnp.int32, (size, size), 1)
            corner = jnp.where(below <= across, probability[:, :size], 0.0)
            if end < span:
                probability = jnp.concatenate([corner, probability[:, size:]], axis=1)
            else:
                probability = corner
            if end > floor:
                place = lax.broadcasted_iota(jnp.int32, (size, 1), 0) + start
                probability = jnp.where(place < limit, probability, 0.0)
            grad_scores = lower(probability * (pressure - delta[h : h + 1, start:]))
            dv = dv + nn(lower(probability), pulled)
            dk = dk + nn(grad_scores, query)
            dq_add = dq_add + nn(jnp.where(own_rows, key_turned, zero), grad_scores)
        dk_ref[start:end, :] = lower(dk)
        dv_ref[start:end, :] = lower(dv)
        if start == 0:
            dqt[...] = dq_add
        else:
            dqt[:, start:] += dq_add
    dq_ref[...] = lower(dqt[...].T * factor)


def self_back(limit, q, k, v, o, do, lse):
    span, wide = q.shape
    pairs = wide // 128
    floor = (span - span // 8 + 1) // 128 * 128
    pair = pl.BlockSpec((span, 128), lambda p, s: (0, p))
    return pl.pallas_call(
        functools.partial(self_back_kernel, span=span, floor=floor, block=256),
        grid_spec=pltpu.PrefetchScalarGridSpec(
            num_scalar_prefetch=1,
            grid=(pairs,),
            in_specs=[pair] * 5 + [pl.BlockSpec((1, 8, span), lambda p, s: (p, 0, 0))],
            out_specs=[pair] * 3,
            scratch_shapes=[pltpu.VMEM((128, span), FULL)],
        ),
        out_shape=[shape((span, wide), ROUND)] * 3,
        compiler_params=params(48),
        cost_estimate=lasting(1.050 * pairs),
        name="self_back",
    )(limit, q, k, v, o, do, lse)


def by_head(values_in, reduce, empty):
    lane = lax.broadcasted_iota(jnp.int32, (1, 128), 1)
    pieces = []
    for start in range(0, values_in.shape[1], 128):
        part = values_in[:, start : start + 128]
        first = reduce(jnp.where(lane < HEAD, part, empty), axis=1, keepdims=True)
        second = reduce(jnp.where(lane >= HEAD, part, empty), axis=1, keepdims=True)
        pieces.append(jnp.where(lane < HEAD, first, second))
    return jnp.concatenate(pieces, axis=1)


def cross_probability(query, keys):
    scores = nt(query * HEAD ** (-0.5), keys)
    weights_exp = jnp.exp(scores - by_head(scores, jnp.max, NEG))
    return weights_exp / by_head(weights_exp, jnp.sum, 0.0)


def in_groups(refs, axis):
    for at in (0, 3):
        yield refs[at][...]
        yield jnp.concatenate([refs[at + 1][...], refs[at + 2][...]], axis=axis)


def middle_forward_kernel(place_ref, frame_ref, *refs):
    mixed, wo, wq, wc = refs[0:6], refs[6:12], refs[12:18], refs[18:24]
    ck_ref, cv_ref, gain_ref, bias_ref = refs[24:28]
    x1_ref, x2_ref, h2_ref, cq_ref, ca_ref, h3_ref = refs[28:]
    x1 = frame_ref[...].astype(FULL)
    for o, weight in zip(in_groups(mixed, 1), in_groups(wo, 0)):
        x1 = x1 + nn(o, weight)
    x1_ref[...] = x1
    scaled, _ = norm_parts(x1)
    h2 = lower(scaled * gain_ref[1:2, :] + bias_ref[1:2, :])
    h2_ref[...] = h2
    for g, weight in enumerate(in_groups(wq, 1)):
        lanes = slice(g * 256, (g + 1) * 256)
        cq = lower(nn(h2, weight))
        cq_ref[:, lanes] = cq
        probability = cross_probability(cq, ck_ref[g])
        ca_ref[:, lanes] = lower(nn(lower(probability), cv_ref[g]))
    crossed = 0.0
    for g, weight in enumerate(in_groups(wc, 0)):
        crossed = crossed + nn(ca_ref[:, g * 256 : (g + 1) * 256], weight)
    x2 = x1_ref[...] + crossed
    x2_ref[...] = x2
    scaled, _ = norm_parts(x2)
    h3_ref[...] = lower(scaled * gain_ref[2:3, :] + bias_ref[2:3, :])


def middle_forward(place, frames, attended, received, wo, wq, wc, ck, cv, gains, biases):
    rows, width = frames.shape
    block = 416
    steps = rows // block
    wide = rows_of(block, width)
    whole = (*wo, *wq, *wc, ck, cv, gains, biases)
    return pl.pallas_call(
        middle_forward_kernel,
        grid_spec=pltpu.PrefetchScalarGridSpec(
            num_scalar_prefetch=1,
            grid=(steps,),
            in_specs=[wide]
            + [
                pl.BlockSpec((block, a.shape[1]), lambda i, s: (s[0] * steps + i, 0))
                for a in attended
            ]
            + [rows_of(block, a.shape[1]) for a in received]
            + [resident(a.shape) for a in whole],
            out_specs=[wide] * 6,
        ),
        out_shape=[shape((rows, width), FULL)] * 2 + [shape((rows, width), ROUND)] * 4,
        compiler_params=params(56),
        cost_estimate=lasting(22),
        name="middle_forward",
    )(place, frames, *attended, *received, *whole)


def keys_kernel(text_ref, weight_ref, out_ref):
    for item in range(2):
        for c in range(2):
            out_ref[item, c] = lower(nn(text_ref[item], weight_ref[c]))


def keys_of(text_states, weights):
    items, states, _ = text_states.shape
    return pl.pallas_call(
        keys_kernel,
        out_shape=shape((items, 2, states, weights.shape[2]), ROUND),
        compiler_params=params(24),
        cost_estimate=lasting(2),
        name="keys_of",
    )(text_states, weights)


def feed_kernel(place_ref, h_ref, d_ref, *refs, parts, carried):
    ups, downs = refs[:parts], refs[parts : 2 * parts]
    before = refs[2 * parts : 2 * parts + carried]
    g_ref, du_ref, out_ref, y_ref = refs[-4:]
    h = h_ref[...]
    d = d_ref[...]
    out = 0.0
    y = 0.0
    for n, (up_ref, down_ref) in enumerate(zip(ups, downs)):
        size = down_ref.shape[0]
        if parts == 1:
            lanes = slice(0, size)
        else:
            column = place_ref[2]
            which = column if n == 0 else 1 - column
            lanes = pl.ds(pl.multiple_of(which * size, 128), size)
        u = nn(h, up_ref[...])
        active, slope = gelu_parts(u)
        g = lower(active)
        g_ref[:, lanes] = g
        du = lower(nt(d, down_ref[...]) * slope)
        du_ref[:, lanes] = du
        out = out + nn(g, down_ref[...])
        y = y + nt(du, up_ref[...])
    if carried:
        out = before[0][...] + out
        y = before[1][...] + y
    out_ref[...] = out.astype(out_ref.dtype)
    y_ref[...] = y.astype(y_ref.dtype)


def feed(place, h, d, ups, downs, kind, half, before=(), shared=()):
    rows, width = h.shape
    block = 416
    steps = rows // block
    hidden = sum(a.shape[0] for a in downs)
    wide = rows_of(block, width)
    kept = pl.BlockSpec((block, hidden), lambda i, s: (i + half * steps, 0))
    there = pl.BlockSpec(memory_space=pl.ANY)
    parts = len(ups)
    at = 3 + 2 * parts + len(before)
    return pl.pallas_call(
        functools.partial(feed_kernel, parts=parts, carried=len(before)),
        grid_spec=pltpu.PrefetchScalarGridSpec(
            num_scalar_prefetch=1,
            grid=(steps,),
            in_specs=[wide, wide]
            + [resident(a.shape) for a in (*ups, *downs)]
            + [wide] * len(before)
            + [there] * len(shared),
            out_specs=[kept, kept, wide, wide],
        ),
        out_shape=[shape((2 * rows, hidden), ROUND)] * 2 + [shape((rows, width), kind)] * 2,
        input_output_aliases={at: 0, at + 1: 1} if shared else {},
        compiler_params=params(58),
        cost_estimate=lasting(13),
        name="feed",
    )(place, h, d, *ups, *downs, *before, *shared)


def up_grad_kernel(mine_ref, other_ref, du_ref, out_ref):
    rows = mine_ref.shape[0]
    total = tn(mine_ref[...], du_ref[:rows, :]) + tn(other_ref[...], du_ref[rows:, :])
    out_ref[...] = total.astype(out_ref.dtype)


def up_grad(mine, other, du, kind):
    rows, width = mine.shape
    hidden = du.shape[1]
    tile = 512
    whole = pl.BlockSpec((rows, width), lambda i: (0, 0), pipeline_mode=pl.Buffered(1))
    return pl.pallas_call(
        up_grad_kernel,
        grid=(hidden // tile,),
        in_specs=[whole, whole, pl.BlockSpec((2 * rows, tile), lambda i: (0, i))],
        out_specs=pl.BlockSpec((width, tile), lambda i: (0, i)),
        out_shape=shape((width, hidden), kind),
        compiler_params=params(48),
        cost_estimate=lasting(0.750),
        name="up_grad",
    )(mine, other, du)


def down_grad_kernel(g_ref, mine_ref, other_ref, out_ref):
    rows = mine_ref.shape[0]
    total = tn(g_ref[:rows, :], mine_ref[...]) + tn(g_ref[rows:, :], other_ref[...])
    out_ref[...] = total.astype(out_ref.dtype)


def down_grad(g, mine, other, kind):
    rows, width = mine.shape
    hidden = g.shape[1]
    tile = 512
    whole = pl.BlockSpec((rows, width), lambda i: (0, 0), pipeline_mode=pl.Buffered(1))
    return pl.pallas_call(
        down_grad_kernel,
        grid=(hidden // tile,),
        in_specs=[pl.BlockSpec((2 * rows, tile), lambda i: (0, i)), whole, whole],
        out_specs=pl.BlockSpec((tile, width), lambda i: (i, 0)),
        out_shape=shape((hidden, width), kind),
        compiler_params=params(48),
        cost_estimate=lasting(0.750),
        name="down_grad",
    )(g, mine, other)


def qkv_grad_kernel(place_ref, h_ref, *refs):
    out_ref = refs[-1]
    rows, width = h_ref.shape[0] // 2, h_ref.shape[1]
    core, near = place_ref[0], place_ref[1]
    halves = (len(refs) - 1) // 3
    total = [0.0] * 3
    for half in range(2):
        turned = h_ref[half * rows : (half + 1) * rows, :].T
        at = pl.multiple_of((core if half == 0 else 1 - core) * rows, 16)
        for c in range(3):
            parts = [refs[3 * n + c][pl.ds(at, rows), :] for n in range(halves)]
            grads = parts[0] if halves == 1 else jnp.concatenate(parts, axis=1)
            total[c] = total[c] + nn(turned, grads)
    for c in range(3):
        part = slice(c * width, (c + 1) * width)
        value = total[c].astype(out_ref.dtype)
        if halves == 1:
            out_ref[part, :] = value
        else:
            out_ref[part, pl.ds(pl.multiple_of(near * 128, 128), 128)] = value[:, :128]
            out_ref[part, pl.ds(pl.multiple_of((1 - near) * 128, 128), 128)] = value[:, 128:]


def qkv_grad(place, h, grads, kind):
    width = h.shape[1]
    return pl.pallas_call(
        qkv_grad_kernel,
        grid_spec=pltpu.PrefetchScalarGridSpec(
            num_scalar_prefetch=1,
            grid=(1,),
            in_specs=[resident(a.shape) for a in (h, *grads)],
            out_specs=resident((3 * width, 256)),
        ),
        out_shape=shape((3 * width, 256), kind),
        compiler_params=params(48),
        cost_estimate=lasting(0.750),
        name="qkv_grad",
    )(place, h, *grads)


def query_grad_kernel(place_ref, mine_ref, other_ref, dm_ref, do_ref, out_ref, *, split):
    column = place_ref[2]
    total = tn(mine_ref[...], dm_ref[...]) + tn(other_ref[...], do_ref[...])
    value = total.astype(out_ref.dtype)
    if split:
        out_ref[:, pl.ds(pl.multiple_of(column * 128, 128), 128)] = value[:, :128]
        out_ref[:, pl.ds(pl.multiple_of((1 - column) * 128, 128), 128)] = value[:, 128:]
    else:
        out_ref[...] = value


def query_grad(place, group, mine, other, d_mine, d_other, kind):
    rows, width = mine.shape
    lanes = pl.BlockSpec((rows, 256), lambda i, s: (0, group))
    return pl.pallas_call(
        functools.partial(query_grad_kernel, split=group == 1),
        grid_spec=pltpu.PrefetchScalarGridSpec(
            num_scalar_prefetch=1,
            grid=(1,),
            in_specs=[resident(mine.shape), resident(other.shape), lanes, lanes],
            out_specs=resident((width, 256)),
        ),
        out_shape=shape((width, 256), kind),
        compiler_params=params(48),
        cost_estimate=lasting(0.429),
        name="query_grad",
    )(place, mine, other, d_mine, d_other)


def outputs_grad_kernel(place_ref, *refs, count):
    o_refs = refs[:count]
    sm_ref, so_ref, am_ref, ao_ref, cm_ref, co_ref, out_ref = refs[count:]
    rows = sm_ref.shape[0]
    core, near, column = place_ref[0], place_ref[1], place_ref[2]
    mine_at = pl.ds(pl.multiple_of(core * rows, 16), rows)
    other_at = pl.ds(pl.multiple_of((1 - core) * rows, 16), rows)
    for n, o_ref in enumerate(o_refs):
        total = tn(o_ref[mine_at, :], sm_ref[...]) + tn(o_ref[other_at, :], so_ref[...])
        if count == 1:
            at = slice(0, 256)
        else:
            at = pl.ds(pl.multiple_of((near if n == 0 else 1 - near) * 128, 128), 128)
        out_ref[at, :] = total.astype(out_ref.dtype)
    total = tn(am_ref[...], cm_ref[...]) + tn(ao_ref[...], co_ref[...])
    value = total.astype(out_ref.dtype)
    if count == 1:
        out_ref[256:, :] = value
    else:
        out_ref[pl.ds(pl.multiple_of(256 + column * 128, 128), 128), :] = value[:128, :]
        out_ref[pl.ds(pl.multiple_of(384 - column * 128, 128), 128), :] = value[128:, :]


def outputs_grad(place, group, o, dself, dself_other, ca, ca_other, dcross, dcross_other, kind):
    rows, width = dself.shape
    lanes = pl.BlockSpec((rows, 256), lambda i, s: (0, group))
    whole = resident((rows, width))
    return pl.pallas_call(
        functools.partial(outputs_grad_kernel, count=len(o)),
        grid_spec=pltpu.PrefetchScalarGridSpec(
            num_scalar_prefetch=1,
            grid=(1,),
            in_specs=[resident(a.shape) for a in o] + [whole, whole, lanes, lanes, whole, whole],
            out_specs=resident((512, width)),
        ),
        out_shape=shape((512, width), kind),
        compiler_params=params(48),
        cost_estimate=lasting(0.643),
        name="outputs_grad",
    )(place, *o, dself, dself_other, ca, ca_other, dcross, dcross_other)


def middle_back_kernel(place_ref, ym_ref, yr_ref, x1_ref, x2_ref, d_ref, cq_ref, *refs):
    wq, wc = refs[0:6], refs[6:12]
    ck_ref, cv_ref, gain_ref = refs[12:15]
    dx1_ref, dself_ref, dcross_ref, dcq_ref, dck_ref, dcv_ref, sums_ref = refs[15:22]
    dck_all, dcv_all = refs[22:]
    step = pl.program_id(0)

    @pl.when(step == 0)
    def _():
        dck_all[...] = jnp.zeros_like(dck_all)
        dcv_all[...] = jnp.zeros_like(dcv_all)
        sums_ref[...] = jnp.zeros_like(sums_ref)

    y3 = ym_ref[...] + yr_ref[...].astype(FULL)
    scaled, inverse = norm_parts(x2_ref[...])
    sums_ref[4:5, :] += jnp.sum(y3 * scaled, axis=0, keepdims=True)
    sums_ref[5:6, :] += jnp.sum(y3, axis=0, keepdims=True)
    dx2 = d_ref[...].astype(FULL) + norm_pull(y3, scaled, inverse, gain_ref[2:3, :])
    dx1_ref[...] = dx2
    dcross = lower(dx2)
    dcross_ref[...] = dcross
    for g, weight in enumerate(in_groups(wc, 0)):
        lanes = slice(g * 256, (g + 1) * 256)
        dcatt = lower(nt(dcross, weight))
        keys = ck_ref[g]
        cq = cq_ref[:, lanes]
        probability = cross_probability(cq, keys)
        weighed = nt(dcatt, cv_ref[g])
        inner = by_head(probability * weighed, jnp.sum, 0.0)
        dcs = lower(probability * (weighed - inner))
        dcq_ref[:, lanes] = lower(nn(dcs, keys) * HEAD ** (-0.5))
        dck_all[g] += tn(dcs, cq * HEAD ** (-0.5))
        dcv_all[g] += tn(lower(probability), dcatt)
    y2 = 0.0
    for g, weight in enumerate(in_groups(wq, 1)):
        y2 = y2 + nt(dcq_ref[:, g * 256 : (g + 1) * 256], weight)
    scaled, inverse = norm_parts(x1_ref[...])
    sums_ref[2:3, :] += jnp.sum(y2 * scaled, axis=0, keepdims=True)
    sums_ref[3:4, :] += jnp.sum(y2, axis=0, keepdims=True)
    dx1 = dx1_ref[...] + norm_pull(y2, scaled, inverse, gain_ref[1:2, :])
    dx1_ref[...] = dx1
    dself_ref[...] = lower(dx1)

    @pl.when(step == pl.num_programs(0) - 1)
    def _():
        for every, result in ((dck_all, dck_ref), (dcv_all, dcv_ref)):
            for g in range(4):
                total = 0.0
                for h in range(4):
                    lane = lax.broadcasted_iota(jnp.int32, (1, 256), 1) // HEAD
                    total = total + jnp.where(lane == h, every[g, h * 64 : (h + 1) * 64, :], 0.0)
                result[g] = total


def middle_back(place, ym, yr, x1, x2, d, cq, wq, wc, ck, cv, gains):
    rows, width = x1.shape
    block = 416
    wide = rows_of(block, width)
    small = pl.BlockSpec((4, 64, 256), lambda i, s: (0, 0, 0))
    whole = (*wq, *wc, ck, cv, gains)
    return pl.pallas_call(
        middle_back_kernel,
        grid_spec=pltpu.PrefetchScalarGridSpec(
            num_scalar_prefetch=1,
            grid=(rows // block,),
            in_specs=[wide] * 6 + [resident(a.shape) for a in whole],
            out_specs=[wide] * 4 + [small, small, pl.BlockSpec((8, width), lambda i, s: (0, 0))],
            scratch_shapes=[pltpu.VMEM((4, 256, 256), FULL)] * 2,
        ),
        out_shape=[shape((rows, width), FULL)]
        + [shape((rows, width), ROUND)] * 3
        + [shape((4, 64, 256), FULL)] * 2
        + [shape((8, width), FULL)],
        compiler_params=params(56),
        cost_estimate=lasting(2.571),
        name="middle_back",
    )(place, ym, yr, x1, x2, d, cq, *whole)


def first_back_kernel(place_ref, *refs):
    y_ref = refs[-1]
    y = 0.0
    for n in range(3):
        for c in range(3):
            y = y + nt(refs[3 * n + c][...], refs[9 + n][c])
    y_ref[...] = y.astype(y_ref.dtype)


def first_back(place, grads, weights, kind):
    span = grads[0].shape[0]
    rows = span // 2
    width = weights[0].shape[1]
    block = 416
    steps = rows // block
    return pl.pallas_call(
        first_back_kernel,
        grid_spec=pltpu.PrefetchScalarGridSpec(
            num_scalar_prefetch=1,
            grid=(steps,),
            in_specs=[
                pl.BlockSpec((block, a.shape[1]), lambda i, s: (s[0] * steps + i, 0))
                for a in grads
            ]
            + [resident(a.shape) for a in weights],
            out_specs=rows_of(block, width),
        ),
        out_shape=shape((rows, width), kind),
        compiler_params=params(40),
        cost_estimate=lasting(0.535),
        name="first_back",
    )(place, *grads, *weights)


def frames_back_kernel(place_ref, ym_ref, yr_ref, dx1_ref, frame_ref, gain_ref, out_ref, sums_ref):
    @pl.when(pl.program_id(0) == 0)
    def _():
        sums_ref[...] = jnp.zeros_like(sums_ref)

    y = ym_ref[...] + yr_ref[...].astype(FULL)
    scaled, inverse = norm_parts(frame_ref[...].astype(FULL))
    sums_ref[0:1, :] += jnp.sum(y * scaled, axis=0, keepdims=True)
    sums_ref[1:2, :] += jnp.sum(y, axis=0, keepdims=True)
    out_ref[...] = lower(dx1_ref[...] + norm_pull(y, scaled, inverse, gain_ref[0:1, :]))


def frames_back(place, ym, yr, dx1, frames, gains):
    rows, width = dx1.shape
    block = 208
    wide = rows_of(block, width)
    return pl.pallas_call(
        frames_back_kernel,
        grid_spec=pltpu.PrefetchScalarGridSpec(
            num_scalar_prefetch=1,
            grid=(rows // block,),
            in_specs=[wide] * 4 + [resident(gains.shape)],
            out_specs=[wide, pl.BlockSpec((8, width), lambda i, s: (0, 0))],
        ),
        out_shape=[shape((rows, width), ROUND), shape((8, width), FULL)],
        compiler_params=params(24),
        cost_estimate=lasting(0.643),
        name="frames_back",
    )(place, ym, yr, dx1, frames, gains)


def chip_local(
    frames, text_states, lengths, loss_mask, norm_gain, norm_bias, w_qkv, w_out, w_cross_q,
    w_cross_kv, w_cross_out, w_up, w_down, cotangent,
):
    at = lax.axis_index("narrow")
    core = at % 2
    side = at // 2
    column = lax.axis_index("wide") % 2
    layer = lax.axis_index("wide") // 2
    near = layer % 2
    place = jnp.stack([core, near, column]).astype(jnp.int32)
    away = jnp.stack([1 - core, near, column]).astype(jnp.int32)
    limit = lax.dynamic_slice(lengths, (side,), (1,))
    rows, width = frames.shape
    join = lax.optimization_barrier

    def over_core(v):
        return lax.ppermute(v, "narrow", CORE_PAIRS)

    def over_y(v):
        return lax.ppermute(v, "narrow", Y_PAIRS)

    def along_wide(v, pairs):
        return lax.ppermute(v, "wide", pairs)

    def half_of(v, which, axis=0):
        half = v.shape[axis] // 2
        return lax.dynamic_slice_in_dim(v, which * half, half, axis=axis)

    def ordered(first, second, which):
        return jnp.where(
            which == 0,
            jnp.concatenate([first, second], axis=0),
            jnp.concatenate([second, first], axis=0),
        )

    def over_z(v):
        return along_wide(v, Z_NEAR)

    def over_x(v):
        return along_wide(v, X_PAIRS)

    def away_rows(v):
        return half_of(v, 1 - core)

    def cross_order(v):
        return jnp.where(column == 0, v, jnp.concatenate([v[..., 128:], v[..., :128]], axis=-1))

    qkv_first = over_y(half_of(w_qkv, near, 2))
    frames_other = over_core(frames)
    h1, q0, k0, v0 = first_project(place, frames, frames_other, norm_gain, norm_bias, w_qkv)
    q0, qkv_first, w_out, w_cross_q, w_cross_out, cotangent = join(
        (q0, qkv_first, w_out, w_cross_q, w_cross_out, cotangent)
    )

    qkv_second = over_z(qkv_first)
    out_first = over_y(half_of(w_out, near))
    query_first = over_y(half_of(w_cross_q, column, 1))
    cross_out_first = over_y(half_of(w_cross_out, column))
    o0, lse0 = self_forward(limit, q0, k0, v0)
    qf, kf, vf = project(place, h1, qkv_first)
    out_other, query_other, cross_out_other = map(over_core, (w_out, w_cross_q, w_cross_out))
    qf, o0, out_first, query_first, cross_out_first, w_up, w_down, *core_got = join(
        (qf, o0, out_first, query_first, cross_out_first, w_up, w_down)
        + (out_other, query_other, cross_out_other)
    )

    out_other, query_other, cross_out_other = core_got
    out_second = over_z(out_first)
    query_second = over_x(query_first)
    cross_out_second = over_x(cross_out_first)
    up_first = over_y(half_of(w_up, column, 1))
    down_sent = half_of(w_down, column)
    o0_other = over_core(away_rows(o0))
    keys = keys_of(text_states, w_cross_kv)
    own_keys = lax.dynamic_index_in_dim(keys, side, keepdims=False)
    keys_y = over_y(lax.dynamic_index_in_dim(keys, 1 - side, keepdims=False))
    of, lse_f = self_forward(limit, qf, kf, vf)
    of, qkv_second, keys_y, o0_other = join((of, qkv_second, keys_y, o0_other))

    qs, ks, vs = project(place, h1, qkv_second)
    of_other = over_core(away_rows(of))
    pair = jnp.stack([own_keys, cross_order(keys_y)])
    pair_other = over_core(pair)
    o_s, lse_s = self_forward(limit, qs, ks, vs)
    o_s, out_second, query_second, cross_out_second, up_first, down_sent, pair_other, of_other = join(
        (o_s, out_second, query_second, cross_out_second, up_first, down_sent, pair_other, of_other)
    )

    down_first = over_y(down_sent)
    up_second = over_x(up_first)
    os_other = over_core(away_rows(o_s))
    dout = jnp.where(loss_mask[:, None] != 0, cotangent, jnp.zeros((), ROUND))

    def pieces(own, first, second, own_other):
        return (own, first, second, own_other, over_core(first), over_core(second))

    wo = pieces(w_out, out_first, out_second, out_other)
    wq = pieces(w_cross_q, query_first, query_second, query_other)
    wc = pieces(w_cross_out, cross_out_first, cross_out_second, cross_out_other)
    text = lax.dynamic_index_in_dim(text_states, side, keepdims=False)
    head_of = jnp.arange(256) // HEAD
    same = head_of[:, None] == head_of[None, :]

    def spread_heads(v):
        return jnp.where(same, jnp.tile(v, (1, 4, 1)), jnp.zeros((), ROUND))

    every = jnp.concatenate([pair, pair_other], axis=0)
    ck, cv = spread_heads(every[:, 0]), spread_heads(every[:, 1])
    x1, x2, h2, cq, ca, h3 = middle_forward(
        place, frames, (o0, of, o_s), (o0_other, of_other, os_other), wo, wq, wc, ck, cv,
        norm_gain, norm_bias,
    )
    h3, ca, h2, up_second, down_first, dout = join((h3, ca, h2, up_second, down_first, dout))

    h3_other = over_core(h3)
    dout_other = over_core(dout)
    down_second = over_x(down_first)
    g0, du0, out_m, y_m = feed(place, h3, dout, (w_up,), (w_down,), FULL, 0)
    g0, du0, out_o, y_o = feed(
        place, h3_other, dout_other, (w_up,), (w_down,), FULL, 1, shared=(g0, du0)
    )
    y_o, down_second, ca, h2 = join((y_o, down_second, ca, h2))

    ups = (up_first, up_second)
    downs = (down_first, down_second)
    g1, du1, out_o, y_o = feed(
        place, h3_other, dout_other, ups, downs, ROUND, 1, before=(out_o, y_o)
    )
    y_received = over_core(y_o)
    h2_other = over_core(h2)
    ca_other = over_core(ca[:, 512:])
    g1, du1, out_m, y_m = feed(
        place, h3, dout, ups, downs, FULL, 0, before=(out_m, y_m), shared=(g1, du1)
    )

    def plus(a, b):
        return lower(a.astype(FULL) + b.astype(FULL))

    across = (column, X_PAIRS)
    down_z = (near, Z_NEAR)
    store = {}
    last = []
    free = []

    def order(*names):
        if free:
            return
        names = tuple(dict.fromkeys((*names, *last)))
        for name, value in zip(names, join(tuple(store[name] for name in names))):
            store[name] = value

    def get(*names):
        return tuple(store[name] for name in names)

    def step(results, make, *needs):
        order(*needs)
        made = make()
        made = made if isinstance(made, (tuple, list)) else (made,)
        store.update(zip(results, made))
        last[:] = results[:1]

    class Sum:
        def __init__(self, name, axes=(across, down_z)):
            self.fly, self.kept, self.axes = name + "_fly", name + "_kept", axes

        def over_y(self, partner):
            order(partner)
            store[self.fly] = over_y(store[partner])

        def first(self, own):
            which, pairs = self.axes[0]
            order(self.fly, own)
            mine, fly = get(own, self.fly)
            away_half = plus(half_of(mine, 1 - which), half_of(fly, 1 - which))
            store[self.kept] = half_of(mine, which).astype(FULL) + half_of(fly, which).astype(FULL)
            store[self.fly] = along_wide(away_half, pairs)
            last[:] = [self.kept]

        def first_alone(self, own):
            which, pairs = self.axes[0]
            store[self.kept] = half_of(store[own], which).astype(FULL)
            store[self.fly] = along_wide(half_of(store[own], 1 - which), pairs)
            last[:] = [self.kept]

        def second(self):
            which, pairs = self.axes[1]
            order(self.fly, self.kept)
            total = store[self.kept] + store[self.fly].astype(FULL)
            store[self.kept] = half_of(total, which)
            store[self.fly] = along_wide(lower(half_of(total, 1 - which)), pairs)
            last[:] = [self.kept]

        def add(self, pairs):
            order(self.fly, self.kept)
            store[self.kept] = plus(*get(self.kept, self.fly))
            store[self.fly] = along_wide(store[self.kept], pairs)
            last[:] = [self.kept]

        def far(self):
            self.add(Z_FAR)

        def back(self):
            self.add(self.axes[1][1])

        def along(self):
            order(self.fly, self.kept)
            store[self.kept] = ordered(*get(self.kept, self.fly), self.axes[1][0])
            store[self.fly] = along_wide(store[self.kept], self.axes[0][1])
            last[:] = [self.kept]

        def end(self, result):
            order(self.fly, self.kept)
            store[result] = ordered(*get(self.kept, self.fly), self.axes[0][0]).astype(FULL)
            last[:] = [result]

    class Row:
        def __init__(self, name, value, move):
            self.fly, self.kept = name + "_fly", name + "_kept"
            store[self.kept] = value
            store[self.fly] = move(value)

        def then(self, move):
            order(self.fly, self.kept)
            store[self.kept] = store[self.kept] + store[self.fly]
            store[self.fly] = move(store[self.kept])
            last[:] = [self.kept]

        def total(self):
            return store[self.kept] + store[self.fly]

    up, down, outs, cross_in = Sum("up"), Sum("down"), Sum("outs"), Sum("cross_in")
    qkv = Sum("qkv", (down_z, across))
    store.update(h3_other=h3_other, du1=du1, g1=g1, du0=du0, g0=g0, y_m=y_m, y_fly=y_received)
    store.update(of=of, o_s=o_s, o0=o0, x2=x2, h2_other=h2_other, ca_other=ca_other)

    def middle():
        dx1, *rest = middle_back(
            place, *get("y_m", "y_fly"), x1, store["x2"], dout, cq, wq, wc, ck, cv, norm_gain
        )
        return (rest[0], dx1, *rest[1:])

    step(["up1"], lambda: up_grad(h3, *get("h3_other", "du1"), ROUND), "du1", "du0")
    up.over_y("up1")
    step(["down1"], lambda: down_grad(store["g1"], dout, dout_other, ROUND), "g1")
    step(["dself", "dx1", "dcross", "dcq", "dck", "dcv", "sums"], middle, "y_fly", "y_m", "x2")
    store["dself_other"] = over_core(store["dself"])
    step(["up0"], lambda: up_grad(h3, *get("h3_other", "du0"), ROUND), "du0")
    order(up.fly, "down1", "dself_other")
    down.over_y("down1")
    up.first("up0")
    step(
        ["dof", "dos", "do0"],
        lambda: pull(place, *get("dself", "dself_other"), (out_first, out_second, w_out)),
        "dself",
        "dself_other",
        "dcross",
        "dcq",
    )
    store["dcross_other"] = over_core(store["dcross"])
    store["dcq_other"] = over_core(store["dcq"][:, 512:])
    d_pair = jnp.stack(get("dck", "dcv"), axis=1)
    store["pair_kept"] = d_pair[:2]
    store["pair_fly"] = over_core(d_pair[2:])
    step(
        ["dqf", "dkf", "dvf"],
        lambda: self_back(limit, qf, kf, vf, store["of"], store["dof"], lse_f),
        "dof",
    )
    def query(g):
        return query_grad(place, g, h2, *get("h2_other", "dcq", "dcq_other"), ROUND)

    def outof(g, *o):
        return outputs_grad(
            place, g, get(*o), *get("dself", "dself_other"), ca,
            *get("ca_other", "dcross", "dcross_other"), ROUND,
        )

    step(["query1"], lambda: query(1), "dcq_other", "h2_other", "pair_fly", "pair_kept")
    pair_sum = lower(store["pair_kept"] + store["pair_fly"])
    store["pair"] = pair_sum[0]
    store["pair_other"] = cross_order(pair_sum[1])
    step(
        ["dqs", "dks", "dvs"],
        lambda: self_back(limit, qs, ks, vs, store["o_s"], store["dos"], lse_s),
        "dos",
    )
    up.second()
    step(["down0"], lambda: down_grad(store["g0"], dout, dout_other, ROUND), "g0")
    yp = ("dqf", "dkf", "dvf", "dqs", "dks", "dvs")
    step(["qkv1"], lambda: qkv_grad(place, h1, get(*yp), ROUND), "dqs")
    order(down.fly, "qkv1", "query1", "pair_other")
    store["query_fly"] = over_y(store["query1"])
    store["pair_y"] = over_y(store["pair_other"])
    qkv.over_y("qkv1")
    down.first("down0")
    step(
        ["dq0", "dk0", "dv0"],
        lambda: self_back(limit, q0, k0, v0, store["o0"], store["do0"], lse0),
        "do0",
    )
    up.far()
    down.second()
    step(["outs1"], lambda: outof(1, "of", "o_s"), "dcross_other", "ca_other")
    outs.over_y("outs1")
    nine = ("dq0", "dk0", "dv0", *yp)
    weights = (w_qkv, qkv_first, qkv_second)
    step(["yo"], lambda: first_back(away, get(*nine), weights, ROUND), "dq0")
    store["yo_fly"] = over_core(store["yo"])
    step(["qkv0"], lambda: qkv_grad(place, h1, get("dq0", "dk0", "dv0"), ROUND), "dq0")
    qkv.first("qkv0")
    step(["query0"], lambda: query(0), "dcq")
    order("query0", "query_fly", "pair", "pair_y")
    other_text = lax.dynamic_index_in_dim(text_states, 1 - side, keepdims=False)
    texts = jnp.concatenate([text, other_text], axis=0)
    pairs = jnp.concatenate(get("pair", "pair_y"), axis=1)
    store["into0"] = jnp.concatenate(
        [
            lower(store["query0"].astype(FULL) + store["query_fly"].astype(FULL)),
            lower(tn(texts, pairs[0])),
            lower(tn(texts, pairs[1])),
        ],
        axis=0,
    )
    cross_in.first_alone("into0")
    up.back()
    step(["ym"], lambda: first_back(place, get(*nine), weights, FULL), "dq0")
    step(
        ["grad_frames", "first_sums"],
        lambda: frames_back(place, *get("ym", "yo_fly", "dx1"), frames, norm_gain),
        "ym",
        "yo_fly",
    )
    norms = Row("norms", store["sums"] + store["first_sums"], over_core)
    down.far()
    norms.then(over_y)
    up.along()
    cross_in.second()
    step(["outs0"], lambda: outof(0, "o0"), "dcross")
    outs.first("outs0")
    norms.then(over_z)
    text_part = 0.0
    for c in range(2):
        text_part = text_part + nt(pairs[c], w_cross_kv[c])
    text_mine, text_theirs = text_part[:64], text_part[64:]
    text_rows = Row("texts", text_mine, lambda v: over_y(text_theirs))
    last[:] = ["texts_kept"]
    qkv.second()
    down.back()
    cross_in.far()
    store["out_fly"] = over_core(out_o)
    text_rows.then(over_core)
    norms.then(lambda v: along_wide(v, Z_FAR))
    outs.second()
    qkv.far()
    order("x2", "out_fly")
    out_rows = lower(store["x2"] + out_m + store["out_fly"].astype(FULL))
    down.along()
    cross_in.back()
    order("texts_fly", "texts_kept")
    text_grad = lower(text_rows.total())
    text_away = over_y(text_grad)
    grad_text = ordered(text_grad[None], text_away[None], side)
    up.end("grad_up")
    outs.far()
    norms.then(over_x)
    qkv.back()
    cross_in.along()
    outs.back()
    down.end("grad_down")
    qkv.along()
    outs.along()
    cross_in.end("grad_in")
    sums = norms.total()
    qkv.end("grad_qkv")
    outs.end("grad_outs")
    grad_in, grad_outs = get("grad_in", "grad_outs")
    return (
        out_rows,
        store["grad_frames"],
        grad_text,
        sums[0:6:2],
        sums[1:6:2],
        store["grad_qkv"].reshape(3, width, 256),
        grad_outs[:256],
        grad_in[:width],
        grad_in[width:].reshape(2, width, 256),
        grad_outs[256:],
        store["grad_up"],
        store["grad_down"],
    )


def solution(mesh):
    chips = dict(mesh.shape) == {"wide": 8, "narrow": 4}
    return jax.shard_map(
        chip_local if chips else general_local,
        mesh=mesh,
        in_specs=(
            P(("wide", "narrow"), None),
            P("wide", None, None),
            P("wide"),
            P(("wide", "narrow")),
            P(),
            P(),
            P(None, None, "narrow"),
            P("narrow", None),
            P(None, "narrow"),
            P(None, None, "narrow"),
            P("narrow", None),
            P(None, "narrow"),
            P("narrow", None),
            P(("wide", "narrow"), None),
        ),
        out_specs=(
            P(("wide", "narrow"), None),
            P(("wide", "narrow"), None),
            P("wide", None, None),
            P(),
            P(),
            P(None, None, "narrow"),
            P("narrow", None),
            P(None, "narrow"),
            P(None, None, "narrow"),
            P("narrow", None),
            P(None, "narrow"),
            P("narrow", None),
        ),
        check_vma=False,
    )
```

```python
import functools

import jax
import jax.numpy as jnp
from jax import lax
from jax.experimental import pallas as pl
from jax.experimental.pallas import tpu as pltpu
from jax.sharding import PartitionSpec as P

HEAD = 64


EPS = 1e-05
NEG = -1e30


def lower(values_in):
    return values_in.astype(jnp.bfloat16)


def product(left_side, right_side, transposed):
    if transposed:
        return lax.dot_general(
            left_side, right_side, (((1,), (1,)), ((), ())), preferred_element_type=jnp.float32
        )
    return jnp.dot(left_side, right_side, preferred_element_type=jnp.float32)


def outer_sum(left_side, right_side):
    return lax.dot_general(
        left_side, right_side, (((0,), (0,)), ((), ())), preferred_element_type=jnp.float32
    )


def normalize(values_in, gain_row, bias_row):
    row_mean = jnp.mean(values_in, axis=-1, keepdims=True)
    centered = values_in - row_mean
    inverse = lax.rsqrt(jnp.mean(centered * centered, axis=-1, keepdims=True) + EPS)
    scaled = centered * inverse
    return (scaled * gain_row + bias_row, scaled, inverse)


def normalize_back(upstream, scaled, inverse, gain_row):
    weighted = upstream * gain_row
    inner_mean = jnp.mean(weighted, axis=-1, keepdims=True)
    along_mean = jnp.mean(weighted * scaled, axis=-1, keepdims=True)
    grad_input = inverse * (weighted - inner_mean - scaled * along_mean)
    return (grad_input, jnp.sum(upstream * scaled, axis=0), jnp.sum(upstream, axis=0))


def gelu_parts(values_in):
    normal_cdf = 0.5 * (1.0 + jax.scipy.special.erf(values_in * 0.7071067811865476))
    normal_pdf = jnp.exp(-0.5 * values_in * values_in) * 0.3989422804014327
    return (values_in * normal_cdf, normal_cdf + values_in * normal_pdf)


def scores_of(query_part, key_part, valid):
    scores = jnp.einsum(
        "bhe,khe->hbk", query_part, key_part, preferred_element_type=jnp.float32
    ) * HEAD ** (-0.5)
    return jnp.where(valid, scores, NEG)


def attend(query_part, key_part, value_part, valid):
    scores = scores_of(query_part, key_part, valid)
    row_top = jnp.max(scores, axis=-1, keepdims=True)
    weights_exp = jnp.exp(scores - row_top)
    denominator = jnp.sum(weights_exp, axis=-1, keepdims=True)
    probability = weights_exp / denominator
    mixed = jnp.einsum(
        "hbk,khe->bhe", lower(probability), value_part, preferred_element_type=jnp.float32
    )
    return (lower(mixed), (row_top + jnp.log(denominator))[..., 0])


def attend_back(query_part, key_part, value_part, valid, summary, upstream):
    scores = scores_of(query_part, key_part, valid)
    probability = jnp.exp(scores - summary[..., None])
    pressure = jnp.einsum("bhe,khe->hbk", upstream, value_part, preferred_element_type=jnp.float32)
    grad_scores = lower(
        probability * (pressure - jnp.sum(probability * pressure, axis=-1, keepdims=True))
    )
    factor = HEAD ** (-0.5)
    grad_query = (
        jnp.einsum("hbk,khe->bhe", grad_scores, key_part, preferred_element_type=jnp.float32)
        * factor
    )
    grad_key = (
        jnp.einsum("hbk,bhe->khe", grad_scores, query_part, preferred_element_type=jnp.float32)
        * factor
    )
    grad_value = jnp.einsum(
        "hbk,bhe->khe", lower(probability), upstream, preferred_element_type=jnp.float32
    )
    return (grad_query, grad_key, grad_value)


def general_local(
    frames,
    text_states,
    lengths,
    loss_mask,
    norm_gain,
    norm_bias,
    w_qkv,
    w_out,
    w_cross_q,
    w_cross_kv,
    w_cross_out,
    w_up,
    w_down,
    cotangent,
):
    row_count = frames.shape[0]
    width = frames.shape[1]
    item_count = lengths.shape[0]
    span = row_count * lax.axis_size("narrow") // item_count
    half_span = span // 2
    inner_width = w_qkv.shape[2]
    head_count = inner_width // HEAD
    text_count = text_states.shape[1]
    full_rows = item_count * span
    places = jnp.arange(span, dtype=jnp.int32)

    def spread(shard_rows):
        return lax.all_gather(shard_rows, "narrow", axis=0, tiled=True)

    def collect(left_side, right_side, transposed):
        return lax.psum_scatter(
            product(
                lax.slice_in_dim(left_side, 0, lax.axis_size("narrow") * row_count, axis=0),
                right_side,
                transposed,
            ),
            "narrow",
            scatter_dimension=0,
            tiled=True,
        )

    def causal(block_index, item_limit):
        query_place = block_index * half_span + jnp.arange(half_span, dtype=jnp.int32)
        return (places[None, :] <= query_place[:, None]) & (places[None, :] < item_limit)

    frame_rows = frames.astype(jnp.float32)
    normed_one, scaled_one, inverse_one = normalize(frame_rows, norm_gain[0], norm_bias[0])
    first_input = spread(lower(normed_one))
    triple = lower(
        jnp.einsum("rd,cde->cre", first_input, w_qkv, preferred_element_type=jnp.float32)
    )
    triple = triple.reshape(3, item_count, span, head_count, HEAD)

    def self_item(packed):
        query_part, key_part, value_part, item_limit = packed
        mixed_list = []
        summary_list = []
        for block_index in range(2):
            mixed, summary = attend(
                query_part[block_index * half_span : (block_index + 1) * half_span],
                key_part,
                value_part,
                causal(block_index, item_limit),
            )
            mixed_list.append(mixed)
            summary_list.append(summary)
        return (jnp.concatenate(mixed_list, axis=0), jnp.stack(summary_list, axis=0))

    attended, self_summary = lax.map(self_item, (triple[0], triple[1], triple[2], lengths))
    attended_flat = attended.reshape(full_rows, inner_width)
    first_rows = frame_rows + collect(attended_flat, w_out, False)
    normed_two, scaled_two, inverse_two = normalize(first_rows, norm_gain[1], norm_bias[1])
    second_input = spread(lower(normed_two))
    cross_query = lower(product(second_input, w_cross_q, False)).reshape(
        item_count, span, head_count, HEAD
    )
    cross_pair = lower(
        jnp.einsum("ntd,cde->cnte", text_states, w_cross_kv, preferred_element_type=jnp.float32)
    )
    cross_pair = cross_pair.reshape(2, item_count, text_count, head_count, HEAD)

    def cross_item(packed):
        query_part, key_part, value_part = packed
        return attend(query_part, key_part, value_part, True)

    cross_mixed, cross_summary = lax.map(cross_item, (cross_query, cross_pair[0], cross_pair[1]))
    cross_flat = cross_mixed.reshape(full_rows, inner_width)
    second_rows = first_rows + collect(cross_flat, w_cross_out, False)
    normed_three, scaled_three, inverse_three = normalize(second_rows, norm_gain[2], norm_bias[2])
    upstream = cotangent.astype(jnp.float32) * loss_mask.astype(jnp.float32)[:, None]
    ffn_grad = lower(upstream)
    ffn_input = spread(lower(normed_three))
    hidden_pre = product(ffn_input, w_up, False)
    active, slope = gelu_parts(hidden_pre)
    active = lower(active)
    out_rows = second_rows + collect(active, w_down, False)
    ffn_full = spread(ffn_grad)
    grad_down = outer_sum(active, ffn_full)
    grad_hidden = lower(product(ffn_full, w_down, True) * slope)
    grad_up = outer_sum(ffn_input, grad_hidden)
    back_three = collect(grad_hidden, w_up, True)
    grad_up, grad_down = (grad_up, grad_down)
    grad_in_three, gain_three, bias_three = normalize_back(
        back_three, scaled_three, inverse_three, norm_gain[2]
    )
    grad_second = upstream + grad_in_three
    cross_full = spread(lower(grad_second))
    grad_cross_out = outer_sum(cross_flat, cross_full)
    cross_upstream = lower(product(cross_full, w_cross_out, True)).reshape(
        item_count, span, head_count, HEAD
    )

    def cross_back(packed):
        query_part, key_part, value_part, summary, upstream_item = packed
        return attend_back(query_part, key_part, value_part, True, summary, upstream_item)

    grad_cq, grad_ck, grad_cv = lax.map(
        cross_back, (cross_query, cross_pair[0], cross_pair[1], cross_summary, cross_upstream)
    )
    grad_cq = lower(grad_cq).reshape(full_rows, inner_width)
    grad_pair = lower(jnp.stack((grad_ck, grad_cv), axis=0)).reshape(
        2, item_count, text_count, inner_width
    )
    grad_cross_q = outer_sum(second_input, grad_cq)
    grad_cross_kv = jnp.einsum(
        "ntd,cnte->cde", text_states, grad_pair, preferred_element_type=jnp.float32
    )
    grad_cross_q, grad_cross_kv, grad_cross_out = (grad_cross_q, grad_cross_kv, grad_cross_out)
    text_partial = jnp.einsum(
        "cnte,cde->ntd", grad_pair, w_cross_kv, preferred_element_type=jnp.float32
    )
    grad_text = lower(lax.psum(text_partial, "narrow"))
    back_two = collect(grad_cq, w_cross_q, True)
    grad_in_two, gain_two, bias_two = normalize_back(
        back_two, scaled_two, inverse_two, norm_gain[1]
    )
    grad_first = grad_second + grad_in_two
    self_full = spread(lower(grad_first))
    grad_out = outer_sum(attended_flat, self_full)
    self_upstream = lower(product(self_full, w_out, True)).reshape(
        item_count, span, head_count, HEAD
    )

    def self_back(packed):
        query_part, key_part, value_part, item_limit, summary, upstream_item = packed
        query_list = []
        key_list = []
        value_list = []
        for block_index in range(2):
            lower_row = block_index * half_span
            grad_query, grad_key, grad_value = attend_back(
                query_part[lower_row : lower_row + half_span],
                key_part,
                value_part,
                causal(block_index, item_limit),
                summary[block_index],
                upstream_item[lower_row : lower_row + half_span],
            )
            query_list.append(grad_query)
            key_list.append(grad_key)
            value_list.append(grad_value)
        return (
            jnp.concatenate(query_list, axis=0),
            key_list[0] + key_list[1],
            value_list[0] + value_list[1],
        )

    grad_q, grad_k, grad_v = lax.map(
        self_back, (triple[0], triple[1], triple[2], lengths, self_summary, self_upstream)
    )
    grad_triple = lower(jnp.stack((grad_q, grad_k, grad_v), axis=0)).reshape(
        3, full_rows, inner_width
    )
    grad_qkv = jnp.einsum(
        "rd,cre->cde", first_input, grad_triple, preferred_element_type=jnp.float32
    )
    grad_qkv, grad_out = (grad_qkv, grad_out)
    merged = grad_triple.transpose(1, 0, 2).reshape(full_rows, 3 * inner_width)
    stacked_weights = w_qkv.transpose(0, 2, 1).reshape(3 * inner_width, width)
    back_one = collect(merged, stacked_weights, False)
    grad_in_one, gain_one, bias_one = normalize_back(
        back_one, scaled_one, inverse_one, norm_gain[0]
    )
    grad_frames = lower(grad_first + grad_in_one)
    gain_terms = jnp.stack((gain_one, gain_two, gain_three), axis=0)
    bias_terms = jnp.stack((bias_one, bias_two, bias_three), axis=0)
    grad_norm_gain, grad_norm_bias = lax.psum((gain_terms, bias_terms), ("wide", "narrow"))
    grad_qkv, grad_out, grad_cross_q, grad_cross_kv, grad_cross_out, grad_up, grad_down = lax.psum(
        (grad_qkv, grad_out, grad_cross_q, grad_cross_kv, grad_cross_out, grad_up, grad_down),
        "wide",
    )
    return (
        lower(out_rows),
        grad_frames,
        grad_text,
        grad_norm_gain,
        grad_norm_bias,
        grad_qkv,
        grad_out,
        grad_cross_q,
        grad_cross_kv,
        grad_cross_out,
        grad_up,
        grad_down,
    )


ROUND = jnp.bfloat16
FULL = jnp.float32
CORE_PAIRS = ((0, 1), (1, 0), (2, 3), (3, 2))
Y_PAIRS = ((0, 2), (2, 0), (1, 3), (3, 1))
X_PAIRS = tuple((i, i ^ 1) for i in range(8))
Z_INWARD = ((0, 2), (1, 3), (6, 4), (7, 5))
Z_MIDDLE = ((2, 4), (4, 2), (3, 5), (5, 3))
Z_OUTWARD = ((2, 0), (3, 1), (4, 6), (5, 7))
Z_NEAR = tuple((i, i ^ 2) for i in range(8))
Z_FAR = tuple((i, i ^ 4) for i in range(8))
MIB = 1 << 20


def nt(a, b):
    return lax.dot_general(a, b, (((1,), (1,)), ((), ())), preferred_element_type=FULL)


def nn(a, b):
    return lax.dot_general(a, b, (((1,), (0,)), ((), ())), preferred_element_type=FULL)


def tn(a, b):
    return lax.dot_general(a, b, (((0,), (0,)), ((), ())), preferred_element_type=FULL)


def shape(dims, kind):
    return jax.ShapeDtypeStruct(dims, kind)


def resident(dims):
    zeros = (0,) * len(dims)
    return pl.BlockSpec(dims, lambda i, s: zeros, pipeline_mode=pl.Buffered(1))


def rows_of(block, width):
    return pl.BlockSpec((block, width), lambda i, s: (i, 0))


def lasting(microseconds):
    flops = int(microseconds * 0.28 * 1.15e9)
    return pl.CostEstimate(flops=flops, bytes_accessed=1000, transcendentals=0)


def params(mib):
    return pltpu.CompilerParams(vmem_limit_bytes=mib * MIB)


def norm_parts(v):
    centered = v - jnp.mean(v, axis=-1, keepdims=True)
    inverse = lax.rsqrt(jnp.mean(centered * centered, axis=-1, keepdims=True) + EPS)
    return centered * inverse, inverse


def norm_pull(y, scaled, inverse, gain_row):
    weighted = y * gain_row
    inner = jnp.mean(weighted, axis=-1, keepdims=True)
    along = jnp.mean(weighted * scaled, axis=-1, keepdims=True)
    return inverse * (weighted - inner - scaled * along)


def first_project_kernel(
    place_ref, mine_ref, other_ref, gain_ref, bias_ref, weight_ref, h_ref, *out_refs
):
    half = pl.program_id(0)

    def run(source):
        for start in range(0, source.shape[0], 208):
            part = slice(start, start + 208)
            scaled, _ = norm_parts(source[part, :].astype(FULL))
            h = lower(scaled * gain_ref[0:1, :] + bias_ref[0:1, :])
            h_ref[part, :] = h
            for c, out_ref in enumerate(out_refs):
                out_ref[part, :] = lower(nn(h, weight_ref[c]))

    @pl.when(half == 0)
    def _():
        run(mine_ref)

    @pl.when(half == 1)
    def _():
        run(other_ref)


def first_project(place, mine, other, gains, biases, weights):
    rows, depth = mine.shape
    count, _, wide = weights.shape
    out = pl.BlockSpec((rows, wide), lambda i, s: ((i + s[0]) % 2, 0))
    return pl.pallas_call(
        first_project_kernel,
        grid_spec=pltpu.PrefetchScalarGridSpec(
            num_scalar_prefetch=1,
            grid=(2,),
            in_specs=[resident(a.shape) for a in (mine, other, gains, biases, weights)],
            out_specs=[rows_of(rows, depth)] + [out] * count,
        ),
        out_shape=[shape((2 * rows, depth), ROUND)] + [shape((2 * rows, wide), ROUND)] * count,
        compiler_params=params(40),
        cost_estimate=lasting(5),
        name="first_project",
    )(place, mine, other, gains, biases, weights)


def project_kernel(place_ref, h_ref, weight_ref, *out_refs):
    count = len(out_refs)
    wide = weight_ref.shape[2]
    weights = jnp.concatenate([weight_ref[c] for c in range(count)], axis=1)
    for start in range(0, h_ref.shape[0], 416):
        part = slice(start, start + 416)
        result = lower(nn(h_ref[part, :], weights))
        for c, out_ref in enumerate(out_refs):
            out_ref[part, :] = result[:, c * wide : (c + 1) * wide]


def project(place, h, weights):
    rows, depth = h.shape[0] // 2, h.shape[1]
    count, _, wide = weights.shape
    out = pl.BlockSpec((rows, wide), lambda i, s: ((i + s[0]) % 2, 0))
    return pl.pallas_call(
        project_kernel,
        grid_spec=pltpu.PrefetchScalarGridSpec(
            num_scalar_prefetch=1,
            grid=(2,),
            in_specs=[rows_of(rows, depth), resident(weights.shape)],
            out_specs=[out] * count,
        ),
        out_shape=[shape((2 * rows, wide), ROUND)] * count,
        compiler_params=params(40),
        cost_estimate=lasting(4),
        name="project",
    )(place, h, weights)


def pull_kernel(place_ref, mine_ref, other_ref, *refs):
    half = pl.program_id(0)
    count = len(refs) // 2

    def run(source):
        for weight_ref, out_ref in zip(refs[:count], refs[count:]):
            out_ref[...] = lower(nt(source[...], weight_ref[...]))

    @pl.when(half == 0)
    def _():
        run(mine_ref)

    @pl.when(half == 1)
    def _():
        run(other_ref)


def pull(place, mine, other, weights):
    rows = mine.shape[0]
    return pl.pallas_call(
        pull_kernel,
        grid_spec=pltpu.PrefetchScalarGridSpec(
            num_scalar_prefetch=1,
            grid=(2,),
            in_specs=[resident(a.shape) for a in (mine, other, *weights)],
            out_specs=[
                pl.BlockSpec((rows, a.shape[0]), lambda i, s: ((i + s[0]) % 2, 0)) for a in weights
            ],
        ),
        out_shape=[shape((2 * rows, a.shape[0]), ROUND) for a in weights],
        compiler_params=params(32),
        cost_estimate=lasting(0.375),
        name="pull",
    )(place, mine, other, *weights)


def blocks_of(span, block):
    return [(start, min(block, span - start)) for start in range(0, span, block)]


def self_forward_kernel(
    limit_ref, q_ref, k_ref, v_ref, o_ref, lse_ref, *, span, floor, block
):
    limit = limit_ref[0]
    lane = lax.broadcasted_iota(jnp.int32, (1, 128), 1)
    row = lax.broadcasted_iota(jnp.int32, (128, 1), 0)
    zero = jnp.zeros((), ROUND)
    value_turned = v_ref[...].T
    for start, size in blocks_of(span, block):
        end = start + size
        mixed_list = []
        for h in range(2):
            own_lanes = (lane < HEAD) if h == 0 else (lane >= HEAD)
            query = jnp.where(own_lanes, q_ref[start:end, :] * HEAD ** (-0.5), zero)
            parts = []
            for low in range(0, end, block):
                high = min(low + block, end)
                scores = nt(k_ref[low:high, :], query)
                if low == start:
                    key = lax.broadcasted_iota(jnp.int32, (size, size), 0)
                    valid = key <= lax.broadcasted_iota(jnp.int32, (size, size), 1)
                    if high > floor:
                        valid = valid & (key + low < limit)
                    scores = jnp.where(valid, scores, NEG)
                elif high > floor:
                    key = lax.broadcasted_iota(jnp.int32, (high - low, 1), 0)
                    scores = jnp.where(key + low < limit, scores, NEG)
                parts.append((low, high, scores))
            top = functools.reduce(
                jnp.maximum, [jnp.max(s, axis=0, keepdims=True) for _, _, s in parts]
            )
            total = 0.0
            mixed = 0.0
            for low, high, scores in parts:
                weights_exp = jnp.exp(scores - top)
                total = total + jnp.sum(weights_exp, axis=0, keepdims=True)
                mixed = mixed + nn(value_turned[:, low:high], lower(weights_exp))
            mixed_list.append(mixed / total)
            lse_ref[0, h : h + 1, start:end] = top + jnp.log(total)
        o_ref[start:end, :] = lower(jnp.where(row < HEAD, mixed_list[0], mixed_list[1]).T)


def self_forward(limit, q, k, v):
    span, wide = q.shape
    pairs = wide // 128
    floor = (span - span // 8 + 1) // 128 * 128
    pair = pl.BlockSpec((span, 128), lambda p, s: (0, p))
    return pl.pallas_call(
        functools.partial(self_forward_kernel, span=span, floor=floor, block=512),
        grid_spec=pltpu.PrefetchScalarGridSpec(
            num_scalar_prefetch=1,
            grid=(pairs,),
            in_specs=[pair] * 3,
            out_specs=[pair, pl.BlockSpec((1, 8, span), lambda p, s: (p, 0, 0))],
        ),
        out_shape=[shape((span, wide), ROUND), shape((pairs, 8, span), FULL)],
        compiler_params=params(56),
        cost_estimate=lasting(7.3 * pairs),
        name="self_forward",
    )(limit, q, k, v)


def self_back_kernel(
    limit_ref, q_ref, k_ref, v_ref, o_ref, do_ref, lse_ref, dq_ref, dk_ref, dv_ref, dqt,
    *, span, floor, block
):
    limit = limit_ref[0]
    lane = lax.broadcasted_iota(jnp.int32, (1, 128), 1)
    row = lax.broadcasted_iota(jnp.int32, (128, 1), 0)
    zero = jnp.zeros((), ROUND)
    factor = HEAD ** (-0.5)
    product_rows = do_ref[...].astype(FULL) * o_ref[...].astype(FULL)
    high = lower(product_rows)
    rest = lower(product_rows - high.astype(FULL))
    pick = lower(
        jnp.concatenate(
            [
                jnp.where(lane < HEAD, 1.0, 0.0),
                jnp.where(lane >= HEAD, 1.0, 0.0),
                jnp.zeros((6, 128), FULL),
            ],
            axis=0,
        )
    )
    delta = nt(pick, high) + nt(pick, rest)
    for start, size in blocks_of(span, block):
        end = start + size
        key = k_ref[start:end, :]
        value = v_ref[start:end, :]
        key_turned = key.T
        dk = 0.0
        dv = 0.0
        dq_add = 0.0
        for h in range(2):
            own_lanes = (lane < HEAD) if h == 0 else (lane >= HEAD)
            own_rows = (row < HEAD) if h == 0 else (row >= HEAD)
            query = jnp.where(own_lanes, q_ref[start:, :] * factor, zero)
            pulled = jnp.where(own_lanes, do_ref[start:, :], zero)
            probability = jnp.exp(nt(key, query) - lse_ref[0, h : h + 1, start:])
            pressure = nt(value, pulled)
            below = lax.broadcasted_iota(jnp.int32, (size, size), 0)
            across = lax.broadcasted_iota(jnp.int32, (size, size), 1)
            corner = jnp.where(below <= across, probability[:, :size], 0.0)
            if end < span:
                probability = jnp.concatenate([corner, probability[:, size:]], axis=1)
            else:
                probability = corner
            if end > floor:
                place = lax.broadcasted_iota(jnp.int32, (size, 1), 0) + start
                probability = jnp.where(place < limit, probability, 0.0)
            grad_scores = lower(probability * (pressure - delta[h : h + 1, start:]))
            dv = dv + nn(lower(probability), pulled)
            dk = dk + nn(grad_scores, query)
            dq_add = dq_add + nn(jnp.where(own_rows, key_turned, zero), grad_scores)
        dk_ref[start:end, :] = lower(dk)
        dv_ref[start:end, :] = lower(dv)
        if start == 0:
            dqt[...] = dq_add
        else:
            dqt[:, start:] += dq_add
    dq_ref[...] = lower(dqt[...].T * factor)


def self_back(limit, q, k, v, o, do, lse):
    span, wide = q.shape
    pairs = wide // 128
    floor = (span - span // 8 + 1) // 128 * 128
    pair = pl.BlockSpec((span, 128), lambda p, s: (0, p))
    return pl.pallas_call(
        functools.partial(self_back_kernel, span=span, floor=floor, block=256),
        grid_spec=pltpu.PrefetchScalarGridSpec(
            num_scalar_prefetch=1,
            grid=(pairs,),
            in_specs=[pair] * 5 + [pl.BlockSpec((1, 8, span), lambda p, s: (p, 0, 0))],
            out_specs=[pair] * 3,
            scratch_shapes=[pltpu.VMEM((128, span), FULL)],
        ),
        out_shape=[shape((span, wide), ROUND)] * 3,
        compiler_params=params(48),
        cost_estimate=lasting(1.050 * pairs),
        name="self_back",
    )(limit, q, k, v, o, do, lse)


def by_head(values_in, reduce, empty):
    lane = lax.broadcasted_iota(jnp.int32, (1, 128), 1)
    pieces = []
    for start in range(0, values_in.shape[1], 128):
        part = values_in[:, start : start + 128]
        first = reduce(jnp.where(lane < HEAD, part, empty), axis=1, keepdims=True)
        second = reduce(jnp.where(lane >= HEAD, part, empty), axis=1, keepdims=True)
        pieces.append(jnp.where(lane < HEAD, first, second))
    return jnp.concatenate(pieces, axis=1)


def cross_probability(query, keys):
    scores = nt(query * HEAD ** (-0.5), keys)
    weights_exp = jnp.exp(scores - by_head(scores, jnp.max, NEG))
    return weights_exp / by_head(weights_exp, jnp.sum, 0.0)


def in_groups(refs, axis):
    for at in (0, 3):
        yield refs[at][...]
        yield jnp.concatenate([refs[at + 1][...], refs[at + 2][...]], axis=axis)


def middle_forward_kernel(place_ref, frame_ref, *refs):
    mixed, wo, wq, wc = refs[0:6], refs[6:12], refs[12:18], refs[18:24]
    ck_ref, cv_ref, gain_ref, bias_ref = refs[24:28]
    x1_ref, x2_ref, h2_ref, cq_ref, ca_ref, h3_ref = refs[28:]
    x1 = frame_ref[...].astype(FULL)
    for o, weight in zip(in_groups(mixed, 1), in_groups(wo, 0)):
        x1 = x1 + nn(o, weight)
    x1_ref[...] = x1
    scaled, _ = norm_parts(x1)
    h2 = lower(scaled * gain_ref[1:2, :] + bias_ref[1:2, :])
    h2_ref[...] = h2
    for g, weight in enumerate(in_groups(wq, 1)):
        lanes = slice(g * 256, (g + 1) * 256)
        cq = lower(nn(h2, weight))
        cq_ref[:, lanes] = cq
        probability = cross_probability(cq, ck_ref[g])
        ca_ref[:, lanes] = lower(nn(lower(probability), cv_ref[g]))
    crossed = 0.0
    for g, weight in enumerate(in_groups(wc, 0)):
        crossed = crossed + nn(ca_ref[:, g * 256 : (g + 1) * 256], weight)
    x2 = x1_ref[...] + crossed
    x2_ref[...] = x2
    scaled, _ = norm_parts(x2)
    h3_ref[...] = lower(scaled * gain_ref[2:3, :] + bias_ref[2:3, :])


def middle_forward(place, frames, attended, received, wo, wq, wc, ck, cv, gains, biases):
    rows, width = frames.shape
    block = 416
    steps = rows // block
    wide = rows_of(block, width)
    whole = (*wo, *wq, *wc, ck, cv, gains, biases)
    return pl.pallas_call(
        middle_forward_kernel,
        grid_spec=pltpu.PrefetchScalarGridSpec(
            num_scalar_prefetch=1,
            grid=(steps,),
            in_specs=[wide]
            + [
                pl.BlockSpec((block, a.shape[1]), lambda i, s: (s[0] * steps + i, 0))
                for a in attended
            ]
            + [rows_of(block, a.shape[1]) for a in received]
            + [resident(a.shape) for a in whole],
            out_specs=[wide] * 6,
        ),
        out_shape=[shape((rows, width), FULL)] * 2 + [shape((rows, width), ROUND)] * 4,
        compiler_params=params(56),
        cost_estimate=lasting(22),
        name="middle_forward",
    )(place, frames, *attended, *received, *whole)


def keys_kernel(text_ref, weight_ref, out_ref):
    for item in range(2):
        for c in range(2):
            out_ref[item, c] = lower(nn(text_ref[item], weight_ref[c]))


def keys_of(text_states, weights):
    items, states, _ = text_states.shape
    return pl.pallas_call(
        keys_kernel,
        out_shape=shape((items, 2, states, weights.shape[2]), ROUND),
        compiler_params=params(24),
        cost_estimate=lasting(2),
        name="keys_of",
    )(text_states, weights)


def feed_kernel(place_ref, h_ref, d_ref, *refs, parts, carried):
    ups, downs = refs[:parts], refs[parts : 2 * parts]
    before = refs[2 * parts : 2 * parts + carried]
    g_ref, du_ref, out_ref, y_ref = refs[-4:]
    h = h_ref[...]
    d = d_ref[...]
    out = 0.0
    y = 0.0
    for n, (up_ref, down_ref) in enumerate(zip(ups, downs)):
        size = down_ref.shape[0]
        if parts == 1:
            lanes = slice(0, size)
        else:
            column = place_ref[2]
            which = column if n == 0 else 1 - column
            lanes = pl.ds(pl.multiple_of(which * size, 128), size)
        u = nn(h, up_ref[...])
        active, slope = gelu_parts(u)
        g = lower(active)
        g_ref[:, lanes] = g
        du = lower(nt(d, down_ref[...]) * slope)
        du_ref[:, lanes] = du
        out = out + nn(g, down_ref[...])
        y = y + nt(du, up_ref[...])
    if carried:
        out = before[0][...] + out
        y = before[1][...] + y
    out_ref[...] = out.astype(out_ref.dtype)
    y_ref[...] = y.astype(y_ref.dtype)


def feed(place, h, d, ups, downs, kind, half, before=(), shared=()):
    rows, width = h.shape
    block = 416
    steps = rows // block
    hidden = sum(a.shape[0] for a in downs)
    wide = rows_of(block, width)
    kept = pl.BlockSpec((block, hidden), lambda i, s: (i + half * steps, 0))
    there = pl.BlockSpec(memory_space=pl.ANY)
    parts = len(ups)
    at = 3 + 2 * parts + len(before)
    return pl.pallas_call(
        functools.partial(feed_kernel, parts=parts, carried=len(before)),
        grid_spec=pltpu.PrefetchScalarGridSpec(
            num_scalar_prefetch=1,
            grid=(steps,),
            in_specs=[wide, wide]
            + [resident(a.shape) for a in (*ups, *downs)]
            + [wide] * len(before)
            + [there] * len(shared),
            out_specs=[kept, kept, wide, wide],
        ),
        out_shape=[shape((2 * rows, hidden), ROUND)] * 2 + [shape((rows, width), kind)] * 2,
        input_output_aliases={at: 0, at + 1: 1} if shared else {},
        compiler_params=params(58),
        cost_estimate=lasting(13),
        name="feed",
    )(place, h, d, *ups, *downs, *before, *shared)


def up_grad_kernel(mine_ref, other_ref, du_ref, out_ref):
    rows = mine_ref.shape[0]
    total = tn(mine_ref[...], du_ref[:rows, :]) + tn(other_ref[...], du_ref[rows:, :])
    out_ref[...] = total.astype(out_ref.dtype)


def up_grad(mine, other, du, kind):
    rows, width = mine.shape
    hidden = du.shape[1]
    tile = 512
    whole = pl.BlockSpec((rows, width), lambda i: (0, 0), pipeline_mode=pl.Buffered(1))
    return pl.pallas_call(
        up_grad_kernel,
        grid=(hidden // tile,),
        in_specs=[whole, whole, pl.BlockSpec((2 * rows, tile), lambda i: (0, i))],
        out_specs=pl.BlockSpec((width, tile), lambda i: (0, i)),
        out_shape=shape((width, hidden), kind),
        compiler_params=params(48),
        cost_estimate=lasting(0.750),
        name="up_grad",
    )(mine, other, du)


def down_grad_kernel(g_ref, mine_ref, other_ref, out_ref):
    rows = mine_ref.shape[0]
    total = tn(g_ref[:rows, :], mine_ref[...]) + tn(g_ref[rows:, :], other_ref[...])
    out_ref[...] = total.astype(out_ref.dtype)


def down_grad(g, mine, other, kind):
    rows, width = mine.shape
    hidden = g.shape[1]
    tile = 512
    whole = pl.BlockSpec((rows, width), lambda i: (0, 0), pipeline_mode=pl.Buffered(1))
    return pl.pallas_call(
        down_grad_kernel,
        grid=(hidden // tile,),
        in_specs=[pl.BlockSpec((2 * rows, tile), lambda i: (0, i)), whole, whole],
        out_specs=pl.BlockSpec((tile, width), lambda i: (i, 0)),
        out_shape=shape((hidden, width), kind),
        compiler_params=params(48),
        cost_estimate=lasting(3.50),
        name="down_grad",
    )(g, mine, other)


def qkv_grad_kernel(place_ref, h_ref, *refs):
    out_ref = refs[-1]
    rows, width = h_ref.shape[0] // 2, h_ref.shape[1]
    core, near = place_ref[0], place_ref[1]
    halves = (len(refs) - 1) // 3
    total = [0.0] * 3
    for half in range(2):
        turned = h_ref[half * rows : (half + 1) * rows, :].T
        at = pl.multiple_of((core if half == 0 else 1 - core) * rows, 16)
        for c in range(3):
            parts = [refs[3 * n + c][pl.ds(at, rows), :] for n in range(halves)]
            grads = parts[0] if halves == 1 else jnp.concatenate(parts, axis=1)
            total[c] = total[c] + nn(turned, grads)
    for c in range(3):
        part = slice(c * width, (c + 1) * width)
        value = total[c].astype(out_ref.dtype)
        if halves == 1:
            out_ref[part, :] = value
        else:
            out_ref[part, pl.ds(pl.multiple_of(near * 128, 128), 128)] = value[:, :128]
            out_ref[part, pl.ds(pl.multiple_of((1 - near) * 128, 128), 128)] = value[:, 128:]


def qkv_grad(place, h, grads, kind):
    width = h.shape[1]
    return pl.pallas_call(
        qkv_grad_kernel,
        grid_spec=pltpu.PrefetchScalarGridSpec(
            num_scalar_prefetch=1,
            grid=(1,),
            in_specs=[resident(a.shape) for a in (h, *grads)],
            out_specs=resident((3 * width, 256)),
        ),
        out_shape=shape((3 * width, 256), kind),
        compiler_params=params(48),
        cost_estimate=lasting(3.50),
        name="qkv_grad",
    )(place, h, *grads)


def query_grad_kernel(place_ref, mine_ref, other_ref, dm_ref, do_ref, out_ref, *, split):
    column = place_ref[2]
    total = tn(mine_ref[...], dm_ref[...]) + tn(other_ref[...], do_ref[...])
    value = total.astype(out_ref.dtype)
    if split:
        out_ref[:, pl.ds(pl.multiple_of(column * 128, 128), 128)] = value[:, :128]
        out_ref[:, pl.ds(pl.multiple_of((1 - column) * 128, 128), 128)] = value[:, 128:]
    else:
        out_ref[...] = value


def query_grad(place, group, mine, other, d_mine, d_other, kind):
    rows, width = mine.shape
    lanes = pl.BlockSpec((rows, 256), lambda i, s: (0, group))
    return pl.pallas_call(
        functools.partial(query_grad_kernel, split=group == 1),
        grid_spec=pltpu.PrefetchScalarGridSpec(
            num_scalar_prefetch=1,
            grid=(1,),
            in_specs=[resident(mine.shape), resident(other.shape), lanes, lanes],
            out_specs=resident((width, 256)),
        ),
        out_shape=shape((width, 256), kind),
        compiler_params=params(48),
        cost_estimate=lasting(0.429),
        name="query_grad",
    )(place, mine, other, d_mine, d_other)


def outputs_grad_kernel(place_ref, *refs, count):
    o_refs = refs[:count]
    sm_ref, so_ref, am_ref, ao_ref, cm_ref, co_ref, out_ref = refs[count:]
    rows = sm_ref.shape[0]
    core, near, column = place_ref[0], place_ref[1], place_ref[2]
    mine_at = pl.ds(pl.multiple_of(core * rows, 16), rows)
    other_at = pl.ds(pl.multiple_of((1 - core) * rows, 16), rows)
    for n, o_ref in enumerate(o_refs):
        total = tn(o_ref[mine_at, :], sm_ref[...]) + tn(o_ref[other_at, :], so_ref[...])
        if count == 1:
            at = slice(0, 256)
        else:
            at = pl.ds(pl.multiple_of((near if n == 0 else 1 - near) * 128, 128), 128)
        out_ref[at, :] = total.astype(out_ref.dtype)
    total = tn(am_ref[...], cm_ref[...]) + tn(ao_ref[...], co_ref[...])
    value = total.astype(out_ref.dtype)
    if count == 1:
        out_ref[256:, :] = value
    else:
        out_ref[pl.ds(pl.multiple_of(256 + column * 128, 128), 128), :] = value[:128, :]
        out_ref[pl.ds(pl.multiple_of(384 - column * 128, 128), 128), :] = value[128:, :]


def outputs_grad(place, group, o, dself, dself_other, ca, ca_other, dcross, dcross_other, kind):
    rows, width = dself.shape
    lanes = pl.BlockSpec((rows, 256), lambda i, s: (0, group))
    whole = resident((rows, width))
    return pl.pallas_call(
        functools.partial(outputs_grad_kernel, count=len(o)),
        grid_spec=pltpu.PrefetchScalarGridSpec(
            num_scalar_prefetch=1,
            grid=(1,),
            in_specs=[resident(a.shape) for a in o] + [whole, whole, lanes, lanes, whole, whole],
            out_specs=resident((512, width)),
        ),
        out_shape=shape((512, width), kind),
        compiler_params=params(48),
        cost_estimate=lasting(0.643),
        name="outputs_grad",
    )(place, *o, dself, dself_other, ca, ca_other, dcross, dcross_other)


def middle_back_kernel(place_ref, ym_ref, yr_ref, x1_ref, x2_ref, d_ref, cq_ref, *refs):
    wq, wc = refs[0:6], refs[6:12]
    ck_ref, cv_ref, gain_ref = refs[12:15]
    dx1_ref, dself_ref, dcross_ref, dcq_ref, dck_ref, dcv_ref, sums_ref = refs[15:22]
    dck_all, dcv_all = refs[22:]
    step = pl.program_id(0)

    @pl.when(step == 0)
    def _():
        dck_all[...] = jnp.zeros_like(dck_all)
        dcv_all[...] = jnp.zeros_like(dcv_all)
        sums_ref[...] = jnp.zeros_like(sums_ref)

    y3 = ym_ref[...] + yr_ref[...].astype(FULL)
    scaled, inverse = norm_parts(x2_ref[...])
    sums_ref[4:5, :] += jnp.sum(y3 * scaled, axis=0, keepdims=True)
    sums_ref[5:6, :] += jnp.sum(y3, axis=0, keepdims=True)
    dx2 = d_ref[...].astype(FULL) + norm_pull(y3, scaled, inverse, gain_ref[2:3, :])
    dx1_ref[...] = dx2
    dcross = lower(dx2)
    dcross_ref[...] = dcross
    for g, weight in enumerate(in_groups(wc, 0)):
        lanes = slice(g * 256, (g + 1) * 256)
        dcatt = lower(nt(dcross, weight))
        keys = ck_ref[g]
        cq = cq_ref[:, lanes]
        probability = cross_probability(cq, keys)
        weighed = nt(dcatt, cv_ref[g])
        inner = by_head(probability * weighed, jnp.sum, 0.0)
        dcs = lower(probability * (weighed - inner))
        dcq_ref[:, lanes] = lower(nn(dcs, keys) * HEAD ** (-0.5))
        dck_all[g] += tn(dcs, cq * HEAD ** (-0.5))
        dcv_all[g] += tn(lower(probability), dcatt)
    y2 = 0.0
    for g, weight in enumerate(in_groups(wq, 1)):
        y2 = y2 + nt(dcq_ref[:, g * 256 : (g + 1) * 256], weight)
    scaled, inverse = norm_parts(x1_ref[...])
    sums_ref[2:3, :] += jnp.sum(y2 * scaled, axis=0, keepdims=True)
    sums_ref[3:4, :] += jnp.sum(y2, axis=0, keepdims=True)
    dx1 = dx1_ref[...] + norm_pull(y2, scaled, inverse, gain_ref[1:2, :])
    dx1_ref[...] = dx1
    dself_ref[...] = lower(dx1)

    @pl.when(step == pl.num_programs(0) - 1)
    def _():
        for every, result in ((dck_all, dck_ref), (dcv_all, dcv_ref)):
            for g in range(4):
                total = 0.0
                for h in range(4):
                    lane = lax.broadcasted_iota(jnp.int32, (1, 256), 1) // HEAD
                    total = total + jnp.where(lane == h, every[g, h * 64 : (h + 1) * 64, :], 0.0)
                result[g] = total


def middle_back(place, ym, yr, x1, x2, d, cq, wq, wc, ck, cv, gains):
    rows, width = x1.shape
    block = 416
    wide = rows_of(block, width)
    small = pl.BlockSpec((4, 64, 256), lambda i, s: (0, 0, 0))
    whole = (*wq, *wc, ck, cv, gains)
    return pl.pallas_call(
        middle_back_kernel,
        grid_spec=pltpu.PrefetchScalarGridSpec(
            num_scalar_prefetch=1,
            grid=(rows // block,),
            in_specs=[wide] * 6 + [resident(a.shape) for a in whole],
            out_specs=[wide] * 4 + [small, small, pl.BlockSpec((8, width), lambda i, s: (0, 0))],
            scratch_shapes=[pltpu.VMEM((4, 256, 256), FULL)] * 2,
        ),
        out_shape=[shape((rows, width), FULL)]
        + [shape((rows, width), ROUND)] * 3
        + [shape((4, 64, 256), FULL)] * 2
        + [shape((8, width), FULL)],
        compiler_params=params(56),
        cost_estimate=lasting(2.571),
        name="middle_back",
    )(place, ym, yr, x1, x2, d, cq, *whole)


def first_back_kernel(place_ref, *refs):
    y_ref = refs[-1]
    y = 0.0
    for n in range(3):
        for c in range(3):
            y = y + nt(refs[3 * n + c][...], refs[9 + n][c])
    y_ref[...] = y.astype(y_ref.dtype)


def first_back(place, grads, weights, kind):
    span = grads[0].shape[0]
    rows = span // 2
    width = weights[0].shape[1]
    block = 416
    steps = rows // block
    return pl.pallas_call(
        first_back_kernel,
        grid_spec=pltpu.PrefetchScalarGridSpec(
            num_scalar_prefetch=1,
            grid=(steps,),
            in_specs=[
                pl.BlockSpec((block, a.shape[1]), lambda i, s: (s[0] * steps + i, 0))
                for a in grads
            ]
            + [resident(a.shape) for a in weights],
            out_specs=rows_of(block, width),
        ),
        out_shape=shape((rows, width), kind),
        compiler_params=params(40),
        cost_estimate=lasting(0.535),
        name="first_back",
    )(place, *grads, *weights)


def frames_back_kernel(place_ref, ym_ref, yr_ref, dx1_ref, frame_ref, gain_ref, out_ref, sums_ref):
    @pl.when(pl.program_id(0) == 0)
    def _():
        sums_ref[...] = jnp.zeros_like(sums_ref)

    y = ym_ref[...] + yr_ref[...].astype(FULL)
    scaled, inverse = norm_parts(frame_ref[...].astype(FULL))
    sums_ref[0:1, :] += jnp.sum(y * scaled, axis=0, keepdims=True)
    sums_ref[1:2, :] += jnp.sum(y, axis=0, keepdims=True)
    out_ref[...] = lower(dx1_ref[...] + norm_pull(y, scaled, inverse, gain_ref[0:1, :]))


def frames_back(place, ym, yr, dx1, frames, gains):
    rows, width = dx1.shape
    block = 208
    wide = rows_of(block, width)
    return pl.pallas_call(
        frames_back_kernel,
        grid_spec=pltpu.PrefetchScalarGridSpec(
            num_scalar_prefetch=1,
            grid=(rows // block,),
            in_specs=[wide] * 4 + [resident(gains.shape)],
            out_specs=[wide, pl.BlockSpec((8, width), lambda i, s: (0, 0))],
        ),
        out_shape=[shape((rows, width), ROUND), shape((8, width), FULL)],
        compiler_params=params(24),
        cost_estimate=lasting(0.643),
        name="frames_back",
    )(place, ym, yr, dx1, frames, gains)


def chip_local(
    frames, text_states, lengths, loss_mask, norm_gain, norm_bias, w_qkv, w_out, w_cross_q,
    w_cross_kv, w_cross_out, w_up, w_down, cotangent,
):
    at = lax.axis_index("narrow")
    core = at % 2
    side = at // 2
    column = lax.axis_index("wide") % 2
    layer = lax.axis_index("wide") // 2
    near = layer % 2
    place = jnp.stack([core, near, column]).astype(jnp.int32)
    away = jnp.stack([1 - core, near, column]).astype(jnp.int32)
    limit = lax.dynamic_slice(lengths, (side,), (1,))
    rows, width = frames.shape
    join = lax.optimization_barrier

    def over_core(v):
        return lax.ppermute(v, "narrow", CORE_PAIRS)

    def over_y(v):
        return lax.ppermute(v, "narrow", Y_PAIRS)

    def along_wide(v, pairs):
        return lax.ppermute(v, "wide", pairs)

    def half_of(v, which, axis=0):
        half = v.shape[axis] // 2
        return lax.dynamic_slice_in_dim(v, which * half, half, axis=axis)

    def ordered(first, second, which):
        return jnp.where(
            which == 0,
            jnp.concatenate([first, second], axis=0),
            jnp.concatenate([second, first], axis=0),
        )

    def over_z(v):
        return along_wide(v, Z_NEAR)

    def over_x(v):
        return along_wide(v, X_PAIRS)

    def away_rows(v):
        return half_of(v, 1 - core)

    def cross_order(v):
        return jnp.where(column == 0, v, jnp.concatenate([v[..., 128:], v[..., :128]], axis=-1))

    qkv_first = over_y(half_of(w_qkv, near, 2))
    frames_other = over_core(frames)
    h1, q0, k0, v0 = first_project(place, frames, frames_other, norm_gain, norm_bias, w_qkv)
    q0, qkv_first, w_out, w_cross_q, w_cross_out, cotangent = join(
        (q0, qkv_first, w_out, w_cross_q, w_cross_out, cotangent)
    )

    qkv_second = over_z(qkv_first)
    out_first = over_y(half_of(w_out, near))
    query_first = over_y(half_of(w_cross_q, column, 1))
    cross_out_first = over_y(half_of(w_cross_out, column))
    o0, lse0 = self_forward(limit, q0, k0, v0)
    qf, kf, vf = project(place, h1, qkv_first)
    out_other, query_other, cross_out_other = map(over_core, (w_out, w_cross_q, w_cross_out))
    qf, o0, out_first, query_first, cross_out_first, w_up, w_down, *core_got = join(
        (qf, o0, out_first, query_first, cross_out_first, w_up, w_down)
        + (out_other, query_other, cross_out_other)
    )

    out_other, query_other, cross_out_other = core_got
    out_second = over_z(out_first)
    query_second = over_x(query_first)
    cross_out_second = over_x(cross_out_first)
    up_first = over_y(half_of(w_up, column, 1))
    down_sent = half_of(w_down, column)
    o0_other = over_core(away_rows(o0))
    keys = keys_of(text_states, w_cross_kv)
    own_keys = lax.dynamic_index_in_dim(keys, side, keepdims=False)
    keys_y = over_y(lax.dynamic_index_in_dim(keys, 1 - side, keepdims=False))
    of, lse_f = self_forward(limit, qf, kf, vf)
    of, qkv_second, keys_y, o0_other = join((of, qkv_second, keys_y, o0_other))

    qs, ks, vs = project(place, h1, qkv_second)
    of_other = over_core(away_rows(of))
    pair = jnp.stack([own_keys, cross_order(keys_y)])
    pair_other = over_core(pair)
    o_s, lse_s = self_forward(limit, qs, ks, vs)
    o_s, out_second, query_second, cross_out_second, up_first, down_sent, pair_other, of_other = join(
        (o_s, out_second, query_second, cross_out_second, up_first, down_sent, pair_other, of_other)
    )

    down_first = over_y(down_sent)
    up_second = over_x(up_first)
    os_other = over_core(away_rows(o_s))
    dout = jnp.where(loss_mask[:, None] != 0, cotangent, jnp.zeros((), ROUND))

    def pieces(own, first, second, own_other):
        return (own, first, second, own_other, over_core(first), over_core(second))

    wo = pieces(w_out, out_first, out_second, out_other)
    wq = pieces(w_cross_q, query_first, query_second, query_other)
    wc = pieces(w_cross_out, cross_out_first, cross_out_second, cross_out_other)
    text = lax.dynamic_index_in_dim(text_states, side, keepdims=False)
    head_of = jnp.arange(256) // HEAD
    same = head_of[:, None] == head_of[None, :]

    def spread_heads(v):
        return jnp.where(same, jnp.tile(v, (1, 4, 1)), jnp.zeros((), ROUND))

    every = jnp.concatenate([pair, pair_other], axis=0)
    ck, cv = spread_heads(every[:, 0]), spread_heads(every[:, 1])
    x1, x2, h2, cq, ca, h3 = middle_forward(
        place, frames, (o0, of, o_s), (o0_other, of_other, os_other), wo, wq, wc, ck, cv,
        norm_gain, norm_bias,
    )
    h3, ca, h2, up_second, down_first, dout = join((h3, ca, h2, up_second, down_first, dout))

    h3_other = over_core(h3)
    dout_other = over_core(dout)
    down_second = over_x(down_first)
    g0, du0, out_m, y_m = feed(place, h3, dout, (w_up,), (w_down,), FULL, 0)
    g0, du0, out_o, y_o = feed(
        place, h3_other, dout_other, (w_up,), (w_down,), FULL, 1, shared=(g0, du0)
    )
    y_o, down_second, ca, h2 = join((y_o, down_second, ca, h2))

    ups = (up_first, up_second)
    downs = (down_first, down_second)
    g1, du1, out_o, y_o = feed(
        place, h3_other, dout_other, ups, downs, ROUND, 1, before=(out_o, y_o)
    )
    y_received = over_core(y_o)
    h2_other = over_core(h2)
    ca_other = over_core(ca[:, 512:])
    g1, du1, out_m, y_m = feed(
        place, h3, dout, ups, downs, FULL, 0, before=(out_m, y_m), shared=(g1, du1)
    )

    def plus(a, b):
        return lower(a.astype(FULL) + b.astype(FULL))

    across = (column, X_PAIRS)
    down_z = (near, Z_NEAR)
    store = {}
    last = []
    free = []

    def order(*names):
        if free:
            return
        names = tuple(dict.fromkeys((*names, *last)))
        for name, value in zip(names, join(tuple(store[name] for name in names))):
            store[name] = value

    def get(*names):
        return tuple(store[name] for name in names)

    def step(results, make, *needs):
        order(*needs)
        made = make()
        made = made if isinstance(made, (tuple, list)) else (made,)
        store.update(zip(results, made))
        last[:] = results[:1]

    class Sum:
        def __init__(self, name, axes=(across, down_z)):
            self.fly, self.kept, self.axes = name + "_fly", name + "_kept", axes

        def over_y(self, partner):
            order(partner)
            store[self.fly] = over_y(store[partner])

        def first(self, own):
            which, pairs = self.axes[0]
            order(self.fly, own)
            mine, fly = get(own, self.fly)
            away_half = plus(half_of(mine, 1 - which), half_of(fly, 1 - which))
            store[self.kept] = half_of(mine, which).astype(FULL) + half_of(fly, which).astype(FULL)
            store[self.fly] = along_wide(away_half, pairs)
            last[:] = [self.kept]

        def first_alone(self, own):
            which, pairs = self.axes[0]
            store[self.kept] = half_of(store[own], which).astype(FULL)
            store[self.fly] = along_wide(half_of(store[own], 1 - which), pairs)
            last[:] = [self.kept]

        def second(self):
            which, pairs = self.axes[1]
            order(self.fly, self.kept)
            total = store[self.kept] + store[self.fly].astype(FULL)
            store[self.kept] = half_of(total, which)
            store[self.fly] = along_wide(lower(half_of(total, 1 - which)), pairs)
            last[:] = [self.kept]

        def add(self, pairs):
            order(self.fly, self.kept)
            store[self.kept] = plus(*get(self.kept, self.fly))
            store[self.fly] = along_wide(store[self.kept], pairs)
            last[:] = [self.kept]

        def far(self):
            self.add(Z_FAR)

        def back(self):
            self.add(self.axes[1][1])

        def along(self):
            order(self.fly, self.kept)
            store[self.kept] = ordered(*get(self.kept, self.fly), self.axes[1][0])
            store[self.fly] = along_wide(store[self.kept], self.axes[0][1])
            last[:] = [self.kept]

        def end(self, result):
            order(self.fly, self.kept)
            store[result] = ordered(*get(self.kept, self.fly), self.axes[0][0]).astype(FULL)
            last[:] = [result]

    class Row:
        def __init__(self, name, value, move):
            self.fly, self.kept = name + "_fly", name + "_kept"
            store[self.kept] = value
            store[self.fly] = move(value)

        def then(self, move):
            order(self.fly, self.kept)
            store[self.kept] = store[self.kept] + store[self.fly]
            store[self.fly] = move(store[self.kept])
            last[:] = [self.kept]

        def total(self):
            return store[self.kept] + store[self.fly]

    up, down, outs, qkv = Sum("up"), Sum("down"), Sum("outs"), Sum("qkv")
    cross_in = Sum("cross_in", (down_z, across))
    store.update(h3_other=h3_other, du1=du1, g1=g1, du0=du0, g0=g0, y_m=y_m, y_fly=y_received)
    store.update(of=of, o_s=o_s, o0=o0, x2=x2, h2_other=h2_other, ca_other=ca_other)

    def middle():
        dx1, *rest = middle_back(
            place, *get("y_m", "y_fly"), x1, store["x2"], dout, cq, wq, wc, ck, cv, norm_gain
        )
        return (rest[0], dx1, *rest[1:])

    step(["up1"], lambda: up_grad(h3, *get("h3_other", "du1"), ROUND), "du1", "du0")
    up.over_y("up1")
    step(["down1"], lambda: down_grad(store["g1"], dout, dout_other, ROUND), "g1")
    step(["dself", "dx1", "dcross", "dcq", "dck", "dcv", "sums"], middle, "y_fly", "y_m", "x2")
    store["dself_other"] = over_core(store["dself"])
    step(["up0"], lambda: up_grad(h3, *get("h3_other", "du0"), ROUND), "du0")
    order(up.fly, "down1", "dself_other")
    down.over_y("down1")
    up.first("up0")
    step(
        ["dof", "dos", "do0"],
        lambda: pull(place, *get("dself", "dself_other"), (out_first, out_second, w_out)),
        "dself",
        "dself_other",
        "dcross",
        "dcq",
    )
    store["dcross_other"] = over_core(store["dcross"])
    store["dcq_other"] = over_core(store["dcq"][:, 512:])
    d_pair = jnp.stack(get("dck", "dcv"), axis=1)
    store["pair_kept"] = d_pair[:2]
    store["pair_fly"] = over_core(d_pair[2:])
    step(
        ["dqf", "dkf", "dvf"],
        lambda: self_back(limit, qf, kf, vf, store["of"], store["dof"], lse_f),
        "dof",
    )
    def query(g):
        return query_grad(place, g, h2, *get("h2_other", "dcq", "dcq_other"), ROUND)

    def outof(g, *o):
        return outputs_grad(
            place, g, get(*o), *get("dself", "dself_other"), ca,
            *get("ca_other", "dcross", "dcross_other"), ROUND,
        )

    step(["query1"], lambda: query(1), "dcq_other", "h2_other", "pair_fly", "pair_kept")
    pair_sum = lower(store["pair_kept"] + store["pair_fly"])
    store["pair"] = pair_sum[0]
    store["pair_other"] = cross_order(pair_sum[1])
    up.second()
    step(
        ["dqs", "dks", "dvs"],
        lambda: self_back(limit, qs, ks, vs, store["o_s"], store["dos"], lse_s),
        "dos",
    )
    up.far()
    step(["down0"], lambda: down_grad(store["g0"], dout, dout_other, ROUND), "g0")
    yp = ("dqf", "dkf", "dvf", "dqs", "dks", "dvs")
    step(["qkv1"], lambda: qkv_grad(place, h1, get(*yp), ROUND), "dqs")
    order(down.fly, "qkv1", "query1", "pair_other")
    store["query_fly"] = over_y(store["query1"])
    store["pair_y"] = over_y(store["pair_other"])
    qkv.over_y("qkv1")
    down.first("down0")
    step(
        ["dq0", "dk0", "dv0"],
        lambda: self_back(limit, q0, k0, v0, store["o0"], store["do0"], lse0),
        "do0",
    )
    down.second()
    up.back()
    step(["outs1"], lambda: outof(1, "of", "o_s"), "dcross_other", "ca_other")
    outs.over_y("outs1")
    nine = ("dq0", "dk0", "dv0", *yp)
    weights = (w_qkv, qkv_first, qkv_second)
    step(["yo"], lambda: first_back(away, get(*nine), weights, ROUND), "dq0")
    store["yo_fly"] = over_core(store["yo"])
    step(["qkv0"], lambda: qkv_grad(place, h1, get("dq0", "dk0", "dv0"), ROUND), "dq0")
    qkv.first("qkv0")
    up.along()
    down.far()
    step(["query0"], lambda: query(0), "dcq")
    order("query0", "query_fly", "pair", "pair_y")
    other_text = lax.dynamic_index_in_dim(text_states, 1 - side, keepdims=False)
    texts = jnp.concatenate([text, other_text], axis=0)
    pairs = jnp.concatenate(get("pair", "pair_y"), axis=1)
    store["into0"] = jnp.concatenate(
        [
            lower(store["query0"].astype(FULL) + store["query_fly"].astype(FULL)),
            lower(tn(texts, pairs[0])),
            lower(tn(texts, pairs[1])),
        ],
        axis=0,
    )
    cross_in.first_alone("into0")
    step(["ym"], lambda: first_back(place, get(*nine), weights, FULL), "dq0")
    step(
        ["grad_frames", "first_sums"],
        lambda: frames_back(place, *get("ym", "yo_fly", "dx1"), frames, norm_gain),
        "ym",
        "yo_fly",
        "outs_fly",
    )
    norms = Row("norms", store["sums"] + store["first_sums"], over_core)
    norms.then(over_y)
    cross_in.second()
    qkv.second()
    step(["outs0"], lambda: outof(0, "o0"), "dcross")
    outs.first("outs0")
    norms.then(over_z)
    text_part = 0.0
    for c in range(2):
        text_part = text_part + nt(pairs[c], w_cross_kv[c])
    text_mine, text_theirs = text_part[:64], text_part[64:]
    text_rows = Row("texts", text_mine, lambda v: over_y(text_theirs))
    last[:] = ["texts_kept"]
    down.back()
    up.end("grad_up")
    cross_in.far()
    store["out_fly"] = over_core(out_o)
    text_rows.then(over_core)
    norms.then(lambda v: along_wide(v, Z_FAR))
    outs.second()
    qkv.far()
    order("x2", "out_fly")
    out_rows = lower(store["x2"] + out_m + store["out_fly"].astype(FULL))
    down.along()
    cross_in.back()
    order("texts_fly", "texts_kept")
    text_grad = lower(text_rows.total())
    text_away = over_y(text_grad)
    grad_text = ordered(text_grad[None], text_away[None], side)
    outs.far()
    norms.then(over_x)
    qkv.back()
    cross_in.along()
    outs.back()
    down.end("grad_down")
    qkv.along()
    outs.along()
    cross_in.end("grad_in")
    sums = norms.total()
    qkv.end("grad_qkv")
    outs.end("grad_outs")
    grad_in, grad_outs = get("grad_in", "grad_outs")
    return (
        out_rows,
        store["grad_frames"],
        grad_text,
        sums[0:6:2],
        sums[1:6:2],
        store["grad_qkv"].reshape(3, width, 256),
        grad_outs[:256],
        grad_in[:width],
        grad_in[width:].reshape(2, width, 256),
        grad_outs[256:],
        store["grad_up"],
        store["grad_down"],
    )


def solution(mesh):
    chips = dict(mesh.shape) == {"wide": 8, "narrow": 4}
    return jax.shard_map(
        chip_local if chips else general_local,
        mesh=mesh,
        in_specs=(
            P(("wide", "narrow"), None),
            P("wide", None, None),
            P("wide"),
            P(("wide", "narrow")),
            P(),
            P(),
            P(None, None, "narrow"),
            P("narrow", None),
            P(None, "narrow"),
            P(None, None, "narrow"),
            P("narrow", None),
            P(None, "narrow"),
            P("narrow", None),
            P(("wide", "narrow"), None),
        ),
        out_specs=(
            P(("wide", "narrow"), None),
            P(("wide", "narrow"), None),
            P("wide", None, None),
            P(),
            P(),
            P(None, None, "narrow"),
            P("narrow", None),
            P(None, "narrow"),
            P(None, None, "narrow"),
            P("narrow", None),
            P(None, "narrow"),
            P("narrow", None),
        ),
        check_vma=False,
    )
```

```python
import functools

import jax
import jax.numpy as jnp
from jax import lax
from jax.experimental import pallas as pl
from jax.experimental.pallas import tpu as pltpu
from jax.sharding import PartitionSpec as P

HEAD = 64


EPS = 1e-05
NEG = -1e30


def lower(values_in):
    return values_in.astype(jnp.bfloat16)


def product(left_side, right_side, transposed):
    if transposed:
        return lax.dot_general(
            left_side, right_side, (((1,), (1,)), ((), ())), preferred_element_type=jnp.float32
        )
    return jnp.dot(left_side, right_side, preferred_element_type=jnp.float32)


def outer_sum(left_side, right_side):
    return lax.dot_general(
        left_side, right_side, (((0,), (0,)), ((), ())), preferred_element_type=jnp.float32
    )


def normalize(values_in, gain_row, bias_row):
    row_mean = jnp.mean(values_in, axis=-1, keepdims=True)
    centered = values_in - row_mean
    inverse = lax.rsqrt(jnp.mean(centered * centered, axis=-1, keepdims=True) + EPS)
    scaled = centered * inverse
    return (scaled * gain_row + bias_row, scaled, inverse)


def normalize_back(upstream, scaled, inverse, gain_row):
    weighted = upstream * gain_row
    inner_mean = jnp.mean(weighted, axis=-1, keepdims=True)
    along_mean = jnp.mean(weighted * scaled, axis=-1, keepdims=True)
    grad_input = inverse * (weighted - inner_mean - scaled * along_mean)
    return (grad_input, jnp.sum(upstream * scaled, axis=0), jnp.sum(upstream, axis=0))


def gelu_parts(values_in):
    normal_cdf = 0.5 * (1.0 + jax.scipy.special.erf(values_in * 0.7071067811865476))
    normal_pdf = jnp.exp(-0.5 * values_in * values_in) * 0.3989422804014327
    return (values_in * normal_cdf, normal_cdf + values_in * normal_pdf)


def scores_of(query_part, key_part, valid):
    scores = jnp.einsum(
        "bhe,khe->hbk", query_part, key_part, preferred_element_type=jnp.float32
    ) * HEAD ** (-0.5)
    return jnp.where(valid, scores, NEG)


def attend(query_part, key_part, value_part, valid):
    scores = scores_of(query_part, key_part, valid)
    row_top = jnp.max(scores, axis=-1, keepdims=True)
    weights_exp = jnp.exp(scores - row_top)
    denominator = jnp.sum(weights_exp, axis=-1, keepdims=True)
    probability = weights_exp / denominator
    mixed = jnp.einsum(
        "hbk,khe->bhe", lower(probability), value_part, preferred_element_type=jnp.float32
    )
    return (lower(mixed), (row_top + jnp.log(denominator))[..., 0])


def attend_back(query_part, key_part, value_part, valid, summary, upstream):
    scores = scores_of(query_part, key_part, valid)
    probability = jnp.exp(scores - summary[..., None])
    pressure = jnp.einsum("bhe,khe->hbk", upstream, value_part, preferred_element_type=jnp.float32)
    grad_scores = lower(
        probability * (pressure - jnp.sum(probability * pressure, axis=-1, keepdims=True))
    )
    factor = HEAD ** (-0.5)
    grad_query = (
        jnp.einsum("hbk,khe->bhe", grad_scores, key_part, preferred_element_type=jnp.float32)
        * factor
    )
    grad_key = (
        jnp.einsum("hbk,bhe->khe", grad_scores, query_part, preferred_element_type=jnp.float32)
        * factor
    )
    grad_value = jnp.einsum(
        "hbk,bhe->khe", lower(probability), upstream, preferred_element_type=jnp.float32
    )
    return (grad_query, grad_key, grad_value)


def general_local(
    frames,
    text_states,
    lengths,
    loss_mask,
    norm_gain,
    norm_bias,
    w_qkv,
    w_out,
    w_cross_q,
    w_cross_kv,
    w_cross_out,
    w_up,
    w_down,
    cotangent,
):
    row_count = frames.shape[0]
    width = frames.shape[1]
    item_count = lengths.shape[0]
    span = row_count * lax.axis_size("narrow") // item_count
    half_span = span // 2
    inner_width = w_qkv.shape[2]
    head_count = inner_width // HEAD
    text_count = text_states.shape[1]
    full_rows = item_count * span
    places = jnp.arange(span, dtype=jnp.int32)

    def spread(shard_rows):
        return lax.all_gather(shard_rows, "narrow", axis=0, tiled=True)

    def collect(left_side, right_side, transposed):
        return lax.psum_scatter(
            product(
                lax.slice_in_dim(left_side, 0, lax.axis_size("narrow") * row_count, axis=0),
                right_side,
                transposed,
            ),
            "narrow",
            scatter_dimension=0,
            tiled=True,
        )

    def causal(block_index, item_limit):
        query_place = block_index * half_span + jnp.arange(half_span, dtype=jnp.int32)
        return (places[None, :] <= query_place[:, None]) & (places[None, :] < item_limit)

    frame_rows = frames.astype(jnp.float32)
    normed_one, scaled_one, inverse_one = normalize(frame_rows, norm_gain[0], norm_bias[0])
    first_input = spread(lower(normed_one))
    triple = lower(
        jnp.einsum("rd,cde->cre", first_input, w_qkv, preferred_element_type=jnp.float32)
    )
    triple = triple.reshape(3, item_count, span, head_count, HEAD)

    def self_item(packed):
        query_part, key_part, value_part, item_limit = packed
        mixed_list = []
        summary_list = []
        for block_index in range(2):
            mixed, summary = attend(
                query_part[block_index * half_span : (block_index + 1) * half_span],
                key_part,
                value_part,
                causal(block_index, item_limit),
            )
            mixed_list.append(mixed)
            summary_list.append(summary)
        return (jnp.concatenate(mixed_list, axis=0), jnp.stack(summary_list, axis=0))

    attended, self_summary = lax.map(self_item, (triple[0], triple[1], triple[2], lengths))
    attended_flat = attended.reshape(full_rows, inner_width)
    first_rows = frame_rows + collect(attended_flat, w_out, False)
    normed_two, scaled_two, inverse_two = normalize(first_rows, norm_gain[1], norm_bias[1])
    second_input = spread(lower(normed_two))
    cross_query = lower(product(second_input, w_cross_q, False)).reshape(
        item_count, span, head_count, HEAD
    )
    cross_pair = lower(
        jnp.einsum("ntd,cde->cnte", text_states, w_cross_kv, preferred_element_type=jnp.float32)
    )
    cross_pair = cross_pair.reshape(2, item_count, text_count, head_count, HEAD)

    def cross_item(packed):
        query_part, key_part, value_part = packed
        return attend(query_part, key_part, value_part, True)

    cross_mixed, cross_summary = lax.map(cross_item, (cross_query, cross_pair[0], cross_pair[1]))
    cross_flat = cross_mixed.reshape(full_rows, inner_width)
    second_rows = first_rows + collect(cross_flat, w_cross_out, False)
    normed_three, scaled_three, inverse_three = normalize(second_rows, norm_gain[2], norm_bias[2])
    upstream = cotangent.astype(jnp.float32) * loss_mask.astype(jnp.float32)[:, None]
    ffn_grad = lower(upstream)
    ffn_input = spread(lower(normed_three))
    hidden_pre = product(ffn_input, w_up, False)
    active, slope = gelu_parts(hidden_pre)
    active = lower(active)
    out_rows = second_rows + collect(active, w_down, False)
    ffn_full = spread(ffn_grad)
    grad_down = outer_sum(active, ffn_full)
    grad_hidden = lower(product(ffn_full, w_down, True) * slope)
    grad_up = outer_sum(ffn_input, grad_hidden)
    back_three = collect(grad_hidden, w_up, True)
    grad_up, grad_down = (grad_up, grad_down)
    grad_in_three, gain_three, bias_three = normalize_back(
        back_three, scaled_three, inverse_three, norm_gain[2]
    )
    grad_second = upstream + grad_in_three
    cross_full = spread(lower(grad_second))
    grad_cross_out = outer_sum(cross_flat, cross_full)
    cross_upstream = lower(product(cross_full, w_cross_out, True)).reshape(
        item_count, span, head_count, HEAD
    )

    def cross_back(packed):
        query_part, key_part, value_part, summary, upstream_item = packed
        return attend_back(query_part, key_part, value_part, True, summary, upstream_item)

    grad_cq, grad_ck, grad_cv = lax.map(
        cross_back, (cross_query, cross_pair[0], cross_pair[1], cross_summary, cross_upstream)
    )
    grad_cq = lower(grad_cq).reshape(full_rows, inner_width)
    grad_pair = lower(jnp.stack((grad_ck, grad_cv), axis=0)).reshape(
        2, item_count, text_count, inner_width
    )
    grad_cross_q = outer_sum(second_input, grad_cq)
    grad_cross_kv = jnp.einsum(
        "ntd,cnte->cde", text_states, grad_pair, preferred_element_type=jnp.float32
    )
    grad_cross_q, grad_cross_kv, grad_cross_out = (grad_cross_q, grad_cross_kv, grad_cross_out)
    text_partial = jnp.einsum(
        "cnte,cde->ntd", grad_pair, w_cross_kv, preferred_element_type=jnp.float32
    )
    grad_text = lower(lax.psum(text_partial, "narrow"))
    back_two = collect(grad_cq, w_cross_q, True)
    grad_in_two, gain_two, bias_two = normalize_back(
        back_two, scaled_two, inverse_two, norm_gain[1]
    )
    grad_first = grad_second + grad_in_two
    self_full = spread(lower(grad_first))
    grad_out = outer_sum(attended_flat, self_full)
    self_upstream = lower(product(self_full, w_out, True)).reshape(
        item_count, span, head_count, HEAD
    )

    def self_back(packed):
        query_part, key_part, value_part, item_limit, summary, upstream_item = packed
        query_list = []
        key_list = []
        value_list = []
        for block_index in range(2):
            lower_row = block_index * half_span
            grad_query, grad_key, grad_value = attend_back(
                query_part[lower_row : lower_row + half_span],
                key_part,
                value_part,
                causal(block_index, item_limit),
                summary[block_index],
                upstream_item[lower_row : lower_row + half_span],
            )
            query_list.append(grad_query)
            key_list.append(grad_key)
            value_list.append(grad_value)
        return (
            jnp.concatenate(query_list, axis=0),
            key_list[0] + key_list[1],
            value_list[0] + value_list[1],
        )

    grad_q, grad_k, grad_v = lax.map(
        self_back, (triple[0], triple[1], triple[2], lengths, self_summary, self_upstream)
    )
    grad_triple = lower(jnp.stack((grad_q, grad_k, grad_v), axis=0)).reshape(
        3, full_rows, inner_width
    )
    grad_qkv = jnp.einsum(
        "rd,cre->cde", first_input, grad_triple, preferred_element_type=jnp.float32
    )
    grad_qkv, grad_out = (grad_qkv, grad_out)
    merged = grad_triple.transpose(1, 0, 2).reshape(full_rows, 3 * inner_width)
    stacked_weights = w_qkv.transpose(0, 2, 1).reshape(3 * inner_width, width)
    back_one = collect(merged, stacked_weights, False)
    grad_in_one, gain_one, bias_one = normalize_back(
        back_one, scaled_one, inverse_one, norm_gain[0]
    )
    grad_frames = lower(grad_first + grad_in_one)
    gain_terms = jnp.stack((gain_one, gain_two, gain_three), axis=0)
    bias_terms = jnp.stack((bias_one, bias_two, bias_three), axis=0)
    grad_norm_gain, grad_norm_bias = lax.psum((gain_terms, bias_terms), ("wide", "narrow"))
    grad_qkv, grad_out, grad_cross_q, grad_cross_kv, grad_cross_out, grad_up, grad_down = lax.psum(
        (grad_qkv, grad_out, grad_cross_q, grad_cross_kv, grad_cross_out, grad_up, grad_down),
        "wide",
    )
    return (
        lower(out_rows),
        grad_frames,
        grad_text,
        grad_norm_gain,
        grad_norm_bias,
        grad_qkv,
        grad_out,
        grad_cross_q,
        grad_cross_kv,
        grad_cross_out,
        grad_up,
        grad_down,
    )


ROUND = jnp.bfloat16
FULL = jnp.float32
CORE_PAIRS = ((0, 1), (1, 0), (2, 3), (3, 2))
Y_PAIRS = ((0, 2), (2, 0), (1, 3), (3, 1))
X_PAIRS = tuple((i, i ^ 1) for i in range(8))
Z_INWARD = ((0, 2), (1, 3), (6, 4), (7, 5))
Z_MIDDLE = ((2, 4), (4, 2), (3, 5), (5, 3))
Z_OUTWARD = ((2, 0), (3, 1), (4, 6), (5, 7))
Z_NEAR = tuple((i, i ^ 2) for i in range(8))
Z_FAR = tuple((i, i ^ 4) for i in range(8))
MIB = 1 << 20


def nt(a, b):
    return lax.dot_general(a, b, (((1,), (1,)), ((), ())), preferred_element_type=FULL)


def nn(a, b):
    return lax.dot_general(a, b, (((1,), (0,)), ((), ())), preferred_element_type=FULL)


def tn(a, b):
    return lax.dot_general(a, b, (((0,), (0,)), ((), ())), preferred_element_type=FULL)


def shape(dims, kind):
    return jax.ShapeDtypeStruct(dims, kind)


def resident(dims):
    zeros = (0,) * len(dims)
    return pl.BlockSpec(dims, lambda i, s: zeros, pipeline_mode=pl.Buffered(1))


def rows_of(block, width):
    return pl.BlockSpec((block, width), lambda i, s: (i, 0))


def lasting(microseconds):
    flops = int(microseconds * 0.28 * 1.15e9)
    return pl.CostEstimate(flops=flops, bytes_accessed=1000, transcendentals=0)


def params(mib):
    return pltpu.CompilerParams(vmem_limit_bytes=mib * MIB)


def norm_parts(v):
    centered = v - jnp.mean(v, axis=-1, keepdims=True)
    inverse = lax.rsqrt(jnp.mean(centered * centered, axis=-1, keepdims=True) + EPS)
    return centered * inverse, inverse


def norm_pull(y, scaled, inverse, gain_row):
    weighted = y * gain_row
    inner = jnp.mean(weighted, axis=-1, keepdims=True)
    along = jnp.mean(weighted * scaled, axis=-1, keepdims=True)
    return inverse * (weighted - inner - scaled * along)


def first_project_kernel(
    place_ref, mine_ref, other_ref, gain_ref, bias_ref, weight_ref, h_ref, *out_refs
):
    half = pl.program_id(0)

    def run(source):
        for start in range(0, source.shape[0], 208):
            part = slice(start, start + 208)
            scaled, _ = norm_parts(source[part, :].astype(FULL))
            h = lower(scaled * gain_ref[0:1, :] + bias_ref[0:1, :])
            h_ref[part, :] = h
            for c, out_ref in enumerate(out_refs):
                out_ref[part, :] = lower(nn(h, weight_ref[c]))

    @pl.when(half == 0)
    def _():
        run(mine_ref)

    @pl.when(half == 1)
    def _():
        run(other_ref)


def first_project(place, mine, other, gains, biases, weights):
    rows, depth = mine.shape
    count, _, wide = weights.shape
    out = pl.BlockSpec((rows, wide), lambda i, s: ((i + s[0]) % 2, 0))
    return pl.pallas_call(
        first_project_kernel,
        grid_spec=pltpu.PrefetchScalarGridSpec(
            num_scalar_prefetch=1,
            grid=(2,),
            in_specs=[resident(a.shape) for a in (mine, other, gains, biases, weights)],
            out_specs=[rows_of(rows, depth)] + [out] * count,
        ),
        out_shape=[shape((2 * rows, depth), ROUND)] + [shape((2 * rows, wide), ROUND)] * count,
        compiler_params=params(40),
        cost_estimate=lasting(5),
        name="first_project",
    )(place, mine, other, gains, biases, weights)


def project_kernel(place_ref, h_ref, weight_ref, *out_refs):
    count = len(out_refs)
    wide = weight_ref.shape[2]
    weights = jnp.concatenate([weight_ref[c] for c in range(count)], axis=1)
    for start in range(0, h_ref.shape[0], 416):
        part = slice(start, start + 416)
        result = lower(nn(h_ref[part, :], weights))
        for c, out_ref in enumerate(out_refs):
            out_ref[part, :] = result[:, c * wide : (c + 1) * wide]


def project(place, h, weights):
    rows, depth = h.shape[0] // 2, h.shape[1]
    count, _, wide = weights.shape
    out = pl.BlockSpec((rows, wide), lambda i, s: ((i + s[0]) % 2, 0))
    return pl.pallas_call(
        project_kernel,
        grid_spec=pltpu.PrefetchScalarGridSpec(
            num_scalar_prefetch=1,
            grid=(2,),
            in_specs=[rows_of(rows, depth), resident(weights.shape)],
            out_specs=[out] * count,
        ),
        out_shape=[shape((2 * rows, wide), ROUND)] * count,
        compiler_params=params(40),
        cost_estimate=lasting(4),
        name="project",
    )(place, h, weights)


def pull_kernel(place_ref, mine_ref, other_ref, *refs):
    half = pl.program_id(0)
    count = len(refs) // 2

    def run(source):
        for weight_ref, out_ref in zip(refs[:count], refs[count:]):
            out_ref[...] = lower(nt(source[...], weight_ref[...]))

    @pl.when(half == 0)
    def _():
        run(mine_ref)

    @pl.when(half == 1)
    def _():
        run(other_ref)


def pull(place, mine, other, weights):
    rows = mine.shape[0]
    return pl.pallas_call(
        pull_kernel,
        grid_spec=pltpu.PrefetchScalarGridSpec(
            num_scalar_prefetch=1,
            grid=(2,),
            in_specs=[resident(a.shape) for a in (mine, other, *weights)],
            out_specs=[
                pl.BlockSpec((rows, a.shape[0]), lambda i, s: ((i + s[0]) % 2, 0)) for a in weights
            ],
        ),
        out_shape=[shape((2 * rows, a.shape[0]), ROUND) for a in weights],
        compiler_params=params(32),
        cost_estimate=lasting(0.375),
        name="pull",
    )(place, mine, other, *weights)


def blocks_of(span, block):
    return [(start, min(block, span - start)) for start in range(0, span, block)]


def self_forward_kernel(
    limit_ref, q_ref, k_ref, v_ref, o_ref, lse_ref, *, span, floor, block
):
    limit = limit_ref[0]
    lane = lax.broadcasted_iota(jnp.int32, (1, 128), 1)
    row = lax.broadcasted_iota(jnp.int32, (128, 1), 0)
    zero = jnp.zeros((), ROUND)
    value_turned = v_ref[...].T
    for start, size in blocks_of(span, block):
        end = start + size
        mixed_list = []
        for h in range(2):
            own_lanes = (lane < HEAD) if h == 0 else (lane >= HEAD)
            query = jnp.where(own_lanes, q_ref[start:end, :] * HEAD ** (-0.5), zero)
            parts = []
            for low in range(0, end, block):
                high = min(low + block, end)
                scores = nt(k_ref[low:high, :], query)
                if low == start:
                    key = lax.broadcasted_iota(jnp.int32, (size, size), 0)
                    valid = key <= lax.broadcasted_iota(jnp.int32, (size, size), 1)
                    if high > floor:
                        valid = valid & (key + low < limit)
                    scores = jnp.where(valid, scores, NEG)
                elif high > floor:
                    key = lax.broadcasted_iota(jnp.int32, (high - low, 1), 0)
                    scores = jnp.where(key + low < limit, scores, NEG)
                parts.append((low, high, scores))
            top = functools.reduce(
                jnp.maximum, [jnp.max(s, axis=0, keepdims=True) for _, _, s in parts]
            )
            total = 0.0
            mixed = 0.0
            for low, high, scores in parts:
                weights_exp = jnp.exp(scores - top)
                total = total + jnp.sum(weights_exp, axis=0, keepdims=True)
                mixed = mixed + nn(value_turned[:, low:high], lower(weights_exp))
            mixed_list.append(mixed / total)
            lse_ref[0, h : h + 1, start:end] = top + jnp.log(total)
        o_ref[start:end, :] = lower(jnp.where(row < HEAD, mixed_list[0], mixed_list[1]).T)


def self_forward(limit, q, k, v):
    span, wide = q.shape
    pairs = wide // 128
    floor = (span - span // 8 + 1) // 128 * 128
    pair = pl.BlockSpec((span, 128), lambda p, s: (0, p))
    return pl.pallas_call(
        functools.partial(self_forward_kernel, span=span, floor=floor, block=512),
        grid_spec=pltpu.PrefetchScalarGridSpec(
            num_scalar_prefetch=1,
            grid=(pairs,),
            in_specs=[pair] * 3,
            out_specs=[pair, pl.BlockSpec((1, 8, span), lambda p, s: (p, 0, 0))],
        ),
        out_shape=[shape((span, wide), ROUND), shape((pairs, 8, span), FULL)],
        compiler_params=params(56),
        cost_estimate=lasting(7.3 * pairs),
        name="self_forward",
    )(limit, q, k, v)


def self_back_kernel(
    limit_ref, q_ref, k_ref, v_ref, o_ref, do_ref, lse_ref, dq_ref, dk_ref, dv_ref, dqt,
    *, span, floor, block
):
    limit = limit_ref[0]
    lane = lax.broadcasted_iota(jnp.int32, (1, 128), 1)
    row = lax.broadcasted_iota(jnp.int32, (128, 1), 0)
    zero = jnp.zeros((), ROUND)
    factor = HEAD ** (-0.5)
    product_rows = do_ref[...].astype(FULL) * o_ref[...].astype(FULL)
    high = lower(product_rows)
    rest = lower(product_rows - high.astype(FULL))
    pick = lower(
        jnp.concatenate(
            [
                jnp.where(lane < HEAD, 1.0, 0.0),
                jnp.where(lane >= HEAD, 1.0, 0.0),
                jnp.zeros((6, 128), FULL),
            ],
            axis=0,
        )
    )
    delta = nt(pick, high) + nt(pick, rest)
    for start, size in blocks_of(span, block):
        end = start + size
        key = k_ref[start:end, :]
        value = v_ref[start:end, :]
        key_turned = key.T
        dk = 0.0
        dv = 0.0
        dq_add = 0.0
        for h in range(2):
            own_lanes = (lane < HEAD) if h == 0 else (lane >= HEAD)
            own_rows = (row < HEAD) if h == 0 else (row >= HEAD)
            query = jnp.where(own_lanes, q_ref[start:, :] * factor, zero)
            pulled = jnp.where(own_lanes, do_ref[start:, :], zero)
            probability = jnp.exp(nt(key, query) - lse_ref[0, h : h + 1, start:])
            pressure = nt(value, pulled)
            below = lax.broadcasted_iota(jnp.int32, (size, size), 0)
            across = lax.broadcasted_iota(jnp.int32, (size, size), 1)
            corner = jnp.where(below <= across, probability[:, :size], 0.0)
            if end < span:
                probability = jnp.concatenate([corner, probability[:, size:]], axis=1)
            else:
                probability = corner
            if end > floor:
                place = lax.broadcasted_iota(jnp.int32, (size, 1), 0) + start
                probability = jnp.where(place < limit, probability, 0.0)
            grad_scores = lower(probability * (pressure - delta[h : h + 1, start:]))
            dv = dv + nn(lower(probability), pulled)
            dk = dk + nn(grad_scores, query)
            dq_add = dq_add + nn(jnp.where(own_rows, key_turned, zero), grad_scores)
        dk_ref[start:end, :] = lower(dk)
        dv_ref[start:end, :] = lower(dv)
        if start == 0:
            dqt[...] = dq_add
        else:
            dqt[:, start:] += dq_add
    dq_ref[...] = lower(dqt[...].T * factor)


def self_back(limit, q, k, v, o, do, lse):
    span, wide = q.shape
    pairs = wide // 128
    floor = (span - span // 8 + 1) // 128 * 128
    pair = pl.BlockSpec((span, 128), lambda p, s: (0, p))
    return pl.pallas_call(
        functools.partial(self_back_kernel, span=span, floor=floor, block=256),
        grid_spec=pltpu.PrefetchScalarGridSpec(
            num_scalar_prefetch=1,
            grid=(pairs,),
            in_specs=[pair] * 5 + [pl.BlockSpec((1, 8, span), lambda p, s: (p, 0, 0))],
            out_specs=[pair] * 3,
            scratch_shapes=[pltpu.VMEM((128, span), FULL)],
        ),
        out_shape=[shape((span, wide), ROUND)] * 3,
        compiler_params=params(48),
        cost_estimate=lasting(1.050 * pairs),
        name="self_back",
    )(limit, q, k, v, o, do, lse)


def by_head(values_in, reduce, empty):
    lane = lax.broadcasted_iota(jnp.int32, (1, 128), 1)
    pieces = []
    for start in range(0, values_in.shape[1], 128):
        part = values_in[:, start : start + 128]
        first = reduce(jnp.where(lane < HEAD, part, empty), axis=1, keepdims=True)
        second = reduce(jnp.where(lane >= HEAD, part, empty), axis=1, keepdims=True)
        pieces.append(jnp.where(lane < HEAD, first, second))
    return jnp.concatenate(pieces, axis=1)


def cross_probability(query, keys):
    scores = nt(query * HEAD ** (-0.5), keys)
    weights_exp = jnp.exp(scores - by_head(scores, jnp.max, NEG))
    return weights_exp / by_head(weights_exp, jnp.sum, 0.0)


def in_groups(refs, axis):
    for at in (0, 3):
        yield refs[at][...]
        yield jnp.concatenate([refs[at + 1][...], refs[at + 2][...]], axis=axis)


def middle_forward_kernel(place_ref, frame_ref, *refs):
    mixed, wo, wq, wc = refs[0:6], refs[6:12], refs[12:18], refs[18:24]
    ck_ref, cv_ref, gain_ref, bias_ref = refs[24:28]
    x1_ref, x2_ref, h2_ref, cq_ref, ca_ref, h3_ref = refs[28:]
    x1 = frame_ref[...].astype(FULL)
    for o, weight in zip(in_groups(mixed, 1), in_groups(wo, 0)):
        x1 = x1 + nn(o, weight)
    x1_ref[...] = x1
    scaled, _ = norm_parts(x1)
    h2 = lower(scaled * gain_ref[1:2, :] + bias_ref[1:2, :])
    h2_ref[...] = h2
    for g, weight in enumerate(in_groups(wq, 1)):
        lanes = slice(g * 256, (g + 1) * 256)
        cq = lower(nn(h2, weight))
        cq_ref[:, lanes] = cq
        probability = cross_probability(cq, ck_ref[g])
        ca_ref[:, lanes] = lower(nn(lower(probability), cv_ref[g]))
    crossed = 0.0
    for g, weight in enumerate(in_groups(wc, 0)):
        crossed = crossed + nn(ca_ref[:, g * 256 : (g + 1) * 256], weight)
    x2 = x1_ref[...] + crossed
    x2_ref[...] = x2
    scaled, _ = norm_parts(x2)
    h3_ref[...] = lower(scaled * gain_ref[2:3, :] + bias_ref[2:3, :])


def middle_forward(place, frames, attended, received, wo, wq, wc, ck, cv, gains, biases):
    rows, width = frames.shape
    block = 416
    steps = rows // block
    wide = rows_of(block, width)
    whole = (*wo, *wq, *wc, ck, cv, gains, biases)
    return pl.pallas_call(
        middle_forward_kernel,
        grid_spec=pltpu.PrefetchScalarGridSpec(
            num_scalar_prefetch=1,
            grid=(steps,),
            in_specs=[wide]
            + [
                pl.BlockSpec((block, a.shape[1]), lambda i, s: (s[0] * steps + i, 0))
                for a in attended
            ]
            + [rows_of(block, a.shape[1]) for a in received]
            + [resident(a.shape) for a in whole],
            out_specs=[wide] * 6,
        ),
        out_shape=[shape((rows, width), FULL)] * 2 + [shape((rows, width), ROUND)] * 4,
        compiler_params=params(56),
        cost_estimate=lasting(22),
        name="middle_forward",
    )(place, frames, *attended, *received, *whole)


def keys_kernel(text_ref, weight_ref, out_ref):
    for item in range(2):
        for c in range(2):
            out_ref[item, c] = lower(nn(text_ref[item], weight_ref[c]))


def keys_of(text_states, weights):
    items, states, _ = text_states.shape
    return pl.pallas_call(
        keys_kernel,
        out_shape=shape((items, 2, states, weights.shape[2]), ROUND),
        compiler_params=params(24),
        cost_estimate=lasting(2),
        name="keys_of",
    )(text_states, weights)


def feed_kernel(place_ref, h_ref, d_ref, *refs, parts, carried):
    ups, downs = refs[:parts], refs[parts : 2 * parts]
    before = refs[2 * parts : 2 * parts + carried]
    g_ref, du_ref, out_ref, y_ref = refs[-4:]
    h = h_ref[...]
    d = d_ref[...]
    out = 0.0
    y = 0.0
    for n, (up_ref, down_ref) in enumerate(zip(ups, downs)):
        size = down_ref.shape[0]
        if parts == 1:
            lanes = slice(0, size)
        else:
            column = place_ref[2]
            which = column if n == 0 else 1 - column
            lanes = pl.ds(pl.multiple_of(which * size, 128), size)
        u = nn(h, up_ref[...])
        active, slope = gelu_parts(u)
        g = lower(active)
        g_ref[:, lanes] = g
        du = lower(nt(d, down_ref[...]) * slope)
        du_ref[:, lanes] = du
        out = out + nn(g, down_ref[...])
        y = y + nt(du, up_ref[...])
    if carried:
        out = before[0][...] + out
        y = before[1][...] + y
    out_ref[...] = out.astype(out_ref.dtype)
    y_ref[...] = y.astype(y_ref.dtype)


def feed(place, h, d, ups, downs, kind, half, before=(), shared=()):
    rows, width = h.shape
    block = 416
    steps = rows // block
    hidden = sum(a.shape[0] for a in downs)
    wide = rows_of(block, width)
    kept = pl.BlockSpec((block, hidden), lambda i, s: (i + half * steps, 0))
    there = pl.BlockSpec(memory_space=pl.ANY)
    parts = len(ups)
    at = 3 + 2 * parts + len(before)
    return pl.pallas_call(
        functools.partial(feed_kernel, parts=parts, carried=len(before)),
        grid_spec=pltpu.PrefetchScalarGridSpec(
            num_scalar_prefetch=1,
            grid=(steps,),
            in_specs=[wide, wide]
            + [resident(a.shape) for a in (*ups, *downs)]
            + [wide] * len(before)
            + [there] * len(shared),
            out_specs=[kept, kept, wide, wide],
        ),
        out_shape=[shape((2 * rows, hidden), ROUND)] * 2 + [shape((rows, width), kind)] * 2,
        input_output_aliases={at: 0, at + 1: 1} if shared else {},
        compiler_params=params(58),
        cost_estimate=lasting(13),
        name="feed",
    )(place, h, d, *ups, *downs, *before, *shared)


def up_grad_kernel(mine_ref, other_ref, du_ref, out_ref):
    rows = mine_ref.shape[0]
    total = tn(mine_ref[...], du_ref[:rows, :]) + tn(other_ref[...], du_ref[rows:, :])
    out_ref[...] = total.astype(out_ref.dtype)


def up_grad(mine, other, du, kind):
    rows, width = mine.shape
    hidden = du.shape[1]
    tile = 512
    whole = pl.BlockSpec((rows, width), lambda i: (0, 0), pipeline_mode=pl.Buffered(1))
    return pl.pallas_call(
        up_grad_kernel,
        grid=(hidden // tile,),
        in_specs=[whole, whole, pl.BlockSpec((2 * rows, tile), lambda i: (0, i))],
        out_specs=pl.BlockSpec((width, tile), lambda i: (0, i)),
        out_shape=shape((width, hidden), kind),
        compiler_params=params(48),
        cost_estimate=lasting(0.750),
        name="up_grad",
    )(mine, other, du)


def down_grad_kernel(g_ref, mine_ref, other_ref, out_ref):
    rows = mine_ref.shape[0]
    total = tn(g_ref[:rows, :], mine_ref[...]) + tn(g_ref[rows:, :], other_ref[...])
    out_ref[...] = total.astype(out_ref.dtype)


def down_grad(g, mine, other, kind):
    rows, width = mine.shape
    hidden = g.shape[1]
    tile = 512
    whole = pl.BlockSpec((rows, width), lambda i: (0, 0), pipeline_mode=pl.Buffered(1))
    return pl.pallas_call(
        down_grad_kernel,
        grid=(hidden // tile,),
        in_specs=[pl.BlockSpec((2 * rows, tile), lambda i: (0, i)), whole, whole],
        out_specs=pl.BlockSpec((tile, width), lambda i: (i, 0)),
        out_shape=shape((hidden, width), kind),
        compiler_params=params(48),
        cost_estimate=lasting(3.50),
        name="down_grad",
    )(g, mine, other)


def qkv_grad_kernel(place_ref, h_ref, *refs):
    out_ref = refs[-1]
    rows, width = h_ref.shape[0] // 2, h_ref.shape[1]
    core, near = place_ref[0], place_ref[1]
    halves = (len(refs) - 1) // 3
    total = [0.0] * 3
    for half in range(2):
        turned = h_ref[half * rows : (half + 1) * rows, :].T
        at = pl.multiple_of((core if half == 0 else 1 - core) * rows, 16)
        for c in range(3):
            parts = [refs[3 * n + c][pl.ds(at, rows), :] for n in range(halves)]
            grads = parts[0] if halves == 1 else jnp.concatenate(parts, axis=1)
            total[c] = total[c] + nn(turned, grads)
    for c in range(3):
        part = slice(c * width, (c + 1) * width)
        value = total[c].astype(out_ref.dtype)
        if halves == 1:
            out_ref[part, :] = value
        else:
            out_ref[part, pl.ds(pl.multiple_of(near * 128, 128), 128)] = value[:, :128]
            out_ref[part, pl.ds(pl.multiple_of((1 - near) * 128, 128), 128)] = value[:, 128:]


def qkv_grad(place, h, grads, kind):
    width = h.shape[1]
    return pl.pallas_call(
        qkv_grad_kernel,
        grid_spec=pltpu.PrefetchScalarGridSpec(
            num_scalar_prefetch=1,
            grid=(1,),
            in_specs=[resident(a.shape) for a in (h, *grads)],
            out_specs=resident((3 * width, 256)),
        ),
        out_shape=shape((3 * width, 256), kind),
        compiler_params=params(48),
        cost_estimate=lasting(3.50),
        name="qkv_grad",
    )(place, h, *grads)


def query_grad_kernel(place_ref, mine_ref, other_ref, dm_ref, do_ref, out_ref, *, split):
    column = place_ref[2]
    total = tn(mine_ref[...], dm_ref[...]) + tn(other_ref[...], do_ref[...])
    value = total.astype(out_ref.dtype)
    if split:
        out_ref[:, pl.ds(pl.multiple_of(column * 128, 128), 128)] = value[:, :128]
        out_ref[:, pl.ds(pl.multiple_of((1 - column) * 128, 128), 128)] = value[:, 128:]
    else:
        out_ref[...] = value


def query_grad(place, group, mine, other, d_mine, d_other, kind):
    rows, width = mine.shape
    lanes = pl.BlockSpec((rows, 256), lambda i, s: (0, group))
    return pl.pallas_call(
        functools.partial(query_grad_kernel, split=group == 1),
        grid_spec=pltpu.PrefetchScalarGridSpec(
            num_scalar_prefetch=1,
            grid=(1,),
            in_specs=[resident(mine.shape), resident(other.shape), lanes, lanes],
            out_specs=resident((width, 256)),
        ),
        out_shape=shape((width, 256), kind),
        compiler_params=params(48),
        cost_estimate=lasting(0.429),
        name="query_grad",
    )(place, mine, other, d_mine, d_other)


def outputs_grad_kernel(place_ref, *refs, count):
    o_refs = refs[:count]
    sm_ref, so_ref, am_ref, ao_ref, cm_ref, co_ref, out_ref = refs[count:]
    rows = sm_ref.shape[0]
    core, near, column = place_ref[0], place_ref[1], place_ref[2]
    mine_at = pl.ds(pl.multiple_of(core * rows, 16), rows)
    other_at = pl.ds(pl.multiple_of((1 - core) * rows, 16), rows)
    for n, o_ref in enumerate(o_refs):
        total = tn(o_ref[mine_at, :], sm_ref[...]) + tn(o_ref[other_at, :], so_ref[...])
        if count == 1:
            at = slice(0, 256)
        else:
            at = pl.ds(pl.multiple_of((near if n == 0 else 1 - near) * 128, 128), 128)
        out_ref[at, :] = total.astype(out_ref.dtype)
    total = tn(am_ref[...], cm_ref[...]) + tn(ao_ref[...], co_ref[...])
    value = total.astype(out_ref.dtype)
    if count == 1:
        out_ref[256:, :] = value
    else:
        out_ref[pl.ds(pl.multiple_of(256 + column * 128, 128), 128), :] = value[:128, :]
        out_ref[pl.ds(pl.multiple_of(384 - column * 128, 128), 128), :] = value[128:, :]


def outputs_grad(place, group, o, dself, dself_other, ca, ca_other, dcross, dcross_other, kind):
    rows, width = dself.shape
    lanes = pl.BlockSpec((rows, 256), lambda i, s: (0, group))
    whole = resident((rows, width))
    return pl.pallas_call(
        functools.partial(outputs_grad_kernel, count=len(o)),
        grid_spec=pltpu.PrefetchScalarGridSpec(
            num_scalar_prefetch=1,
            grid=(1,),
            in_specs=[resident(a.shape) for a in o] + [whole, whole, lanes, lanes, whole, whole],
            out_specs=resident((512, width)),
        ),
        out_shape=shape((512, width), kind),
        compiler_params=params(48),
        cost_estimate=lasting(0.643),
        name="outputs_grad",
    )(place, *o, dself, dself_other, ca, ca_other, dcross, dcross_other)


def middle_back_kernel(place_ref, ym_ref, yr_ref, x1_ref, x2_ref, d_ref, cq_ref, *refs):
    wq, wc = refs[0:6], refs[6:12]
    ck_ref, cv_ref, gain_ref = refs[12:15]
    dx1_ref, dself_ref, dcross_ref, dcq_ref, dck_ref, dcv_ref, sums_ref = refs[15:22]
    dck_all, dcv_all = refs[22:]
    step = pl.program_id(0)

    @pl.when(step == 0)
    def _():
        dck_all[...] = jnp.zeros_like(dck_all)
        dcv_all[...] = jnp.zeros_like(dcv_all)
        sums_ref[...] = jnp.zeros_like(sums_ref)

    y3 = ym_ref[...] + yr_ref[...].astype(FULL)
    scaled, inverse = norm_parts(x2_ref[...])
    sums_ref[4:5, :] += jnp.sum(y3 * scaled, axis=0, keepdims=True)
    sums_ref[5:6, :] += jnp.sum(y3, axis=0, keepdims=True)
    dx2 = d_ref[...].astype(FULL) + norm_pull(y3, scaled, inverse, gain_ref[2:3, :])
    dx1_ref[...] = dx2
    dcross = lower(dx2)
    dcross_ref[...] = dcross
    for g, weight in enumerate(in_groups(wc, 0)):
        lanes = slice(g * 256, (g + 1) * 256)
        dcatt = lower(nt(dcross, weight))
        keys = ck_ref[g]
        cq = cq_ref[:, lanes]
        probability = cross_probability(cq, keys)
        weighed = nt(dcatt, cv_ref[g])
        inner = by_head(probability * weighed, jnp.sum, 0.0)
        dcs = lower(probability * (weighed - inner))
        dcq_ref[:, lanes] = lower(nn(dcs, keys) * HEAD ** (-0.5))
        dck_all[g] += tn(dcs, cq * HEAD ** (-0.5))
        dcv_all[g] += tn(lower(probability), dcatt)
    y2 = 0.0
    for g, weight in enumerate(in_groups(wq, 1)):
        y2 = y2 + nt(dcq_ref[:, g * 256 : (g + 1) * 256], weight)
    scaled, inverse = norm_parts(x1_ref[...])
    sums_ref[2:3, :] += jnp.sum(y2 * scaled, axis=0, keepdims=True)
    sums_ref[3:4, :] += jnp.sum(y2, axis=0, keepdims=True)
    dx1 = dx1_ref[...] + norm_pull(y2, scaled, inverse, gain_ref[1:2, :])
    dx1_ref[...] = dx1
    dself_ref[...] = lower(dx1)

    @pl.when(step == pl.num_programs(0) - 1)
    def _():
        for every, result in ((dck_all, dck_ref), (dcv_all, dcv_ref)):
            for g in range(4):
                total = 0.0
                for h in range(4):
                    lane = lax.broadcasted_iota(jnp.int32, (1, 256), 1) // HEAD
                    total = total + jnp.where(lane == h, every[g, h * 64 : (h + 1) * 64, :], 0.0)
                result[g] = total


def middle_back(place, ym, yr, x1, x2, d, cq, wq, wc, ck, cv, gains):
    rows, width = x1.shape
    block = 416
    wide = rows_of(block, width)
    small = pl.BlockSpec((4, 64, 256), lambda i, s: (0, 0, 0))
    whole = (*wq, *wc, ck, cv, gains)
    return pl.pallas_call(
        middle_back_kernel,
        grid_spec=pltpu.PrefetchScalarGridSpec(
            num_scalar_prefetch=1,
            grid=(rows // block,),
            in_specs=[wide] * 6 + [resident(a.shape) for a in whole],
            out_specs=[wide] * 4 + [small, small, pl.BlockSpec((8, width), lambda i, s: (0, 0))],
            scratch_shapes=[pltpu.VMEM((4, 256, 256), FULL)] * 2,
        ),
        out_shape=[shape((rows, width), FULL)]
        + [shape((rows, width), ROUND)] * 3
        + [shape((4, 64, 256), FULL)] * 2
        + [shape((8, width), FULL)],
        compiler_params=params(56),
        cost_estimate=lasting(2.571),
        name="middle_back",
    )(place, ym, yr, x1, x2, d, cq, *whole)


def first_back_kernel(place_ref, *refs):
    y_ref = refs[-1]
    y = 0.0
    for n in range(3):
        for c in range(3):
            y = y + nt(refs[3 * n + c][...], refs[9 + n][c])
    y_ref[...] = y.astype(y_ref.dtype)


def first_back(place, grads, weights, kind):
    span = grads[0].shape[0]
    rows = span // 2
    width = weights[0].shape[1]
    block = 416
    steps = rows // block
    return pl.pallas_call(
        first_back_kernel,
        grid_spec=pltpu.PrefetchScalarGridSpec(
            num_scalar_prefetch=1,
            grid=(steps,),
            in_specs=[
                pl.BlockSpec((block, a.shape[1]), lambda i, s: (s[0] * steps + i, 0))
                for a in grads
            ]
            + [resident(a.shape) for a in weights],
            out_specs=rows_of(block, width),
        ),
        out_shape=shape((rows, width), kind),
        compiler_params=params(40),
        cost_estimate=lasting(0.535),
        name="first_back",
    )(place, *grads, *weights)


def frames_back_kernel(place_ref, ym_ref, yr_ref, dx1_ref, frame_ref, gain_ref, out_ref, sums_ref):
    @pl.when(pl.program_id(0) == 0)
    def _():
        sums_ref[...] = jnp.zeros_like(sums_ref)

    y = ym_ref[...] + yr_ref[...].astype(FULL)
    scaled, inverse = norm_parts(frame_ref[...].astype(FULL))
    sums_ref[0:1, :] += jnp.sum(y * scaled, axis=0, keepdims=True)
    sums_ref[1:2, :] += jnp.sum(y, axis=0, keepdims=True)
    out_ref[...] = lower(dx1_ref[...] + norm_pull(y, scaled, inverse, gain_ref[0:1, :]))


def frames_back(place, ym, yr, dx1, frames, gains):
    rows, width = dx1.shape
    block = 208
    wide = rows_of(block, width)
    return pl.pallas_call(
        frames_back_kernel,
        grid_spec=pltpu.PrefetchScalarGridSpec(
            num_scalar_prefetch=1,
            grid=(rows // block,),
            in_specs=[wide] * 4 + [resident(gains.shape)],
            out_specs=[wide, pl.BlockSpec((8, width), lambda i, s: (0, 0))],
        ),
        out_shape=[shape((rows, width), ROUND), shape((8, width), FULL)],
        compiler_params=params(24),
        cost_estimate=lasting(0.643),
        name="frames_back",
    )(place, ym, yr, dx1, frames, gains)


def chip_local(
    frames, text_states, lengths, loss_mask, norm_gain, norm_bias, w_qkv, w_out, w_cross_q,
    w_cross_kv, w_cross_out, w_up, w_down, cotangent,
):
    at = lax.axis_index("narrow")
    core = at % 2
    side = at // 2
    column = lax.axis_index("wide") % 2
    layer = lax.axis_index("wide") // 2
    near = layer % 2
    place = jnp.stack([core, near, column]).astype(jnp.int32)
    away = jnp.stack([1 - core, near, column]).astype(jnp.int32)
    limit = lax.dynamic_slice(lengths, (side,), (1,))
    rows, width = frames.shape
    join = lax.optimization_barrier

    def over_core(v):
        return lax.ppermute(v, "narrow", CORE_PAIRS)

    def over_y(v):
        return lax.ppermute(v, "narrow", Y_PAIRS)

    def along_wide(v, pairs):
        return lax.ppermute(v, "wide", pairs)

    def half_of(v, which, axis=0):
        half = v.shape[axis] // 2
        return lax.dynamic_slice_in_dim(v, which * half, half, axis=axis)

    def ordered(first, second, which):
        return jnp.where(
            which == 0,
            jnp.concatenate([first, second], axis=0),
            jnp.concatenate([second, first], axis=0),
        )

    def over_z(v):
        return along_wide(v, Z_NEAR)

    def over_x(v):
        return along_wide(v, X_PAIRS)

    def away_rows(v):
        return half_of(v, 1 - core)

    def cross_order(v):
        return jnp.where(column == 0, v, jnp.concatenate([v[..., 128:], v[..., :128]], axis=-1))

    qkv_first = over_y(half_of(w_qkv, near, 2))
    frames_other = over_core(frames)
    h1, q0, k0, v0 = first_project(place, frames, frames_other, norm_gain, norm_bias, w_qkv)
    q0, qkv_first, w_out, w_cross_q, w_cross_out, cotangent = join(
        (q0, qkv_first, w_out, w_cross_q, w_cross_out, cotangent)
    )

    qkv_second = over_z(qkv_first)
    both_first = over_y(
        jnp.concatenate([half_of(w_out, near), half_of(w_cross_out, column)], axis=0)
    )
    query_first = over_y(half_of(w_cross_q, column, 1))
    o0, lse0 = self_forward(limit, q0, k0, v0)
    qf, kf, vf = project(place, h1, qkv_first)
    out_other, query_other, cross_out_other = map(over_core, (w_out, w_cross_q, w_cross_out))
    qf, o0, both_first, query_first, w_up, w_down, *core_got = join(
        (qf, o0, both_first, query_first, w_up, w_down)
        + (out_other, query_other, cross_out_other)
    )
    out_first, cross_out_first = both_first[:128], both_first[128:]

    out_other, query_other, cross_out_other = core_got
    out_second = over_z(out_first)
    query_second = over_x(query_first)
    cross_out_second = over_x(cross_out_first)
    up_first = over_y(half_of(w_up, column, 1))
    down_sent = half_of(w_down, column)
    o0_other = over_core(away_rows(o0))
    keys = keys_of(text_states, w_cross_kv)
    own_keys = lax.dynamic_index_in_dim(keys, side, keepdims=False)
    keys_y = over_y(lax.dynamic_index_in_dim(keys, 1 - side, keepdims=False))
    of, lse_f = self_forward(limit, qf, kf, vf)
    of, qkv_second, keys_y, o0_other = join((of, qkv_second, keys_y, o0_other))

    qs, ks, vs = project(place, h1, qkv_second)
    of_other = over_core(away_rows(of))
    pair = jnp.stack([own_keys, cross_order(keys_y)])
    pair_other = over_core(pair)
    o_s, lse_s = self_forward(limit, qs, ks, vs)
    o_s, out_second, query_second, cross_out_second, up_first, down_sent, pair_other, of_other = join(
        (o_s, out_second, query_second, cross_out_second, up_first, down_sent, pair_other, of_other)
    )

    down_first = over_y(down_sent)
    up_second = over_x(up_first)
    os_other = over_core(away_rows(o_s))
    dout = jnp.where(loss_mask[:, None] != 0, cotangent, jnp.zeros((), ROUND))

    def pieces(own, first, second, own_other):
        return (own, first, second, own_other, over_core(first), over_core(second))

    wo = pieces(w_out, out_first, out_second, out_other)
    wq = pieces(w_cross_q, query_first, query_second, query_other)
    wc = pieces(w_cross_out, cross_out_first, cross_out_second, cross_out_other)
    text = lax.dynamic_index_in_dim(text_states, side, keepdims=False)
    head_of = jnp.arange(256) // HEAD
    same = head_of[:, None] == head_of[None, :]

    def spread_heads(v):
        return jnp.where(same, jnp.tile(v, (1, 4, 1)), jnp.zeros((), ROUND))

    every = jnp.concatenate([pair, pair_other], axis=0)
    ck, cv = spread_heads(every[:, 0]), spread_heads(every[:, 1])
    x1, x2, h2, cq, ca, h3 = middle_forward(
        place, frames, (o0, of, o_s), (o0_other, of_other, os_other), wo, wq, wc, ck, cv,
        norm_gain, norm_bias,
    )
    h3, ca, h2, up_second, down_first, dout = join((h3, ca, h2, up_second, down_first, dout))

    h3_other = over_core(h3)
    dout_other = over_core(dout)
    down_second = over_x(down_first)
    g0, du0, out_m, y_m = feed(place, h3, dout, (w_up,), (w_down,), FULL, 0)
    g0, du0, out_o, y_o = feed(
        place, h3_other, dout_other, (w_up,), (w_down,), FULL, 1, shared=(g0, du0)
    )
    y_o, down_second, ca, h2 = join((y_o, down_second, ca, h2))

    ups = (up_first, up_second)
    downs = (down_first, down_second)
    g1, du1, out_o, y_o = feed(
        place, h3_other, dout_other, ups, downs, ROUND, 1, before=(out_o, y_o)
    )
    y_received = over_core(y_o)
    h2_other = over_core(h2)
    ca_other = over_core(ca[:, 512:])
    g1, du1, out_m, y_m = feed(
        place, h3, dout, ups, downs, FULL, 0, before=(out_m, y_m), shared=(g1, du1)
    )

    def plus(a, b):
        return lower(a.astype(FULL) + b.astype(FULL))

    across = (column, X_PAIRS)
    down_z = (near, Z_NEAR)
    store = {}
    last = []
    free = []

    def order(*names):
        if free:
            return
        names = tuple(dict.fromkeys((*names, *last)))
        for name, value in zip(names, join(tuple(store[name] for name in names))):
            store[name] = value

    def get(*names):
        return tuple(store[name] for name in names)

    def step(results, make, *needs):
        order(*needs)
        made = make()
        made = made if isinstance(made, (tuple, list)) else (made,)
        store.update(zip(results, made))
        last[:] = results[:1]

    class Sum:
        def __init__(self, name, axes=(across, down_z)):
            self.fly, self.kept, self.axes = name + "_fly", name + "_kept", axes

        def over_y(self, partner):
            order(partner)
            store[self.fly] = over_y(store[partner])

        def first(self, own):
            which, pairs = self.axes[0]
            order(self.fly, own)
            mine, fly = get(own, self.fly)
            away_half = plus(half_of(mine, 1 - which), half_of(fly, 1 - which))
            store[self.kept] = half_of(mine, which).astype(FULL) + half_of(fly, which).astype(FULL)
            store[self.fly] = along_wide(away_half, pairs)
            last[:] = [self.kept]

        def first_alone(self, own):
            which, pairs = self.axes[0]
            store[self.kept] = half_of(store[own], which).astype(FULL)
            store[self.fly] = along_wide(half_of(store[own], 1 - which), pairs)
            last[:] = [self.kept]

        def second(self):
            which, pairs = self.axes[1]
            order(self.fly, self.kept)
            total = store[self.kept] + store[self.fly].astype(FULL)
            store[self.kept] = half_of(total, which)
            store[self.fly] = along_wide(lower(half_of(total, 1 - which)), pairs)
            last[:] = [self.kept]

        def add(self, pairs):
            order(self.fly, self.kept)
            store[self.kept] = plus(*get(self.kept, self.fly))
            store[self.fly] = along_wide(store[self.kept], pairs)
            last[:] = [self.kept]

        def far(self):
            self.add(Z_FAR)

        def back(self):
            self.add(self.axes[1][1])

        def along(self):
            order(self.fly, self.kept)
            store[self.kept] = ordered(*get(self.kept, self.fly), self.axes[1][0])
            store[self.fly] = along_wide(store[self.kept], self.axes[0][1])
            last[:] = [self.kept]

        def end(self, result):
            order(self.fly, self.kept)
            store[result] = ordered(*get(self.kept, self.fly), self.axes[0][0]).astype(FULL)
            last[:] = [result]

    class Row:
        def __init__(self, name, value, move):
            self.fly, self.kept = name + "_fly", name + "_kept"
            store[self.kept] = value
            store[self.fly] = move(value)

        def then(self, move):
            order(self.fly, self.kept)
            store[self.kept] = store[self.kept] + store[self.fly]
            store[self.fly] = move(store[self.kept])
            last[:] = [self.kept]

        def total(self):
            return store[self.kept] + store[self.fly]

    up, down, outs, qkv = Sum("up"), Sum("down"), Sum("outs"), Sum("qkv")
    cross_in = Sum("cross_in", (down_z, across))
    store.update(h3_other=h3_other, du1=du1, g1=g1, du0=du0, g0=g0, y_m=y_m, y_fly=y_received)
    store.update(of=of, o_s=o_s, o0=o0, x2=x2, h2_other=h2_other, ca_other=ca_other)

    def middle():
        dx1, *rest = middle_back(
            place, *get("y_m", "y_fly"), x1, store["x2"], dout, cq, wq, wc, ck, cv, norm_gain
        )
        return (rest[0], dx1, *rest[1:])

    step(["up1"], lambda: up_grad(h3, *get("h3_other", "du1"), ROUND), "du1", "du0")
    up.over_y("up1")
    step(["down1"], lambda: down_grad(store["g1"], dout, dout_other, ROUND), "g1")
    step(["dself", "dx1", "dcross", "dcq", "dck", "dcv", "sums"], middle, "y_fly", "y_m", "x2")
    store["dself_other"] = over_core(store["dself"])
    step(["up0"], lambda: up_grad(h3, *get("h3_other", "du0"), ROUND), "du0")
    order(up.fly, "down1", "dself_other")
    down.over_y("down1")
    up.first("up0")
    step(
        ["dof", "dos", "do0"],
        lambda: pull(place, *get("dself", "dself_other"), (out_first, out_second, w_out)),
        "dself",
        "dself_other",
        "dcross",
        "dcq",
    )
    store["dcross_other"] = over_core(store["dcross"])
    store["dcq_other"] = over_core(store["dcq"][:, 512:])
    d_pair = jnp.stack(get("dck", "dcv"), axis=1)
    store["pair_kept"] = d_pair[:2]
    store["pair_fly"] = over_core(d_pair[2:])
    step(
        ["dqf", "dkf", "dvf"],
        lambda: self_back(limit, qf, kf, vf, store["of"], store["dof"], lse_f),
        "dof",
    )
    def query(g):
        return query_grad(place, g, h2, *get("h2_other", "dcq", "dcq_other"), ROUND)

    def outof(g, *o):
        return outputs_grad(
            place, g, get(*o), *get("dself", "dself_other"), ca,
            *get("ca_other", "dcross", "dcross_other"), ROUND,
        )

    step(["query1"], lambda: query(1), "dcq_other", "h2_other", "pair_fly", "pair_kept")
    pair_sum = lower(store["pair_kept"] + store["pair_fly"])
    store["pair"] = pair_sum[0]
    store["pair_other"] = cross_order(pair_sum[1])
    up.second()
    step(
        ["dqs", "dks", "dvs"],
        lambda: self_back(limit, qs, ks, vs, store["o_s"], store["dos"], lse_s),
        "dos",
    )
    up.far()
    step(["down0"], lambda: down_grad(store["g0"], dout, dout_other, ROUND), "g0")
    yp = ("dqf", "dkf", "dvf", "dqs", "dks", "dvs")
    step(["qkv1"], lambda: qkv_grad(place, h1, get(*yp), ROUND), "dqs")
    order(down.fly, "qkv1", "query1", "pair_other")
    store["query_fly"] = over_y(store["query1"])
    store["pair_y"] = over_y(store["pair_other"])
    qkv.over_y("qkv1")
    down.first("down0")
    step(
        ["dq0", "dk0", "dv0"],
        lambda: self_back(limit, q0, k0, v0, store["o0"], store["do0"], lse0),
        "do0",
    )
    down.second()
    up.back()
    step(["outs1"], lambda: outof(1, "of", "o_s"), "dcross_other", "ca_other")
    outs.over_y("outs1")
    nine = ("dq0", "dk0", "dv0", *yp)
    weights = (w_qkv, qkv_first, qkv_second)
    step(["yo"], lambda: first_back(away, get(*nine), weights, ROUND), "dq0")
    store["yo_fly"] = over_core(store["yo"])
    step(["qkv0"], lambda: qkv_grad(place, h1, get("dq0", "dk0", "dv0"), ROUND), "dq0")
    qkv.first("qkv0")
    up.along()
    down.far()
    step(["query0"], lambda: query(0), "dcq")
    order("query0", "query_fly", "pair", "pair_y")
    other_text = lax.dynamic_index_in_dim(text_states, 1 - side, keepdims=False)
    texts = jnp.concatenate([text, other_text], axis=0)
    pairs = jnp.concatenate(get("pair", "pair_y"), axis=1)
    store["into0"] = jnp.concatenate(
        [
            lower(store["query0"].astype(FULL) + store["query_fly"].astype(FULL)),
            lower(tn(texts, pairs[0])),
            lower(tn(texts, pairs[1])),
        ],
        axis=0,
    )
    cross_in.first_alone("into0")
    step(["ym"], lambda: first_back(place, get(*nine), weights, FULL), "dq0")
    step(
        ["grad_frames", "first_sums"],
        lambda: frames_back(place, *get("ym", "yo_fly", "dx1"), frames, norm_gain),
        "ym",
        "yo_fly",
        "outs_fly",
    )
    norms = Row("norms", store["sums"] + store["first_sums"], over_core)
    norms.then(over_y)
    cross_in.second()
    qkv.second()
    step(["outs0"], lambda: outof(0, "o0"), "dcross")
    outs.first("outs0")
    norms.then(over_z)
    text_part = 0.0
    for c in range(2):
        text_part = text_part + nt(pairs[c], w_cross_kv[c])
    text_mine, text_theirs = text_part[:64], text_part[64:]
    text_rows = Row("texts", text_mine, lambda v: over_y(text_theirs))
    last[:] = ["texts_kept"]
    down.back()
    up.end("grad_up")
    cross_in.far()
    store["out_fly"] = over_core(out_o)
    text_rows.then(over_core)
    outs.second()
    qkv.far()
    norms.then(lambda v: along_wide(v, Z_FAR))
    order("x2", "out_fly")
    out_rows = lower(store["x2"] + out_m + store["out_fly"].astype(FULL))
    down.along()
    cross_in.back()
    order("texts_fly", "texts_kept")
    text_grad = lower(text_rows.total())
    text_away = over_y(text_grad)
    grad_text = ordered(text_grad[None], text_away[None], side)
    outs.far()
    norms.then(over_x)
    qkv.back()
    cross_in.along()
    outs.back()
    down.end("grad_down")
    qkv.along()
    outs.along()
    cross_in.end("grad_in")
    sums = norms.total()
    qkv.end("grad_qkv")
    outs.end("grad_outs")
    grad_in, grad_outs = get("grad_in", "grad_outs")
    return (
        out_rows,
        store["grad_frames"],
        grad_text,
        sums[0:6:2],
        sums[1:6:2],
        store["grad_qkv"].reshape(3, width, 256),
        grad_outs[:256],
        grad_in[:width],
        grad_in[width:].reshape(2, width, 256),
        grad_outs[256:],
        store["grad_up"],
        store["grad_down"],
    )


def solution(mesh):
    chips = dict(mesh.shape) == {"wide": 8, "narrow": 4}
    return jax.shard_map(
        chip_local if chips else general_local,
        mesh=mesh,
        in_specs=(
            P(("wide", "narrow"), None),
            P("wide", None, None),
            P("wide"),
            P(("wide", "narrow")),
            P(),
            P(),
            P(None, None, "narrow"),
            P("narrow", None),
            P(None, "narrow"),
            P(None, None, "narrow"),
            P("narrow", None),
            P(None, "narrow"),
            P("narrow", None),
            P(("wide", "narrow"), None),
        ),
        out_specs=(
            P(("wide", "narrow"), None),
            P(("wide", "narrow"), None),
            P("wide", None, None),
            P(),
            P(),
            P(None, None, "narrow"),
            P("narrow", None),
            P(None, "narrow"),
            P(None, None, "narrow"),
            P("narrow", None),
            P(None, "narrow"),
            P("narrow", None),
        ),
        check_vma=False,
    )
```

```python
import functools

import jax
import jax.numpy as jnp
from jax import lax
from jax.experimental import pallas as pl
from jax.experimental.pallas import tpu as pltpu
from jax.sharding import PartitionSpec as P

HEAD = 64


EPS = 1e-05
NEG = -1e30


def lower(values_in):
    return values_in.astype(jnp.bfloat16)


def product(left_side, right_side, transposed):
    if transposed:
        return lax.dot_general(
            left_side, right_side, (((1,), (1,)), ((), ())), preferred_element_type=jnp.float32
        )
    return jnp.dot(left_side, right_side, preferred_element_type=jnp.float32)


def outer_sum(left_side, right_side):
    return lax.dot_general(
        left_side, right_side, (((0,), (0,)), ((), ())), preferred_element_type=jnp.float32
    )


def normalize(values_in, gain_row, bias_row):
    row_mean = jnp.mean(values_in, axis=-1, keepdims=True)
    centered = values_in - row_mean
    inverse = lax.rsqrt(jnp.mean(centered * centered, axis=-1, keepdims=True) + EPS)
    scaled = centered * inverse
    return (scaled * gain_row + bias_row, scaled, inverse)


def normalize_back(upstream, scaled, inverse, gain_row):
    weighted = upstream * gain_row
    inner_mean = jnp.mean(weighted, axis=-1, keepdims=True)
    along_mean = jnp.mean(weighted * scaled, axis=-1, keepdims=True)
    grad_input = inverse * (weighted - inner_mean - scaled * along_mean)
    return (grad_input, jnp.sum(upstream * scaled, axis=0), jnp.sum(upstream, axis=0))


def gelu_parts(values_in):
    normal_cdf = 0.5 * (1.0 + jax.scipy.special.erf(values_in * 0.7071067811865476))
    normal_pdf = jnp.exp(-0.5 * values_in * values_in) * 0.3989422804014327
    return (values_in * normal_cdf, normal_cdf + values_in * normal_pdf)


def scores_of(query_part, key_part, valid):
    scores = jnp.einsum(
        "bhe,khe->hbk", query_part, key_part, preferred_element_type=jnp.float32
    ) * HEAD ** (-0.5)
    return jnp.where(valid, scores, NEG)


def attend(query_part, key_part, value_part, valid):
    scores = scores_of(query_part, key_part, valid)
    row_top = jnp.max(scores, axis=-1, keepdims=True)
    weights_exp = jnp.exp(scores - row_top)
    denominator = jnp.sum(weights_exp, axis=-1, keepdims=True)
    probability = weights_exp / denominator
    mixed = jnp.einsum(
        "hbk,khe->bhe", lower(probability), value_part, preferred_element_type=jnp.float32
    )
    return (lower(mixed), (row_top + jnp.log(denominator))[..., 0])


def attend_back(query_part, key_part, value_part, valid, summary, upstream):
    scores = scores_of(query_part, key_part, valid)
    probability = jnp.exp(scores - summary[..., None])
    pressure = jnp.einsum("bhe,khe->hbk", upstream, value_part, preferred_element_type=jnp.float32)
    grad_scores = lower(
        probability * (pressure - jnp.sum(probability * pressure, axis=-1, keepdims=True))
    )
    factor = HEAD ** (-0.5)
    grad_query = (
        jnp.einsum("hbk,khe->bhe", grad_scores, key_part, preferred_element_type=jnp.float32)
        * factor
    )
    grad_key = (
        jnp.einsum("hbk,bhe->khe", grad_scores, query_part, preferred_element_type=jnp.float32)
        * factor
    )
    grad_value = jnp.einsum(
        "hbk,bhe->khe", lower(probability), upstream, preferred_element_type=jnp.float32
    )
    return (grad_query, grad_key, grad_value)


def general_local(
    frames,
    text_states,
    lengths,
    loss_mask,
    norm_gain,
    norm_bias,
    w_qkv,
    w_out,
    w_cross_q,
    w_cross_kv,
    w_cross_out,
    w_up,
    w_down,
    cotangent,
):
    row_count = frames.shape[0]
    width = frames.shape[1]
    item_count = lengths.shape[0]
    span = row_count * lax.axis_size("narrow") // item_count
    half_span = span // 2
    inner_width = w_qkv.shape[2]
    head_count = inner_width // HEAD
    text_count = text_states.shape[1]
    full_rows = item_count * span
    places = jnp.arange(span, dtype=jnp.int32)

    def spread(shard_rows):
        return lax.all_gather(shard_rows, "narrow", axis=0, tiled=True)

    def collect(left_side, right_side, transposed):
        return lax.psum_scatter(
            product(
                lax.slice_in_dim(left_side, 0, lax.axis_size("narrow") * row_count, axis=0),
                right_side,
                transposed,
            ),
            "narrow",
            scatter_dimension=0,
            tiled=True,
        )

    def causal(block_index, item_limit):
        query_place = block_index * half_span + jnp.arange(half_span, dtype=jnp.int32)
        return (places[None, :] <= query_place[:, None]) & (places[None, :] < item_limit)

    frame_rows = frames.astype(jnp.float32)
    normed_one, scaled_one, inverse_one = normalize(frame_rows, norm_gain[0], norm_bias[0])
    first_input = spread(lower(normed_one))
    triple = lower(
        jnp.einsum("rd,cde->cre", first_input, w_qkv, preferred_element_type=jnp.float32)
    )
    triple = triple.reshape(3, item_count, span, head_count, HEAD)

    def self_item(packed):
        query_part, key_part, value_part, item_limit = packed
        mixed_list = []
        summary_list = []
        for block_index in range(2):
            mixed, summary = attend(
                query_part[block_index * half_span : (block_index + 1) * half_span],
                key_part,
                value_part,
                causal(block_index, item_limit),
            )
            mixed_list.append(mixed)
            summary_list.append(summary)
        return (jnp.concatenate(mixed_list, axis=0), jnp.stack(summary_list, axis=0))

    attended, self_summary = lax.map(self_item, (triple[0], triple[1], triple[2], lengths))
    attended_flat = attended.reshape(full_rows, inner_width)
    first_rows = frame_rows + collect(attended_flat, w_out, False)
    normed_two, scaled_two, inverse_two = normalize(first_rows, norm_gain[1], norm_bias[1])
    second_input = spread(lower(normed_two))
    cross_query = lower(product(second_input, w_cross_q, False)).reshape(
        item_count, span, head_count, HEAD
    )
    cross_pair = lower(
        jnp.einsum("ntd,cde->cnte", text_states, w_cross_kv, preferred_element_type=jnp.float32)
    )
    cross_pair = cross_pair.reshape(2, item_count, text_count, head_count, HEAD)

    def cross_item(packed):
        query_part, key_part, value_part = packed
        return attend(query_part, key_part, value_part, True)

    cross_mixed, cross_summary = lax.map(cross_item, (cross_query, cross_pair[0], cross_pair[1]))
    cross_flat = cross_mixed.reshape(full_rows, inner_width)
    second_rows = first_rows + collect(cross_flat, w_cross_out, False)
    normed_three, scaled_three, inverse_three = normalize(second_rows, norm_gain[2], norm_bias[2])
    upstream = cotangent.astype(jnp.float32) * loss_mask.astype(jnp.float32)[:, None]
    ffn_grad = lower(upstream)
    ffn_input = spread(lower(normed_three))
    hidden_pre = product(ffn_input, w_up, False)
    active, slope = gelu_parts(hidden_pre)
    active = lower(active)
    out_rows = second_rows + collect(active, w_down, False)
    ffn_full = spread(ffn_grad)
    grad_down = outer_sum(active, ffn_full)
    grad_hidden = lower(product(ffn_full, w_down, True) * slope)
    grad_up = outer_sum(ffn_input, grad_hidden)
    back_three = collect(grad_hidden, w_up, True)
    grad_up, grad_down = (grad_up, grad_down)
    grad_in_three, gain_three, bias_three = normalize_back(
        back_three, scaled_three, inverse_three, norm_gain[2]
    )
    grad_second = upstream + grad_in_three
    cross_full = spread(lower(grad_second))
    grad_cross_out = outer_sum(cross_flat, cross_full)
    cross_upstream = lower(product(cross_full, w_cross_out, True)).reshape(
        item_count, span, head_count, HEAD
    )

    def cross_back(packed):
        query_part, key_part, value_part, summary, upstream_item = packed
        return attend_back(query_part, key_part, value_part, True, summary, upstream_item)

    grad_cq, grad_ck, grad_cv = lax.map(
        cross_back, (cross_query, cross_pair[0], cross_pair[1], cross_summary, cross_upstream)
    )
    grad_cq = lower(grad_cq).reshape(full_rows, inner_width)
    grad_pair = lower(jnp.stack((grad_ck, grad_cv), axis=0)).reshape(
        2, item_count, text_count, inner_width
    )
    grad_cross_q = outer_sum(second_input, grad_cq)
    grad_cross_kv = jnp.einsum(
        "ntd,cnte->cde", text_states, grad_pair, preferred_element_type=jnp.float32
    )
    grad_cross_q, grad_cross_kv, grad_cross_out = (grad_cross_q, grad_cross_kv, grad_cross_out)
    text_partial = jnp.einsum(
        "cnte,cde->ntd", grad_pair, w_cross_kv, preferred_element_type=jnp.float32
    )
    grad_text = lower(lax.psum(text_partial, "narrow"))
    back_two = collect(grad_cq, w_cross_q, True)
    grad_in_two, gain_two, bias_two = normalize_back(
        back_two, scaled_two, inverse_two, norm_gain[1]
    )
    grad_first = grad_second + grad_in_two
    self_full = spread(lower(grad_first))
    grad_out = outer_sum(attended_flat, self_full)
    self_upstream = lower(product(self_full, w_out, True)).reshape(
        item_count, span, head_count, HEAD
    )

    def self_back(packed):
        query_part, key_part, value_part, item_limit, summary, upstream_item = packed
        query_list = []
        key_list = []
        value_list = []
        for block_index in range(2):
            lower_row = block_index * half_span
            grad_query, grad_key, grad_value = attend_back(
                query_part[lower_row : lower_row + half_span],
                key_part,
                value_part,
                causal(block_index, item_limit),
                summary[block_index],
                upstream_item[lower_row : lower_row + half_span],
            )
            query_list.append(grad_query)
            key_list.append(grad_key)
            value_list.append(grad_value)
        return (
            jnp.concatenate(query_list, axis=0),
            key_list[0] + key_list[1],
            value_list[0] + value_list[1],
        )

    grad_q, grad_k, grad_v = lax.map(
        self_back, (triple[0], triple[1], triple[2], lengths, self_summary, self_upstream)
    )
    grad_triple = lower(jnp.stack((grad_q, grad_k, grad_v), axis=0)).reshape(
        3, full_rows, inner_width
    )
    grad_qkv = jnp.einsum(
        "rd,cre->cde", first_input, grad_triple, preferred_element_type=jnp.float32
    )
    grad_qkv, grad_out = (grad_qkv, grad_out)
    merged = grad_triple.transpose(1, 0, 2).reshape(full_rows, 3 * inner_width)
    stacked_weights = w_qkv.transpose(0, 2, 1).reshape(3 * inner_width, width)
    back_one = collect(merged, stacked_weights, False)
    grad_in_one, gain_one, bias_one = normalize_back(
        back_one, scaled_one, inverse_one, norm_gain[0]
    )
    grad_frames = lower(grad_first + grad_in_one)
    gain_terms = jnp.stack((gain_one, gain_two, gain_three), axis=0)
    bias_terms = jnp.stack((bias_one, bias_two, bias_three), axis=0)
    grad_norm_gain, grad_norm_bias = lax.psum((gain_terms, bias_terms), ("wide", "narrow"))
    grad_qkv, grad_out, grad_cross_q, grad_cross_kv, grad_cross_out, grad_up, grad_down = lax.psum(
        (grad_qkv, grad_out, grad_cross_q, grad_cross_kv, grad_cross_out, grad_up, grad_down),
        "wide",
    )
    return (
        lower(out_rows),
        grad_frames,
        grad_text,
        grad_norm_gain,
        grad_norm_bias,
        grad_qkv,
        grad_out,
        grad_cross_q,
        grad_cross_kv,
        grad_cross_out,
        grad_up,
        grad_down,
    )


ROUND = jnp.bfloat16
FULL = jnp.float32
CORE_PAIRS = ((0, 1), (1, 0), (2, 3), (3, 2))
Y_PAIRS = ((0, 2), (2, 0), (1, 3), (3, 1))
X_PAIRS = tuple((i, i ^ 1) for i in range(8))
Z_INWARD = ((0, 2), (1, 3), (6, 4), (7, 5))
Z_MIDDLE = ((2, 4), (4, 2), (3, 5), (5, 3))
Z_OUTWARD = ((2, 0), (3, 1), (4, 6), (5, 7))
Z_NEAR = tuple((i, i ^ 2) for i in range(8))
Z_FAR = tuple((i, i ^ 4) for i in range(8))
MIB = 1 << 20


def nt(a, b):
    return lax.dot_general(a, b, (((1,), (1,)), ((), ())), preferred_element_type=FULL)


def nn(a, b):
    return lax.dot_general(a, b, (((1,), (0,)), ((), ())), preferred_element_type=FULL)


def tn(a, b):
    return lax.dot_general(a, b, (((0,), (0,)), ((), ())), preferred_element_type=FULL)


def shape(dims, kind):
    return jax.ShapeDtypeStruct(dims, kind)


def resident(dims):
    zeros = (0,) * len(dims)
    return pl.BlockSpec(dims, lambda i, s: zeros, pipeline_mode=pl.Buffered(1))


def rows_of(block, width):
    return pl.BlockSpec((block, width), lambda i, s: (i, 0))


def lasting(microseconds):
    flops = int(microseconds * 0.28 * 1.15e9)
    return pl.CostEstimate(flops=flops, bytes_accessed=1000, transcendentals=0)


def params(mib):
    return pltpu.CompilerParams(vmem_limit_bytes=mib * MIB)


def norm_parts(v):
    centered = v - jnp.mean(v, axis=-1, keepdims=True)
    inverse = lax.rsqrt(jnp.mean(centered * centered, axis=-1, keepdims=True) + EPS)
    return centered * inverse, inverse


def norm_pull(y, scaled, inverse, gain_row):
    weighted = y * gain_row
    inner = jnp.mean(weighted, axis=-1, keepdims=True)
    along = jnp.mean(weighted * scaled, axis=-1, keepdims=True)
    return inverse * (weighted - inner - scaled * along)


def first_project_kernel(
    place_ref, mine_ref, other_ref, gain_ref, bias_ref, weight_ref, h_ref, *out_refs
):
    half = pl.program_id(0)

    def run(source):
        for start in range(0, source.shape[0], 208):
            part = slice(start, start + 208)
            scaled, _ = norm_parts(source[part, :].astype(FULL))
            h = lower(scaled * gain_ref[0:1, :] + bias_ref[0:1, :])
            h_ref[part, :] = h
            for c, out_ref in enumerate(out_refs):
                out_ref[part, :] = lower(nn(h, weight_ref[c]))

    @pl.when(half == 0)
    def _():
        run(mine_ref)

    @pl.when(half == 1)
    def _():
        run(other_ref)


def first_project(place, mine, other, gains, biases, weights):
    rows, depth = mine.shape
    count, _, wide = weights.shape
    out = pl.BlockSpec((rows, wide), lambda i, s: ((i + s[0]) % 2, 0))
    return pl.pallas_call(
        first_project_kernel,
        grid_spec=pltpu.PrefetchScalarGridSpec(
            num_scalar_prefetch=1,
            grid=(2,),
            in_specs=[resident(a.shape) for a in (mine, other, gains, biases, weights)],
            out_specs=[rows_of(rows, depth)] + [out] * count,
        ),
        out_shape=[shape((2 * rows, depth), ROUND)] + [shape((2 * rows, wide), ROUND)] * count,
        compiler_params=params(40),
        cost_estimate=lasting(5),
        name="first_project",
    )(place, mine, other, gains, biases, weights)


def project_kernel(place_ref, h_ref, weight_ref, *out_refs):
    count = len(out_refs)
    wide = weight_ref.shape[2]
    weights = jnp.concatenate([weight_ref[c] for c in range(count)], axis=1)
    for start in range(0, h_ref.shape[0], 416):
        part = slice(start, start + 416)
        result = lower(nn(h_ref[part, :], weights))
        for c, out_ref in enumerate(out_refs):
            out_ref[part, :] = result[:, c * wide : (c + 1) * wide]


def project(place, h, weights):
    rows, depth = h.shape[0] // 2, h.shape[1]
    count, _, wide = weights.shape
    out = pl.BlockSpec((rows, wide), lambda i, s: ((i + s[0]) % 2, 0))
    return pl.pallas_call(
        project_kernel,
        grid_spec=pltpu.PrefetchScalarGridSpec(
            num_scalar_prefetch=1,
            grid=(2,),
            in_specs=[rows_of(rows, depth), resident(weights.shape)],
            out_specs=[out] * count,
        ),
        out_shape=[shape((2 * rows, wide), ROUND)] * count,
        compiler_params=params(40),
        cost_estimate=lasting(4),
        name="project",
    )(place, h, weights)


def pull_kernel(place_ref, mine_ref, other_ref, *refs):
    half = pl.program_id(0)
    count = len(refs) // 2

    def run(source):
        for weight_ref, out_ref in zip(refs[:count], refs[count:]):
            out_ref[...] = lower(nt(source[...], weight_ref[...]))

    @pl.when(half == 0)
    def _():
        run(mine_ref)

    @pl.when(half == 1)
    def _():
        run(other_ref)


def pull(place, mine, other, weights):
    rows = mine.shape[0]
    return pl.pallas_call(
        pull_kernel,
        grid_spec=pltpu.PrefetchScalarGridSpec(
            num_scalar_prefetch=1,
            grid=(2,),
            in_specs=[resident(a.shape) for a in (mine, other, *weights)],
            out_specs=[
                pl.BlockSpec((rows, a.shape[0]), lambda i, s: ((i + s[0]) % 2, 0)) for a in weights
            ],
        ),
        out_shape=[shape((2 * rows, a.shape[0]), ROUND) for a in weights],
        compiler_params=params(32),
        cost_estimate=lasting(0.375),
        name="pull",
    )(place, mine, other, *weights)


def blocks_of(span, block):
    return [(start, min(block, span - start)) for start in range(0, span, block)]


def self_forward_kernel(
    limit_ref, q_ref, k_ref, v_ref, o_ref, lse_ref, *, span, floor, block
):
    limit = limit_ref[0]
    lane = lax.broadcasted_iota(jnp.int32, (1, 128), 1)
    row = lax.broadcasted_iota(jnp.int32, (128, 1), 0)
    zero = jnp.zeros((), ROUND)
    value_turned = v_ref[...].T
    for start, size in blocks_of(span, block):
        end = start + size
        mixed_list = []
        for h in range(2):
            own_lanes = (lane < HEAD) if h == 0 else (lane >= HEAD)
            query = jnp.where(own_lanes, q_ref[start:end, :] * HEAD ** (-0.5), zero)
            parts = []
            for low in range(0, end, block):
                high = min(low + block, end)
                scores = nt(k_ref[low:high, :], query)
                if low == start:
                    key = lax.broadcasted_iota(jnp.int32, (size, size), 0)
                    valid = key <= lax.broadcasted_iota(jnp.int32, (size, size), 1)
                    if high > floor:
                        valid = valid & (key + low < limit)
                    scores = jnp.where(valid, scores, NEG)
                elif high > floor:
                    key = lax.broadcasted_iota(jnp.int32, (high - low, 1), 0)
                    scores = jnp.where(key + low < limit, scores, NEG)
                parts.append((low, high, scores))
            top = functools.reduce(
                jnp.maximum, [jnp.max(s, axis=0, keepdims=True) for _, _, s in parts]
            )
            total = 0.0
            mixed = 0.0
            for low, high, scores in parts:
                weights_exp = jnp.exp(scores - top)
                total = total + jnp.sum(weights_exp, axis=0, keepdims=True)
                mixed = mixed + nn(value_turned[:, low:high], lower(weights_exp))
            mixed_list.append(mixed / total)
            lse_ref[0, h : h + 1, start:end] = top + jnp.log(total)
        o_ref[start:end, :] = lower(jnp.where(row < HEAD, mixed_list[0], mixed_list[1]).T)


def self_forward(limit, q, k, v):
    span, wide = q.shape
    pairs = wide // 128
    floor = (span - span // 8 + 1) // 128 * 128
    pair = pl.BlockSpec((span, 128), lambda p, s: (0, p))
    return pl.pallas_call(
        functools.partial(self_forward_kernel, span=span, floor=floor, block=512),
        grid_spec=pltpu.PrefetchScalarGridSpec(
            num_scalar_prefetch=1,
            grid=(pairs,),
            in_specs=[pair] * 3,
            out_specs=[pair, pl.BlockSpec((1, 8, span), lambda p, s: (p, 0, 0))],
        ),
        out_shape=[shape((span, wide), ROUND), shape((pairs, 8, span), FULL)],
        compiler_params=params(56),
        cost_estimate=lasting(7.3 * pairs),
        name="self_forward",
    )(limit, q, k, v)


def self_back_kernel(
    limit_ref, q_ref, k_ref, v_ref, o_ref, do_ref, lse_ref, dq_ref, dk_ref, dv_ref, dqt,
    *, span, floor, block
):
    limit = limit_ref[0]
    lane = lax.broadcasted_iota(jnp.int32, (1, 128), 1)
    row = lax.broadcasted_iota(jnp.int32, (128, 1), 0)
    zero = jnp.zeros((), ROUND)
    factor = HEAD ** (-0.5)
    product_rows = do_ref[...].astype(FULL) * o_ref[...].astype(FULL)
    high = lower(product_rows)
    rest = lower(product_rows - high.astype(FULL))
    pick = lower(
        jnp.concatenate(
            [
                jnp.where(lane < HEAD, 1.0, 0.0),
                jnp.where(lane >= HEAD, 1.0, 0.0),
                jnp.zeros((6, 128), FULL),
            ],
            axis=0,
        )
    )
    delta = nt(pick, high) + nt(pick, rest)
    for start, size in blocks_of(span, block):
        end = start + size
        key = k_ref[start:end, :]
        value = v_ref[start:end, :]
        key_turned = key.T
        dk = 0.0
        dv = 0.0
        dq_add = 0.0
        for h in range(2):
            own_lanes = (lane < HEAD) if h == 0 else (lane >= HEAD)
            own_rows = (row < HEAD) if h == 0 else (row >= HEAD)
            query = jnp.where(own_lanes, q_ref[start:, :] * factor, zero)
            pulled = jnp.where(own_lanes, do_ref[start:, :], zero)
            probability = jnp.exp(nt(key, query) - lse_ref[0, h : h + 1, start:])
            pressure = nt(value, pulled)
            below = lax.broadcasted_iota(jnp.int32, (size, size), 0)
            across = lax.broadcasted_iota(jnp.int32, (size, size), 1)
            corner = jnp.where(below <= across, probability[:, :size], 0.0)
            if end < span:
                probability = jnp.concatenate([corner, probability[:, size:]], axis=1)
            else:
                probability = corner
            if end > floor:
                place = lax.broadcasted_iota(jnp.int32, (size, 1), 0) + start
                probability = jnp.where(place < limit, probability, 0.0)
            grad_scores = lower(probability * (pressure - delta[h : h + 1, start:]))
            dv = dv + nn(lower(probability), pulled)
            dk = dk + nn(grad_scores, query)
            dq_add = dq_add + nn(jnp.where(own_rows, key_turned, zero), grad_scores)
        dk_ref[start:end, :] = lower(dk)
        dv_ref[start:end, :] = lower(dv)
        if start == 0:
            dqt[...] = dq_add
        else:
            dqt[:, start:] += dq_add
    dq_ref[...] = lower(dqt[...].T * factor)


def self_back(limit, q, k, v, o, do, lse):
    span, wide = q.shape
    pairs = wide // 128
    floor = (span - span // 8 + 1) // 128 * 128
    pair = pl.BlockSpec((span, 128), lambda p, s: (0, p))
    return pl.pallas_call(
        functools.partial(self_back_kernel, span=span, floor=floor, block=256),
        grid_spec=pltpu.PrefetchScalarGridSpec(
            num_scalar_prefetch=1,
            grid=(pairs,),
            in_specs=[pair] * 5 + [pl.BlockSpec((1, 8, span), lambda p, s: (p, 0, 0))],
            out_specs=[pair] * 3,
            scratch_shapes=[pltpu.VMEM((128, span), FULL)],
        ),
        out_shape=[shape((span, wide), ROUND)] * 3,
        compiler_params=params(48),
        cost_estimate=lasting(1.050 * pairs),
        name="self_back",
    )(limit, q, k, v, o, do, lse)


def by_head(values_in, reduce, empty):
    lane = lax.broadcasted_iota(jnp.int32, (1, 128), 1)
    pieces = []
    for start in range(0, values_in.shape[1], 128):
        part = values_in[:, start : start + 128]
        first = reduce(jnp.where(lane < HEAD, part, empty), axis=1, keepdims=True)
        second = reduce(jnp.where(lane >= HEAD, part, empty), axis=1, keepdims=True)
        pieces.append(jnp.where(lane < HEAD, first, second))
    return jnp.concatenate(pieces, axis=1)


def cross_probability(query, keys):
    scores = nt(query * HEAD ** (-0.5), keys)
    weights_exp = jnp.exp(scores - by_head(scores, jnp.max, NEG))
    return weights_exp / by_head(weights_exp, jnp.sum, 0.0)


def in_groups(refs, axis):
    for at in (0, 3):
        yield refs[at][...]
        yield jnp.concatenate([refs[at + 1][...], refs[at + 2][...]], axis=axis)


def middle_forward_kernel(place_ref, frame_ref, *refs):
    mixed, wo, wq, wc = refs[0:6], refs[6:12], refs[12:18], refs[18:24]
    ck_ref, cv_ref, gain_ref, bias_ref = refs[24:28]
    x1_ref, x2_ref, h2_ref, cq_ref, ca_ref, h3_ref = refs[28:]
    x1 = frame_ref[...].astype(FULL)
    for o, weight in zip(in_groups(mixed, 1), in_groups(wo, 0)):
        x1 = x1 + nn(o, weight)
    x1_ref[...] = x1
    scaled, _ = norm_parts(x1)
    h2 = lower(scaled * gain_ref[1:2, :] + bias_ref[1:2, :])
    h2_ref[...] = h2
    for g, weight in enumerate(in_groups(wq, 1)):
        lanes = slice(g * 256, (g + 1) * 256)
        cq = lower(nn(h2, weight))
        cq_ref[:, lanes] = cq
        probability = cross_probability(cq, ck_ref[g])
        ca_ref[:, lanes] = lower(nn(lower(probability), cv_ref[g]))
    crossed = 0.0
    for g, weight in enumerate(in_groups(wc, 0)):
        crossed = crossed + nn(ca_ref[:, g * 256 : (g + 1) * 256], weight)
    x2 = x1_ref[...] + crossed
    x2_ref[...] = x2
    scaled, _ = norm_parts(x2)
    h3_ref[...] = lower(scaled * gain_ref[2:3, :] + bias_ref[2:3, :])


def middle_forward(place, frames, attended, received, wo, wq, wc, ck, cv, gains, biases):
    rows, width = frames.shape
    block = 416
    steps = rows // block
    wide = rows_of(block, width)
    whole = (*wo, *wq, *wc, ck, cv, gains, biases)
    return pl.pallas_call(
        middle_forward_kernel,
        grid_spec=pltpu.PrefetchScalarGridSpec(
            num_scalar_prefetch=1,
            grid=(steps,),
            in_specs=[wide]
            + [
                pl.BlockSpec((block, a.shape[1]), lambda i, s: (s[0] * steps + i, 0))
                for a in attended
            ]
            + [rows_of(block, a.shape[1]) for a in received]
            + [resident(a.shape) for a in whole],
            out_specs=[wide] * 6,
        ),
        out_shape=[shape((rows, width), FULL)] * 2 + [shape((rows, width), ROUND)] * 4,
        compiler_params=params(56),
        cost_estimate=lasting(22),
        name="middle_forward",
    )(place, frames, *attended, *received, *whole)


def keys_kernel(text_ref, weight_ref, out_ref):
    for item in range(2):
        for c in range(2):
            out_ref[item, c] = lower(nn(text_ref[item], weight_ref[c]))


def keys_of(text_states, weights):
    items, states, _ = text_states.shape
    return pl.pallas_call(
        keys_kernel,
        out_shape=shape((items, 2, states, weights.shape[2]), ROUND),
        compiler_params=params(24),
        cost_estimate=lasting(2),
        name="keys_of",
    )(text_states, weights)


def feed_kernel(place_ref, h_ref, d_ref, *refs, parts, carried):
    ups, downs = refs[:parts], refs[parts : 2 * parts]
    before = refs[2 * parts : 2 * parts + carried]
    g_ref, du_ref, out_ref, y_ref = refs[-4:]
    h = h_ref[...]
    d = d_ref[...]
    out = 0.0
    y = 0.0
    for n, (up_ref, down_ref) in enumerate(zip(ups, downs)):
        size = down_ref.shape[0]
        if parts == 1:
            lanes = slice(0, size)
        else:
            column = place_ref[2]
            which = column if n == 0 else 1 - column
            lanes = pl.ds(pl.multiple_of(which * size, 128), size)
        u = nn(h, up_ref[...])
        active, slope = gelu_parts(u)
        g = lower(active)
        g_ref[:, lanes] = g
        du = lower(nt(d, down_ref[...]) * slope)
        du_ref[:, lanes] = du
        out = out + nn(g, down_ref[...])
        y = y + nt(du, up_ref[...])
    if carried:
        out = before[0][...] + out
        y = before[1][...] + y
    out_ref[...] = out.astype(out_ref.dtype)
    y_ref[...] = y.astype(y_ref.dtype)


def feed(place, h, d, ups, downs, kind, half, before=(), shared=()):
    rows, width = h.shape
    block = 416
    steps = rows // block
    hidden = sum(a.shape[0] for a in downs)
    wide = rows_of(block, width)
    kept = pl.BlockSpec((block, hidden), lambda i, s: (i + half * steps, 0))
    there = pl.BlockSpec(memory_space=pl.ANY)
    parts = len(ups)
    at = 3 + 2 * parts + len(before)
    return pl.pallas_call(
        functools.partial(feed_kernel, parts=parts, carried=len(before)),
        grid_spec=pltpu.PrefetchScalarGridSpec(
            num_scalar_prefetch=1,
            grid=(steps,),
            in_specs=[wide, wide]
            + [resident(a.shape) for a in (*ups, *downs)]
            + [wide] * len(before)
            + [there] * len(shared),
            out_specs=[kept, kept, wide, wide],
        ),
        out_shape=[shape((2 * rows, hidden), ROUND)] * 2 + [shape((rows, width), kind)] * 2,
        input_output_aliases={at: 0, at + 1: 1} if shared else {},
        compiler_params=params(58),
        cost_estimate=lasting(13),
        name="feed",
    )(place, h, d, *ups, *downs, *before, *shared)


def up_grad_kernel(mine_ref, other_ref, du_ref, out_ref):
    rows = mine_ref.shape[0]
    total = tn(mine_ref[...], du_ref[:rows, :]) + tn(other_ref[...], du_ref[rows:, :])
    out_ref[...] = total.astype(out_ref.dtype)


def up_grad(mine, other, du, kind):
    rows, width = mine.shape
    hidden = du.shape[1]
    tile = 512
    whole = pl.BlockSpec((rows, width), lambda i: (0, 0), pipeline_mode=pl.Buffered(1))
    return pl.pallas_call(
        up_grad_kernel,
        grid=(hidden // tile,),
        in_specs=[whole, whole, pl.BlockSpec((2 * rows, tile), lambda i: (0, i))],
        out_specs=pl.BlockSpec((width, tile), lambda i: (0, i)),
        out_shape=shape((width, hidden), kind),
        compiler_params=params(48),
        cost_estimate=lasting(0.750),
        name="up_grad",
    )(mine, other, du)


def down_grad_kernel(g_ref, mine_ref, other_ref, out_ref):
    rows = mine_ref.shape[0]
    total = tn(g_ref[:rows, :], mine_ref[...]) + tn(g_ref[rows:, :], other_ref[...])
    out_ref[...] = total.astype(out_ref.dtype)


def down_grad(g, mine, other, kind):
    rows, width = mine.shape
    hidden = g.shape[1]
    tile = 512
    whole = pl.BlockSpec((rows, width), lambda i: (0, 0), pipeline_mode=pl.Buffered(1))
    return pl.pallas_call(
        down_grad_kernel,
        grid=(hidden // tile,),
        in_specs=[pl.BlockSpec((2 * rows, tile), lambda i: (0, i)), whole, whole],
        out_specs=pl.BlockSpec((tile, width), lambda i: (i, 0)),
        out_shape=shape((hidden, width), kind),
        compiler_params=params(48),
        cost_estimate=lasting(3.50),
        name="down_grad",
    )(g, mine, other)


def qkv_grad_kernel(place_ref, h_ref, *refs):
    out_ref = refs[-1]
    rows, width = h_ref.shape[0] // 2, h_ref.shape[1]
    core, near = place_ref[0], place_ref[1]
    halves = (len(refs) - 1) // 3
    total = [0.0] * 3
    for half in range(2):
        turned = h_ref[half * rows : (half + 1) * rows, :].T
        at = pl.multiple_of((core if half == 0 else 1 - core) * rows, 16)
        for c in range(3):
            parts = [refs[3 * n + c][pl.ds(at, rows), :] for n in range(halves)]
            grads = parts[0] if halves == 1 else jnp.concatenate(parts, axis=1)
            total[c] = total[c] + nn(turned, grads)
    for c in range(3):
        part = slice(c * width, (c + 1) * width)
        value = total[c].astype(out_ref.dtype)
        if halves == 1:
            out_ref[part, :] = value
        else:
            out_ref[part, pl.ds(pl.multiple_of(near * 128, 128), 128)] = value[:, :128]
            out_ref[part, pl.ds(pl.multiple_of((1 - near) * 128, 128), 128)] = value[:, 128:]


def qkv_grad(place, h, grads, kind):
    width = h.shape[1]
    return pl.pallas_call(
        qkv_grad_kernel,
        grid_spec=pltpu.PrefetchScalarGridSpec(
            num_scalar_prefetch=1,
            grid=(1,),
            in_specs=[resident(a.shape) for a in (h, *grads)],
            out_specs=resident((3 * width, 256)),
        ),
        out_shape=shape((3 * width, 256), kind),
        compiler_params=params(48),
        cost_estimate=lasting(3.50),
        name="qkv_grad",
    )(place, h, *grads)


def query_grad_kernel(place_ref, mine_ref, other_ref, dm_ref, do_ref, out_ref, *, split):
    column = place_ref[2]
    total = tn(mine_ref[...], dm_ref[...]) + tn(other_ref[...], do_ref[...])
    value = total.astype(out_ref.dtype)
    if split:
        out_ref[:, pl.ds(pl.multiple_of(column * 128, 128), 128)] = value[:, :128]
        out_ref[:, pl.ds(pl.multiple_of((1 - column) * 128, 128), 128)] = value[:, 128:]
    else:
        out_ref[...] = value


def query_grad(place, group, mine, other, d_mine, d_other, kind):
    rows, width = mine.shape
    lanes = pl.BlockSpec((rows, 256), lambda i, s: (0, group))
    return pl.pallas_call(
        functools.partial(query_grad_kernel, split=group == 1),
        grid_spec=pltpu.PrefetchScalarGridSpec(
            num_scalar_prefetch=1,
            grid=(1,),
            in_specs=[resident(mine.shape), resident(other.shape), lanes, lanes],
            out_specs=resident((width, 256)),
        ),
        out_shape=shape((width, 256), kind),
        compiler_params=params(48),
        cost_estimate=lasting(0.429),
        name="query_grad",
    )(place, mine, other, d_mine, d_other)


def outputs_grad_kernel(place_ref, *refs, count):
    o_refs = refs[:count]
    sm_ref, so_ref, am_ref, ao_ref, cm_ref, co_ref, out_ref = refs[count:]
    rows = sm_ref.shape[0]
    core, near, column = place_ref[0], place_ref[1], place_ref[2]
    mine_at = pl.ds(pl.multiple_of(core * rows, 16), rows)
    other_at = pl.ds(pl.multiple_of((1 - core) * rows, 16), rows)
    for n, o_ref in enumerate(o_refs):
        total = tn(o_ref[mine_at, :], sm_ref[...]) + tn(o_ref[other_at, :], so_ref[...])
        if count == 1:
            at = slice(0, 256)
        else:
            at = pl.ds(pl.multiple_of((near if n == 0 else 1 - near) * 128, 128), 128)
        out_ref[at, :] = total.astype(out_ref.dtype)
    total = tn(am_ref[...], cm_ref[...]) + tn(ao_ref[...], co_ref[...])
    value = total.astype(out_ref.dtype)
    if count == 1:
        out_ref[256:, :] = value
    else:
        out_ref[pl.ds(pl.multiple_of(256 + column * 128, 128), 128), :] = value[:128, :]
        out_ref[pl.ds(pl.multiple_of(384 - column * 128, 128), 128), :] = value[128:, :]


def outputs_grad(place, group, o, dself, dself_other, ca, ca_other, dcross, dcross_other, kind):
    rows, width = dself.shape
    lanes = pl.BlockSpec((rows, 256), lambda i, s: (0, group))
    whole = resident((rows, width))
    return pl.pallas_call(
        functools.partial(outputs_grad_kernel, count=len(o)),
        grid_spec=pltpu.PrefetchScalarGridSpec(
            num_scalar_prefetch=1,
            grid=(1,),
            in_specs=[resident(a.shape) for a in o] + [whole, whole, lanes, lanes, whole, whole],
            out_specs=resident((512, width)),
        ),
        out_shape=shape((512, width), kind),
        compiler_params=params(48),
        cost_estimate=lasting(0.643),
        name="outputs_grad",
    )(place, *o, dself, dself_other, ca, ca_other, dcross, dcross_other)


def middle_back_kernel(place_ref, ym_ref, yr_ref, x1_ref, x2_ref, d_ref, cq_ref, *refs):
    wq, wc = refs[0:6], refs[6:12]
    ck_ref, cv_ref, gain_ref = refs[12:15]
    dx1_ref, dself_ref, dcross_ref, dcq_ref, dck_ref, dcv_ref, sums_ref = refs[15:22]
    dck_all, dcv_all = refs[22:]
    step = pl.program_id(0)

    @pl.when(step == 0)
    def _():
        dck_all[...] = jnp.zeros_like(dck_all)
        dcv_all[...] = jnp.zeros_like(dcv_all)
        sums_ref[...] = jnp.zeros_like(sums_ref)

    y3 = ym_ref[...] + yr_ref[...].astype(FULL)
    scaled, inverse = norm_parts(x2_ref[...])
    sums_ref[4:5, :] += jnp.sum(y3 * scaled, axis=0, keepdims=True)
    sums_ref[5:6, :] += jnp.sum(y3, axis=0, keepdims=True)
    dx2 = d_ref[...].astype(FULL) + norm_pull(y3, scaled, inverse, gain_ref[2:3, :])
    dx1_ref[...] = dx2
    dcross = lower(dx2)
    dcross_ref[...] = dcross
    for g, weight in enumerate(in_groups(wc, 0)):
        lanes = slice(g * 256, (g + 1) * 256)
        dcatt = lower(nt(dcross, weight))
        keys = ck_ref[g]
        cq = cq_ref[:, lanes]
        probability = cross_probability(cq, keys)
        weighed = nt(dcatt, cv_ref[g])
        inner = by_head(probability * weighed, jnp.sum, 0.0)
        dcs = lower(probability * (weighed - inner))
        dcq_ref[:, lanes] = lower(nn(dcs, keys) * HEAD ** (-0.5))
        dck_all[g] += tn(dcs, cq * HEAD ** (-0.5))
        dcv_all[g] += tn(lower(probability), dcatt)
    y2 = 0.0
    for g, weight in enumerate(in_groups(wq, 1)):
        y2 = y2 + nt(dcq_ref[:, g * 256 : (g + 1) * 256], weight)
    scaled, inverse = norm_parts(x1_ref[...])
    sums_ref[2:3, :] += jnp.sum(y2 * scaled, axis=0, keepdims=True)
    sums_ref[3:4, :] += jnp.sum(y2, axis=0, keepdims=True)
    dx1 = dx1_ref[...] + norm_pull(y2, scaled, inverse, gain_ref[1:2, :])
    dx1_ref[...] = dx1
    dself_ref[...] = lower(dx1)

    @pl.when(step == pl.num_programs(0) - 1)
    def _():
        for every, result in ((dck_all, dck_ref), (dcv_all, dcv_ref)):
            for g in range(4):
                total = 0.0
                for h in range(4):
                    lane = lax.broadcasted_iota(jnp.int32, (1, 256), 1) // HEAD
                    total = total + jnp.where(lane == h, every[g, h * 64 : (h + 1) * 64, :], 0.0)
                result[g] = total


def middle_back(place, ym, yr, x1, x2, d, cq, wq, wc, ck, cv, gains):
    rows, width = x1.shape
    block = 416
    wide = rows_of(block, width)
    small = pl.BlockSpec((4, 64, 256), lambda i, s: (0, 0, 0))
    whole = (*wq, *wc, ck, cv, gains)
    return pl.pallas_call(
        middle_back_kernel,
        grid_spec=pltpu.PrefetchScalarGridSpec(
            num_scalar_prefetch=1,
            grid=(rows // block,),
            in_specs=[wide] * 6 + [resident(a.shape) for a in whole],
            out_specs=[wide] * 4 + [small, small, pl.BlockSpec((8, width), lambda i, s: (0, 0))],
            scratch_shapes=[pltpu.VMEM((4, 256, 256), FULL)] * 2,
        ),
        out_shape=[shape((rows, width), FULL)]
        + [shape((rows, width), ROUND)] * 3
        + [shape((4, 64, 256), FULL)] * 2
        + [shape((8, width), FULL)],
        compiler_params=params(56),
        cost_estimate=lasting(2.571),
        name="middle_back",
    )(place, ym, yr, x1, x2, d, cq, *whole)


def first_back_kernel(place_ref, *refs):
    y_ref = refs[-1]
    y = 0.0
    for n in range(3):
        for c in range(3):
            y = y + nt(refs[3 * n + c][...], refs[9 + n][c])
    y_ref[...] = y.astype(y_ref.dtype)


def first_back(place, grads, weights, kind):
    span = grads[0].shape[0]
    rows = span // 2
    width = weights[0].shape[1]
    block = 416
    steps = rows // block
    return pl.pallas_call(
        first_back_kernel,
        grid_spec=pltpu.PrefetchScalarGridSpec(
            num_scalar_prefetch=1,
            grid=(steps,),
            in_specs=[
                pl.BlockSpec((block, a.shape[1]), lambda i, s: (s[0] * steps + i, 0))
                for a in grads
            ]
            + [resident(a.shape) for a in weights],
            out_specs=rows_of(block, width),
        ),
        out_shape=shape((rows, width), kind),
        compiler_params=params(40),
        cost_estimate=lasting(0.535),
        name="first_back",
    )(place, *grads, *weights)


def frames_back_kernel(place_ref, ym_ref, yr_ref, dx1_ref, frame_ref, gain_ref, out_ref, sums_ref):
    @pl.when(pl.program_id(0) == 0)
    def _():
        sums_ref[...] = jnp.zeros_like(sums_ref)

    y = ym_ref[...] + yr_ref[...].astype(FULL)
    scaled, inverse = norm_parts(frame_ref[...].astype(FULL))
    sums_ref[0:1, :] += jnp.sum(y * scaled, axis=0, keepdims=True)
    sums_ref[1:2, :] += jnp.sum(y, axis=0, keepdims=True)
    out_ref[...] = lower(dx1_ref[...] + norm_pull(y, scaled, inverse, gain_ref[0:1, :]))


def frames_back(place, ym, yr, dx1, frames, gains):
    rows, width = dx1.shape
    block = 208
    wide = rows_of(block, width)
    return pl.pallas_call(
        frames_back_kernel,
        grid_spec=pltpu.PrefetchScalarGridSpec(
            num_scalar_prefetch=1,
            grid=(rows // block,),
            in_specs=[wide] * 4 + [resident(gains.shape)],
            out_specs=[wide, pl.BlockSpec((8, width), lambda i, s: (0, 0))],
        ),
        out_shape=[shape((rows, width), ROUND), shape((8, width), FULL)],
        compiler_params=params(24),
        cost_estimate=lasting(0.643),
        name="frames_back",
    )(place, ym, yr, dx1, frames, gains)


def chip_local(
    frames, text_states, lengths, loss_mask, norm_gain, norm_bias, w_qkv, w_out, w_cross_q,
    w_cross_kv, w_cross_out, w_up, w_down, cotangent,
):
    at = lax.axis_index("narrow")
    core = at % 2
    side = at // 2
    column = lax.axis_index("wide") % 2
    layer = lax.axis_index("wide") // 2
    near = layer % 2
    place = jnp.stack([core, near, column]).astype(jnp.int32)
    away = jnp.stack([1 - core, near, column]).astype(jnp.int32)
    limit = lax.dynamic_slice(lengths, (side,), (1,))
    rows, width = frames.shape
    join = lax.optimization_barrier

    def over_core(v):
        return lax.ppermute(v, "narrow", CORE_PAIRS)

    def over_y(v):
        return lax.ppermute(v, "narrow", Y_PAIRS)

    def along_wide(v, pairs):
        return lax.ppermute(v, "wide", pairs)

    def half_of(v, which, axis=0):
        half = v.shape[axis] // 2
        return lax.dynamic_slice_in_dim(v, which * half, half, axis=axis)

    def ordered(first, second, which):
        return jnp.where(
            which == 0,
            jnp.concatenate([first, second], axis=0),
            jnp.concatenate([second, first], axis=0),
        )

    def over_z(v):
        return along_wide(v, Z_NEAR)

    def over_x(v):
        return along_wide(v, X_PAIRS)

    def away_rows(v):
        return half_of(v, 1 - core)

    def cross_order(v):
        return jnp.where(column == 0, v, jnp.concatenate([v[..., 128:], v[..., :128]], axis=-1))

    qkv_first = over_y(half_of(w_qkv, near, 2))
    frames_other = over_core(frames)
    h1, q0, k0, v0 = first_project(place, frames, frames_other, norm_gain, norm_bias, w_qkv)
    q0, qkv_first, w_out, w_cross_q, w_cross_out, cotangent = join(
        (q0, qkv_first, w_out, w_cross_q, w_cross_out, cotangent)
    )

    qkv_second = over_z(qkv_first)
    both_first = over_y(
        jnp.concatenate([half_of(w_out, near), half_of(w_cross_out, column)], axis=0)
    )
    query_first = over_y(half_of(w_cross_q, column, 1))
    o0, lse0 = self_forward(limit, q0, k0, v0)
    qf, kf, vf = project(place, h1, qkv_first)
    out_other, query_other, cross_out_other = map(over_core, (w_out, w_cross_q, w_cross_out))
    qf, o0, both_first, query_first, w_up, w_down, *core_got = join(
        (qf, o0, both_first, query_first, w_up, w_down)
        + (out_other, query_other, cross_out_other)
    )
    out_first, cross_out_first = both_first[:128], both_first[128:]

    out_other, query_other, cross_out_other = core_got
    out_second = over_z(out_first)
    query_second = over_x(query_first)
    cross_out_second = over_x(cross_out_first)
    up_first = over_y(half_of(w_up, column, 1))
    down_sent = half_of(w_down, column)
    o0_other = over_core(away_rows(o0))
    keys = keys_of(text_states, w_cross_kv)
    own_keys = lax.dynamic_index_in_dim(keys, side, keepdims=False)
    keys_y = over_y(lax.dynamic_index_in_dim(keys, 1 - side, keepdims=False))
    of, lse_f = self_forward(limit, qf, kf, vf)
    of, qkv_second, keys_y, o0_other = join((of, qkv_second, keys_y, o0_other))

    qs, ks, vs = project(place, h1, qkv_second)
    of_other = over_core(away_rows(of))
    pair = jnp.stack([own_keys, cross_order(keys_y)])
    pair_other = over_core(pair)
    o_s, lse_s = self_forward(limit, qs, ks, vs)
    o_s, out_second, query_second, cross_out_second, up_first, down_sent, pair_other, of_other = join(
        (o_s, out_second, query_second, cross_out_second, up_first, down_sent, pair_other, of_other)
    )

    down_first = over_y(down_sent)
    up_second = over_x(up_first)
    os_other = over_core(away_rows(o_s))
    dout = jnp.where(loss_mask[:, None] != 0, cotangent, jnp.zeros((), ROUND))

    def pieces(own, first, second, own_other):
        return (own, first, second, own_other, over_core(first), over_core(second))

    wo = pieces(w_out, out_first, out_second, out_other)
    wq = pieces(w_cross_q, query_first, query_second, query_other)
    wc = pieces(w_cross_out, cross_out_first, cross_out_second, cross_out_other)
    text = lax.dynamic_index_in_dim(text_states, side, keepdims=False)
    head_of = jnp.arange(256) // HEAD
    same = head_of[:, None] == head_of[None, :]

    def spread_heads(v):
        return jnp.where(same, jnp.tile(v, (1, 4, 1)), jnp.zeros((), ROUND))

    every = jnp.concatenate([pair, pair_other], axis=0)
    ck, cv = spread_heads(every[:, 0]), spread_heads(every[:, 1])
    x1, x2, h2, cq, ca, h3 = middle_forward(
        place, frames, (o0, of, o_s), (o0_other, of_other, os_other), wo, wq, wc, ck, cv,
        norm_gain, norm_bias,
    )
    h3, ca, h2, up_second, down_first, dout = join((h3, ca, h2, up_second, down_first, dout))

    h3_other = over_core(h3)
    dout_other = over_core(dout)
    down_second = over_x(down_first)
    g0, du0, out_m, y_m = feed(place, h3, dout, (w_up,), (w_down,), FULL, 0)
    g0, du0, out_o, y_o = feed(
        place, h3_other, dout_other, (w_up,), (w_down,), FULL, 1, shared=(g0, du0)
    )
    y_o, down_second, ca, h2 = join((y_o, down_second, ca, h2))

    ups = (up_first, up_second)
    downs = (down_first, down_second)
    g1, du1, out_o, y_o = feed(
        place, h3_other, dout_other, ups, downs, ROUND, 1, before=(out_o, y_o)
    )
    y_received = over_core(y_o)
    h2_other = over_core(h2)
    ca_other = over_core(ca[:, 512:])
    g1, du1, out_m, y_m = feed(
        place, h3, dout, ups, downs, FULL, 0, before=(out_m, y_m), shared=(g1, du1)
    )

    def plus(a, b):
        return lower(a.astype(FULL) + b.astype(FULL))

    across = (column, X_PAIRS)
    down_z = (near, Z_NEAR)
    store = {}
    last = []
    free = []

    def order(*names):
        if free:
            return
        names = tuple(dict.fromkeys((*names, *last)))
        for name, value in zip(names, join(tuple(store[name] for name in names))):
            store[name] = value

    def get(*names):
        return tuple(store[name] for name in names)

    def step(results, make, *needs):
        order(*needs)
        made = make()
        made = made if isinstance(made, (tuple, list)) else (made,)
        store.update(zip(results, made))
        last[:] = results[:1]

    class Sum:
        def __init__(self, name, axes=(across, down_z)):
            self.fly, self.kept, self.axes = name + "_fly", name + "_kept", axes

        def over_y(self, partner):
            order(partner)
            store[self.fly] = over_y(store[partner])

        def first(self, own):
            which, pairs = self.axes[0]
            order(self.fly, own)
            mine, fly = get(own, self.fly)
            away_half = plus(half_of(mine, 1 - which), half_of(fly, 1 - which))
            store[self.kept] = half_of(mine, which).astype(FULL) + half_of(fly, which).astype(FULL)
            store[self.fly] = along_wide(away_half, pairs)
            last[:] = [self.kept]

        def first_alone(self, own):
            which, pairs = self.axes[0]
            store[self.kept] = half_of(store[own], which).astype(FULL)
            store[self.fly] = along_wide(half_of(store[own], 1 - which), pairs)
            last[:] = [self.kept]

        def second(self):
            which, pairs = self.axes[1]
            order(self.fly, self.kept)
            total = store[self.kept] + store[self.fly].astype(FULL)
            store[self.kept] = half_of(total, which)
            store[self.fly] = along_wide(lower(half_of(total, 1 - which)), pairs)
            last[:] = [self.kept]

        def add(self, pairs):
            order(self.fly, self.kept)
            store[self.kept] = plus(*get(self.kept, self.fly))
            store[self.fly] = along_wide(store[self.kept], pairs)
            last[:] = [self.kept]

        def far(self):
            self.add(Z_FAR)

        def back(self):
            self.add(self.axes[1][1])

        def along(self):
            order(self.fly, self.kept)
            store[self.kept] = ordered(*get(self.kept, self.fly), self.axes[1][0])
            store[self.fly] = along_wide(store[self.kept], self.axes[0][1])
            last[:] = [self.kept]

        def end(self, result):
            order(self.fly, self.kept)
            store[result] = ordered(*get(self.kept, self.fly), self.axes[0][0]).astype(FULL)
            last[:] = [result]

    class Row:
        def __init__(self, name, value, move):
            self.fly, self.kept = name + "_fly", name + "_kept"
            store[self.kept] = value
            store[self.fly] = move(value)

        def then(self, move):
            order(self.fly, self.kept)
            store[self.kept] = store[self.kept] + store[self.fly]
            store[self.fly] = move(store[self.kept])
            last[:] = [self.kept]

        def total(self):
            return store[self.kept] + store[self.fly]

    up, down, outs, qkv = Sum("up"), Sum("down"), Sum("outs"), Sum("qkv")
    cross_in = Sum("cross_in", (down_z, across))
    store.update(h3_other=h3_other, du1=du1, g1=g1, du0=du0, g0=g0, y_m=y_m, y_fly=y_received)
    store.update(of=of, o_s=o_s, o0=o0, x2=x2, h2_other=h2_other, ca_other=ca_other)

    def middle():
        dx1, *rest = middle_back(
            place, *get("y_m", "y_fly"), x1, store["x2"], dout, cq, wq, wc, ck, cv, norm_gain
        )
        return (rest[0], dx1, *rest[1:])

    step(["up1"], lambda: up_grad(h3, *get("h3_other", "du1"), ROUND), "du1", "du0")
    up.over_y("up1")
    step(["down1"], lambda: down_grad(store["g1"], dout, dout_other, ROUND), "g1")
    step(["dself", "dx1", "dcross", "dcq", "dck", "dcv", "sums"], middle, "y_fly", "y_m", "x2")
    store["dself_other"] = over_core(store["dself"])
    step(["up0"], lambda: up_grad(h3, *get("h3_other", "du0"), ROUND), "du0")
    order(up.fly, "down1", "dself_other")
    down.over_y("down1")
    up.first("up0")
    step(
        ["dof", "dos", "do0"],
        lambda: pull(place, *get("dself", "dself_other"), (out_first, out_second, w_out)),
        "dself",
        "dself_other",
        "dcross",
        "dcq",
    )
    store["dcross_other"] = over_core(store["dcross"])
    store["dcq_other"] = over_core(store["dcq"][:, 512:])
    d_pair = jnp.stack(get("dck", "dcv"), axis=1)
    store["pair_kept"] = d_pair[:2]
    store["pair_fly"] = over_core(d_pair[2:])
    step(
        ["dqf", "dkf", "dvf"],
        lambda: self_back(limit, qf, kf, vf, store["of"], store["dof"], lse_f),
        "dof",
    )
    def query(g):
        return query_grad(place, g, h2, *get("h2_other", "dcq", "dcq_other"), ROUND)

    def outof(g, *o):
        return outputs_grad(
            place, g, get(*o), *get("dself", "dself_other"), ca,
            *get("ca_other", "dcross", "dcross_other"), ROUND,
        )

    step(["query1"], lambda: query(1), "dcq_other", "h2_other", "pair_fly", "pair_kept")
    pair_sum = lower(store["pair_kept"] + store["pair_fly"])
    store["pair"] = pair_sum[0]
    store["pair_other"] = cross_order(pair_sum[1])
    up.second()
    step(
        ["dqs", "dks", "dvs"],
        lambda: self_back(limit, qs, ks, vs, store["o_s"], store["dos"], lse_s),
        "dos",
    )
    up.far()
    step(["down0"], lambda: down_grad(store["g0"], dout, dout_other, ROUND), "g0")
    yp = ("dqf", "dkf", "dvf", "dqs", "dks", "dvs")
    step(["qkv1"], lambda: qkv_grad(place, h1, get(*yp), ROUND), "dqs")
    order(down.fly, "qkv1", "query1", "pair_other")
    store["query_fly"] = over_y(store["query1"])
    store["pair_y"] = over_y(store["pair_other"])
    qkv.over_y("qkv1")
    down.first("down0")
    step(
        ["dq0", "dk0", "dv0"],
        lambda: self_back(limit, q0, k0, v0, store["o0"], store["do0"], lse0),
        "do0",
    )
    down.second()
    up.back()
    step(["outs1"], lambda: outof(1, "of", "o_s"), "dcross_other", "ca_other")
    outs.over_y("outs1")
    nine = ("dq0", "dk0", "dv0", *yp)
    weights = (w_qkv, qkv_first, qkv_second)
    step(["yo"], lambda: first_back(away, get(*nine), weights, ROUND), "dq0")
    store["yo_fly"] = over_core(store["yo"])
    step(["qkv0"], lambda: qkv_grad(place, h1, get("dq0", "dk0", "dv0"), ROUND), "dq0")
    qkv.first("qkv0")
    up.along()
    down.far()
    step(["query0"], lambda: query(0), "dcq")
    order("query0", "query_fly", "pair", "pair_y")
    other_text = lax.dynamic_index_in_dim(text_states, 1 - side, keepdims=False)
    texts = jnp.concatenate([text, other_text], axis=0)
    pairs = jnp.concatenate(get("pair", "pair_y"), axis=1)
    store["into0"] = jnp.concatenate(
        [
            lower(store["query0"].astype(FULL) + store["query_fly"].astype(FULL)),
            lower(tn(texts, pairs[0])),
            lower(tn(texts, pairs[1])),
        ],
        axis=0,
    )
    cross_in.first_alone("into0")
    step(["ym"], lambda: first_back(place, get(*nine), weights, FULL), "dq0")
    step(
        ["grad_frames", "first_sums"],
        lambda: frames_back(place, *get("ym", "yo_fly", "dx1"), frames, norm_gain),
        "ym",
        "yo_fly",
        "outs_fly",
    )
    norms = Row("norms", store["sums"] + store["first_sums"], over_core)
    norms.then(over_y)
    cross_in.second()
    qkv.second()
    step(["outs0"], lambda: outof(0, "o0"), "dcross")
    outs.first("outs0")
    norms.then(over_z)
    text_part = 0.0
    for c in range(2):
        text_part = text_part + nt(pairs[c], w_cross_kv[c])
    text_mine, text_theirs = text_part[:64], text_part[64:]
    text_rows = Row("texts", text_mine, lambda v: over_y(text_theirs))
    last[:] = ["texts_kept"]
    down.back()
    up.end("grad_up")
    cross_in.far()
    store["out_fly"] = over_core(out_o)
    text_rows.then(over_core)
    norms.then(lambda v: along_wide(v, Z_FAR))
    outs.second()
    qkv.far()
    order("x2", "out_fly")
    out_rows = lower(store["x2"] + out_m + store["out_fly"].astype(FULL))
    down.along()
    cross_in.back()
    order("texts_fly", "texts_kept")
    text_grad = lower(text_rows.total())
    text_away = over_y(text_grad)
    grad_text = ordered(text_grad[None], text_away[None], side)
    outs.far()
    norms.then(over_x)
    qkv.back()
    cross_in.along()
    outs.back()
    down.end("grad_down")
    qkv.along()
    outs.along()
    cross_in.end("grad_in")
    sums = norms.total()
    qkv.end("grad_qkv")
    outs.end("grad_outs")
    grad_in, grad_outs = get("grad_in", "grad_outs")
    return (
        out_rows,
        store["grad_frames"],
        grad_text,
        sums[0:6:2],
        sums[1:6:2],
        store["grad_qkv"].reshape(3, width, 256),
        grad_outs[:256],
        grad_in[:width],
        grad_in[width:].reshape(2, width, 256),
        grad_outs[256:],
        store["grad_up"],
        store["grad_down"],
    )


def solution(mesh):
    chips = dict(mesh.shape) == {"wide": 8, "narrow": 4}
    return jax.shard_map(
        chip_local if chips else general_local,
        mesh=mesh,
        in_specs=(
            P(("wide", "narrow"), None),
            P("wide", None, None),
            P("wide"),
            P(("wide", "narrow")),
            P(),
            P(),
            P(None, None, "narrow"),
            P("narrow", None),
            P(None, "narrow"),
            P(None, None, "narrow"),
            P("narrow", None),
            P(None, "narrow"),
            P("narrow", None),
            P(("wide", "narrow"), None),
        ),
        out_specs=(
            P(("wide", "narrow"), None),
            P(("wide", "narrow"), None),
            P("wide", None, None),
            P(),
            P(),
            P(None, None, "narrow"),
            P("narrow", None),
            P(None, "narrow"),
            P(None, None, "narrow"),
            P("narrow", None),
            P(None, "narrow"),
            P("narrow", None),
        ),
        check_vma=False,
    )
```
